32 devices in a mesh: dp: 8 (over z, x), seq: 4 (over y, core).
Axes of the slice: x: 2, y: 2, z: 4, core: 2. Of those that a mesh axis runs over, the one named last changes fastest.
Arguments:
- word_states: bfloat16 [16, 512, 768], P('dp', 'seq'), may hold values from -6 to 6
- segments: int32 [16, 512], P('dp'), may hold values from 0 to 3, as said below
- entity_ids: int32 [16, 128], P('dp'), may hold values from 0 to 65535
- entity_pos: int32 [16, 128], P('dp'), may hold values from 0 to 511
- ent_table: float32 [65536, 256], P(('dp', 'seq')), may hold values from -6 to 6
- first_moment: float32 [65536, 256], P(('dp', 'seq')), may hold values from -1.75 to 1.75
- second_moment: float32 [65536, 256], P(('dp', 'seq')), may hold values from 0.01 to 1
- ent_proj: bfloat16 [256, 768], replicated, may hold values from -0.375 to 0.375
- pos_table: bfloat16 [512, 768], replicated, may hold values from -3 to 3
- query_weight: bfloat16 [4, 768, 768], replicated, may hold values from -0.21875 to 0.21875
- query_bias: bfloat16 [4, 768], replicated, may hold values from -1.75 to 1.75
- key_weight: bfloat16 [768, 768], replicated, may hold values from -0.21875 to 0.21875
- key_bias: bfloat16 [768], replicated, may hold values from -3 to 3
- value_weight: bfloat16 [768, 768], replicated, may hold values from -0.21875 to 0.21875
- value_bias: bfloat16 [768], replicated, may hold values from -3 to 3
- out_weight: bfloat16 [768, 768], replicated, may hold values from -2.5 to 2.5
- out_bias: bfloat16 [768], replicated, may hold values from -1.75 to 1.75
- norm_gain: bfloat16 [2, 768], replicated, may hold values from 0.5 to 1.5
- norm_shift: bfloat16 [2, 768], replicated, may hold values from -1.75 to 1.75
- up_weight: bfloat16 [768, 3072], replicated, may hold values from -0.21875 to 0.21875
- up_bias: bfloat16 [3072], replicated, may hold values from -1.75 to 1.75
- down_weight: bfloat16 [3072, 768], replicated, may hold values from -0.109375 to 0.109375
- down_bias: bfloat16 [768], replicated, may hold values from -1.75 to 1.75
- word_cot: bfloat16 [16, 512, 768], P('dp', 'seq'), may hold values from -6 to 6
- ent_cot: bfloat16 [16, 128, 768], P('dp', 'seq'), may hold values from -6 to 6
Outputs:
- word_out: bfloat16 [16, 512, 768], P('dp', 'seq')
- ent_out: bfloat16 [16, 128, 768], P('dp', 'seq')
- word_grad: float32 [16, 512, 768], P('dp', 'seq')
- proj_grad: float32 [256, 768], P('dp')
- pos_grad: float32 [512, 768], P('dp')
- query_grad: float32 [4, 768, 768], P(None, 'dp')
- query_bias_grad: float32 [4, 768], P(None, 'dp')
- key_grad: float32 [768, 768], P('dp')
- key_bias_grad: float32 [768], P('dp')
- value_grad: float32 [768, 768], P('dp')
- value_bias_grad: float32 [768], P('dp')
- out_grad: float32 [768, 768], P('dp')
- out_bias_grad: float32 [768], P('dp')
- gain_grad: float32 [2, 768], P(None, 'dp')
- shift_grad: float32 [2, 768], P(None, 'dp')
- up_grad: float32 [768, 3072], P('dp')
- up_bias_grad: float32 [3072], P('dp')
- down_grad: float32 [3072, 768], P('dp')
- down_bias_grad: float32 [768], P('dp')
- table_grad: float32 [65536, 256], P(('dp', 'seq'))
- table_update: float32 [65536, 256], P(('dp', 'seq'))
- new_second: float32 [65536, 256], P(('dp', 'seq'))
The draws below stay inside these ranges and needn't reach their ends.
Inputs may be any that keep to these rules, and one draw needn't show every extreme that they name: `segments`: within a sequence segment numbers start at 0 and never fall; in each aligned block of 2 sequences one sequence is a single segment.
All inputs are finite; a program needn't handle non-finite values.
Results may differ from the reference program's by a relative error of at most 0.028.
Values may be sent and summed in bfloat16 or wider, within the bound.
A program may use at most 192 MiB of HBM per device.

```python
import math
import jax
import jax.numpy as jnp
import numpy as np
from jax import lax

D = 768
HEADS = 12
HEAD = 64
FF = 3072
EDIM = 256
WORDS = 512
ENTS = 128
SEQ_DEV = 2
SEQS = 16
ENT_ROWS = 65536


def draw_segments(key, part):
    key = jax.random.fold_in(key, 11)
    cut_key, pick_key = jax.random.split(key)
    cut_points = jax.random.randint(cut_key, (SEQS, 3), 1, WORDS)
    places = jnp.arange(WORDS)
    counted = jnp.sum((places[None, :, None] >= cut_points[:, None, :]).astype(jnp.int32), axis=-1)
    chosen = jax.random.randint(pick_key, (SEQS // SEQ_DEV,), 0, SEQ_DEV)
    single = jnp.arange(SEQS) % SEQ_DEV == jnp.repeat(chosen, SEQ_DEV)
    return jnp.where(single[:, None], 0, counted).astype(jnp.int32)


def with_ends(values, key, least, top_value):
    dims = values.shape
    place = [jax.random.randint(jax.random.fold_in(key, axis), (), 0, dims[axis]) for axis in range(len(dims))]
    values = values.at[tuple(place)].set(least)
    longest = dims.index(max(dims))
    place[longest] = (place[longest] + 1) % dims[longest]
    return values.at[tuple(place)].set(top_value)


def steps_of(stream_key, dims, pieces, low, top_value):
    factor_of = 1.0
    for dim, parts in pieces:
        heights = jax.random.uniform(jax.random.fold_in(jax.random.fold_in(stream_key, 6), dim), (parts,), jnp.float32, low / len(pieces), top_value / len(pieces))
        factor_of = factor_of * jnp.repeat(jnp.exp(heights), dims[dim] // parts).reshape((-1,) + (1,) * (len(dims) - 1 - dim))
    return factor_of


def cumulative_ranks(amount, lean):
    portions = [(1 << 20) // math.isqrt(rank ** lean) + 1 for rank in range(1, amount + 1)]
    scale = 1 + sum(portions) // (1 << 30)
    return np.cumsum(np.array([max(1, weight // scale) for weight in portions]))


def ranked_ids(stream_key, shape, amount, skew):
    table = cumulative_ranks(amount, skew)
    pick = jax.random.randint(jax.random.fold_in(stream_key, 1), shape, 0, int(table[amount - 1]))
    grade = jnp.searchsorted(jnp.asarray(table, jnp.int32), pick, side="right")
    return jax.random.permutation(jax.random.fold_in(stream_key, 2), amount)[grade].astype(jnp.int32)


def bell_draw(key, extent, scale, reach, cuts=(), dtype=jnp.bfloat16):
    level = steps_of(key, extent, cuts, -0.22, 0.18) if cuts else 1.0
    values = jax.random.normal(key, extent, jnp.float32) * scale * level
    return jnp.minimum(jnp.maximum(values, -reach), reach).astype(dtype)


def setup_inputs(seed: int = 0) -> dict:
    keys = jax.random.split(jax.random.key(seed), 26)
    word_states = bell_draw(keys[0], (SEQS, WORDS, D), 1.0, 6.0, ((0, 8), (1, 4)))
    segments = draw_segments(jax.random.fold_in(keys[25], 71), 0)
    entity_ids = with_ends(ranked_ids(keys[2], (SEQS, ENTS), ENT_ROWS, 2), jax.random.fold_in(keys[2], 3), 0, ENT_ROWS - 1).astype(jnp.int32)
    entity_pos = with_ends(jax.random.randint(keys[3], (SEQS, ENTS), 0, WORDS), jax.random.fold_in(keys[3], 1), 0, WORDS - 1).astype(jnp.int32)
    ent_table = bell_draw(keys[4], (ENT_ROWS, EDIM), 1.0, 6.0, ((0, 32),), jnp.float32)
    first_moment = bell_draw(keys[5], (ENT_ROWS, EDIM), 0.3, 1.75, ((0, 32),), jnp.float32)
    second_moment = jnp.clip(jnp.exp(math.log(1.0) - 4.6051702 * jax.random.uniform(keys[6], (ENT_ROWS, EDIM), jnp.float32) ** steps_of(keys[6], (ENT_ROWS, EDIM), ((0, 32),), -0.2, 0.2)), 0.01, 1.0)
    ent_proj = bell_draw(keys[7], (EDIM, D), EDIM ** -0.5, 0.375)
    pos_table = bell_draw(keys[8], (WORDS, D), 0.5, 3.0)
    query_weight = bell_draw(keys[9], (4, D, D), D ** -0.5, 0.21875)
    query_bias = bell_draw(keys[10], (4, D), 0.3, 1.75)
    key_weight = bell_draw(keys[11], (D, D), D ** -0.5, 0.21875)
    key_bias = bell_draw(keys[12], (D,), 0.5, 3.0)
    value_weight = bell_draw(keys[13], (D, D), D ** -0.5, 0.21875)
    value_bias = bell_draw(keys[14], (D,), 0.5, 3.0)
    out_weight = bell_draw(keys[15], (D, D), (max(D // 128, 1)) ** -0.5, 2.5)
    out_bias = bell_draw(keys[16], (D,), 0.3, 1.75)
    norm_gain = jnp.clip(1.0 + 0.1 * jax.random.normal(keys[17], (2, D), jnp.float32), 0.5, 1.5).astype(jnp.bfloat16)
    norm_shift = bell_draw(keys[18], (2, D), 0.3, 1.75)
    up_weight = bell_draw(keys[19], (D, FF), D ** -0.5, 0.21875)
    up_bias = bell_draw(keys[20], (FF,), 0.3, 1.75)
    down_weight = bell_draw(keys[21], (FF, D), FF ** -0.5, 0.109375)
    down_bias = bell_draw(keys[22], (D,), 0.3, 1.75)
    word_cot = bell_draw(keys[23], (SEQS, WORDS, D), 1.0, 6.0, ((0, 8), (1, 4)))
    ent_cot = bell_draw(keys[24], (SEQS, ENTS, D), 1.0, 6.0, ((0, 8), (1, 4)))
    return {"word_states": word_states, "segments": segments, "entity_ids": entity_ids, "entity_pos": entity_pos, "ent_table": ent_table, "first_moment": first_moment, "second_moment": second_moment, "ent_proj": ent_proj, "pos_table": pos_table, "query_weight": query_weight, "query_bias": query_bias, "key_weight": key_weight, "key_bias": key_bias, "value_weight": value_weight, "value_bias": value_bias, "out_weight": out_weight, "out_bias": out_bias, "norm_gain": norm_gain, "norm_shift": norm_shift, "up_weight": up_weight, "up_bias": up_bias, "down_weight": down_weight, "down_bias": down_bias, "word_cot": word_cot, "ent_cot": ent_cot}


@jax.custom_vjp
def low(v):
    return lax.optimization_barrier(v.astype(jnp.bfloat16)).astype(jnp.float32)

@jax.custom_vjp
def low_back(v):
    return v

def low_keep(v):
    return (low(v), None)

def low_pass(kept, grad):
    return (grad,)

def back_keep(v):
    return (v, None)

def back_low(kept, grad):
    return (low(grad),)
low.defvjp(low_keep, low_pass)
low_back.defvjp(back_keep, back_low)
norm_eps = 1e-05
beta_one = 0.9
beta_two = 0.98
adam_eps = 1e-06
adam_step = 10.0
masked_score = -1e+30

def highest(form, left, right):
    return jnp.einsum(form, left, right, precision=lax.Precision.HIGHEST)

def layer_norm(value, gain, shift):
    center = value - lax.optimization_barrier(jnp.mean(value, axis=-1, keepdims=True))
    spread = lax.optimization_barrier(jnp.mean(center * center, axis=-1, keepdims=True))
    return center * lax.rsqrt(spread + norm_eps) * gain + shift

def layer(params, word_in, rows_in, segs_in, places_in):
    proj, pos_tab, query_w, query_b, key_w, key_b, value_w, value_b, out_w, out_b, gains, shifts, up_w, up_b, down_w, down_b = params
    pick_pos = (places_in[..., None] == jnp.arange(WORDS)[None, None, :]).astype(jnp.float32)
    ent_emb = low_back(highest('gek,kd->ged', low(rows_in), proj))
    ent_hidden = ent_emb + highest('gew,wd->ged', pick_pos, pos_tab)
    hidden = jnp.concatenate([word_in, ent_hidden], axis=1)
    flat_low = low(hidden)
    word_low = flat_low[:, :WORDS]
    ent_low = flat_low[:, WORDS:]

    def make_query(part_low, which_q):
        return low(low_back(highest('gtd,de->gte', part_low, query_w[which_q])) + query_b[which_q])
    to_words = jnp.concatenate([make_query(word_low, 0), make_query(ent_low, 2)], axis=1)
    to_ents = jnp.concatenate([make_query(word_low, 1), make_query(ent_low, 3)], axis=1)
    key_low = low(low_back(highest('gtd,de->gte', flat_low, key_w)) + key_b)
    value_low = low(low_back(highest('gtd,de->gte', flat_low, value_w)) + value_b)
    groups = hidden.shape[0]
    tok_count = hidden.shape[1]

    def to_heads(tensor):
        return tensor.reshape(groups, tok_count, HEADS, HEAD)
    heads_key = to_heads(key_low)
    word_raw = highest('gqhc,gkhc->ghqk', to_heads(to_words), heads_key[:, :WORDS])
    ent_raw = highest('gqhc,gkhc->ghqk', to_heads(to_ents), heads_key[:, WORDS:])
    scores = low_back(jnp.concatenate([word_raw, ent_raw], axis=-1) * (1.0 / math.sqrt(HEAD)))
    token_seg = jnp.concatenate([segs_in, jnp.take_along_axis(segs_in, places_in, axis=1)], axis=1)
    same_doc = token_seg[:, :, None] == token_seg[:, None, :]
    scores = jnp.where(same_doc[:, None], scores, masked_score)
    attn_prob = jax.nn.softmax(scores, axis=-1)
    mixed_heads = highest('ghqk,gkhc->gqhc', low(attn_prob), to_heads(value_low))
    mixed_heads = low(low_back(mixed_heads.reshape(groups, tok_count, D)))
    attn_out = low_back(highest('gtd,de->gte', mixed_heads, out_w)) + out_b
    normed = layer_norm(hidden + attn_out, gains[0], shifts[0])
    up_sum = low_back(highest('gtd,df->gtf', low(normed), up_w)) + up_b
    activated = jax.nn.gelu(up_sum, approximate=False)
    down_sum = low_back(highest('gtf,fd->gtd', low(activated), down_w)) + down_b
    return layer_norm(normed + down_sum, gains[1], shifts[1])

def reference(word_states, segments, entity_ids, entity_pos, ent_table, first_moment, second_moment, ent_proj, pos_table, query_weight, query_bias, key_weight, key_bias, value_weight, value_bias, out_weight, out_bias, norm_gain, norm_shift, up_weight, up_bias, down_weight, down_bias, word_cot, ent_cot):
    params = tuple((weight_arr.astype(jnp.float32) for weight_arr in (ent_proj, pos_table, query_weight, query_bias, key_weight, key_bias, value_weight, value_bias, out_weight, out_bias, norm_gain, norm_shift, up_weight, up_bias, down_weight, down_bias)))
    group_count = SEQS // SEQ_DEV

    def regroup(array):
        return array.reshape((group_count, SEQ_DEV) + array.shape[1:])
    rows_all = jnp.take(ent_table, entity_ids, axis=0)
    inputs = (regroup(word_states.astype(jnp.float32)), regroup(rows_all), regroup(segments), regroup(entity_pos), regroup(word_cot.astype(jnp.float32)), regroup(ent_cot.astype(jnp.float32)))
    zero_grads = jax.tree.map(jnp.zeros_like, params)

    def group_step(totals, batch_in):
        word_in, rows_in, segs_in, places_in, cot_words, cot_ents = batch_in

        def run_layer(param_set, word_arg, rows_arg):
            return layer(param_set, word_arg, rows_arg, segs_in, places_in)
        result, pullback = jax.vjp(run_layer, params, word_in, rows_in)
        grads, words_grad, rows_grad = pullback(jnp.concatenate([cot_words, cot_ents], axis=1))
        totals = jax.tree.map(jnp.add, totals, grads)
        return (totals, (result[:, :WORDS].astype(jnp.bfloat16), result[:, WORDS:].astype(jnp.bfloat16), words_grad, rows_grad))
    totals, (word_out, ent_out, word_grad, rows_grad) = lax.scan(group_step, zero_grads, inputs)
    word_out = word_out.reshape(SEQS, WORDS, D)
    ent_out = ent_out.reshape(SEQS, ENTS, D)
    word_grad = word_grad.reshape(SEQS, WORDS, D)
    flat_ids = entity_ids.reshape(-1).astype(jnp.int32)
    table_grad = jnp.zeros((ENT_ROWS, EDIM), jnp.float32).at[flat_ids].add(rows_grad.reshape(SEQS * ENTS, EDIM))
    touched = (jnp.zeros((ENT_ROWS,), jnp.int32).at[flat_ids].add(1) > 0)[:, None]
    mean_new = beta_one * first_moment + (1.0 - beta_one) * table_grad
    square_new = beta_two * second_moment + (1.0 - beta_two) * table_grad * table_grad
    direction = mean_new / (1.0 - beta_one ** adam_step) / (jnp.sqrt(square_new / (1.0 - beta_two ** adam_step)) + adam_eps)
    table_update = jnp.where(touched, direction, 0.0)
    new_second = jnp.where(touched, square_new, second_moment)
    return (word_out, ent_out, word_grad, totals[0], totals[1], totals[2], totals[3], totals[4], totals[5], totals[6], totals[7], totals[8], totals[9], totals[10], totals[11], totals[12], totals[13], totals[14], totals[15], table_grad, table_update, new_second)
```

```python
import functools
import math

import jax
import jax.numpy as jnp
from jax import lax
from jax.experimental import pallas as pl
from jax.experimental.pallas import tpu as pltpu
from jax.sharding import PartitionSpec as P

HEADS = 12
HEAD = 64


norm_eps = 1e-05
beta_one = 0.9
beta_two = 0.98
adam_eps = 1e-06
adam_step = 10.0
masked_score = -1e30

MESH = pl.DeviceIdType.MESH
CHUNKS = 8


def chunk_plan(rows):
    units = rows // 64
    count = min(CHUNKS, units)
    plan, base = [], 0
    for i in range(count):
        size = 64 * ((units * (i + 1)) // count - (units * i) // count)
        plan.append((base, size, i % 2 == 0))
        base += size
    return plan


def add_rows(total, parts, leading, rows):
    step = 16
    for candidate in (64, 48, 32):
        if rows % candidate == 0:
            step = candidate
            break

    def block(i, _):
        lead, row = i // (rows // step), pl.multiple_of((i % (rows // step)) * step, 16)
        where = (lead, pl.ds(row, step))
        value = total[where].astype(jnp.float32)
        for part in parts:
            value = value + part[where].astype(jnp.float32)
        total[where] = value.astype(total.dtype)
        return 0

    lax.fori_loop(0, leading * (rows // step), block, 0)


def reduce_kernel(plan, nz, grads, out, *scratch):
    count = len(plan)
    held, from_core, from_y, from_x, from_z = (scratch[i * count : (i + 1) * count] for i in range(5))
    reduced, local_sem, send_sem, recv_sem = scratch[5 * count :]
    dp, seq = lax.axis_index("dp"), lax.axis_index("seq")
    z, x = dp // 2, dp % 2
    y, core = seq // 2, seq % 2
    other_core = (dp, y * 2 + 1 - core)
    other_y = (dp, (1 - y) * 2 + core)
    other_x = (z * 2 + 1 - x, seq)
    ahead = [(((z + k) % nz) * 2 + x, seq) for k in range(1, nz)]
    partners = [other_core, other_y, other_x] + ahead
    barrier = pltpu.get_barrier_semaphore()
    for partner in partners:
        pl.semaphore_signal(barrier, inc=1, device_id=partner, device_id_type=MESH)
    pl.semaphore_wait(barrier, len(partners))

    def remote(src, dst, sem, device):
        return pltpu.make_async_remote_copy(
            src_ref=src,
            dst_ref=dst,
            send_sem=send_sem.at[sem],
            recv_sem=recv_sem.at[sem],
            device_id=device,
            device_id_type=MESH,
        )

    def sem(chunk, stage):
        return chunk * (4 + nz) + stage

    def rows_at(start, size):
        return pl.ds(pl.multiple_of(start, 16), size)

    open_copies = []
    steps = {}

    def send(src, dst, which, device):
        copy = remote(src, dst, which, device)
        copy.start()
        open_copies.append(copy)
        return copy

    def start_core(k):
        base, size, _ = plan[k]
        half = size // 2
        steps[k, "core"] = send(
            grads.at[:, :, rows_at(base + (1 - core) * half, half)], from_core[k], sem(k, 0), other_core
        )
        own = pltpu.make_async_copy(
            grads.at[:, :, rows_at(base + core * half, half)], held[k], local_sem.at[k]
        )
        own.start()
        steps[k, "own"] = own

    def flat(ref, *lead):
        return ref.at[lead]

    def after_core(k):
        base, size, y_first = plan[k]
        half, part = size // 2, size // 4
        steps[k, "own"].wait()
        steps[k, "core"].wait_recv()
        for i in range(2):
            add_rows(held[k].at[:, i], [from_core[k].at[:, i]], nz, half)
        if y_first:
            steps[k, "y"] = send(
                held[k].at[:, :, rows_at((1 - y) * part, part)], from_y[k], sem(k, 1), other_y
            )
        else:
            steps[k, "x"] = send(held[k].at[:, 1 - x], from_x[k], sem(k, 2), other_x)

    def own_rows(k):
        base, size, y_first = plan[k]
        part = size // 4
        return (rows_at(y * part, part), part) if y_first else (pl.ds(0, size // 2), size // 2)

    def after_y(k):
        base, size, y_first = plan[k]
        if not y_first:
            return
        where, part = own_rows(k)
        steps[k, "y"].wait_recv()
        for i in range(2):
            add_rows(held[k].at[:, i, where], [from_y[k].at[:, i]], nz, part)
        steps[k, "x"] = send(held[k].at[:, 1 - x, where], from_x[k], sem(k, 2), other_x)

    def after_x(k):
        where, part = own_rows(k)
        steps[k, "x"].wait_recv()
        add_rows(held[k].at[:, x, where], [from_x[k]], nz, part)
        for j, device in enumerate(ahead):
            steps[k, "z", j] = send(
                held[k].at[(z + 1 + j) % nz, x, where], from_z[k].at[j], sem(k, 5 + j), device
            )

    def after_z(k):
        base, size, y_first = plan[k]
        half = size // 2
        where, part = own_rows(k)
        for j in range(nz - 1):
            steps[k, "z", j].wait_recv()
        mine = held[k].at[z, x, where]
        target = rows_at(base + core * half + (y * part if y_first else 0), part)
        step = 16

        def block(i, _):
            row = pl.ds(pl.multiple_of(i * step, 16), step)
            value = mine[row].astype(jnp.float32)
            for j in range(nz - 1):
                value = value + from_z[k][j, row].astype(jnp.float32)
            mine[row] = value.astype(jnp.bfloat16)
            return 0

        lax.fori_loop(0, part // step, block, 0)
        if y_first:
            own = pltpu.make_async_copy(mine, reduced.at[target], local_sem.at[count + k])
            own.start()
            steps[k, "keep"] = own
            steps[k, "y2"] = send(mine, reduced.at[target], sem(k, 3), other_y)
        else:
            steps[k, "y2"] = send(mine, from_y[k], sem(k, 3), other_y)

    def after_y_again(k):
        base, size, y_first = plan[k]
        half = size // 2
        mine = rows_at(base + core * half, half)
        steps[k, "y2"].wait_recv()
        if y_first:
            steps[k, "keep"].wait()
        else:
            own = held[k].at[z, x]
            step = 16

            def block(i, _):
                row = pl.ds(pl.multiple_of(i * step, 16), step)
                target = pl.ds(pl.multiple_of(base + core * half + i * step, 16), step)
                value = own[row].astype(jnp.float32) + from_y[k][row].astype(jnp.float32)
                reduced[target] = value.astype(jnp.bfloat16)
                return 0

            lax.fori_loop(0, half // step, block, 0)
        steps[k, "core2"] = send(reduced.at[mine], reduced.at[mine], sem(k, 4), other_core)

    def after_core_again(k):
        steps[k, "core2"].wait_recv()

    for k in range(count):
        start_core(k)
    stages = [after_core, after_y, after_x, after_z, after_y_again, after_core_again]
    for tick in range(count + len(stages) - 1):
        for s in reversed(range(len(stages))):
            if 0 <= tick - s < count:
                stages[s](tick - s)
    for copy in open_copies:
        copy.wait_send()
    final = pltpu.make_async_copy(reduced, out, local_sem.at[2 * count])
    final.start()
    final.wait()


def reduce_grads(grads):
    n_dp, rows, columns = grads.shape
    nz = n_dp // 2
    plan = chunk_plan(rows)
    count = len(plan)
    low = jnp.bfloat16
    halves = [size // 2 for _, size, _ in plan]
    scratch = (
        [pltpu.VMEM((nz, 2, half, columns), low) for half in halves]
        + [pltpu.VMEM((nz, 2, half, columns), low) for half in halves]
        + [
            pltpu.VMEM((nz, 2, size // 4, columns) if y_first else (size // 2, columns), low)
            for _, size, y_first in plan
        ]
        + [
            pltpu.VMEM((nz, size // 4 if y_first else size // 2, columns), low)
            for _, size, y_first in plan
        ]
        + [
            pltpu.VMEM((nz - 1, size // 4 if y_first else size // 2, columns), low)
            for _, size, y_first in plan
        ]
        + [
            pltpu.VMEM((rows, columns), low),
            pltpu.SemaphoreType.DMA((2 * count + 1,)),
            pltpu.SemaphoreType.DMA((count * (4 + nz),)),
            pltpu.SemaphoreType.DMA((count * (4 + nz),)),
        ]
    )
    return pl.pallas_call(
        functools.partial(reduce_kernel, plan, nz),
        out_shape=jax.ShapeDtypeStruct((rows, columns), low),
        in_specs=[pl.BlockSpec(memory_space=pl.ANY)],
        out_specs=pl.BlockSpec(memory_space=pl.ANY),
        scratch_shapes=scratch,
        compiler_params=pltpu.CompilerParams(
            collective_id=1, has_side_effects=True, vmem_limit_bytes=56 * 1024 * 1024
        ),
        name="reduce_grads",
    )(grads.reshape(nz, 2, rows, columns))


def from_behind(block, axis, distance):
    devices = range(lax.axis_size(axis))
    route = [((i - distance) % len(devices), i) for i in devices]
    return lax.ppermute(block, axis, route)


def product(form, left, right):
    return jnp.einsum(form, left, right, preferred_element_type=jnp.float32)


def norm_forward(value, gain, shift):
    center = value - jnp.mean(value, axis=-1, keepdims=True)
    inverse = lax.rsqrt(jnp.mean(center * center, axis=-1, keepdims=True) + norm_eps)
    normal = center * inverse
    return (normal * gain + shift, normal, inverse)


def norm_backward(grad_out, normal, inverse, gain):
    scaled = grad_out * gain
    grad_in = inverse * (
        scaled
        - jnp.mean(scaled, axis=-1, keepdims=True)
        - normal * jnp.mean(scaled * normal, axis=-1, keepdims=True)
    )
    return (grad_in, jnp.sum(grad_out * normal, axis=(0, 1)), jnp.sum(grad_out, axis=(0, 1)))


def gelu_slope(value):
    return 0.5 * (1.0 + lax.erf(value / math.sqrt(2.0))) + value * jnp.exp(
        -0.5 * value * value
    ) / math.sqrt(2.0 * math.pi)


def on_device(
    word_states,
    segments,
    entity_ids,
    entity_pos,
    ent_table,
    first_moment,
    second_moment,
    ent_proj,
    pos_table,
    query_weight,
    query_bias,
    key_weight,
    key_bias,
    value_weight,
    value_bias,
    out_weight,
    out_bias,
    norm_gain,
    norm_shift,
    up_weight,
    up_bias,
    down_weight,
    down_bias,
    word_cot,
    ent_cot,
):
    cycle_size = lax.axis_size("seq")
    cycle_pos = lax.axis_index("seq")
    seqs_here, word_here, width = word_states.shape
    ent_here = ent_cot.shape[1]
    tok_here = word_here + ent_here
    all_words = segments.shape[1]
    score_scale = 1.0 / math.sqrt(HEAD)
    ent_ids_here = lax.dynamic_slice_in_dim(entity_ids, cycle_pos * ent_here, ent_here, 1)
    ent_pos_here = lax.dynamic_slice_in_dim(entity_pos, cycle_pos * ent_here, ent_here, 1)
    requests = ent_ids_here.reshape(-1)
    asked = lax.all_gather(requests, ("dp", "seq"), axis=0, tiled=True)
    rows_dev = ent_table.shape[0]
    local_row = asked - lax.axis_index(("dp", "seq")) * rows_dev
    owned = (local_row >= 0) & (local_row < rows_dev)
    safe_row = jnp.clip(local_row, 0, rows_dev - 1)
    answers = jnp.where(owned[:, None], jnp.take(ent_table, safe_row, axis=0), 0.0).astype(
        jnp.bfloat16
    )
    returned = lax.all_to_all(answers, ("dp", "seq"), split_axis=0, concat_axis=0, tiled=True)
    sources = returned.shape[0] // requests.shape[0]
    ent_rows = jnp.sum(returned.reshape(sources, requests.shape[0], -1), axis=0)
    ent_rows = ent_rows.reshape(seqs_here, ent_here, -1)
    pick_pos = (ent_pos_here[..., None] == jnp.arange(all_words)[None, None, :]).astype(
        jnp.bfloat16
    )
    ent_hidden = product("sek,kd->sed", ent_rows, ent_proj) + product(
        "sew,wd->sed", pick_pos, pos_table
    )
    hidden = jnp.concatenate([word_states.astype(jnp.float32), ent_hidden], axis=1)
    hidden_low = hidden.astype(jnp.bfloat16)
    word_low = hidden_low[:, :word_here]
    ent_low = hidden_low[:, word_here:]

    def make_query(part_low, which_q):
        return (
            product("std,de->ste", part_low, query_weight[which_q])
            + query_bias[which_q].astype(jnp.float32)
        ).astype(jnp.bfloat16)

    to_words = jnp.concatenate([make_query(word_low, 0), make_query(ent_low, 2)], axis=1)
    to_ents = jnp.concatenate([make_query(word_low, 1), make_query(ent_low, 3)], axis=1)
    key_low = (
        product("std,de->ste", hidden_low, key_weight) + key_bias.astype(jnp.float32)
    ).astype(jnp.bfloat16)
    value_low = (
        product("std,de->ste", hidden_low, value_weight) + value_bias.astype(jnp.float32)
    ).astype(jnp.bfloat16)

    def to_heads(tensor):
        return tensor.reshape(seqs_here, tok_here, HEADS, HEAD)

    query_words = to_heads(to_words)
    query_ents = to_heads(to_ents)

    def token_segments(source):
        word_seg = lax.dynamic_slice_in_dim(segments, source * word_here, word_here, 1)
        ent_place = lax.dynamic_slice_in_dim(entity_pos, source * ent_here, ent_here, 1)
        return jnp.concatenate([word_seg, jnp.take_along_axis(segments, ent_place, axis=1)], axis=1)

    query_seg = token_segments(cycle_pos)

    def block_scores(block_keys, source):
        heads_key = to_heads(block_keys)
        word_part = product("sqhc,skhc->shqk", query_words, heads_key[:, :word_here])
        ent_part = product("sqhc,skhc->shqk", query_ents, heads_key[:, word_here:])
        same_doc = query_seg[:, :, None] == token_segments(source)[:, None, :]
        scaled_raw = jnp.concatenate([word_part, ent_part], axis=-1) * score_scale
        return (jnp.where(same_doc[:, None], scaled_raw, masked_score), same_doc)

    run_max = jnp.full((seqs_here, HEADS, tok_here), masked_score, jnp.float32)
    run_sum = jnp.zeros((seqs_here, HEADS, tok_here), jnp.float32)
    run_acc = jnp.zeros((seqs_here, tok_here, HEADS, HEAD), jnp.float32)
    block_key, block_value = (key_low, value_low)
    for cycle_step in range(cycle_size):
        source = (cycle_pos - cycle_step) % cycle_size
        scores, same_doc = block_scores(block_key, source)
        new_max = jnp.maximum(run_max, jnp.max(scores, axis=-1))
        weights = jnp.where(same_doc[:, None], jnp.exp(scores - new_max[..., None]), 0.0)
        factor = jnp.exp(run_max - new_max)
        run_sum = run_sum * factor + jnp.sum(weights, axis=-1)
        run_acc = run_acc * jnp.transpose(factor, (0, 2, 1))[..., None] + product(
            "shqk,skhc->sqhc", weights.astype(jnp.bfloat16), to_heads(block_value)
        )
        run_max = new_max
        if cycle_step + 1 < cycle_size:
            block_key, block_value = from_behind((block_key, block_value), "seq", 1)
    mixed = (run_acc / jnp.transpose(run_sum, (0, 2, 1))[..., None]).reshape(
        seqs_here, tok_here, width
    )
    mixed_low = mixed.astype(jnp.bfloat16)
    log_total = run_max + jnp.log(run_sum)
    attn_out = product("std,de->ste", mixed_low, out_weight) + out_bias.astype(jnp.float32)
    normed, normal_one, inverse_one = norm_forward(
        hidden + attn_out, norm_gain[0].astype(jnp.float32), norm_shift[0].astype(jnp.float32)
    )
    normed_low = normed.astype(jnp.bfloat16)
    up_sum = product("std,df->stf", normed_low, up_weight) + up_bias.astype(jnp.float32)
    activated_low = jax.nn.gelu(up_sum, approximate=False).astype(jnp.bfloat16)
    down_sum = product("stf,fd->std", activated_low, down_weight) + down_bias.astype(jnp.float32)
    output, normal_two, inverse_two = norm_forward(
        normed + down_sum, norm_gain[1].astype(jnp.float32), norm_shift[1].astype(jnp.float32)
    )
    word_out = output[:, :word_here].astype(jnp.bfloat16)
    ent_out = output[:, word_here:].astype(jnp.bfloat16)
    cotangent = jnp.concatenate([word_cot, ent_cot], axis=1).astype(jnp.float32)
    grad_two, gain_two, shift_two = norm_backward(
        cotangent, normal_two, inverse_two, norm_gain[1].astype(jnp.float32)
    )
    grad_down_low = grad_two.astype(jnp.bfloat16)
    down_grad = product("stf,std->fd", activated_low, grad_down_low)
    down_bias_grad = jnp.sum(grad_two, axis=(0, 1))
    grad_up = product("std,fd->stf", grad_down_low, down_weight) * gelu_slope(up_sum)
    up_bias_grad = jnp.sum(grad_up, axis=(0, 1))
    grad_up_low = grad_up.astype(jnp.bfloat16)
    up_grads = [
        product("std,stf->df", normed_low, grad_up_low[..., i : i + width])
        for i in range(0, grad_up_low.shape[-1], width)
    ]
    grad_normed = grad_two + product("stf,df->std", grad_up_low, up_weight)
    grad_one, gain_one, shift_one = norm_backward(
        grad_normed, normal_one, inverse_one, norm_gain[0].astype(jnp.float32)
    )
    out_bias_grad = jnp.sum(grad_one, axis=(0, 1))
    grad_attn_low = grad_one.astype(jnp.bfloat16)
    out_grad = product("std,ste->de", mixed_low, grad_attn_low)
    grad_mixed_low = product("ste,de->std", grad_attn_low, out_weight).astype(jnp.bfloat16)
    grad_heads_low = to_heads(grad_mixed_low)
    delta = jnp.transpose(
        jnp.sum(grad_heads_low.astype(jnp.float32) * to_heads(mixed), axis=-1), (0, 2, 1)
    )
    grad_q_words = jnp.zeros((seqs_here, tok_here, HEADS, HEAD), jnp.float32)
    grad_q_ents = jnp.zeros((seqs_here, tok_here, HEADS, HEAD), jnp.float32)
    moving_key = jnp.zeros((seqs_here, tok_here, HEADS, HEAD), jnp.float32)
    moving_value = jnp.zeros((seqs_here, tok_here, HEADS, HEAD), jnp.float32)
    block_key, block_value = (key_low, value_low)
    for cycle_step in range(cycle_size):
        source = (cycle_pos - cycle_step) % cycle_size
        scores, same_doc = block_scores(block_key, source)
        weights = jnp.where(same_doc[:, None], jnp.exp(scores - log_total[..., None]), 0.0)
        heads_key = to_heads(block_key)
        heads_value = to_heads(block_value)
        moving_value = moving_value + product(
            "shqk,sqhc->skhc", weights.astype(jnp.bfloat16), grad_heads_low
        )
        grad_weights = product("sqhc,skhc->shqk", grad_heads_low, heads_value)
        grad_scores = (weights * (grad_weights - delta[..., None])).astype(jnp.bfloat16)
        word_scores = grad_scores[..., :word_here]
        ent_scores = grad_scores[..., word_here:]
        grad_q_words = grad_q_words + score_scale * product(
            "shqk,skhc->sqhc", word_scores, heads_key[:, :word_here]
        )
        grad_q_ents = grad_q_ents + score_scale * product(
            "shqk,skhc->sqhc", ent_scores, heads_key[:, word_here:]
        )
        key_step = jnp.concatenate(
            [
                product("shqk,sqhc->skhc", word_scores, query_words),
                product("shqk,sqhc->skhc", ent_scores, query_ents),
            ],
            axis=1,
        )
        moving_key = moving_key + score_scale * key_step
        moving_key, moving_value = (
            from_behind(moving_key.astype(jnp.bfloat16), "seq", 1).astype(moving_key.dtype),
            from_behind(moving_value.astype(jnp.bfloat16), "seq", 1).astype(moving_value.dtype),
        )
        if cycle_step + 1 < cycle_size:
            block_key, block_value = from_behind((block_key, block_value), "seq", 1)
    grad_value = moving_value.reshape(seqs_here, tok_here, width)
    value_bias_grad = jnp.sum(grad_value, axis=(0, 1))
    grad_value_low = grad_value.astype(jnp.bfloat16)
    grad_key = moving_key.reshape(seqs_here, tok_here, width)
    key_bias_grad = jnp.sum(grad_key, axis=(0, 1))
    grad_key_low = grad_key.astype(jnp.bfloat16)
    words_query = grad_q_words.reshape(seqs_here, tok_here, width)
    ents_query = grad_q_ents.reshape(seqs_here, tok_here, width)
    query_bias_grad = jnp.stack(
        [
            jnp.sum(words_query[:, :word_here], axis=(0, 1)),
            jnp.sum(ents_query[:, :word_here], axis=(0, 1)),
            jnp.sum(words_query[:, word_here:], axis=(0, 1)),
            jnp.sum(ents_query[:, word_here:], axis=(0, 1)),
        ]
    )
    words_query_low = words_query.astype(jnp.bfloat16)
    ents_query_low = ents_query.astype(jnp.bfloat16)
    query_grad = jnp.stack(
        [
            product("std,ste->de", word_low, words_query_low[:, :word_here]),
            product("std,ste->de", word_low, ents_query_low[:, :word_here]),
            product("std,ste->de", ent_low, words_query_low[:, word_here:]),
            product("std,ste->de", ent_low, ents_query_low[:, word_here:]),
        ]
    )
    key_grad = product("std,ste->de", hidden_low, grad_key_low)
    value_grad = product("std,ste->de", hidden_low, grad_value_low)
    query_back = jnp.concatenate(
        [
            product("ste,de->std", words_query_low[:, :word_here], query_weight[0])
            + product("ste,de->std", ents_query_low[:, :word_here], query_weight[1]),
            product("ste,de->std", words_query_low[:, word_here:], query_weight[2])
            + product("ste,de->std", ents_query_low[:, word_here:], query_weight[3]),
        ],
        axis=1,
    )
    grad_hidden = (
        grad_one
        + query_back
        + product("ste,de->std", grad_key_low, key_weight)
        + product("ste,de->std", grad_value_low, value_weight)
    )
    word_grad = grad_hidden[:, :word_here]
    ent_grad = grad_hidden[:, word_here:]
    pos_grad = jnp.einsum(
        "sew,sed->wd", pick_pos.astype(jnp.float32), ent_grad, precision=lax.Precision.HIGHEST
    )
    ent_grad_low = ent_grad.astype(jnp.bfloat16)
    proj_grad = product("sek,sed->kd", ent_rows, ent_grad_low)
    row_grad = product("sed,kd->sek", ent_grad_low, ent_proj).reshape(requests.shape[0], -1)
    gathered = lax.all_gather(
        row_grad.astype(jnp.bfloat16), ("dp", "seq"), axis=0, tiled=True
    ).astype(row_grad.dtype)
    drop_row = jnp.where(owned, local_row, rows_dev)
    table_grad = jnp.zeros_like(ent_table).at[drop_row].add(gathered, mode="drop")
    hits = jnp.zeros((rows_dev,), jnp.int32).at[drop_row].add(1, mode="drop")
    touched = (hits > 0)[:, None]
    n_dp = lax.axis_size("dp")

    def slabs(grad):
        return grad.astype(jnp.bfloat16).reshape(n_dp, -1, width)

    biases = [query_bias_grad[i] for i in range(4)] + [
        key_bias_grad,
        value_bias_grad,
        out_bias_grad,
        gain_one,
        gain_two,
        shift_one,
        shift_two,
    ]
    biases += [up_bias_grad, down_bias_grad]
    bias_slabs = jnp.concatenate(
        [bias.astype(jnp.bfloat16).reshape(n_dp, -1) for bias in biases], axis=1
    )
    bias_rows = -(-bias_slabs.shape[1] // width)
    bias_slabs = jnp.pad(bias_slabs, ((0, 0), (0, bias_rows * width - bias_slabs.shape[1])))
    sections = [slabs(proj_grad), slabs(pos_grad)]
    sections += [slabs(query_grad[i]) for i in range(4)]
    sections += [slabs(key_grad), slabs(value_grad), slabs(out_grad)]
    sections += [slabs(part) for part in up_grads]
    sections += [slabs(down_grad), bias_slabs.reshape(n_dp, bias_rows, width)]
    starts = [0]
    for section in sections:
        starts.append(starts[-1] + section.shape[1])
    spare = -starts[-1] % 64
    sections.append(jnp.zeros((n_dp, spare, width), jnp.bfloat16))
    reduced = reduce_grads(jnp.concatenate(sections, axis=1)).astype(jnp.float32)
    parts = [reduced[starts[i] : starts[i + 1]] for i in range(len(starts) - 1)]
    bias_flat = parts[14].reshape(-1)
    bias_parts, place = [], 0
    for bias in biases:
        size = bias.shape[0] // n_dp
        bias_parts.append(bias_flat[place : place + size])
        place += size
    shares = (
        parts[0],
        parts[1],
        jnp.stack(parts[2:6]),
        jnp.stack(bias_parts[:4]),
        parts[6],
        bias_parts[4],
        parts[7],
        bias_parts[5],
        parts[8],
        bias_parts[6],
        jnp.stack(bias_parts[7:9]),
        jnp.stack(bias_parts[9:11]),
        jnp.concatenate(parts[9:13], axis=1),
        bias_parts[11],
        parts[13],
        bias_parts[12],
    )
    mean_new = beta_one * first_moment + (1.0 - beta_one) * table_grad
    square_new = beta_two * second_moment + (1.0 - beta_two) * table_grad * table_grad
    direction = (
        mean_new
        / (1.0 - beta_one**adam_step)
        / (jnp.sqrt(square_new / (1.0 - beta_two**adam_step)) + adam_eps)
    )
    table_update = jnp.where(touched, direction, 0.0)
    new_second = jnp.where(touched, square_new, second_moment)
    return (
        word_out,
        ent_out,
        word_grad,
        shares[0],
        shares[1],
        shares[2],
        shares[3],
        shares[4],
        shares[5],
        shares[6],
        shares[7],
        shares[8],
        shares[9],
        shares[10],
        shares[11],
        shares[12],
        shares[13],
        shares[14],
        shares[15],
        table_grad,
        table_update,
        new_second,
    )


def solution(mesh):
    return jax.shard_map(
        on_device,
        mesh=mesh,
        in_specs=(
            P("dp", "seq", None),
            P("dp", None),
            P("dp", None),
            P("dp", None),
            P(("dp", "seq"), None),
            P(("dp", "seq"), None),
            P(("dp", "seq"), None),
            P(),
            P(),
            P(),
            P(),
            P(),
            P(),
            P(),
            P(),
            P(),
            P(),
            P(),
            P(),
            P(),
            P(),
            P(),
            P(),
            P("dp", "seq", None),
            P("dp", "seq", None),
        ),
        out_specs=(
            P("dp", "seq", None),
            P("dp", "seq", None),
            P("dp", "seq", None),
            P("dp", None),
            P("dp", None),
            P(None, "dp", None),
            P(None, "dp"),
            P("dp", None),
            P("dp"),
            P("dp", None),
            P("dp"),
            P("dp", None),
            P("dp"),
            P(None, "dp"),
            P(None, "dp"),
            P("dp", None),
            P("dp"),
            P("dp", None),
            P("dp"),
            P(("dp", "seq"), None),
            P(("dp", "seq"), None),
            P(("dp", "seq"), None),
        ),
        check_vma=False,
    )
```

```python
import functools
import math

import jax
import jax.numpy as jnp
from jax import lax
from jax.experimental import pallas as pl
from jax.experimental.pallas import tpu as pltpu
from jax.sharding import PartitionSpec as P

HEADS = 12
HEAD = 64
LANES = 128
MESH = pl.DeviceIdType.MESH
LOW = jnp.bfloat16
F32 = jnp.float32
VMEM_BYTES = 58 * 1024 * 1024

norm_eps = 1e-05
beta_one = 0.9
beta_two = 0.98
adam_eps = 1e-06
adam_step = 10.0
masked_score = -1e30


def dot(left, right):
    return jnp.dot(left, right, preferred_element_type=F32)


def dot_rows(left, right):
    return lax.dot_general(left, right, (((1,), (1,)), ((), ())), preferred_element_type=F32)


def dot_columns(left, right):
    return lax.dot_general(left, right, (((0,), (0,)), ((), ())), preferred_element_type=F32)


def span(start, size, unit):
    if isinstance(start, int):
        return pl.ds(start, size)
    return pl.ds(pl.multiple_of(start, unit), size)


def padded(rows):
    return -(-rows // 16) * 16


def loop(count, body, carry=0):
    return lax.fori_loop(0, count, body, carry)


class Place:
    def __init__(self, nz):
        self.dp, self.seq = lax.axis_index("dp"), lax.axis_index("seq")
        self.z, self.x = self.dp // 2, self.dp % 2
        self.y, self.core = self.seq // 2, self.seq % 2
        self.nz = nz
        self.other_core = (self.dp, self.y * 2 + 1 - self.core)
        self.other_y = (self.dp, (1 - self.y) * 2 + self.core)
        self.diagonal = (self.dp, (1 - self.y) * 2 + 1 - self.core)
        self.other_x = (self.z * 2 + 1 - self.x, self.seq)
        self.ahead = [(((self.z + k) % nz) * 2 + self.x, self.seq) for k in range(1, nz)]

    def z_ahead(self, k):
        return (self.z + k) % self.nz


def meet(partners):
    barrier = pltpu.get_barrier_semaphore()
    for partner in partners:
        pl.semaphore_signal(barrier, inc=1, device_id=partner, device_id_type=MESH)
    pl.semaphore_wait(barrier, len(partners))


class Copies:
    def __init__(self, send_sem, recv_sem, local_sem):
        self.send_sem, self.recv_sem, self.local_sem = send_sem, recv_sem, local_sem
        self.count, self.local_count = 0, 0
        self.sent = []

    def make(self, src, dst, device):
        copy = pltpu.make_async_remote_copy(
            src_ref=src,
            dst_ref=dst,
            send_sem=self.send_sem.at[self.count],
            recv_sem=self.recv_sem.at[self.count],
            device_id=device,
            device_id_type=MESH,
        )
        self.count += 1
        return copy

    def send(self, src, dst, device):
        copy = self.make(src, dst, device)
        copy.start()
        self.sent.append(copy)
        return copy

    def local(self, src, dst):
        copy = pltpu.make_async_copy(src, dst, self.local_sem.at[self.local_count])
        self.local_count += 1
        copy.start()
        return copy

    def finish(self):
        for copy in self.sent:
            copy.wait_send()


def copy_semaphores(remote, local):
    return [
        pltpu.SemaphoreType.DMA((remote,)),
        pltpu.SemaphoreType.DMA((remote,)),
        pltpu.SemaphoreType.DMA((local,)),
    ]


ANY = pl.BlockSpec(memory_space=pl.ANY)
IN_VMEM = pl.BlockSpec(memory_space=pltpu.VMEM)


def call(kernel, outs, in_specs, out_specs, scratch, name, collective_id=None):
    params = {"vmem_limit_bytes": VMEM_BYTES}
    if collective_id is not None:
        params.update(collective_id=collective_id, has_side_effects=True)
    return pl.pallas_call(
        kernel,
        out_shape=[jax.ShapeDtypeStruct(shape, dtype) for shape, dtype in outs],
        in_specs=in_specs,
        out_specs=out_specs,
        scratch_shapes=scratch,
        compiler_params=pltpu.CompilerParams(**params),
        name=name,
    )


def fetch_kernel(nz, words, word_cot, ent_cot, ids, table, all_words, word_cots, ent_cots, all_ids, rows_out, *scratch):
    table_full, table_low, picked, answers, held, from_core, from_x, from_z, from_y, ids_here = scratch[:10]
    copies = Copies(*scratch[10:])
    place = Place(nz)
    z, x, y, core = place.z, place.x, place.y, place.core
    n_dp = 2 * nz
    word_here, ent_here = words.shape[1], ent_cot.shape[1]
    ents = ids.shape[1]
    dp_others = [((place.dp + k) % n_dp, place.seq) for k in range(1, n_dp)]
    meet([place.other_core, place.other_y, place.diagonal] + dp_others)
    whole_table = copies.local(table, table_full)
    own_ids = copies.local(ids, ids_here.at[place.dp])
    id_copies = [copies.send(ids, ids_here.at[place.dp], device) for device in dp_others]
    quarter = span(place.seq * word_here, word_here, 128)
    word_copies = [
        copies.send(words.at[1 - core], all_words.at[quarter], place.diagonal),
        copies.send(words.at[core], all_words.at[quarter], place.other_y),
        copies.send(words.at[1 - core], all_words.at[quarter], place.other_core),
        copies.send(word_cot.at[1 - core], word_cots.at[span(core * word_here, word_here, 128)], place.other_core),
        copies.send(ent_cot.at[1 - core], ent_cots.at[span(core * ent_here, ent_here, 32)], place.other_core),
    ]
    local = [
        copies.local(words.at[core], all_words.at[quarter]),
        copies.local(word_cot.at[core], word_cots.at[span(core * word_here, word_here, 128)]),
        copies.local(ent_cot.at[core], ent_cots.at[span(core * ent_here, ent_here, 32)]),
    ]
    whole_table.wait()
    rows_dev = table.shape[0]

    def narrow(i, _):
        where = span(i * 128, 128, 128)
        table_low[where] = table_full[where].astype(LOW)
        return 0

    loop(rows_dev // 128, narrow)
    own_ids.wait()
    for copy in id_copies:
        copy.wait_recv()
    ids_out = copies.local(ids_here, all_ids)
    base = (place.dp * 4 + place.seq) * rows_dev
    tiles = rows_dev // LANES

    def look_up(zz, _):
        for xx in range(2):
            for s in range(2):
                asked = ids_here[zz * 2 + xx, pl.ds(s, 1), :] - base
                column = jnp.transpose(jnp.broadcast_to(asked, (ents, ents)))
                for j in range(tiles):
                    number = lax.broadcasted_iota(jnp.int32, (ents, LANES), 1) + j * LANES
                    hit = jnp.where(column == number, 1.0, 0.0).astype(LOW)
                    picked[pl.ds((xx * 2 + s) * ents, ents), pl.ds(j * LANES, LANES)] = hit
        answer = dot(picked[...], table_low[...]).astype(LOW)
        answers[zz] = answer.reshape(2, 2, ents, answer.shape[-1])
        return 0

    loop(nz, look_up)

    core_copy = copies.send(answers.at[:, :, 1 - core], from_core, place.other_core)
    core_copy.wait_recv()
    for xx in range(2):

        def add_core(zz, _):
            held[zz, xx] = answers[zz, xx, core] + from_core[zz, xx]
            return 0

        loop(nz, add_core)
    x_copy = copies.send(held.at[:, 1 - x], from_x, place.other_x)
    x_copy.wait_recv()

    def add_x(zz, _):
        held[zz, x] = held[zz, x] + from_x[zz]
        return 0

    loop(nz, add_x)
    z_copies = [
        copies.send(held.at[place.z_ahead(k + 1), x], from_z.at[k], device) for k, device in enumerate(place.ahead)
    ]
    total = held[z, x]
    for k in range(nz - 1):
        z_copies[k].wait_recv()
        total = total + from_z[k]
    from_y[0] = total
    y_copy = copies.send(from_y.at[0], from_y.at[1], place.other_y)
    y_copy.wait_recv()
    rows_out[...] = from_y[0] + from_y[1]
    for copy in word_copies:
        copy.wait_recv()
    for copy in local + [ids_out]:
        copy.wait()
    copies.finish()


def fetch(nz, words, word_cot, ent_cot, ids, table):
    _, word_here, width = words.shape
    ent_here, ents, (rows_dev, edim) = ent_cot.shape[1], ids.shape[1], table.shape
    n_dp = 2 * nz
    return call(
        functools.partial(fetch_kernel, nz),
        [
            ((4 * word_here, width), LOW),
            ((2 * word_here, width), LOW),
            ((2 * ent_here, width), LOW),
            ((n_dp, 2, ents), jnp.int32),
            ((ents, edim), LOW),
        ],
        [ANY] * 5,
        [ANY] * 4 + [IN_VMEM],
        [
            pltpu.VMEM((rows_dev, edim), F32),
            pltpu.VMEM((rows_dev, edim), LOW),
            pltpu.VMEM((4 * ents, rows_dev), LOW),
            pltpu.VMEM((nz, 2, 2, ents, edim), LOW),
            pltpu.VMEM((nz, 2, ents, edim), LOW),
            pltpu.VMEM((nz, 2, ents, edim), LOW),
            pltpu.VMEM((nz, ents, edim), LOW),
            pltpu.VMEM((nz - 1, ents, edim), LOW),
            pltpu.VMEM((2, ents, edim), LOW),
            pltpu.VMEM((n_dp, 2, ents), jnp.int32),
        ]
        + copy_semaphores(n_dp + 4 + 2 + nz + 2, 6),
        "fetch",
        1,
    )(words, word_cot, ent_cot, ids, table)


def lane_mask(rows, head):
    lane = lax.broadcasted_iota(jnp.int32, (rows, LANES), 1)
    return (lane >= head * HEAD) & (lane < (head + 1) * HEAD)


def as_column(row):
    parts = [
        jnp.transpose(jnp.broadcast_to(row[:, i : i + LANES], (LANES, LANES)))
        for i in range(0, row.shape[1], LANES)
    ]
    return jnp.concatenate(parts, axis=0) if len(parts) > 1 else parts[0]


def forward_kernel(
    words, rows, ent_pos, segments, ent_proj, pos_table, query_weight, query_bias, key_weight, key_bias, value_weight, value_bias,
    ent_hidden, hidden_low, query_words, query_ents, keys, values, probs, mixed,
    query_here, key_here, value_here, values_turned, mask, mixed_turned, local_sem,
):
    y = lax.axis_index("seq") // 2
    half = keys.shape[1]
    all_words, ents = words.shape[0], rows.shape[0]
    tokens = all_words + ents
    columns = span(y * half, half, LANES)
    weight_copies = [
        pltpu.make_async_copy(query_weight.at[:, :, columns], query_here, local_sem.at[0]),
        pltpu.make_async_copy(key_weight.at[:, columns], key_here, local_sem.at[1]),
        pltpu.make_async_copy(value_weight.at[:, columns], value_here, local_sem.at[2]),
    ]
    for copy in weight_copies:
        copy.start()
    position = as_column(ent_pos[...])
    picks = []
    for j in range(all_words // LANES):
        number = lax.broadcasted_iota(jnp.int32, (ents, LANES), 1) + j * LANES
        picks.append(jnp.where(position == number, 1.0, 0.0))
    pick = jnp.concatenate(picks, axis=1)
    word_seg = segments[...].astype(F32)
    ent_seg = jnp.sum(pick * word_seg, axis=1, keepdims=True)
    ent_hidden[...] = dot(rows[...], ent_proj[...]) + dot(pick.astype(LOW), pos_table[...])
    hidden_low[:all_words] = words[...]
    hidden_low[all_words:] = ent_hidden[...].astype(LOW)
    ent_row = jnp.transpose(jnp.broadcast_to(ent_seg, (ents, LANES)))[:1]
    seg_row = jnp.concatenate([word_seg, ent_row], axis=1)
    seg_column = jnp.concatenate([as_column(word_seg), jnp.broadcast_to(ent_seg, (ents, LANES))], axis=0)
    for j in range(tokens // LANES):
        here = slice(j * LANES, (j + 1) * LANES)
        mask[:, here] = jnp.where(seg_column == seg_row[:, here], 0.0, masked_score)

    query_b = query_bias[:, columns].astype(F32)
    for copy in weight_copies:
        copy.wait()
    word_low, ent_low = hidden_low[:all_words], hidden_low[all_words:]
    query_words[:all_words] = (dot(word_low, query_here[0]) + query_b[0:1]).astype(LOW)
    query_ents[:all_words] = (dot(word_low, query_here[1]) + query_b[1:2]).astype(LOW)
    query_words[all_words:] = (dot(ent_low, query_here[2]) + query_b[2:3]).astype(LOW)
    query_ents[all_words:] = (dot(ent_low, query_here[3]) + query_b[3:4]).astype(LOW)
    keys[...] = (dot(hidden_low[...], key_here[...]) + key_bias[:, columns].astype(F32)).astype(LOW)
    value = dot(hidden_low[...], value_here[...]) + value_bias[:, columns].astype(F32)
    values[...] = value.astype(LOW)
    values_turned[...] = jnp.transpose(value).astype(LOW)
    scale = 1.0 / math.sqrt(HEAD)
    tiles = tokens // LANES

    def tile(i, _):
        pair, place = i // tiles, span((i % tiles) * LANES, LANES, LANES)
        lanes = span(pair * LANES, LANES, LANES)
        key = keys[:, lanes]
        query_w, query_e = query_words[place, lanes], query_ents[place, lanes]
        turned = values_turned[lanes, :]
        total = jnp.zeros((LANES, LANES), F32)
        for head in range(2):
            own_key = jnp.where(lane_mask(tokens, head), key, jnp.zeros_like(key))
            raw = jnp.concatenate(
                [dot_rows(own_key[:all_words], query_w), dot_rows(own_key[all_words:], query_e)], axis=0
            )
            score = raw * scale + mask[:, place]
            weight = jnp.exp(score - jnp.max(score, axis=0, keepdims=True))
            prob = (weight * (1.0 / jnp.sum(weight, axis=0, keepdims=True))).astype(LOW)
            probs[pair * 2 + head, :, place] = prob
            row = lax.broadcasted_iota(jnp.int32, (LANES, tokens), 0)
            own_rows = (row >= head * HEAD) & (row < (head + 1) * HEAD)
            total = total + dot(jnp.where(own_rows, turned, jnp.zeros_like(turned)), prob)
        mixed[place, lanes] = jnp.transpose(total).astype(LOW)
        return 0

    loop(half // LANES * tiles, tile)


def forward(words, rows, ent_pos, segments, ent_proj, pos_table, query_weight, query_bias, key_weight, key_bias, value_weight, value_bias):
    all_words, width = words.shape
    ents = rows.shape[0]
    tokens, half = all_words + ents, width // 2
    return call(
        forward_kernel,
        [
            ((ents, width), F32),
            ((tokens, width), LOW),
            ((tokens, half), LOW),
            ((tokens, half), LOW),
            ((tokens, half), LOW),
            ((tokens, half), LOW),
            ((HEADS // 2, tokens, tokens), LOW),
            ((tokens, half), LOW),
        ],
        [IN_VMEM] * 6 + [ANY, IN_VMEM, ANY, IN_VMEM, ANY, IN_VMEM],
        [IN_VMEM] * 8,
        [
            pltpu.VMEM((4, width, half), LOW),
            pltpu.VMEM((width, half), LOW),
            pltpu.VMEM((width, half), LOW),
            pltpu.VMEM((half, tokens), LOW),
            pltpu.VMEM((tokens, tokens), F32),
            pltpu.VMEM((LANES, tokens), F32),
            pltpu.SemaphoreType.DMA((3,)),
        ],
        "forward",
    )(words, rows, ent_pos, segments, ent_proj, pos_table, query_weight, query_bias, key_weight, key_bias, value_weight, value_bias)


ROW_BLOCK = 32


def lane_mean(value):
    return jnp.mean(value, axis=-1, keepdims=True)


def column_sum(value):
    return jnp.sum(value, axis=0, keepdims=True)


class Several:
    def __init__(self, copies):
        self.copies = copies

    def wait(self):
        for copy in self.copies:
            copy.wait()


def middle_kernel(
    nz, words, ent_hidden, mixed, out_weight, out_bias, gains, shifts, up_weight, up_bias, down_weight, down_bias, word_cots, ent_cots,
    word_out, ent_out, grad_one, grad_mixed, grads, bias_out,
    out_here, up_here, down_here, mixed_full, from_y, hidden, work, normed, normed_low, normal_one, inverse_one,
    act, slope, output, cot, grad_two, grad_two_low, grad_up_low, grad_one_low, grad_mixed_here, stage, down_stage, send_sem, recv_sem, local_sem,
):
    copies = Copies(send_sem, recv_sem, local_sem)
    place = Place(nz)
    y, core = place.y, place.core
    n_dp = 2 * nz
    all_words, width = words.shape
    ents = ent_hidden.shape[0]
    half = mixed.shape[1]
    word_half, ent_half = all_words // 2, ents // 2
    tokens = word_half + ent_half
    ff = up_weight.shape[1]
    parts = ff // width
    meet([place.other_core, place.other_y])

    def token_rows(side):
        return span(side * word_half, word_half, LANES), span(all_words + side * ent_half, ent_half, 64)

    mine, theirs = token_rows(y), token_rows(1 - y)
    mixed_copies = [
        copies.send(mixed.at[theirs[0]], from_y.at[pl.ds(0, word_half)], place.other_y),
        copies.send(mixed.at[theirs[1]], from_y.at[pl.ds(word_half, ent_half)], place.other_y),
    ]
    weight_copies = [
        copies.local(out_weight, out_here),
        copies.local(up_weight, up_here),
        copies.local(down_weight, down_here),
    ]
    cot_copies = [
        copies.local(word_cots, cot.at[pl.ds(0, word_half)]),
        copies.local(ent_cots, cot.at[pl.ds(word_half, ent_half)]),
    ]
    gain, shift = gains[...].astype(F32), shifts[...].astype(F32)
    out_b, down_b, up_b = out_bias[...].astype(F32), down_bias[...].astype(F32), up_bias[...].astype(F32)
    hidden[:word_half] = words[mine[0]].astype(F32)
    hidden[word_half:] = ent_hidden[span(y * ent_half, ent_half, 64)]
    own_columns, other_columns = span(y * half, half, LANES), span((1 - y) * half, half, LANES)
    mixed_full[:word_half, own_columns] = mixed[mine[0]]
    mixed_full[word_half:, own_columns] = mixed[mine[1]]
    for copy in mixed_copies:
        copy.wait_recv()
    mixed_full[:, other_columns] = from_y[...]
    weight_copies[0].wait()
    work[...] = dot(mixed_full[...], out_here[...])
    blocks = tokens // ROW_BLOCK

    def norm_one(i, _):
        rows = span(i * ROW_BLOCK, ROW_BLOCK, ROW_BLOCK)
        value = hidden[rows] + (work[rows] + out_b)
        center = value - lane_mean(value)
        inverse = lax.rsqrt(lane_mean(center * center) + norm_eps)
        normal = center * inverse
        result = normal * gain[0:1] + shift[0:1]
        normal_one[rows] = normal
        inverse_one[rows] = jnp.broadcast_to(inverse, (ROW_BLOCK, LANES))
        normed[rows] = result
        normed_low[rows] = result.astype(LOW)
        return 0

    loop(blocks, norm_one)
    weight_copies[1].wait()
    weight_copies[2].wait()
    for j in range(parts):
        columns = slice(j * width, (j + 1) * width)
        work[...] = dot(normed_low[...], up_here[:, columns]) + up_b[:, columns]

        def gelu(i, _):
            rows = span(i * 16, 16, 16)
            value = work[rows]
            below = 0.5 * (1.0 + lax.erf(value * (1.0 / math.sqrt(2.0))))
            density = jnp.exp(-0.5 * value * value) * (1.0 / math.sqrt(2.0 * math.pi))
            act[rows, columns] = (value * below).astype(LOW)
            slope[rows, columns] = below + value * density
            return 0

        loop(tokens // 16, gelu)
    for copy in cot_copies:
        copy.wait()
    work[...] = dot(act[...], down_here[...])

    def norm_two(i, sums):
        rows = span(i * ROW_BLOCK, ROW_BLOCK, ROW_BLOCK)
        value = normed[rows] + (work[rows] + down_b)
        center = value - lane_mean(value)
        inverse = lax.rsqrt(lane_mean(center * center) + norm_eps)
        normal = center * inverse
        output[rows] = (normal * gain[1:2] + shift[1:2]).astype(LOW)
        given = cot[rows].astype(F32)
        scaled = given * gain[1:2]
        result = inverse * (scaled - lane_mean(scaled) - normal * lane_mean(scaled * normal))
        grad_two[rows] = result
        grad_two_low[rows] = result.astype(LOW)
        return (
            sums[0] + column_sum(given * normal),
            sums[1] + column_sum(given),
            sums[2] + column_sum(result),
        )

    nothing = jnp.zeros((1, width), F32)
    gain_two, shift_two, down_sum = loop(blocks, norm_two, (nothing, nothing, nothing))
    own_quarter = span(core * (word_half // 2), word_half // 2, LANES)
    other_quarter = span((1 - core) * (word_half // 2), word_half // 2, LANES)
    ent_quarter = ent_half // 2
    own_ents = span(word_half + core * ent_quarter, ent_quarter, 32)
    other_ents = span(word_half + (1 - core) * ent_quarter, ent_quarter, 32)
    out_copies = [
        copies.send(output.at[other_quarter], word_out.at[core], place.other_core),
        copies.send(output.at[other_ents], ent_out.at[core], place.other_core),
    ]
    out_local = [
        copies.local(output.at[own_quarter], word_out.at[core]),
        copies.local(output.at[own_ents], ent_out.at[core]),
    ]
    down_rows, row_part, row_pad = ff // n_dp, width // n_dp, padded(width // n_dp)
    staged = [None, None]
    turn = [0]

    def put_out(value, base, rows_in):
        slot = turn[0] % 2
        turn[0] += 1
        if staged[slot] is not None:
            staged[slot].wait()
        value = value.astype(LOW).reshape(nz, 2, rows_in, width)
        stage[slot, :, :, pl.ds(0, rows_in)] = value
        size = padded(rows_in)
        staged[slot] = copies.local(stage.at[slot, :, :, pl.ds(0, size)], grads.at[:, :, pl.ds(base, size)])

    down_staged = [None, None]
    for j in range(parts):
        columns = slice(j * width, (j + 1) * width)
        value = dot_columns(act[:, columns], grad_two_low[...]).astype(LOW)
        if down_staged[j % 2] is not None:
            down_staged[j % 2].wait()
        down_stage[j % 2] = value
        per = width // down_rows
        down_staged[j % 2] = Several([
            copies.local(
                down_stage.at[j % 2, pl.ds(d * down_rows, down_rows)],
                grads.at[(j * per + d) // 2, (j * per + d) % 2, pl.ds(0, down_rows)],
            )
            for d in range(per)
        ])
    up_sums = []
    for j in range(parts):
        columns = slice(j * width, (j + 1) * width)
        work[...] = dot_rows(grad_two_low[...], down_here[columns, :])

        def grad_gelu(i, total):
            rows = span(i * 16, 16, 16)
            value = work[rows] * slope[rows, columns]
            grad_up_low[rows, columns] = value.astype(LOW)
            return total + column_sum(value)

        up_sums.append(loop(tokens // 16, grad_gelu, nothing))
        put_out(dot_columns(normed_low[...], grad_up_low[:, columns]), down_rows + j * row_pad, row_part)
    work[...] = dot_rows(grad_up_low[...], up_here[...])

    def back_one(i, sums):
        rows = span(i * ROW_BLOCK, ROW_BLOCK, ROW_BLOCK)
        given = grad_two[rows] + work[rows]
        normal = normal_one[rows]
        inverse = inverse_one[rows, 0:1]
        scaled = given * gain[0:1]
        result = inverse * (scaled - lane_mean(scaled) - normal * lane_mean(scaled * normal))
        grad_one[rows] = result
        grad_one_low[rows] = result.astype(LOW)
        return (
            sums[0] + column_sum(given * normal),
            sums[1] + column_sum(given),
            sums[2] + column_sum(result),
        )

    gain_one, shift_one, out_sum = loop(blocks, back_one, (nothing, nothing, nothing))
    other_out = out_here[other_columns, :]
    grad_mixed_here[1] = dot_rows(grad_one_low[...], other_out).astype(LOW)
    mixed_back = [
        copies.send(grad_mixed_here.at[1, pl.ds(0, word_half)], grad_mixed.at[mine[0]], place.other_y),
        copies.send(grad_mixed_here.at[1, pl.ds(word_half, ent_half)], grad_mixed.at[mine[1]], place.other_y),
    ]
    grad_mixed_here[0] = dot_rows(grad_one_low[...], out_here[own_columns, :]).astype(LOW)
    mixed_own = [
        copies.local(grad_mixed_here.at[0, pl.ds(0, word_half)], grad_mixed.at[mine[0]]),
        copies.local(grad_mixed_here.at[0, pl.ds(word_half, ent_half)], grad_mixed.at[mine[1]]),
    ]
    put_out(dot_columns(mixed_full[...], grad_one_low[...]), down_rows + parts * row_pad, row_part)
    bias_rows = [out_sum, gain_one, gain_two, shift_one, shift_two] + up_sums + [down_sum]
    for i, row in enumerate(bias_rows):
        bias_out[i : i + 1] = row
    for copy in staged + down_staged:
        copy.wait()
    for copy in mixed_back + out_copies:
        copy.wait_recv()
    for copy in mixed_own + out_local:
        copy.wait()
    copies.finish()


def middle(nz, words, ent_hidden, mixed, out_weight, out_bias, gains, shifts, up_weight, up_bias, down_weight, down_bias, word_cots, ent_cots):
    n_dp = 2 * nz
    all_words, width = words.shape
    ents, half, ff = ent_hidden.shape[0], mixed.shape[1], up_weight.shape[1]
    tokens = (all_words + ents) // 2
    parts = ff // width
    row_pad = padded(width // n_dp)
    slab = ff // n_dp + (parts + 1) * row_pad
    return call(
        functools.partial(middle_kernel, nz),
        [
            ((2, all_words // 4, width), LOW),
            ((2, ents // 4, width), LOW),
            ((tokens, width), F32),
            ((all_words + ents, half), LOW),
            ((nz, 2, slab, width), LOW),
            ((6 + parts, width), F32),
        ],
        [IN_VMEM] * 3 + [ANY] + [IN_VMEM] * 3 + [ANY, IN_VMEM, ANY, IN_VMEM, ANY, ANY],
        [ANY, ANY, IN_VMEM, ANY, ANY, IN_VMEM],
        [
            pltpu.VMEM((width, width), LOW),
            pltpu.VMEM((width, ff), LOW),
            pltpu.VMEM((ff, width), LOW),
            pltpu.VMEM((tokens, width), LOW),
            pltpu.VMEM((tokens, half), LOW),
            pltpu.VMEM((tokens, width), F32),
            pltpu.VMEM((tokens, width), F32),
            pltpu.VMEM((tokens, width), F32),
            pltpu.VMEM((tokens, width), LOW),
            pltpu.VMEM((tokens, width), F32),
            pltpu.VMEM((tokens, LANES), F32),
            pltpu.VMEM((tokens, ff), LOW),
            pltpu.VMEM((tokens, ff), F32),
            pltpu.VMEM((tokens, width), LOW),
            pltpu.VMEM((tokens, width), LOW),
            pltpu.VMEM((tokens, width), F32),
            pltpu.VMEM((tokens, width), LOW),
            pltpu.VMEM((tokens, ff), LOW),
            pltpu.VMEM((tokens, width), LOW),
            pltpu.VMEM((2, tokens, half), LOW),
            pltpu.VMEM((2, nz, 2, row_pad, width), LOW),
            pltpu.VMEM((2, width, width), LOW),
        ]
        + copy_semaphores(8, 40 + 4 * n_dp),
        "middle",
        2,
    )(words, ent_hidden, mixed, out_weight, out_bias, gains, shifts, up_weight, up_bias, down_weight, down_bias, word_cots, ent_cots)


def backward_kernel(
    nz, all_words, hidden_low, query_words, query_ents, keys, values, probs, grad_mixed, query_weight, key_weight, value_weight,
    grad_hidden, grads, bias_out,
    query_here, key_here, value_here, keys_turned, grad_scores, grad_query_words, grad_query_ents, grad_keys, grad_values, hidden_turned, stage, local_sem,
):
    y = lax.axis_index("seq") // 2
    tokens, half = keys.shape
    width = hidden_low.shape[1]
    ents = tokens - all_words
    n_dp = 2 * nz
    columns = span(y * half, half, LANES)
    weight_copies = [
        pltpu.make_async_copy(query_weight.at[:, :, columns], query_here, local_sem.at[0]),
        pltpu.make_async_copy(key_weight.at[:, columns], key_here, local_sem.at[1]),
        pltpu.make_async_copy(value_weight.at[:, columns], value_here, local_sem.at[2]),
    ]
    for copy in weight_copies:
        copy.start()
    for i in range(half // LANES):
        lanes = slice(i * LANES, (i + 1) * LANES)
        keys_turned[lanes, :] = jnp.transpose(keys[:, lanes].astype(F32)).astype(LOW)
    for i in range(width // LANES):
        lanes = slice(i * LANES, (i + 1) * LANES)
        hidden_turned[lanes, :] = jnp.transpose(hidden_low[:, lanes].astype(F32)).astype(LOW)
    scale = 1.0 / math.sqrt(HEAD)
    tiles = tokens // LANES

    def pair_step(pair, _):
        lanes = span(pair * LANES, LANES, LANES)
        grad_query_w = jnp.zeros((LANES, tokens), F32)
        grad_query_e = jnp.zeros((LANES, tokens), F32)
        grad_key_w = jnp.zeros((all_words, LANES), F32)
        grad_key_e = jnp.zeros((ents, LANES), F32)
        grad_value = jnp.zeros((tokens, LANES), F32)
        for head in range(2):
            own = lane_mask(tokens, head)
            value = values[:, lanes]
            own_value = jnp.where(own, value, jnp.zeros_like(value))

            def tile(i, _):
                place = span(i * LANES, LANES, LANES)
                grad_prob = dot_rows(own_value, grad_mixed[place, lanes])
                prob = probs[pair * 2 + head, :, place].astype(F32)
                both = prob * grad_prob
                grad_scores[:, place] = (both - prob * jnp.sum(both, axis=0, keepdims=True)).astype(LOW)
                return 0

            loop(tiles, tile)
            given = grad_mixed[:, lanes]
            grad_value += dot(probs[pair * 2 + head], jnp.where(own, given, jnp.zeros_like(given)))
            query_w, query_e = query_words[:, lanes], query_ents[:, lanes]
            grad_key_w += dot(grad_scores[:all_words], jnp.where(own, query_w, jnp.zeros_like(query_w)))
            grad_key_e += dot(grad_scores[all_words:], jnp.where(own, query_e, jnp.zeros_like(query_e)))
            row = lax.broadcasted_iota(jnp.int32, (LANES, tokens), 0)
            own_rows = (row >= head * HEAD) & (row < (head + 1) * HEAD)
            turned = keys_turned[lanes, :]
            turned = jnp.where(own_rows, turned, jnp.zeros_like(turned))
            grad_query_w += dot(turned[:, :all_words], grad_scores[:all_words])
            grad_query_e += dot(turned[:, all_words:], grad_scores[all_words:])
        grad_query_w = jnp.transpose(grad_query_w) * scale
        grad_query_e = jnp.transpose(grad_query_e) * scale
        grad_key_w, grad_key_e = grad_key_w * scale, grad_key_e * scale
        sums = [
            column_sum(grad_query_w[:all_words]),
            column_sum(grad_query_e[:all_words]),
            column_sum(grad_query_w[all_words:]),
            column_sum(grad_query_e[all_words:]),
            column_sum(grad_key_w) + column_sum(grad_key_e),
            column_sum(grad_value),
        ]
        for i, total in enumerate(sums):
            bias_out[i : i + 1, lanes] = total
        grad_query_words[:, lanes] = grad_query_w.astype(LOW)
        grad_query_ents[:, lanes] = grad_query_e.astype(LOW)
        grad_keys[:all_words, lanes] = grad_key_w.astype(LOW)
        grad_keys[all_words:, lanes] = grad_key_e.astype(LOW)
        grad_values[:, lanes] = grad_value.astype(LOW)
        return 0

    loop(half // LANES, pair_step)
    for copy in weight_copies:
        copy.wait()
    row_part, row_pad = width // n_dp, padded(width // n_dp)
    staged = [None, None]
    word_turned, ent_turned = hidden_turned[:, :all_words], hidden_turned[:, all_words:]
    products = [
        lambda: dot(word_turned, grad_query_words[:all_words]),
        lambda: dot(word_turned, grad_query_ents[:all_words]),
        lambda: dot(ent_turned, grad_query_words[all_words:]),
        lambda: dot(ent_turned, grad_query_ents[all_words:]),
        lambda: dot(hidden_turned[...], grad_keys[...]),
        lambda: dot(hidden_turned[...], grad_values[...]),
    ]
    for i, product in enumerate(products):
        value = product().astype(LOW).reshape(nz, 2, row_part, half)
        if staged[i % 2] is not None:
            staged[i % 2].wait()
        stage[i % 2, :, :, pl.ds(0, row_part)] = value
        staged[i % 2] = pltpu.make_async_copy(
            stage.at[i % 2], grads.at[:, :, pl.ds(i * row_pad, row_pad)], local_sem.at[3 + i]
        )
        staged[i % 2].start()
    shared = (dot_rows(grad_keys[...], key_here[...]) + dot_rows(grad_values[...], value_here[...]))
    grad_hidden[:all_words] = (
        shared[:all_words]
        + dot_rows(grad_query_words[:all_words], query_here[0])
        + dot_rows(grad_query_ents[:all_words], query_here[1])
    ).astype(LOW)
    grad_hidden[all_words:] = (
        shared[all_words:]
        + dot_rows(grad_query_words[all_words:], query_here[2])
        + dot_rows(grad_query_ents[all_words:], query_here[3])
    ).astype(LOW)
    for copy in staged:
        copy.wait()


def backward(nz, all_words, hidden_low, query_words, query_ents, keys, values, probs, grad_mixed, query_weight, key_weight, value_weight):
    tokens, width = hidden_low.shape
    half = keys.shape[1]
    row_pad = padded(width // (2 * nz))
    return call(
        functools.partial(backward_kernel, nz, all_words),
        [((tokens, width), LOW), ((nz, 2, 6 * row_pad, half), LOW), ((8, half), F32)],
        [IN_VMEM] * 7 + [ANY] * 3,
        [IN_VMEM, ANY, IN_VMEM],
        [
            pltpu.VMEM((4, width, half), LOW),
            pltpu.VMEM((width, half), LOW),
            pltpu.VMEM((width, half), LOW),
            pltpu.VMEM((half, tokens), LOW),
            pltpu.VMEM((tokens, tokens), LOW),
            pltpu.VMEM((tokens, half), LOW),
            pltpu.VMEM((tokens, half), LOW),
            pltpu.VMEM((tokens, half), LOW),
            pltpu.VMEM((tokens, half), LOW),
            pltpu.VMEM((width, tokens), LOW),
            pltpu.VMEM((2, nz, 2, row_pad, half), LOW),
            pltpu.SemaphoreType.DMA((9,)),
        ],
        "backward",
    )(hidden_low, query_words, query_ents, keys, values, probs, grad_mixed, query_weight, key_weight, value_weight)


def blocks_of(rows):
    for size in (96, 64, 48, 32):
        if rows % size == 0:
            return size
    return 16


def add_blocks(target, parts, leading, rows):
    size = blocks_of(rows)
    count = rows // size

    def block(i, _):
        lead, row = i // count, (i % count) * size
        where = span(row, size, 16)
        value = parts[0](lead, where).astype(F32)
        for part in parts[1:]:
            value = value + part(lead, where).astype(F32)
        target(lead, where, value.astype(LOW))
        return 0

    loop(leading * count, block)


class Job:
    def __init__(self, grads, reduced, base, size, order, columns):
        self.grads, self.reduced, self.base, self.size, self.order, self.columns = grads, reduced, base, size, order, columns
        self.half = size // 2
        self.part = size // 4 if order == "yxz" else size // 2

    def scratch(self, nz):
        shapes = [(nz, 2, self.half, self.columns)] * 2
        if self.order == "yxz":
            shapes.append((nz, 2, self.part, self.columns))
        elif self.order == "xzy":
            shapes.append((2, self.part, self.columns))
        shapes += [(nz, self.part, self.columns), (nz - 1, self.part, self.columns)]
        return [pltpu.VMEM(shape, LOW) for shape in shapes]

    def remote_count(self, nz):
        return 1 + (1 if self.order != "xz" else 0) + 1 + (nz - 1) + 1 + 1

    def steps(self, place, copies, scratch):
        nz, z, x, y, core = place.nz, place.z, place.x, place.y, place.core
        base, half, part, order = self.base, self.half, self.part, self.order
        held, from_core = scratch[:2]
        from_y = scratch[2] if order != "xz" else None
        from_x, from_z = scratch[-2:]
        live = {}

        def start():
            theirs, own = span(base + (1 - core) * half, half, 16), span(base + core * half, half, 16)
            live["core"] = copies.send(self.grads.at[:, :, theirs], from_core, place.other_core)
            live["own"] = copies.local(self.grads.at[:, :, own], held)

        own_rows = span(y * part, part, 16) if order == "yxz" else pl.ds(0, part)
        final_rows = span(base + core * half + (y * part if order == "yxz" else 0), part, 16)

        def send_x():
            live["x"] = copies.send(held.at[:, 1 - x, own_rows], from_x, place.other_x)

        def after_core():
            live["own"].wait()
            live["core"].wait_recv()

            def put(i, where, value):
                held[i // 2, i % 2, where] = value

            add_blocks(
                put,
                [lambda i, where: held[i // 2, i % 2, where], lambda i, where: from_core[i // 2, i % 2, where]],
                2 * nz,
                half,
            )
            if order == "yxz":
                live["y"] = copies.send(held.at[:, :, span((1 - y) * part, part, 16)], from_y, place.other_y)
            else:
                send_x()

        def shifted(where):
            return span(y * part + where.start, where.size, 16) if order == "yxz" else where

        def after_y():
            live["y"].wait_recv()

            def put(i, where, value):
                held[i // 2, i % 2, shifted(where)] = value

            add_blocks(
                put,
                [lambda i, where: held[i // 2, i % 2, shifted(where)], lambda i, where: from_y[i // 2, i % 2, where]],
                2 * nz,
                part,
            )
            send_x()

        def after_x():
            live["x"].wait_recv()

            def put(i, where, value):
                held[i, x, shifted(where)] = value

            add_blocks(
                put, [lambda i, where: held[i, x, shifted(where)], lambda i, where: from_x[i, where]], nz, part
            )
            live["z"] = [
                copies.send(held.at[place.z_ahead(k + 1), x, own_rows], from_z.at[k], device)
                for k, device in enumerate(place.ahead)
            ]

        def after_z():
            for copy in live["z"]:
                copy.wait_recv()

            def put(i, where, value):
                if order == "yxz":
                    self.reduced[span(base + core * half + y * part + where.start, where.size, 16)] = value
                elif order == "xz":
                    self.reduced[y, span(base + core * half + where.start, where.size, 16)] = value
                else:
                    from_y[0, where] = value

            def parts(k):
                return lambda i, where: from_z[k, where]

            add_blocks(
                put, [lambda i, where: held[z, x, shifted(where)]] + [parts(k) for k in range(nz - 1)], 1, part
            )
            if order == "yxz":
                view = self.reduced.at[final_rows]
                live["y2"] = copies.send(view, view, place.other_y)
            elif order == "xz":
                view = self.reduced.at[y, final_rows]
                live["y2"] = copies.send(view, view, place.other_y)
            else:
                live["y2"] = copies.send(from_y.at[0], from_y.at[1], place.other_y)

        def after_gather():
            live["y2"].wait_recv()
            mine = span(base + core * half, half, 16)
            if order == "xzy":

                def put(i, where, value):
                    self.reduced[span(base + core * half + where.start, where.size, 16)] = value

                add_blocks(put, [lambda i, where: from_y[0, where], lambda i, where: from_y[1, where]], 1, part)
            view = self.reduced.at[:, mine] if order == "xz" else self.reduced.at[mine]
            live["core2"] = copies.send(view, view, place.other_core)

        def end():
            live["core2"].wait_recv()

        middle_steps = [after_core, after_y, after_x] if order == "yxz" else [after_core, after_x]
        return [start] + middle_steps + [after_z, after_gather, end]


def job_spans(rows):
    spans, base, turn = [], 0, 0
    while base < rows:
        size, order = (192, "yxz") if turn % 2 == 0 else (96, "xzy")
        if base + size > rows:
            size = rows - base
            order = "yxz" if size % 64 == 0 else "xzy"
        spans.append((base, size, order))
        base += size
        turn += 1
    return spans


def finish_kernel(nz, plan, ent_rows_pad, bias_rows, grad_hidden, grad_one, rows, ent_pos, ent_proj, ffn_grads, attn_grads, bias_heads, bias_middle,
                  word_grad, ffn_reduced, attn_reduced, ent_reduced, bias_out, row_grads, *scratch):
    copies = Copies(*scratch[-3:])
    given, total, ent_grads, ffn_sum, attn_sum, ent_sum, bias_held, bias_from, all_rows = scratch[:9]
    place = Place(nz)
    z, x, y, core = place.z, place.x, place.y, place.core
    n_dp = 2 * nz
    tokens, width = grad_one.shape
    ents = rows.shape[0]
    ent_half = ents // 2
    word_half = tokens - ent_half
    all_words = 2 * word_half
    half = bias_heads.shape[1]
    meet([place.other_core, place.other_y, place.other_x] + place.ahead)
    theirs = span((1 - y) * word_half, word_half, LANES), span(all_words + (1 - y) * ent_half, ent_half, 64)
    mine = span(y * word_half, word_half, LANES), span(all_words + y * ent_half, ent_half, 64)
    hidden_copies = [
        copies.send(grad_hidden.at[theirs[1]], given.at[pl.ds(word_half, ent_half)], place.other_y),
        copies.send(grad_hidden.at[theirs[0]], given.at[pl.ds(0, word_half)], place.other_y),
    ]
    jobs, at = [], 9
    sources = {"ffn": (ffn_grads, ffn_sum), "attn": (attn_grads, attn_sum), "ent": (ent_grads, ent_sum)}
    for name, base, size, order, columns in plan:
        job = Job(*sources[name], base, size, order, columns)
        used = len(job.scratch(nz))
        jobs.append((name, job.steps(place, copies, scratch[at : at + used])))
        at += used
    for name, steps in jobs:
        if name != "ent":
            steps.pop(0)()

    bias_held[...] = jnp.zeros_like(bias_held)
    bias_full = bias_heads[0:6].astype(LOW)
    bias_held[0:6, span(y * half, half, LANES)] = bias_full.astype(F32)
    bias_held[6:bias_rows] = bias_middle[...]
    live = {}

    def bias_send(key, index, device):
        bias_from[2 * index] = bias_held[...].astype(LOW)
        live[key] = copies.send(bias_from.at[2 * index], bias_from.at[2 * index + 1], device)

    def bias_take(key, index):
        live[key].wait_recv()
        bias_held[...] = bias_from[2 * index].astype(F32) + bias_from[2 * index + 1].astype(F32)

    def bias_core():
        bias_send("core", 0, place.other_core)

    def bias_y():
        bias_take("core", 0)
        bias_send("y", 1, place.other_y)

    def bias_x():
        bias_take("y", 1)
        bias_send("x", 2, place.other_x)

    def bias_z():
        bias_take("x", 2)
        bias_from[6] = bias_held[...].astype(LOW)
        live["z"] = [copies.send(bias_from.at[6], bias_from.at[7 + k], device) for k, device in enumerate(place.ahead)]

    def bias_end():
        value = bias_from[6].astype(F32)
        for k, copy in enumerate(live["z"]):
            copy.wait_recv()
            value = value + bias_from[7 + k].astype(F32)
        bias_out[...] = value

    for copy in hidden_copies:
        copy.wait_recv()

    def hidden_block(i, _):
        where = span(i * 32, 32, 32)
        own = span(y * word_half + i * 32, 32, 32)
        total[where] = grad_one[where] + (grad_hidden[own].astype(F32) + given[where].astype(F32))
        return 0

    def ent_block(i, _):
        where = span(word_half + i * 32, 32, 32)
        own = span(all_words + y * ent_half + i * 32, 32, 32)
        total[where] = grad_one[where] + (grad_hidden[own].astype(F32) + given[where].astype(F32))
        return 0

    loop(ent_half // 32, ent_block)
    grad_ent = total[word_half:]
    grad_ent_low = grad_ent.astype(LOW)
    row_grad = dot_rows(grad_ent_low, ent_proj[...]).astype(LOW)
    all_rows[place.dp, core, span(y * ent_half, ent_half, 64)] = row_grad
    live_rows = {}

    def rows_y():
        view = all_rows.at[place.dp, core, span(y * ent_half, ent_half, 64)]
        live_rows["y"] = copies.send(view, view, place.other_y)

    def rows_z():
        live_rows["y"].wait_recv()
        view = all_rows.at[place.dp, core]
        live_rows["z"] = [copies.send(view, view, device) for device in place.ahead]

    def rows_x():
        for copy in live_rows["z"]:
            copy.wait_recv()
        live_rows["x"] = []
        for k in range(nz):
            view = all_rows.at[place.z_ahead(k) * 2 + x, core]
            live_rows["x"].append(copies.send(view, view, place.other_x))

    def rows_core():
        for copy in live_rows["x"]:
            copy.wait_recv()
        view = all_rows.at[:, core]
        live_rows["core"] = copies.send(view, view, place.other_core)

    def rows_end():
        live_rows["core"].wait_recv()
        live_rows["out"] = copies.local(all_rows, row_grads)

    rows_y()
    bias_core()
    loop(word_half // 32, hidden_block)
    quarter = word_half // 2
    own_quarter = span(core * quarter, quarter, LANES)
    other_quarter = span((1 - core) * quarter, quarter, LANES)
    word_copy = copies.send(total.at[other_quarter], word_grad.at[core], place.other_core)
    word_local = copies.local(total.at[own_quarter], word_grad.at[core])
    proj_rows, pos_rows = rows.shape[1] // n_dp, all_words // n_dp
    proj_pad = padded(proj_rows)
    picks = []
    for j in range(all_words // LANES):
        number = lax.broadcasted_iota(jnp.int32, (LANES, ents), 0) + j * LANES
        picks.append(jnp.where(number == ent_pos[...], 1.0, 0.0))
    pick = jnp.concatenate(picks, axis=0)
    here = lax.broadcasted_iota(jnp.int32, (all_words, ents), 1) // ent_half == y
    pick = jnp.where(here, pick, 0.0).astype(LOW)
    rest = (grad_ent - grad_ent_low.astype(F32)).astype(LOW)
    pos_grad = dot(pick, jnp.concatenate([grad_ent_low, grad_ent_low], axis=0)) + dot(
        pick, jnp.concatenate([rest, rest], axis=0)
    )
    proj_grad = dot_columns(rows[span(y * ent_half, ent_half, 64)], grad_ent_low)
    ent_grads[...] = jnp.zeros_like(ent_grads)
    ent_grads[:, :, pl.ds(0, proj_rows)] = proj_grad.astype(LOW).reshape(nz, 2, proj_rows, width)
    ent_grads[:, :, pl.ds(proj_pad, pos_rows)] = pos_grad.astype(LOW).reshape(nz, 2, pos_rows, width)
    for name, steps in jobs:
        if name == "ent":
            steps.pop(0)()

    streams = [(0, [rows_z, rows_x, rows_core, rows_end]), (0, [bias_y, bias_x, bias_z, bias_end])]
    ffn_number = 0
    for number, (name, steps) in enumerate(jobs):
        streams.append((number, steps))
    last = max(offset + len(steps) for offset, steps in streams)
    for tick in range(last):
        for offset, steps in streams:
            if 0 <= tick - offset < len(steps):
                steps[tick - offset]()
    out_copies = [
        copies.local(ffn_sum, ffn_reduced),
        copies.local(attn_sum, attn_reduced),
        copies.local(ent_sum, ent_reduced),
    ]
    word_copy.wait_recv()
    word_local.wait()
    live_rows["out"].wait()
    for copy in out_copies:
        copy.wait()
    copies.finish()


def finish(nz, grad_hidden, grad_one, rows, ent_pos, ent_proj, ffn_grads, attn_grads, bias_heads, bias_middle):
    n_dp = 2 * nz
    tokens, width = grad_one.shape
    ents, edim = rows.shape
    all_words = (tokens - ents // 2) * 2
    half = bias_heads.shape[1]
    ffn_rows, attn_rows = ffn_grads.shape[2], attn_grads.shape[2]
    ent_pad = padded(edim // n_dp) + padded(all_words // n_dp)
    bias_rows = 6 + bias_middle.shape[0]
    plan = [("ffn", base, size, order, width) for base, size, order in job_spans(ffn_rows)]
    plan.append(("ent", 0, ent_pad, "xzy", width))
    attn_size = 192 if attn_rows % 192 == 0 else attn_rows
    plan += [("attn", base, attn_size, "xz", half) for base in range(0, attn_rows, attn_size)]
    scratch = [
        pltpu.VMEM((tokens, width), LOW),
        pltpu.VMEM((tokens, width), F32),
        pltpu.VMEM((nz, 2, ent_pad, width), LOW),
        pltpu.VMEM((ffn_rows, width), LOW),
        pltpu.VMEM((2, attn_rows, half), LOW),
        pltpu.VMEM((ent_pad, width), LOW),
        pltpu.VMEM((bias_rows, width), F32),
        pltpu.VMEM((6 + nz, bias_rows, width), LOW),
        pltpu.VMEM((n_dp, 2, ents, edim), LOW),
    ]
    remote = 40 + 2 * nz + 2 * nz
    for _, base, size, order, columns in plan:
        job = Job(None, None, base, size, order, columns)
        scratch += job.scratch(nz)
        remote += job.remote_count(nz)
    scratch += copy_semaphores(remote, len(plan) + 8)
    return call(
        functools.partial(finish_kernel, nz, plan, ent_pad, bias_rows),
        [
            ((2, all_words // 4, width), F32),
            ((ffn_rows, width), LOW),
            ((2, attn_rows, half), LOW),
            ((ent_pad, width), LOW),
            ((bias_rows, width), F32),
            ((n_dp, 2, ents, edim), LOW),
        ],
        [IN_VMEM] * 5 + [ANY] * 2 + [IN_VMEM] * 2,
        [ANY] * 4 + [IN_VMEM, ANY],
        scratch,
        "finish",
        3,
    )(grad_hidden, grad_one, rows, ent_pos, ent_proj, ffn_grads, attn_grads, bias_heads, bias_middle)


def table_kernel(ids, row_grads, first, second, table_grad, update, new_second, hits):
    rows_block, edim = first.shape
    groups, ents = ids.shape
    base = (lax.axis_index("dp") * 4 + lax.axis_index("seq")) * (rows_block * pl.num_programs(0))
    base = base + pl.program_id(0) * rows_block
    number = lax.broadcasted_iota(jnp.int32, (rows_block, ents), 0) + base
    count = jnp.zeros((rows_block, ents), F32)
    for i in range(groups):
        hit = jnp.where(ids[i : i + 1, :] == number, 1.0, 0.0)
        count = count + hit
        hits[:, i * ents : (i + 1) * ents] = hit.astype(LOW)
    grad = dot(hits[...], row_grads[...])
    touched = jnp.sum(count, axis=1, keepdims=True) > 0.0
    mean_new = beta_one * first[...] + (1.0 - beta_one) * grad
    square_new = beta_two * second[...] + (1.0 - beta_two) * grad * grad
    direction = (
        mean_new
        / (1.0 - beta_one**adam_step)
        / (jnp.sqrt(square_new / (1.0 - beta_two**adam_step)) + adam_eps)
    )
    table_grad[...] = grad
    update[...] = jnp.where(touched, direction, 0.0)
    new_second[...] = jnp.where(touched, square_new, second[...])


def table_step(ids, row_grads, first, second):
    rows, edim = first.shape
    groups, ents = ids.shape
    block = 256
    whole = lambda shape: pl.BlockSpec(shape, lambda i: (0, 0))
    part = pl.BlockSpec((block, edim), lambda i: (i, 0))
    return pl.pallas_call(
        table_kernel,
        grid=(rows // block,),
        out_shape=[jax.ShapeDtypeStruct((rows, edim), F32)] * 3,
        in_specs=[whole((groups, ents)), whole((groups * ents, edim)), part, part],
        out_specs=[part] * 3,
        scratch_shapes=[pltpu.VMEM((block, groups * ents), LOW)],
        compiler_params=pltpu.CompilerParams(vmem_limit_bytes=VMEM_BYTES),
        name="table_step",
    )(ids, row_grads, first, second)


def widen_kernel(n_dp, ffn, attn, ent, proj_grad, pos_grad, query_grad, key_grad, value_grad, out_grad, up_grad, down_grad):
    width = ffn.shape[1]
    part, down_rows = out_grad.shape[0], down_grad.shape[0]
    pad = padded(part)
    proj_pad = padded(proj_grad.shape[0])
    proj_grad[...] = ent[: proj_grad.shape[0]].astype(F32)
    pos_grad[...] = ent[proj_pad : proj_pad + pos_grad.shape[0]].astype(F32)
    down_grad[...] = ffn[:down_rows].astype(F32)
    parts = up_grad.shape[1] // width
    for j in range(parts):
        base = down_rows + j * pad
        up_grad[:, j * width : (j + 1) * width] = ffn[base : base + part].astype(F32)
    base = down_rows + parts * pad
    out_grad[...] = ffn[base : base + part].astype(F32)
    half = attn.shape[2]
    for side in range(2):
        columns = slice(side * half, (side + 1) * half)
        for i in range(4):
            query_grad[i, :, columns] = attn[side, i * pad : i * pad + part].astype(F32)
        key_grad[:, columns] = attn[side, 4 * pad : 4 * pad + part].astype(F32)
        value_grad[:, columns] = attn[side, 5 * pad : 5 * pad + part].astype(F32)


def widen(n_dp, ff, all_words, edim, ffn, attn, ent):
    width = ffn.shape[1]
    part = width // n_dp
    shapes = [
        (edim // n_dp, width),
        (all_words // n_dp, width),
        (4, part, width),
        (part, width),
        (part, width),
        (part, width),
        (part, ff),
        (ff // n_dp, width),
    ]
    return call(
        functools.partial(widen_kernel, n_dp),
        [(shape, F32) for shape in shapes],
        [IN_VMEM] * 3,
        [IN_VMEM] * 8,
        [],
        "widen",
    )(ffn, attn, ent)


def on_device(
    word_states,
    segments,
    entity_ids,
    entity_pos,
    ent_table,
    first_moment,
    second_moment,
    ent_proj,
    pos_table,
    query_weight,
    query_bias,
    key_weight,
    key_bias,
    value_weight,
    value_bias,
    out_weight,
    out_bias,
    norm_gain,
    norm_shift,
    up_weight,
    up_bias,
    down_weight,
    down_bias,
    word_cot,
    ent_cot,
):
    n_dp = lax.axis_size("dp")
    nz = n_dp // 2
    dp, core = lax.axis_index("dp"), lax.axis_index("seq") % 2
    width, ff = up_weight.shape
    all_words, edim = segments.shape[1], ent_table.shape[1]
    ent_pos = lax.dynamic_slice_in_dim(entity_pos, core, 1, 0)
    segments_here = lax.dynamic_slice_in_dim(segments, core, 1, 0)
    words, word_cots, ent_cots, all_ids, rows = fetch(nz, word_states, word_cot, ent_cot, entity_ids, ent_table)
    ent_hidden, hidden_low, query_words, query_ents, keys, values, probs, mixed = forward(
        words,
        rows,
        ent_pos,
        segments_here,
        ent_proj,
        pos_table,
        query_weight,
        query_bias,
        key_weight,
        key_bias.reshape(1, width),
        value_weight,
        value_bias.reshape(1, width),
    )
    word_out, ent_out, grad_one, grad_mixed, ffn_grads, bias_middle = middle(
        nz,
        words,
        ent_hidden,
        mixed,
        out_weight,
        out_bias.reshape(1, width),
        norm_gain,
        norm_shift,
        up_weight,
        up_bias.reshape(1, ff),
        down_weight,
        down_bias.reshape(1, width),
        word_cots,
        ent_cots,
    )
    grad_hidden, attn_grads, bias_heads = backward(
        nz, all_words, hidden_low, query_words, query_ents, keys, values, probs, grad_mixed, query_weight, key_weight, value_weight
    )
    word_grad, ffn_sum, attn_sum, ent_sum, bias_sum, row_grads = finish(
        nz, grad_hidden, grad_one, rows, ent_pos, ent_proj, ffn_grads, attn_grads, bias_heads, bias_middle
    )
    ents = entity_ids.shape[1]
    table_grad, table_update, new_second = table_step(
        all_ids.reshape(-1, ents), row_grads.reshape(-1, edim), first_moment, second_moment
    )
    proj_grad, pos_grad, query_grad, key_grad, value_grad, out_grad, up_grad, down_grad = widen(
        n_dp, ff, all_words, edim, ffn_sum, attn_sum, ent_sum
    )
    part = width // n_dp
    bias = lax.dynamic_slice(bias_sum, (0, dp * part), (bias_sum.shape[0], part))
    up_rows = 11 + ff // width
    up_bias_grad = lax.dynamic_slice(bias_sum[11:up_rows].reshape(-1), (dp * (ff // n_dp),), (ff // n_dp,))
    return (
        word_out,
        ent_out,
        word_grad,
        proj_grad,
        pos_grad,
        query_grad,
        bias[:4],
        key_grad,
        bias[4],
        value_grad,
        bias[5],
        out_grad,
        bias[6],
        bias[7:9],
        bias[9:11],
        up_grad,
        up_bias_grad,
        down_grad,
        bias[up_rows],
        table_grad,
        table_update,
        new_second,
    )


def solution(mesh):
    return jax.shard_map(
        on_device,
        mesh=mesh,
        in_specs=(
            P("dp", "seq", None),
            P("dp", None),
            P("dp", None),
            P("dp", None),
            P(("dp", "seq"), None),
            P(("dp", "seq"), None),
            P(("dp", "seq"), None),
            P(),
            P(),
            P(),
            P(),
            P(),
            P(),
            P(),
            P(),
            P(),
            P(),
            P(),
            P(),
            P(),
            P(),
            P(),
            P(),
            P("dp", "seq", None),
            P("dp", "seq", None),
        ),
        out_specs=(
            P("dp", "seq", None),
            P("dp", "seq", None),
            P("dp", "seq", None),
            P("dp", None),
            P("dp", None),
            P(None, "dp", None),
            P(None, "dp"),
            P("dp", None),
            P("dp"),
            P("dp", None),
            P("dp"),
            P("dp", None),
            P("dp"),
            P(None, "dp"),
            P(None, "dp"),
            P("dp", None),
            P("dp"),
            P("dp", None),
            P("dp"),
            P(("dp", "seq"), None),
            P(("dp", "seq"), None),
            P(("dp", "seq"), None),
        ),
        check_vma=False,
    )
```

```python
import functools
import math

import jax
import jax.numpy as jnp
from jax import lax
from jax.experimental import pallas as pl
from jax.experimental.pallas import tpu as pltpu
from jax.sharding import PartitionSpec as P

HEADS = 12
HEAD = 64
LANES = 128
MESH = pl.DeviceIdType.MESH
LOW = jnp.bfloat16
F32 = jnp.float32
VMEM_BYTES = 61 * 1024 * 1024

norm_eps = 1e-05
beta_one = 0.9
beta_two = 0.98
adam_eps = 1e-06
adam_step = 10.0
masked_score = -1e30


def dot(left, right):
    return jnp.dot(left, right, preferred_element_type=F32)


def dot_rows(left, right):
    return lax.dot_general(left, right, (((1,), (1,)), ((), ())), preferred_element_type=F32)


def dot_columns(left, right):
    return lax.dot_general(left, right, (((0,), (0,)), ((), ())), preferred_element_type=F32)


def span(start, size, unit):
    if isinstance(start, int):
        return pl.ds(start, size)
    return pl.ds(pl.multiple_of(start, unit), size)


def padded(rows):
    return -(-rows // 16) * 16


def loop(count, body, carry=0):
    return lax.fori_loop(0, count, body, carry)


class Place:
    def __init__(self, nz):
        self.dp, self.seq = lax.axis_index("dp"), lax.axis_index("seq")
        self.z, self.x = self.dp // 2, self.dp % 2
        self.y, self.core = self.seq // 2, self.seq % 2
        self.nz = nz
        self.other_core = (self.dp, self.y * 2 + 1 - self.core)
        self.other_y = (self.dp, (1 - self.y) * 2 + self.core)
        self.diagonal = (self.dp, (1 - self.y) * 2 + 1 - self.core)
        self.other_x = (self.z * 2 + 1 - self.x, self.seq)
        self.ahead = [(((self.z + k) % nz) * 2 + self.x, self.seq) for k in range(1, nz)]

    def z_ahead(self, k):
        return (self.z + k) % self.nz


def meet(partners):
    barrier = pltpu.get_barrier_semaphore()
    for partner in partners:
        pl.semaphore_signal(barrier, inc=1, device_id=partner, device_id_type=MESH)
    pl.semaphore_wait(barrier, len(partners))


class Copies:
    def __init__(self, send_sem, recv_sem, local_sem):
        self.send_sem, self.recv_sem, self.local_sem = send_sem, recv_sem, local_sem
        self.count, self.local_count = 0, 0
        self.sent = []

    def make(self, src, dst, device):
        copy = pltpu.make_async_remote_copy(
            src_ref=src,
            dst_ref=dst,
            send_sem=self.send_sem.at[self.count],
            recv_sem=self.recv_sem.at[self.count],
            device_id=device,
            device_id_type=MESH,
        )
        self.count += 1
        return copy

    def send(self, src, dst, device):
        copy = self.make(src, dst, device)
        copy.start()
        self.sent.append(copy)
        return copy

    def local(self, src, dst):
        copy = pltpu.make_async_copy(src, dst, self.local_sem.at[self.local_count])
        self.local_count += 1
        copy.start()
        return copy

    def finish(self):
        for copy in self.sent:
            copy.wait_send()


def copy_semaphores(remote, local):
    return [
        pltpu.SemaphoreType.DMA((remote,)),
        pltpu.SemaphoreType.DMA((remote,)),
        pltpu.SemaphoreType.DMA((local,)),
    ]


ANY = pl.BlockSpec(memory_space=pl.ANY)
IN_VMEM = pl.BlockSpec(memory_space=pltpu.VMEM)


def call(kernel, outs, in_specs, out_specs, scratch, name, collective_id=None):
    params = {"vmem_limit_bytes": VMEM_BYTES}
    if collective_id is not None:
        params.update(collective_id=collective_id, has_side_effects=True)
    return pl.pallas_call(
        kernel,
        out_shape=[jax.ShapeDtypeStruct(shape, dtype) for shape, dtype in outs],
        in_specs=in_specs,
        out_specs=out_specs,
        scratch_shapes=scratch,
        compiler_params=pltpu.CompilerParams(**params),
        name=name,
    )


def fetch_kernel(nz, words, word_cot, ent_cot, ids, table, all_words, word_cots, ent_cots, all_ids, rows_out, *scratch):
    table_full, table_low, picked, answers, held, from_core, from_x, from_z, from_y, ids_here = scratch[:10]
    copies = Copies(*scratch[10:])
    place = Place(nz)
    z, x, y, core = place.z, place.x, place.y, place.core
    n_dp = 2 * nz
    word_here, ent_here = words.shape[1], ent_cot.shape[1]
    ents = ids.shape[1]
    dp_others = [((place.dp + k) % n_dp, place.seq) for k in range(1, n_dp)]
    meet([place.other_core, place.other_y, place.diagonal] + dp_others)
    whole_table = copies.local(table, table_full)
    own_ids = copies.local(ids, ids_here.at[place.dp])
    id_copies = [copies.send(ids, ids_here.at[place.dp], device) for device in dp_others]
    quarter = span(place.seq * word_here, word_here, 128)
    word_copies = [
        copies.send(words.at[1 - core], all_words.at[quarter], place.diagonal),
        copies.send(words.at[core], all_words.at[quarter], place.other_y),
        copies.send(words.at[1 - core], all_words.at[quarter], place.other_core),
        copies.send(word_cot.at[1 - core], word_cots.at[span(core * word_here, word_here, 128)], place.other_core),
        copies.send(ent_cot.at[1 - core], ent_cots.at[span(core * ent_here, ent_here, 32)], place.other_core),
    ]
    local = [
        copies.local(words.at[core], all_words.at[quarter]),
        copies.local(word_cot.at[core], word_cots.at[span(core * word_here, word_here, 128)]),
        copies.local(ent_cot.at[core], ent_cots.at[span(core * ent_here, ent_here, 32)]),
    ]
    whole_table.wait()
    rows_dev = table.shape[0]

    def narrow(i, _):
        where = span(i * 128, 128, 128)
        table_low[where] = table_full[where].astype(LOW)
        return 0

    loop(rows_dev // 128, narrow)
    own_ids.wait()
    for copy in id_copies:
        copy.wait_recv()
    ids_out = copies.local(ids_here, all_ids)
    base = (place.dp * 4 + place.seq) * rows_dev
    tiles = rows_dev // LANES

    def look_up(zz, _):
        for xx in range(2):
            for s in range(2):
                asked = ids_here[zz * 2 + xx, pl.ds(s, 1), :] - base
                column = jnp.transpose(jnp.broadcast_to(asked, (ents, ents)))
                for j in range(tiles):
                    number = lax.broadcasted_iota(jnp.int32, (ents, LANES), 1) + j * LANES
                    hit = jnp.where(column == number, 1.0, 0.0).astype(LOW)
                    picked[pl.ds((xx * 2 + s) * ents, ents), pl.ds(j * LANES, LANES)] = hit
        answer = dot(picked[...], table_low[...]).astype(LOW)
        answers[zz] = answer.reshape(2, 2, ents, answer.shape[-1])
        return 0

    loop(nz, look_up)

    core_copy = copies.send(answers.at[:, :, 1 - core], from_core, place.other_core)
    core_copy.wait_recv()
    for xx in range(2):

        def add_core(zz, _):
            held[zz, xx] = answers[zz, xx, core] + from_core[zz, xx]
            return 0

        loop(nz, add_core)
    x_copy = copies.send(held.at[:, 1 - x], from_x, place.other_x)
    x_copy.wait_recv()

    def add_x(zz, _):
        held[zz, x] = held[zz, x] + from_x[zz]
        return 0

    loop(nz, add_x)
    z_copies = [
        copies.send(held.at[place.z_ahead(k + 1), x], from_z.at[k], device) for k, device in enumerate(place.ahead)
    ]
    total = held[z, x]
    for k in range(nz - 1):
        z_copies[k].wait_recv()
        total = total + from_z[k]
    from_y[0] = total
    y_copy = copies.send(from_y.at[0], from_y.at[1], place.other_y)
    y_copy.wait_recv()
    rows_out[...] = from_y[0] + from_y[1]
    for copy in word_copies:
        copy.wait_recv()
    for copy in local + [ids_out]:
        copy.wait()
    copies.finish()


def fetch(nz, words, word_cot, ent_cot, ids, table):
    _, word_here, width = words.shape
    ent_here, ents, (rows_dev, edim) = ent_cot.shape[1], ids.shape[1], table.shape
    n_dp = 2 * nz
    return call(
        functools.partial(fetch_kernel, nz),
        [
            ((4 * word_here, width), LOW),
            ((2 * word_here, width), LOW),
            ((2 * ent_here, width), LOW),
            ((n_dp, 2, ents), jnp.int32),
            ((ents, edim), LOW),
        ],
        [ANY] * 5,
        [ANY] * 4 + [IN_VMEM],
        [
            pltpu.VMEM((rows_dev, edim), F32),
            pltpu.VMEM((rows_dev, edim), LOW),
            pltpu.VMEM((4 * ents, rows_dev), LOW),
            pltpu.VMEM((nz, 2, 2, ents, edim), LOW),
            pltpu.VMEM((nz, 2, ents, edim), LOW),
            pltpu.VMEM((nz, 2, ents, edim), LOW),
            pltpu.VMEM((nz, ents, edim), LOW),
            pltpu.VMEM((nz - 1, ents, edim), LOW),
            pltpu.VMEM((2, ents, edim), LOW),
            pltpu.VMEM((n_dp, 2, ents), jnp.int32),
        ]
        + copy_semaphores(n_dp + 4 + 2 + nz + 2, 6),
        "fetch",
        1,
    )(words, word_cot, ent_cot, ids, table)


def lane_mask(rows, head):
    lane = lax.broadcasted_iota(jnp.int32, (rows, LANES), 1)
    return (lane >= head * HEAD) & (lane < (head + 1) * HEAD)


def as_column(row):
    parts = [
        jnp.transpose(jnp.broadcast_to(row[:, i : i + LANES], (LANES, LANES)))
        for i in range(0, row.shape[1], LANES)
    ]
    return jnp.concatenate(parts, axis=0) if len(parts) > 1 else parts[0]


def forward_kernel(
    words, rows, ent_pos, segments, ent_proj, pos_table, query_weight, query_bias, key_weight, key_bias, value_weight, value_bias,
    ent_hidden, hidden_low, query_words, query_ents, keys, values, probs, mixed,
    query_here, key_here, value_here, values_turned, mask, mixed_turned, local_sem,
):
    y = lax.axis_index("seq") // 2
    half = keys.shape[1]
    all_words, ents = words.shape[0], rows.shape[0]
    tokens = all_words + ents
    columns = span(y * half, half, LANES)
    weight_copies = [
        pltpu.make_async_copy(query_weight.at[:, :, columns], query_here, local_sem.at[0]),
        pltpu.make_async_copy(key_weight.at[:, columns], key_here, local_sem.at[1]),
        pltpu.make_async_copy(value_weight.at[:, columns], value_here, local_sem.at[2]),
    ]
    for copy in weight_copies:
        copy.start()
    position = as_column(ent_pos[...])
    picks = []
    for j in range(all_words // LANES):
        number = lax.broadcasted_iota(jnp.int32, (ents, LANES), 1) + j * LANES
        picks.append(jnp.where(position == number, 1.0, 0.0))
    pick = jnp.concatenate(picks, axis=1)
    word_seg = segments[...].astype(F32)
    ent_seg = jnp.sum(pick * word_seg, axis=1, keepdims=True)
    ent_hidden[...] = dot(rows[...], ent_proj[...]) + dot(pick.astype(LOW), pos_table[...])
    hidden_low[:all_words] = words[...]
    hidden_low[all_words:] = ent_hidden[...].astype(LOW)
    ent_row = jnp.transpose(jnp.broadcast_to(ent_seg, (ents, LANES)))[:1]
    seg_row = jnp.concatenate([word_seg, ent_row], axis=1)
    seg_column = jnp.concatenate([as_column(word_seg), jnp.broadcast_to(ent_seg, (ents, LANES))], axis=0)
    for j in range(tokens // LANES):
        here = slice(j * LANES, (j + 1) * LANES)
        mask[:, here] = jnp.where(seg_column == seg_row[:, here], 0.0, masked_score)

    query_b = query_bias[:, columns].astype(F32)
    for copy in weight_copies:
        copy.wait()
    word_low, ent_low = hidden_low[:all_words], hidden_low[all_words:]
    query_words[:all_words] = (dot(word_low, query_here[0]) + query_b[0:1]).astype(LOW)
    query_ents[:all_words] = (dot(word_low, query_here[1]) + query_b[1:2]).astype(LOW)
    query_words[all_words:] = (dot(ent_low, query_here[2]) + query_b[2:3]).astype(LOW)
    query_ents[all_words:] = (dot(ent_low, query_here[3]) + query_b[3:4]).astype(LOW)
    keys[...] = (dot(hidden_low[...], key_here[...]) + key_bias[:, columns].astype(F32)).astype(LOW)
    value = dot(hidden_low[...], value_here[...]) + value_bias[:, columns].astype(F32)
    values[...] = value.astype(LOW)
    values_turned[...] = jnp.transpose(value).astype(LOW)
    scale = 1.0 / math.sqrt(HEAD)
    tiles = tokens // LANES

    def tile(i, _):
        pair, place = i // tiles, span((i % tiles) * LANES, LANES, LANES)
        lanes = span(pair * LANES, LANES, LANES)
        key = keys[:, lanes]
        query_w, query_e = query_words[place, lanes], query_ents[place, lanes]
        turned = values_turned[lanes, :]
        total = jnp.zeros((LANES, LANES), F32)
        for head in range(2):
            own_key = jnp.where(lane_mask(tokens, head), key, jnp.zeros_like(key))
            raw = jnp.concatenate(
                [dot_rows(own_key[:all_words], query_w), dot_rows(own_key[all_words:], query_e)], axis=0
            )
            score = raw * scale + mask[:, place]
            weight = jnp.exp(score - jnp.max(score, axis=0, keepdims=True))
            prob = (weight * (1.0 / jnp.sum(weight, axis=0, keepdims=True))).astype(LOW)
            probs[pair * 2 + head, :, place] = prob
            row = lax.broadcasted_iota(jnp.int32, (LANES, tokens), 0)
            own_rows = (row >= head * HEAD) & (row < (head + 1) * HEAD)
            total = total + dot(jnp.where(own_rows, turned, jnp.zeros_like(turned)), prob)
        mixed[place, lanes] = jnp.transpose(total).astype(LOW)
        return 0

    loop(half // LANES * tiles, tile)


def forward(words, rows, ent_pos, segments, ent_proj, pos_table, query_weight, query_bias, key_weight, key_bias, value_weight, value_bias):
    all_words, width = words.shape
    ents = rows.shape[0]
    tokens, half = all_words + ents, width // 2
    return call(
        forward_kernel,
        [
            ((ents, width), F32),
            ((tokens, width), LOW),
            ((tokens, half), LOW),
            ((tokens, half), LOW),
            ((tokens, half), LOW),
            ((tokens, half), LOW),
            ((HEADS // 2, tokens, tokens), LOW),
            ((tokens, half), LOW),
        ],
        [IN_VMEM] * 6 + [ANY, IN_VMEM, ANY, IN_VMEM, ANY, IN_VMEM],
        [IN_VMEM] * 8,
        [
            pltpu.VMEM((4, width, half), LOW),
            pltpu.VMEM((width, half), LOW),
            pltpu.VMEM((width, half), LOW),
            pltpu.VMEM((half, tokens), LOW),
            pltpu.VMEM((tokens, tokens), F32),
            pltpu.VMEM((LANES, tokens), F32),
            pltpu.SemaphoreType.DMA((3,)),
        ],
        "forward",
    )(words, rows, ent_pos, segments, ent_proj, pos_table, query_weight, query_bias, key_weight, key_bias, value_weight, value_bias)


ROW_BLOCK = 32


def lane_mean(value):
    return jnp.mean(value, axis=-1, keepdims=True)


def column_sum(value):
    return jnp.sum(value, axis=0, keepdims=True)


class Several:
    def __init__(self, copies):
        self.copies = copies

    def wait(self):
        for copy in self.copies:
            copy.wait()


def middle_kernel(
    nz, words, ent_hidden, mixed, out_weight, out_bias, gains, shifts, up_weight, up_bias, down_weight, down_bias, word_cots, ent_cots,
    word_out, ent_out, grad_one, grad_mixed, grads, bias_out,
    out_here, up_here, down_here, mixed_full, from_y, hidden, work, normed, normed_low, normal_one, inverse_one,
    act, slope, output, cot, grad_two, grad_two_low, grad_up_low, grad_one_low, grad_mixed_here, stage, down_stage, send_sem, recv_sem, local_sem,
):
    copies = Copies(send_sem, recv_sem, local_sem)
    place = Place(nz)
    y, core = place.y, place.core
    n_dp = 2 * nz
    all_words, width = words.shape
    ents = ent_hidden.shape[0]
    half = mixed.shape[1]
    word_half, ent_half = all_words // 2, ents // 2
    tokens = word_half + ent_half
    ff = up_weight.shape[1]
    parts = ff // width
    meet([place.other_core, place.other_y])

    def token_rows(side):
        return span(side * word_half, word_half, LANES), span(all_words + side * ent_half, ent_half, 64)

    mine, theirs = token_rows(y), token_rows(1 - y)
    mixed_copies = [
        copies.send(mixed.at[theirs[0]], from_y.at[pl.ds(0, word_half)], place.other_y),
        copies.send(mixed.at[theirs[1]], from_y.at[pl.ds(word_half, ent_half)], place.other_y),
    ]
    weight_copies = [
        copies.local(out_weight, out_here),
        copies.local(up_weight, up_here),
        copies.local(down_weight, down_here),
    ]
    cot_copies = [
        copies.local(word_cots, cot.at[pl.ds(0, word_half)]),
        copies.local(ent_cots, cot.at[pl.ds(word_half, ent_half)]),
    ]
    gain, shift = gains[...].astype(F32), shifts[...].astype(F32)
    out_b, down_b, up_b = out_bias[...].astype(F32), down_bias[...].astype(F32), up_bias[...].astype(F32)
    hidden[:word_half] = words[mine[0]].astype(F32)
    hidden[word_half:] = ent_hidden[span(y * ent_half, ent_half, 64)]
    own_columns, other_columns = span(y * half, half, LANES), span((1 - y) * half, half, LANES)
    mixed_full[:word_half, own_columns] = mixed[mine[0]]
    mixed_full[word_half:, own_columns] = mixed[mine[1]]
    for copy in mixed_copies:
        copy.wait_recv()
    mixed_full[:, other_columns] = from_y[...]
    weight_copies[0].wait()
    work[...] = dot(mixed_full[...], out_here[...])
    blocks = tokens // ROW_BLOCK

    def norm_one(i, _):
        rows = span(i * ROW_BLOCK, ROW_BLOCK, ROW_BLOCK)
        value = hidden[rows] + (work[rows] + out_b)
        center = value - lane_mean(value)
        inverse = lax.rsqrt(lane_mean(center * center) + norm_eps)
        normal = center * inverse
        result = normal * gain[0:1] + shift[0:1]
        normal_one[rows] = normal
        inverse_one[rows] = jnp.broadcast_to(inverse, (ROW_BLOCK, LANES))
        normed[rows] = result
        normed_low[rows] = result.astype(LOW)
        return 0

    loop(blocks, norm_one)
    weight_copies[1].wait()
    weight_copies[2].wait()
    for j in range(parts):
        columns = slice(j * width, (j + 1) * width)
        work[...] = dot(normed_low[...], up_here[:, columns]) + up_b[:, columns]

        def gelu(i, _):
            rows = span(i * 16, 16, 16)
            value = work[rows]
            below = 0.5 * (1.0 + lax.erf(value * (1.0 / math.sqrt(2.0))))
            density = jnp.exp(-0.5 * value * value) * (1.0 / math.sqrt(2.0 * math.pi))
            act[rows, columns] = (value * below).astype(LOW)
            slope[rows, columns] = below + value * density
            return 0

        loop(tokens // 16, gelu)
    for copy in cot_copies:
        copy.wait()
    work[...] = dot(act[...], down_here[...])

    def norm_two(i, sums):
        rows = span(i * ROW_BLOCK, ROW_BLOCK, ROW_BLOCK)
        value = normed[rows] + (work[rows] + down_b)
        center = value - lane_mean(value)
        inverse = lax.rsqrt(lane_mean(center * center) + norm_eps)
        normal = center * inverse
        output[rows] = (normal * gain[1:2] + shift[1:2]).astype(LOW)
        given = cot[rows].astype(F32)
        scaled = given * gain[1:2]
        result = inverse * (scaled - lane_mean(scaled) - normal * lane_mean(scaled * normal))
        grad_two[rows] = result
        grad_two_low[rows] = result.astype(LOW)
        return (
            sums[0] + column_sum(given * normal),
            sums[1] + column_sum(given),
            sums[2] + column_sum(result),
        )

    nothing = jnp.zeros((1, width), F32)
    gain_two, shift_two, down_sum = loop(blocks, norm_two, (nothing, nothing, nothing))
    own_quarter = span(core * (word_half // 2), word_half // 2, LANES)
    other_quarter = span((1 - core) * (word_half // 2), word_half // 2, LANES)
    ent_quarter = ent_half // 2
    own_ents = span(word_half + core * ent_quarter, ent_quarter, 32)
    other_ents = span(word_half + (1 - core) * ent_quarter, ent_quarter, 32)
    out_copies = [
        copies.send(output.at[other_quarter], word_out.at[core], place.other_core),
        copies.send(output.at[other_ents], ent_out.at[core], place.other_core),
    ]
    out_local = [
        copies.local(output.at[own_quarter], word_out.at[core]),
        copies.local(output.at[own_ents], ent_out.at[core]),
    ]
    down_rows, row_part, row_pad = ff // n_dp, width // n_dp, padded(width // n_dp)
    staged = [None, None]
    turn = [0]

    def put_out(value, base, rows_in):
        slot = turn[0] % 2
        turn[0] += 1
        if staged[slot] is not None:
            staged[slot].wait()
        value = value.astype(LOW).reshape(nz, 2, rows_in, width)
        stage[slot, :, :, pl.ds(0, rows_in)] = value
        size = padded(rows_in)
        staged[slot] = copies.local(stage.at[slot, :, :, pl.ds(0, size)], grads.at[:, :, pl.ds(base, size)])

    down_staged = [None, None]
    for j in range(parts):
        columns = slice(j * width, (j + 1) * width)
        value = dot_columns(act[:, columns], grad_two_low[...]).astype(LOW)
        if down_staged[j % 2] is not None:
            down_staged[j % 2].wait()
        down_stage[j % 2] = value
        per = width // down_rows
        down_staged[j % 2] = Several([
            copies.local(
                down_stage.at[j % 2, pl.ds(d * down_rows, down_rows)],
                grads.at[(j * per + d) // 2, (j * per + d) % 2, pl.ds(0, down_rows)],
            )
            for d in range(per)
        ])
    up_sums = []
    for j in range(parts):
        columns = slice(j * width, (j + 1) * width)
        work[...] = dot_rows(grad_two_low[...], down_here[columns, :])

        def grad_gelu(i, total):
            rows = span(i * 16, 16, 16)
            value = work[rows] * slope[rows, columns]
            grad_up_low[rows, columns] = value.astype(LOW)
            return total + column_sum(value)

        up_sums.append(loop(tokens // 16, grad_gelu, nothing))
        put_out(dot_columns(normed_low[...], grad_up_low[:, columns]), down_rows + j * row_pad, row_part)
    work[...] = dot_rows(grad_up_low[...], up_here[...])

    def back_one(i, sums):
        rows = span(i * ROW_BLOCK, ROW_BLOCK, ROW_BLOCK)
        given = grad_two[rows] + work[rows]
        normal = normal_one[rows]
        inverse = inverse_one[rows, 0:1]
        scaled = given * gain[0:1]
        result = inverse * (scaled - lane_mean(scaled) - normal * lane_mean(scaled * normal))
        grad_one[rows] = result
        grad_one_low[rows] = result.astype(LOW)
        return (
            sums[0] + column_sum(given * normal),
            sums[1] + column_sum(given),
            sums[2] + column_sum(result),
        )

    gain_one, shift_one, out_sum = loop(blocks, back_one, (nothing, nothing, nothing))
    other_out = out_here[other_columns, :]
    grad_mixed_here[1] = dot_rows(grad_one_low[...], other_out).astype(LOW)
    mixed_back = [
        copies.send(grad_mixed_here.at[1, pl.ds(0, word_half)], grad_mixed.at[mine[0]], place.other_y),
        copies.send(grad_mixed_here.at[1, pl.ds(word_half, ent_half)], grad_mixed.at[mine[1]], place.other_y),
    ]
    grad_mixed_here[0] = dot_rows(grad_one_low[...], out_here[own_columns, :]).astype(LOW)
    mixed_own = [
        copies.local(grad_mixed_here.at[0, pl.ds(0, word_half)], grad_mixed.at[mine[0]]),
        copies.local(grad_mixed_here.at[0, pl.ds(word_half, ent_half)], grad_mixed.at[mine[1]]),
    ]
    put_out(dot_columns(mixed_full[...], grad_one_low[...]), down_rows + parts * row_pad, row_part)
    bias_rows = [out_sum, gain_one, gain_two, shift_one, shift_two] + up_sums + [down_sum]
    for i, row in enumerate(bias_rows):
        bias_out[i : i + 1] = row
    for copy in staged + down_staged:
        copy.wait()
    for copy in mixed_back + out_copies:
        copy.wait_recv()
    for copy in mixed_own + out_local:
        copy.wait()
    copies.finish()


def middle(nz, words, ent_hidden, mixed, out_weight, out_bias, gains, shifts, up_weight, up_bias, down_weight, down_bias, word_cots, ent_cots):
    n_dp = 2 * nz
    all_words, width = words.shape
    ents, half, ff = ent_hidden.shape[0], mixed.shape[1], up_weight.shape[1]
    tokens = (all_words + ents) // 2
    parts = ff // width
    row_pad = padded(width // n_dp)
    slab = ff // n_dp + (parts + 1) * row_pad
    return call(
        functools.partial(middle_kernel, nz),
        [
            ((2, all_words // 4, width), LOW),
            ((2, ents // 4, width), LOW),
            ((tokens, width), F32),
            ((all_words + ents, half), LOW),
            ((nz, 2, slab, width), LOW),
            ((6 + parts, width), F32),
        ],
        [IN_VMEM] * 3 + [ANY] + [IN_VMEM] * 3 + [ANY, IN_VMEM, ANY, IN_VMEM, ANY, ANY],
        [ANY, ANY, IN_VMEM, ANY, ANY, IN_VMEM],
        [
            pltpu.VMEM((width, width), LOW),
            pltpu.VMEM((width, ff), LOW),
            pltpu.VMEM((ff, width), LOW),
            pltpu.VMEM((tokens, width), LOW),
            pltpu.VMEM((tokens, half), LOW),
            pltpu.VMEM((tokens, width), F32),
            pltpu.VMEM((tokens, width), F32),
            pltpu.VMEM((tokens, width), F32),
            pltpu.VMEM((tokens, width), LOW),
            pltpu.VMEM((tokens, width), F32),
            pltpu.VMEM((tokens, LANES), F32),
            pltpu.VMEM((tokens, ff), LOW),
            pltpu.VMEM((tokens, ff), F32),
            pltpu.VMEM((tokens, width), LOW),
            pltpu.VMEM((tokens, width), LOW),
            pltpu.VMEM((tokens, width), F32),
            pltpu.VMEM((tokens, width), LOW),
            pltpu.VMEM((tokens, ff), LOW),
            pltpu.VMEM((tokens, width), LOW),
            pltpu.VMEM((2, tokens, half), LOW),
            pltpu.VMEM((2, nz, 2, row_pad, width), LOW),
            pltpu.VMEM((2, width, width), LOW),
        ]
        + copy_semaphores(8, 40 + 4 * n_dp),
        "middle",
        2,
    )(words, ent_hidden, mixed, out_weight, out_bias, gains, shifts, up_weight, up_bias, down_weight, down_bias, word_cots, ent_cots)


class Engine:
    RATES = {"core": 300e3, "x": 50e3, "y": 50e3, "z": 12.5e3}
    LATENCY = 1.5

    def __init__(self):
        self.clock, self.free, self.streams = 0.0, {}, []

    def transfer(self, link, size):
        start = max(self.clock, self.free.get(link, 0.0))
        self.free[link] = start + size / self.RATES[link]
        return self.free[link] + self.LATENCY

    def add(self, steps):
        self.streams.append([self.clock, list(steps)])
        self.poll()

    def run(self, stream):
        self.clock = max(self.clock, stream[0])
        ready = stream[1].pop(0)()
        stream[0] = self.clock if ready is None else ready

    def next(self):
        live = [stream for stream in self.streams if stream[1]]
        return min(live, key=lambda stream: stream[0]) if live else None

    def poll(self):
        while (stream := self.next()) is not None and stream[0] <= self.clock:
            self.run(stream)

    def work(self, time):
        self.clock += time
        self.poll()

    def drain(self):
        while (stream := self.next()) is not None:
            self.run(stream)


def blocks_of(rows):
    for size in (96, 64, 48, 32):
        if rows % size == 0:
            return size
    return 16


def add_blocks(engine, target, parts, leading, rows, columns):
    size = blocks_of(rows)
    count = rows // size

    def block(i, _):
        lead, row = i // count, (i % count) * size
        where = span(row, size, 16)
        if len(parts) == 2:
            value = parts[0](lead, where) + parts[1](lead, where)
        else:
            value = parts[0](lead, where).astype(F32)
            for part in parts[1:]:
                value = value + part(lead, where).astype(F32)
            value = value.astype(LOW)
        target(lead, where, value)
        return 0

    loop(leading * count, block)
    engine.clock += 0.3 + leading * rows * columns / 1e6


class Job:
    def __init__(self, grads, reduced, base, size, order, columns, resident):
        self.grads, self.reduced, self.base, self.size, self.order, self.columns = grads, reduced, base, size, order, columns
        self.resident = resident
        self.half = size // 2
        self.part = size // 4 if order == "yxz" else size // 2

    def scratch(self, nz):
        shapes = [(nz, 2, self.half, self.columns)] * (1 if self.resident else 2)
        if self.order == "yxz":
            shapes.append((nz, 2, self.part, self.columns))
        elif self.order == "xzy":
            shapes.append((2, self.part, self.columns))
        shapes += [(nz, self.part, self.columns), (nz - 1, self.part, self.columns)]
        return [pltpu.VMEM(shape, LOW) for shape in shapes]

    def remote_count(self, nz):
        return 1 + (1 if self.order != "xz" else 0) + 1 + (nz - 1) + 1 + 1

    def steps(self, engine, place, copies, scratch):
        nz, z, x, y, core = place.nz, place.z, place.x, place.y, place.core
        base, half, part, order, columns = self.base, self.half, self.part, self.order, self.columns
        if self.resident:
            scratch = [self.grads.at[:, :, span(base + core * half, half, 16)]] + list(scratch)
        held, from_core = scratch[:2]
        from_y = scratch[2] if order != "xz" else None
        from_x, from_z = scratch[-2:]
        live = {}
        row_bytes = 2 * columns

        def start():
            theirs, own = span(base + (1 - core) * half, half, 16), span(base + core * half, half, 16)
            live["core"] = copies.send(self.grads.at[:, :, theirs], from_core, place.other_core)
            if not self.resident:
                live["own"] = copies.local(self.grads.at[:, :, own], held)
            return engine.transfer("core", 2 * nz * half * row_bytes)

        own_rows = span(y * part, part, 16) if order == "yxz" else pl.ds(0, part)
        final_rows = span(base + core * half + (y * part if order == "yxz" else 0), part, 16)

        def send_x():
            live["x"] = copies.send(held.at[:, 1 - x, own_rows], from_x, place.other_x)
            return engine.transfer("x", nz * part * row_bytes)

        def after_core():
            if not self.resident:
                live["own"].wait()
            live["core"].wait_recv()

            def put(i, where, value):
                held[i // 2, i % 2, where] = value

            add_blocks(
                engine,
                put,
                [lambda i, where: held[i // 2, i % 2, where], lambda i, where: from_core[i // 2, i % 2, where]],
                2 * nz,
                half,
                columns,
            )
            if order == "yxz":
                live["y"] = copies.send(held.at[:, :, span((1 - y) * part, part, 16)], from_y, place.other_y)
                return engine.transfer("y", 2 * nz * part * row_bytes)
            return send_x()

        def shifted(where):
            return span(y * part + where.start, where.size, 16) if order == "yxz" else where

        def after_y():
            live["y"].wait_recv()

            def put(i, where, value):
                held[i // 2, i % 2, shifted(where)] = value

            add_blocks(
                engine,
                put,
                [lambda i, where: held[i // 2, i % 2, shifted(where)], lambda i, where: from_y[i // 2, i % 2, where]],
                2 * nz,
                part,
                columns,
            )
            return send_x()

        def after_x():
            live["x"].wait_recv()

            def put(i, where, value):
                held[i, x, shifted(where)] = value

            add_blocks(
                engine,
                put,
                [lambda i, where: held[i, x, shifted(where)], lambda i, where: from_x[i, where]],
                nz,
                part,
                columns,
            )
            live["z"] = [
                copies.send(held.at[place.z_ahead(k + 1), x, own_rows], from_z.at[k], device)
                for k, device in enumerate(place.ahead)
            ]
            return engine.transfer("z", part * row_bytes)

        def after_z():
            for copy in live["z"]:
                copy.wait_recv()

            def put(i, where, value):
                if order == "yxz":
                    self.reduced[span(base + core * half + y * part + where.start, where.size, 16)] = value
                elif order == "xz":
                    self.reduced[y, span(base + core * half + where.start, where.size, 16)] = value
                else:
                    from_y[0, where] = value

            def parts(k):
                return lambda i, where: from_z[k, where]

            add_blocks(
                engine,
                put,
                [lambda i, where: held[z, x, shifted(where)]] + [parts(k) for k in range(nz - 1)],
                1,
                part,
                columns,
            )
            if order == "yxz":
                view = self.reduced.at[final_rows]
                live["y2"] = copies.send(view, view, place.other_y)
            elif order == "xz":
                view = self.reduced.at[y, final_rows]
                live["y2"] = copies.send(view, view, place.other_y)
            else:
                live["y2"] = copies.send(from_y.at[0], from_y.at[1], place.other_y)
            return engine.transfer("y", part * row_bytes)

        def after_gather():
            live["y2"].wait_recv()
            mine = span(base + core * half, half, 16)
            if order == "xzy":

                def put(i, where, value):
                    self.reduced[span(base + core * half + where.start, where.size, 16)] = value

                add_blocks(
                    engine, put, [lambda i, where: from_y[0, where], lambda i, where: from_y[1, where]], 1, part, columns
                )
            view = self.reduced.at[:, mine] if order == "xz" else self.reduced.at[mine]
            live["core2"] = copies.send(view, view, place.other_core)
            return engine.transfer("core", 2 * half * row_bytes)

        def end():
            live["core2"].wait_recv()

        middle_steps = [after_core, after_y, after_x] if order == "yxz" else [after_core, after_x]
        return [start] + middle_steps + [after_z, after_gather, end]


def job_spans(rows):
    spans, base, turn = [], 0, 0
    while base < rows:
        size, order = ((192, "yxz"), (96, "xzy"))[turn % 2]
        if base + size > rows:
            size = rows - base
            order = "yxz" if size % 64 == 0 else "xzy"
        if order == "yxz" and size == 192:
            spans += [(base, 128, order), (base + 128, 64, order)]
        else:
            spans.append((base, size, order))
        base += size
        turn += 1
    return spans


def backward_kernel(
    nz, all_words, plan, hidden_low, query_words, query_ents, keys, values, probs, grad_mixed, query_weight, key_weight, value_weight,
    ffn_grads, grad_one, rows, ent_pos, ent_proj, bias_middle, ids,
    word_grad, ffn_reduced, attn_reduced, ent_reduced, bias_out, table_grad, touched, *scratch,
):
    (query_here, key_here, value_here, keys_turned, grad_scores, grad_query_words, grad_query_ents, grad_keys, grad_values, hidden_turned,
     grad_hidden, attn_grads, bias_heads, given, total, ent_grads, ffn_sum, attn_sum, ent_sum, bias_held, bias_from, all_rows, hits,
    ) = scratch[:23]
    copies = Copies(*scratch[-3:])
    engine = Engine()
    place = Place(nz)
    z, x, y, core = place.z, place.x, place.y, place.core
    n_dp = 2 * nz
    tokens, half = keys.shape
    width = hidden_low.shape[1]
    ents = tokens - all_words
    word_half, ent_half = all_words // 2, ents // 2
    meet([place.other_core, place.other_y, place.other_x] + place.ahead)
    jobs, at = [], 23
    sources = {"ffn": (ffn_grads, ffn_sum), "attn": (attn_grads, attn_sum), "ent": (ent_grads, ent_sum)}
    for name, base, size, order, columns in plan:
        job = Job(*sources[name], base, size, order, columns, name != "ffn")
        used = len(job.scratch(nz))
        jobs.append((name, job.steps(engine, place, copies, scratch[at : at + used])))
        at += used
    for name, steps in jobs:
        if name == "ffn":
            engine.add(steps)
    columns = span(y * half, half, LANES)
    weight_copies = [
        copies.local(query_weight.at[:, :, columns], query_here),
        copies.local(key_weight.at[:, columns], key_here),
        copies.local(value_weight.at[:, columns], value_here),
    ]
    for i in range(half // LANES):
        lanes = slice(i * LANES, (i + 1) * LANES)
        keys_turned[lanes, :] = jnp.transpose(keys[:, lanes].astype(F32)).astype(LOW)
    for i in range(width // LANES):
        lanes = slice(i * LANES, (i + 1) * LANES)
        hidden_turned[lanes, :] = jnp.transpose(hidden_low[:, lanes].astype(F32)).astype(LOW)
    engine.work(2.0)
    scale = 1.0 / math.sqrt(HEAD)
    tiles = tokens // LANES

    for pair in range(half // LANES):
        lanes = slice(pair * LANES, (pair + 1) * LANES)
        grad_query_w = jnp.zeros((LANES, tokens), F32)
        grad_query_e = jnp.zeros((LANES, tokens), F32)
        grad_key_w = jnp.zeros((all_words, LANES), F32)
        grad_key_e = jnp.zeros((ents, LANES), F32)
        grad_value = jnp.zeros((tokens, LANES), F32)
        for head in range(2):
            own = lane_mask(tokens, head)
            value = values[:, lanes]
            own_value = jnp.where(own, value, jnp.zeros_like(value))

            def tile(i, _):
                where = span(i * LANES, LANES, LANES)
                grad_prob = dot_rows(own_value, grad_mixed[where, lanes])
                prob = probs[pair * 2 + head, :, where].astype(F32)
                both = prob * grad_prob
                grad_scores[:, where] = (both - prob * jnp.sum(both, axis=0, keepdims=True)).astype(LOW)
                return 0

            loop(tiles, tile)
            engine.work(1.7)
            given_heads = grad_mixed[:, lanes]
            grad_value += dot(probs[pair * 2 + head], jnp.where(own, given_heads, jnp.zeros_like(given_heads)))
            query_w, query_e = query_words[:, lanes], query_ents[:, lanes]
            grad_key_w += dot(grad_scores[:all_words], jnp.where(own, query_w, jnp.zeros_like(query_w)))
            grad_key_e += dot(grad_scores[all_words:], jnp.where(own, query_e, jnp.zeros_like(query_e)))
            row = lax.broadcasted_iota(jnp.int32, (LANES, tokens), 0)
            own_rows = (row >= head * HEAD) & (row < (head + 1) * HEAD)
            turned = keys_turned[lanes, :]
            turned = jnp.where(own_rows, turned, jnp.zeros_like(turned))
            grad_query_w += dot(turned[:, :all_words], grad_scores[:all_words])
            grad_query_e += dot(turned[:, all_words:], grad_scores[all_words:])
            engine.work(1.7)
        grad_query_w = jnp.transpose(grad_query_w) * scale
        grad_query_e = jnp.transpose(grad_query_e) * scale
        grad_key_w, grad_key_e = grad_key_w * scale, grad_key_e * scale
        sums = [
            column_sum(grad_query_w[:all_words]),
            column_sum(grad_query_e[:all_words]),
            column_sum(grad_query_w[all_words:]),
            column_sum(grad_query_e[all_words:]),
            column_sum(grad_key_w) + column_sum(grad_key_e),
            column_sum(grad_value),
        ]
        for i, sum_row in enumerate(sums):
            bias_heads[i : i + 1, lanes] = sum_row
        grad_query_words[:, lanes] = grad_query_w.astype(LOW)
        grad_query_ents[:, lanes] = grad_query_e.astype(LOW)
        grad_keys[:all_words, lanes] = grad_key_w.astype(LOW)
        grad_keys[all_words:, lanes] = grad_key_e.astype(LOW)
        grad_values[:, lanes] = grad_value.astype(LOW)
        engine.work(0.5)

    for copy in weight_copies:
        copy.wait()
    theirs = span((1 - y) * word_half, word_half, LANES), span(all_words + (1 - y) * ent_half, ent_half, 64)
    ent_rows, word_rows = slice(all_words, tokens), slice(0, all_words)

    def hidden_part(here, first, second):
        grad_hidden[here] = (
            dot_rows(grad_keys[here], key_here[...])
            + dot_rows(grad_values[here], value_here[...])
            + dot_rows(grad_query_words[here], query_here[first])
            + dot_rows(grad_query_ents[here], query_here[second])
        ).astype(LOW)

    hidden_part(ent_rows, 2, 3)
    ent_copy = copies.send(grad_hidden.at[theirs[1]], given.at[pl.ds(word_half, ent_half)], place.other_y)
    ent_ready = engine.transfer("y", ent_half * width * 2)
    engine.work(0.7)
    row_part, row_pad = width // n_dp, padded(width // n_dp)
    word_turned, ent_turned = hidden_turned[:, :all_words], hidden_turned[:, all_words:]
    attn_jobs = [steps for name, steps in jobs if name == "attn"]

    def attn_product(i, value):
        attn_grads[:, :, pl.ds(i * row_pad, row_part)] = value.astype(LOW).reshape(nz, 2, row_part, half)
        per = 6 // len(attn_jobs)
        if i % per == per - 1:
            engine.add(attn_jobs[i // per])
        engine.work(0.6)

    attn_product(0, dot(word_turned, grad_query_words[:all_words]))
    attn_product(1, dot(word_turned, grad_query_ents[:all_words]))
    hidden_part(word_rows, 0, 1)
    word_copy = copies.send(grad_hidden.at[theirs[0]], given.at[pl.ds(0, word_half)], place.other_y)
    word_ready = engine.transfer("y", word_half * width * 2)
    engine.work(1.5)

    bias_rows = bias_held.shape[0]
    bias_held[...] = jnp.zeros_like(bias_held)
    bias_held[0:6, span(y * half, half, LANES)] = bias_heads[0:6]
    bias_held[6:bias_rows] = bias_middle[...]
    live = {}
    bias_bytes = bias_rows * width * 2

    def bias_send(key, index, device):
        bias_from[2 * index] = bias_held[...].astype(LOW)
        live[key] = copies.send(bias_from.at[2 * index], bias_from.at[2 * index + 1], device)
        return engine.transfer(key, bias_bytes)

    def bias_take(key, index):
        live[key].wait_recv()
        bias_held[...] = bias_from[2 * index].astype(F32) + bias_from[2 * index + 1].astype(F32)

    def bias_core():
        return bias_send("core", 0, place.other_core)

    def bias_y():
        bias_take("core", 0)
        return bias_send("y", 1, place.other_y)

    def bias_x():
        bias_take("y", 1)
        return bias_send("x", 2, place.other_x)

    def bias_z():
        bias_take("x", 2)
        bias_from[6] = bias_held[...].astype(LOW)
        live["z"] = [copies.send(bias_from.at[6], bias_from.at[7 + k], device) for k, device in enumerate(place.ahead)]
        return engine.transfer("z", bias_bytes)

    def bias_end():
        value = bias_from[6].astype(F32)
        for k, copy in enumerate(live["z"]):
            copy.wait_recv()
            value = value + bias_from[7 + k].astype(F32)
        bias_out[...] = value

    live_rows = {}

    def sum_hidden(start, count, own_start):
        def block(i, _):
            where = span(start + i * 32, 32, 32)
            own = span(own_start + i * 32, 32, 32)
            total[where] = grad_one[where] + (grad_hidden[own].astype(F32) + given[where].astype(F32))
            return 0

        loop(count // 32, block)

    row_bytes = ent_half * ent_proj.shape[0] * 2

    def rows_y():
        ent_copy.wait_recv()
        sum_hidden(word_half, ent_half, all_words + y * ent_half)
        row_grad = dot_rows(total[word_half:].astype(LOW), ent_proj[...]).astype(LOW)
        all_rows[place.dp, core, span(y * ent_half, ent_half, 64)] = row_grad
        view = all_rows.at[place.dp, core, span(y * ent_half, ent_half, 64)]
        live_rows["y"] = copies.send(view, view, place.other_y)
        return engine.transfer("y", row_bytes)

    def rows_z():
        live_rows["y"].wait_recv()
        view = all_rows.at[place.dp, core]
        live_rows["z"] = [copies.send(view, view, device) for device in place.ahead]
        return engine.transfer("z", 2 * row_bytes)

    def rows_x():
        for copy in live_rows["z"]:
            copy.wait_recv()
        live_rows["x"] = []
        for k in range(nz):
            view = all_rows.at[place.z_ahead(k) * 2 + x, core]
            live_rows["x"].append(copies.send(view, view, place.other_x))
        return engine.transfer("x", nz * 2 * row_bytes)

    def rows_core():
        for copy in live_rows["x"]:
            copy.wait_recv()
        view = all_rows.at[:, core]
        live_rows["core"] = copies.send(view, view, place.other_core)
        return engine.transfer("core", n_dp * 2 * row_bytes)

    rows_dev = table_grad.shape[0]
    table_block = hits.shape[0]
    base_row = (place.dp * 4 + place.seq) * rows_dev
    table_copies = []

    def table_part(i):
        def step():
            if i == 0:
                live_rows["core"].wait_recv()
            groups = ids.shape[0]
            number = lax.broadcasted_iota(jnp.int32, (table_block, ents), 0) + (base_row + i * table_block)
            count = jnp.zeros((table_block, ents), F32)
            for group in range(groups):
                hit = jnp.where(ids[group : group + 1, :] == number, 1.0, 0.0)
                count = count + hit
                hits[:, group * ents : (group + 1) * ents] = hit.astype(LOW)
            here = pl.ds(i * table_block, table_block)
            dps = min(n_dp, 8)
            grad = None
            for first in range(0, n_dp, dps):
                given_rows = all_rows[first : first + dps].reshape(dps * 2 * ents, ent_proj.shape[0])
                part = dot(hits[:, first * 2 * ents : (first + dps) * 2 * ents], given_rows)
                grad = part if grad is None else grad + part
            table_grad[here] = grad
            named = jnp.sum(count, axis=1, keepdims=True)
            touched[here] = jnp.broadcast_to(named, (table_block, LANES)).astype(LOW)
            engine.clock += 1.2

        return step

    engine.add([lambda: ent_ready, rows_y, rows_z, rows_x, rows_core] + [table_part(i) for i in range(rows_dev // table_block)])
    engine.add([bias_core, bias_y, bias_x, bias_z, bias_end])
    attn_product(2, dot(ent_turned, grad_query_words[all_words:]))
    attn_product(3, dot(ent_turned, grad_query_ents[all_words:]))
    attn_product(4, dot(hidden_turned[...], grad_keys[...]))
    attn_product(5, dot(hidden_turned[...], grad_values[...]))
    quarter = word_half // 2
    own_quarter = span(core * quarter, quarter, LANES)
    other_quarter = span((1 - core) * quarter, quarter, LANES)
    live_words = {}

    def words_sum():
        word_copy.wait_recv()
        sum_hidden(0, word_half, y * word_half)
        engine.clock += 0.5
        live_words["send"] = copies.send(total.at[other_quarter], word_grad.at[core], place.other_core)
        live_words["own"] = copies.local(total.at[own_quarter], word_grad.at[core])
        return engine.transfer("core", quarter * width * 4)

    def words_end():
        live_words["send"].wait_recv()
        live_words["own"].wait()

    engine.add([lambda: word_ready, words_sum, words_end])

    def ent_part():
        proj_rows, pos_rows = rows.shape[1] // n_dp, all_words // n_dp
        proj_pad = padded(proj_rows)
        picks = []
        for j in range(all_words // LANES):
            number = lax.broadcasted_iota(jnp.int32, (LANES, ents), 0) + j * LANES
            picks.append(jnp.where(number == ent_pos[...], 1.0, 0.0))
        pick = jnp.concatenate(picks, axis=0)
        here = lax.broadcasted_iota(jnp.int32, (all_words, ents), 1) // ent_half == y
        pick = jnp.where(here, pick, 0.0).astype(LOW)
        grad_ent = total[word_half:]
        grad_ent_low = grad_ent.astype(LOW)
        rest = (grad_ent - grad_ent_low.astype(F32)).astype(LOW)
        pos_grad = dot(pick, jnp.concatenate([grad_ent_low, grad_ent_low], axis=0)) + dot(
            pick, jnp.concatenate([rest, rest], axis=0)
        )
        proj_grad = dot_columns(rows[span(y * ent_half, ent_half, 64)], grad_ent_low)
        ent_grads[:, :, pl.ds(0, proj_rows)] = proj_grad.astype(LOW).reshape(nz, 2, proj_rows, width)
        ent_grads[:, :, pl.ds(proj_pad, pos_rows)] = pos_grad.astype(LOW).reshape(nz, 2, pos_rows, width)
        engine.clock += 1.0

    ent_steps = [steps for name, steps in jobs if name == "ent"][0]
    engine.add([lambda: max(engine.clock, ent_ready + 1.0), ent_part] + ent_steps)
    engine.drain()
    out_copies = [
        copies.local(ffn_sum, ffn_reduced),
        copies.local(attn_sum, attn_reduced),
        copies.local(ent_sum, ent_reduced),
    ]
    for copy in out_copies:
        copy.wait()
    copies.finish()


def backward(
    nz, all_words, hidden_low, query_words, query_ents, keys, values, probs, grad_mixed, query_weight, key_weight, value_weight,
    ffn_grads, grad_one, rows, ent_pos, ent_proj, bias_middle, ids, rows_dev,
):
    n_dp = 2 * nz
    tokens, width = hidden_low.shape
    half = keys.shape[1]
    ents, edim = rows.shape
    part = grad_one.shape[0]
    ffn_rows, attn_rows = ffn_grads.shape[2], 6 * padded(width // n_dp)
    ent_pad = padded(edim // n_dp) + padded(all_words // n_dp)
    bias_rows = 6 + bias_middle.shape[0]
    plan = [("ffn", base, size, order, width) for base, size, order in job_spans(ffn_rows)]
    attn_size = attn_rows // 3
    plan += [("attn", base, attn_size, "xz", half) for base in range(0, attn_rows, attn_size)]
    plan.append(("ent", 0, ent_pad, "xzy", width))
    scratch = [
        pltpu.VMEM((4, width, half), LOW),
        pltpu.VMEM((width, half), LOW),
        pltpu.VMEM((width, half), LOW),
        pltpu.VMEM((half, tokens), LOW),
        pltpu.VMEM((tokens, tokens), LOW),
        pltpu.VMEM((tokens, half), LOW),
        pltpu.VMEM((tokens, half), LOW),
        pltpu.VMEM((tokens, half), LOW),
        pltpu.VMEM((tokens, half), LOW),
        pltpu.VMEM((width, tokens), LOW),
        pltpu.VMEM((tokens, width), LOW),
        pltpu.VMEM((nz, 2, attn_rows, half), LOW),
        pltpu.VMEM((8, half), F32),
        pltpu.VMEM((part, width), LOW),
        pltpu.VMEM((part, width), F32),
        pltpu.VMEM((nz, 2, ent_pad, width), LOW),
        pltpu.VMEM((ffn_rows, width), LOW),
        pltpu.VMEM((2, attn_rows, half), LOW),
        pltpu.VMEM((ent_pad, width), LOW),
        pltpu.VMEM((bias_rows, width), F32),
        pltpu.VMEM((6 + nz, bias_rows, width), LOW),
        pltpu.VMEM((n_dp, 2, ents, edim), LOW),
        pltpu.VMEM((min(256, max(64, 524288 // (n_dp * 2 * ents))), n_dp * 2 * ents), LOW),
    ]
    remote = 2 + 1 + 3 + nz + 1 + nz + nz + 2 + 4
    for name, base, size, order, columns in plan:
        job = Job(None, None, base, size, order, columns, name != "ffn")
        scratch += job.scratch(nz)
        remote += job.remote_count(nz)
    scratch += copy_semaphores(remote, len(plan) + 10)
    return call(
        functools.partial(backward_kernel, nz, all_words, plan),
        [
            ((2, all_words // 4, width), F32),
            ((ffn_rows, width), LOW),
            ((2, attn_rows, half), LOW),
            ((ent_pad, width), LOW),
            ((bias_rows, width), F32),
            ((rows_dev, edim), F32),
            ((rows_dev, LANES), LOW),
        ],
        [IN_VMEM] * 7 + [ANY] * 4 + [IN_VMEM] * 6,
        [ANY] * 4 + [IN_VMEM] * 3,
        scratch,
        "backward",
        3,
    )(hidden_low, query_words, query_ents, keys, values, probs, grad_mixed, query_weight, key_weight, value_weight,
      ffn_grads, grad_one, rows, ent_pos, ent_proj, bias_middle, ids)


def last_kernel(
    n_dp, table_grad, touched, first, second, ffn, attn, ent, bias, words_low, ents_low, words_grad,
    table_out, update, new_second, proj_grad, pos_grad, query_grad, key_grad, value_grad, out_grad, up_grad, down_grad, bias_out, up_bias, word_out, ent_out, word_grad,
    sems,
):
    step = pl.program_id(0)
    pairs = [(words_low, word_out), (ents_low, ent_out), (words_grad, word_grad)]
    through = [pltpu.make_async_copy(src, dst, sems.at[i]) for i, (src, dst) in enumerate(pairs)]

    @pl.when(step == 0)
    def _():
        for copy in through:
            copy.start()

    grad = table_grad[...]
    hit = touched[:, 0:1].astype(F32) > 0.0
    mean_new = beta_one * first[...] + (1.0 - beta_one) * grad
    square_new = beta_two * second[...] + (1.0 - beta_two) * grad * grad
    direction = (
        mean_new
        / (1.0 - beta_one**adam_step)
        / (jnp.sqrt(square_new / (1.0 - beta_two**adam_step)) + adam_eps)
    )
    table_out[...] = grad
    update[...] = jnp.where(hit, direction, 0.0)
    new_second[...] = jnp.where(hit, square_new, second[...])
    width = ffn.shape[1]
    part, down_rows = out_grad.shape[0], down_grad.shape[0]
    pad = padded(part)
    proj_pad = padded(proj_grad.shape[0])
    parts = up_grad.shape[1] // width
    half = attn.shape[2]

    @pl.when(step == 0)
    def _():
        down_grad[...] = ffn[:down_rows].astype(F32)

    @pl.when(step == 1)
    def _():
        for j in range(parts):
            base = down_rows + j * pad
            up_grad[:, j * width : (j + 1) * width] = ffn[base : base + part].astype(F32)

    @pl.when(step == 2)
    def _():
        base = down_rows + parts * pad
        out_grad[...] = ffn[base : base + part].astype(F32)
        proj_grad[...] = ent[: proj_grad.shape[0]].astype(F32)
        pos_grad[...] = ent[proj_pad : proj_pad + pos_grad.shape[0]].astype(F32)
        for side in range(2):
            columns = slice(side * half, (side + 1) * half)
            key_grad[:, columns] = attn[side, 4 * pad : 4 * pad + part].astype(F32)
            value_grad[:, columns] = attn[side, 5 * pad : 5 * pad + part].astype(F32)

    @pl.when(step == 3)
    def _():
        for side in range(2):
            columns = slice(side * half, (side + 1) * half)
            for i in range(4):
                query_grad[i, :, columns] = attn[side, i * pad : i * pad + part].astype(F32)
        dp = lax.axis_index("dp")

        def own_columns(value, size, start):
            lane = lax.broadcasted_iota(jnp.int32, (value.shape[1], size), 0)
            want = lax.broadcasted_iota(jnp.int32, (value.shape[1], size), 1) + start
            pick = jnp.where(lane == want, 1.0, 0.0)
            return jnp.dot(value, pick, precision=lax.Precision.HIGHEST, preferred_element_type=F32)

        bias_out[...] = own_columns(bias[...], part, dp * part)
        up = jnp.concatenate([bias[11 + j : 12 + j] for j in range(parts)], axis=1)
        size = up_bias.shape[1]
        if size % LANES == 0:
            per = width // size
            row = bias[pl.ds(11 + dp // per, 1), :]
            chosen = row[:, :size]
            for i in range(1, per):
                chosen = jnp.where(dp % per == i, row[:, i * size : (i + 1) * size], chosen)
            up_bias[...] = chosen
        else:
            up_bias[...] = own_columns(up, size, dp * size)

    @pl.when(step == pl.num_programs(0) - 1)
    def _():
        for copy in through:
            copy.wait()


def last(n_dp, ff, all_words, table_grad, touched, first, second, ffn, attn, ent, bias, words_low, ents_low, words_grad):
    width = ffn.shape[1]
    rows, edim = first.shape
    part = width // n_dp
    block = 256
    blocked = lambda columns: pl.BlockSpec((block, columns), lambda i: (i, 0))
    whole = lambda shape: pl.BlockSpec(shape, lambda i: (0,) * len(shape))
    shapes = [
        (edim // n_dp, width),
        (all_words // n_dp, width),
        (4, part, width),
        (part, width),
        (part, width),
        (part, width),
        (part, ff),
        (ff // n_dp, width),
        (bias.shape[0], part),
        (1, ff // n_dp),
    ]
    through = [words_low, ents_low, words_grad]
    return pl.pallas_call(
        functools.partial(last_kernel, n_dp),
        grid=(rows // block,),
        out_shape=[jax.ShapeDtypeStruct((rows, edim), F32)] * 3
        + [jax.ShapeDtypeStruct(shape, F32) for shape in shapes]
        + [jax.ShapeDtypeStruct(array.shape, array.dtype) for array in through],
        in_specs=[blocked(edim), blocked(LANES), blocked(edim), blocked(edim)]
        + [whole(array.shape) for array in (ffn, attn, ent, bias)]
        + [ANY] * 3,
        out_specs=[blocked(edim)] * 3 + [whole(shape) for shape in shapes] + [ANY] * 3,
        scratch_shapes=[pltpu.SemaphoreType.DMA((3,))],
        compiler_params=pltpu.CompilerParams(vmem_limit_bytes=VMEM_BYTES),
        name="last",
    )(table_grad, touched, first, second, ffn, attn, ent, bias, words_low, ents_low, words_grad)


def on_device(
    word_states,
    segments,
    entity_ids,
    entity_pos,
    ent_table,
    first_moment,
    second_moment,
    ent_proj,
    pos_table,
    query_weight,
    query_bias,
    key_weight,
    key_bias,
    value_weight,
    value_bias,
    out_weight,
    out_bias,
    norm_gain,
    norm_shift,
    up_weight,
    up_bias,
    down_weight,
    down_bias,
    word_cot,
    ent_cot,
):
    n_dp = lax.axis_size("dp")
    nz = n_dp // 2
    core = lax.axis_index("seq") % 2
    width, ff = up_weight.shape
    all_words = segments.shape[1]
    ent_pos = lax.dynamic_slice_in_dim(entity_pos, core, 1, 0)
    segments_here = lax.dynamic_slice_in_dim(segments, core, 1, 0)
    words, word_cots, ent_cots, all_ids, rows = fetch(nz, word_states, word_cot, ent_cot, entity_ids, ent_table)
    ent_hidden, hidden_low, query_words, query_ents, keys, values, probs, mixed = forward(
        words,
        rows,
        ent_pos,
        segments_here,
        ent_proj,
        pos_table,
        query_weight,
        query_bias,
        key_weight,
        key_bias.reshape(1, width),
        value_weight,
        value_bias.reshape(1, width),
    )
    word_out, ent_out, grad_one, grad_mixed, ffn_grads, bias_middle = middle(
        nz,
        words,
        ent_hidden,
        mixed,
        out_weight,
        out_bias.reshape(1, width),
        norm_gain,
        norm_shift,
        up_weight,
        up_bias.reshape(1, ff),
        down_weight,
        down_bias.reshape(1, width),
        word_cots,
        ent_cots,
    )
    ents = entity_ids.shape[1]
    word_grad, ffn_sum, attn_sum, ent_sum, bias_sum, table_grad, touched = backward(
        nz, all_words, hidden_low, query_words, query_ents, keys, values, probs, grad_mixed, query_weight, key_weight, value_weight,
        ffn_grads, grad_one, rows, ent_pos, ent_proj, bias_middle, all_ids.reshape(-1, ents), ent_table.shape[0],
    )
    (table_grad, table_update, new_second, proj_grad, pos_grad, query_grad, key_grad, value_grad, out_grad, up_grad, down_grad, bias, up_bias_grad,
     word_out, ent_out, word_grad,
    ) = last(
        n_dp, ff, all_words, table_grad, touched, first_moment, second_moment, ffn_sum, attn_sum, ent_sum, bias_sum, word_out, ent_out, word_grad
    )
    up_rows = 11 + ff // width
    return (
        word_out,
        ent_out,
        word_grad,
        proj_grad,
        pos_grad,
        query_grad,
        bias[:4],
        key_grad,
        bias[4],
        value_grad,
        bias[5],
        out_grad,
        bias[6],
        bias[7:9],
        bias[9:11],
        up_grad,
        up_bias_grad[0],
        down_grad,
        bias[up_rows],
        table_grad,
        table_update,
        new_second,
    )


def solution(mesh):
    return jax.shard_map(
        on_device,
        mesh=mesh,
        in_specs=(
            P("dp", "seq", None),
            P("dp", None),
            P("dp", None),
            P("dp", None),
            P(("dp", "seq"), None),
            P(("dp", "seq"), None),
            P(("dp", "seq"), None),
            P(),
            P(),
            P(),
            P(),
            P(),
            P(),
            P(),
            P(),
            P(),
            P(),
            P(),
            P(),
            P(),
            P(),
            P(),
            P(),
            P("dp", "seq", None),
            P("dp", "seq", None),
        ),
        out_specs=(
            P("dp", "seq", None),
            P("dp", "seq", None),
            P("dp", "seq", None),
            P("dp", None),
            P("dp", None),
            P(None, "dp", None),
            P(None, "dp"),
            P("dp", None),
            P("dp"),
            P("dp", None),
            P("dp"),
            P("dp", None),
            P("dp"),
            P(None, "dp"),
            P(None, "dp"),
            P("dp", None),
            P("dp"),
            P("dp", None),
            P("dp"),
            P(("dp", "seq"), None),
            P(("dp", "seq"), None),
            P(("dp", "seq"), None),
        ),
        check_vma=False,
    )
```

```python
import functools
import math

import jax
import jax.numpy as jnp
from jax import lax
from jax.experimental import pallas as pl
from jax.experimental.pallas import tpu as pltpu
from jax.sharding import PartitionSpec as P

HEADS = 12
HEAD = 64
LANES = 128
MESH = pl.DeviceIdType.MESH
LOW = jnp.bfloat16
F32 = jnp.float32
VMEM_BYTES = 61 * 1024 * 1024

norm_eps = 1e-05
beta_one = 0.9
beta_two = 0.98
adam_eps = 1e-06
adam_step = 10.0
masked_score = -1e30


def dot(left, right):
    return jnp.dot(left, right, preferred_element_type=F32)


def dot_rows(left, right):
    return lax.dot_general(left, right, (((1,), (1,)), ((), ())), preferred_element_type=F32)


def dot_columns(left, right):
    return lax.dot_general(left, right, (((0,), (0,)), ((), ())), preferred_element_type=F32)


def span(start, size, unit):
    if isinstance(start, int):
        return pl.ds(start, size)
    return pl.ds(pl.multiple_of(start, unit), size)


def padded(rows):
    return -(-rows // 16) * 16


def loop(count, body, carry=0):
    return lax.fori_loop(0, count, body, carry)


class Place:
    def __init__(self, nz):
        self.dp, self.seq = lax.axis_index("dp"), lax.axis_index("seq")
        self.z, self.x = self.dp // 2, self.dp % 2
        self.y, self.core = self.seq // 2, self.seq % 2
        self.nz = nz
        self.other_core = (self.dp, self.y * 2 + 1 - self.core)
        self.other_y = (self.dp, (1 - self.y) * 2 + self.core)
        self.diagonal = (self.dp, (1 - self.y) * 2 + 1 - self.core)
        self.other_x = (self.z * 2 + 1 - self.x, self.seq)
        self.ahead = [(((self.z + k) % nz) * 2 + self.x, self.seq) for k in range(1, nz)]

    def z_ahead(self, k):
        return (self.z + k) % self.nz


def meet(partners):
    barrier = pltpu.get_barrier_semaphore()
    for partner in partners:
        pl.semaphore_signal(barrier, inc=1, device_id=partner, device_id_type=MESH)
    pl.semaphore_wait(barrier, len(partners))


class Copies:
    def __init__(self, send_sem, recv_sem, local_sem):
        self.send_sem, self.recv_sem, self.local_sem = send_sem, recv_sem, local_sem
        self.count, self.local_count = 0, 0
        self.sent = []

    def make(self, src, dst, device):
        copy = pltpu.make_async_remote_copy(
            src_ref=src,
            dst_ref=dst,
            send_sem=self.send_sem.at[self.count],
            recv_sem=self.recv_sem.at[self.count],
            device_id=device,
            device_id_type=MESH,
        )
        self.count += 1
        return copy

    def send(self, src, dst, device):
        copy = self.make(src, dst, device)
        copy.start()
        self.sent.append(copy)
        return copy

    def local(self, src, dst):
        copy = pltpu.make_async_copy(src, dst, self.local_sem.at[self.local_count])
        self.local_count += 1
        copy.start()
        return copy

    def finish(self):
        for copy in self.sent:
            copy.wait_send()


def copy_semaphores(remote, local):
    return [
        pltpu.SemaphoreType.DMA((remote,)),
        pltpu.SemaphoreType.DMA((remote,)),
        pltpu.SemaphoreType.DMA((local,)),
    ]


ANY = pl.BlockSpec(memory_space=pl.ANY)
IN_VMEM = pl.BlockSpec(memory_space=pltpu.VMEM)


def call(kernel, outs, in_specs, out_specs, scratch, name, collective_id=None):
    params = {"vmem_limit_bytes": VMEM_BYTES}
    if collective_id is not None:
        params.update(collective_id=collective_id, has_side_effects=True)
    return pl.pallas_call(
        kernel,
        out_shape=[jax.ShapeDtypeStruct(shape, dtype) for shape, dtype in outs],
        in_specs=in_specs,
        out_specs=out_specs,
        scratch_shapes=scratch,
        compiler_params=pltpu.CompilerParams(**params),
        name=name,
    )


def fetch_kernel(nz, words, word_cot, ent_cot, ids, table, all_words, word_cots, ent_cots, all_ids, rows_out, *scratch):
    table_full, table_low, picked, answers, held, from_core, from_x, from_z, from_y, ids_here = scratch[:10]
    copies = Copies(*scratch[10:])
    place = Place(nz)
    z, x, y, core = place.z, place.x, place.y, place.core
    n_dp = 2 * nz
    word_here, ent_here = words.shape[1], ent_cot.shape[1]
    ents = ids.shape[1]
    dp_others = [((place.dp + k) % n_dp, place.seq) for k in range(1, n_dp)]
    meet([place.other_core, place.other_y, place.diagonal] + dp_others)
    whole_table = copies.local(table, table_full)
    ids_here[place.dp] = ids[...]
    id_copies = [copies.send(ids, ids_here.at[place.dp], device) for device in dp_others]
    quarter = span(place.seq * word_here, word_here, 128)
    word_copies = [
        copies.send(words.at[1 - core], all_words.at[quarter], place.diagonal),
        copies.send(words.at[core], all_words.at[quarter], place.other_y),
        copies.send(words.at[1 - core], all_words.at[quarter], place.other_core),
        copies.send(word_cot.at[1 - core], word_cots.at[span(core * word_here, word_here, 128)], place.other_core),
        copies.send(ent_cot.at[1 - core], ent_cots.at[span(core * ent_here, ent_here, 32)], place.other_core),
    ]
    all_words[quarter] = words[core]
    word_cots[span(core * word_here, word_here, 128)] = word_cot[core]
    ent_cots[span(core * ent_here, ent_here, 32)] = ent_cot[core]
    whole_table.wait()
    rows_dev = table.shape[0]

    def narrow(i, _):
        where = span(i * 128, 128, 128)
        table_low[where] = table_full[where].astype(LOW)
        return 0

    loop(rows_dev // 128, narrow)
    for copy in id_copies:
        copy.wait_recv()
    all_ids[...] = ids_here[...]
    base = (place.dp * 4 + place.seq) * rows_dev
    tiles = rows_dev // LANES

    def look_up(zz):
        def group(g, _):
            asked = ids_here[zz * 2 + g // 2, pl.ds(g % 2, 1), :] - base
            column = jnp.transpose(jnp.broadcast_to(asked, (ents, ents)))
            for j in range(tiles):
                number = lax.broadcasted_iota(jnp.int32, (ents, LANES), 1) + j * LANES
                hit = jnp.where(column == number, 1.0, 0.0).astype(LOW)
                picked[span(g * ents, ents, ents), pl.ds(j * LANES, LANES)] = hit
            return 0

        loop(4, group)
        answer = dot(picked[...], table_low[...]).astype(LOW)
        answers[zz] = answer.reshape(2, 2, ents, answer.shape[-1])

    order = [place.z_ahead(k + 1) for k in range(nz)]
    core_copies, x_copies, z_copies = [], [], []

    def after_core(k):
        zz = order[k]
        core_copies[k].wait_recv()
        held[zz] = answers[zz, :, core] + from_core[zz]
        x_copies.append(copies.send(held.at[zz, 1 - x], from_x.at[zz], place.other_x))

    def after_x(k):
        zz = order[k]
        x_copies[k].wait_recv()
        held[zz, x] = held[zz, x] + from_x[zz]
        if k < nz - 1:
            z_copies.append(copies.send(held.at[zz, x], from_z.at[k], place.ahead[k]))

    for k in range(nz + 2):
        if k < nz:
            look_up(order[k])
            core_copies.append(copies.send(answers.at[order[k], :, 1 - core], from_core.at[order[k]], place.other_core))
        if 0 <= k - 1 < nz:
            after_core(k - 1)
        if 0 <= k - 2:
            after_x(k - 2)
    total = held[z, x]
    for k in range(nz - 1):
        z_copies[k].wait_recv()
        total = total + from_z[k]
    from_y[0] = total
    y_copy = copies.send(from_y.at[0], from_y.at[1], place.other_y)
    y_copy.wait_recv()
    rows_out[...] = from_y[0] + from_y[1]
    for copy in word_copies:
        copy.wait_recv()
    copies.finish()


def fetch(nz, words, word_cot, ent_cot, ids, table):
    _, word_here, width = words.shape
    ent_here, ents, (rows_dev, edim) = ent_cot.shape[1], ids.shape[1], table.shape
    n_dp = 2 * nz
    return call(
        functools.partial(fetch_kernel, nz),
        [
            ((4 * word_here, width), LOW),
            ((2 * word_here, width), LOW),
            ((2 * ent_here, width), LOW),
            ((n_dp, 2, ents), jnp.int32),
            ((ents, edim), LOW),
        ],
        [IN_VMEM] * 4 + [ANY],
        [IN_VMEM] * 5,
        [
            pltpu.VMEM((rows_dev, edim), F32),
            pltpu.VMEM((rows_dev, edim), LOW),
            pltpu.VMEM((4 * ents, rows_dev), LOW),
            pltpu.VMEM((nz, 2, 2, ents, edim), LOW),
            pltpu.VMEM((nz, 2, ents, edim), LOW),
            pltpu.VMEM((nz, 2, ents, edim), LOW),
            pltpu.VMEM((nz, ents, edim), LOW),
            pltpu.VMEM((nz - 1, ents, edim), LOW),
            pltpu.VMEM((2, ents, edim), LOW),
            pltpu.VMEM((n_dp, 2, ents), jnp.int32),
        ]
        + copy_semaphores(n_dp + 4 + 3 * nz + 2, 1),
        "fetch",
        1,
    )(words, word_cot, ent_cot, ids, table)


def lane_mask(rows, head):
    lane = lax.broadcasted_iota(jnp.int32, (rows, LANES), 1)
    return (lane >= head * HEAD) & (lane < (head + 1) * HEAD)


def row_of(vector):
    return vector[...].astype(F32).reshape(1, vector.shape[0])


def own_half(vector, y):
    row = row_of(vector)
    half = row.shape[1] // 2
    return jnp.where(y == 0, row[:, :half], row[:, half:])


def as_column(row):
    parts = [
        jnp.transpose(jnp.broadcast_to(row[:, i : i + LANES], (LANES, LANES)))
        for i in range(0, row.shape[1], LANES)
    ]
    return jnp.concatenate(parts, axis=0) if len(parts) > 1 else parts[0]


def forward_kernel(
    words, rows, ent_pos, segments, ent_proj, pos_table, query_weight, query_bias, key_weight, key_bias, value_weight, value_bias,
    ent_hidden, hidden_low, query_words, query_ents, keys, values, probs, mixed,
    query_here, key_here, value_here, values_turned, mask, mixed_turned, local_sem,
):
    y, core = lax.axis_index("seq") // 2, lax.axis_index("seq") % 2
    half = keys.shape[1]
    all_words, ents = words.shape[0], rows.shape[0]
    ent_pos, segments = ent_pos[pl.ds(core, 1), :], segments[pl.ds(core, 1), :]
    tokens = all_words + ents
    columns = span(y * half, half, LANES)
    weight_copies = [
        pltpu.make_async_copy(query_weight.at[:, :, columns], query_here, local_sem.at[0]),
        pltpu.make_async_copy(key_weight.at[:, columns], key_here, local_sem.at[1]),
        pltpu.make_async_copy(value_weight.at[:, columns], value_here, local_sem.at[2]),
    ]
    for copy in weight_copies:
        copy.start()
    position = as_column(ent_pos)
    picks = []
    for j in range(all_words // LANES):
        number = lax.broadcasted_iota(jnp.int32, (ents, LANES), 1) + j * LANES
        picks.append(jnp.where(position == number, 1.0, 0.0))
    pick = jnp.concatenate(picks, axis=1)
    word_seg = segments.astype(F32)
    ent_seg = jnp.sum(pick * word_seg, axis=1, keepdims=True)
    ent_hidden[...] = dot(rows[...], ent_proj[...]) + dot(pick.astype(LOW), pos_table[...])
    hidden_low[:all_words] = words[...]
    hidden_low[all_words:] = ent_hidden[...].astype(LOW)
    ent_row = jnp.transpose(jnp.broadcast_to(ent_seg, (ents, LANES)))[:1]
    seg_row = jnp.concatenate([word_seg, ent_row], axis=1)
    seg_column = jnp.concatenate([as_column(word_seg), jnp.broadcast_to(ent_seg, (ents, LANES))], axis=0)
    for j in range(tokens // LANES):
        here = slice(j * LANES, (j + 1) * LANES)
        mask[:, here] = jnp.where(seg_column == seg_row[:, here], 0.0, masked_score)

    query_b = query_bias[:, columns].astype(F32)
    for copy in weight_copies:
        copy.wait()
    word_low, ent_low = hidden_low[:all_words], hidden_low[all_words:]
    query_words[:all_words] = (dot(word_low, query_here[0]) + query_b[0:1]).astype(LOW)
    query_ents[:all_words] = (dot(word_low, query_here[1]) + query_b[1:2]).astype(LOW)
    query_words[all_words:] = (dot(ent_low, query_here[2]) + query_b[2:3]).astype(LOW)
    query_ents[all_words:] = (dot(ent_low, query_here[3]) + query_b[3:4]).astype(LOW)
    keys[...] = (dot(hidden_low[...], key_here[...]) + own_half(key_bias, y)).astype(LOW)
    value = dot(hidden_low[...], value_here[...]) + own_half(value_bias, y)
    values[...] = value.astype(LOW)
    values_turned[...] = jnp.transpose(value).astype(LOW)
    scale = 1.0 / math.sqrt(HEAD)
    tiles = tokens // LANES

    def tile(i, _):
        pair, place = i // tiles, span((i % tiles) * LANES, LANES, LANES)
        lanes = span(pair * LANES, LANES, LANES)
        key = keys[:, lanes]
        query_w, query_e = query_words[place, lanes], query_ents[place, lanes]
        turned = values_turned[lanes, :]
        total = jnp.zeros((LANES, LANES), F32)
        for head in range(2):
            own_key = jnp.where(lane_mask(tokens, head), key, jnp.zeros_like(key))
            raw = jnp.concatenate(
                [dot_rows(own_key[:all_words], query_w), dot_rows(own_key[all_words:], query_e)], axis=0
            )
            score = raw * scale + mask[:, place]
            weight = jnp.exp(score - jnp.max(score, axis=0, keepdims=True))
            prob = (weight * (1.0 / jnp.sum(weight, axis=0, keepdims=True))).astype(LOW)
            probs[pair * 2 + head, :, place] = prob
            row = lax.broadcasted_iota(jnp.int32, (LANES, tokens), 0)
            own_rows = (row >= head * HEAD) & (row < (head + 1) * HEAD)
            total = total + dot(jnp.where(own_rows, turned, jnp.zeros_like(turned)), prob)
        mixed[place, lanes] = jnp.transpose(total).astype(LOW)
        return 0

    loop(half // LANES * tiles, tile)


def forward(words, rows, ent_pos, segments, ent_proj, pos_table, query_weight, query_bias, key_weight, key_bias, value_weight, value_bias):
    all_words, width = words.shape
    ents = rows.shape[0]
    tokens, half = all_words + ents, width // 2
    return call(
        forward_kernel,
        [
            ((ents, width), F32),
            ((tokens, width), LOW),
            ((tokens, half), LOW),
            ((tokens, half), LOW),
            ((tokens, half), LOW),
            ((tokens, half), LOW),
            ((HEADS // 2, tokens, tokens), LOW),
            ((tokens, half), LOW),
        ],
        [IN_VMEM] * 6 + [ANY, IN_VMEM, ANY, IN_VMEM, ANY, IN_VMEM],
        [IN_VMEM] * 8,
        [
            pltpu.VMEM((4, width, half), LOW),
            pltpu.VMEM((width, half), LOW),
            pltpu.VMEM((width, half), LOW),
            pltpu.VMEM((half, tokens), LOW),
            pltpu.VMEM((tokens, tokens), F32),
            pltpu.VMEM((LANES, tokens), F32),
            pltpu.SemaphoreType.DMA((3,)),
        ],
        "forward",
    )(words, rows, ent_pos, segments, ent_proj, pos_table, query_weight, query_bias, key_weight, key_bias, value_weight, value_bias)


ROW_BLOCK = 32


def lane_mean(value):
    return jnp.mean(value, axis=-1, keepdims=True)


def column_sum(value):
    return jnp.sum(value, axis=0, keepdims=True)


class Several:
    def __init__(self, copies):
        self.copies = copies

    def wait(self):
        for copy in self.copies:
            copy.wait()


def middle_kernel(
    nz, words, ent_hidden, mixed, out_weight, out_bias, gains, shifts, up_weight, up_bias, down_weight, down_bias, word_cots, ent_cots,
    word_out, ent_out, grad_one, grad_mixed, grads, bias_out,
    out_here, up_here, down_here, mixed_full, from_y, hidden, work, normed, normed_low, normal_one, inverse_one,
    act, slope, output, cot, grad_two, grad_two_low, grad_up_low, grad_one_low, grad_mixed_here, stage, down_stage, send_sem, recv_sem, local_sem,
):
    copies = Copies(send_sem, recv_sem, local_sem)
    place = Place(nz)
    y, core = place.y, place.core
    n_dp = 2 * nz
    all_words, width = words.shape
    ents = ent_hidden.shape[0]
    half = mixed.shape[1]
    word_half, ent_half = all_words // 2, ents // 2
    tokens = word_half + ent_half
    ff = up_weight.shape[1]
    parts = ff // width
    meet([place.other_core, place.other_y])

    def token_rows(side):
        return span(side * word_half, word_half, LANES), span(all_words + side * ent_half, ent_half, 64)

    mine, theirs = token_rows(y), token_rows(1 - y)
    mixed_copies = [
        copies.send(mixed.at[theirs[0]], from_y.at[pl.ds(0, word_half)], place.other_y),
        copies.send(mixed.at[theirs[1]], from_y.at[pl.ds(word_half, ent_half)], place.other_y),
    ]
    weight_copies = [
        copies.local(out_weight, out_here),
        copies.local(up_weight, up_here),
        copies.local(down_weight, down_here),
    ]
    cot_copies = [
        copies.local(word_cots, cot.at[pl.ds(0, word_half)]),
        copies.local(ent_cots, cot.at[pl.ds(word_half, ent_half)]),
    ]
    gain, shift = gains[...].astype(F32), shifts[...].astype(F32)
    out_b, down_b, up_b = row_of(out_bias), row_of(down_bias), row_of(up_bias)
    hidden[:word_half] = words[mine[0]].astype(F32)
    hidden[word_half:] = ent_hidden[span(y * ent_half, ent_half, 64)]
    own_columns, other_columns = span(y * half, half, LANES), span((1 - y) * half, half, LANES)
    mixed_full[:word_half, own_columns] = mixed[mine[0]]
    mixed_full[word_half:, own_columns] = mixed[mine[1]]
    for copy in mixed_copies:
        copy.wait_recv()
    mixed_full[:, other_columns] = from_y[...]
    weight_copies[0].wait()
    work[...] = dot(mixed_full[...], out_here[...])
    blocks = tokens // ROW_BLOCK

    def norm_one(i, _):
        rows = span(i * ROW_BLOCK, ROW_BLOCK, ROW_BLOCK)
        value = hidden[rows] + (work[rows] + out_b)
        center = value - lane_mean(value)
        inverse = lax.rsqrt(lane_mean(center * center) + norm_eps)
        normal = center * inverse
        result = normal * gain[0:1] + shift[0:1]
        normal_one[rows] = normal
        inverse_one[rows] = jnp.broadcast_to(inverse, (ROW_BLOCK, LANES))
        normed[rows] = result
        normed_low[rows] = result.astype(LOW)
        return 0

    loop(blocks, norm_one)
    weight_copies[1].wait()
    weight_copies[2].wait()
    for j in range(parts):
        columns = slice(j * width, (j + 1) * width)
        work[...] = dot(normed_low[...], up_here[:, columns]) + up_b[:, columns]

        def gelu(i, _):
            rows = span(i * 16, 16, 16)
            value = work[rows]
            below = 0.5 * (1.0 + lax.erf(value * (1.0 / math.sqrt(2.0))))
            density = jnp.exp(-0.5 * value * value) * (1.0 / math.sqrt(2.0 * math.pi))
            act[rows, columns] = (value * below).astype(LOW)
            slope[rows, columns] = below + value * density
            return 0

        loop(tokens // 16, gelu)
    for copy in cot_copies:
        copy.wait()
    work[...] = dot(act[...], down_here[...])

    def norm_two(i, sums):
        rows = span(i * ROW_BLOCK, ROW_BLOCK, ROW_BLOCK)
        value = normed[rows] + (work[rows] + down_b)
        center = value - lane_mean(value)
        inverse = lax.rsqrt(lane_mean(center * center) + norm_eps)
        normal = center * inverse
        output[rows] = (normal * gain[1:2] + shift[1:2]).astype(LOW)
        given = cot[rows].astype(F32)
        scaled = given * gain[1:2]
        result = inverse * (scaled - lane_mean(scaled) - normal * lane_mean(scaled * normal))
        grad_two[rows] = result
        grad_two_low[rows] = result.astype(LOW)
        return (
            sums[0] + column_sum(given * normal),
            sums[1] + column_sum(given),
            sums[2] + column_sum(result),
        )

    nothing = jnp.zeros((1, width), F32)
    gain_two, shift_two, down_sum = loop(blocks, norm_two, (nothing, nothing, nothing))
    own_quarter = span(core * (word_half // 2), word_half // 2, LANES)
    other_quarter = span((1 - core) * (word_half // 2), word_half // 2, LANES)
    ent_quarter = ent_half // 2
    own_ents = span(word_half + core * ent_quarter, ent_quarter, 32)
    other_ents = span(word_half + (1 - core) * ent_quarter, ent_quarter, 32)
    out_copies = [
        copies.send(output.at[other_quarter], word_out.at[core], place.other_core),
        copies.send(output.at[other_ents], ent_out.at[core], place.other_core),
    ]
    out_local = [
        copies.local(output.at[own_quarter], word_out.at[core]),
        copies.local(output.at[own_ents], ent_out.at[core]),
    ]
    down_rows, row_part, row_pad = ff // n_dp, width // n_dp, padded(width // n_dp)
    staged = [None, None]
    turn = [0]

    def put_out(value, base, rows_in):
        slot = turn[0] % 2
        turn[0] += 1
        if staged[slot] is not None:
            staged[slot].wait()
        value = value.astype(LOW).reshape(nz, 2, rows_in, width)
        stage[slot, :, :, pl.ds(0, rows_in)] = value
        size = padded(rows_in)
        staged[slot] = copies.local(stage.at[slot, :, :, pl.ds(0, size)], grads.at[:, :, pl.ds(base, size)])

    down_staged = [None, None]
    for j in range(parts):
        columns = slice(j * width, (j + 1) * width)
        value = dot_columns(act[:, columns], grad_two_low[...]).astype(LOW)
        if down_staged[j % 2] is not None:
            down_staged[j % 2].wait()
        down_stage[j % 2] = value
        per = width // down_rows
        down_staged[j % 2] = Several([
            copies.local(
                down_stage.at[j % 2, pl.ds(d * down_rows, down_rows)],
                grads.at[(j * per + d) // 2, (j * per + d) % 2, pl.ds(0, down_rows)],
            )
            for d in range(per)
        ])
    up_sums = []
    for j in range(parts):
        columns = slice(j * width, (j + 1) * width)
        work[...] = dot_rows(grad_two_low[...], down_here[columns, :])

        def grad_gelu(i, total):
            rows = span(i * 16, 16, 16)
            value = work[rows] * slope[rows, columns]
            grad_up_low[rows, columns] = value.astype(LOW)
            return total + column_sum(value)

        up_sums.append(loop(tokens // 16, grad_gelu, nothing))
        put_out(dot_columns(normed_low[...], grad_up_low[:, columns]), down_rows + j * row_pad, row_part)
    work[...] = dot_rows(grad_up_low[...], up_here[...])

    def back_one(i, sums):
        rows = span(i * ROW_BLOCK, ROW_BLOCK, ROW_BLOCK)
        given = grad_two[rows] + work[rows]
        normal = normal_one[rows]
        inverse = inverse_one[rows, 0:1]
        scaled = given * gain[0:1]
        result = inverse * (scaled - lane_mean(scaled) - normal * lane_mean(scaled * normal))
        grad_one[rows] = result
        grad_one_low[rows] = result.astype(LOW)
        return (
            sums[0] + column_sum(given * normal),
            sums[1] + column_sum(given),
            sums[2] + column_sum(result),
        )

    gain_one, shift_one, out_sum = loop(blocks, back_one, (nothing, nothing, nothing))
    other_out = out_here[other_columns, :]
    grad_mixed_here[1] = dot_rows(grad_one_low[...], other_out).astype(LOW)
    mixed_back = [
        copies.send(grad_mixed_here.at[1, pl.ds(0, word_half)], grad_mixed.at[mine[0]], place.other_y),
        copies.send(grad_mixed_here.at[1, pl.ds(word_half, ent_half)], grad_mixed.at[mine[1]], place.other_y),
    ]
    grad_mixed_here[0] = dot_rows(grad_one_low[...], out_here[own_columns, :]).astype(LOW)
    mixed_own = [
        copies.local(grad_mixed_here.at[0, pl.ds(0, word_half)], grad_mixed.at[mine[0]]),
        copies.local(grad_mixed_here.at[0, pl.ds(word_half, ent_half)], grad_mixed.at[mine[1]]),
    ]
    put_out(dot_columns(mixed_full[...], grad_one_low[...]), down_rows + parts * row_pad, row_part)
    bias_rows = [out_sum, gain_one, gain_two, shift_one, shift_two] + up_sums + [down_sum]
    for i, row in enumerate(bias_rows):
        bias_out[i : i + 1] = row
    for copy in staged + down_staged:
        copy.wait()
    for copy in mixed_back + out_copies:
        copy.wait_recv()
    for copy in mixed_own + out_local:
        copy.wait()
    copies.finish()


def middle(nz, words, ent_hidden, mixed, out_weight, out_bias, gains, shifts, up_weight, up_bias, down_weight, down_bias, word_cots, ent_cots):
    n_dp = 2 * nz
    all_words, width = words.shape
    ents, half, ff = ent_hidden.shape[0], mixed.shape[1], up_weight.shape[1]
    tokens = (all_words + ents) // 2
    parts = ff // width
    row_pad = padded(width // n_dp)
    slab = ff // n_dp + (parts + 1) * row_pad
    return call(
        functools.partial(middle_kernel, nz),
        [
            ((2, all_words // 4, width), LOW),
            ((2, ents // 4, width), LOW),
            ((tokens, width), F32),
            ((all_words + ents, half), LOW),
            ((nz, 2, slab, width), LOW),
            ((6 + parts, width), F32),
        ],
        [IN_VMEM] * 3 + [ANY] + [IN_VMEM] * 3 + [ANY, IN_VMEM, ANY, IN_VMEM, ANY, ANY],
        [ANY, ANY, IN_VMEM, ANY, ANY, IN_VMEM],
        [
            pltpu.VMEM((width, width), LOW),
            pltpu.VMEM((width, ff), LOW),
            pltpu.VMEM((ff, width), LOW),
            pltpu.VMEM((tokens, width), LOW),
            pltpu.VMEM((tokens, half), LOW),
            pltpu.VMEM((tokens, width), F32),
            pltpu.VMEM((tokens, width), F32),
            pltpu.VMEM((tokens, width), F32),
            pltpu.VMEM((tokens, width), LOW),
            pltpu.VMEM((tokens, width), F32),
            pltpu.VMEM((tokens, LANES), F32),
            pltpu.VMEM((tokens, ff), LOW),
            pltpu.VMEM((tokens, ff), F32),
            pltpu.VMEM((tokens, width), LOW),
            pltpu.VMEM((tokens, width), LOW),
            pltpu.VMEM((tokens, width), F32),
            pltpu.VMEM((tokens, width), LOW),
            pltpu.VMEM((tokens, ff), LOW),
            pltpu.VMEM((tokens, width), LOW),
            pltpu.VMEM((2, tokens, half), LOW),
            pltpu.VMEM((2, nz, 2, row_pad, width), LOW),
            pltpu.VMEM((2, width, width), LOW),
        ]
        + copy_semaphores(8, 40 + 4 * n_dp),
        "middle",
        2,
    )(words, ent_hidden, mixed, out_weight, out_bias, gains, shifts, up_weight, up_bias, down_weight, down_bias, word_cots, ent_cots)


class Engine:
    RATES = {"core": 300e3, "x": 50e3, "y": 50e3, "z": 12.5e3}
    LATENCY = 1.5

    def __init__(self):
        self.clock, self.free, self.streams = 0.0, {}, []

    def transfer(self, link, size):
        start = max(self.clock, self.free.get(link, 0.0))
        self.free[link] = start + size / self.RATES[link]
        return self.free[link] + self.LATENCY

    def add(self, steps):
        self.streams.append([self.clock, list(steps)])
        self.poll()

    def run(self, stream):
        self.clock = max(self.clock, stream[0])
        ready = stream[1].pop(0)()
        stream[0] = self.clock if ready is None else ready

    def next(self):
        live = [stream for stream in self.streams if stream[1]]
        return min(live, key=lambda stream: stream[0]) if live else None

    def poll(self):
        while (stream := self.next()) is not None and stream[0] <= self.clock:
            self.run(stream)

    def work(self, time):
        self.clock += time
        self.poll()

    def drain(self):
        while (stream := self.next()) is not None:
            self.run(stream)


def blocks_of(rows):
    for size in (96, 64, 48, 32):
        if rows % size == 0:
            return size
    return 16


def add_blocks(engine, target, parts, leading, rows, columns):
    size = blocks_of(rows)
    count = rows // size

    def block(i, _):
        lead, row = i // count, (i % count) * size
        where = span(row, size, 16)
        if len(parts) == 2:
            value = parts[0](lead, where) + parts[1](lead, where)
        else:
            value = parts[0](lead, where).astype(F32)
            for part in parts[1:]:
                value = value + part(lead, where).astype(F32)
            value = value.astype(LOW)
        target(lead, where, value)
        return 0

    loop(leading * count, block)
    engine.clock += 0.3 + leading * rows * columns / 1e6


class Job:
    def __init__(self, grads, reduced, base, size, order, columns, resident):
        self.grads, self.reduced, self.base, self.size, self.order, self.columns = grads, reduced, base, size, order, columns
        self.resident = resident
        self.half = size // 2
        self.part = size // 4 if order == "yxz" else size // 2

    def scratch(self, nz):
        shapes = [(nz, 2, self.half, self.columns)] * (1 if self.resident else 2)
        if self.order == "yxz":
            shapes.append((nz, 2, self.part, self.columns))
        elif self.order == "xzy":
            shapes.append((2, self.part, self.columns))
        shapes += [(nz, self.part, self.columns), (nz - 1, self.part, self.columns)]
        return [pltpu.VMEM(shape, LOW) for shape in shapes]

    def remote_count(self, nz):
        return 1 + (1 if self.order != "xz" else 0) + 1 + (nz - 1) + 1 + 1

    def steps(self, engine, place, copies, scratch):
        nz, z, x, y, core = place.nz, place.z, place.x, place.y, place.core
        base, half, part, order, columns = self.base, self.half, self.part, self.order, self.columns
        if self.resident:
            scratch = [self.grads.at[:, :, span(base + core * half, half, 16)]] + list(scratch)
        held, from_core = scratch[:2]
        from_y = scratch[2] if order != "xz" else None
        from_x, from_z = scratch[-2:]
        live = {}
        row_bytes = 2 * columns

        def start():
            theirs, own = span(base + (1 - core) * half, half, 16), span(base + core * half, half, 16)
            live["core"] = copies.send(self.grads.at[:, :, theirs], from_core, place.other_core)
            if not self.resident:
                live["own"] = copies.local(self.grads.at[:, :, own], held)
            return engine.transfer("core", 2 * nz * half * row_bytes)

        own_rows = span(y * part, part, 16) if order == "yxz" else pl.ds(0, part)
        final_rows = span(base + core * half + (y * part if order == "yxz" else 0), part, 16)

        def send_x():
            live["x"] = copies.send(held.at[:, 1 - x, own_rows], from_x, place.other_x)
            return engine.transfer("x", nz * part * row_bytes)

        def after_core():
            if not self.resident:
                live["own"].wait()
            live["core"].wait_recv()

            def put(i, where, value):
                held[i // 2, i % 2, where] = value

            add_blocks(
                engine,
                put,
                [lambda i, where: held[i // 2, i % 2, where], lambda i, where: from_core[i // 2, i % 2, where]],
                2 * nz,
                half,
                columns,
            )
            if order == "yxz":
                live["y"] = copies.send(held.at[:, :, span((1 - y) * part, part, 16)], from_y, place.other_y)
                return engine.transfer("y", 2 * nz * part * row_bytes)
            return send_x()

        def shifted(where):
            return span(y * part + where.start, where.size, 16) if order == "yxz" else where

        def after_y():
            live["y"].wait_recv()

            def put(i, where, value):
                held[i // 2, i % 2, shifted(where)] = value

            add_blocks(
                engine,
                put,
                [lambda i, where: held[i // 2, i % 2, shifted(where)], lambda i, where: from_y[i // 2, i % 2, where]],
                2 * nz,
                part,
                columns,
            )
            return send_x()

        def after_x():
            live["x"].wait_recv()

            def put(i, where, value):
                held[i, x, shifted(where)] = value

            add_blocks(
                engine,
                put,
                [lambda i, where: held[i, x, shifted(where)], lambda i, where: from_x[i, where]],
                nz,
                part,
                columns,
            )
            live["z"] = [
                copies.send(held.at[place.z_ahead(k + 1), x, own_rows], from_z.at[k], device)
                for k, device in enumerate(place.ahead)
            ]
            return engine.transfer("z", part * row_bytes)

        def after_z():
            for copy in live["z"]:
                copy.wait_recv()

            def put(i, where, value):
                if order == "yxz":
                    self.reduced[span(base + core * half + y * part + where.start, where.size, 16)] = value
                elif order == "xz":
                    self.reduced[y, span(base + core * half + where.start, where.size, 16)] = value
                else:
                    from_y[0, where] = value

            def parts(k):
                return lambda i, where: from_z[k, where]

            add_blocks(
                engine,
                put,
                [lambda i, where: held[z, x, shifted(where)]] + [parts(k) for k in range(nz - 1)],
                1,
                part,
                columns,
            )
            if order == "yxz":
                view = self.reduced.at[final_rows]
                live["y2"] = copies.send(view, view, place.other_y)
            elif order == "xz":
                view = self.reduced.at[y, final_rows]
                live["y2"] = copies.send(view, view, place.other_y)
            else:
                live["y2"] = copies.send(from_y.at[0], from_y.at[1], place.other_y)
            return engine.transfer("y", part * row_bytes)

        def after_gather():
            live["y2"].wait_recv()
            mine = span(base + core * half, half, 16)
            if order == "xzy":

                def put(i, where, value):
                    self.reduced[span(base + core * half + where.start, where.size, 16)] = value

                add_blocks(
                    engine, put, [lambda i, where: from_y[0, where], lambda i, where: from_y[1, where]], 1, part, columns
                )
            view = self.reduced.at[:, mine] if order == "xz" else self.reduced.at[mine]
            live["core2"] = copies.send(view, view, place.other_core)
            return engine.transfer("core", 2 * half * row_bytes)

        def end():
            live["core2"].wait_recv()

        middle_steps = [after_core, after_y, after_x] if order == "yxz" else [after_core, after_x]
        return [start] + middle_steps + [after_z, after_gather, end]


def job_spans(rows):
    spans, base, turn = [], 0, 0
    while base < rows:
        size, order = ((192, "yxz"), (96, "xzy"))[turn % 2]
        if base + size > rows:
            size = rows - base
            order = "yxz" if size % 64 == 0 else "xzy"
        if order == "yxz" and size == 192:
            spans += [(base, 128, order), (base + 128, 64, order)]
        else:
            spans.append((base, size, order))
        base += size
        turn += 1
    return spans


def backward_kernel(
    nz, all_words, plan, hidden_low, query_words, query_ents, keys, values, probs, grad_mixed, query_weight, key_weight, value_weight,
    ffn_grads, grad_one, rows, ent_pos, ent_proj, bias_middle, ids,
    word_grad, ffn_reduced, attn_reduced, ent_reduced, bias_out, table_grad, touched, *scratch,
):
    (query_here, key_here, value_here, keys_turned, grad_scores, grad_query_words, grad_query_ents, grad_keys, grad_values, hidden_turned,
     grad_hidden, attn_grads, bias_heads, given, total, ent_grads, ffn_sum, attn_sum, ent_sum, bias_held, bias_from, all_rows, hits,
    ) = scratch[:23]
    copies = Copies(*scratch[-3:])
    engine = Engine()
    place = Place(nz)
    z, x, y, core = place.z, place.x, place.y, place.core
    n_dp = 2 * nz
    tokens, half = keys.shape
    width = hidden_low.shape[1]
    ents = tokens - all_words
    word_half, ent_half = all_words // 2, ents // 2
    ent_pos = ent_pos[pl.ds(core, 1), :]
    meet([place.other_core, place.other_y, place.other_x] + place.ahead)
    jobs, at = [], 23
    sources = {"ffn": (ffn_grads, ffn_sum), "attn": (attn_grads, attn_sum), "ent": (ent_grads, ent_sum)}
    for name, base, size, order, columns in plan:
        job = Job(*sources[name], base, size, order, columns, name != "ffn")
        used = len(job.scratch(nz))
        jobs.append((name, job.steps(engine, place, copies, scratch[at : at + used])))
        at += used
    for name, steps in jobs:
        if name == "ffn":
            engine.add(steps)
    columns = span(y * half, half, LANES)
    weight_copies = [
        copies.local(query_weight.at[:, :, columns], query_here),
        copies.local(key_weight.at[:, columns], key_here),
        copies.local(value_weight.at[:, columns], value_here),
    ]
    for i in range(half // LANES):
        lanes = slice(i * LANES, (i + 1) * LANES)
        keys_turned[lanes, :] = jnp.transpose(keys[:, lanes].astype(F32)).astype(LOW)
    for i in range(width // LANES):
        lanes = slice(i * LANES, (i + 1) * LANES)
        hidden_turned[lanes, :] = jnp.transpose(hidden_low[:, lanes].astype(F32)).astype(LOW)
    engine.work(2.0)
    scale = 1.0 / math.sqrt(HEAD)
    tiles = tokens // LANES

    for pair in range(half // LANES):
        lanes = slice(pair * LANES, (pair + 1) * LANES)
        grad_query_w = jnp.zeros((LANES, tokens), F32)
        grad_query_e = jnp.zeros((LANES, tokens), F32)
        grad_key_w = jnp.zeros((all_words, LANES), F32)
        grad_key_e = jnp.zeros((ents, LANES), F32)
        grad_value = jnp.zeros((tokens, LANES), F32)
        for head in range(2):
            own = lane_mask(tokens, head)
            value = values[:, lanes]
            own_value = jnp.where(own, value, jnp.zeros_like(value))

            def tile(i, _):
                where = span(i * LANES, LANES, LANES)
                grad_prob = dot_rows(own_value, grad_mixed[where, lanes])
                prob = probs[pair * 2 + head, :, where].astype(F32)
                both = prob * grad_prob
                grad_scores[:, where] = (both - prob * jnp.sum(both, axis=0, keepdims=True)).astype(LOW)
                return 0

            loop(tiles, tile)
            engine.work(1.7)
            given_heads = grad_mixed[:, lanes]
            grad_value += dot(probs[pair * 2 + head], jnp.where(own, given_heads, jnp.zeros_like(given_heads)))
            query_w, query_e = query_words[:, lanes], query_ents[:, lanes]
            grad_key_w += dot(grad_scores[:all_words], jnp.where(own, query_w, jnp.zeros_like(query_w)))
            grad_key_e += dot(grad_scores[all_words:], jnp.where(own, query_e, jnp.zeros_like(query_e)))
            row = lax.broadcasted_iota(jnp.int32, (LANES, tokens), 0)
            own_rows = (row >= head * HEAD) & (row < (head + 1) * HEAD)
            turned = keys_turned[lanes, :]
            turned = jnp.where(own_rows, turned, jnp.zeros_like(turned))
            grad_query_w += dot(turned[:, :all_words], grad_scores[:all_words])
            grad_query_e += dot(turned[:, all_words:], grad_scores[all_words:])
            engine.work(1.7)
        grad_query_w = jnp.transpose(grad_query_w) * scale
        grad_query_e = jnp.transpose(grad_query_e) * scale
        grad_key_w, grad_key_e = grad_key_w * scale, grad_key_e * scale
        sums = [
            column_sum(grad_query_w[:all_words]),
            column_sum(grad_query_e[:all_words]),
            column_sum(grad_query_w[all_words:]),
            column_sum(grad_query_e[all_words:]),
            column_sum(grad_key_w) + column_sum(grad_key_e),
            column_sum(grad_value),
        ]
        for i, sum_row in enumerate(sums):
            bias_heads[i : i + 1, lanes] = sum_row
        grad_query_words[:, lanes] = grad_query_w.astype(LOW)
        grad_query_ents[:, lanes] = grad_query_e.astype(LOW)
        grad_keys[:all_words, lanes] = grad_key_w.astype(LOW)
        grad_keys[all_words:, lanes] = grad_key_e.astype(LOW)
        grad_values[:, lanes] = grad_value.astype(LOW)
        engine.work(0.5)

    for copy in weight_copies:
        copy.wait()
    theirs = span((1 - y) * word_half, word_half, LANES), span(all_words + (1 - y) * ent_half, ent_half, 64)
    ent_rows, word_rows = slice(all_words, tokens), slice(0, all_words)

    def hidden_part(here, first, second):
        grad_hidden[here] = (
            dot_rows(grad_keys[here], key_here[...])
            + dot_rows(grad_values[here], value_here[...])
            + dot_rows(grad_query_words[here], query_here[first])
            + dot_rows(grad_query_ents[here], query_here[second])
        ).astype(LOW)

    hidden_part(ent_rows, 2, 3)
    ent_copy = copies.send(grad_hidden.at[theirs[1]], given.at[pl.ds(word_half, ent_half)], place.other_y)
    ent_ready = engine.transfer("y", ent_half * width * 2)
    engine.work(0.7)
    row_part, row_pad = width // n_dp, padded(width // n_dp)
    word_turned, ent_turned = hidden_turned[:, :all_words], hidden_turned[:, all_words:]
    attn_jobs = [steps for name, steps in jobs if name == "attn"]

    def attn_product(i, value):
        attn_grads[:, :, pl.ds(i * row_pad, row_part)] = value.astype(LOW).reshape(nz, 2, row_part, half)
        per = 6 // len(attn_jobs)
        if i % per == per - 1:
            engine.add(attn_jobs[i // per])
        engine.work(0.6)

    attn_product(0, dot(word_turned, grad_query_words[:all_words]))
    attn_product(1, dot(word_turned, grad_query_ents[:all_words]))
    hidden_part(word_rows, 0, 1)
    word_copy = copies.send(grad_hidden.at[theirs[0]], given.at[pl.ds(0, word_half)], place.other_y)
    word_ready = engine.transfer("y", word_half * width * 2)
    engine.work(1.5)

    bias_rows = bias_held.shape[0]
    bias_held[...] = jnp.zeros_like(bias_held)
    bias_held[0:6, span(y * half, half, LANES)] = bias_heads[0:6]
    bias_held[6:bias_rows] = bias_middle[...]
    live = {}
    bias_bytes = bias_rows * width * 2

    def bias_send(key, index, device):
        bias_from[2 * index] = bias_held[...].astype(LOW)
        live[key] = copies.send(bias_from.at[2 * index], bias_from.at[2 * index + 1], device)
        return engine.transfer(key, bias_bytes)

    def bias_take(key, index):
        live[key].wait_recv()
        bias_held[...] = bias_from[2 * index].astype(F32) + bias_from[2 * index + 1].astype(F32)

    def bias_core():
        return bias_send("core", 0, place.other_core)

    def bias_y():
        bias_take("core", 0)
        return bias_send("y", 1, place.other_y)

    def bias_x():
        bias_take("y", 1)
        return bias_send("x", 2, place.other_x)

    def bias_z():
        bias_take("x", 2)
        bias_from[6] = bias_held[...].astype(LOW)
        live["z"] = [copies.send(bias_from.at[6], bias_from.at[7 + k], device) for k, device in enumerate(place.ahead)]
        return engine.transfer("z", bias_bytes)

    def bias_end():
        value = bias_from[6].astype(F32)
        for k, copy in enumerate(live["z"]):
            copy.wait_recv()
            value = value + bias_from[7 + k].astype(F32)
        bias_out[...] = value

    live_rows = {}

    def sum_hidden(start, count, own_start):
        def block(i, _):
            where = span(start + i * 32, 32, 32)
            own = span(own_start + i * 32, 32, 32)
            total[where] = grad_one[where] + (grad_hidden[own].astype(F32) + given[where].astype(F32))
            return 0

        loop(count // 32, block)

    row_bytes = ent_half * ent_proj.shape[0] * 2

    def rows_y():
        ent_copy.wait_recv()
        sum_hidden(word_half, ent_half, all_words + y * ent_half)
        row_grad = dot_rows(total[word_half:].astype(LOW), ent_proj[...]).astype(LOW)
        all_rows[place.dp, core, span(y * ent_half, ent_half, 64)] = row_grad
        view = all_rows.at[place.dp, core, span(y * ent_half, ent_half, 64)]
        live_rows["y"] = copies.send(view, view, place.other_y)
        return engine.transfer("y", row_bytes)

    def rows_z():
        live_rows["y"].wait_recv()
        view = all_rows.at[place.dp, core]
        live_rows["z"] = [copies.send(view, view, device) for device in place.ahead]
        return engine.transfer("z", 2 * row_bytes)

    def rows_x():
        for copy in live_rows["z"]:
            copy.wait_recv()
        live_rows["x"] = []
        for k in range(nz):
            view = all_rows.at[place.z_ahead(k) * 2 + x, core]
            live_rows["x"].append(copies.send(view, view, place.other_x))
        return engine.transfer("x", nz * 2 * row_bytes)

    def rows_core():
        for copy in live_rows["x"]:
            copy.wait_recv()
        view = all_rows.at[:, core]
        live_rows["core"] = copies.send(view, view, place.other_core)
        return engine.transfer("core", n_dp * 2 * row_bytes)

    rows_dev = table_grad.shape[0]
    table_block = hits.shape[0]
    base_row = (place.dp * 4 + place.seq) * rows_dev
    table_copies = []

    def table_part(i):
        def step():
            if i == 0:
                live_rows["core"].wait_recv()
            groups = ids.shape[0]
            number = lax.broadcasted_iota(jnp.int32, (table_block, ents), 0) + (base_row + i * table_block)
            count = jnp.zeros((table_block, ents), F32)
            for group in range(groups):
                hit = jnp.where(ids[group : group + 1, :] == number, 1.0, 0.0)
                count = count + hit
                hits[:, group * ents : (group + 1) * ents] = hit.astype(LOW)
            here = pl.ds(i * table_block, table_block)
            dps = min(n_dp, 8)
            grad = None
            for first in range(0, n_dp, dps):
                given_rows = all_rows[first : first + dps].reshape(dps * 2 * ents, ent_proj.shape[0])
                part = dot(hits[:, first * 2 * ents : (first + dps) * 2 * ents], given_rows)
                grad = part if grad is None else grad + part
            table_grad[here] = grad
            named = jnp.sum(count, axis=1, keepdims=True)
            touched[here] = jnp.broadcast_to(named, (table_block, LANES)).astype(LOW)
            engine.clock += 1.2

        return step

    engine.add([lambda: ent_ready, rows_y, rows_z, rows_x, rows_core] + [table_part(i) for i in range(rows_dev // table_block)])
    engine.add([bias_core, bias_y, bias_x, bias_z, bias_end])
    attn_product(2, dot(ent_turned, grad_query_words[all_words:]))
    attn_product(3, dot(ent_turned, grad_query_ents[all_words:]))
    attn_product(4, dot(hidden_turned[...], grad_keys[...]))
    attn_product(5, dot(hidden_turned[...], grad_values[...]))
    quarter = word_half // 2
    own_quarter = span(core * quarter, quarter, LANES)
    other_quarter = span((1 - core) * quarter, quarter, LANES)
    live_words = {}

    def words_sum():
        word_copy.wait_recv()
        sum_hidden(0, word_half, y * word_half)
        engine.clock += 0.5
        live_words["send"] = copies.send(total.at[other_quarter], word_grad.at[core], place.other_core)
        live_words["own"] = copies.local(total.at[own_quarter], word_grad.at[core])
        return engine.transfer("core", quarter * width * 4)

    def words_end():
        live_words["send"].wait_recv()
        live_words["own"].wait()

    engine.add([lambda: word_ready, words_sum, words_end])

    def ent_part():
        proj_rows, pos_rows = rows.shape[1] // n_dp, all_words // n_dp
        proj_pad = padded(proj_rows)
        picks = []
        for j in range(all_words // LANES):
            number = lax.broadcasted_iota(jnp.int32, (LANES, ents), 0) + j * LANES
            picks.append(jnp.where(number == ent_pos, 1.0, 0.0))
        pick = jnp.concatenate(picks, axis=0)
        here = lax.broadcasted_iota(jnp.int32, (all_words, ents), 1) // ent_half == y
        pick = jnp.where(here, pick, 0.0).astype(LOW)
        grad_ent = total[word_half:]
        grad_ent_low = grad_ent.astype(LOW)
        rest = (grad_ent - grad_ent_low.astype(F32)).astype(LOW)
        pos_grad = dot(pick, jnp.concatenate([grad_ent_low, grad_ent_low], axis=0)) + dot(
            pick, jnp.concatenate([rest, rest], axis=0)
        )
        proj_grad = dot_columns(rows[span(y * ent_half, ent_half, 64)], grad_ent_low)
        ent_grads[:, :, pl.ds(0, proj_rows)] = proj_grad.astype(LOW).reshape(nz, 2, proj_rows, width)
        ent_grads[:, :, pl.ds(proj_pad, pos_rows)] = pos_grad.astype(LOW).reshape(nz, 2, pos_rows, width)
        engine.clock += 1.0

    ent_steps = [steps for name, steps in jobs if name == "ent"][0]
    engine.add([lambda: max(engine.clock, ent_ready + 1.0), ent_part] + ent_steps)
    engine.drain()
    out_copies = [
        copies.local(ffn_sum, ffn_reduced),
        copies.local(attn_sum, attn_reduced),
        copies.local(ent_sum, ent_reduced),
    ]
    for copy in out_copies:
        copy.wait()
    copies.finish()


def backward(
    nz, all_words, hidden_low, query_words, query_ents, keys, values, probs, grad_mixed, query_weight, key_weight, value_weight,
    ffn_grads, grad_one, rows, ent_pos, ent_proj, bias_middle, ids, rows_dev,
):
    n_dp = 2 * nz
    tokens, width = hidden_low.shape
    half = keys.shape[1]
    ents, edim = rows.shape
    part = grad_one.shape[0]
    ffn_rows, attn_rows = ffn_grads.shape[2], 6 * padded(width // n_dp)
    ent_pad = padded(edim // n_dp) + padded(all_words // n_dp)
    bias_rows = 6 + bias_middle.shape[0]
    plan = [("ffn", base, size, order, width) for base, size, order in job_spans(ffn_rows)]
    attn_size = attn_rows // 3
    plan += [("attn", base, attn_size, "xz", half) for base in range(0, attn_rows, attn_size)]
    plan.append(("ent", 0, ent_pad, "xzy", width))
    scratch = [
        pltpu.VMEM((4, width, half), LOW),
        pltpu.VMEM((width, half), LOW),
        pltpu.VMEM((width, half), LOW),
        pltpu.VMEM((half, tokens), LOW),
        pltpu.VMEM((tokens, tokens), LOW),
        pltpu.VMEM((tokens, half), LOW),
        pltpu.VMEM((tokens, half), LOW),
        pltpu.VMEM((tokens, half), LOW),
        pltpu.VMEM((tokens, half), LOW),
        pltpu.VMEM((width, tokens), LOW),
        pltpu.VMEM((tokens, width), LOW),
        pltpu.VMEM((nz, 2, attn_rows, half), LOW),
        pltpu.VMEM((8, half), F32),
        pltpu.VMEM((part, width), LOW),
        pltpu.VMEM((part, width), F32),
        pltpu.VMEM((nz, 2, ent_pad, width), LOW),
        pltpu.VMEM((ffn_rows, width), LOW),
        pltpu.VMEM((2, attn_rows, half), LOW),
        pltpu.VMEM((ent_pad, width), LOW),
        pltpu.VMEM((bias_rows, width), F32),
        pltpu.VMEM((6 + nz, bias_rows, width), LOW),
        pltpu.VMEM((n_dp, 2, ents, edim), LOW),
        pltpu.VMEM((min(256, max(64, 524288 // (n_dp * 2 * ents))), n_dp * 2 * ents), LOW),
    ]
    remote = 2 + 1 + 3 + nz + 1 + nz + nz + 2 + 4
    for name, base, size, order, columns in plan:
        job = Job(None, None, base, size, order, columns, name != "ffn")
        scratch += job.scratch(nz)
        remote += job.remote_count(nz)
    scratch += copy_semaphores(remote, len(plan) + 10)
    return call(
        functools.partial(backward_kernel, nz, all_words, plan),
        [
            ((2, all_words // 4, width), F32),
            ((ffn_rows, width), LOW),
            ((2, attn_rows, half), LOW),
            ((ent_pad, width), LOW),
            ((bias_rows, width), F32),
            ((rows_dev, edim), F32),
            ((rows_dev, LANES), LOW),
        ],
        [IN_VMEM] * 7 + [ANY] * 4 + [IN_VMEM] * 6,
        [ANY] * 4 + [IN_VMEM] * 3,
        scratch,
        "backward",
        3,
    )(hidden_low, query_words, query_ents, keys, values, probs, grad_mixed, query_weight, key_weight, value_weight,
      ffn_grads, grad_one, rows, ent_pos, ent_proj, bias_middle, ids)


def last_kernel(
    n_dp, table_grad, touched, first, second, ffn, attn, ent, bias, words_low, ents_low, words_grad,
    table_out, update, new_second, proj_grad, pos_grad, query_grad, key_grad, value_grad, out_grad, up_grad, down_grad, query_bias, gain_grad, shift_grad, key_bias, value_bias, out_bias, down_bias, up_bias,
    word_out, ent_out, word_grad,
):
    step = pl.program_id(0)
    grad = table_grad[...]
    hit = touched[:, 0:1].astype(F32) > 0.0
    mean_new = beta_one * first[...] + (1.0 - beta_one) * grad
    square_new = beta_two * second[...] + (1.0 - beta_two) * grad * grad
    direction = (
        mean_new
        / (1.0 - beta_one**adam_step)
        / (jnp.sqrt(square_new / (1.0 - beta_two**adam_step)) + adam_eps)
    )
    table_out[...] = grad
    update[...] = jnp.where(hit, direction, 0.0)
    new_second[...] = jnp.where(hit, square_new, second[...])
    width = ffn.shape[1]
    part, down_rows = out_grad.shape[0], down_grad.shape[0]
    pad = padded(part)
    proj_pad = padded(proj_grad.shape[0])
    parts = up_grad.shape[1] // width
    half = attn.shape[2]

    @pl.when(step == 0)
    def _():
        down_grad[...] = ffn[:down_rows].astype(F32)

    @pl.when(step == 1)
    def _():
        for j in range(parts):
            base = down_rows + j * pad
            up_grad[:, j * width : (j + 1) * width] = ffn[base : base + part].astype(F32)

    @pl.when(step == 2)
    def _():
        base = down_rows + parts * pad
        out_grad[...] = ffn[base : base + part].astype(F32)
        proj_grad[...] = ent[: proj_grad.shape[0]].astype(F32)
        pos_grad[...] = ent[proj_pad : proj_pad + pos_grad.shape[0]].astype(F32)
        for side in range(2):
            columns = slice(side * half, (side + 1) * half)
            key_grad[:, columns] = attn[side, 4 * pad : 4 * pad + part].astype(F32)
            value_grad[:, columns] = attn[side, 5 * pad : 5 * pad + part].astype(F32)

    @pl.when(step == 3)
    def _():
        for side in range(2):
            columns = slice(side * half, (side + 1) * half)
            for i in range(4):
                query_grad[i, :, columns] = attn[side, i * pad : i * pad + part].astype(F32)
        dp = lax.axis_index("dp")

        def own_columns(value, size, start):
            lane = lax.broadcasted_iota(jnp.int32, (value.shape[1], size), 0)
            want = lax.broadcasted_iota(jnp.int32, (value.shape[1], size), 1) + start
            pick = jnp.where(lane == want, 1.0, 0.0)
            return jnp.dot(value, pick, precision=lax.Precision.HIGHEST, preferred_element_type=F32)

        own = own_columns(bias[...], part, dp * part)
        query_bias[...] = own[0:4]
        gain_grad[...] = own[7:9]
        shift_grad[...] = own[9:11]
        for vector, i in ((key_bias, 4), (value_bias, 5), (out_bias, 6), (down_bias, 11 + parts)):
            vector[...] = own[i : i + 1].reshape(part)
        up = jnp.concatenate([bias[11 + j : 12 + j] for j in range(parts)], axis=1)
        size = up_bias.shape[0]
        if size % LANES == 0:
            per = width // size
            row = bias[pl.ds(11 + dp // per, 1), :]
            chosen = row[:, :size]
            for i in range(1, per):
                chosen = jnp.where(dp % per == i, row[:, i * size : (i + 1) * size], chosen)
            up_bias[...] = chosen.reshape(size)
        else:
            up_bias[...] = own_columns(up, size, dp * size).reshape(size)

    @pl.when(step == 4)
    def _():
        word_out[...] = words_low[...]
        ent_out[...] = ents_low[...]
        word_grad[...] = words_grad[...]


def last(n_dp, ff, all_words, table_grad, touched, first, second, ffn, attn, ent, bias, words_low, ents_low, words_grad):
    width = ffn.shape[1]
    rows, edim = first.shape
    part = width // n_dp
    block = 256
    blocked = lambda columns: pl.BlockSpec((block, columns), lambda i: (i, 0))
    whole = lambda shape: pl.BlockSpec(shape, lambda i: (0,) * len(shape))
    shapes = [
        (edim // n_dp, width),
        (all_words // n_dp, width),
        (4, part, width),
        (part, width),
        (part, width),
        (part, width),
        (part, ff),
        (ff // n_dp, width),
        (4, part),
        (2, part),
        (2, part),
        (part,),
        (part,),
        (part,),
        (part,),
        (ff // n_dp,),
    ]
    through = [words_low, ents_low, words_grad]
    return pl.pallas_call(
        functools.partial(last_kernel, n_dp),
        grid=(rows // block,),
        out_shape=[jax.ShapeDtypeStruct((rows, edim), F32)] * 3
        + [jax.ShapeDtypeStruct(shape, F32) for shape in shapes]
        + [jax.ShapeDtypeStruct(array.shape, array.dtype) for array in through],
        in_specs=[blocked(edim), blocked(LANES), blocked(edim), blocked(edim)]
        + [whole(array.shape) for array in (ffn, attn, ent, bias)]
        + [whole(array.shape) for array in through],
        out_specs=[blocked(edim)] * 3 + [whole(shape) for shape in shapes] + [whole(array.shape) for array in through],
        compiler_params=pltpu.CompilerParams(vmem_limit_bytes=VMEM_BYTES),
        name="last",
    )(table_grad, touched, first, second, ffn, attn, ent, bias, words_low, ents_low, words_grad)


def on_device(
    word_states,
    segments,
    entity_ids,
    entity_pos,
    ent_table,
    first_moment,
    second_moment,
    ent_proj,
    pos_table,
    query_weight,
    query_bias,
    key_weight,
    key_bias,
    value_weight,
    value_bias,
    out_weight,
    out_bias,
    norm_gain,
    norm_shift,
    up_weight,
    up_bias,
    down_weight,
    down_bias,
    word_cot,
    ent_cot,
):
    n_dp = lax.axis_size("dp")
    nz = n_dp // 2
    width, ff = up_weight.shape
    all_words = segments.shape[1]
    words, word_cots, ent_cots, all_ids, rows = fetch(nz, word_states, word_cot, ent_cot, entity_ids, ent_table)
    ent_hidden, hidden_low, query_words, query_ents, keys, values, probs, mixed = forward(
        words,
        rows,
        entity_pos,
        segments,
        ent_proj,
        pos_table,
        query_weight,
        query_bias,
        key_weight,
        key_bias,
        value_weight,
        value_bias,
    )
    word_out, ent_out, grad_one, grad_mixed, ffn_grads, bias_middle = middle(
        nz,
        words,
        ent_hidden,
        mixed,
        out_weight,
        out_bias,
        norm_gain,
        norm_shift,
        up_weight,
        up_bias,
        down_weight,
        down_bias,
        word_cots,
        ent_cots,
    )
    ents = entity_ids.shape[1]
    word_grad, ffn_sum, attn_sum, ent_sum, bias_sum, table_grad, touched = backward(
        nz, all_words, hidden_low, query_words, query_ents, keys, values, probs, grad_mixed, query_weight, key_weight, value_weight,
        ffn_grads, grad_one, rows, entity_pos, ent_proj, bias_middle, all_ids.reshape(-1, ents), ent_table.shape[0],
    )
    (table_grad, table_update, new_second, proj_grad, pos_grad, query_grad, key_grad, value_grad, out_grad, up_grad, down_grad,
     query_bias_grad, gain_grad, shift_grad, key_bias_grad, value_bias_grad, out_bias_grad, down_bias_grad, up_bias_grad,
     word_out, ent_out, word_grad,
    ) = last(
        n_dp, ff, all_words, table_grad, touched, first_moment, second_moment, ffn_sum, attn_sum, ent_sum, bias_sum, word_out, ent_out, word_grad
    )
    return (
        word_out,
        ent_out,
        word_grad,
        proj_grad,
        pos_grad,
        query_grad,
        query_bias_grad,
        key_grad,
        key_bias_grad,
        value_grad,
        value_bias_grad,
        out_grad,
        out_bias_grad,
        gain_grad,
        shift_grad,
        up_grad,
        up_bias_grad,
        down_grad,
        down_bias_grad,
        table_grad,
        table_update,
        new_second,
    )


def solution(mesh):
    return jax.shard_map(
        on_device,
        mesh=mesh,
        in_specs=(
            P("dp", "seq", None),
            P("dp", None),
            P("dp", None),
            P("dp", None),
            P(("dp", "seq"), None),
            P(("dp", "seq"), None),
            P(("dp", "seq"), None),
            P(),
            P(),
            P(),
            P(),
            P(),
            P(),
            P(),
            P(),
            P(),
            P(),
            P(),
            P(),
            P(),
            P(),
            P(),
            P(),
            P("dp", "seq", None),
            P("dp", "seq", None),
        ),
        out_specs=(
            P("dp", "seq", None),
            P("dp", "seq", None),
            P("dp", "seq", None),
            P("dp", None),
            P("dp", None),
            P(None, "dp", None),
            P(None, "dp"),
            P("dp", None),
            P("dp"),
            P("dp", None),
            P("dp"),
            P("dp", None),
            P("dp"),
            P(None, "dp"),
            P(None, "dp"),
            P("dp", None),
            P("dp"),
            P("dp", None),
            P("dp"),
            P(("dp", "seq"), None),
            P(("dp", "seq"), None),
            P(("dp", "seq"), None),
        ),
        check_vma=False,
    )
```

```python
import functools
import math

import jax
import jax.numpy as jnp
from jax import lax
from jax.experimental import pallas as pl
from jax.experimental.pallas import tpu as pltpu
from jax.sharding import PartitionSpec as P

HEADS = 12
HEAD = 64
LANES = 128
MESH = pl.DeviceIdType.MESH
LOW = jnp.bfloat16
F32 = jnp.float32
VMEM_BYTES = 62 * 1024 * 1024

norm_eps = 1e-05
beta_one = 0.9
beta_two = 0.98
adam_eps = 1e-06
adam_step = 10.0
masked_score = -1e30


def dot(left, right):
    return jnp.dot(left, right, preferred_element_type=F32)


def dot_rows(left, right):
    return lax.dot_general(left, right, (((1,), (1,)), ((), ())), preferred_element_type=F32)


def dot_columns(left, right):
    return lax.dot_general(left, right, (((0,), (0,)), ((), ())), preferred_element_type=F32)


def span(start, size, unit):
    if isinstance(start, int):
        return pl.ds(start, size)
    return pl.ds(pl.multiple_of(start, unit), size)


def padded(rows):
    return -(-rows // 16) * 16


def loop(count, body, carry=0):
    return lax.fori_loop(0, count, body, carry)


class Place:
    def __init__(self, nz):
        self.dp, self.seq = lax.axis_index("dp"), lax.axis_index("seq")
        self.z, self.x = self.dp // 2, self.dp % 2
        self.y, self.core = self.seq // 2, self.seq % 2
        self.nz = nz
        self.other_core = (self.dp, self.y * 2 + 1 - self.core)
        self.other_y = (self.dp, (1 - self.y) * 2 + self.core)
        self.diagonal = (self.dp, (1 - self.y) * 2 + 1 - self.core)
        self.other_x = (self.z * 2 + 1 - self.x, self.seq)
        self.ahead = [(((self.z + k) % nz) * 2 + self.x, self.seq) for k in range(1, nz)]

    def z_ahead(self, k):
        return (self.z + k) % self.nz


def meet(partners):
    barrier = pltpu.get_barrier_semaphore()
    for partner in partners:
        pl.semaphore_signal(barrier, inc=1, device_id=partner, device_id_type=MESH)
    pl.semaphore_wait(barrier, len(partners))


class Remote:
    def __init__(self, copies, number, src, dst, device):
        self.copies, self.number, self.src, self.dst, self.device = copies, number, src, dst, device
        self.open = True

    def make(self, landing=False):
        return pltpu.make_async_remote_copy(
            src_ref=self.dst() if landing else self.src(),
            dst_ref=self.dst(),
            send_sem=self.copies.send_sem.at[self.number],
            recv_sem=self.copies.recv_sem.at[self.number],
            device_id=self.device,
            device_id_type=MESH,
        )

    def wait_recv(self):
        self.make(landing=True).wait_recv()

    def wait_send(self):
        if self.open:
            self.make().wait_send()
        self.open = False


class Local:
    def __init__(self, copies, number, src, dst):
        self.copies, self.number, self.src, self.dst = copies, number, src, dst

    def make(self):
        return pltpu.make_async_copy(self.src(), self.dst(), self.copies.local_sem.at[self.number])

    def wait(self):
        self.make().wait()


class Copies:
    def __init__(self, send_sem, recv_sem, local_sem):
        self.send_sem, self.recv_sem, self.local_sem = send_sem, recv_sem, local_sem
        self.local_count = 0
        self.sent = []

    def send(self, src, dst, device):
        copy = Remote(self, len(self.sent), src, dst, device)
        copy.make().start()
        self.sent.append(copy)
        return copy

    def local(self, src, dst):
        copy = Local(self, self.local_count, src, dst)
        self.local_count += 1
        copy.make().start()
        return copy

    def finish(self):
        for copy in self.sent:
            copy.wait_send()


def copy_semaphores(remote, local):
    return [
        pltpu.SemaphoreType.DMA((remote,)),
        pltpu.SemaphoreType.DMA((remote,)),
        pltpu.SemaphoreType.DMA((local,)),
    ]


ANY = pl.BlockSpec(memory_space=pl.ANY)
IN_VMEM = pl.BlockSpec(memory_space=pltpu.VMEM)


def call(kernel, outs, in_specs, out_specs, scratch, name, collective_id=None):
    params = {"vmem_limit_bytes": VMEM_BYTES}
    if collective_id is not None:
        params.update(collective_id=collective_id, has_side_effects=True)
    return pl.pallas_call(
        kernel,
        out_shape=[jax.ShapeDtypeStruct(shape, dtype) for shape, dtype in outs],
        in_specs=in_specs,
        out_specs=out_specs,
        scratch_shapes=scratch,
        compiler_params=pltpu.CompilerParams(**params),
        name=name,
    )


def fetch_kernel(nz, words, word_cot, ent_cot, ids, table, all_words, word_cots, ent_cots, all_ids, rows_out, *scratch):
    table_full, table_low, picked, answers, held, from_core, from_x, from_z, from_y, ids_here = scratch[:10]
    copies = Copies(*scratch[10:])
    place = Place(nz)
    z, x, y, core = place.z, place.x, place.y, place.core
    n_dp = 2 * nz
    word_here, ent_here = words.shape[1], ent_cot.shape[1]
    ents = ids.shape[1]
    dp_others = [((place.dp + k) % n_dp, place.seq) for k in range(1, n_dp)]
    meet([place.other_core, place.other_y, place.diagonal] + dp_others)
    whole_table = copies.local(lambda: table, lambda: table_full)
    ids_here[place.dp] = ids[...]
    id_copies = [copies.send(lambda: ids, lambda: ids_here.at[place.dp], device) for device in dp_others]
    quarter = span(place.seq * word_here, word_here, 128)
    word_copies = [
        copies.send(lambda: words.at[1 - core], lambda: all_words.at[quarter], place.diagonal),
        copies.send(lambda: words.at[core], lambda: all_words.at[quarter], place.other_y),
        copies.send(lambda: words.at[1 - core], lambda: all_words.at[quarter], place.other_core),
        copies.send(lambda: word_cot.at[1 - core], lambda: word_cots.at[span(core * word_here, word_here, 128)], place.other_core),
        copies.send(lambda: ent_cot.at[1 - core], lambda: ent_cots.at[span(core * ent_here, ent_here, 32)], place.other_core),
    ]
    all_words[quarter] = words[core]
    word_cots[span(core * word_here, word_here, 128)] = word_cot[core]
    ent_cots[span(core * ent_here, ent_here, 32)] = ent_cot[core]
    whole_table.wait()
    rows_dev = table.shape[0]

    def narrow(i, _):
        where = span(i * 128, 128, 128)
        table_low[where] = table_full[where].astype(LOW)
        return 0

    loop(rows_dev // 128, narrow)
    for copy in id_copies:
        copy.wait_recv()
    all_ids[...] = ids_here[...]
    base = (place.dp * 4 + place.seq) * rows_dev
    tiles = rows_dev // LANES

    def look_up(zz):
        def group(g, _):
            asked = ids_here[zz * 2 + g // 2, pl.ds(g % 2, 1), :] - base
            column = jnp.transpose(jnp.broadcast_to(asked, (ents, ents)))
            for j in range(tiles):
                number = lax.broadcasted_iota(jnp.int32, (ents, LANES), 1) + j * LANES
                hit = jnp.where(column == number, 1.0, 0.0).astype(LOW)
                picked[span(g * ents, ents, ents), pl.ds(j * LANES, LANES)] = hit
            return 0

        loop(4, group)
        answer = dot(picked[...], table_low[...]).astype(LOW)
        answers[zz] = answer.reshape(2, 2, ents, answer.shape[-1])

    order = [place.z_ahead(k + 1) for k in range(nz)]
    core_copies, x_copies, z_copies = [], [], []

    def core_send(zz):
        return copies.send(lambda: answers.at[zz, :, 1 - core], lambda: from_core.at[zz], place.other_core)

    def after_core(k):
        zz = order[k]
        core_copies[k].wait_recv()
        held[zz] = answers[zz, :, core] + from_core[zz]
        x_copies.append(copies.send(lambda: held.at[zz, 1 - x], lambda: from_x.at[zz], place.other_x))

    def after_x(k):
        zz = order[k]
        x_copies[k].wait_recv()
        held[zz, x] = held[zz, x] + from_x[zz]
        if k < nz - 1:
            z_copies.append(copies.send(lambda: held.at[zz, x], lambda: from_z.at[k], place.ahead[k]))

    for k in range(nz + 2):
        if k < nz:
            look_up(order[k])
            core_copies.append(core_send(order[k]))
        if 0 <= k - 1 < nz:
            after_core(k - 1)
        if 0 <= k - 2:
            after_x(k - 2)
    total = held[z, x]
    for k in range(nz - 1):
        z_copies[k].wait_recv()
        total = total + from_z[k]
    from_y[0] = total
    y_copy = copies.send(lambda: from_y.at[0], lambda: from_y.at[1], place.other_y)
    y_copy.wait_recv()
    rows_out[...] = from_y[0] + from_y[1]
    for copy in word_copies:
        copy.wait_recv()
    copies.finish()


def fetch(nz, words, word_cot, ent_cot, ids, table):
    _, word_here, width = words.shape
    ent_here, ents, (rows_dev, edim) = ent_cot.shape[1], ids.shape[1], table.shape
    n_dp = 2 * nz
    return call(
        functools.partial(fetch_kernel, nz),
        [
            ((4 * word_here, width), LOW),
            ((2 * word_here, width), LOW),
            ((2 * ent_here, width), LOW),
            ((n_dp, 2, ents), jnp.int32),
            ((ents, edim), LOW),
        ],
        [IN_VMEM] * 4 + [ANY],
        [IN_VMEM] * 5,
        [
            pltpu.VMEM((rows_dev, edim), F32),
            pltpu.VMEM((rows_dev, edim), LOW),
            pltpu.VMEM((4 * ents, rows_dev), LOW),
            pltpu.VMEM((nz, 2, 2, ents, edim), LOW),
            pltpu.VMEM((nz, 2, ents, edim), LOW),
            pltpu.VMEM((nz, 2, ents, edim), LOW),
            pltpu.VMEM((nz, ents, edim), LOW),
            pltpu.VMEM((nz - 1, ents, edim), LOW),
            pltpu.VMEM((2, ents, edim), LOW),
            pltpu.VMEM((n_dp, 2, ents), jnp.int32),
        ]
        + copy_semaphores(n_dp + 4 + 3 * nz + 2, 1),
        "fetch",
        1,
    )(words, word_cot, ent_cot, ids, table)


def lane_mask(rows, head):
    lane = lax.broadcasted_iota(jnp.int32, (rows, LANES), 1)
    return (lane >= head * HEAD) & (lane < (head + 1) * HEAD)


def row_of(vector):
    return vector[...].astype(F32).reshape(1, vector.shape[0])


def own_half(vector, y):
    row = row_of(vector)
    half = row.shape[1] // 2
    return jnp.where(y == 0, row[:, :half], row[:, half:])


def as_column(row):
    parts = [
        jnp.transpose(jnp.broadcast_to(row[:, i : i + LANES], (LANES, LANES)))
        for i in range(0, row.shape[1], LANES)
    ]
    return jnp.concatenate(parts, axis=0) if len(parts) > 1 else parts[0]


def forward_kernel(
    words, rows, ent_pos, segments, ent_proj, pos_table, query_weight, query_bias, key_weight, key_bias, value_weight, value_bias,
    ent_hidden, hidden_low, query_words, query_ents, keys, values, probs, mixed,
    query_here, key_here, value_here, values_turned, mask, mixed_turned, local_sem,
):
    y, core = lax.axis_index("seq") // 2, lax.axis_index("seq") % 2
    half = keys.shape[1]
    all_words, ents = words.shape[0], rows.shape[0]
    ent_pos, segments = ent_pos[pl.ds(core, 1), :], segments[pl.ds(core, 1), :]
    tokens = all_words + ents
    columns = span(y * half, half, LANES)
    weight_copies = [
        pltpu.make_async_copy(query_weight.at[:, :, columns], query_here, local_sem.at[0]),
        pltpu.make_async_copy(key_weight.at[:, columns], key_here, local_sem.at[1]),
        pltpu.make_async_copy(value_weight.at[:, columns], value_here, local_sem.at[2]),
    ]
    for copy in weight_copies:
        copy.start()
    position = as_column(ent_pos)
    picks = []
    for j in range(all_words // LANES):
        number = lax.broadcasted_iota(jnp.int32, (ents, LANES), 1) + j * LANES
        picks.append(jnp.where(position == number, 1.0, 0.0))
    pick = jnp.concatenate(picks, axis=1)
    word_seg = segments.astype(F32)
    ent_seg = jnp.sum(pick * word_seg, axis=1, keepdims=True)
    ent_hidden[...] = dot(rows[...], ent_proj[...]) + dot(pick.astype(LOW), pos_table[...])
    hidden_low[:all_words] = words[...]
    hidden_low[all_words:] = ent_hidden[...].astype(LOW)
    ent_row = jnp.transpose(jnp.broadcast_to(ent_seg, (ents, LANES)))[:1]
    seg_row = jnp.concatenate([word_seg, ent_row], axis=1)
    seg_column = jnp.concatenate([as_column(word_seg), jnp.broadcast_to(ent_seg, (ents, LANES))], axis=0)
    for j in range(tokens // LANES):
        here = slice(j * LANES, (j + 1) * LANES)
        mask[:, here] = jnp.where(seg_column == seg_row[:, here], 0.0, masked_score)

    query_b = query_bias[:, columns].astype(F32)
    for copy in weight_copies:
        copy.wait()
    word_low, ent_low = hidden_low[:all_words], hidden_low[all_words:]
    query_words[:all_words] = (dot(word_low, query_here[0]) + query_b[0:1]).astype(LOW)
    query_ents[:all_words] = (dot(word_low, query_here[1]) + query_b[1:2]).astype(LOW)
    query_words[all_words:] = (dot(ent_low, query_here[2]) + query_b[2:3]).astype(LOW)
    query_ents[all_words:] = (dot(ent_low, query_here[3]) + query_b[3:4]).astype(LOW)
    keys[...] = (dot(hidden_low[...], key_here[...]) + own_half(key_bias, y)).astype(LOW)
    value = dot(hidden_low[...], value_here[...]) + own_half(value_bias, y)
    values[...] = value.astype(LOW)
    values_turned[...] = jnp.transpose(value).astype(LOW)
    scale = 1.0 / math.sqrt(HEAD)
    tiles = tokens // LANES

    def tile(i, _):
        pair, place = i // tiles, span((i % tiles) * LANES, LANES, LANES)
        lanes = span(pair * LANES, LANES, LANES)
        key = keys[:, lanes]
        query_w, query_e = query_words[place, lanes], query_ents[place, lanes]
        turned = values_turned[lanes, :]
        total = jnp.zeros((LANES, LANES), F32)
        for head in range(2):
            own_key = jnp.where(lane_mask(tokens, head), key, jnp.zeros_like(key))
            raw = jnp.concatenate(
                [dot_rows(own_key[:all_words], query_w), dot_rows(own_key[all_words:], query_e)], axis=0
            )
            score = raw * scale + mask[:, place]
            weight = jnp.exp(score - jnp.max(score, axis=0, keepdims=True))
            prob = (weight * (1.0 / jnp.sum(weight, axis=0, keepdims=True))).astype(LOW)
            probs[pair * 2 + head, :, place] = prob
            row = lax.broadcasted_iota(jnp.int32, (LANES, tokens), 0)
            own_rows = (row >= head * HEAD) & (row < (head + 1) * HEAD)
            total = total + dot(jnp.where(own_rows, turned, jnp.zeros_like(turned)), prob)
        mixed[place, lanes] = jnp.transpose(total).astype(LOW)
        return 0

    loop(half // LANES * tiles, tile)


def forward(words, rows, ent_pos, segments, ent_proj, pos_table, query_weight, query_bias, key_weight, key_bias, value_weight, value_bias):
    all_words, width = words.shape
    ents = rows.shape[0]
    tokens, half = all_words + ents, width // 2
    return call(
        forward_kernel,
        [
            ((ents, width), F32),
            ((tokens, width), LOW),
            ((tokens, half), LOW),
            ((tokens, half), LOW),
            ((tokens, half), LOW),
            ((tokens, half), LOW),
            ((HEADS // 2, tokens, tokens), LOW),
            ((tokens, half), LOW),
        ],
        [IN_VMEM] * 6 + [ANY, IN_VMEM, ANY, IN_VMEM, ANY, IN_VMEM],
        [IN_VMEM] * 8,
        [
            pltpu.VMEM((4, width, half), LOW),
            pltpu.VMEM((width, half), LOW),
            pltpu.VMEM((width, half), LOW),
            pltpu.VMEM((half, tokens), LOW),
            pltpu.VMEM((tokens, tokens), F32),
            pltpu.VMEM((LANES, tokens), F32),
            pltpu.SemaphoreType.DMA((3,)),
        ],
        "forward",
    )(words, rows, ent_pos, segments, ent_proj, pos_table, query_weight, query_bias, key_weight, key_bias, value_weight, value_bias)


class Engine:
    RATES = {"core": 300e3, "x": 50e3, "y": 50e3, "z": 12.5e3}
    LATENCY = 1.5

    def __init__(self):
        self.clock, self.free, self.streams = 0.0, {}, []

    def transfer(self, link, size):
        start = max(self.clock, self.free.get(link, 0.0))
        self.free[link] = start + size / self.RATES[link]
        return self.free[link] + self.LATENCY

    def add(self, steps):
        self.streams.append([self.clock, list(steps)])
        self.poll()

    def run(self, stream):
        self.clock = max(self.clock, stream[0])
        ready = stream[1].pop(0)()
        stream[0] = self.clock if ready is None else ready

    def next(self):
        live = [stream for stream in self.streams if stream[1]]
        return min(live, key=lambda stream: stream[0]) if live else None

    def poll(self):
        while (stream := self.next()) is not None and stream[0] <= self.clock:
            self.run(stream)

    def work(self, time):
        self.clock += time
        self.poll()

    def drain(self):
        while (stream := self.next()) is not None:
            self.run(stream)


def blocks_of(rows):
    for size in (96, 64, 48, 32):
        if rows % size == 0:
            return size
    return 16


def add_blocks(engine, target, parts, leading, rows, columns):
    size = blocks_of(rows)
    count = rows // size

    def block(i, _):
        lead, row = i // count, (i % count) * size
        where = span(row, size, 16)
        if len(parts) == 2:
            value = parts[0](lead, where) + parts[1](lead, where)
        else:
            value = parts[0](lead, where).astype(F32)
            for part in parts[1:]:
                value = value + part(lead, where).astype(F32)
            value = value.astype(LOW)
        target(lead, where, value)
        return 0

    loop(leading * count, block)
    engine.clock += 0.3 + leading * rows * columns / 1e6


class Job:
    def __init__(self, grads, reduced, base, size, order, columns):
        self.grads, self.reduced, self.base, self.size, self.order, self.columns = grads, reduced, base, size, order, columns
        self.half = size // 2
        self.part = size // 4 if order == "yxz" else size // 2

    def scratch(self, nz, resident):
        shapes = [(nz, 2, self.half, self.columns)] * (1 if resident else 2)
        if self.order == "yxz":
            shapes.append((nz, 2, self.part, self.columns))
        elif self.order == "xzy":
            shapes.append((2, self.part, self.columns))
        shapes += [(nz, self.part, self.columns), (nz - 1, self.part, self.columns)]
        return [pltpu.VMEM(shape, LOW) for shape in shapes]

    def remote_count(self, nz):
        return 1 + (1 if self.order != "xz" else 0) + 1 + (nz - 1) + 1 + 1

    def prepare(self, engine, place, copies, scratch):
        nz, z, x, y, core = place.nz, place.z, place.x, place.y, place.core
        base, half, part, order, columns = self.base, self.half, self.part, self.order, self.columns
        if self.grads is not None:
            scratch = [self.grads.at[:, :, span(base + core * half, half, 16)]] + list(scratch)
        self.held, from_core = scratch[:2]
        held = self.held
        from_y = scratch[2] if order != "xz" else None
        from_x, from_z = scratch[-2:]
        live = {}
        row_bytes = 2 * columns
        theirs = span(base + (1 - core) * half, half, 16)
        mine = span(base + core * half, half, 16)
        own_rows = span(y * part, part, 16) if order == "yxz" else pl.ds(0, part)
        final_rows = span(base + core * half + (y * part if order == "yxz" else 0), part, 16)

        def start(source=None):
            if source is None:
                source = lambda: self.grads.at[:, :, theirs]
            self.sent = live["core"] = copies.send(source, lambda: from_core, place.other_core)
            return engine.transfer("core", 2 * nz * half * row_bytes)

        def send_x():
            live["x"] = copies.send(lambda: held.at[:, 1 - x, own_rows], lambda: from_x, place.other_x)
            return engine.transfer("x", nz * part * row_bytes)

        def after_core():
            live["core"].wait_recv()

            def put(i, where, value):
                held[i // 2, i % 2, where] = value

            add_blocks(
                engine,
                put,
                [lambda i, where: held[i // 2, i % 2, where], lambda i, where: from_core[i // 2, i % 2, where]],
                2 * nz,
                half,
                columns,
            )
            if order == "yxz":
                live["y"] = copies.send(
                    lambda: held.at[:, :, span((1 - y) * part, part, 16)], lambda: from_y, place.other_y
                )
                return engine.transfer("y", 2 * nz * part * row_bytes)
            return send_x()

        def shifted(where):
            return span(y * part + where.start, where.size, 16) if order == "yxz" else where

        def after_y():
            live["y"].wait_recv()

            def put(i, where, value):
                held[i // 2, i % 2, shifted(where)] = value

            add_blocks(
                engine,
                put,
                [lambda i, where: held[i // 2, i % 2, shifted(where)], lambda i, where: from_y[i // 2, i % 2, where]],
                2 * nz,
                part,
                columns,
            )
            return send_x()

        def send_z(k):
            return copies.send(
                lambda: held.at[place.z_ahead(k + 1), x, own_rows], lambda: from_z.at[k], place.ahead[k]
            )

        def after_x():
            live["x"].wait_recv()

            def put(i, where, value):
                held[i, x, shifted(where)] = value

            add_blocks(
                engine,
                put,
                [lambda i, where: held[i, x, shifted(where)], lambda i, where: from_x[i, where]],
                nz,
                part,
                columns,
            )
            live["z"] = [send_z(k) for k in range(nz - 1)]
            return engine.transfer("z", part * row_bytes)

        def after_z():
            for copy in live["z"]:
                copy.wait_recv()

            def put(i, where, value):
                if order == "yxz":
                    self.reduced[span(base + core * half + y * part + where.start, where.size, 16)] = value
                elif order == "xz":
                    self.reduced[y, span(base + core * half + where.start, where.size, 16)] = value
                else:
                    from_y[0, where] = value

            def parts(k):
                return lambda i, where: from_z[k, where]

            add_blocks(
                engine,
                put,
                [lambda i, where: held[z, x, shifted(where)]] + [parts(k) for k in range(nz - 1)],
                1,
                part,
                columns,
            )
            if order == "xzy":
                live["y2"] = copies.send(lambda: from_y.at[0], lambda: from_y.at[1], place.other_y)
            else:
                view = lambda: self.reduced.at[final_rows] if order == "yxz" else self.reduced.at[y, final_rows]
                live["y2"] = copies.send(view, view, place.other_y)
            return engine.transfer("y", part * row_bytes)

        def after_gather():
            live["y2"].wait_recv()
            if order == "xzy":

                def put(i, where, value):
                    self.reduced[span(base + core * half + where.start, where.size, 16)] = value

                add_blocks(
                    engine, put, [lambda i, where: from_y[0, where], lambda i, where: from_y[1, where]], 1, part, columns
                )
            view = lambda: self.reduced.at[:, mine] if order == "xz" else self.reduced.at[mine]
            live["core2"] = copies.send(view, view, place.other_core)
            return engine.transfer("core", 2 * half * row_bytes)

        def end():
            live["core2"].wait_recv()

        middle_steps = [after_core, after_y, after_x] if order == "yxz" else [after_core, after_x]
        self.begin, self.rest = start, middle_steps + [after_z, after_gather, end]

    def launch(self, engine, source=None):
        engine.add([lambda: self.begin(source)] + self.rest)


def lane_mean(value):
    return jnp.mean(value, axis=-1, keepdims=True)


def column_sum(value):
    return jnp.sum(value, axis=0, keepdims=True)


ROW_BLOCK = 32


def ffn_plan(n_dp, width, ff):
    down_rows, row_pad = ff // n_dp, padded(width // n_dp)
    size = 128 if down_rows % 128 == 0 else 32
    order = "yxz" if size % 64 == 0 else "xzy"
    plan = [(base, size, order) for base in range(0, down_rows, size)]
    base = down_rows
    for pair in range(ff // width // 2):
        order = "yxz" if pair % 2 == 0 and row_pad % 32 == 0 else "xzy"
        plan.append((base, 2 * row_pad, order))
        base += 2 * row_pad
    plan.append((base, row_pad, "xzy"))
    return plan


def layer_kernel(
    nz, plan, words, ent_hidden, mixed, out_weight, out_bias, gains, shifts, up_weight, up_bias, down_weight, down_bias, word_cots, ent_cots,
    hidden_low_in, query_words_in, query_ents_in, keys_in, values_in, probs_in, query_weight, key_weight, value_weight, rows, ent_pos, ent_proj, ids,
    word_out, ent_out, word_grad, ffn_reduced, attn_reduced, ent_reduced, bias_out, table_grad, touched, *scratch,
):
    (from_y_mixed, grad_mixed, grad_one, given, ffn_sum, attn_sum, ent_sum, bias_held, bias_from, all_rows, bias_heads, bias_middle) = scratch[:12]
    copies = Copies(*scratch[-3:])
    engine = Engine()
    place = Place(nz)
    z, x, y, core = place.z, place.x, place.y, place.core
    n_dp = 2 * nz
    tokens, half = mixed.shape
    width = 2 * half
    ents = ent_hidden.shape[0]
    all_words = tokens - ents
    word_half, ent_half = all_words // 2, ents // 2
    part_tokens = tokens // 2
    ff = up_weight.shape[1]
    parts = ff // width
    row_part, row_pad, down_rows = width // n_dp, padded(width // n_dp), ff // n_dp
    meet([place.other_core, place.other_y, place.other_x] + place.ahead)

    jobs = {"ffn": [], "attn": [], "ent": []}

    def make_jobs(names, sources):
        at = 12
        for name, base, size, order, columns in plan:
            job = Job(*sources.get(name, (None, None)), base, size, order, columns)
            used = len(job.scratch(nz, name != "ffn"))
            if name in names:
                job.prepare(engine, place, copies, scratch[at : at + used])
                jobs[name].append(job)
            at += used

    make_jobs(["ffn"], {"ffn": (None, ffn_sum)})

    def token_rows(side):
        return span(side * word_half, word_half, LANES), span(all_words + side * ent_half, ent_half, 64)

    mine, theirs = token_rows(y), token_rows(1 - y)
    own_columns, other_columns = span(y * half, half, LANES), span((1 - y) * half, half, LANES)
    word_part, ent_part = pl.ds(0, word_half), pl.ds(word_half, ent_half)
    mixed_copies = [
        copies.send(lambda: mixed.at[theirs[0]], lambda: from_y_mixed.at[word_part], place.other_y),
        copies.send(lambda: mixed.at[theirs[1]], lambda: from_y_mixed.at[ent_part], place.other_y),
    ]
    engine.transfer("y", part_tokens * half * 2)
    out_copies, mixed_back = [], []

    def forward_phase(
        out_here, up_here, down_here, word_here, ent_here, mixed_full, work, normed_low, normal_one, inverse_one,
        act, slope, output, cot, grad_two, grad_two_low, grad_up_low, grad_one_low, grad_mixed_here, normed_turned, staged,
    ):
        weight_copies = [
            copies.local(lambda: out_weight, lambda: out_here),
            copies.local(lambda: words.at[mine[0]], lambda: word_here),
            copies.local(lambda: ent_hidden.at[span(y * ent_half, ent_half, 64)], lambda: ent_here),
            copies.local(lambda: up_weight, lambda: up_here),
            copies.local(lambda: down_weight, lambda: down_here),
            copies.local(lambda: word_cots, lambda: cot.at[word_part]),
            copies.local(lambda: ent_cots, lambda: cot.at[ent_part]),
        ]
        gain, shift = gains[...].astype(F32), shifts[...].astype(F32)
        out_b, down_b, up_b = row_of(out_bias), row_of(down_bias), row_of(up_bias)
        mixed_full[word_part, own_columns] = mixed[mine[0]]
        mixed_full[ent_part, own_columns] = mixed[mine[1]]
        for copy in weight_copies[:3]:
            copy.wait()
        for copy in mixed_copies:
            copy.wait_recv()
        mixed_full[:, other_columns] = from_y_mixed[...]
        work[...] = dot(mixed_full[...], out_here[...])

        def norm_one(residual):
            def step(i, _):
                rows = span(residual[1] + i * ROW_BLOCK, ROW_BLOCK, ROW_BLOCK)
                value = residual[0][span(i * ROW_BLOCK, ROW_BLOCK, ROW_BLOCK)].astype(F32) + (work[rows] + out_b)
                center = value - lane_mean(value)
                inverse = lax.rsqrt(lane_mean(center * center) + norm_eps)
                normal = center * inverse
                result = normal * gain[0:1] + shift[0:1]
                normal_one[rows] = normal
                inverse_one[rows] = jnp.broadcast_to(inverse, (ROW_BLOCK, LANES))
                normed_low[rows] = result.astype(LOW)
                return 0

            return step

        loop(word_half // ROW_BLOCK, norm_one((word_here, 0)))
        loop(ent_half // ROW_BLOCK, norm_one((ent_here, word_half)))
        weight_copies[3].wait()
        for j in range(parts):
            columns = slice(j * width, (j + 1) * width)
            work[...] = dot(normed_low[...], up_here[:, columns]) + up_b[:, columns]

            def gelu(i, _):
                rows = span(i * 16, 16, 16)
                value = work[rows]
                below = 0.5 * (1.0 + lax.erf(value * (1.0 / math.sqrt(2.0))))
                density = jnp.exp(-0.5 * value * value) * (1.0 / math.sqrt(2.0 * math.pi))
                act[rows, columns] = (value * below).astype(LOW)
                slope[rows, columns] = (below + value * density).astype(LOW)
                return 0

            loop(part_tokens // 16, gelu)
        normed_turned[...] = jnp.transpose(normed_low[...].astype(F32)).astype(LOW)
        for copy in weight_copies[4:]:
            copy.wait()
        work[...] = dot(act[...], down_here[...])

        def norm_two(i, sums):
            rows = span(i * ROW_BLOCK, ROW_BLOCK, ROW_BLOCK)
            value = (normal_one[rows] * gain[0:1] + shift[0:1]) + (work[rows] + down_b)
            center = value - lane_mean(value)
            inverse = lax.rsqrt(lane_mean(center * center) + norm_eps)
            normal = center * inverse
            output[rows] = (normal * gain[1:2] + shift[1:2]).astype(LOW)
            cotangent = cot[rows].astype(F32)
            scaled = cotangent * gain[1:2]
            result = inverse * (scaled - lane_mean(scaled) - normal * lane_mean(scaled * normal))
            grad_two[rows] = result
            grad_two_low[rows] = result.astype(LOW)
            return (
                sums[0] + column_sum(cotangent * normal),
                sums[1] + column_sum(cotangent),
                sums[2] + column_sum(result),
            )

        nothing = jnp.zeros((1, width), F32)
        gain_two, shift_two, down_sum = loop(part_tokens // ROW_BLOCK, norm_two, (nothing, nothing, nothing))
        quarter, ent_quarter = word_half // 2, ent_half // 2
        out_copies.extend([
            copies.send(
                lambda: output.at[span((1 - core) * quarter, quarter, LANES)], lambda: word_out.at[core], place.other_core
            ),
            copies.send(
                lambda: output.at[span(word_half + (1 - core) * ent_quarter, ent_quarter, 32)],
                lambda: ent_out.at[core],
                place.other_core,
            ),
        ])
        out_local = [
            copies.local(lambda: output.at[span(core * quarter, quarter, LANES)], lambda: word_out.at[core]),
            copies.local(
                lambda: output.at[span(word_half + core * ent_quarter, ent_quarter, 32)], lambda: ent_out.at[core]
            ),
        ]
        engine.clock = 0.0
        engine.free = {}
        sent, turn = [None, None], [0]

        def slot():
            number = turn[0] % 2
            turn[0] += 1
            if sent[number] is not None:
                sent[number].wait_send()
            return number

        def split(job, number, rows_in):
            job_half = job.half

            def keep(i, _):
                job.held[i // 2, i % 2] = staged[number, i // 2, i % 2, span(core * job_half, job_half, 16)]
                return 0

            loop(n_dp, keep)
            job.launch(
                engine, lambda: staged.at[number, :, :, span((1 - core) * job_half, job_half, 16)]
            )
            sent[number] = job.sent
            engine.work(0.3)

        def down_block(job):
            number = slot()
            if down_rows % 128:
                per = width // down_rows
                for j in range(parts):
                    value = dot_columns(act[:, j * width : (j + 1) * width], grad_two_low[...])
                    value = value.reshape(per, down_rows, width)[:, job.base : job.base + job.size].astype(LOW)
                    for d in range(per):
                        slab = j * per + d
                        staged[number, slab // 2, slab % 2, pl.ds(0, job.size)] = value[d]
            else:
                for slab in range(n_dp):
                    start = slab * down_rows + job.base
                    value = dot_columns(act[:, start : start + job.size], grad_two_low[...])
                    staged[number, slab // 2, slab % 2, pl.ds(0, job.size)] = value.astype(LOW)
            engine.work(1.3)
            split(job, number, job.size)

        def up_block(job, pair):
            own = grad_up_low[:, span((2 * pair + core) * width, width, LANES)]
            value = dot(normed_turned[...], own).astype(LOW).reshape(nz, 2, row_part, width)
            job.held[:, :, pl.ds(0, row_part)] = value
            number = slot()
            other = grad_up_low[:, span((2 * pair + 1 - core) * width, width, LANES)]
            value = dot(normed_turned[...], other).astype(LOW).reshape(nz, 2, row_part, width)
            staged[number, :, :, pl.ds(0, row_part)] = value
            engine.work(1.8)
            job.launch(engine, lambda: staged.at[number, :, :, pl.ds(0, row_pad)])
            sent[number] = job.sent

        up_sums = []

        def grad_up(j):
            columns = slice(j * width, (j + 1) * width)
            work[...] = dot_rows(grad_two_low[...], down_here[columns, :])

            def grad_gelu(i, total_row):
                rows = span(i * 16, 16, 16)
                value = work[rows] * slope[rows, columns].astype(F32)
                grad_up_low[rows, columns] = value.astype(LOW)
                return total_row + column_sum(value)

            up_sums.append(loop(part_tokens // 16, grad_gelu, nothing))
            engine.work(1.6)

        downs = [job for job in jobs["ffn"] if job.base < down_rows]
        ups = [job for job in jobs["ffn"] if down_rows <= job.base][:-1]
        for job in downs:
            down_block(job)
        for j in range(parts):
            grad_up(j)
            if j % 2 == 1:
                up_block(ups[j // 2], j // 2)
        work[...] = dot_rows(grad_up_low[...], up_here[...])
        engine.work(2.0)

        def back_one(i, sums):
            rows = span(i * ROW_BLOCK, ROW_BLOCK, ROW_BLOCK)
            upper = grad_two[rows] + work[rows]
            normal = normal_one[rows]
            inverse = inverse_one[rows, 0:1]
            scaled = upper * gain[0:1]
            result = inverse * (scaled - lane_mean(scaled) - normal * lane_mean(scaled * normal))
            grad_one[rows] = result
            grad_one_low[rows] = result.astype(LOW)
            return (
                sums[0] + column_sum(upper * normal),
                sums[1] + column_sum(upper),
                sums[2] + column_sum(result),
            )

        gain_one, shift_one, out_sum = loop(part_tokens // ROW_BLOCK, back_one, (nothing, nothing, nothing))
        engine.work(1.0)
        grad_mixed_here[...] = dot_rows(grad_one_low[...], out_here[other_columns, :]).astype(LOW)
        mixed_back.extend([
            copies.send(lambda: grad_mixed_here.at[word_part], lambda: grad_mixed.at[mine[0]], place.other_y),
            copies.send(lambda: grad_mixed_here.at[ent_part], lambda: grad_mixed.at[mine[1]], place.other_y),
        ])
        engine.transfer("y", part_tokens * half * 2)
        own = dot_rows(grad_one_low[...], out_here[own_columns, :]).astype(LOW)
        grad_mixed[mine[0]] = own[:word_half]
        grad_mixed[mine[1]] = own[word_half:]
        engine.work(1.0)
        number = slot()
        value = dot_columns(mixed_full[...], grad_one_low[...]).astype(LOW)
        staged[number, :, :, pl.ds(0, row_part)] = value.reshape(nz, 2, row_part, width)
        engine.work(0.8)
        split(jobs["ffn"][-1], number, row_pad)
        bias_rows = [out_sum, gain_one, gain_two, shift_one, shift_two] + up_sums + [down_sum]
        for i, row in enumerate(bias_rows):
            bias_middle[i : i + 1] = row
        for copy in sent:
            copy.wait_send()
        for copy in mixed_back + out_copies:
            copy.wait_send()
        for copy in out_local:
            copy.wait()

    tall = lambda columns, dtype: pltpu.VMEM((part_tokens, columns), dtype)
    stage_rows = max([job.size for job in jobs["ffn"] if job.base < down_rows] + [row_pad])
    pl.run_scoped(
        forward_phase,
        pltpu.VMEM((width, width), LOW),
        pltpu.VMEM((width, ff), LOW),
        pltpu.VMEM((ff, width), LOW),
        pltpu.VMEM((word_half, width), LOW),
        pltpu.VMEM((ent_half, width), F32),
        tall(width, LOW),
        tall(width, F32),
        tall(width, LOW),
        tall(width, F32),
        tall(LANES, F32),
        tall(ff, LOW),
        tall(ff, LOW),
        tall(width, LOW),
        tall(width, LOW),
        tall(width, F32),
        tall(width, LOW),
        tall(ff, LOW),
        tall(width, LOW),
        tall(half, LOW),
        pltpu.VMEM((width, part_tokens), LOW),
        pltpu.VMEM((2, nz, 2, stage_rows, width), LOW),
    )
    live_words = {}

    def backward_phase(
        hidden_low, query_words, query_ents, keys, values, probs, query_here, key_here, value_here, keys_turned, grad_scores,
        grad_query_words, grad_query_ents, grad_keys, grad_values, hidden_turned, grad_hidden, hits, total, attn_grads, ent_grads, table_here, touched_here,
    ):
        make_jobs(["attn", "ent"], {"attn": (attn_grads, attn_sum), "ent": (ent_grads, ent_sum)})
        columns = span(y * half, half, LANES)
        copies_in = [
            copies.local(lambda: values_in, lambda: values),
            copies.local(lambda: keys_in, lambda: keys),
            copies.local(lambda: query_words_in, lambda: query_words),
            copies.local(lambda: query_ents_in, lambda: query_ents),
        ]
        prob_copies = []
        for head in range(probs.shape[0]):
            prob_copies.append(
                copies.local(lambda head=head: probs_in.at[head], lambda head=head: probs.at[head])
            )
        hidden_copy = copies.local(lambda: hidden_low_in, lambda: hidden_low)
        weight_copies = [
            copies.local(lambda: query_weight.at[:, :, columns], lambda: query_here),
            copies.local(lambda: key_weight.at[:, columns], lambda: key_here),
            copies.local(lambda: value_weight.at[:, columns], lambda: value_here),
        ]
        for copy in copies_in:
            copy.wait()
        for i in range(half // LANES):
            lanes = slice(i * LANES, (i + 1) * LANES)
            keys_turned[lanes, :] = jnp.transpose(keys[:, lanes].astype(F32)).astype(LOW)
        hidden_copy.wait()
        for i in range(width // LANES):
            lanes = slice(i * LANES, (i + 1) * LANES)
            hidden_turned[lanes, :] = jnp.transpose(hidden_low[:, lanes].astype(F32)).astype(LOW)
        for copy in mixed_back:
            copy.wait_recv()
        engine.work(2.0)
        scale = 1.0 / math.sqrt(HEAD)
        tiles = tokens // LANES

        for pair in range(half // LANES):
            lanes = slice(pair * LANES, (pair + 1) * LANES)
            grad_query_w = jnp.zeros((LANES, tokens), F32)
            grad_query_e = jnp.zeros((LANES, tokens), F32)
            grad_key_w = jnp.zeros((all_words, LANES), F32)
            grad_key_e = jnp.zeros((ents, LANES), F32)
            grad_value = jnp.zeros((tokens, LANES), F32)
            for head in range(2):
                own = lane_mask(tokens, head)
                value = values[:, lanes]
                own_value = jnp.where(own, value, jnp.zeros_like(value))
                prob_copies[pair * 2 + head].wait()

                def tile(i, _):
                    where = span(i * LANES, LANES, LANES)
                    grad_prob = dot_rows(own_value, grad_mixed[where, lanes])
                    prob = probs[pair * 2 + head, :, where].astype(F32)
                    both = prob * grad_prob
                    grad_scores[:, where] = (both - prob * jnp.sum(both, axis=0, keepdims=True)).astype(LOW)
                    return 0

                loop(tiles, tile)
                engine.work(1.7)
                given_heads = grad_mixed[:, lanes]
                grad_value += dot(probs[pair * 2 + head], jnp.where(own, given_heads, jnp.zeros_like(given_heads)))
                query_w, query_e = query_words[:, lanes], query_ents[:, lanes]
                grad_key_w += dot(grad_scores[:all_words], jnp.where(own, query_w, jnp.zeros_like(query_w)))
                grad_key_e += dot(grad_scores[all_words:], jnp.where(own, query_e, jnp.zeros_like(query_e)))
                row = lax.broadcasted_iota(jnp.int32, (LANES, tokens), 0)
                own_rows = (row >= head * HEAD) & (row < (head + 1) * HEAD)
                turned = keys_turned[lanes, :]
                turned = jnp.where(own_rows, turned, jnp.zeros_like(turned))
                grad_query_w += dot(turned[:, :all_words], grad_scores[:all_words])
                grad_query_e += dot(turned[:, all_words:], grad_scores[all_words:])
                engine.work(1.7)
            grad_query_w = jnp.transpose(grad_query_w) * scale
            grad_query_e = jnp.transpose(grad_query_e) * scale
            grad_key_w, grad_key_e = grad_key_w * scale, grad_key_e * scale
            sums = [
                column_sum(grad_query_w[:all_words]),
                column_sum(grad_query_e[:all_words]),
                column_sum(grad_query_w[all_words:]),
                column_sum(grad_query_e[all_words:]),
                column_sum(grad_key_w) + column_sum(grad_key_e),
                column_sum(grad_value),
            ]
            for i, sum_row in enumerate(sums):
                bias_heads[i : i + 1, lanes] = sum_row
            grad_query_words[:, lanes] = grad_query_w.astype(LOW)
            grad_query_ents[:, lanes] = grad_query_e.astype(LOW)
            grad_keys[:all_words, lanes] = grad_key_w.astype(LOW)
            grad_keys[all_words:, lanes] = grad_key_e.astype(LOW)
            grad_values[:, lanes] = grad_value.astype(LOW)
            engine.work(0.5)

        for copy in weight_copies:
            copy.wait()
        ent_rows, word_rows = slice(all_words, tokens), slice(0, all_words)

        def hidden_part(here, first, second):
            grad_hidden[here] = (
                dot_rows(grad_keys[here], key_here[...])
                + dot_rows(grad_values[here], value_here[...])
                + dot_rows(grad_query_words[here], query_here[first])
                + dot_rows(grad_query_ents[here], query_here[second])
            ).astype(LOW)

        hidden_part(ent_rows, 2, 3)
        ent_copy = copies.send(lambda: grad_hidden.at[theirs[1]], lambda: given.at[ent_part], place.other_y)
        ent_ready = engine.transfer("y", ent_half * width * 2)
        engine.work(0.7)
        word_turned, ent_turned = hidden_turned[:, :all_words], hidden_turned[:, all_words:]
        attn_jobs = jobs["attn"]

        def attn_product(i, value):
            attn_grads[:, :, pl.ds(i * row_pad, row_part)] = value.astype(LOW).reshape(nz, 2, row_part, half)
            per = 6 // len(attn_jobs)
            if i % per == per - 1:
                attn_jobs[i // per].launch(engine)
            engine.work(0.6)

        attn_product(0, dot(word_turned, grad_query_words[:all_words]))
        attn_product(1, dot(word_turned, grad_query_ents[:all_words]))

        live_rows = {}

        def sum_hidden(start, count, own_start):
            def block(i, _):
                where = span(start + i * 32, 32, 32)
                own = span(own_start + i * 32, 32, 32)
                total[where] = grad_one[where] + (grad_hidden[own].astype(F32) + given[where].astype(F32))
                return 0

            loop(count // 32, block)

        row_bytes = ent_half * ent_proj.shape[0] * 2

        def rows_y():
            ent_copy.wait_recv()
            sum_hidden(word_half, ent_half, all_words + y * ent_half)
            row_grad = dot_rows(total[word_half:].astype(LOW), ent_proj[...]).astype(LOW)
            all_rows[place.dp, core, span(y * ent_half, ent_half, 64)] = row_grad
            view = lambda: all_rows.at[place.dp, core, span(y * ent_half, ent_half, 64)]
            live_rows["y"] = copies.send(view, view, place.other_y)
            return engine.transfer("y", row_bytes)

        def rows_z():
            live_rows["y"].wait_recv()
            view = lambda: all_rows.at[place.dp, core]
            live_rows["z"] = [copies.send(view, view, device) for device in place.ahead]
            return engine.transfer("z", 2 * row_bytes)

        def rows_x():
            for copy in live_rows["z"]:
                copy.wait_recv()
            live_rows["x"] = []
            for k in range(nz):
                view = lambda k=k: all_rows.at[place.z_ahead(k) * 2 + x, core]
                live_rows["x"].append(copies.send(view, view, place.other_x))
            return engine.transfer("x", nz * 2 * row_bytes)

        def rows_core():
            for copy in live_rows["x"]:
                copy.wait_recv()
            view = lambda: all_rows.at[:, core]
            live_rows["core"] = copies.send(view, view, place.other_core)
            return engine.transfer("core", n_dp * 2 * row_bytes)

        rows_dev = table_grad.shape[0]
        table_copies = []
        base_row = (place.dp * 4 + place.seq) * rows_dev

        def table_part(i):
            def step():
                if i == 0:
                    live_rows["core"].wait_recv()
                groups = ids.shape[0]
                number = lax.broadcasted_iota(jnp.int32, (table_block, ents), 0) + (base_row + i * table_block)
                count = jnp.zeros((table_block, ents), F32)
                for group in range(groups):
                    hit = jnp.where(ids[group : group + 1, :] == number, 1.0, 0.0)
                    count = count + hit
                    hits[:, group * ents : (group + 1) * ents] = hit.astype(LOW)
                here = pl.ds(i * table_block, table_block)
                for copy in table_copies[2 * i - 4 : 2 * i - 2] if i >= 2 else []:
                    copy.wait()
                dps = min(n_dp, 8)
                grad = None
                for first in range(0, n_dp, dps):
                    given_rows = all_rows[first : first + dps].reshape(dps * 2 * ents, ent_proj.shape[0])
                    value = dot(hits[:, first * 2 * ents : (first + dps) * 2 * ents], given_rows)
                    grad = value if grad is None else grad + value
                table_here[i % 2] = grad
                named = jnp.sum(count, axis=1, keepdims=True)
                touched_here[i % 2] = jnp.broadcast_to(named, (table_block, LANES)).astype(LOW)
                table_copies.append(copies.local(lambda: table_here.at[i % 2], lambda: table_grad.at[here]))
                table_copies.append(copies.local(lambda: touched_here.at[i % 2], lambda: touched.at[here]))
                engine.clock += 1.2

            return step

        engine.add(
            [lambda: ent_ready, rows_y, rows_z, rows_x, rows_core] + [table_part(i) for i in range(rows_dev // table_block)]
        )
        hidden_part(word_rows, 0, 1)
        word_copy = copies.send(lambda: grad_hidden.at[theirs[0]], lambda: given.at[word_part], place.other_y)
        word_ready = engine.transfer("y", word_half * width * 2)
        engine.work(1.5)

        bias_rows = bias_held.shape[0]
        bias_held[...] = jnp.zeros_like(bias_held)
        bias_held[0:6, columns] = bias_heads[0:6]
        bias_held[6:bias_rows] = bias_middle[0 : bias_rows - 6]
        live = {}
        bias_bytes = bias_rows * width * 2

        def bias_send(key, index, device):
            bias_from[2 * index] = bias_held[...].astype(LOW)
            live[key] = copies.send(lambda: bias_from.at[2 * index], lambda: bias_from.at[2 * index + 1], device)
            return engine.transfer(key, bias_bytes)

        def bias_take(key, index):
            live[key].wait_recv()
            bias_held[...] = bias_from[2 * index].astype(F32) + bias_from[2 * index + 1].astype(F32)

        def bias_core():
            return bias_send("core", 0, place.other_core)

        def bias_y():
            bias_take("core", 0)
            return bias_send("y", 1, place.other_y)

        def bias_x():
            bias_take("y", 1)
            return bias_send("x", 2, place.other_x)

        def bias_z():
            bias_take("x", 2)
            bias_from[6] = bias_held[...].astype(LOW)
            live["z"] = [
                copies.send(lambda: bias_from.at[6], lambda k=k: bias_from.at[7 + k], device)
                for k, device in enumerate(place.ahead)
            ]
            return engine.transfer("z", bias_bytes)

        def bias_end():
            value = bias_from[6].astype(F32)
            for k, copy in enumerate(live["z"]):
                copy.wait_recv()
                value = value + bias_from[7 + k].astype(F32)
            bias_out[...] = value

        engine.add([bias_core, bias_y, bias_x, bias_z, bias_end])
        attn_product(2, dot(ent_turned, grad_query_words[all_words:]))
        attn_product(3, dot(ent_turned, grad_query_ents[all_words:]))
        attn_product(4, dot(hidden_turned[...], grad_keys[...]))
        attn_product(5, dot(hidden_turned[...], grad_values[...]))
        quarter = word_half // 2

        def words_sum():
            word_copy.wait_recv()
            sum_hidden(0, word_half, y * word_half)
            engine.clock += 0.5
            live_words["send"] = copies.send(
                lambda: total.at[span((1 - core) * quarter, quarter, LANES)], lambda: word_grad.at[core], place.other_core
            )
            live_words["own"] = copies.local(
                lambda: total.at[span(core * quarter, quarter, LANES)], lambda: word_grad.at[core]
            )
            return engine.transfer("core", quarter * width * 4)

        def words_end():
            live_words["send"].wait_recv()
            live_words["own"].wait()

        engine.add([lambda: word_ready, words_sum, words_end])

        def ent_products():
            proj_rows, pos_rows = rows.shape[1] // n_dp, all_words // n_dp
            proj_pad = padded(proj_rows)
            position = ent_pos[pl.ds(core, 1), :]
            picks = []
            for j in range(all_words // LANES):
                number = lax.broadcasted_iota(jnp.int32, (LANES, ents), 0) + j * LANES
                picks.append(jnp.where(number == position, 1.0, 0.0))
            pick = jnp.concatenate(picks, axis=0)
            here = lax.broadcasted_iota(jnp.int32, (all_words, ents), 1) // ent_half == y
            pick = jnp.where(here, pick, 0.0).astype(LOW)
            grad_ent = total[word_half:]
            grad_ent_low = grad_ent.astype(LOW)
            rest = (grad_ent - grad_ent_low.astype(F32)).astype(LOW)
            pos_grad = dot(pick, jnp.concatenate([grad_ent_low, grad_ent_low], axis=0)) + dot(
                pick, jnp.concatenate([rest, rest], axis=0)
            )
            proj_grad = dot_columns(rows[span(y * ent_half, ent_half, 64)], grad_ent_low)
            ent_grads[:, :, pl.ds(0, proj_rows)] = proj_grad.astype(LOW).reshape(nz, 2, proj_rows, width)
            ent_grads[:, :, pl.ds(proj_pad, pos_rows)] = pos_grad.astype(LOW).reshape(nz, 2, pos_rows, width)
            engine.clock += 1.0

        ent_job = jobs["ent"][0]
        engine.add([lambda: max(engine.clock, ent_ready + 1.0), ent_products, lambda: ent_job.begin()] + ent_job.rest)
        engine.drain()
        for copy in table_copies[-4:]:
            copy.wait()
        copies.finish()

    table_block = min(256, max(64, 524288 // (n_dp * 2 * ents)))
    pl.run_scoped(
        backward_phase,
        pltpu.VMEM((tokens, width), LOW),
        pltpu.VMEM((tokens, half), LOW),
        pltpu.VMEM((tokens, half), LOW),
        pltpu.VMEM((tokens, half), LOW),
        pltpu.VMEM((tokens, half), LOW),
        pltpu.VMEM((HEADS // 2, tokens, tokens), LOW),
        pltpu.VMEM((4, width, half), LOW),
        pltpu.VMEM((width, half), LOW),
        pltpu.VMEM((width, half), LOW),
        pltpu.VMEM((half, tokens), LOW),
        pltpu.VMEM((tokens, tokens), LOW),
        pltpu.VMEM((tokens, half), LOW),
        pltpu.VMEM((tokens, half), LOW),
        pltpu.VMEM((tokens, half), LOW),
        pltpu.VMEM((tokens, half), LOW),
        pltpu.VMEM((width, tokens), LOW),
        pltpu.VMEM((tokens, width), LOW),
        pltpu.VMEM((table_block, n_dp * 2 * ents), LOW),
        pltpu.VMEM((part_tokens, width), F32),
        pltpu.VMEM((nz, 2, 6 * row_pad, half), LOW),
        pltpu.VMEM((nz, 2, ent_sum.shape[0], width), LOW),
        pltpu.VMEM((2, table_block, ent_proj.shape[0]), F32),
        pltpu.VMEM((2, table_block, LANES), LOW),
    )
    last_copies = [
        copies.local(lambda: ffn_sum, lambda: ffn_reduced),
        copies.local(lambda: attn_sum, lambda: attn_reduced),
        copies.local(lambda: ent_sum, lambda: ent_reduced),
    ]
    for copy in out_copies:
        copy.wait_recv()
    for copy in last_copies:
        copy.wait()
    copies.finish()


def layer(
    nz, rows_dev, words, ent_hidden, mixed, out_weight, out_bias, gains, shifts, up_weight, up_bias, down_weight, down_bias, word_cots, ent_cots,
    hidden_low, query_words, query_ents, keys, values, probs, query_weight, key_weight, value_weight, rows, ent_pos, ent_proj, ids,
):
    n_dp = 2 * nz
    tokens, width = hidden_low.shape
    half = keys.shape[1]
    ents, edim = rows.shape
    all_words = tokens - ents
    part, ff = tokens // 2, up_weight.shape[1]
    ffn_blocks = ffn_plan(n_dp, width, ff)
    ffn_rows, attn_rows = ffn_blocks[-1][0] + ffn_blocks[-1][1], 6 * padded(width // n_dp)
    ent_pad = padded(edim // n_dp) + padded(all_words // n_dp)
    bias_rows = 12 + ff // width
    plan = [("ffn", base, size, order, width) for base, size, order in ffn_blocks]
    attn_size = attn_rows // 3
    plan += [("attn", base, attn_size, "xz", half) for base in range(0, attn_rows, attn_size)]
    plan.append(("ent", 0, ent_pad, "xzy", width))
    scratch = [
        pltpu.VMEM((part, half), LOW),
        pltpu.VMEM((tokens, half), LOW),
        pltpu.VMEM((part, width), F32),
        pltpu.VMEM((part, width), LOW),
        pltpu.VMEM((ffn_rows, width), LOW),
        pltpu.VMEM((2, attn_rows, half), LOW),
        pltpu.VMEM((ent_pad, width), LOW),
        pltpu.VMEM((bias_rows, width), F32),
        pltpu.VMEM((6 + nz, bias_rows, width), LOW),
        pltpu.VMEM((n_dp, 2, ents, edim), LOW),
        pltpu.VMEM((8, half), F32),
        pltpu.VMEM((16, width), F32),
    ]
    remote = 8 + 2 + 1 + 3 + nz + 1 + nz + nz + 2 + 4
    for name, base, size, order, columns in plan:
        job = Job(None, None, base, size, order, columns)
        scratch += job.scratch(nz, name != "ffn")
        remote += job.remote_count(nz)
    scratch += copy_semaphores(remote, 40 + 2 * (rows_dev // 64))
    return call(
        functools.partial(layer_kernel, nz, plan),
        [
            ((2, all_words // 4, width), LOW),
            ((2, ents // 4, width), LOW),
            ((2, all_words // 4, width), F32),
            ((ffn_rows, width), LOW),
            ((2, attn_rows, half), LOW),
            ((ent_pad, width), LOW),
            ((bias_rows, width), F32),
            ((rows_dev, edim), F32),
            ((rows_dev, LANES), LOW),
        ],
        [ANY] * 2 + [IN_VMEM, ANY] + [IN_VMEM] * 3 + [ANY, IN_VMEM, ANY, IN_VMEM] + [ANY] * 2 + [ANY] * 9 + [IN_VMEM] * 4,
        [ANY] * 6 + [IN_VMEM, ANY, ANY],
        scratch,
        "layer",
        2,
    )(words, ent_hidden, mixed, out_weight, out_bias, gains, shifts, up_weight, up_bias, down_weight, down_bias, word_cots, ent_cots,
      hidden_low, query_words, query_ents, keys, values, probs, query_weight, key_weight, value_weight, rows, ent_pos, ent_proj, ids)


def last_kernel(
    n_dp, table_grad, touched, first, second, ffn, attn, ent, bias, words_low, ents_low, words_grad,
    table_out, update, new_second, proj_grad, pos_grad, query_grad, key_grad, value_grad, out_grad, up_grad, down_grad, query_bias, gain_grad, shift_grad, key_bias, value_bias, out_bias, down_bias, up_bias,
    word_out, ent_out, word_grad,
):
    step = pl.program_id(0)
    grad = table_grad[...]
    hit = touched[:, 0:1].astype(F32) > 0.0
    mean_new = beta_one * first[...] + (1.0 - beta_one) * grad
    square_new = beta_two * second[...] + (1.0 - beta_two) * grad * grad
    direction = (
        mean_new
        / (1.0 - beta_one**adam_step)
        / (jnp.sqrt(square_new / (1.0 - beta_two**adam_step)) + adam_eps)
    )
    table_out[...] = grad
    update[...] = jnp.where(hit, direction, 0.0)
    new_second[...] = jnp.where(hit, square_new, second[...])
    width = ffn.shape[1]
    part, down_rows = out_grad.shape[0], down_grad.shape[0]
    pad = padded(part)
    proj_pad = padded(proj_grad.shape[0])
    parts = up_grad.shape[1] // width
    half = attn.shape[2]

    @pl.when(step == 0)
    def _():
        down_grad[...] = ffn[:down_rows].astype(F32)

    @pl.when(step == 1)
    def _():
        for j in range(parts):
            base = down_rows + j * pad
            up_grad[:, j * width : (j + 1) * width] = ffn[base : base + part].astype(F32)

    @pl.when(step == 2)
    def _():
        base = down_rows + parts * pad
        out_grad[...] = ffn[base : base + part].astype(F32)
        proj_grad[...] = ent[: proj_grad.shape[0]].astype(F32)
        pos_grad[...] = ent[proj_pad : proj_pad + pos_grad.shape[0]].astype(F32)
        for side in range(2):
            columns = slice(side * half, (side + 1) * half)
            key_grad[:, columns] = attn[side, 4 * pad : 4 * pad + part].astype(F32)
            value_grad[:, columns] = attn[side, 5 * pad : 5 * pad + part].astype(F32)

    @pl.when(step == 3)
    def _():
        for side in range(2):
            columns = slice(side * half, (side + 1) * half)
            for i in range(4):
                query_grad[i, :, columns] = attn[side, i * pad : i * pad + part].astype(F32)
        dp = lax.axis_index("dp")

        def own_columns(value, size, start):
            lane = lax.broadcasted_iota(jnp.int32, (value.shape[1], size), 0)
            want = lax.broadcasted_iota(jnp.int32, (value.shape[1], size), 1) + start
            pick = jnp.where(lane == want, 1.0, 0.0)
            return jnp.dot(value, pick, precision=lax.Precision.HIGHEST, preferred_element_type=F32)

        own = own_columns(bias[...], part, dp * part)
        query_bias[...] = own[0:4]
        gain_grad[...] = own[7:9]
        shift_grad[...] = own[9:11]
        for vector, i in ((key_bias, 4), (value_bias, 5), (out_bias, 6), (down_bias, 11 + parts)):
            vector[...] = own[i : i + 1].reshape(part)
        up = jnp.concatenate([bias[11 + j : 12 + j] for j in range(parts)], axis=1)
        size = up_bias.shape[0]
        if size % LANES == 0:
            per = width // size
            row = bias[pl.ds(11 + dp // per, 1), :]
            chosen = row[:, :size]
            for i in range(1, per):
                chosen = jnp.where(dp % per == i, row[:, i * size : (i + 1) * size], chosen)
            up_bias[...] = chosen.reshape(size)
        else:
            up_bias[...] = own_columns(up, size, dp * size).reshape(size)

    @pl.when(step == 4)
    def _():
        word_out[...] = words_low[...]
        ent_out[...] = ents_low[...]
        word_grad[...] = words_grad[...]


def last(n_dp, ff, all_words, table_grad, touched, first, second, ffn, attn, ent, bias, words_low, ents_low, words_grad):
    width = ffn.shape[1]
    rows, edim = first.shape
    part = width // n_dp
    block = 256
    blocked = lambda columns: pl.BlockSpec((block, columns), lambda i: (i, 0))
    whole = lambda shape: pl.BlockSpec(shape, lambda i: (0,) * len(shape))
    shapes = [
        (edim // n_dp, width),
        (all_words // n_dp, width),
        (4, part, width),
        (part, width),
        (part, width),
        (part, width),
        (part, ff),
        (ff // n_dp, width),
        (4, part),
        (2, part),
        (2, part),
        (part,),
        (part,),
        (part,),
        (part,),
        (ff // n_dp,),
    ]
    through = [words_low, ents_low, words_grad]
    return pl.pallas_call(
        functools.partial(last_kernel, n_dp),
        grid=(rows // block,),
        out_shape=[jax.ShapeDtypeStruct((rows, edim), F32)] * 3
        + [jax.ShapeDtypeStruct(shape, F32) for shape in shapes]
        + [jax.ShapeDtypeStruct(array.shape, array.dtype) for array in through],
        in_specs=[blocked(edim), blocked(LANES), blocked(edim), blocked(edim)]
        + [whole(array.shape) for array in (ffn, attn, ent, bias)]
        + [whole(array.shape) for array in through],
        out_specs=[blocked(edim)] * 3 + [whole(shape) for shape in shapes] + [whole(array.shape) for array in through],
        compiler_params=pltpu.CompilerParams(vmem_limit_bytes=VMEM_BYTES),
        name="last",
    )(table_grad, touched, first, second, ffn, attn, ent, bias, words_low, ents_low, words_grad)


def on_device(
    word_states,
    segments,
    entity_ids,
    entity_pos,
    ent_table,
    first_moment,
    second_moment,
    ent_proj,
    pos_table,
    query_weight,
    query_bias,
    key_weight,
    key_bias,
    value_weight,
    value_bias,
    out_weight,
    out_bias,
    norm_gain,
    norm_shift,
    up_weight,
    up_bias,
    down_weight,
    down_bias,
    word_cot,
    ent_cot,
):
    n_dp = lax.axis_size("dp")
    nz = n_dp // 2
    width, ff = up_weight.shape
    all_words = segments.shape[1]
    words, word_cots, ent_cots, all_ids, rows = fetch(nz, word_states, word_cot, ent_cot, entity_ids, ent_table)
    ent_hidden, hidden_low, query_words, query_ents, keys, values, probs, mixed = forward(
        words,
        rows,
        entity_pos,
        segments,
        ent_proj,
        pos_table,
        query_weight,
        query_bias,
        key_weight,
        key_bias,
        value_weight,
        value_bias,
    )
    ents = entity_ids.shape[1]
    word_out, ent_out, word_grad, ffn_sum, attn_sum, ent_sum, bias_sum, table_grad, touched = layer(
        nz, ent_table.shape[0], words, ent_hidden, mixed, out_weight, out_bias, norm_gain, norm_shift, up_weight, up_bias, down_weight, down_bias,
        word_cots, ent_cots, hidden_low, query_words, query_ents, keys, values, probs, query_weight, key_weight, value_weight,
        rows, entity_pos, ent_proj, all_ids.reshape(-1, ents),
    )
    (table_grad, table_update, new_second, proj_grad, pos_grad, query_grad, key_grad, value_grad, out_grad, up_grad, down_grad,
     query_bias_grad, gain_grad, shift_grad, key_bias_grad, value_bias_grad, out_bias_grad, down_bias_grad, up_bias_grad,
     word_out, ent_out, word_grad,
    ) = last(
        n_dp, ff, all_words, table_grad, touched, first_moment, second_moment, ffn_sum, attn_sum, ent_sum, bias_sum, word_out, ent_out, word_grad
    )
    return (
        word_out,
        ent_out,
        word_grad,
        proj_grad,
        pos_grad,
        query_grad,
        query_bias_grad,
        key_grad,
        key_bias_grad,
        value_grad,
        value_bias_grad,
        out_grad,
        out_bias_grad,
        gain_grad,
        shift_grad,
        up_grad,
        up_bias_grad,
        down_grad,
        down_bias_grad,
        table_grad,
        table_update,
        new_second,
    )


def solution(mesh):
    return jax.shard_map(
        on_device,
        mesh=mesh,
        in_specs=(
            P("dp", "seq", None),
            P("dp", None),
            P("dp", None),
            P("dp", None),
            P(("dp", "seq"), None),
            P(("dp", "seq"), None),
            P(("dp", "seq"), None),
            P(),
            P(),
            P(),
            P(),
            P(),
            P(),
            P(),
            P(),
            P(),
            P(),
            P(),
            P(),
            P(),
            P(),
            P(),
            P(),
            P("dp", "seq", None),
            P("dp", "seq", None),
        ),
        out_specs=(
            P("dp", "seq", None),
            P("dp", "seq", None),
            P("dp", "seq", None),
            P("dp", None),
            P("dp", None),
            P(None, "dp", None),
            P(None, "dp"),
            P("dp", None),
            P("dp"),
            P("dp", None),
            P("dp"),
            P("dp", None),
            P("dp"),
            P(None, "dp"),
            P(None, "dp"),
            P("dp", None),
            P("dp"),
            P("dp", None),
            P("dp"),
            P(("dp", "seq"), None),
            P(("dp", "seq"), None),
            P(("dp", "seq"), None),
        ),
        check_vma=False,
    )
```

```python
import functools
import math

import jax
import jax.numpy as jnp
from jax import lax
from jax.experimental import pallas as pl
from jax.experimental.pallas import tpu as pltpu
from jax.sharding import PartitionSpec as P

HEADS = 12
HEAD = 64
LANES = 128
MESH = pl.DeviceIdType.MESH
LOW = jnp.bfloat16
F32 = jnp.float32
VMEM_BYTES = 62 * 1024 * 1024

norm_eps = 1e-05
beta_one = 0.9
beta_two = 0.98
adam_eps = 1e-06
adam_step = 10.0
masked_score = -1e30


def dot(left, right):
    return jnp.dot(left, right, preferred_element_type=F32)


def dot_rows(left, right):
    return lax.dot_general(left, right, (((1,), (1,)), ((), ())), preferred_element_type=F32)


def dot_columns(left, right):
    return lax.dot_general(left, right, (((0,), (0,)), ((), ())), preferred_element_type=F32)


def span(start, size, unit):
    if isinstance(start, int):
        return pl.ds(start, size)
    return pl.ds(pl.multiple_of(start, unit), size)


def padded(rows):
    return -(-rows // 16) * 16


def loop(count, body, carry=0, unroll=1):
    def steps(i, carried):
        for k in range(unroll):
            carried = body(i * unroll + k, carried)
        return carried

    return lax.fori_loop(0, count // unroll, steps, carry)


class Place:
    def __init__(self, nz):
        self.dp, self.seq = lax.axis_index("dp"), lax.axis_index("seq")
        self.z, self.x = self.dp // 2, self.dp % 2
        self.y, self.core = self.seq // 2, self.seq % 2
        self.nz = nz
        self.other_core = (self.dp, self.y * 2 + 1 - self.core)
        self.other_y = (self.dp, (1 - self.y) * 2 + self.core)
        self.diagonal = (self.dp, (1 - self.y) * 2 + 1 - self.core)
        self.other_x = (self.z * 2 + 1 - self.x, self.seq)
        self.ahead = [(((self.z + k) % nz) * 2 + self.x, self.seq) for k in range(1, nz)]

    def z_ahead(self, k):
        return (self.z + k) % self.nz


def meet(partners):
    barrier = pltpu.get_barrier_semaphore()
    for partner in partners:
        pl.semaphore_signal(barrier, inc=1, device_id=partner, device_id_type=MESH)
    pl.semaphore_wait(barrier, len(partners))


class Remote:
    def __init__(self, copies, number, src, dst, device):
        self.copies, self.number, self.src, self.dst, self.device = copies, number, src, dst, device
        self.open = True

    def make(self, landing=False):
        return pltpu.make_async_remote_copy(
            src_ref=self.dst() if landing else self.src(),
            dst_ref=self.dst(),
            send_sem=self.copies.send_sem.at[self.number],
            recv_sem=self.copies.recv_sem.at[self.number],
            device_id=self.device,
            device_id_type=MESH,
        )

    def wait_recv(self):
        self.make(landing=True).wait_recv()

    def wait_send(self):
        if self.open:
            self.make().wait_send()
        self.open = False


class Local:
    def __init__(self, copies, number, src, dst):
        self.copies, self.number, self.src, self.dst = copies, number, src, dst

    def make(self):
        return pltpu.make_async_copy(self.src(), self.dst(), self.copies.local_sem.at[self.number])

    def wait(self):
        self.make().wait()


class Copies:
    def __init__(self, send_sem, recv_sem, local_sem):
        self.send_sem, self.recv_sem, self.local_sem = send_sem, recv_sem, local_sem
        self.local_count = 0
        self.sent = []

    def send(self, src, dst, device):
        copy = Remote(self, len(self.sent), src, dst, device)
        copy.make().start()
        self.sent.append(copy)
        return copy

    def local(self, src, dst):
        copy = Local(self, self.local_count, src, dst)
        self.local_count += 1
        copy.make().start()
        return copy

    def finish(self):
        for copy in self.sent:
            copy.wait_send()


def copy_semaphores(remote, local):
    return [
        pltpu.SemaphoreType.DMA((remote,)),
        pltpu.SemaphoreType.DMA((remote,)),
        pltpu.SemaphoreType.DMA((local,)),
    ]


ANY = pl.BlockSpec(memory_space=pl.ANY)
IN_VMEM = pl.BlockSpec(memory_space=pltpu.VMEM)


def call(kernel, outs, in_specs, out_specs, scratch, name, collective_id=None):
    params = {"vmem_limit_bytes": VMEM_BYTES}
    if collective_id is not None:
        params.update(collective_id=collective_id, has_side_effects=True)
    return pl.pallas_call(
        kernel,
        out_shape=[jax.ShapeDtypeStruct(shape, dtype) for shape, dtype in outs],
        in_specs=in_specs,
        out_specs=out_specs,
        scratch_shapes=scratch,
        compiler_params=pltpu.CompilerParams(**params),
        name=name,
    )


def fetch_kernel(nz, words, word_cot, ent_cot, ids, table, all_words, word_cots, ent_cots, all_ids, rows_out, *scratch):
    table_full, table_low, picked, answers, held, from_core, from_x, from_z, from_y, ids_here = scratch[:10]
    copies = Copies(*scratch[10:])
    place = Place(nz)
    z, x, y, core = place.z, place.x, place.y, place.core
    n_dp = 2 * nz
    word_here, ent_here = words.shape[1], ent_cot.shape[1]
    ents = ids.shape[1]
    dp_others = [((place.dp + k) % n_dp, place.seq) for k in range(1, n_dp)]
    meet([place.other_core, place.other_y, place.diagonal] + dp_others)
    whole_table = copies.local(lambda: table, lambda: table_full)
    ids_here[place.dp] = ids[...]
    id_copies = [copies.send(lambda: ids, lambda: ids_here.at[place.dp], device) for device in dp_others]
    quarter = span(place.seq * word_here, word_here, 128)
    word_copies = [
        copies.send(lambda: words.at[1 - core], lambda: all_words.at[quarter], place.diagonal),
        copies.send(lambda: words.at[core], lambda: all_words.at[quarter], place.other_y),
        copies.send(lambda: words.at[1 - core], lambda: all_words.at[quarter], place.other_core),
        copies.send(lambda: word_cot.at[1 - core], lambda: word_cots.at[span(core * word_here, word_here, 128)], place.other_core),
        copies.send(lambda: ent_cot.at[1 - core], lambda: ent_cots.at[span(core * ent_here, ent_here, 32)], place.other_core),
    ]
    all_words[quarter] = words[core]
    word_cots[span(core * word_here, word_here, 128)] = word_cot[core]
    ent_cots[span(core * ent_here, ent_here, 32)] = ent_cot[core]
    whole_table.wait()
    rows_dev = table.shape[0]

    def narrow(i, _):
        where = span(i * 128, 128, 128)
        table_low[where] = table_full[where].astype(LOW)
        return 0

    loop(rows_dev // 128, narrow)
    for copy in id_copies:
        copy.wait_recv()
    all_ids[...] = ids_here[...]
    base = (place.dp * 4 + place.seq) * rows_dev
    tiles = rows_dev // LANES

    def look_up(zz):
        def group(g, _):
            asked = ids_here[zz * 2 + g // 2, pl.ds(g % 2, 1), :] - base
            column = jnp.transpose(jnp.broadcast_to(asked, (ents, ents)))
            for j in range(tiles):
                number = lax.broadcasted_iota(jnp.int32, (ents, LANES), 1) + j * LANES
                hit = jnp.where(column == number, 1.0, 0.0).astype(LOW)
                picked[span(g * ents, ents, ents), pl.ds(j * LANES, LANES)] = hit
            return 0

        loop(4, group)
        answer = dot(picked[...], table_low[...]).astype(LOW)
        answers[zz] = answer.reshape(2, 2, ents, answer.shape[-1])

    order = [place.z_ahead(k + 1) for k in range(nz)]
    core_copies, x_copies, z_copies = [], [], []

    def core_send(zz):
        return copies.send(lambda: answers.at[zz, :, 1 - core], lambda: from_core.at[zz], place.other_core)

    def after_core(k):
        zz = order[k]
        core_copies[k].wait_recv()
        held[zz] = answers[zz, :, core] + from_core[zz]
        x_copies.append(copies.send(lambda: held.at[zz, 1 - x], lambda: from_x.at[zz], place.other_x))

    def after_x(k):
        zz = order[k]
        x_copies[k].wait_recv()
        held[zz, x] = held[zz, x] + from_x[zz]
        if k < nz - 1:
            z_copies.append(copies.send(lambda: held.at[zz, x], lambda: from_z.at[k], place.ahead[k]))

    for k in range(nz + 2):
        if k < nz:
            look_up(order[k])
            core_copies.append(core_send(order[k]))
        if 0 <= k - 1 < nz:
            after_core(k - 1)
        if 0 <= k - 2:
            after_x(k - 2)
    total = held[z, x]
    for k in range(nz - 1):
        z_copies[k].wait_recv()
        total = total + from_z[k]
    from_y[0] = total
    y_copy = copies.send(lambda: from_y.at[0], lambda: from_y.at[1], place.other_y)
    y_copy.wait_recv()
    rows_out[...] = from_y[0] + from_y[1]
    for copy in word_copies:
        copy.wait_recv()
    copies.finish()


def fetch(nz, words, word_cot, ent_cot, ids, table):
    _, word_here, width = words.shape
    ent_here, ents, (rows_dev, edim) = ent_cot.shape[1], ids.shape[1], table.shape
    n_dp = 2 * nz
    return call(
        functools.partial(fetch_kernel, nz),
        [
            ((4 * word_here, width), LOW),
            ((2 * word_here, width), LOW),
            ((2 * ent_here, width), LOW),
            ((n_dp, 2, ents), jnp.int32),
            ((ents, edim), LOW),
        ],
        [IN_VMEM] * 4 + [ANY],
        [IN_VMEM] * 5,
        [
            pltpu.VMEM((rows_dev, edim), F32),
            pltpu.VMEM((rows_dev, edim), LOW),
            pltpu.VMEM((4 * ents, rows_dev), LOW),
            pltpu.VMEM((nz, 2, 2, ents, edim), LOW),
            pltpu.VMEM((nz, 2, ents, edim), LOW),
            pltpu.VMEM((nz, 2, ents, edim), LOW),
            pltpu.VMEM((nz, ents, edim), LOW),
            pltpu.VMEM((nz - 1, ents, edim), LOW),
            pltpu.VMEM((2, ents, edim), LOW),
            pltpu.VMEM((n_dp, 2, ents), jnp.int32),
        ]
        + copy_semaphores(n_dp + 4 + 3 * nz + 2, 1),
        "fetch",
        1,
    )(words, word_cot, ent_cot, ids, table)


def lane_mask(rows, head):
    lane = lax.broadcasted_iota(jnp.int32, (rows, LANES), 1)
    return (lane >= head * HEAD) & (lane < (head + 1) * HEAD)


def row_of(vector):
    return vector[...].astype(F32).reshape(1, vector.shape[0])


def own_half(vector, y):
    row = row_of(vector)
    half = row.shape[1] // 2
    return jnp.where(y == 0, row[:, :half], row[:, half:])


def as_column(row):
    parts = [
        jnp.transpose(jnp.broadcast_to(row[:, i : i + LANES], (LANES, LANES)))
        for i in range(0, row.shape[1], LANES)
    ]
    return jnp.concatenate(parts, axis=0) if len(parts) > 1 else parts[0]


def forward_kernel(
    words, rows, ent_pos, segments, ent_proj, pos_table, query_weight, query_bias, key_weight, key_bias, value_weight, value_bias,
    ent_hidden, hidden_low, query_words, query_ents, keys, values, probs, mixed,
    query_here, key_here, value_here, values_turned, mask, mixed_turned, local_sem,
):
    y, core = lax.axis_index("seq") // 2, lax.axis_index("seq") % 2
    half = keys.shape[1]
    all_words, ents = words.shape[0], rows.shape[0]
    ent_pos, segments = ent_pos[pl.ds(core, 1), :], segments[pl.ds(core, 1), :]
    tokens = all_words + ents
    columns = span(y * half, half, LANES)
    weight_copies = [
        pltpu.make_async_copy(query_weight.at[:, :, columns], query_here, local_sem.at[0]),
        pltpu.make_async_copy(key_weight.at[:, columns], key_here, local_sem.at[1]),
        pltpu.make_async_copy(value_weight.at[:, columns], value_here, local_sem.at[2]),
    ]
    for copy in weight_copies:
        copy.start()
    position = as_column(ent_pos)
    picks = []
    for j in range(all_words // LANES):
        number = lax.broadcasted_iota(jnp.int32, (ents, LANES), 1) + j * LANES
        picks.append(jnp.where(position == number, 1.0, 0.0))
    pick = jnp.concatenate(picks, axis=1)
    word_seg = segments.astype(F32)
    ent_seg = jnp.sum(pick * word_seg, axis=1, keepdims=True)
    ent_hidden[...] = dot(rows[...], ent_proj[...]) + dot(pick.astype(LOW), pos_table[...])
    hidden_low[:all_words] = words[...]
    hidden_low[all_words:] = ent_hidden[...].astype(LOW)
    ent_row = jnp.transpose(jnp.broadcast_to(ent_seg, (ents, LANES)))[:1]
    seg_row = jnp.concatenate([word_seg, ent_row], axis=1)
    seg_column = jnp.concatenate([as_column(word_seg), jnp.broadcast_to(ent_seg, (ents, LANES))], axis=0)
    for j in range(tokens // LANES):
        here = slice(j * LANES, (j + 1) * LANES)
        mask[:, here] = jnp.where(seg_column == seg_row[:, here], 0.0, masked_score)

    query_b = query_bias[:, columns].astype(F32)
    for copy in weight_copies:
        copy.wait()
    word_low, ent_low = hidden_low[:all_words], hidden_low[all_words:]
    query_words[:all_words] = (dot(word_low, query_here[0]) + query_b[0:1]).astype(LOW)
    query_ents[:all_words] = (dot(word_low, query_here[1]) + query_b[1:2]).astype(LOW)
    query_words[all_words:] = (dot(ent_low, query_here[2]) + query_b[2:3]).astype(LOW)
    query_ents[all_words:] = (dot(ent_low, query_here[3]) + query_b[3:4]).astype(LOW)
    keys[...] = (dot(hidden_low[...], key_here[...]) + own_half(key_bias, y)).astype(LOW)
    value = dot(hidden_low[...], value_here[...]) + own_half(value_bias, y)
    values[...] = value.astype(LOW)
    values_turned[...] = jnp.transpose(value).astype(LOW)
    scale = 1.0 / math.sqrt(HEAD)
    tiles = tokens // LANES

    def pair_step(pair, _):
        lanes = span(pair * LANES, LANES, LANES)
        key, turned = keys[:, lanes], values_turned[lanes, :]
        row = lax.broadcasted_iota(jnp.int32, (LANES, tokens), 0)
        own_key, own_turned = [], []
        for head in range(2):
            own_key.append(jnp.where(lane_mask(tokens, head), key, jnp.zeros_like(key)))
            own_rows = (row >= head * HEAD) & (row < (head + 1) * HEAD)
            own_turned.append(jnp.where(own_rows, turned, jnp.zeros_like(turned)))
        for i in range(tiles):
            place = slice(i * LANES, (i + 1) * LANES)
            query_w, query_e = query_words[place, lanes], query_ents[place, lanes]
            total = None
            for head in range(2):
                raw = jnp.concatenate(
                    [dot_rows(own_key[head][:all_words], query_w), dot_rows(own_key[head][all_words:], query_e)], axis=0
                )
                score = raw * scale + mask[:, place]
                weight = jnp.exp(score - jnp.max(score, axis=0, keepdims=True))
                prob = (weight * (1.0 / jnp.sum(weight, axis=0, keepdims=True))).astype(LOW)
                probs[pair * 2 + head, :, place] = prob
                part = dot(own_turned[head], prob)
                total = part if total is None else total + part
            mixed[place, lanes] = jnp.transpose(total).astype(LOW)
        return 0

    loop(half // LANES, pair_step)


def forward(words, rows, ent_pos, segments, ent_proj, pos_table, query_weight, query_bias, key_weight, key_bias, value_weight, value_bias):
    all_words, width = words.shape
    ents = rows.shape[0]
    tokens, half = all_words + ents, width // 2
    return call(
        forward_kernel,
        [
            ((ents, width), F32),
            ((tokens, width), LOW),
            ((tokens, half), LOW),
            ((tokens, half), LOW),
            ((tokens, half), LOW),
            ((tokens, half), LOW),
            ((HEADS // 2, tokens, tokens), LOW),
            ((tokens, half), LOW),
        ],
        [IN_VMEM] * 6 + [ANY, IN_VMEM, ANY, IN_VMEM, ANY, IN_VMEM],
        [IN_VMEM] * 8,
        [
            pltpu.VMEM((4, width, half), LOW),
            pltpu.VMEM((width, half), LOW),
            pltpu.VMEM((width, half), LOW),
            pltpu.VMEM((half, tokens), LOW),
            pltpu.VMEM((tokens, tokens), F32),
            pltpu.VMEM((LANES, tokens), F32),
            pltpu.SemaphoreType.DMA((3,)),
        ],
        "forward",
    )(words, rows, ent_pos, segments, ent_proj, pos_table, query_weight, query_bias, key_weight, key_bias, value_weight, value_bias)


class Engine:
    RATES = {"core": 300e3, "x": 85e3, "y": 85e3, "z": 25e3}
    LATENCY = 2.0

    def __init__(self):
        self.clock, self.free, self.streams = 0.0, {}, []

    def transfer(self, link, size):
        start = max(self.clock, self.free.get(link, 0.0))
        self.free[link] = start + size / self.RATES[link]
        return self.free[link] + self.LATENCY

    def add(self, steps):
        self.streams.append([self.clock, list(steps)])
        self.poll()

    def run(self, stream):
        self.clock = max(self.clock, stream[0])
        ready = stream[1].pop(0)()
        stream[0] = self.clock if ready is None else ready

    def next(self):
        live = [stream for stream in self.streams if stream[1]]
        return min(live, key=lambda stream: stream[0]) if live else None

    def poll(self):
        while (stream := self.next()) is not None and stream[0] <= self.clock:
            self.run(stream)

    def work(self, time):
        self.clock += time
        self.poll()

    def drain(self):
        while (stream := self.next()) is not None:
            self.run(stream)


def blocks_of(rows):
    for size in (96, 64, 48, 32):
        if rows % size == 0:
            return size
    return 16


def add_blocks(engine, target, parts, leading, rows, columns):
    size = blocks_of(rows)
    count = rows // size

    def block(i, _):
        lead, row = i // count, (i % count) * size
        where = span(row, size, 16)
        if len(parts) == 2:
            value = parts[0](lead, where) + parts[1](lead, where)
        else:
            value = parts[0](lead, where).astype(F32)
            for part in parts[1:]:
                value = value + part(lead, where).astype(F32)
            value = value.astype(LOW)
        target(lead, where, value)
        return 0

    loop(leading * count, block)
    engine.clock += 0.3 + leading * rows * columns / 1e6


class Job:
    def __init__(self, grads, reduced, base, size, order, columns):
        self.grads, self.reduced, self.base, self.size, self.order, self.columns = grads, reduced, base, size, order, columns
        self.half = size // 2
        self.part = size // 4 if order == "yxz" else size // 2

    def scratch(self, nz, resident):
        shapes = [(nz, 2, self.half, self.columns)] * (1 if resident else 2)
        if self.order == "yxz":
            shapes.append((nz, 2, self.part, self.columns))
        elif self.order == "xzy":
            shapes.append((2, self.part, self.columns))
        shapes += [(nz, self.part, self.columns), (nz - 1, self.part, self.columns)]
        return [pltpu.VMEM(shape, LOW) for shape in shapes]

    def remote_count(self, nz):
        return 1 + (1 if self.order != "xz" else 0) + 1 + (nz - 1) + 1 + 1

    def prepare(self, engine, place, copies, scratch):
        nz, z, x, y, core = place.nz, place.z, place.x, place.y, place.core
        base, half, part, order, columns = self.base, self.half, self.part, self.order, self.columns
        if self.grads is not None:
            scratch = [self.grads.at[:, :, span(base + core * half, half, 16)]] + list(scratch)
        self.held, from_core = scratch[:2]
        held = self.held
        from_y = scratch[2] if order != "xz" else None
        from_x, from_z = scratch[-2:]
        live = {}
        row_bytes = 2 * columns
        theirs = span(base + (1 - core) * half, half, 16)
        mine = span(base + core * half, half, 16)
        own_rows = span(y * part, part, 16) if order == "yxz" else pl.ds(0, part)
        final_rows = span(base + core * half + (y * part if order == "yxz" else 0), part, 16)

        def start(source=None):
            if source is None:
                source = lambda: self.grads.at[:, :, theirs]
            self.sent = live["core"] = copies.send(source, lambda: from_core, place.other_core)
            return engine.transfer("core", 2 * nz * half * row_bytes)

        def send_x():
            live["x"] = copies.send(lambda: held.at[:, 1 - x, own_rows], lambda: from_x, place.other_x)
            return engine.transfer("x", nz * part * row_bytes)

        def after_core():
            live["core"].wait_recv()

            def put(i, where, value):
                held[i // 2, i % 2, where] = value

            add_blocks(
                engine,
                put,
                [lambda i, where: held[i // 2, i % 2, where], lambda i, where: from_core[i // 2, i % 2, where]],
                2 * nz,
                half,
                columns,
            )
            if order == "yxz":
                live["y"] = copies.send(
                    lambda: held.at[:, :, span((1 - y) * part, part, 16)], lambda: from_y, place.other_y
                )
                return engine.transfer("y", 2 * nz * part * row_bytes)
            return send_x()

        def shifted(where):
            return span(y * part + where.start, where.size, 16) if order == "yxz" else where

        def after_y():
            live["y"].wait_recv()

            def put(i, where, value):
                held[i // 2, i % 2, shifted(where)] = value

            add_blocks(
                engine,
                put,
                [lambda i, where: held[i // 2, i % 2, shifted(where)], lambda i, where: from_y[i // 2, i % 2, where]],
                2 * nz,
                part,
                columns,
            )
            return send_x()

        def send_z(k):
            return copies.send(
                lambda: held.at[place.z_ahead(k + 1), x, own_rows], lambda: from_z.at[k], place.ahead[k]
            )

        def after_x():
            live["x"].wait_recv()

            def put(i, where, value):
                held[i, x, shifted(where)] = value

            add_blocks(
                engine,
                put,
                [lambda i, where: held[i, x, shifted(where)], lambda i, where: from_x[i, where]],
                nz,
                part,
                columns,
            )
            live["z"] = [send_z(k) for k in range(nz - 1)]
            return engine.transfer("z", part * row_bytes)

        def after_z():
            for copy in live["z"]:
                copy.wait_recv()

            def put(i, where, value):
                if order == "yxz":
                    self.reduced[span(base + core * half + y * part + where.start, where.size, 16)] = value
                elif order == "xz":
                    self.reduced[y, span(base + core * half + where.start, where.size, 16)] = value
                else:
                    from_y[0, where] = value

            def parts(k):
                return lambda i, where: from_z[k, where]

            add_blocks(
                engine,
                put,
                [lambda i, where: held[z, x, shifted(where)]] + [parts(k) for k in range(nz - 1)],
                1,
                part,
                columns,
            )
            if order == "xzy":
                live["y2"] = copies.send(lambda: from_y.at[0], lambda: from_y.at[1], place.other_y)
            else:
                view = lambda: self.reduced.at[final_rows] if order == "yxz" else self.reduced.at[y, final_rows]
                live["y2"] = copies.send(view, view, place.other_y)
            return engine.transfer("y", part * row_bytes)

        def after_gather():
            live["y2"].wait_recv()
            if order == "xzy":

                def put(i, where, value):
                    self.reduced[span(base + core * half + where.start, where.size, 16)] = value

                add_blocks(
                    engine, put, [lambda i, where: from_y[0, where], lambda i, where: from_y[1, where]], 1, part, columns
                )
            view = lambda: self.reduced.at[:, mine] if order == "xz" else self.reduced.at[mine]
            live["core2"] = copies.send(view, view, place.other_core)
            return engine.transfer("core", 2 * half * row_bytes)

        def end():
            live["core2"].wait_recv()

        middle_steps = [after_core, after_y, after_x] if order == "yxz" else [after_core, after_x]
        self.begin, self.rest = start, middle_steps + [after_z, after_gather, end]

    def launch(self, engine, source=None):
        engine.add([lambda: self.begin(source)] + self.rest)


def lane_mean(value):
    return jnp.mean(value, axis=-1, keepdims=True)


def column_sum(value):
    return jnp.sum(value, axis=0, keepdims=True)


ROW_BLOCK = 32


def ffn_plan(n_dp, width, ff):
    down_rows, row_pad = ff // n_dp, padded(width // n_dp)
    size = 128 if down_rows % 128 == 0 else 32
    order = "yxz" if size % 64 == 0 else "xzy"
    plan = [(base, size, order) for base in range(0, down_rows, size)]
    base = down_rows
    for pair in range(ff // width // 2):
        order = "yxz" if pair % 2 == 0 and row_pad % 32 == 0 else "xzy"
        plan.append((base, 2 * row_pad, order))
        base += 2 * row_pad
    plan.append((base, row_pad, "xzy"))
    return plan


def layer_kernel(
    nz, plan, words, ent_hidden, mixed, out_weight, out_bias, gains, shifts, up_weight, up_bias, down_weight, down_bias, word_cots, ent_cots,
    hidden_low_in, query_words_in, query_ents_in, keys_in, values_in, probs_in, query_weight, key_weight, value_weight, rows, ent_pos, ent_proj, ids,
    word_out, ent_out, word_grad, ffn_reduced, attn_reduced, ent_reduced, bias_out, table_grad, touched, *scratch,
):
    (from_y_mixed, grad_mixed, grad_one, given, ffn_sum, attn_sum, ent_sum, bias_held, bias_from, all_rows, bias_heads, bias_middle) = scratch[:12]
    copies = Copies(*scratch[-3:])
    engine = Engine()
    place = Place(nz)
    z, x, y, core = place.z, place.x, place.y, place.core
    n_dp = 2 * nz
    tokens, half = mixed.shape
    width = 2 * half
    ents = ent_hidden.shape[0]
    all_words = tokens - ents
    word_half, ent_half = all_words // 2, ents // 2
    part_tokens = tokens // 2
    ff = up_weight.shape[1]
    parts = ff // width
    row_part, row_pad, down_rows = width // n_dp, padded(width // n_dp), ff // n_dp
    meet([place.other_core, place.other_y, place.other_x] + place.ahead)

    jobs = {"ffn": [], "attn": [], "ent": []}

    def make_jobs(names, sources):
        at = 12
        for name, base, size, order, columns in plan:
            job = Job(*sources.get(name, (None, None)), base, size, order, columns)
            used = len(job.scratch(nz, name != "ffn"))
            if name in names:
                job.prepare(engine, place, copies, scratch[at : at + used])
                jobs[name].append(job)
            at += used

    make_jobs(["ffn"], {"ffn": (None, ffn_sum)})

    def token_rows(side):
        return span(side * word_half, word_half, LANES), span(all_words + side * ent_half, ent_half, 64)

    mine, theirs = token_rows(y), token_rows(1 - y)
    own_columns, other_columns = span(y * half, half, LANES), span((1 - y) * half, half, LANES)
    word_part, ent_part = pl.ds(0, word_half), pl.ds(word_half, ent_half)
    mixed_copies = [
        copies.send(lambda: mixed.at[theirs[0]], lambda: from_y_mixed.at[word_part], place.other_y),
        copies.send(lambda: mixed.at[theirs[1]], lambda: from_y_mixed.at[ent_part], place.other_y),
    ]
    engine.transfer("y", part_tokens * half * 2)
    out_copies, mixed_back = [], []

    def forward_phase(
        out_here, up_here, down_here, word_here, ent_here, mixed_full, work, normed_low, normal_one, inverse_one,
        act, slope, output, cot, grad_two, grad_two_low, grad_up_low, grad_one_low, grad_mixed_here, normed_turned, staged,
    ):
        weight_copies = [
            copies.local(lambda: out_weight, lambda: out_here),
            copies.local(lambda: words.at[mine[0]], lambda: word_here),
            copies.local(lambda: ent_hidden.at[span(y * ent_half, ent_half, 64)], lambda: ent_here),
            copies.local(lambda: up_weight, lambda: up_here),
            copies.local(lambda: down_weight, lambda: down_here),
            copies.local(lambda: word_cots, lambda: cot.at[word_part]),
            copies.local(lambda: ent_cots, lambda: cot.at[ent_part]),
        ]
        gain, shift = gains[...].astype(F32), shifts[...].astype(F32)
        out_b, down_b, up_b = row_of(out_bias), row_of(down_bias), row_of(up_bias)
        mixed_full[word_part, own_columns] = mixed[mine[0]]
        mixed_full[ent_part, own_columns] = mixed[mine[1]]
        for copy in weight_copies[:3]:
            copy.wait()
        for copy in mixed_copies:
            copy.wait_recv()
        mixed_full[:, other_columns] = from_y_mixed[...]
        work[...] = dot(mixed_full[...], out_here[...])

        def norm_one(residual):
            def step(i, _):
                rows = span(residual[1] + i * ROW_BLOCK, ROW_BLOCK, ROW_BLOCK)
                value = residual[0][span(i * ROW_BLOCK, ROW_BLOCK, ROW_BLOCK)].astype(F32) + (work[rows] + out_b)
                center = value - lane_mean(value)
                inverse = lax.rsqrt(lane_mean(center * center) + norm_eps)
                normal = center * inverse
                result = normal * gain[0:1] + shift[0:1]
                normal_one[rows] = normal
                inverse_one[rows] = jnp.broadcast_to(inverse, (ROW_BLOCK, LANES))
                normed_low[rows] = result.astype(LOW)
                return 0

            return step

        loop(word_half // ROW_BLOCK, norm_one((word_here, 0)), 0, 2)
        loop(ent_half // ROW_BLOCK, norm_one((ent_here, word_half)), 0, 2)
        weight_copies[3].wait()
        for j in range(parts):
            columns = slice(j * width, (j + 1) * width)
            work[...] = dot(normed_low[...], up_here[:, columns]) + up_b[:, columns]

            def gelu(i, _):
                rows = span(i * ROW_BLOCK, ROW_BLOCK, ROW_BLOCK)
                value = work[rows]
                below = 0.5 * (1.0 + lax.erf(value * (1.0 / math.sqrt(2.0))))
                density = jnp.exp(-0.5 * value * value) * (1.0 / math.sqrt(2.0 * math.pi))
                act[rows, columns] = (value * below).astype(LOW)
                slope[rows, columns] = (below + value * density).astype(LOW)
                return 0

            loop(part_tokens // ROW_BLOCK, gelu)
        normed_turned[...] = jnp.transpose(normed_low[...].astype(F32)).astype(LOW)
        for copy in weight_copies[4:]:
            copy.wait()
        work[...] = dot(act[...], down_here[...])

        def norm_two(i, sums):
            rows = span(i * ROW_BLOCK, ROW_BLOCK, ROW_BLOCK)
            value = (normal_one[rows] * gain[0:1] + shift[0:1]) + (work[rows] + down_b)
            center = value - lane_mean(value)
            inverse = lax.rsqrt(lane_mean(center * center) + norm_eps)
            normal = center * inverse
            output[rows] = (normal * gain[1:2] + shift[1:2]).astype(LOW)
            cotangent = cot[rows].astype(F32)
            scaled = cotangent * gain[1:2]
            result = inverse * (scaled - lane_mean(scaled) - normal * lane_mean(scaled * normal))
            grad_two[rows] = result
            grad_two_low[rows] = result.astype(LOW)
            return (
                sums[0] + column_sum(cotangent * normal),
                sums[1] + column_sum(cotangent),
                sums[2] + column_sum(result),
            )

        nothing = jnp.zeros((1, width), F32)
        gain_two, shift_two, down_sum = loop(part_tokens // ROW_BLOCK, norm_two, (nothing, nothing, nothing), 2)
        quarter, ent_quarter = word_half // 2, ent_half // 2
        out_copies.extend([
            copies.send(
                lambda: output.at[span((1 - core) * quarter, quarter, LANES)], lambda: word_out.at[core], place.other_core
            ),
            copies.send(
                lambda: output.at[span(word_half + (1 - core) * ent_quarter, ent_quarter, 32)],
                lambda: ent_out.at[core],
                place.other_core,
            ),
        ])
        out_local = [
            copies.local(lambda: output.at[span(core * quarter, quarter, LANES)], lambda: word_out.at[core]),
            copies.local(
                lambda: output.at[span(word_half + core * ent_quarter, ent_quarter, 32)], lambda: ent_out.at[core]
            ),
        ]
        engine.clock = 0.0
        engine.free = {}
        sent, turn = [None, None], [0]

        def slot():
            number = turn[0] % 2
            turn[0] += 1
            if sent[number] is not None:
                sent[number].wait_send()
            return number

        def split(job, number, rows_in):
            job_half = job.half

            def keep(i, _):
                job.held[i // 2, i % 2] = staged[number, i // 2, i % 2, span(core * job_half, job_half, 16)]
                return 0

            loop(n_dp, keep)
            job.launch(
                engine, lambda: staged.at[number, :, :, span((1 - core) * job_half, job_half, 16)]
            )
            sent[number] = job.sent
            engine.work(0.3)

        def down_block(job):
            number = slot()
            if down_rows % 128:
                per = width // down_rows
                for j in range(parts):
                    value = dot_columns(act[:, j * width : (j + 1) * width], grad_two_low[...])
                    value = value.reshape(per, down_rows, width)[:, job.base : job.base + job.size].astype(LOW)
                    for d in range(per):
                        slab = j * per + d
                        staged[number, slab // 2, slab % 2, pl.ds(0, job.size)] = value[d]
            else:
                for slab in range(n_dp):
                    start = slab * down_rows + job.base
                    value = dot_columns(act[:, start : start + job.size], grad_two_low[...])
                    staged[number, slab // 2, slab % 2, pl.ds(0, job.size)] = value.astype(LOW)
            engine.work(1.3)
            split(job, number, job.size)

        def up_block(job, pair):
            own = grad_up_low[:, span((2 * pair + core) * width, width, LANES)]
            value = dot(normed_turned[...], own).astype(LOW).reshape(nz, 2, row_part, width)
            job.held[:, :, pl.ds(0, row_part)] = value
            number = slot()
            other = grad_up_low[:, span((2 * pair + 1 - core) * width, width, LANES)]
            value = dot(normed_turned[...], other).astype(LOW).reshape(nz, 2, row_part, width)
            staged[number, :, :, pl.ds(0, row_part)] = value
            engine.work(1.8)
            job.launch(engine, lambda: staged.at[number, :, :, pl.ds(0, row_pad)])
            sent[number] = job.sent

        up_sums = []

        def grad_up(j):
            columns = slice(j * width, (j + 1) * width)
            work[...] = dot_rows(grad_two_low[...], down_here[columns, :])

            def grad_gelu(i, total_row):
                rows = span(i * ROW_BLOCK, ROW_BLOCK, ROW_BLOCK)
                value = work[rows] * slope[rows, columns].astype(F32)
                grad_up_low[rows, columns] = value.astype(LOW)
                return total_row + column_sum(value)

            up_sums.append(loop(part_tokens // ROW_BLOCK, grad_gelu, nothing, 2))
            engine.work(1.6)

        downs = [job for job in jobs["ffn"] if job.base < down_rows]
        ups = [job for job in jobs["ffn"] if down_rows <= job.base][:-1]
        for job in downs:
            down_block(job)
        for j in range(parts):
            grad_up(j)
            if j % 2 == 1:
                up_block(ups[j // 2], j // 2)
        work[...] = dot_rows(grad_up_low[...], up_here[...])
        engine.work(2.0)

        def back_one(i, sums):
            rows = span(i * ROW_BLOCK, ROW_BLOCK, ROW_BLOCK)
            upper = grad_two[rows] + work[rows]
            normal = normal_one[rows]
            inverse = inverse_one[rows, 0:1]
            scaled = upper * gain[0:1]
            result = inverse * (scaled - lane_mean(scaled) - normal * lane_mean(scaled * normal))
            grad_one[rows] = result
            grad_one_low[rows] = result.astype(LOW)
            return (
                sums[0] + column_sum(upper * normal),
                sums[1] + column_sum(upper),
                sums[2] + column_sum(result),
            )

        gain_one, shift_one, out_sum = loop(part_tokens // ROW_BLOCK, back_one, (nothing, nothing, nothing), 2)
        engine.work(1.0)
        grad_mixed_here[...] = dot_rows(grad_one_low[...], out_here[other_columns, :]).astype(LOW)
        mixed_back.extend([
            copies.send(lambda: grad_mixed_here.at[word_part], lambda: grad_mixed.at[mine[0]], place.other_y),
            copies.send(lambda: grad_mixed_here.at[ent_part], lambda: grad_mixed.at[mine[1]], place.other_y),
        ])
        engine.transfer("y", part_tokens * half * 2)
        own = dot_rows(grad_one_low[...], out_here[own_columns, :]).astype(LOW)
        grad_mixed[mine[0]] = own[:word_half]
        grad_mixed[mine[1]] = own[word_half:]
        engine.work(1.0)
        number = slot()
        value = dot_columns(mixed_full[...], grad_one_low[...]).astype(LOW)
        staged[number, :, :, pl.ds(0, row_part)] = value.reshape(nz, 2, row_part, width)
        engine.work(0.8)
        split(jobs["ffn"][-1], number, row_pad)
        bias_rows = [out_sum, gain_one, gain_two, shift_one, shift_two] + up_sums + [down_sum]
        for i, row in enumerate(bias_rows):
            bias_middle[i : i + 1] = row
        for copy in sent:
            copy.wait_send()
        for copy in mixed_back + out_copies:
            copy.wait_send()
        for copy in out_local:
            copy.wait()

    tall = lambda columns, dtype: pltpu.VMEM((part_tokens, columns), dtype)
    stage_rows = max([job.size for job in jobs["ffn"] if job.base < down_rows] + [row_pad])
    pl.run_scoped(
        forward_phase,
        pltpu.VMEM((width, width), LOW),
        pltpu.VMEM((width, ff), LOW),
        pltpu.VMEM((ff, width), LOW),
        pltpu.VMEM((word_half, width), LOW),
        pltpu.VMEM((ent_half, width), F32),
        tall(width, LOW),
        tall(width, F32),
        tall(width, LOW),
        tall(width, F32),
        tall(LANES, F32),
        tall(ff, LOW),
        tall(ff, LOW),
        tall(width, LOW),
        tall(width, LOW),
        tall(width, F32),
        tall(width, LOW),
        tall(ff, LOW),
        tall(width, LOW),
        tall(half, LOW),
        pltpu.VMEM((width, part_tokens), LOW),
        pltpu.VMEM((2, nz, 2, stage_rows, width), LOW),
    )
    live_words = {}

    def backward_phase(
        hidden_low, query_words, query_ents, keys, values, probs, query_here, key_here, value_here, keys_turned, grad_score_pair,
        grad_query_words, grad_query_ents, grad_keys, grad_values, hidden_turned, grad_hidden, hits, total, attn_grads, ent_grads, table_here, touched_here,
    ):
        make_jobs(["attn", "ent"], {"attn": (attn_grads, attn_sum), "ent": (ent_grads, ent_sum)})
        columns = span(y * half, half, LANES)
        copies_in = [
            copies.local(lambda: values_in, lambda: values),
            copies.local(lambda: keys_in, lambda: keys),
            copies.local(lambda: query_words_in, lambda: query_words),
            copies.local(lambda: query_ents_in, lambda: query_ents),
        ]
        prob_copies = []
        for head in range(probs.shape[0]):
            prob_copies.append(
                copies.local(lambda head=head: probs_in.at[head], lambda head=head: probs.at[head])
            )
        hidden_copy = copies.local(lambda: hidden_low_in, lambda: hidden_low)
        weight_copies = [
            copies.local(lambda: query_weight.at[:, :, columns], lambda: query_here),
            copies.local(lambda: key_weight.at[:, columns], lambda: key_here),
            copies.local(lambda: value_weight.at[:, columns], lambda: value_here),
        ]
        for copy in copies_in:
            copy.wait()
        for i in range(half // LANES):
            lanes = slice(i * LANES, (i + 1) * LANES)
            keys_turned[lanes, :] = jnp.transpose(keys[:, lanes].astype(F32)).astype(LOW)
        hidden_copy.wait()
        for i in range(width // LANES):
            lanes = slice(i * LANES, (i + 1) * LANES)
            hidden_turned[lanes, :] = jnp.transpose(hidden_low[:, lanes].astype(F32)).astype(LOW)
        for copy in mixed_back:
            copy.wait_recv()
        engine.work(2.0)
        scale = 1.0 / math.sqrt(HEAD)
        tiles = tokens // LANES

        for pair in range(half // LANES):
            lanes = slice(pair * LANES, (pair + 1) * LANES)
            grad_query_w = jnp.zeros((LANES, tokens), F32)
            grad_query_e = jnp.zeros((LANES, tokens), F32)
            grad_key_w = jnp.zeros((all_words, LANES), F32)
            grad_key_e = jnp.zeros((ents, LANES), F32)
            grad_value = jnp.zeros((tokens, LANES), F32)
            for head in range(2):
                own = lane_mask(tokens, head)
                value = values[:, lanes]
                own_value = jnp.where(own, value, jnp.zeros_like(value))
                prob_copies[pair * 2 + head].wait()

                grad_scores = grad_score_pair.at[head]
                for i in range(tiles):
                    where = slice(i * LANES, (i + 1) * LANES)
                    grad_prob = dot_rows(own_value, grad_mixed[where, lanes])
                    prob = probs[pair * 2 + head, :, where].astype(F32)
                    both = prob * grad_prob
                    grad_scores[:, where] = (both - prob * jnp.sum(both, axis=0, keepdims=True)).astype(LOW)
                engine.work(1.7)
                given_heads = grad_mixed[:, lanes]
                grad_value += dot(probs[pair * 2 + head], jnp.where(own, given_heads, jnp.zeros_like(given_heads)))
                query_w, query_e = query_words[:, lanes], query_ents[:, lanes]
                grad_key_w += dot(grad_scores[:all_words], jnp.where(own, query_w, jnp.zeros_like(query_w)))
                grad_key_e += dot(grad_scores[all_words:], jnp.where(own, query_e, jnp.zeros_like(query_e)))
                row = lax.broadcasted_iota(jnp.int32, (LANES, tokens), 0)
                own_rows = (row >= head * HEAD) & (row < (head + 1) * HEAD)
                turned = keys_turned[lanes, :]
                turned = jnp.where(own_rows, turned, jnp.zeros_like(turned))
                grad_query_w += dot(turned[:, :all_words], grad_scores[:all_words])
                grad_query_e += dot(turned[:, all_words:], grad_scores[all_words:])
                engine.work(1.7)
            grad_query_w = jnp.transpose(grad_query_w) * scale
            grad_query_e = jnp.transpose(grad_query_e) * scale
            grad_key_w, grad_key_e = grad_key_w * scale, grad_key_e * scale
            sums = [
                column_sum(grad_query_w[:all_words]),
                column_sum(grad_query_e[:all_words]),
                column_sum(grad_query_w[all_words:]),
                column_sum(grad_query_e[all_words:]),
                column_sum(grad_key_w) + column_sum(grad_key_e),
                column_sum(grad_value),
            ]
            for i, sum_row in enumerate(sums):
                bias_heads[i : i + 1, lanes] = sum_row
            grad_query_words[:, lanes] = grad_query_w.astype(LOW)
            grad_query_ents[:, lanes] = grad_query_e.astype(LOW)
            grad_keys[:all_words, lanes] = grad_key_w.astype(LOW)
            grad_keys[all_words:, lanes] = grad_key_e.astype(LOW)
            grad_values[:, lanes] = grad_value.astype(LOW)
            engine.work(0.5)

        for copy in weight_copies:
            copy.wait()
        ent_rows, word_rows = slice(all_words, tokens), slice(0, all_words)

        def hidden_part(here, first, second):
            grad_hidden[here] = (
                dot_rows(grad_keys[here], key_here[...])
                + dot_rows(grad_values[here], value_here[...])
                + dot_rows(grad_query_words[here], query_here[first])
                + dot_rows(grad_query_ents[here], query_here[second])
            ).astype(LOW)

        hidden_part(ent_rows, 2, 3)
        ent_copy = copies.send(lambda: grad_hidden.at[theirs[1]], lambda: given.at[ent_part], place.other_y)
        ent_ready = engine.transfer("y", ent_half * width * 2)
        engine.work(0.7)
        word_turned, ent_turned = hidden_turned[:, :all_words], hidden_turned[:, all_words:]
        attn_jobs = jobs["attn"]

        def attn_product(i, value):
            attn_grads[:, :, pl.ds(i * row_pad, row_part)] = value.astype(LOW).reshape(nz, 2, row_part, half)
            per = 6 // len(attn_jobs)
            if i % per == per - 1:
                attn_jobs[i // per].launch(engine)
            engine.work(0.6)

        attn_product(0, dot(word_turned, grad_query_words[:all_words]))
        attn_product(1, dot(word_turned, grad_query_ents[:all_words]))

        live_rows = {}

        def sum_hidden(start, count, own_start):
            def block(i, _):
                where = span(start + i * 32, 32, 32)
                own = span(own_start + i * 32, 32, 32)
                total[where] = grad_one[where] + (grad_hidden[own].astype(F32) + given[where].astype(F32))
                return 0

            loop(count // 32, block)

        row_bytes = ent_half * ent_proj.shape[0] * 2

        def rows_y():
            ent_copy.wait_recv()
            sum_hidden(word_half, ent_half, all_words + y * ent_half)
            row_grad = dot_rows(total[word_half:].astype(LOW), ent_proj[...]).astype(LOW)
            all_rows[place.dp, core, span(y * ent_half, ent_half, 64)] = row_grad
            view = lambda: all_rows.at[place.dp, core, span(y * ent_half, ent_half, 64)]
            live_rows["y"] = copies.send(view, view, place.other_y)
            return engine.transfer("y", row_bytes)

        def rows_z():
            live_rows["y"].wait_recv()
            view = lambda: all_rows.at[place.dp, core]
            live_rows["z"] = [copies.send(view, view, device) for device in place.ahead]
            return engine.transfer("z", 2 * row_bytes)

        def rows_x():
            for copy in live_rows["z"]:
                copy.wait_recv()
            live_rows["x"] = []
            for k in range(nz):
                view = lambda k=k: all_rows.at[place.z_ahead(k) * 2 + x, core]
                live_rows["x"].append(copies.send(view, view, place.other_x))
            return engine.transfer("x", nz * 2 * row_bytes)

        def rows_core():
            for copy in live_rows["x"]:
                copy.wait_recv()
            view = lambda: all_rows.at[:, core]
            live_rows["core"] = copies.send(view, view, place.other_core)
            return engine.transfer("core", n_dp * 2 * row_bytes)

        rows_dev = table_grad.shape[0]
        table_copies = []
        base_row = (place.dp * 4 + place.seq) * rows_dev

        def table_part(i):
            def step():
                if i == 0:
                    live_rows["core"].wait_recv()
                groups = ids.shape[0]
                number = lax.broadcasted_iota(jnp.int32, (table_block, ents), 0) + (base_row + i * table_block)
                count = jnp.zeros((table_block, ents), F32)
                for group in range(groups):
                    hit = jnp.where(ids[group : group + 1, :] == number, 1.0, 0.0)
                    count = count + hit
                    hits[:, group * ents : (group + 1) * ents] = hit.astype(LOW)
                here = pl.ds(i * table_block, table_block)
                for copy in table_copies[2 * i - 4 : 2 * i - 2] if i >= 2 else []:
                    copy.wait()
                dps = min(n_dp, 8)
                grad = None
                for first in range(0, n_dp, dps):
                    given_rows = all_rows[first : first + dps].reshape(dps * 2 * ents, ent_proj.shape[0])
                    value = dot(hits[:, first * 2 * ents : (first + dps) * 2 * ents], given_rows)
                    grad = value if grad is None else grad + value
                table_here[i % 2] = grad
                named = jnp.sum(count, axis=1, keepdims=True)
                touched_here[i % 2] = jnp.broadcast_to(named, (table_block, LANES)).astype(LOW)
                table_copies.append(copies.local(lambda: table_here.at[i % 2], lambda: table_grad.at[here]))
                table_copies.append(copies.local(lambda: touched_here.at[i % 2], lambda: touched.at[here]))
                engine.clock += 1.2

            return step

        engine.add(
            [lambda: ent_ready, rows_y, rows_z, rows_x, rows_core] + [table_part(i) for i in range(rows_dev // table_block)]
        )
        hidden_part(word_rows, 0, 1)
        word_copy = copies.send(lambda: grad_hidden.at[theirs[0]], lambda: given.at[word_part], place.other_y)
        word_ready = engine.transfer("y", word_half * width * 2)
        engine.work(1.5)

        bias_rows = bias_held.shape[0]
        bias_held[...] = jnp.zeros_like(bias_held)
        bias_held[0:6, columns] = bias_heads[0:6]
        bias_held[6:bias_rows] = bias_middle[0 : bias_rows - 6]
        live = {}
        bias_bytes = bias_rows * width * 2

        def bias_send(key, index, device):
            bias_from[2 * index] = bias_held[...].astype(LOW)
            live[key] = copies.send(lambda: bias_from.at[2 * index], lambda: bias_from.at[2 * index + 1], device)
            return engine.transfer(key, bias_bytes)

        def bias_take(key, index):
            live[key].wait_recv()
            bias_held[...] = bias_from[2 * index].astype(F32) + bias_from[2 * index + 1].astype(F32)

        def bias_core():
            return bias_send("core", 0, place.other_core)

        def bias_y():
            bias_take("core", 0)
            return bias_send("y", 1, place.other_y)

        def bias_x():
            bias_take("y", 1)
            return bias_send("x", 2, place.other_x)

        def bias_z():
            bias_take("x", 2)
            bias_from[6] = bias_held[...].astype(LOW)
            live["z"] = [
                copies.send(lambda: bias_from.at[6], lambda k=k: bias_from.at[7 + k], device)
                for k, device in enumerate(place.ahead)
            ]
            return engine.transfer("z", bias_bytes)

        def bias_end():
            value = bias_from[6].astype(F32)
            for k, copy in enumerate(live["z"]):
                copy.wait_recv()
                value = value + bias_from[7 + k].astype(F32)
            bias_out[...] = value

        engine.add([bias_core, bias_y, bias_x, bias_z, bias_end])
        attn_product(2, dot(ent_turned, grad_query_words[all_words:]))
        attn_product(3, dot(ent_turned, grad_query_ents[all_words:]))
        attn_product(4, dot(hidden_turned[...], grad_keys[...]))
        attn_product(5, dot(hidden_turned[...], grad_values[...]))
        quarter = word_half // 2

        def words_sum():
            word_copy.wait_recv()
            sum_hidden(0, word_half, y * word_half)
            engine.clock += 0.5
            live_words["send"] = copies.send(
                lambda: total.at[span((1 - core) * quarter, quarter, LANES)], lambda: word_grad.at[core], place.other_core
            )
            live_words["own"] = copies.local(
                lambda: total.at[span(core * quarter, quarter, LANES)], lambda: word_grad.at[core]
            )
            return engine.transfer("core", quarter * width * 4)

        def words_end():
            live_words["send"].wait_recv()
            live_words["own"].wait()

        engine.add([lambda: word_ready, words_sum, words_end])

        def ent_products():
            proj_rows, pos_rows = rows.shape[1] // n_dp, all_words // n_dp
            proj_pad = padded(proj_rows)
            position = ent_pos[pl.ds(core, 1), :]
            picks = []
            for j in range(all_words // LANES):
                number = lax.broadcasted_iota(jnp.int32, (LANES, ents), 0) + j * LANES
                picks.append(jnp.where(number == position, 1.0, 0.0))
            pick = jnp.concatenate(picks, axis=0)
            here = lax.broadcasted_iota(jnp.int32, (all_words, ents), 1) // ent_half == y
            pick = jnp.where(here, pick, 0.0).astype(LOW)
            grad_ent = total[word_half:]
            grad_ent_low = grad_ent.astype(LOW)
            rest = (grad_ent - grad_ent_low.astype(F32)).astype(LOW)
            pos_grad = dot(pick, jnp.concatenate([grad_ent_low, grad_ent_low], axis=0)) + dot(
                pick, jnp.concatenate([rest, rest], axis=0)
            )
            proj_grad = dot_columns(rows[span(y * ent_half, ent_half, 64)], grad_ent_low)
            ent_grads[:, :, pl.ds(0, proj_rows)] = proj_grad.astype(LOW).reshape(nz, 2, proj_rows, width)
            ent_grads[:, :, pl.ds(proj_pad, pos_rows)] = pos_grad.astype(LOW).reshape(nz, 2, pos_rows, width)
            engine.clock += 1.0

        ent_job = jobs["ent"][0]
        engine.add([lambda: max(engine.clock, ent_ready + 1.0), ent_products, lambda: ent_job.begin()] + ent_job.rest)
        engine.drain()
        for copy in table_copies[-4:]:
            copy.wait()
        copies.finish()

    table_block = min(256, max(64, 524288 // (n_dp * 2 * ents)))
    pl.run_scoped(
        backward_phase,
        pltpu.VMEM((tokens, width), LOW),
        pltpu.VMEM((tokens, half), LOW),
        pltpu.VMEM((tokens, half), LOW),
        pltpu.VMEM((tokens, half), LOW),
        pltpu.VMEM((tokens, half), LOW),
        pltpu.VMEM((HEADS // 2, tokens, tokens), LOW),
        pltpu.VMEM((4, width, half), LOW),
        pltpu.VMEM((width, half), LOW),
        pltpu.VMEM((width, half), LOW),
        pltpu.VMEM((half, tokens), LOW),
        pltpu.VMEM((2, tokens, tokens), LOW),
        pltpu.VMEM((tokens, half), LOW),
        pltpu.VMEM((tokens, half), LOW),
        pltpu.VMEM((tokens, half), LOW),
        pltpu.VMEM((tokens, half), LOW),
        pltpu.VMEM((width, tokens), LOW),
        pltpu.VMEM((tokens, width), LOW),
        pltpu.VMEM((table_block, n_dp * 2 * ents), LOW),
        pltpu.VMEM((part_tokens, width), F32),
        pltpu.VMEM((nz, 2, 6 * row_pad, half), LOW),
        pltpu.VMEM((nz, 2, ent_sum.shape[0], width), LOW),
        pltpu.VMEM((2, table_block, ent_proj.shape[0]), F32),
        pltpu.VMEM((2, table_block, LANES), LOW),
    )
    last_copies = [
        copies.local(lambda: ffn_sum, lambda: ffn_reduced),
        copies.local(lambda: attn_sum, lambda: attn_reduced),
        copies.local(lambda: ent_sum, lambda: ent_reduced),
    ]
    for copy in out_copies:
        copy.wait_recv()
    for copy in last_copies:
        copy.wait()
    copies.finish()


def layer(
    nz, rows_dev, words, ent_hidden, mixed, out_weight, out_bias, gains, shifts, up_weight, up_bias, down_weight, down_bias, word_cots, ent_cots,
    hidden_low, query_words, query_ents, keys, values, probs, query_weight, key_weight, value_weight, rows, ent_pos, ent_proj, ids,
):
    n_dp = 2 * nz
    tokens, width = hidden_low.shape
    half = keys.shape[1]
    ents, edim = rows.shape
    all_words = tokens - ents
    part, ff = tokens // 2, up_weight.shape[1]
    ffn_blocks = ffn_plan(n_dp, width, ff)
    ffn_rows, attn_rows = ffn_blocks[-1][0] + ffn_blocks[-1][1], 6 * padded(width // n_dp)
    ent_pad = padded(edim // n_dp) + padded(all_words // n_dp)
    bias_rows = 12 + ff // width
    plan = [("ffn", base, size, order, width) for base, size, order in ffn_blocks]
    attn_size = attn_rows // 3
    plan += [("attn", base, attn_size, "xz", half) for base in range(0, attn_rows, attn_size)]
    plan.append(("ent", 0, ent_pad, "xzy", width))
    scratch = [
        pltpu.VMEM((part, half), LOW),
        pltpu.VMEM((tokens, half), LOW),
        pltpu.VMEM((part, width), F32),
        pltpu.VMEM((part, width), LOW),
        pltpu.VMEM((ffn_rows, width), LOW),
        pltpu.VMEM((2, attn_rows, half), LOW),
        pltpu.VMEM((ent_pad, width), LOW),
        pltpu.VMEM((bias_rows, width), F32),
        pltpu.VMEM((6 + nz, bias_rows, width), LOW),
        pltpu.VMEM((n_dp, 2, ents, edim), LOW),
        pltpu.VMEM((8, half), F32),
        pltpu.VMEM((16, width), F32),
    ]
    remote = 8 + 2 + 1 + 3 + nz + 1 + nz + nz + 2 + 4
    for name, base, size, order, columns in plan:
        job = Job(None, None, base, size, order, columns)
        scratch += job.scratch(nz, name != "ffn")
        remote += job.remote_count(nz)
    scratch += copy_semaphores(remote, 40 + 2 * (rows_dev // 64))
    return call(
        functools.partial(layer_kernel, nz, plan),
        [
            ((2, all_words // 4, width), LOW),
            ((2, ents // 4, width), LOW),
            ((2, all_words // 4, width), F32),
            ((ffn_rows, width), LOW),
            ((2, attn_rows, half), LOW),
            ((ent_pad, width), LOW),
            ((bias_rows, width), F32),
            ((rows_dev, edim), F32),
            ((rows_dev, LANES), LOW),
        ],
        [ANY] * 2 + [IN_VMEM, ANY] + [IN_VMEM] * 3 + [ANY, IN_VMEM, ANY, IN_VMEM] + [ANY] * 2 + [ANY] * 9 + [IN_VMEM] * 4,
        [ANY] * 6 + [IN_VMEM, ANY, ANY],
        scratch,
        "layer",
        2,
    )(words, ent_hidden, mixed, out_weight, out_bias, gains, shifts, up_weight, up_bias, down_weight, down_bias, word_cots, ent_cots,
      hidden_low, query_words, query_ents, keys, values, probs, query_weight, key_weight, value_weight, rows, ent_pos, ent_proj, ids)


def last_kernel(
    n_dp, table_grad, touched, first, second, ffn, attn, ent, bias, words_low, ents_low, words_grad,
    table_out, update, new_second, proj_grad, pos_grad, query_grad, key_grad, value_grad, out_grad, up_grad, down_grad, query_bias, gain_grad, shift_grad, key_bias, value_bias, out_bias, down_bias, up_bias,
    word_out, ent_out, word_grad,
):
    step = pl.program_id(0)
    grad = table_grad[...]
    hit = touched[:, 0:1].astype(F32) > 0.0
    mean_new = beta_one * first[...] + (1.0 - beta_one) * grad
    square_new = beta_two * second[...] + (1.0 - beta_two) * grad * grad
    direction = (
        mean_new
        / (1.0 - beta_one**adam_step)
        / (jnp.sqrt(square_new / (1.0 - beta_two**adam_step)) + adam_eps)
    )
    table_out[...] = grad
    update[...] = jnp.where(hit, direction, 0.0)
    new_second[...] = jnp.where(hit, square_new, second[...])
    width = ffn.shape[1]
    part, down_rows = out_grad.shape[0], down_grad.shape[0]
    pad = padded(part)
    proj_pad = padded(proj_grad.shape[0])
    parts = up_grad.shape[1] // width
    half = attn.shape[2]

    @pl.when(step == 0)
    def _():
        down_grad[...] = ffn[:down_rows].astype(F32)

    @pl.when(step == 1)
    def _():
        for j in range(parts):
            base = down_rows + j * pad
            up_grad[:, j * width : (j + 1) * width] = ffn[base : base + part].astype(F32)

    @pl.when(step == 2)
    def _():
        base = down_rows + parts * pad
        out_grad[...] = ffn[base : base + part].astype(F32)
        proj_grad[...] = ent[: proj_grad.shape[0]].astype(F32)
        pos_grad[...] = ent[proj_pad : proj_pad + pos_grad.shape[0]].astype(F32)
        for side in range(2):
            columns = slice(side * half, (side + 1) * half)
            key_grad[:, columns] = attn[side, 4 * pad : 4 * pad + part].astype(F32)
            value_grad[:, columns] = attn[side, 5 * pad : 5 * pad + part].astype(F32)

    @pl.when(step == 3)
    def _():
        for side in range(2):
            columns = slice(side * half, (side + 1) * half)
            for i in range(4):
                query_grad[i, :, columns] = attn[side, i * pad : i * pad + part].astype(F32)
        dp = lax.axis_index("dp")

        def own_columns(value, size, start):
            lane = lax.broadcasted_iota(jnp.int32, (value.shape[1], size), 0)
            want = lax.broadcasted_iota(jnp.int32, (value.shape[1], size), 1) + start
            pick = jnp.where(lane == want, 1.0, 0.0)
            return jnp.dot(value, pick, precision=lax.Precision.HIGHEST, preferred_element_type=F32)

        own = own_columns(bias[...], part, dp * part)
        query_bias[...] = own[0:4]
        gain_grad[...] = own[7:9]
        shift_grad[...] = own[9:11]
        for vector, i in ((key_bias, 4), (value_bias, 5), (out_bias, 6), (down_bias, 11 + parts)):
            vector[...] = own[i : i + 1].reshape(part)
        up = jnp.concatenate([bias[11 + j : 12 + j] for j in range(parts)], axis=1)
        size = up_bias.shape[0]
        if size % LANES == 0:
            per = width // size
            row = bias[pl.ds(11 + dp // per, 1), :]
            chosen = row[:, :size]
            for i in range(1, per):
                chosen = jnp.where(dp % per == i, row[:, i * size : (i + 1) * size], chosen)
            up_bias[...] = chosen.reshape(size)
        else:
            up_bias[...] = own_columns(up, size, dp * size).reshape(size)

    @pl.when(step == 4)
    def _():
        word_out[...] = words_low[...]
        ent_out[...] = ents_low[...]
        word_grad[...] = words_grad[...]


def last(n_dp, ff, all_words, table_grad, touched, first, second, ffn, attn, ent, bias, words_low, ents_low, words_grad):
    width = ffn.shape[1]
    rows, edim = first.shape
    part = width // n_dp
    block = 256
    blocked = lambda columns: pl.BlockSpec((block, columns), lambda i: (i, 0))
    whole = lambda shape: pl.BlockSpec(shape, lambda i: (0,) * len(shape))
    shapes = [
        (edim // n_dp, width),
        (all_words // n_dp, width),
        (4, part, width),
        (part, width),
        (part, width),
        (part, width),
        (part, ff),
        (ff // n_dp, width),
        (4, part),
        (2, part),
        (2, part),
        (part,),
        (part,),
        (part,),
        (part,),
        (ff // n_dp,),
    ]
    through = [words_low, ents_low, words_grad]
    return pl.pallas_call(
        functools.partial(last_kernel, n_dp),
        grid=(rows // block,),
        out_shape=[jax.ShapeDtypeStruct((rows, edim), F32)] * 3
        + [jax.ShapeDtypeStruct(shape, F32) for shape in shapes]
        + [jax.ShapeDtypeStruct(array.shape, array.dtype) for array in through],
        in_specs=[blocked(edim), blocked(LANES), blocked(edim), blocked(edim)]
        + [whole(array.shape) for array in (ffn, attn, ent, bias)]
        + [whole(array.shape) for array in through],
        out_specs=[blocked(edim)] * 3 + [whole(shape) for shape in shapes] + [whole(array.shape) for array in through],
        compiler_params=pltpu.CompilerParams(vmem_limit_bytes=VMEM_BYTES),
        name="last",
    )(table_grad, touched, first, second, ffn, attn, ent, bias, words_low, ents_low, words_grad)


def on_device(
    word_states,
    segments,
    entity_ids,
    entity_pos,
    ent_table,
    first_moment,
    second_moment,
    ent_proj,
    pos_table,
    query_weight,
    query_bias,
    key_weight,
    key_bias,
    value_weight,
    value_bias,
    out_weight,
    out_bias,
    norm_gain,
    norm_shift,
    up_weight,
    up_bias,
    down_weight,
    down_bias,
    word_cot,
    ent_cot,
):
    n_dp = lax.axis_size("dp")
    nz = n_dp // 2
    width, ff = up_weight.shape
    all_words = segments.shape[1]
    words, word_cots, ent_cots, all_ids, rows = fetch(nz, word_states, word_cot, ent_cot, entity_ids, ent_table)
    ent_hidden, hidden_low, query_words, query_ents, keys, values, probs, mixed = forward(
        words,
        rows,
        entity_pos,
        segments,
        ent_proj,
        pos_table,
        query_weight,
        query_bias,
        key_weight,
        key_bias,
        value_weight,
        value_bias,
    )
    ents = entity_ids.shape[1]
    word_out, ent_out, word_grad, ffn_sum, attn_sum, ent_sum, bias_sum, table_grad, touched = layer(
        nz, ent_table.shape[0], words, ent_hidden, mixed, out_weight, out_bias, norm_gain, norm_shift, up_weight, up_bias, down_weight, down_bias,
        word_cots, ent_cots, hidden_low, query_words, query_ents, keys, values, probs, query_weight, key_weight, value_weight,
        rows, entity_pos, ent_proj, all_ids.reshape(-1, ents),
    )
    (table_grad, table_update, new_second, proj_grad, pos_grad, query_grad, key_grad, value_grad, out_grad, up_grad, down_grad,
     query_bias_grad, gain_grad, shift_grad, key_bias_grad, value_bias_grad, out_bias_grad, down_bias_grad, up_bias_grad,
     word_out, ent_out, word_grad,
    ) = last(
        n_dp, ff, all_words, table_grad, touched, first_moment, second_moment, ffn_sum, attn_sum, ent_sum, bias_sum, word_out, ent_out, word_grad
    )
    return (
        word_out,
        ent_out,
        word_grad,
        proj_grad,
        pos_grad,
        query_grad,
        query_bias_grad,
        key_grad,
        key_bias_grad,
        value_grad,
        value_bias_grad,
        out_grad,
        out_bias_grad,
        gain_grad,
        shift_grad,
        up_grad,
        up_bias_grad,
        down_grad,
        down_bias_grad,
        table_grad,
        table_update,
        new_second,
    )


def solution(mesh):
    return jax.shard_map(
        on_device,
        mesh=mesh,
        in_specs=(
            P("dp", "seq", None),
            P("dp", None),
            P("dp", None),
            P("dp", None),
            P(("dp", "seq"), None),
            P(("dp", "seq"), None),
            P(("dp", "seq"), None),
            P(),
            P(),
            P(),
            P(),
            P(),
            P(),
            P(),
            P(),
            P(),
            P(),
            P(),
            P(),
            P(),
            P(),
            P(),
            P(),
            P("dp", "seq", None),
            P("dp", "seq", None),
        ),
        out_specs=(
            P("dp", "seq", None),
            P("dp", "seq", None),
            P("dp", "seq", None),
            P("dp", None),
            P("dp", None),
            P(None, "dp", None),
            P(None, "dp"),
            P("dp", None),
            P("dp"),
            P("dp", None),
            P("dp"),
            P("dp", None),
            P("dp"),
            P(None, "dp"),
            P(None, "dp"),
            P("dp", None),
            P("dp"),
            P("dp", None),
            P("dp"),
            P(("dp", "seq"), None),
            P(("dp", "seq"), None),
            P(("dp", "seq"), None),
        ),
        check_vma=False,
    )
```

```python
import functools
import math

import jax
import jax.numpy as jnp
from jax import lax
from jax.experimental import pallas as pl
from jax.experimental.pallas import tpu as pltpu
from jax.sharding import PartitionSpec as P

HEADS = 12
HEAD = 64
LANES = 128
MESH = pl.DeviceIdType.MESH
LOW = jnp.bfloat16
F32 = jnp.float32
VMEM_BYTES = 125 * 512 * 1024

norm_eps = 1e-05
beta_one = 0.9
beta_two = 0.98
adam_eps = 1e-06
adam_step = 10.0
masked_score = -1e30


def dot(left, right):
    return jnp.dot(left, right, preferred_element_type=F32)


def dot_rows(left, right):
    return lax.dot_general(left, right, (((1,), (1,)), ((), ())), preferred_element_type=F32)


def dot_columns(left, right):
    return lax.dot_general(left, right, (((0,), (0,)), ((), ())), preferred_element_type=F32)


def span(start, size, unit):
    if isinstance(start, int):
        return pl.ds(start, size)
    return pl.ds(pl.multiple_of(start, unit), size)


def padded(rows):
    return -(-rows // 16) * 16


def loop(count, body, carry=0, unroll=1):
    def steps(i, carried):
        for k in range(unroll):
            carried = body(i * unroll + k, carried)
        return carried

    return lax.fori_loop(0, count // unroll, steps, carry)


class Place:
    def __init__(self, nz):
        self.dp, self.seq = lax.axis_index("dp"), lax.axis_index("seq")
        self.z, self.x = self.dp // 2, self.dp % 2
        self.y, self.core = self.seq // 2, self.seq % 2
        self.nz = nz
        self.other_core = (self.dp, self.y * 2 + 1 - self.core)
        self.other_y = (self.dp, (1 - self.y) * 2 + self.core)
        self.diagonal = (self.dp, (1 - self.y) * 2 + 1 - self.core)
        self.other_x = (self.z * 2 + 1 - self.x, self.seq)
        self.ahead = [(((self.z + k) % nz) * 2 + self.x, self.seq) for k in range(1, nz)]

    def z_ahead(self, k):
        return (self.z + k) % self.nz


def meet(partners):
    barrier = pltpu.get_barrier_semaphore()
    for partner in partners:
        pl.semaphore_signal(barrier, inc=1, device_id=partner, device_id_type=MESH)
    pl.semaphore_wait(barrier, len(partners))


class Remote:
    def __init__(self, copies, number, src, dst, device):
        self.copies, self.number, self.src, self.dst, self.device = copies, number, src, dst, device
        self.open = True

    def make(self, landing=False):
        return pltpu.make_async_remote_copy(
            src_ref=self.dst() if landing else self.src(),
            dst_ref=self.dst(),
            send_sem=self.copies.send_sem.at[self.number],
            recv_sem=self.copies.recv_sem.at[self.number],
            device_id=self.device,
            device_id_type=MESH,
        )

    def wait_recv(self):
        self.make(landing=True).wait_recv()

    def wait_send(self):
        if self.open:
            self.make().wait_send()
        self.open = False


class Local:
    def __init__(self, copies, number, src, dst):
        self.copies, self.number, self.src, self.dst = copies, number, src, dst

    def make(self):
        return pltpu.make_async_copy(self.src(), self.dst(), self.copies.local_sem.at[self.number])

    def wait(self):
        self.make().wait()


class Copies:
    def __init__(self, send_sem, recv_sem, local_sem):
        self.send_sem, self.recv_sem, self.local_sem = send_sem, recv_sem, local_sem
        self.local_count = 0
        self.sent = []

    def send(self, src, dst, device):
        copy = Remote(self, len(self.sent), src, dst, device)
        copy.make().start()
        self.sent.append(copy)
        return copy

    def local(self, src, dst):
        copy = Local(self, self.local_count, src, dst)
        self.local_count += 1
        copy.make().start()
        return copy

    def finish(self):
        for copy in self.sent:
            copy.wait_send()


def copy_semaphores(remote, local):
    return [
        pltpu.SemaphoreType.DMA((remote,)),
        pltpu.SemaphoreType.DMA((remote,)),
        pltpu.SemaphoreType.DMA((local,)),
    ]


ANY = pl.BlockSpec(memory_space=pl.ANY)
IN_VMEM = pl.BlockSpec(memory_space=pltpu.VMEM)


def call(kernel, outs, in_specs, out_specs, scratch, name, collective_id=None):
    params = {"vmem_limit_bytes": VMEM_BYTES}
    if collective_id is not None:
        params.update(collective_id=collective_id, has_side_effects=True)
    return pl.pallas_call(
        kernel,
        out_shape=[jax.ShapeDtypeStruct(shape, dtype) for shape, dtype in outs],
        in_specs=in_specs,
        out_specs=out_specs,
        scratch_shapes=scratch,
        compiler_params=pltpu.CompilerParams(**params),
        name=name,
    )


def fetch_kernel(nz, words, word_cot, ent_cot, ids, table, all_words, word_cots, ent_cots, all_ids, rows_out, *scratch):
    table_full, table_low, picked, answers, held, from_core, from_x, from_z, from_y, ids_here = scratch[:10]
    copies = Copies(*scratch[10:])
    place = Place(nz)
    z, x, y, core = place.z, place.x, place.y, place.core
    n_dp = 2 * nz
    word_here, ent_here = words.shape[1], ent_cot.shape[1]
    ents = ids.shape[1]
    dp_others = [((place.dp + k) % n_dp, place.seq) for k in range(1, n_dp)]
    meet([place.other_core, place.other_y, place.diagonal] + dp_others)
    whole_table = copies.local(lambda: table, lambda: table_full)
    ids_here[place.dp] = ids[...]
    id_copies = [copies.send(lambda: ids, lambda: ids_here.at[place.dp], device) for device in dp_others]
    quarter = span(place.seq * word_here, word_here, 128)
    word_copies = [
        copies.send(lambda: words.at[1 - core], lambda: all_words.at[quarter], place.diagonal),
        copies.send(lambda: words.at[core], lambda: all_words.at[quarter], place.other_y),
        copies.send(lambda: words.at[1 - core], lambda: all_words.at[quarter], place.other_core),
        copies.send(lambda: word_cot.at[1 - core], lambda: word_cots.at[span(core * word_here, word_here, 128)], place.other_core),
        copies.send(lambda: ent_cot.at[1 - core], lambda: ent_cots.at[span(core * ent_here, ent_here, 32)], place.other_core),
    ]
    all_words[quarter] = words[core]
    word_cots[span(core * word_here, word_here, 128)] = word_cot[core]
    ent_cots[span(core * ent_here, ent_here, 32)] = ent_cot[core]
    whole_table.wait()
    rows_dev = table.shape[0]

    def narrow(i, _):
        where = span(i * 128, 128, 128)
        table_low[where] = table_full[where].astype(LOW)
        return 0

    loop(rows_dev // 128, narrow)
    for copy in id_copies:
        copy.wait_recv()
    all_ids[...] = ids_here[...]
    base = (place.dp * 4 + place.seq) * rows_dev
    tiles = rows_dev // LANES

    def look_up(zz):
        def group(g, _):
            asked = ids_here[zz * 2 + g // 2, pl.ds(g % 2, 1), :] - base
            column = jnp.transpose(jnp.broadcast_to(asked, (ents, ents)))
            for j in range(tiles):
                number = lax.broadcasted_iota(jnp.int32, (ents, LANES), 1) + j * LANES
                hit = jnp.where(column == number, 1.0, 0.0).astype(LOW)
                picked[span(g * ents, ents, ents), pl.ds(j * LANES, LANES)] = hit
            return 0

        loop(4, group)
        answer = dot(picked[...], table_low[...]).astype(LOW)
        answers[zz] = answer.reshape(2, 2, ents, answer.shape[-1])

    order = [place.z_ahead(k + 1) for k in range(nz)]
    core_copies, x_copies, z_copies = [], [], []

    def core_send(zz):
        return copies.send(lambda: answers.at[zz, :, 1 - core], lambda: from_core.at[zz], place.other_core)

    def after_core(k):
        zz = order[k]
        core_copies[k].wait_recv()
        held[zz] = answers[zz, :, core] + from_core[zz]
        x_copies.append(copies.send(lambda: held.at[zz, 1 - x], lambda: from_x.at[zz], place.other_x))

    def after_x(k):
        zz = order[k]
        x_copies[k].wait_recv()
        held[zz, x] = held[zz, x] + from_x[zz]
        if k < nz - 1:
            z_copies.append(copies.send(lambda: held.at[zz, x], lambda: from_z.at[k], place.ahead[k]))

    for k in range(nz + 2):
        if k < nz:
            look_up(order[k])
            core_copies.append(core_send(order[k]))
        if 0 <= k - 1 < nz:
            after_core(k - 1)
        if 0 <= k - 2:
            after_x(k - 2)
    total = held[z, x]
    for k in range(nz - 1):
        z_copies[k].wait_recv()
        total = total + from_z[k]
    from_y[0] = total
    y_copy = copies.send(lambda: from_y.at[0], lambda: from_y.at[1], place.other_y)
    y_copy.wait_recv()
    rows_out[...] = from_y[0] + from_y[1]
    for copy in word_copies:
        copy.wait_recv()
    copies.finish()


def fetch(nz, words, word_cot, ent_cot, ids, table):
    _, word_here, width = words.shape
    ent_here, ents, (rows_dev, edim) = ent_cot.shape[1], ids.shape[1], table.shape
    n_dp = 2 * nz
    return call(
        functools.partial(fetch_kernel, nz),
        [
            ((4 * word_here, width), LOW),
            ((2 * word_here, width), LOW),
            ((2 * ent_here, width), LOW),
            ((n_dp, 2, ents), jnp.int32),
            ((ents, edim), LOW),
        ],
        [IN_VMEM] * 4 + [ANY],
        [IN_VMEM] * 5,
        [
            pltpu.VMEM((rows_dev, edim), F32),
            pltpu.VMEM((rows_dev, edim), LOW),
            pltpu.VMEM((4 * ents, rows_dev), LOW),
            pltpu.VMEM((nz, 2, 2, ents, edim), LOW),
            pltpu.VMEM((nz, 2, ents, edim), LOW),
            pltpu.VMEM((nz, 2, ents, edim), LOW),
            pltpu.VMEM((nz, ents, edim), LOW),
            pltpu.VMEM((nz - 1, ents, edim), LOW),
            pltpu.VMEM((2, ents, edim), LOW),
            pltpu.VMEM((n_dp, 2, ents), jnp.int32),
        ]
        + copy_semaphores(n_dp + 4 + 3 * nz + 2, 1),
        "fetch",
        1,
    )(words, word_cot, ent_cot, ids, table)


def lane_mask(rows, head):
    lane = lax.broadcasted_iota(jnp.int32, (rows, LANES), 1)
    return (lane >= head * HEAD) & (lane < (head + 1) * HEAD)


def row_of(vector):
    return vector[...].astype(F32).reshape(1, vector.shape[0])


def own_half(vector, y):
    row = row_of(vector)
    half = row.shape[1] // 2
    return jnp.where(y == 0, row[:, :half], row[:, half:])


def as_column(row):
    parts = [
        jnp.transpose(jnp.broadcast_to(row[:, i : i + LANES], (LANES, LANES)))
        for i in range(0, row.shape[1], LANES)
    ]
    return jnp.concatenate(parts, axis=0) if len(parts) > 1 else parts[0]


def forward_kernel(
    words, rows, ent_pos, segments, ent_proj, pos_table, query_weight, query_bias, key_weight, key_bias, value_weight, value_bias,
    ent_hidden, hidden_turned, query_words, query_ents, keys, values, probs, mixed,
    hidden_low, query_here, key_here, value_here, values_turned, mask, local_sem,
):
    y, core = lax.axis_index("seq") // 2, lax.axis_index("seq") % 2
    half = keys.shape[1]
    all_words, ents = words.shape[0], rows.shape[0]
    ent_pos, segments = ent_pos[pl.ds(core, 1), :], segments[pl.ds(core, 1), :]
    tokens = all_words + ents
    columns = span(y * half, half, LANES)
    weight_copies = [
        pltpu.make_async_copy(query_weight.at[:, :, columns], query_here, local_sem.at[0]),
        pltpu.make_async_copy(key_weight.at[:, columns], key_here, local_sem.at[1]),
        pltpu.make_async_copy(value_weight.at[:, columns], value_here, local_sem.at[2]),
    ]
    for copy in weight_copies:
        copy.start()
    position = as_column(ent_pos)
    picks = []
    for j in range(all_words // LANES):
        number = lax.broadcasted_iota(jnp.int32, (ents, LANES), 1) + j * LANES
        picks.append(jnp.where(position == number, 1.0, 0.0))
    pick = jnp.concatenate(picks, axis=1)
    word_seg = segments.astype(F32)
    ent_seg = jnp.sum(pick * word_seg, axis=1, keepdims=True)
    ent_hidden[...] = dot(rows[...], ent_proj[...]) + dot(pick.astype(LOW), pos_table[...])
    hidden_low[:all_words] = words[...]
    hidden_low[all_words:] = ent_hidden[...].astype(LOW)
    ent_row = jnp.transpose(jnp.broadcast_to(ent_seg, (ents, LANES)))[:1]
    seg_row = jnp.concatenate([word_seg, ent_row], axis=1)
    seg_column = jnp.concatenate([as_column(word_seg), jnp.broadcast_to(ent_seg, (ents, LANES))], axis=0)
    for j in range(tokens // LANES):
        here = slice(j * LANES, (j + 1) * LANES)
        mask[:, here] = jnp.where(seg_column == seg_row[:, here], 0.0, masked_score)

    query_b = query_bias[:, columns].astype(F32)
    for copy in weight_copies:
        copy.wait()
    word_low, ent_low = hidden_low[:all_words], hidden_low[all_words:]
    query_words[:all_words] = (dot(word_low, query_here[0]) + query_b[0:1]).astype(LOW)
    query_ents[:all_words] = (dot(word_low, query_here[1]) + query_b[1:2]).astype(LOW)
    query_words[all_words:] = (dot(ent_low, query_here[2]) + query_b[2:3]).astype(LOW)
    query_ents[all_words:] = (dot(ent_low, query_here[3]) + query_b[3:4]).astype(LOW)
    keys[...] = (dot(hidden_low[...], key_here[...]) + own_half(key_bias, y)).astype(LOW)
    value = dot(hidden_low[...], value_here[...]) + own_half(value_bias, y)
    values[...] = value.astype(LOW)
    values_turned[...] = jnp.transpose(value).astype(LOW)
    for i in range(words.shape[1] // LANES):
        here = slice(i * LANES, (i + 1) * LANES)
        hidden_turned[here, :] = jnp.transpose(hidden_low[:, here].astype(F32)).astype(LOW)
    scale = 1.0 / math.sqrt(HEAD)
    tiles = tokens // LANES

    def pair_step(pair, _):
        lanes = span(pair * LANES, LANES, LANES)
        key, turned = keys[:, lanes], values_turned[lanes, :]
        row = lax.broadcasted_iota(jnp.int32, (LANES, tokens), 0)
        own_key, own_turned = [], []
        for head in range(2):
            own_key.append(jnp.where(lane_mask(tokens, head), key, jnp.zeros_like(key)))
            own_rows = (row >= head * HEAD) & (row < (head + 1) * HEAD)
            own_turned.append(jnp.where(own_rows, turned, jnp.zeros_like(turned)))
        for i in range(tiles):
            place = slice(i * LANES, (i + 1) * LANES)
            query_w, query_e = query_words[place, lanes], query_ents[place, lanes]
            total = None
            for head in range(2):
                raw = jnp.concatenate(
                    [dot_rows(own_key[head][:all_words], query_w), dot_rows(own_key[head][all_words:], query_e)], axis=0
                )
                score = raw * scale + mask[:, place]
                weight = jnp.exp(score - jnp.max(score, axis=0, keepdims=True))
                prob = (weight * (1.0 / jnp.sum(weight, axis=0, keepdims=True))).astype(LOW)
                probs[pair * 2 + head, :, place] = prob
                part = dot(own_turned[head], prob)
                total = part if total is None else total + part
            mixed[place, lanes] = jnp.transpose(total).astype(LOW)
        return 0

    loop(half // LANES, pair_step)


def forward(words, rows, ent_pos, segments, ent_proj, pos_table, query_weight, query_bias, key_weight, key_bias, value_weight, value_bias):
    all_words, width = words.shape
    ents = rows.shape[0]
    tokens, half = all_words + ents, width // 2
    return call(
        forward_kernel,
        [
            ((ents, width), F32),
            ((width, tokens), LOW),
            ((tokens, half), LOW),
            ((tokens, half), LOW),
            ((tokens, half), LOW),
            ((tokens, half), LOW),
            ((HEADS // 2, tokens, tokens), LOW),
            ((tokens, half), LOW),
        ],
        [IN_VMEM] * 6 + [ANY, IN_VMEM, ANY, IN_VMEM, ANY, IN_VMEM],
        [IN_VMEM] * 8,
        [
            pltpu.VMEM((tokens, width), LOW),
            pltpu.VMEM((4, width, half), LOW),
            pltpu.VMEM((width, half), LOW),
            pltpu.VMEM((width, half), LOW),
            pltpu.VMEM((half, tokens), LOW),
            pltpu.VMEM((tokens, tokens), F32),
            pltpu.SemaphoreType.DMA((3,)),
        ],
        "forward",
    )(words, rows, ent_pos, segments, ent_proj, pos_table, query_weight, query_bias, key_weight, key_bias, value_weight, value_bias)


class Engine:
    RATES = {"core": 130e3, "x": 75e3, "y": 75e3, "z": 22e3}
    LATENCY = 2.0

    def __init__(self):
        self.clock, self.free, self.streams = 0.0, {}, []

    def transfer(self, link, size):
        start = max(self.clock, self.free.get(link, 0.0))
        self.free[link] = start + size / self.RATES[link]
        return self.free[link] + self.LATENCY

    def add(self, steps):
        self.streams.append([self.clock, list(steps)])
        self.poll()

    def run(self, stream):
        self.clock = max(self.clock, stream[0])
        ready = stream[1].pop(0)()
        stream[0] = self.clock if ready is None else ready

    def next(self):
        live = [stream for stream in self.streams if stream[1]]
        return min(live, key=lambda stream: stream[0]) if live else None

    def poll(self):
        while (stream := self.next()) is not None and stream[0] <= self.clock:
            self.run(stream)

    def work(self, time):
        self.clock += time
        self.poll()

    def drain(self):
        while (stream := self.next()) is not None:
            self.run(stream)


def blocks_of(rows):
    for size in (96, 64, 48, 32):
        if rows % size == 0:
            return size
    return 16


def add_blocks(engine, target, parts, leading, rows, columns):
    size = blocks_of(rows)
    count = rows // size

    def block(i, _):
        lead, row = i // count, (i % count) * size
        where = span(row, size, 16)
        if len(parts) == 2:
            value = parts[0](lead, where) + parts[1](lead, where)
        else:
            value = parts[0](lead, where).astype(F32)
            for part in parts[1:]:
                value = value + part(lead, where).astype(F32)
            value = value.astype(LOW)
        target(lead, where, value)
        return 0

    loop(leading * count, block)
    engine.clock += 0.3 + leading * rows * columns / 1e6


class Job:
    def __init__(self, grads, reduced, base, size, order, columns):
        self.grads, self.reduced, self.base, self.size, self.order, self.columns = grads, reduced, base, size, order, columns
        self.half = size // 2
        self.part = size // 4 if order == "yxz" else size // 2

    def scratch(self, nz):
        shapes = [(nz, 2, self.half, self.columns)]
        if self.order == "yxz":
            shapes.append((nz, 2, self.part, self.columns))
        elif self.order == "xzy":
            shapes.append((2, self.part, self.columns))
        shapes += [(nz, self.part, self.columns), (nz - 1, self.part, self.columns)]
        return [pltpu.VMEM(shape, LOW) for shape in shapes]

    def remote_count(self, nz):
        return 1 + (1 if self.order != "xz" else 0) + 1 + (nz - 1) + 1 + 1

    def prepare(self, engine, place, copies, scratch):
        nz, z, x, y, core = place.nz, place.z, place.x, place.y, place.core
        base, half, part, order, columns = self.base, self.half, self.part, self.order, self.columns
        held = self.grads.at[:, :, span(base + core * half, half, 16)]
        from_core = scratch[0]
        from_y = scratch[1] if order != "xz" else None
        from_x, from_z = scratch[-2:]
        live = {}
        row_bytes = 2 * columns
        theirs = span(base + (1 - core) * half, half, 16)
        mine = span(base + core * half, half, 16)
        own_rows = span(y * part, part, 16) if order == "yxz" else pl.ds(0, part)
        final_rows = span(base + core * half + (y * part if order == "yxz" else 0), part, 16)

        def start():
            live["core"] = copies.send(lambda: self.grads.at[:, :, theirs], lambda: from_core, place.other_core)
            return engine.transfer("core", 2 * nz * half * row_bytes)

        def send_x():
            live["x"] = copies.send(lambda: held.at[:, 1 - x, own_rows], lambda: from_x, place.other_x)
            return engine.transfer("x", nz * part * row_bytes)

        def after_core():
            live["core"].wait_recv()

            def put(i, where, value):
                held[i // 2, i % 2, where] = value

            add_blocks(
                engine,
                put,
                [lambda i, where: held[i // 2, i % 2, where], lambda i, where: from_core[i // 2, i % 2, where]],
                2 * nz,
                half,
                columns,
            )
            if order == "yxz":
                live["y"] = copies.send(
                    lambda: held.at[:, :, span((1 - y) * part, part, 16)], lambda: from_y, place.other_y
                )
                return engine.transfer("y", 2 * nz * part * row_bytes)
            return send_x()

        def shifted(where):
            return span(y * part + where.start, where.size, 16) if order == "yxz" else where

        def after_y():
            live["y"].wait_recv()

            def put(i, where, value):
                held[i // 2, i % 2, shifted(where)] = value

            add_blocks(
                engine,
                put,
                [lambda i, where: held[i // 2, i % 2, shifted(where)], lambda i, where: from_y[i // 2, i % 2, where]],
                2 * nz,
                part,
                columns,
            )
            return send_x()

        def send_z(k):
            return copies.send(
                lambda: held.at[place.z_ahead(k + 1), x, own_rows], lambda: from_z.at[k], place.ahead[k]
            )

        def after_x():
            live["x"].wait_recv()

            def put(i, where, value):
                held[i, x, shifted(where)] = value

            add_blocks(
                engine,
                put,
                [lambda i, where: held[i, x, shifted(where)], lambda i, where: from_x[i, where]],
                nz,
                part,
                columns,
            )
            live["z"] = [send_z(k) for k in range(nz - 1)]
            return engine.transfer("z", part * row_bytes)

        def after_z():
            for copy in live["z"]:
                copy.wait_recv()

            def put(i, where, value):
                if order == "yxz":
                    self.reduced[span(base + core * half + y * part + where.start, where.size, 16)] = value
                elif order == "xz":
                    self.reduced[y, span(base + core * half + where.start, where.size, 16)] = value
                else:
                    from_y[0, where] = value

            def parts(k):
                return lambda i, where: from_z[k, where]

            add_blocks(
                engine,
                put,
                [lambda i, where: held[z, x, shifted(where)]] + [parts(k) for k in range(nz - 1)],
                1,
                part,
                columns,
            )
            if order == "xzy":
                live["y2"] = copies.send(lambda: from_y.at[0], lambda: from_y.at[1], place.other_y)
            else:
                view = lambda: self.reduced.at[final_rows] if order == "yxz" else self.reduced.at[y, final_rows]
                live["y2"] = copies.send(view, view, place.other_y)
            return engine.transfer("y", part * row_bytes)

        def after_gather():
            live["y2"].wait_recv()
            if order == "xzy":

                def put(i, where, value):
                    self.reduced[span(base + core * half + where.start, where.size, 16)] = value

                add_blocks(
                    engine, put, [lambda i, where: from_y[0, where], lambda i, where: from_y[1, where]], 1, part, columns
                )
            view = lambda: self.reduced.at[:, mine] if order == "xz" else self.reduced.at[mine]
            live["core2"] = copies.send(view, view, place.other_core)
            return engine.transfer("core", 2 * half * row_bytes)

        def end():
            live["core2"].wait_recv()

        middle_steps = [after_core, after_y, after_x] if order == "yxz" else [after_core, after_x]
        self.steps = [start] + middle_steps + [after_z, after_gather, end]


def lane_mean(value):
    return jnp.mean(value, axis=-1, keepdims=True)


def column_sum(value):
    return jnp.sum(value, axis=0, keepdims=True)


ROW_BLOCK = 32


def ffn_plan(n_dp, width, ff):
    down_rows, row_pad = ff // n_dp, padded(width // n_dp)
    size = 128 if down_rows % 128 == 0 else 32
    order = "yxz" if size % 64 == 0 else "xzy"
    plan = [(base, size, order) for base in range(0, down_rows, size)]
    base = down_rows
    for pair in range(ff // width // 2):
        order = "yxz" if pair % 2 == 0 and row_pad % 32 == 0 else "xzy"
        plan.append((base, 2 * row_pad, order))
        base += 2 * row_pad
    plan.append((base, row_pad, "xzy"))
    return plan


def layer_kernel(
    nz, plan, words, ent_hidden, mixed, out_weight, out_bias, gains, shifts, up_weight, up_bias, down_weight, down_bias, word_cots, ent_cots,
    hidden_turned_in, query_words_in, query_ents_in, keys_in, values_in, probs_in, query_weight, key_weight, value_weight, rows, ent_pos, ent_proj, ids,
    word_out, ent_out, word_grad, ffn_reduced, attn_reduced, ent_reduced, bias_out, table_grad, touched, *scratch,
):
    (from_y_mixed, grad_mixed, grad_one, given, ffn_sum, attn_sum, ent_sum, bias_held, bias_from, all_rows, bias_heads, bias_middle,
     ffn_grads, grad_mixed_here) = scratch[:14]
    copies = Copies(*scratch[-3:])
    engine = Engine()
    place = Place(nz)
    z, x, y, core = place.z, place.x, place.y, place.core
    n_dp = 2 * nz
    tokens, half = mixed.shape
    width = 2 * half
    ents = ent_hidden.shape[0]
    all_words = tokens - ents
    word_half, ent_half = all_words // 2, ents // 2
    part_tokens = tokens // 2
    ff = up_weight.shape[1]
    parts = ff // width
    row_part, row_pad, down_rows = width // n_dp, padded(width // n_dp), ff // n_dp
    meet([place.other_core, place.other_y, place.other_x] + place.ahead)

    jobs = {"ffn": [], "attn": [], "ent": []}

    def make_jobs(names, sources):
        at = 14
        for name, base, size, order, columns in plan:
            job = Job(*sources.get(name, (None, None)), base, size, order, columns)
            used = len(job.scratch(nz))
            if name in names:
                job.prepare(engine, place, copies, scratch[at : at + used])
                jobs[name].append(job)
            at += used

    make_jobs(["ffn"], {"ffn": (ffn_grads, ffn_sum)})

    def token_rows(side):
        return span(side * word_half, word_half, LANES), span(all_words + side * ent_half, ent_half, 64)

    mine, theirs = token_rows(y), token_rows(1 - y)
    own_columns, other_columns = span(y * half, half, LANES), span((1 - y) * half, half, LANES)
    word_part, ent_part = pl.ds(0, word_half), pl.ds(word_half, ent_half)
    mixed_copies = [
        copies.send(lambda: mixed.at[theirs[0]], lambda: from_y_mixed.at[word_part], place.other_y),
        copies.send(lambda: mixed.at[theirs[1]], lambda: from_y_mixed.at[ent_part], place.other_y),
    ]
    engine.transfer("y", part_tokens * half * 2)
    out_copies, mixed_back = [], []

    def forward_phase(
        out_here, up_here, down_here, word_here, ent_here, mixed_full, work, normed_low, normal_one, inverse_one,
        act, slope, output, grad_two, grad_two_low, grad_one_low, normed_turned,
    ):
        cot, grad_up_low = output, slope
        weight_copies = [
            copies.local(lambda: out_weight, lambda: out_here),
            copies.local(lambda: words.at[mine[0]], lambda: word_here),
            copies.local(lambda: ent_hidden.at[span(y * ent_half, ent_half, 64)], lambda: ent_here),
            copies.local(lambda: up_weight, lambda: up_here),
            copies.local(lambda: down_weight, lambda: down_here),
            copies.local(lambda: word_cots, lambda: cot.at[word_part]),
            copies.local(lambda: ent_cots, lambda: cot.at[ent_part]),
        ]
        gain, shift = gains[...].astype(F32), shifts[...].astype(F32)
        out_b, down_b, up_b = row_of(out_bias), row_of(down_bias), row_of(up_bias)
        mixed_full[word_part, own_columns] = mixed[mine[0]]
        mixed_full[ent_part, own_columns] = mixed[mine[1]]
        for copy in weight_copies[:3]:
            copy.wait()
        for copy in mixed_copies:
            copy.wait_recv()
        mixed_full[:, other_columns] = from_y_mixed[...]
        work[...] = dot(mixed_full[...], out_here[...])

        def norm_one(residual):
            def step(i, _):
                rows = span(residual[1] + i * ROW_BLOCK, ROW_BLOCK, ROW_BLOCK)
                value = residual[0][span(i * ROW_BLOCK, ROW_BLOCK, ROW_BLOCK)].astype(F32) + (work[rows] + out_b)
                center = value - lane_mean(value)
                inverse = lax.rsqrt(lane_mean(center * center) + norm_eps)
                normal = center * inverse
                result = normal * gain[0:1] + shift[0:1]
                normal_one[rows] = normal
                inverse_one[rows] = jnp.broadcast_to(inverse, (ROW_BLOCK, LANES))
                normed_low[rows] = result.astype(LOW)
                return 0

            return step

        loop(word_half // ROW_BLOCK, norm_one((word_here, 0)), 0, 2)
        loop(ent_half // ROW_BLOCK, norm_one((ent_here, word_half)), 0, 2)
        weight_copies[3].wait()
        for j in range(parts):
            columns = slice(j * width, (j + 1) * width)
            work[...] = dot(normed_low[...], up_here[:, columns]) + up_b[:, columns]

            def gelu(i, _):
                rows = span(i * ROW_BLOCK, ROW_BLOCK, ROW_BLOCK)
                value = work[rows]
                below = 0.5 * (1.0 + lax.erf(value * (1.0 / math.sqrt(2.0))))
                density = jnp.exp(-0.5 * value * value) * (1.0 / math.sqrt(2.0 * math.pi))
                act[rows, columns] = (value * below).astype(LOW)
                slope[rows, columns] = (below + value * density).astype(LOW)
                return 0

            loop(part_tokens // ROW_BLOCK, gelu)
        normed_turned[...] = jnp.transpose(normed_low[...].astype(F32)).astype(LOW)
        for copy in weight_copies[4:]:
            copy.wait()
        work[...] = dot(act[...], down_here[...])

        def norm_two(i, sums):
            rows = span(i * ROW_BLOCK, ROW_BLOCK, ROW_BLOCK)
            value = (normal_one[rows] * gain[0:1] + shift[0:1]) + (work[rows] + down_b)
            center = value - lane_mean(value)
            inverse = lax.rsqrt(lane_mean(center * center) + norm_eps)
            normal = center * inverse
            cotangent = cot[rows].astype(F32)
            output[rows] = (normal * gain[1:2] + shift[1:2]).astype(LOW)
            scaled = cotangent * gain[1:2]
            result = inverse * (scaled - lane_mean(scaled) - normal * lane_mean(scaled * normal))
            grad_two[rows] = result
            grad_two_low[rows] = result.astype(LOW)
            return (
                sums[0] + column_sum(cotangent * normal),
                sums[1] + column_sum(cotangent),
                sums[2] + column_sum(result),
            )

        nothing = jnp.zeros((1, width), F32)
        gain_two, shift_two, down_sum = loop(part_tokens // ROW_BLOCK, norm_two, (nothing, nothing, nothing), 2)
        quarter, ent_quarter = word_half // 2, ent_half // 2
        out_copies.extend([
            copies.send(
                lambda: output.at[span((1 - core) * quarter, quarter, LANES)], lambda: word_out.at[core], place.other_core
            ),
            copies.send(
                lambda: output.at[span(word_half + (1 - core) * ent_quarter, ent_quarter, 32)],
                lambda: ent_out.at[core],
                place.other_core,
            ),
        ])
        out_local = [
            copies.local(lambda: output.at[span(core * quarter, quarter, LANES)], lambda: word_out.at[core]),
            copies.local(
                lambda: output.at[span(word_half + core * ent_quarter, ent_quarter, 32)], lambda: ent_out.at[core]
            ),
        ]
        engine.clock = 0.0
        engine.free = {}
        def put(base, value):
            ffn_grads[:, :, pl.ds(base, row_part)] = value.astype(LOW).reshape(nz, 2, row_part, width)

        def down_block(job):
            if down_rows % 128:
                per = width // down_rows
                for j in range(parts):
                    value = dot_columns(act[:, j * width : (j + 1) * width], grad_two_low[...])
                    value = value.reshape(per, down_rows, width)[:, job.base : job.base + job.size].astype(LOW)
                    for d in range(per):
                        slab = j * per + d
                        ffn_grads[slab // 2, slab % 2, pl.ds(job.base, job.size)] = value[d]
            else:
                for slab in range(n_dp):
                    start = slab * down_rows + job.base
                    value = dot_columns(act[:, start : start + job.size], grad_two_low[...])
                    ffn_grads[slab // 2, slab % 2, pl.ds(job.base, job.size)] = value.astype(LOW)
            engine.work(1.3)
            engine.add(job.steps)

        up_sums = []

        def grad_up(j):
            columns = slice(j * width, (j + 1) * width)
            work[...] = dot_rows(grad_two_low[...], down_here[columns, :])

            def grad_gelu(i, total_row):
                rows = span(i * ROW_BLOCK, ROW_BLOCK, ROW_BLOCK)
                value = work[rows] * slope[rows, columns].astype(F32)
                grad_up_low[rows, columns] = value.astype(LOW)
                return total_row + column_sum(value)

            up_sums.append(loop(part_tokens // ROW_BLOCK, grad_gelu, nothing, 2))
            engine.work(1.6)
            put(down_rows + j * row_pad, dot(normed_turned[...], grad_up_low[:, columns]))
            engine.work(0.9)

        downs = [job for job in jobs["ffn"] if job.base < down_rows]
        ups = [job for job in jobs["ffn"] if down_rows <= job.base][:-1]
        for job in downs:
            down_block(job)
        for j in range(parts):
            grad_up(j)
            if j % 2 == 1:
                engine.add(ups[j // 2].steps)
        work[...] = dot_rows(grad_up_low[...], up_here[...])
        engine.work(2.0)

        def back_one(i, sums):
            rows = span(i * ROW_BLOCK, ROW_BLOCK, ROW_BLOCK)
            upper = grad_two[rows] + work[rows]
            normal = normal_one[rows]
            inverse = inverse_one[rows, 0:1]
            scaled = upper * gain[0:1]
            result = inverse * (scaled - lane_mean(scaled) - normal * lane_mean(scaled * normal))
            grad_one[rows] = result
            grad_one_low[rows] = result.astype(LOW)
            return (
                sums[0] + column_sum(upper * normal),
                sums[1] + column_sum(upper),
                sums[2] + column_sum(result),
            )

        gain_one, shift_one, out_sum = loop(part_tokens // ROW_BLOCK, back_one, (nothing, nothing, nothing), 2)
        engine.work(1.0)
        grad_mixed_here[...] = dot_rows(grad_one_low[...], out_here[other_columns, :]).astype(LOW)
        mixed_back.extend([
            copies.send(lambda: grad_mixed_here.at[word_part], lambda: grad_mixed.at[mine[0]], place.other_y),
            copies.send(lambda: grad_mixed_here.at[ent_part], lambda: grad_mixed.at[mine[1]], place.other_y),
        ])
        engine.transfer("y", part_tokens * half * 2)
        own = dot_rows(grad_one_low[...], out_here[own_columns, :]).astype(LOW)
        grad_mixed[mine[0]] = own[:word_half]
        grad_mixed[mine[1]] = own[word_half:]
        engine.work(1.0)
        put(down_rows + parts * row_pad, dot_columns(mixed_full[...], grad_one_low[...]))
        engine.work(0.8)
        engine.add(jobs["ffn"][-1].steps)
        bias_rows = [out_sum, gain_one, gain_two, shift_one, shift_two] + up_sums + [down_sum]
        for i, row in enumerate(bias_rows):
            bias_middle[i : i + 1] = row
        for copy in out_copies:
            copy.wait_send()
        for copy in out_local:
            copy.wait()

    tall = lambda columns, dtype: pltpu.VMEM((part_tokens, columns), dtype)
    pl.run_scoped(
        forward_phase,
        pltpu.VMEM((width, width), LOW),
        pltpu.VMEM((width, ff), LOW),
        pltpu.VMEM((ff, width), LOW),
        pltpu.VMEM((word_half, width), LOW),
        pltpu.VMEM((ent_half, width), F32),
        tall(width, LOW),
        tall(width, F32),
        tall(width, LOW),
        tall(width, F32),
        tall(LANES, F32),
        tall(ff, LOW),
        tall(ff, LOW),
        tall(width, LOW),
        tall(width, F32),
        tall(width, LOW),
        tall(width, LOW),
        pltpu.VMEM((width, part_tokens), LOW),
    )
    live_words = {}

    def backward_phase(
        query_words, query_ents, keys, values, probs, query_here, key_here, value_here, keys_turned,
        grad_query_words, grad_query_ents, grad_keys, grad_values, hidden_turned, grad_hidden, hits, attn_grads, ent_grads, table_here, touched_here,
    ):
        total = grad_one
        make_jobs(["attn", "ent"], {"attn": (attn_grads, attn_sum), "ent": (ent_grads, ent_sum)})
        columns = span(y * half, half, LANES)
        copies_in = [
            copies.local(lambda: values_in, lambda: values),
            copies.local(lambda: keys_in, lambda: keys),
            copies.local(lambda: query_words_in, lambda: query_words),
            copies.local(lambda: query_ents_in, lambda: query_ents),
        ]
        prob_copies = []
        for head in range(probs.shape[0]):
            prob_copies.append(
                copies.local(lambda head=head: probs_in.at[head], lambda head=head: probs.at[head])
            )
        hidden_copy = copies.local(lambda: hidden_turned_in, lambda: hidden_turned)
        weight_copies = [
            copies.local(lambda: query_weight.at[:, :, columns], lambda: query_here),
            copies.local(lambda: key_weight.at[:, columns], lambda: key_here),
            copies.local(lambda: value_weight.at[:, columns], lambda: value_here),
        ]
        for copy in copies_in:
            copy.wait()
        for i in range(half // LANES):
            lanes = slice(i * LANES, (i + 1) * LANES)
            keys_turned[lanes, :] = jnp.transpose(keys[:, lanes].astype(F32)).astype(LOW)
        for copy in mixed_back:
            copy.wait_recv()
        engine.work(2.0)
        scale = 1.0 / math.sqrt(HEAD)
        tiles = tokens // LANES

        for pair in range(half // LANES):
            lanes = slice(pair * LANES, (pair + 1) * LANES)
            grad_query_w = jnp.zeros((LANES, tokens), F32)
            grad_query_e = jnp.zeros((LANES, tokens), F32)
            grad_key_w = jnp.zeros((all_words, LANES), F32)
            grad_key_e = jnp.zeros((ents, LANES), F32)
            grad_value = jnp.zeros((tokens, LANES), F32)
            for head in range(2):
                own = lane_mask(tokens, head)
                value = values[:, lanes]
                own_value = jnp.where(own, value, jnp.zeros_like(value))
                prob_copies[pair * 2 + head].wait()

                given_heads = grad_mixed[:, lanes]
                grad_scores = probs.at[pair * 2 + head]
                grad_value += dot(grad_scores[...], jnp.where(own, given_heads, jnp.zeros_like(given_heads)))
                for i in range(tiles):
                    where = slice(i * LANES, (i + 1) * LANES)
                    grad_prob = dot_rows(own_value, grad_mixed[where, lanes])
                    prob = grad_scores[:, where].astype(F32)
                    both = prob * grad_prob
                    grad_scores[:, where] = (both - prob * jnp.sum(both, axis=0, keepdims=True)).astype(LOW)
                engine.work(1.7)
                query_w, query_e = query_words[:, lanes], query_ents[:, lanes]
                grad_key_w += dot(grad_scores[:all_words], jnp.where(own, query_w, jnp.zeros_like(query_w)))
                grad_key_e += dot(grad_scores[all_words:], jnp.where(own, query_e, jnp.zeros_like(query_e)))
                row = lax.broadcasted_iota(jnp.int32, (LANES, tokens), 0)
                own_rows = (row >= head * HEAD) & (row < (head + 1) * HEAD)
                turned = keys_turned[lanes, :]
                turned = jnp.where(own_rows, turned, jnp.zeros_like(turned))
                grad_query_w += dot(turned[:, :all_words], grad_scores[:all_words])
                grad_query_e += dot(turned[:, all_words:], grad_scores[all_words:])
                engine.work(1.7)
            grad_query_w = jnp.transpose(grad_query_w) * scale
            grad_query_e = jnp.transpose(grad_query_e) * scale
            grad_key_w, grad_key_e = grad_key_w * scale, grad_key_e * scale
            sums = [
                column_sum(grad_query_w[:all_words]),
                column_sum(grad_query_e[:all_words]),
                column_sum(grad_query_w[all_words:]),
                column_sum(grad_query_e[all_words:]),
                column_sum(grad_key_w) + column_sum(grad_key_e),
                column_sum(grad_value),
            ]
            for i, sum_row in enumerate(sums):
                bias_heads[i : i + 1, lanes] = sum_row
            grad_query_words[:, lanes] = grad_query_w.astype(LOW)
            grad_query_ents[:, lanes] = grad_query_e.astype(LOW)
            grad_keys[:all_words, lanes] = grad_key_w.astype(LOW)
            grad_keys[all_words:, lanes] = grad_key_e.astype(LOW)
            grad_values[:, lanes] = grad_value.astype(LOW)
            engine.work(0.5)

        for copy in weight_copies + [hidden_copy]:
            copy.wait()
        ent_rows, word_rows = slice(all_words, tokens), slice(0, all_words)

        def hidden_part(here, first, second):
            grad_hidden[here] = (
                dot_rows(grad_keys[here], key_here[...])
                + dot_rows(grad_values[here], value_here[...])
                + dot_rows(grad_query_words[here], query_here[first])
                + dot_rows(grad_query_ents[here], query_here[second])
            ).astype(LOW)

        hidden_part(ent_rows, 2, 3)
        ent_copy = copies.send(lambda: grad_hidden.at[theirs[1]], lambda: given.at[ent_part], place.other_y)
        ent_ready = engine.transfer("y", ent_half * width * 2)
        engine.work(0.7)
        word_turned, ent_turned = hidden_turned[:, :all_words], hidden_turned[:, all_words:]
        attn_jobs = jobs["attn"]

        def attn_product(i, value):
            attn_grads[:, :, pl.ds(i * row_pad, row_part)] = value.astype(LOW).reshape(nz, 2, row_part, half)
            per = 6 // len(attn_jobs)
            if i % per == per - 1:
                engine.add(attn_jobs[i // per].steps)
            engine.work(0.6)

        attn_product(0, dot(word_turned, grad_query_words[:all_words]))
        attn_product(1, dot(word_turned, grad_query_ents[:all_words]))

        live_rows = {}

        def sum_hidden(start, count, own_start):
            def block(i, _):
                where = span(start + i * 32, 32, 32)
                own = span(own_start + i * 32, 32, 32)
                total[where] = grad_one[where] + (grad_hidden[own].astype(F32) + given[where].astype(F32))
                return 0

            loop(count // 32, block)

        row_bytes = ent_half * ent_proj.shape[0] * 2

        def rows_y():
            ent_copy.wait_recv()
            sum_hidden(word_half, ent_half, all_words + y * ent_half)
            row_grad = dot_rows(total[word_half:].astype(LOW), ent_proj[...]).astype(LOW)
            all_rows[place.dp, core, span(y * ent_half, ent_half, 64)] = row_grad
            view = lambda: all_rows.at[place.dp, core, span(y * ent_half, ent_half, 64)]
            live_rows["y"] = copies.send(view, view, place.other_y)
            return engine.transfer("y", row_bytes)

        def rows_z():
            live_rows["y"].wait_recv()
            view = lambda: all_rows.at[place.dp, core]
            live_rows["z"] = [copies.send(view, view, device) for device in place.ahead]
            return engine.transfer("z", 2 * row_bytes)

        def rows_x():
            for copy in live_rows["z"]:
                copy.wait_recv()
            live_rows["x"] = []
            for k in range(nz):
                view = lambda k=k: all_rows.at[place.z_ahead(k) * 2 + x, core]
                live_rows["x"].append(copies.send(view, view, place.other_x))
            return engine.transfer("x", nz * 2 * row_bytes)

        def rows_core():
            for copy in live_rows["x"]:
                copy.wait_recv()
            view = lambda: all_rows.at[:, core]
            live_rows["core"] = copies.send(view, view, place.other_core)
            return engine.transfer("core", n_dp * 2 * row_bytes)

        rows_dev = table_grad.shape[0]
        table_copies = []
        base_row = (place.dp * 4 + place.seq) * rows_dev

        def table_part(i):
            def step():
                if i == 0:
                    live_rows["core"].wait_recv()
                groups = ids.shape[0]
                number = lax.broadcasted_iota(jnp.int32, (table_block, ents), 0) + (base_row + i * table_block)
                count = jnp.zeros((table_block, ents), F32)
                for group in range(groups):
                    hit = jnp.where(ids[group : group + 1, :] == number, 1.0, 0.0)
                    count = count + hit
                    hits[:, group * ents : (group + 1) * ents] = hit.astype(LOW)
                here = pl.ds(i * table_block, table_block)
                for copy in table_copies[2 * i - 4 : 2 * i - 2] if i >= 2 else []:
                    copy.wait()
                dps = min(n_dp, 8)
                grad = None
                for first in range(0, n_dp, dps):
                    given_rows = all_rows[first : first + dps].reshape(dps * 2 * ents, ent_proj.shape[0])
                    value = dot(hits[:, first * 2 * ents : (first + dps) * 2 * ents], given_rows)
                    grad = value if grad is None else grad + value
                table_here[i % 2] = grad
                named = jnp.sum(count, axis=1, keepdims=True)
                touched_here[i % 2] = jnp.broadcast_to(named, (table_block, LANES)).astype(LOW)
                table_copies.append(copies.local(lambda: table_here.at[i % 2], lambda: table_grad.at[here]))
                table_copies.append(copies.local(lambda: touched_here.at[i % 2], lambda: touched.at[here]))
                engine.clock += 1.2

            return step

        engine.add(
            [lambda: ent_ready, rows_y, rows_z, rows_x, rows_core] + [table_part(i) for i in range(rows_dev // table_block)]
        )
        hidden_part(word_rows, 0, 1)
        word_copy = copies.send(lambda: grad_hidden.at[theirs[0]], lambda: given.at[word_part], place.other_y)
        word_ready = engine.transfer("y", word_half * width * 2)
        engine.work(1.5)

        bias_rows = bias_held.shape[0]
        bias_held[...] = jnp.zeros_like(bias_held)
        bias_held[0:6, columns] = bias_heads[0:6]
        bias_held[6:bias_rows] = bias_middle[0 : bias_rows - 6]
        live = {}
        bias_bytes = bias_rows * width * 2

        def bias_send(key, index, device):
            bias_from[2 * index] = bias_held[...].astype(LOW)
            live[key] = copies.send(lambda: bias_from.at[2 * index], lambda: bias_from.at[2 * index + 1], device)
            return engine.transfer(key, bias_bytes)

        def bias_take(key, index):
            live[key].wait_recv()
            bias_held[...] = bias_from[2 * index].astype(F32) + bias_from[2 * index + 1].astype(F32)

        def bias_core():
            return bias_send("core", 0, place.other_core)

        def bias_y():
            bias_take("core", 0)
            return bias_send("y", 1, place.other_y)

        def bias_x():
            bias_take("y", 1)
            return bias_send("x", 2, place.other_x)

        def bias_z():
            bias_take("x", 2)
            bias_from[6] = bias_held[...].astype(LOW)
            live["z"] = [
                copies.send(lambda: bias_from.at[6], lambda k=k: bias_from.at[7 + k], device)
                for k, device in enumerate(place.ahead)
            ]
            return engine.transfer("z", bias_bytes)

        def bias_end():
            value = bias_from[6].astype(F32)
            for k, copy in enumerate(live["z"]):
                copy.wait_recv()
                value = value + bias_from[7 + k].astype(F32)
            bias_out[...] = value

        engine.add([bias_core, bias_y, bias_x, bias_z, bias_end])
        attn_product(2, dot(ent_turned, grad_query_words[all_words:]))
        attn_product(3, dot(ent_turned, grad_query_ents[all_words:]))
        attn_product(4, dot(hidden_turned[...], grad_keys[...]))
        attn_product(5, dot(hidden_turned[...], grad_values[...]))
        quarter = word_half // 2

        def words_sum():
            word_copy.wait_recv()
            sum_hidden(0, word_half, y * word_half)
            engine.clock += 0.5
            live_words["send"] = copies.send(
                lambda: total.at[span((1 - core) * quarter, quarter, LANES)], lambda: word_grad.at[core], place.other_core
            )
            live_words["own"] = copies.local(
                lambda: total.at[span(core * quarter, quarter, LANES)], lambda: word_grad.at[core]
            )
            return engine.transfer("core", quarter * width * 4)

        def words_end():
            live_words["send"].wait_recv()
            live_words["own"].wait()

        engine.add([lambda: word_ready, words_sum, words_end])

        def ent_products():
            proj_rows, pos_rows = rows.shape[1] // n_dp, all_words // n_dp
            proj_pad = padded(proj_rows)
            position = ent_pos[pl.ds(core, 1), :]
            picks = []
            for j in range(all_words // LANES):
                number = lax.broadcasted_iota(jnp.int32, (LANES, ents), 0) + j * LANES
                picks.append(jnp.where(number == position, 1.0, 0.0))
            pick = jnp.concatenate(picks, axis=0)
            here = lax.broadcasted_iota(jnp.int32, (all_words, ents), 1) // ent_half == y
            pick = jnp.where(here, pick, 0.0).astype(LOW)
            grad_ent = total[word_half:]
            grad_ent_low = grad_ent.astype(LOW)
            rest = (grad_ent - grad_ent_low.astype(F32)).astype(LOW)
            pos_grad = dot(pick, jnp.concatenate([grad_ent_low, grad_ent_low], axis=0)) + dot(
                pick, jnp.concatenate([rest, rest], axis=0)
            )
            proj_grad = dot_columns(rows[span(y * ent_half, ent_half, 64)], grad_ent_low)
            ent_grads[:, :, pl.ds(0, proj_rows)] = proj_grad.astype(LOW).reshape(nz, 2, proj_rows, width)
            ent_grads[:, :, pl.ds(proj_pad, pos_rows)] = pos_grad.astype(LOW).reshape(nz, 2, pos_rows, width)
            engine.clock += 1.0

        ent_job = jobs["ent"][0]
        engine.add([lambda: max(engine.clock, ent_ready + 1.0), ent_products] + ent_job.steps)
        engine.drain()
        for copy in table_copies[-4:]:
            copy.wait()
        copies.finish()

    table_block = 256 if n_dp * 2 * ents <= 2048 else 32
    pl.run_scoped(
        backward_phase,
        pltpu.VMEM((tokens, half), LOW),
        pltpu.VMEM((tokens, half), LOW),
        pltpu.VMEM((tokens, half), LOW),
        pltpu.VMEM((tokens, half), LOW),
        pltpu.VMEM((HEADS // 2, tokens, tokens), LOW),
        pltpu.VMEM((4, width, half), LOW),
        pltpu.VMEM((width, half), LOW),
        pltpu.VMEM((width, half), LOW),
        pltpu.VMEM((half, tokens), LOW),
        pltpu.VMEM((tokens, half), LOW),
        pltpu.VMEM((tokens, half), LOW),
        pltpu.VMEM((tokens, half), LOW),
        pltpu.VMEM((tokens, half), LOW),
        pltpu.VMEM((width, tokens), LOW),
        pltpu.VMEM((tokens, width), LOW),
        pltpu.VMEM((table_block, n_dp * 2 * ents), LOW),
        pltpu.VMEM((nz, 2, 6 * row_pad, half), LOW),
        pltpu.VMEM((nz, 2, ent_sum.shape[0], width), LOW),
        pltpu.VMEM((2, table_block, ent_proj.shape[0]), F32),
        pltpu.VMEM((2, table_block, LANES), LOW),
    )
    last_copies = [
        copies.local(lambda: ffn_sum, lambda: ffn_reduced),
        copies.local(lambda: attn_sum, lambda: attn_reduced),
        copies.local(lambda: ent_sum, lambda: ent_reduced),
    ]
    for copy in out_copies:
        copy.wait_recv()
    for copy in last_copies:
        copy.wait()
    copies.finish()


def layer(
    nz, rows_dev, words, ent_hidden, mixed, out_weight, out_bias, gains, shifts, up_weight, up_bias, down_weight, down_bias, word_cots, ent_cots,
    hidden_turned, query_words, query_ents, keys, values, probs, query_weight, key_weight, value_weight, rows, ent_pos, ent_proj, ids,
):
    n_dp = 2 * nz
    width, tokens = hidden_turned.shape
    half = keys.shape[1]
    ents, edim = rows.shape
    all_words = tokens - ents
    part, ff = tokens // 2, up_weight.shape[1]
    ffn_blocks = ffn_plan(n_dp, width, ff)
    ffn_rows, attn_rows = ffn_blocks[-1][0] + ffn_blocks[-1][1], 6 * padded(width // n_dp)
    ent_pad = padded(edim // n_dp) + padded(all_words // n_dp)
    bias_rows = 12 + ff // width
    plan = [("ffn", base, size, order, width) for base, size, order in ffn_blocks]
    attn_size = attn_rows // 3
    plan += [("attn", base, attn_size, "xz", half) for base in range(0, attn_rows, attn_size)]
    plan.append(("ent", 0, ent_pad, "xzy", width))
    scratch = [
        pltpu.VMEM((part, half), LOW),
        pltpu.VMEM((tokens, half), LOW),
        pltpu.VMEM((part, width), F32),
        pltpu.VMEM((part, width), LOW),
        pltpu.VMEM((ffn_rows, width), LOW),
        pltpu.VMEM((2, attn_rows, half), LOW),
        pltpu.VMEM((ent_pad, width), LOW),
        pltpu.VMEM((bias_rows, width), F32),
        pltpu.VMEM((6 + nz, bias_rows, width), LOW),
        pltpu.VMEM((n_dp, 2, ents, edim), LOW),
        pltpu.VMEM((8, half), F32),
        pltpu.VMEM((16, width), F32),
        pltpu.VMEM((nz, 2, ffn_rows, width), LOW),
        pltpu.VMEM((part, half), LOW),
    ]
    remote = 8 + 2 + 1 + 3 + nz + 1 + nz + nz + 2 + 4
    for name, base, size, order, columns in plan:
        job = Job(None, None, base, size, order, columns)
        scratch += job.scratch(nz)
        remote += job.remote_count(nz)
    scratch += copy_semaphores(remote, 40 + 2 * (rows_dev // 32))
    return call(
        functools.partial(layer_kernel, nz, plan),
        [
            ((2, all_words // 4, width), LOW),
            ((2, ents // 4, width), LOW),
            ((2, all_words // 4, width), F32),
            ((ffn_rows, width), LOW),
            ((2, attn_rows, half), LOW),
            ((ent_pad, width), LOW),
            ((bias_rows, width), F32),
            ((rows_dev, edim), F32),
            ((rows_dev, LANES), LOW),
        ],
        [ANY] * 2 + [IN_VMEM, ANY] + [IN_VMEM] * 3 + [ANY, IN_VMEM, ANY, IN_VMEM] + [ANY] * 2 + [ANY] * 9 + [IN_VMEM] * 4,
        [ANY] * 6 + [IN_VMEM, ANY, ANY],
        scratch,
        "layer",
        2,
    )(words, ent_hidden, mixed, out_weight, out_bias, gains, shifts, up_weight, up_bias, down_weight, down_bias, word_cots, ent_cots,
      hidden_turned, query_words, query_ents, keys, values, probs, query_weight, key_weight, value_weight, rows, ent_pos, ent_proj, ids)


def last_kernel(
    n_dp, table_grad, touched, first, second, ffn, attn, ent, bias, words_low, ents_low, words_grad,
    table_out, update, new_second, proj_grad, pos_grad, query_grad, key_grad, value_grad, out_grad, up_grad, down_grad, query_bias, gain_grad, shift_grad, key_bias, value_bias, out_bias, down_bias, up_bias,
    word_out, ent_out, word_grad,
):
    step = pl.program_id(0)
    grad = table_grad[...]
    hit = touched[:, 0:1].astype(F32) > 0.0
    mean_new = beta_one * first[...] + (1.0 - beta_one) * grad
    square_new = beta_two * second[...] + (1.0 - beta_two) * grad * grad
    direction = (
        mean_new
        / (1.0 - beta_one**adam_step)
        / (jnp.sqrt(square_new / (1.0 - beta_two**adam_step)) + adam_eps)
    )
    table_out[...] = grad
    update[...] = jnp.where(hit, direction, 0.0)
    new_second[...] = jnp.where(hit, square_new, second[...])
    width = ffn.shape[1]
    part, down_rows = out_grad.shape[0], down_grad.shape[0]
    pad = padded(part)
    proj_pad = padded(proj_grad.shape[0])
    parts = up_grad.shape[1] // width
    half = attn.shape[2]

    @pl.when(step == 0)
    def _():
        down_grad[...] = ffn[:down_rows].astype(F32)

    @pl.when(step == 1)
    def _():
        for j in range(parts):
            base = down_rows + j * pad
            up_grad[:, j * width : (j + 1) * width] = ffn[base : base + part].astype(F32)

    @pl.when(step == 2)
    def _():
        base = down_rows + parts * pad
        out_grad[...] = ffn[base : base + part].astype(F32)
        proj_grad[...] = ent[: proj_grad.shape[0]].astype(F32)
        pos_grad[...] = ent[proj_pad : proj_pad + pos_grad.shape[0]].astype(F32)
        for side in range(2):
            columns = slice(side * half, (side + 1) * half)
            key_grad[:, columns] = attn[side, 4 * pad : 4 * pad + part].astype(F32)
            value_grad[:, columns] = attn[side, 5 * pad : 5 * pad + part].astype(F32)

    @pl.when(step == 3)
    def _():
        for side in range(2):
            columns = slice(side * half, (side + 1) * half)
            for i in range(4):
                query_grad[i, :, columns] = attn[side, i * pad : i * pad + part].astype(F32)
        dp = lax.axis_index("dp")

        def own_columns(value, size, start):
            lane = lax.broadcasted_iota(jnp.int32, (value.shape[1], size), 0)
            want = lax.broadcasted_iota(jnp.int32, (value.shape[1], size), 1) + start
            pick = jnp.where(lane == want, 1.0, 0.0)
            return jnp.dot(value, pick, precision=lax.Precision.HIGHEST, preferred_element_type=F32)

        own = own_columns(bias[...], part, dp * part)
        query_bias[...] = own[0:4]
        gain_grad[...] = own[7:9]
        shift_grad[...] = own[9:11]
        for vector, i in ((key_bias, 4), (value_bias, 5), (out_bias, 6), (down_bias, 11 + parts)):
            vector[...] = own[i : i + 1].reshape(part)
        up = jnp.concatenate([bias[11 + j : 12 + j] for j in range(parts)], axis=1)
        size = up_bias.shape[0]
        if size % LANES == 0:
            per = width // size
            row = bias[pl.ds(11 + dp // per, 1), :]
            chosen = row[:, :size]
            for i in range(1, per):
                chosen = jnp.where(dp % per == i, row[:, i * size : (i + 1) * size], chosen)
            up_bias[...] = chosen.reshape(size)
        else:
            up_bias[...] = own_columns(up, size, dp * size).reshape(size)

    @pl.when(step == 4)
    def _():
        word_out[...] = words_low[...]
        ent_out[...] = ents_low[...]
        word_grad[...] = words_grad[...]


def last(n_dp, ff, all_words, table_grad, touched, first, second, ffn, attn, ent, bias, words_low, ents_low, words_grad):
    width = ffn.shape[1]
    rows, edim = first.shape
    part = width // n_dp
    block = 256
    blocked = lambda columns: pl.BlockSpec((block, columns), lambda i: (i, 0))
    whole = lambda shape: pl.BlockSpec(shape, lambda i: (0,) * len(shape))
    shapes = [
        (edim // n_dp, width),
        (all_words // n_dp, width),
        (4, part, width),
        (part, width),
        (part, width),
        (part, width),
        (part, ff),
        (ff // n_dp, width),
        (4, part),
        (2, part),
        (2, part),
        (part,),
        (part,),
        (part,),
        (part,),
        (ff // n_dp,),
    ]
    through = [words_low, ents_low, words_grad]
    return pl.pallas_call(
        functools.partial(last_kernel, n_dp),
        grid=(rows // block,),
        out_shape=[jax.ShapeDtypeStruct((rows, edim), F32)] * 3
        + [jax.ShapeDtypeStruct(shape, F32) for shape in shapes]
        + [jax.ShapeDtypeStruct(array.shape, array.dtype) for array in through],
        in_specs=[blocked(edim), blocked(LANES), blocked(edim), blocked(edim)]
        + [whole(array.shape) for array in (ffn, attn, ent, bias)]
        + [whole(array.shape) for array in through],
        out_specs=[blocked(edim)] * 3 + [whole(shape) for shape in shapes] + [whole(array.shape) for array in through],
        compiler_params=pltpu.CompilerParams(vmem_limit_bytes=VMEM_BYTES),
        name="last",
    )(table_grad, touched, first, second, ffn, attn, ent, bias, words_low, ents_low, words_grad)


def on_device(
    word_states,
    segments,
    entity_ids,
    entity_pos,
    ent_table,
    first_moment,
    second_moment,
    ent_proj,
    pos_table,
    query_weight,
    query_bias,
    key_weight,
    key_bias,
    value_weight,
    value_bias,
    out_weight,
    out_bias,
    norm_gain,
    norm_shift,
    up_weight,
    up_bias,
    down_weight,
    down_bias,
    word_cot,
    ent_cot,
):
    n_dp = lax.axis_size("dp")
    nz = n_dp // 2
    width, ff = up_weight.shape
    all_words = segments.shape[1]
    words, word_cots, ent_cots, all_ids, rows = fetch(nz, word_states, word_cot, ent_cot, entity_ids, ent_table)
    ent_hidden, hidden_turned, query_words, query_ents, keys, values, probs, mixed = forward(
        words,
        rows,
        entity_pos,
        segments,
        ent_proj,
        pos_table,
        query_weight,
        query_bias,
        key_weight,
        key_bias,
        value_weight,
        value_bias,
    )
    ents = entity_ids.shape[1]
    word_out, ent_out, word_grad, ffn_sum, attn_sum, ent_sum, bias_sum, table_grad, touched = layer(
        nz, ent_table.shape[0], words, ent_hidden, mixed, out_weight, out_bias, norm_gain, norm_shift, up_weight, up_bias, down_weight, down_bias,
        word_cots, ent_cots, hidden_turned, query_words, query_ents, keys, values, probs, query_weight, key_weight, value_weight,
        rows, entity_pos, ent_proj, all_ids.reshape(-1, ents),
    )
    (table_grad, table_update, new_second, proj_grad, pos_grad, query_grad, key_grad, value_grad, out_grad, up_grad, down_grad,
     query_bias_grad, gain_grad, shift_grad, key_bias_grad, value_bias_grad, out_bias_grad, down_bias_grad, up_bias_grad,
     word_out, ent_out, word_grad,
    ) = last(
        n_dp, ff, all_words, table_grad, touched, first_moment, second_moment, ffn_sum, attn_sum, ent_sum, bias_sum, word_out, ent_out, word_grad
    )
    return (
        word_out,
        ent_out,
        word_grad,
        proj_grad,
        pos_grad,
        query_grad,
        query_bias_grad,
        key_grad,
        key_bias_grad,
        value_grad,
        value_bias_grad,
        out_grad,
        out_bias_grad,
        gain_grad,
        shift_grad,
        up_grad,
        up_bias_grad,
        down_grad,
        down_bias_grad,
        table_grad,
        table_update,
        new_second,
    )


def solution(mesh):
    return jax.shard_map(
        on_device,
        mesh=mesh,
        in_specs=(
            P("dp", "seq", None),
            P("dp", None),
            P("dp", None),
            P("dp", None),
            P(("dp", "seq"), None),
            P(("dp", "seq"), None),
            P(("dp", "seq"), None),
            P(),
            P(),
            P(),
            P(),
            P(),
            P(),
            P(),
            P(),
            P(),
            P(),
            P(),
            P(),
            P(),
            P(),
            P(),
            P(),
            P("dp", "seq", None),
            P("dp", "seq", None),
        ),
        out_specs=(
            P("dp", "seq", None),
            P("dp", "seq", None),
            P("dp", "seq", None),
            P("dp", None),
            P("dp", None),
            P(None, "dp", None),
            P(None, "dp"),
            P("dp", None),
            P("dp"),
            P("dp", None),
            P("dp"),
            P("dp", None),
            P("dp"),
            P(None, "dp"),
            P(None, "dp"),
            P("dp", None),
            P("dp"),
            P("dp", None),
            P("dp"),
            P(("dp", "seq"), None),
            P(("dp", "seq"), None),
            P(("dp", "seq"), None),
        ),
        check_vma=False,
    )
```

```python
import functools
import math

import jax
import jax.numpy as jnp
from jax import lax
from jax.experimental import pallas as pl
from jax.experimental.pallas import tpu as pltpu
from jax.sharding import PartitionSpec as P

HEADS = 12
HEAD = 64
LANES = 128
MESH = pl.DeviceIdType.MESH
LOW = jnp.bfloat16
F32 = jnp.float32
VMEM_BYTES = 125 * 512 * 1024

norm_eps = 1e-05
beta_one = 0.9
beta_two = 0.98
adam_eps = 1e-06
adam_step = 10.0
masked_score = -1e30


def dot(left, right):
    return jnp.dot(left, right, preferred_element_type=F32)


def dot_rows(left, right):
    return lax.dot_general(left, right, (((1,), (1,)), ((), ())), preferred_element_type=F32)


def dot_columns(left, right):
    return lax.dot_general(left, right, (((0,), (0,)), ((), ())), preferred_element_type=F32)


def span(start, size, unit):
    if isinstance(start, int):
        return pl.ds(start, size)
    return pl.ds(pl.multiple_of(start, unit), size)


def padded(rows):
    return -(-rows // 16) * 16


def loop(count, body, carry=0, unroll=1):
    def steps(i, carried):
        for k in range(unroll):
            carried = body(i * unroll + k, carried)
        return carried

    return lax.fori_loop(0, count // unroll, steps, carry)


class Place:
    def __init__(self, nz):
        self.dp, self.seq = lax.axis_index("dp"), lax.axis_index("seq")
        self.z, self.x = self.dp // 2, self.dp % 2
        self.y, self.core = self.seq // 2, self.seq % 2
        self.nz = nz
        self.other_core = (self.dp, self.y * 2 + 1 - self.core)
        self.other_y = (self.dp, (1 - self.y) * 2 + self.core)
        self.diagonal = (self.dp, (1 - self.y) * 2 + 1 - self.core)
        self.other_x = (self.z * 2 + 1 - self.x, self.seq)
        self.ahead = [(((self.z + k) % nz) * 2 + self.x, self.seq) for k in range(1, nz)]

    def z_ahead(self, k):
        return (self.z + k) % self.nz


def meet(partners):
    barrier = pltpu.get_barrier_semaphore()
    for partner in partners:
        pl.semaphore_signal(barrier, inc=1, device_id=partner, device_id_type=MESH)
    pl.semaphore_wait(barrier, len(partners))


class Remote:
    def __init__(self, copies, number, src, dst, device):
        self.copies, self.number, self.src, self.dst, self.device = copies, number, src, dst, device
        self.open = True

    def make(self, landing=False):
        return pltpu.make_async_remote_copy(
            src_ref=self.dst() if landing else self.src(),
            dst_ref=self.dst(),
            send_sem=self.copies.send_sem.at[self.number],
            recv_sem=self.copies.recv_sem.at[self.number],
            device_id=self.device,
            device_id_type=MESH,
        )

    def wait_recv(self):
        self.make(landing=True).wait_recv()

    def wait_send(self):
        if self.open:
            self.make().wait_send()
        self.open = False


class Local:
    def __init__(self, copies, number, src, dst):
        self.copies, self.number, self.src, self.dst = copies, number, src, dst

    def make(self):
        return pltpu.make_async_copy(self.src(), self.dst(), self.copies.local_sem.at[self.number])

    def wait(self):
        self.make().wait()


class Copies:
    def __init__(self, send_sem, recv_sem, local_sem):
        self.send_sem, self.recv_sem, self.local_sem = send_sem, recv_sem, local_sem
        self.local_count = 0
        self.sent = []

    def send(self, src, dst, device):
        copy = Remote(self, len(self.sent), src, dst, device)
        copy.make().start()
        self.sent.append(copy)
        return copy

    def local(self, src, dst):
        copy = Local(self, self.local_count, src, dst)
        self.local_count += 1
        copy.make().start()
        return copy

    def finish(self):
        for copy in self.sent:
            copy.wait_send()


def copy_semaphores(remote, local):
    return [
        pltpu.SemaphoreType.DMA((remote,)),
        pltpu.SemaphoreType.DMA((remote,)),
        pltpu.SemaphoreType.DMA((local,)),
    ]


ANY = pl.BlockSpec(memory_space=pl.ANY)
IN_VMEM = pl.BlockSpec(memory_space=pltpu.VMEM)


def call(kernel, outs, in_specs, out_specs, scratch, name, collective_id=None):
    params = {"vmem_limit_bytes": VMEM_BYTES}
    if collective_id is not None:
        params.update(collective_id=collective_id, has_side_effects=True)
    return pl.pallas_call(
        kernel,
        out_shape=[jax.ShapeDtypeStruct(shape, dtype) for shape, dtype in outs],
        in_specs=in_specs,
        out_specs=out_specs,
        scratch_shapes=scratch,
        compiler_params=pltpu.CompilerParams(**params),
        name=name,
    )


def fetch_kernel(nz, words, word_cot, ent_cot, ids, table, all_words, word_cots, ent_cots, all_ids, rows_out, *scratch):
    table_full, table_low, picked, answers, held, from_core, from_x, from_z, from_y, ids_here = scratch[:10]
    copies = Copies(*scratch[10:])
    place = Place(nz)
    z, x, y, core = place.z, place.x, place.y, place.core
    n_dp = 2 * nz
    word_here, ent_here = words.shape[1], ent_cot.shape[1]
    ents = ids.shape[1]
    dp_others = [((place.dp + k) % n_dp, place.seq) for k in range(1, n_dp)]
    meet([place.other_core, place.other_y, place.diagonal] + dp_others)
    whole_table = copies.local(lambda: table, lambda: table_full)
    ids_here[place.dp] = ids[...]
    id_copies = [copies.send(lambda: ids, lambda: ids_here.at[place.dp], device) for device in dp_others]
    quarter = span(place.seq * word_here, word_here, 128)
    word_copies = [
        copies.send(lambda: words.at[1 - core], lambda: all_words.at[quarter], place.diagonal),
        copies.send(lambda: words.at[core], lambda: all_words.at[quarter], place.other_y),
        copies.send(lambda: words.at[1 - core], lambda: all_words.at[quarter], place.other_core),
        copies.send(lambda: word_cot.at[1 - core], lambda: word_cots.at[span(core * word_here, word_here, 128)], place.other_core),
        copies.send(lambda: ent_cot.at[1 - core], lambda: ent_cots.at[span(core * ent_here, ent_here, 32)], place.other_core),
    ]
    all_words[quarter] = words[core]
    word_cots[span(core * word_here, word_here, 128)] = word_cot[core]
    ent_cots[span(core * ent_here, ent_here, 32)] = ent_cot[core]
    whole_table.wait()
    rows_dev = table.shape[0]

    def narrow(i, _):
        where = span(i * 128, 128, 128)
        table_low[where] = table_full[where].astype(LOW)
        return 0

    loop(rows_dev // 128, narrow)
    for copy in id_copies:
        copy.wait_recv()
    all_ids[...] = ids_here[...]
    base = (place.dp * 4 + place.seq) * rows_dev
    tiles = rows_dev // LANES

    def look_up(zz):
        def group(g, _):
            asked = ids_here[zz * 2 + g // 2, pl.ds(g % 2, 1), :] - base
            column = jnp.transpose(jnp.broadcast_to(asked, (ents, ents)))
            for j in range(tiles):
                number = lax.broadcasted_iota(jnp.int32, (ents, LANES), 1) + j * LANES
                hit = jnp.where(column == number, 1.0, 0.0).astype(LOW)
                picked[span(g * ents, ents, ents), pl.ds(j * LANES, LANES)] = hit
            return 0

        loop(4, group)
        answer = dot(picked[...], table_low[...]).astype(LOW)
        answers[zz] = answer.reshape(2, 2, ents, answer.shape[-1])

    order = [place.z_ahead(k + 1) for k in range(nz)]
    core_copies, x_copies, z_copies = [], [], []

    def core_send(zz):
        return copies.send(lambda: answers.at[zz, :, 1 - core], lambda: from_core.at[zz], place.other_core)

    def after_core(k):
        zz = order[k]
        core_copies[k].wait_recv()
        held[zz] = answers[zz, :, core] + from_core[zz]
        x_copies.append(copies.send(lambda: held.at[zz, 1 - x], lambda: from_x.at[zz], place.other_x))

    def after_x(k):
        zz = order[k]
        x_copies[k].wait_recv()
        held[zz, x] = held[zz, x] + from_x[zz]
        if k < nz - 1:
            z_copies.append(copies.send(lambda: held.at[zz, x], lambda: from_z.at[k], place.ahead[k]))

    for k in range(nz + 2):
        if k < nz:
            look_up(order[k])
            core_copies.append(core_send(order[k]))
        if 0 <= k - 1 < nz:
            after_core(k - 1)
        if 0 <= k - 2:
            after_x(k - 2)
    total = held[z, x]
    for k in range(nz - 1):
        z_copies[k].wait_recv()
        total = total + from_z[k]
    from_y[0] = total
    y_copy = copies.send(lambda: from_y.at[0], lambda: from_y.at[1], place.other_y)
    y_copy.wait_recv()
    rows_out[...] = from_y[0] + from_y[1]
    for copy in word_copies:
        copy.wait_recv()
    copies.finish()


def fetch(nz, words, word_cot, ent_cot, ids, table):
    _, word_here, width = words.shape
    ent_here, ents, (rows_dev, edim) = ent_cot.shape[1], ids.shape[1], table.shape
    n_dp = 2 * nz
    return call(
        functools.partial(fetch_kernel, nz),
        [
            ((4 * word_here, width), LOW),
            ((2 * word_here, width), LOW),
            ((2 * ent_here, width), LOW),
            ((n_dp, 2, ents), jnp.int32),
            ((ents, edim), LOW),
        ],
        [IN_VMEM] * 4 + [ANY],
        [IN_VMEM] * 5,
        [
            pltpu.VMEM((rows_dev, edim), F32),
            pltpu.VMEM((rows_dev, edim), LOW),
            pltpu.VMEM((4 * ents, rows_dev), LOW),
            pltpu.VMEM((nz, 2, 2, ents, edim), LOW),
            pltpu.VMEM((nz, 2, ents, edim), LOW),
            pltpu.VMEM((nz, 2, ents, edim), LOW),
            pltpu.VMEM((nz, ents, edim), LOW),
            pltpu.VMEM((nz - 1, ents, edim), LOW),
            pltpu.VMEM((2, ents, edim), LOW),
            pltpu.VMEM((n_dp, 2, ents), jnp.int32),
        ]
        + copy_semaphores(n_dp + 4 + 3 * nz + 2, 1),
        "fetch",
        1,
    )(words, word_cot, ent_cot, ids, table)


def lane_mask(rows, head):
    lane = lax.broadcasted_iota(jnp.int32, (rows, LANES), 1)
    return (lane >= head * HEAD) & (lane < (head + 1) * HEAD)


def row_of(vector):
    return vector[...].astype(F32).reshape(1, vector.shape[0])


def own_half(vector, y):
    row = row_of(vector)
    half = row.shape[1] // 2
    return jnp.where(y == 0, row[:, :half], row[:, half:])


def as_column(row):
    parts = [
        jnp.transpose(jnp.broadcast_to(row[:, i : i + LANES], (LANES, LANES)))
        for i in range(0, row.shape[1], LANES)
    ]
    return jnp.concatenate(parts, axis=0) if len(parts) > 1 else parts[0]


def forward_kernel(
    words, rows, ent_pos, segments, ent_proj, pos_table, query_weight, query_bias, key_weight, key_bias, value_weight, value_bias,
    ent_hidden, hidden_turned, query_words, query_ents, keys, values, probs, mixed,
    hidden_low, query_here, key_here, value_here, values_turned, mask, local_sem,
):
    y, core = lax.axis_index("seq") // 2, lax.axis_index("seq") % 2
    half = keys.shape[1]
    all_words, ents = words.shape[0], rows.shape[0]
    ent_pos, segments = ent_pos[pl.ds(core, 1), :], segments[pl.ds(core, 1), :]
    tokens = all_words + ents
    columns = span(y * half, half, LANES)
    weight_copies = [
        pltpu.make_async_copy(query_weight.at[:, :, columns], query_here, local_sem.at[0]),
        pltpu.make_async_copy(key_weight.at[:, columns], key_here, local_sem.at[1]),
        pltpu.make_async_copy(value_weight.at[:, columns], value_here, local_sem.at[2]),
    ]
    for copy in weight_copies:
        copy.start()
    position = as_column(ent_pos)
    picks = []
    for j in range(all_words // LANES):
        number = lax.broadcasted_iota(jnp.int32, (ents, LANES), 1) + j * LANES
        picks.append(jnp.where(position == number, 1.0, 0.0))
    pick = jnp.concatenate(picks, axis=1)
    word_seg = segments.astype(F32)
    ent_seg = jnp.sum(pick * word_seg, axis=1, keepdims=True)
    ent_hidden[...] = dot(rows[...], ent_proj[...]) + dot(pick.astype(LOW), pos_table[...])
    hidden_low[:all_words] = words[...]
    hidden_low[all_words:] = ent_hidden[...].astype(LOW)
    ent_row = jnp.transpose(jnp.broadcast_to(ent_seg, (ents, LANES)))[:1]
    seg_row = jnp.concatenate([word_seg, ent_row], axis=1)
    seg_column = jnp.concatenate([as_column(word_seg), jnp.broadcast_to(ent_seg, (ents, LANES))], axis=0)
    for j in range(tokens // LANES):
        here = slice(j * LANES, (j + 1) * LANES)
        mask[:, here] = jnp.where(seg_column == seg_row[:, here], 0.0, masked_score)

    query_b = query_bias[:, columns].astype(F32)
    for copy in weight_copies:
        copy.wait()
    word_low, ent_low = hidden_low[:all_words], hidden_low[all_words:]
    query_words[:all_words] = (dot(word_low, query_here[0]) + query_b[0:1]).astype(LOW)
    query_ents[:all_words] = (dot(word_low, query_here[1]) + query_b[1:2]).astype(LOW)
    query_words[all_words:] = (dot(ent_low, query_here[2]) + query_b[2:3]).astype(LOW)
    query_ents[all_words:] = (dot(ent_low, query_here[3]) + query_b[3:4]).astype(LOW)
    keys[...] = (dot(hidden_low[...], key_here[...]) + own_half(key_bias, y)).astype(LOW)
    value = dot(hidden_low[...], value_here[...]) + own_half(value_bias, y)
    values[...] = value.astype(LOW)
    values_turned[...] = jnp.transpose(value).astype(LOW)
    for i in range(words.shape[1] // LANES):
        here = slice(i * LANES, (i + 1) * LANES)
        hidden_turned[here, :] = jnp.transpose(hidden_low[:, here].astype(F32)).astype(LOW)
    scale = 1.0 / math.sqrt(HEAD)
    tiles = tokens // LANES

    def pair_step(pair, _):
        lanes = span(pair * LANES, LANES, LANES)
        key, turned = keys[:, lanes], values_turned[lanes, :]
        row = lax.broadcasted_iota(jnp.int32, (LANES, tokens), 0)
        own_key, own_turned = [], []
        for head in range(2):
            own_key.append(jnp.where(lane_mask(tokens, head), key, jnp.zeros_like(key)))
            own_rows = (row >= head * HEAD) & (row < (head + 1) * HEAD)
            own_turned.append(jnp.where(own_rows, turned, jnp.zeros_like(turned)))
        for i in range(tiles):
            place = slice(i * LANES, (i + 1) * LANES)
            query_w, query_e = query_words[place, lanes], query_ents[place, lanes]
            total = None
            for head in range(2):
                raw = jnp.concatenate(
                    [dot_rows(own_key[head][:all_words], query_w), dot_rows(own_key[head][all_words:], query_e)], axis=0
                )
                score = raw * scale + mask[:, place]
                weight = jnp.exp(score - jnp.max(score, axis=0, keepdims=True))
                prob = (weight * (1.0 / jnp.sum(weight, axis=0, keepdims=True))).astype(LOW)
                probs[pair * 2 + head, :, place] = prob
                part = dot(own_turned[head], prob)
                total = part if total is None else total + part
            mixed[place, lanes] = jnp.transpose(total).astype(LOW)
        return 0

    loop(half // LANES, pair_step)


def forward(words, rows, ent_pos, segments, ent_proj, pos_table, query_weight, query_bias, key_weight, key_bias, value_weight, value_bias):
    all_words, width = words.shape
    ents = rows.shape[0]
    tokens, half = all_words + ents, width // 2
    return call(
        forward_kernel,
        [
            ((ents, width), F32),
            ((width, tokens), LOW),
            ((tokens, half), LOW),
            ((tokens, half), LOW),
            ((tokens, half), LOW),
            ((tokens, half), LOW),
            ((HEADS // 2, tokens, tokens), LOW),
            ((tokens, half), LOW),
        ],
        [IN_VMEM] * 6 + [ANY, IN_VMEM, ANY, IN_VMEM, ANY, IN_VMEM],
        [IN_VMEM] * 8,
        [
            pltpu.VMEM((tokens, width), LOW),
            pltpu.VMEM((4, width, half), LOW),
            pltpu.VMEM((width, half), LOW),
            pltpu.VMEM((width, half), LOW),
            pltpu.VMEM((half, tokens), LOW),
            pltpu.VMEM((tokens, tokens), F32),
            pltpu.SemaphoreType.DMA((3,)),
        ],
        "forward",
    )(words, rows, ent_pos, segments, ent_proj, pos_table, query_weight, query_bias, key_weight, key_bias, value_weight, value_bias)


class Engine:
    RATES = {"core": 200e3, "x": 60e3, "y": 60e3, "z": 15e3}
    LATENCY = 3.0

    def __init__(self):
        self.clock, self.free, self.streams = 0.0, {}, []

    def transfer(self, link, size):
        start = max(self.clock, self.free.get(link, 0.0))
        self.free[link] = start + size / self.RATES[link]
        return self.free[link] + self.LATENCY

    def add(self, steps):
        self.streams.append([self.clock, list(steps)])
        self.poll()

    def run(self, stream):
        self.clock = max(self.clock, stream[0])
        ready = stream[1].pop(0)()
        stream[0] = self.clock if ready is None else ready

    def next(self):
        live = [stream for stream in self.streams if stream[1]]
        return min(live, key=lambda stream: stream[0]) if live else None

    def poll(self):
        while (stream := self.next()) is not None and stream[0] <= self.clock:
            self.run(stream)

    def work(self, time):
        self.clock += time
        self.poll()

    def drain(self):
        while (stream := self.next()) is not None:
            self.run(stream)


def blocks_of(rows):
    for size in (96, 64, 48, 32):
        if rows % size == 0:
            return size
    return 16


def add_blocks(engine, target, parts, leading, rows, columns):
    size = blocks_of(rows)
    count = rows // size

    def block(i, _):
        lead, row = i // count, (i % count) * size
        where = span(row, size, 16)
        if len(parts) == 2:
            value = parts[0](lead, where) + parts[1](lead, where)
        else:
            value = parts[0](lead, where).astype(F32)
            for part in parts[1:]:
                value = value + part(lead, where).astype(F32)
            value = value.astype(LOW)
        target(lead, where, value)
        return 0

    loop(leading * count, block)
    engine.clock += 0.3 + leading * rows * columns / 1e6


class Job:
    def __init__(self, grads, reduced, base, size, order, columns):
        self.grads, self.reduced, self.base, self.size, self.order, self.columns = grads, reduced, base, size, order, columns
        self.half = size // 2
        self.part = size // 4 if order == "yxz" else size // 2

    def scratch(self, nz):
        shapes = [(nz, 2, self.half, self.columns)]
        if self.order == "yxz":
            shapes.append((nz, 2, self.part, self.columns))
        elif self.order == "xzy":
            shapes.append((2, self.part, self.columns))
        shapes += [(nz, self.part, self.columns), (nz - 1, self.part, self.columns)]
        return [pltpu.VMEM(shape, LOW) for shape in shapes]

    def remote_count(self, nz):
        return 1 + (1 if self.order != "xz" else 0) + 1 + (nz - 1) + 1 + 1

    def prepare(self, engine, place, copies, scratch):
        nz, z, x, y, core = place.nz, place.z, place.x, place.y, place.core
        base, half, part, order, columns = self.base, self.half, self.part, self.order, self.columns
        held = self.grads.at[:, :, span(base + core * half, half, 16)]
        from_core = scratch[0]
        from_y = scratch[1] if order != "xz" else None
        from_x, from_z = scratch[-2:]
        live = {}
        row_bytes = 2 * columns
        theirs = span(base + (1 - core) * half, half, 16)
        mine = span(base + core * half, half, 16)
        own_rows = span(y * part, part, 16) if order == "yxz" else pl.ds(0, part)
        final_rows = span(base + core * half + (y * part if order == "yxz" else 0), part, 16)

        def start():
            live["core"] = copies.send(lambda: self.grads.at[:, :, theirs], lambda: from_core, place.other_core)
            return engine.transfer("core", 2 * nz * half * row_bytes)

        def send_x():
            live["x"] = copies.send(lambda: held.at[:, 1 - x, own_rows], lambda: from_x, place.other_x)
            return engine.transfer("x", nz * part * row_bytes)

        def after_core():
            live["core"].wait_recv()

            def put(i, where, value):
                held[i // 2, i % 2, where] = value

            add_blocks(
                engine,
                put,
                [lambda i, where: held[i // 2, i % 2, where], lambda i, where: from_core[i // 2, i % 2, where]],
                2 * nz,
                half,
                columns,
            )
            if order == "yxz":
                live["y"] = copies.send(
                    lambda: held.at[:, :, span((1 - y) * part, part, 16)], lambda: from_y, place.other_y
                )
                return engine.transfer("y", 2 * nz * part * row_bytes)
            return send_x()

        def shifted(where):
            return span(y * part + where.start, where.size, 16) if order == "yxz" else where

        def after_y():
            live["y"].wait_recv()

            def put(i, where, value):
                held[i // 2, i % 2, shifted(where)] = value

            add_blocks(
                engine,
                put,
                [lambda i, where: held[i // 2, i % 2, shifted(where)], lambda i, where: from_y[i // 2, i % 2, where]],
                2 * nz,
                part,
                columns,
            )
            return send_x()

        def send_z(k):
            return copies.send(
                lambda: held.at[place.z_ahead(k + 1), x, own_rows], lambda: from_z.at[k], place.ahead[k]
            )

        def after_x():
            live["x"].wait_recv()

            def put(i, where, value):
                held[i, x, shifted(where)] = value

            add_blocks(
                engine,
                put,
                [lambda i, where: held[i, x, shifted(where)], lambda i, where: from_x[i, where]],
                nz,
                part,
                columns,
            )
            live["z"] = [send_z(k) for k in range(nz - 1)]
            return engine.transfer("z", part * row_bytes)

        def after_z():
            for copy in live["z"]:
                copy.wait_recv()

            def put(i, where, value):
                if order == "yxz":
                    self.reduced[span(base + core * half + y * part + where.start, where.size, 16)] = value
                elif order == "xz":
                    self.reduced[y, span(base + core * half + where.start, where.size, 16)] = value
                else:
                    from_y[0, where] = value

            def parts(k):
                return lambda i, where: from_z[k, where]

            add_blocks(
                engine,
                put,
                [lambda i, where: held[z, x, shifted(where)]] + [parts(k) for k in range(nz - 1)],
                1,
                part,
                columns,
            )
            if order == "xzy":
                live["y2"] = copies.send(lambda: from_y.at[0], lambda: from_y.at[1], place.other_y)
            else:
                view = lambda: self.reduced.at[final_rows] if order == "yxz" else self.reduced.at[y, final_rows]
                live["y2"] = copies.send(view, view, place.other_y)
            return engine.transfer("y", part * row_bytes)

        def after_gather():
            live["y2"].wait_recv()
            if order == "xzy":

                def put(i, where, value):
                    self.reduced[span(base + core * half + where.start, where.size, 16)] = value

                add_blocks(
                    engine, put, [lambda i, where: from_y[0, where], lambda i, where: from_y[1, where]], 1, part, columns
                )
            view = lambda: self.reduced.at[:, mine] if order == "xz" else self.reduced.at[mine]
            live["core2"] = copies.send(view, view, place.other_core)
            return engine.transfer("core", 2 * half * row_bytes)

        def end():
            live["core2"].wait_recv()

        middle_steps = [after_core, after_y, after_x] if order == "yxz" else [after_core, after_x]
        self.steps = [start] + middle_steps + [after_z, after_gather, end]


def lane_mean(value):
    return jnp.mean(value, axis=-1, keepdims=True)


def column_sum(value):
    return jnp.sum(value, axis=0, keepdims=True)


ROW_BLOCK = 32


def ffn_plan(n_dp, width, ff):
    down_rows, row_pad = ff // n_dp, padded(width // n_dp)
    size = 128 if down_rows % 128 == 0 else 32
    order = "yxz" if size % 64 == 0 else "xzy"
    plan = [(base, size, order) for base in range(0, down_rows, size)]
    base = down_rows
    for pair in range(ff // width // 2):
        order = "yxz" if pair % 2 == 0 and row_pad % 32 == 0 else "xzy"
        plan.append((base, 2 * row_pad, order))
        base += 2 * row_pad
    plan.append((base, row_pad, "xzy"))
    return plan


def layer_kernel(
    nz, plan, words, ent_hidden, mixed, out_weight, out_bias, gains, shifts, up_weight, up_bias, down_weight, down_bias, word_cots, ent_cots,
    hidden_turned_in, query_words_in, query_ents_in, keys_in, values_in, probs_in, query_weight, key_weight, value_weight, rows, ent_pos, ent_proj, ids,
    word_out, ent_out, word_grad, ffn_reduced, attn_reduced, ent_reduced, bias_out, table_grad, touched, *scratch,
):
    (from_y_mixed, grad_mixed, grad_one, given, ffn_sum, attn_sum, ent_sum, bias_held, bias_from, all_rows, bias_heads, bias_middle,
     ffn_grads, grad_mixed_here, row_parts) = scratch[:15]
    copies = Copies(*scratch[-3:])
    engine = Engine()
    place = Place(nz)
    z, x, y, core = place.z, place.x, place.y, place.core
    n_dp = 2 * nz
    tokens, half = mixed.shape
    width = 2 * half
    ents = ent_hidden.shape[0]
    all_words = tokens - ents
    word_half, ent_half = all_words // 2, ents // 2
    part_tokens = tokens // 2
    ff = up_weight.shape[1]
    parts = ff // width
    row_part, row_pad, down_rows = width // n_dp, padded(width // n_dp), ff // n_dp
    meet([place.other_core, place.other_y, place.other_x] + place.ahead)

    jobs = {"ffn": [], "attn": [], "ent": []}

    def make_jobs(names, sources):
        at = 15
        for name, number, base, size, order, columns in plan:
            grads, reduced = sources.get(name, (None, None))
            if name == "attn" and grads is not None:
                grads, reduced = grads.at[number], reduced.at[number]
            job = Job(grads, reduced, base, size, order, columns)
            used = len(job.scratch(nz))
            if name in names:
                job.prepare(engine, place, copies, scratch[at : at + used])
                jobs[name].append(job)
            at += used

    make_jobs(["ffn"], {"ffn": (ffn_grads, ffn_sum)})

    def token_rows(side):
        return span(side * word_half, word_half, LANES), span(all_words + side * ent_half, ent_half, 64)

    mine, theirs = token_rows(y), token_rows(1 - y)
    own_columns, other_columns = span(y * half, half, LANES), span((1 - y) * half, half, LANES)
    word_part, ent_part = pl.ds(0, word_half), pl.ds(word_half, ent_half)
    mixed_copies = [
        copies.send(lambda: mixed.at[theirs[0]], lambda: from_y_mixed.at[word_part], place.other_y),
        copies.send(lambda: mixed.at[theirs[1]], lambda: from_y_mixed.at[ent_part], place.other_y),
    ]
    engine.transfer("y", part_tokens * half * 2)
    out_copies, mixed_back = [], []

    def forward_phase(
        out_here, up_here, down_here, word_here, ent_here, mixed_full, work, normed_low, normal_one, inverse_one,
        act, slope, output, grad_two, grad_two_low, grad_one_low, normed_turned,
    ):
        cot, grad_up_low = output, slope
        weight_copies = [
            copies.local(lambda: out_weight, lambda: out_here),
            copies.local(lambda: words.at[mine[0]], lambda: word_here),
            copies.local(lambda: ent_hidden.at[span(y * ent_half, ent_half, 64)], lambda: ent_here),
            copies.local(lambda: up_weight, lambda: up_here),
            copies.local(lambda: down_weight, lambda: down_here),
            copies.local(lambda: word_cots, lambda: cot.at[word_part]),
            copies.local(lambda: ent_cots, lambda: cot.at[ent_part]),
        ]
        gain, shift = gains[...].astype(F32), shifts[...].astype(F32)
        out_b, down_b, up_b = row_of(out_bias), row_of(down_bias), row_of(up_bias)
        mixed_full[word_part, own_columns] = mixed[mine[0]]
        mixed_full[ent_part, own_columns] = mixed[mine[1]]
        for copy in weight_copies[:3]:
            copy.wait()
        for copy in mixed_copies:
            copy.wait_recv()
        mixed_full[:, other_columns] = from_y_mixed[...]
        work[...] = dot(mixed_full[...], out_here[...])

        def norm_one(residual):
            def step(i, _):
                rows = span(residual[1] + i * ROW_BLOCK, ROW_BLOCK, ROW_BLOCK)
                value = residual[0][span(i * ROW_BLOCK, ROW_BLOCK, ROW_BLOCK)].astype(F32) + (work[rows] + out_b)
                center = value - lane_mean(value)
                inverse = lax.rsqrt(lane_mean(center * center) + norm_eps)
                normal = center * inverse
                result = normal * gain[0:1] + shift[0:1]
                normal_one[rows] = normal
                inverse_one[rows] = jnp.broadcast_to(inverse, (ROW_BLOCK, LANES))
                normed_low[rows] = result.astype(LOW)
                return 0

            return step

        loop(word_half // ROW_BLOCK, norm_one((word_here, 0)), 0, 2)
        loop(ent_half // ROW_BLOCK, norm_one((ent_here, word_half)), 0, 2)
        weight_copies[3].wait()
        for j in range(parts):
            columns = slice(j * width, (j + 1) * width)
            work[...] = dot(normed_low[...], up_here[:, columns]) + up_b[:, columns]

            def gelu(i, _):
                rows = span(i * ROW_BLOCK, ROW_BLOCK, ROW_BLOCK)
                value = work[rows]
                below = 0.5 * (1.0 + lax.erf(value * (1.0 / math.sqrt(2.0))))
                density = jnp.exp(-0.5 * value * value) * (1.0 / math.sqrt(2.0 * math.pi))
                act[rows, columns] = (value * below).astype(LOW)
                slope[rows, columns] = (below + value * density).astype(LOW)
                return 0

            loop(part_tokens // ROW_BLOCK, gelu)
        normed_turned[...] = jnp.transpose(normed_low[...].astype(F32)).astype(LOW)
        for copy in weight_copies[4:]:
            copy.wait()
        work[...] = dot(act[...], down_here[...])

        def norm_two(i, sums):
            rows = span(i * ROW_BLOCK, ROW_BLOCK, ROW_BLOCK)
            value = (normal_one[rows] * gain[0:1] + shift[0:1]) + (work[rows] + down_b)
            center = value - lane_mean(value)
            inverse = lax.rsqrt(lane_mean(center * center) + norm_eps)
            normal = center * inverse
            cotangent = cot[rows].astype(F32)
            output[rows] = (normal * gain[1:2] + shift[1:2]).astype(LOW)
            scaled = cotangent * gain[1:2]
            result = inverse * (scaled - lane_mean(scaled) - normal * lane_mean(scaled * normal))
            grad_two[rows] = result
            grad_two_low[rows] = result.astype(LOW)
            return (
                sums[0] + column_sum(cotangent * normal),
                sums[1] + column_sum(cotangent),
                sums[2] + column_sum(result),
            )

        nothing = jnp.zeros((1, width), F32)
        gain_two, shift_two, down_sum = loop(part_tokens // ROW_BLOCK, norm_two, (nothing, nothing, nothing), 2)
        quarter, ent_quarter = word_half // 2, ent_half // 2
        out_copies.extend([
            copies.send(
                lambda: output.at[span((1 - core) * quarter, quarter, LANES)], lambda: word_out.at[core], place.other_core
            ),
            copies.send(
                lambda: output.at[span(word_half + (1 - core) * ent_quarter, ent_quarter, 32)],
                lambda: ent_out.at[core],
                place.other_core,
            ),
        ])
        out_local = [
            copies.local(lambda: output.at[span(core * quarter, quarter, LANES)], lambda: word_out.at[core]),
            copies.local(
                lambda: output.at[span(word_half + core * ent_quarter, ent_quarter, 32)], lambda: ent_out.at[core]
            ),
        ]
        engine.clock = 0.0
        engine.free = {}
        def put(base, value):
            ffn_grads[:, :, pl.ds(base, row_part)] = value.astype(LOW).reshape(nz, 2, row_part, width)

        def down_block(job):
            if down_rows % 128:
                per = width // down_rows
                for j in range(parts):
                    value = dot_columns(act[:, j * width : (j + 1) * width], grad_two_low[...])
                    value = value.reshape(per, down_rows, width)[:, job.base : job.base + job.size].astype(LOW)
                    for d in range(per):
                        slab = j * per + d
                        ffn_grads[slab // 2, slab % 2, pl.ds(job.base, job.size)] = value[d]
            else:
                for slab in range(n_dp):
                    start = slab * down_rows + job.base
                    value = dot_columns(act[:, start : start + job.size], grad_two_low[...])
                    ffn_grads[slab // 2, slab % 2, pl.ds(job.base, job.size)] = value.astype(LOW)
            engine.work(1.3)
            engine.add(job.steps)

        up_sums = []

        def grad_up(j):
            columns = slice(j * width, (j + 1) * width)
            work[...] = dot_rows(grad_two_low[...], down_here[columns, :])

            def grad_gelu(i, total_row):
                rows = span(i * ROW_BLOCK, ROW_BLOCK, ROW_BLOCK)
                value = work[rows] * slope[rows, columns].astype(F32)
                grad_up_low[rows, columns] = value.astype(LOW)
                return total_row + column_sum(value)

            up_sums.append(loop(part_tokens // ROW_BLOCK, grad_gelu, nothing, 2))
            engine.work(1.6)
            put(down_rows + j * row_pad, dot(normed_turned[...], grad_up_low[:, columns]))
            engine.work(0.9)

        downs = [job for job in jobs["ffn"] if job.base < down_rows]
        ups = [job for job in jobs["ffn"] if down_rows <= job.base][:-1]
        for job in downs:
            down_block(job)
        for j in range(parts):
            grad_up(j)
            if j % 2 == 1:
                engine.add(ups[j // 2].steps)
        work[...] = dot_rows(grad_up_low[...], up_here[...])
        engine.work(2.0)

        def back_one(i, sums):
            rows = span(i * ROW_BLOCK, ROW_BLOCK, ROW_BLOCK)
            upper = grad_two[rows] + work[rows]
            normal = normal_one[rows]
            inverse = inverse_one[rows, 0:1]
            scaled = upper * gain[0:1]
            result = inverse * (scaled - lane_mean(scaled) - normal * lane_mean(scaled * normal))
            grad_one[rows] = result
            grad_one_low[rows] = result.astype(LOW)
            return (
                sums[0] + column_sum(upper * normal),
                sums[1] + column_sum(upper),
                sums[2] + column_sum(result),
            )

        gain_one, shift_one, out_sum = loop(part_tokens // ROW_BLOCK, back_one, (nothing, nothing, nothing), 2)
        engine.work(1.0)
        grad_mixed_here[...] = dot_rows(grad_one_low[...], out_here[other_columns, :]).astype(LOW)
        mixed_back.extend([
            copies.send(lambda: grad_mixed_here.at[word_part], lambda: grad_mixed.at[mine[0]], place.other_y),
            copies.send(lambda: grad_mixed_here.at[ent_part], lambda: grad_mixed.at[mine[1]], place.other_y),
        ])
        engine.transfer("y", part_tokens * half * 2)
        own = dot_rows(grad_one_low[...], out_here[own_columns, :]).astype(LOW)
        grad_mixed[mine[0]] = own[:word_half]
        grad_mixed[mine[1]] = own[word_half:]
        engine.work(1.0)
        put(down_rows + parts * row_pad, dot_columns(mixed_full[...], grad_one_low[...]))
        engine.work(0.8)
        engine.add(jobs["ffn"][-1].steps)
        bias_rows = [out_sum, gain_one, gain_two, shift_one, shift_two] + up_sums + [down_sum]
        for i, row in enumerate(bias_rows):
            bias_middle[i : i + 1] = row
        for copy in out_copies:
            copy.wait_send()
        for copy in out_local:
            copy.wait()

    tall = lambda columns, dtype: pltpu.VMEM((part_tokens, columns), dtype)
    pl.run_scoped(
        forward_phase,
        pltpu.VMEM((width, width), LOW),
        pltpu.VMEM((width, ff), LOW),
        pltpu.VMEM((ff, width), LOW),
        pltpu.VMEM((word_half, width), LOW),
        pltpu.VMEM((ent_half, width), F32),
        tall(width, LOW),
        tall(width, F32),
        tall(width, LOW),
        tall(width, F32),
        tall(LANES, F32),
        tall(ff, LOW),
        tall(ff, LOW),
        tall(width, LOW),
        tall(width, F32),
        tall(width, LOW),
        tall(width, LOW),
        pltpu.VMEM((width, part_tokens), LOW),
    )
    live_words = {}

    def backward_phase(
        query_words, query_ents, keys, values, probs, query_here, key_here, value_here, keys_turned,
        grad_query_words, grad_query_ents, grad_keys, grad_values, hidden_turned, grad_hidden, hits, attn_grads, ent_grads, table_here, touched_here,
    ):
        total = grad_one
        make_jobs(["attn", "ent"], {"attn": (attn_grads, attn_sum), "ent": (ent_grads, ent_sum)})
        columns = span(y * half, half, LANES)
        copies_in = [
            copies.local(lambda: values_in, lambda: values),
            copies.local(lambda: keys_in, lambda: keys),
            copies.local(lambda: query_words_in, lambda: query_words),
            copies.local(lambda: query_ents_in, lambda: query_ents),
        ]
        prob_copies = []
        for head in range(probs.shape[0]):
            prob_copies.append(
                copies.local(lambda head=head: probs_in.at[head], lambda head=head: probs.at[head])
            )
        hidden_copy = copies.local(lambda: hidden_turned_in, lambda: hidden_turned)
        weight_copies = [
            copies.local(lambda: query_weight.at[:, :, columns], lambda: query_here),
            copies.local(lambda: key_weight.at[:, columns], lambda: key_here),
            copies.local(lambda: value_weight.at[:, columns], lambda: value_here),
        ]
        for copy in copies_in:
            copy.wait()
        for i in range(half // LANES):
            lanes = slice(i * LANES, (i + 1) * LANES)
            keys_turned[lanes, :] = jnp.transpose(keys[:, lanes].astype(F32)).astype(LOW)
        for copy in mixed_back:
            copy.wait_recv()
        engine.work(2.0)
        scale = 1.0 / math.sqrt(HEAD)
        tiles = tokens // LANES

        def pair_products(pair):
            lanes = slice(pair * LANES, (pair + 1) * LANES)
            word_turned, ent_turned = hidden_turned[:, :all_words], hidden_turned[:, all_words:]
            products = [
                dot(word_turned, grad_query_words[:all_words, lanes]),
                dot(word_turned, grad_query_ents[:all_words, lanes]),
                dot(ent_turned, grad_query_words[all_words:, lanes]),
                dot(ent_turned, grad_query_ents[all_words:, lanes]),
                dot(hidden_turned[...], grad_keys[:, lanes]),
                dot(hidden_turned[...], grad_values[:, lanes]),
            ]
            for i, value in enumerate(products):
                attn_grads[pair, :, :, pl.ds(i * row_pad, row_part)] = value.astype(LOW).reshape(nz, 2, row_part, LANES)
            engine.work(1.5)
            engine.add(jobs["attn"][pair].steps)

        for pair in range(half // LANES):
            lanes = slice(pair * LANES, (pair + 1) * LANES)
            grad_query_w = jnp.zeros((LANES, tokens), F32)
            grad_query_e = jnp.zeros((LANES, tokens), F32)
            grad_key_w = jnp.zeros((all_words, LANES), F32)
            grad_key_e = jnp.zeros((ents, LANES), F32)
            grad_value = jnp.zeros((tokens, LANES), F32)
            for head in range(2):
                own = lane_mask(tokens, head)
                value = values[:, lanes]
                own_value = jnp.where(own, value, jnp.zeros_like(value))
                prob_copies[pair * 2 + head].wait()

                given_heads = grad_mixed[:, lanes]
                grad_scores = probs.at[pair * 2 + head]
                grad_value += dot(grad_scores[...], jnp.where(own, given_heads, jnp.zeros_like(given_heads)))
                for i in range(tiles):
                    where = slice(i * LANES, (i + 1) * LANES)
                    grad_prob = dot_rows(own_value, grad_mixed[where, lanes])
                    prob = grad_scores[:, where].astype(F32)
                    both = prob * grad_prob
                    grad_scores[:, where] = (both - prob * jnp.sum(both, axis=0, keepdims=True)).astype(LOW)
                engine.work(1.7)
                query_w, query_e = query_words[:, lanes], query_ents[:, lanes]
                grad_key_w += dot(grad_scores[:all_words], jnp.where(own, query_w, jnp.zeros_like(query_w)))
                grad_key_e += dot(grad_scores[all_words:], jnp.where(own, query_e, jnp.zeros_like(query_e)))
                row = lax.broadcasted_iota(jnp.int32, (LANES, tokens), 0)
                own_rows = (row >= head * HEAD) & (row < (head + 1) * HEAD)
                turned = keys_turned[lanes, :]
                turned = jnp.where(own_rows, turned, jnp.zeros_like(turned))
                grad_query_w += dot(turned[:, :all_words], grad_scores[:all_words])
                grad_query_e += dot(turned[:, all_words:], grad_scores[all_words:])
                engine.work(1.7)
            grad_query_w = jnp.transpose(grad_query_w) * scale
            grad_query_e = jnp.transpose(grad_query_e) * scale
            grad_key_w, grad_key_e = grad_key_w * scale, grad_key_e * scale
            sums = [
                column_sum(grad_query_w[:all_words]),
                column_sum(grad_query_e[:all_words]),
                column_sum(grad_query_w[all_words:]),
                column_sum(grad_query_e[all_words:]),
                column_sum(grad_key_w) + column_sum(grad_key_e),
                column_sum(grad_value),
            ]
            for i, sum_row in enumerate(sums):
                bias_heads[i : i + 1, lanes] = sum_row
            grad_query_words[:, lanes] = grad_query_w.astype(LOW)
            grad_query_ents[:, lanes] = grad_query_e.astype(LOW)
            grad_keys[:all_words, lanes] = grad_key_w.astype(LOW)
            grad_keys[all_words:, lanes] = grad_key_e.astype(LOW)
            grad_values[:, lanes] = grad_value.astype(LOW)
            engine.work(0.5)
            if pair == 0:
                hidden_copy.wait()
            if pair + 1 < half // LANES:
                pair_products(pair)

        for copy in weight_copies:
            copy.wait()
        ent_rows, word_rows = slice(all_words, tokens), slice(0, all_words)

        def hidden_part(here, first, second):
            grad_hidden[here] = (
                dot_rows(grad_keys[here], key_here[...])
                + dot_rows(grad_values[here], value_here[...])
                + dot_rows(grad_query_words[here], query_here[first])
                + dot_rows(grad_query_ents[here], query_here[second])
            ).astype(LOW)

        hidden_part(ent_rows, 2, 3)
        own_ents = lax.broadcasted_iota(jnp.int32, (ents, width), 0) // ent_half == y
        twice = jnp.concatenate([grad_one[word_half:], grad_one[word_half:]], axis=0)
        ent_sum_part = grad_hidden[ent_rows].astype(F32) + jnp.where(own_ents, twice, 0.0)
        row_parts[0] = dot_rows(ent_sum_part.astype(LOW), ent_proj[...]).astype(LOW)
        rows_copy = copies.send(lambda: row_parts.at[0], lambda: row_parts.at[1], place.other_y)
        row_bytes = ents * ent_proj.shape[0] * 2
        rows_ready = engine.transfer("y", row_bytes)
        engine.work(0.7)
        pair_products(half // LANES - 1)
        ent_copy = copies.send(lambda: grad_hidden.at[theirs[1]], lambda: given.at[ent_part], place.other_y)
        ent_ready = engine.transfer("y", ent_half * width * 2)

        live_rows = {}

        def sum_hidden(start, count, own_start):
            def block(i, _):
                where = span(start + i * 32, 32, 32)
                own = span(own_start + i * 32, 32, 32)
                total[where] = grad_one[where] + (grad_hidden[own].astype(F32) + given[where].astype(F32))
                return 0

            loop(count // 32, block)

        def rows_z():
            rows_copy.wait_recv()
            all_rows[place.dp, core] = row_parts[0] + row_parts[1]
            view = lambda: all_rows.at[place.dp, core]
            live_rows["z"] = [copies.send(view, view, device) for device in place.ahead]
            return engine.transfer("z", row_bytes)

        def rows_x():
            for copy in live_rows["z"]:
                copy.wait_recv()
            live_rows["x"] = []
            for k in range(nz):
                view = lambda k=k: all_rows.at[place.z_ahead(k) * 2 + x, core]
                live_rows["x"].append(copies.send(view, view, place.other_x))
            return engine.transfer("x", nz * row_bytes)

        def rows_core():
            for copy in live_rows["x"]:
                copy.wait_recv()
            view = lambda: all_rows.at[:, core]
            live_rows["core"] = copies.send(view, view, place.other_core)
            return engine.transfer("core", n_dp * row_bytes)

        rows_dev = table_grad.shape[0]
        table_copies = []
        base_row = (place.dp * 4 + place.seq) * rows_dev

        def table_part(i):
            def step():
                if i == 0:
                    live_rows["core"].wait_recv()
                groups = ids.shape[0]
                number = lax.broadcasted_iota(jnp.int32, (table_block, ents), 0) + (base_row + i * table_block)
                count = jnp.zeros((table_block, ents), F32)
                for group in range(groups):
                    hit = jnp.where(ids[group : group + 1, :] == number, 1.0, 0.0)
                    count = count + hit
                    hits[:, group * ents : (group + 1) * ents] = hit.astype(LOW)
                here = pl.ds(i * table_block, table_block)
                for copy in table_copies[2 * i - 4 : 2 * i - 2] if i >= 2 else []:
                    copy.wait()
                dps = min(n_dp, 8)
                grad = None
                for first in range(0, n_dp, dps):
                    given_rows = all_rows[first : first + dps].reshape(dps * 2 * ents, ent_proj.shape[0])
                    value = dot(hits[:, first * 2 * ents : (first + dps) * 2 * ents], given_rows)
                    grad = value if grad is None else grad + value
                table_here[i % 2] = grad
                named = jnp.sum(count, axis=1, keepdims=True)
                touched_here[i % 2] = jnp.broadcast_to(named, (table_block, LANES)).astype(LOW)
                table_copies.append(copies.local(lambda: table_here.at[i % 2], lambda: table_grad.at[here]))
                table_copies.append(copies.local(lambda: touched_here.at[i % 2], lambda: touched.at[here]))
                engine.clock += 1.2

            return step

        engine.add(
            [lambda: rows_ready, rows_z, rows_x, rows_core] + [table_part(i) for i in range(rows_dev // table_block)]
        )
        hidden_part(word_rows, 0, 1)
        word_copy = copies.send(lambda: grad_hidden.at[theirs[0]], lambda: given.at[word_part], place.other_y)
        word_ready = engine.transfer("y", word_half * width * 2)
        engine.work(1.5)

        bias_rows = bias_held.shape[0]
        bias_held[...] = jnp.zeros_like(bias_held)
        bias_held[0:6, columns] = bias_heads[0:6]
        bias_held[6:bias_rows] = bias_middle[0 : bias_rows - 6]
        live = {}
        bias_bytes = bias_rows * width * 2

        def bias_send(key, index, device):
            bias_from[2 * index] = bias_held[...].astype(LOW)
            live[key] = copies.send(lambda: bias_from.at[2 * index], lambda: bias_from.at[2 * index + 1], device)
            return engine.transfer(key, bias_bytes)

        def bias_take(key, index):
            live[key].wait_recv()
            bias_held[...] = bias_from[2 * index].astype(F32) + bias_from[2 * index + 1].astype(F32)

        def bias_core():
            return bias_send("core", 0, place.other_core)

        def bias_y():
            bias_take("core", 0)
            return bias_send("y", 1, place.other_y)

        def bias_x():
            bias_take("y", 1)
            return bias_send("x", 2, place.other_x)

        def bias_z():
            bias_take("x", 2)
            bias_from[6] = bias_held[...].astype(LOW)
            live["z"] = [
                copies.send(lambda: bias_from.at[6], lambda k=k: bias_from.at[7 + k], device)
                for k, device in enumerate(place.ahead)
            ]
            return engine.transfer("z", bias_bytes)

        def bias_end():
            value = bias_from[6].astype(F32)
            for k, copy in enumerate(live["z"]):
                copy.wait_recv()
                value = value + bias_from[7 + k].astype(F32)
            bias_out[...] = value

        engine.add([bias_core, bias_y, bias_x, bias_z, bias_end])
        quarter = word_half // 2

        def words_sum():
            word_copy.wait_recv()
            sum_hidden(0, word_half, y * word_half)
            engine.clock += 0.5
            live_words["send"] = copies.send(
                lambda: total.at[span((1 - core) * quarter, quarter, LANES)], lambda: word_grad.at[core], place.other_core
            )
            live_words["own"] = copies.local(
                lambda: total.at[span(core * quarter, quarter, LANES)], lambda: word_grad.at[core]
            )
            return engine.transfer("core", quarter * width * 4)

        def words_end():
            live_words["send"].wait_recv()
            live_words["own"].wait()

        engine.add([lambda: word_ready, words_sum, words_end])

        def ent_products():
            ent_copy.wait_recv()
            sum_hidden(word_half, ent_half, all_words + y * ent_half)
            proj_rows, pos_rows = rows.shape[1] // n_dp, all_words // n_dp
            proj_pad = padded(proj_rows)
            position = ent_pos[pl.ds(core, 1), :]
            picks = []
            for j in range(all_words // LANES):
                number = lax.broadcasted_iota(jnp.int32, (LANES, ents), 0) + j * LANES
                picks.append(jnp.where(number == position, 1.0, 0.0))
            pick = jnp.concatenate(picks, axis=0)
            here = lax.broadcasted_iota(jnp.int32, (all_words, ents), 1) // ent_half == y
            pick = jnp.where(here, pick, 0.0).astype(LOW)
            grad_ent = total[word_half:]
            grad_ent_low = grad_ent.astype(LOW)
            rest = (grad_ent - grad_ent_low.astype(F32)).astype(LOW)
            pos_grad = dot(pick, jnp.concatenate([grad_ent_low, grad_ent_low], axis=0)) + dot(
                pick, jnp.concatenate([rest, rest], axis=0)
            )
            proj_grad = dot_columns(rows[span(y * ent_half, ent_half, 64)], grad_ent_low)
            ent_grads[:, :, pl.ds(0, proj_rows)] = proj_grad.astype(LOW).reshape(nz, 2, proj_rows, width)
            ent_grads[:, :, pl.ds(proj_pad, pos_rows)] = pos_grad.astype(LOW).reshape(nz, 2, pos_rows, width)
            engine.clock += 1.0

        ent_job = jobs["ent"][0]
        engine.add([lambda: ent_ready, ent_products] + ent_job.steps)
        engine.drain()
        for copy in table_copies[-4:]:
            copy.wait()
        copies.finish()

    table_block = 256 if n_dp * 2 * ents <= 2048 else 32
    pl.run_scoped(
        backward_phase,
        pltpu.VMEM((tokens, half), LOW),
        pltpu.VMEM((tokens, half), LOW),
        pltpu.VMEM((tokens, half), LOW),
        pltpu.VMEM((tokens, half), LOW),
        pltpu.VMEM((HEADS // 2, tokens, tokens), LOW),
        pltpu.VMEM((4, width, half), LOW),
        pltpu.VMEM((width, half), LOW),
        pltpu.VMEM((width, half), LOW),
        pltpu.VMEM((half, tokens), LOW),
        pltpu.VMEM((tokens, half), LOW),
        pltpu.VMEM((tokens, half), LOW),
        pltpu.VMEM((tokens, half), LOW),
        pltpu.VMEM((tokens, half), LOW),
        pltpu.VMEM((width, tokens), LOW),
        pltpu.VMEM((tokens, width), LOW),
        pltpu.VMEM((table_block, n_dp * 2 * ents), LOW),
        pltpu.VMEM((half // LANES, nz, 2, 6 * row_pad, LANES), LOW),
        pltpu.VMEM((nz, 2, ent_sum.shape[0], width), LOW),
        pltpu.VMEM((2, table_block, ent_proj.shape[0]), F32),
        pltpu.VMEM((2, table_block, LANES), LOW),
    )
    last_copies = [
        copies.local(lambda: ffn_sum, lambda: ffn_reduced),
        copies.local(lambda: attn_sum, lambda: attn_reduced),
        copies.local(lambda: ent_sum, lambda: ent_reduced),
    ]
    for copy in out_copies:
        copy.wait_recv()
    for copy in last_copies:
        copy.wait()
    copies.finish()


def layer(
    nz, rows_dev, words, ent_hidden, mixed, out_weight, out_bias, gains, shifts, up_weight, up_bias, down_weight, down_bias, word_cots, ent_cots,
    hidden_turned, query_words, query_ents, keys, values, probs, query_weight, key_weight, value_weight, rows, ent_pos, ent_proj, ids,
):
    n_dp = 2 * nz
    width, tokens = hidden_turned.shape
    half = keys.shape[1]
    ents, edim = rows.shape
    all_words = tokens - ents
    part, ff = tokens // 2, up_weight.shape[1]
    ffn_blocks = ffn_plan(n_dp, width, ff)
    ffn_rows, attn_rows = ffn_blocks[-1][0] + ffn_blocks[-1][1], 6 * padded(width // n_dp)
    ent_pad = padded(edim // n_dp) + padded(all_words // n_dp)
    bias_rows = 12 + ff // width
    plan = [("ffn", 0, base, size, order, width) for base, size, order in ffn_blocks]
    plan += [("attn", pair, 0, attn_rows, "xz", LANES) for pair in range(half // LANES)]
    plan.append(("ent", 0, 0, ent_pad, "xzy", width))
    scratch = [
        pltpu.VMEM((part, half), LOW),
        pltpu.VMEM((tokens, half), LOW),
        pltpu.VMEM((part, width), F32),
        pltpu.VMEM((part, width), LOW),
        pltpu.VMEM((ffn_rows, width), LOW),
        pltpu.VMEM((half // LANES, 2, attn_rows, LANES), LOW),
        pltpu.VMEM((ent_pad, width), LOW),
        pltpu.VMEM((bias_rows, width), F32),
        pltpu.VMEM((6 + nz, bias_rows, width), LOW),
        pltpu.VMEM((n_dp, 2, ents, edim), LOW),
        pltpu.VMEM((8, half), F32),
        pltpu.VMEM((16, width), F32),
        pltpu.VMEM((nz, 2, ffn_rows, width), LOW),
        pltpu.VMEM((part, half), LOW),
        pltpu.VMEM((2, ents, edim), LOW),
    ]
    remote = 8 + 2 + 1 + 3 + nz + 1 + nz + nz + 2 + 4
    for name, _, base, size, order, columns in plan:
        job = Job(None, None, base, size, order, columns)
        scratch += job.scratch(nz)
        remote += job.remote_count(nz)
    scratch += copy_semaphores(remote, 40 + 2 * (rows_dev // 32))
    return call(
        functools.partial(layer_kernel, nz, plan),
        [
            ((2, all_words // 4, width), LOW),
            ((2, ents // 4, width), LOW),
            ((2, all_words // 4, width), F32),
            ((ffn_rows, width), LOW),
            ((half // LANES, 2, attn_rows, LANES), LOW),
            ((ent_pad, width), LOW),
            ((bias_rows, width), F32),
            ((rows_dev, edim), F32),
            ((rows_dev, LANES), LOW),
        ],
        [ANY] * 2 + [IN_VMEM, ANY] + [IN_VMEM] * 3 + [ANY, IN_VMEM, ANY, IN_VMEM] + [ANY] * 2 + [ANY] * 9 + [IN_VMEM] * 4,
        [ANY] * 6 + [IN_VMEM, ANY, ANY],
        scratch,
        "layer",
        2,
    )(words, ent_hidden, mixed, out_weight, out_bias, gains, shifts, up_weight, up_bias, down_weight, down_bias, word_cots, ent_cots,
      hidden_turned, query_words, query_ents, keys, values, probs, query_weight, key_weight, value_weight, rows, ent_pos, ent_proj, ids)


def last_kernel(
    n_dp, table_grad, touched, first, second, ffn, attn, ent, bias, words_low, ents_low, words_grad,
    table_out, update, new_second, proj_grad, pos_grad, query_grad, key_grad, value_grad, out_grad, up_grad, down_grad, query_bias, gain_grad, shift_grad, key_bias, value_bias, out_bias, down_bias, up_bias,
    word_out, ent_out, word_grad,
):
    step = pl.program_id(0)
    grad = table_grad[...]
    hit = touched[:, 0:1].astype(F32) > 0.0
    mean_new = beta_one * first[...] + (1.0 - beta_one) * grad
    square_new = beta_two * second[...] + (1.0 - beta_two) * grad * grad
    direction = (
        mean_new
        / (1.0 - beta_one**adam_step)
        / (jnp.sqrt(square_new / (1.0 - beta_two**adam_step)) + adam_eps)
    )
    table_out[...] = grad
    update[...] = jnp.where(hit, direction, 0.0)
    new_second[...] = jnp.where(hit, square_new, second[...])
    width = ffn.shape[1]
    part, down_rows = out_grad.shape[0], down_grad.shape[0]
    pad = padded(part)
    proj_pad = padded(proj_grad.shape[0])
    parts = up_grad.shape[1] // width
    pairs = attn.shape[0]
    half = pairs * LANES

    @pl.when(step == 0)
    def _():
        down_grad[...] = ffn[:down_rows].astype(F32)

    @pl.when(step == 1)
    def _():
        for j in range(parts):
            base = down_rows + j * pad
            up_grad[:, j * width : (j + 1) * width] = ffn[base : base + part].astype(F32)

    @pl.when(step == 2)
    def _():
        base = down_rows + parts * pad
        out_grad[...] = ffn[base : base + part].astype(F32)
        proj_grad[...] = ent[: proj_grad.shape[0]].astype(F32)
        pos_grad[...] = ent[proj_pad : proj_pad + pos_grad.shape[0]].astype(F32)
        for side in range(2):
            for pair in range(pairs):
                columns = slice(side * half + pair * LANES, side * half + (pair + 1) * LANES)
                key_grad[:, columns] = attn[pair, side, 4 * pad : 4 * pad + part].astype(F32)
                value_grad[:, columns] = attn[pair, side, 5 * pad : 5 * pad + part].astype(F32)

    @pl.when(step == 3)
    def _():
        for side in range(2):
            for pair in range(pairs):
                columns = slice(side * half + pair * LANES, side * half + (pair + 1) * LANES)
                for i in range(4):
                    query_grad[i, :, columns] = attn[pair, side, i * pad : i * pad + part].astype(F32)
        dp = lax.axis_index("dp")

        def own_columns(value, size, start):
            lane = lax.broadcasted_iota(jnp.int32, (value.shape[1], size), 0)
            want = lax.broadcasted_iota(jnp.int32, (value.shape[1], size), 1) + start
            pick = jnp.where(lane == want, 1.0, 0.0)
            return jnp.dot(value, pick, precision=lax.Precision.HIGHEST, preferred_element_type=F32)

        own = own_columns(bias[...], part, dp * part)
        query_bias[...] = own[0:4]
        gain_grad[...] = own[7:9]
        shift_grad[...] = own[9:11]
        for vector, i in ((key_bias, 4), (value_bias, 5), (out_bias, 6), (down_bias, 11 + parts)):
            vector[...] = own[i : i + 1].reshape(part)
        up = jnp.concatenate([bias[11 + j : 12 + j] for j in range(parts)], axis=1)
        size = up_bias.shape[0]
        if size % LANES == 0:
            per = width // size
            row = bias[pl.ds(11 + dp // per, 1), :]
            chosen = row[:, :size]
            for i in range(1, per):
                chosen = jnp.where(dp % per == i, row[:, i * size : (i + 1) * size], chosen)
            up_bias[...] = chosen.reshape(size)
        else:
            up_bias[...] = own_columns(up, size, dp * size).reshape(size)

    @pl.when(step == 0)
    def _():
        word_out[...] = words_low[...]
        ent_out[...] = ents_low[...]
        word_grad[...] = words_grad[...]


def last(n_dp, ff, all_words, table_grad, touched, first, second, ffn, attn, ent, bias, words_low, ents_low, words_grad):
    width = ffn.shape[1]
    rows, edim = first.shape
    part = width // n_dp
    block = 512
    blocked = lambda columns: pl.BlockSpec((block, columns), lambda i: (i, 0))
    whole = lambda shape: pl.BlockSpec(shape, lambda i: (0,) * len(shape))
    shapes = [
        (edim // n_dp, width),
        (all_words // n_dp, width),
        (4, part, width),
        (part, width),
        (part, width),
        (part, width),
        (part, ff),
        (ff // n_dp, width),
        (4, part),
        (2, part),
        (2, part),
        (part,),
        (part,),
        (part,),
        (part,),
        (ff // n_dp,),
    ]
    through = [words_low, ents_low, words_grad]
    return pl.pallas_call(
        functools.partial(last_kernel, n_dp),
        grid=(rows // block,),
        out_shape=[jax.ShapeDtypeStruct((rows, edim), F32)] * 3
        + [jax.ShapeDtypeStruct(shape, F32) for shape in shapes]
        + [jax.ShapeDtypeStruct(array.shape, array.dtype) for array in through],
        in_specs=[blocked(edim), blocked(LANES), blocked(edim), blocked(edim)]
        + [whole(array.shape) for array in (ffn, attn, ent, bias)]
        + [whole(array.shape) for array in through],
        out_specs=[blocked(edim)] * 3 + [whole(shape) for shape in shapes] + [whole(array.shape) for array in through],
        compiler_params=pltpu.CompilerParams(vmem_limit_bytes=VMEM_BYTES),
        name="last",
    )(table_grad, touched, first, second, ffn, attn, ent, bias, words_low, ents_low, words_grad)


def on_device(
    word_states,
    segments,
    entity_ids,
    entity_pos,
    ent_table,
    first_moment,
    second_moment,
    ent_proj,
    pos_table,
    query_weight,
    query_bias,
    key_weight,
    key_bias,
    value_weight,
    value_bias,
    out_weight,
    out_bias,
    norm_gain,
    norm_shift,
    up_weight,
    up_bias,
    down_weight,
    down_bias,
    word_cot,
    ent_cot,
):
    n_dp = lax.axis_size("dp")
    nz = n_dp // 2
    width, ff = up_weight.shape
    all_words = segments.shape[1]
    words, word_cots, ent_cots, all_ids, rows = fetch(nz, word_states, word_cot, ent_cot, entity_ids, ent_table)
    ent_hidden, hidden_turned, query_words, query_ents, keys, values, probs, mixed = forward(
        words,
        rows,
        entity_pos,
        segments,
        ent_proj,
        pos_table,
        query_weight,
        query_bias,
        key_weight,
        key_bias,
        value_weight,
        value_bias,
    )
    ents = entity_ids.shape[1]
    word_out, ent_out, word_grad, ffn_sum, attn_sum, ent_sum, bias_sum, table_grad, touched = layer(
        nz, ent_table.shape[0], words, ent_hidden, mixed, out_weight, out_bias, norm_gain, norm_shift, up_weight, up_bias, down_weight, down_bias,
        word_cots, ent_cots, hidden_turned, query_words, query_ents, keys, values, probs, query_weight, key_weight, value_weight,
        rows, entity_pos, ent_proj, all_ids.reshape(-1, ents),
    )
    (table_grad, table_update, new_second, proj_grad, pos_grad, query_grad, key_grad, value_grad, out_grad, up_grad, down_grad,
     query_bias_grad, gain_grad, shift_grad, key_bias_grad, value_bias_grad, out_bias_grad, down_bias_grad, up_bias_grad,
     word_out, ent_out, word_grad,
    ) = last(
        n_dp, ff, all_words, table_grad, touched, first_moment, second_moment, ffn_sum, attn_sum, ent_sum, bias_sum, word_out, ent_out, word_grad
    )
    return (
        word_out,
        ent_out,
        word_grad,
        proj_grad,
        pos_grad,
        query_grad,
        query_bias_grad,
        key_grad,
        key_bias_grad,
        value_grad,
        value_bias_grad,
        out_grad,
        out_bias_grad,
        gain_grad,
        shift_grad,
        up_grad,
        up_bias_grad,
        down_grad,
        down_bias_grad,
        table_grad,
        table_update,
        new_second,
    )


def solution(mesh):
    return jax.shard_map(
        on_device,
        mesh=mesh,
        in_specs=(
            P("dp", "seq", None),
            P("dp", None),
            P("dp", None),
            P("dp", None),
            P(("dp", "seq"), None),
            P(("dp", "seq"), None),
            P(("dp", "seq"), None),
            P(),
            P(),
            P(),
            P(),
            P(),
            P(),
            P(),
            P(),
            P(),
            P(),
            P(),
            P(),
            P(),
            P(),
            P(),
            P(),
            P("dp", "seq", None),
            P("dp", "seq", None),
        ),
        out_specs=(
            P("dp", "seq", None),
            P("dp", "seq", None),
            P("dp", "seq", None),
            P("dp", None),
            P("dp", None),
            P(None, "dp", None),
            P(None, "dp"),
            P("dp", None),
            P("dp"),
            P("dp", None),
            P("dp"),
            P("dp", None),
            P("dp"),
            P(None, "dp"),
            P(None, "dp"),
            P("dp", None),
            P("dp"),
            P("dp", None),
            P("dp"),
            P(("dp", "seq"), None),
            P(("dp", "seq"), None),
            P(("dp", "seq"), None),
        ),
        check_vma=False,
    )
```

```python
import functools
import math

import jax
import jax.numpy as jnp
from jax import lax
from jax.experimental import pallas as pl
from jax.experimental.pallas import tpu as pltpu
from jax.sharding import PartitionSpec as P

HEADS = 12
HEAD = 64
LANES = 128
MESH = pl.DeviceIdType.MESH
LOW = jnp.bfloat16
F32 = jnp.float32
VMEM_BYTES = 125 * 512 * 1024

norm_eps = 1e-05
beta_one = 0.9
beta_two = 0.98
adam_eps = 1e-06
adam_step = 10.0
masked_score = -1e30


def dot(left, right):
    return jnp.dot(left, right, preferred_element_type=F32)


def dot_rows(left, right):
    return lax.dot_general(left, right, (((1,), (1,)), ((), ())), preferred_element_type=F32)


def dot_columns(left, right):
    return lax.dot_general(left, right, (((0,), (0,)), ((), ())), preferred_element_type=F32)


def span(start, size, unit):
    if isinstance(start, int):
        return pl.ds(start, size)
    return pl.ds(pl.multiple_of(start, unit), size)


def padded(rows):
    return -(-rows // 16) * 16


def loop(count, body, carry=0, unroll=1):
    def steps(i, carried):
        for k in range(unroll):
            carried = body(i * unroll + k, carried)
        return carried

    return lax.fori_loop(0, count // unroll, steps, carry)


class Place:
    def __init__(self, nz):
        self.dp, self.seq = lax.axis_index("dp"), lax.axis_index("seq")
        self.z, self.x = self.dp // 2, self.dp % 2
        self.y, self.core = self.seq // 2, self.seq % 2
        self.nz = nz
        self.other_core = (self.dp, self.y * 2 + 1 - self.core)
        self.other_y = (self.dp, (1 - self.y) * 2 + self.core)
        self.diagonal = (self.dp, (1 - self.y) * 2 + 1 - self.core)
        self.other_x = (self.z * 2 + 1 - self.x, self.seq)
        self.ahead = [(((self.z + k) % nz) * 2 + self.x, self.seq) for k in range(1, nz)]

    def z_ahead(self, k):
        return (self.z + k) % self.nz


def meet(partners):
    barrier = pltpu.get_barrier_semaphore()
    for partner in partners:
        pl.semaphore_signal(barrier, inc=1, device_id=partner, device_id_type=MESH)
    pl.semaphore_wait(barrier, len(partners))


class Remote:
    def __init__(self, copies, number, src, dst, device):
        self.copies, self.number, self.src, self.dst, self.device = copies, number, src, dst, device
        self.open = True

    def make(self, landing=False):
        return pltpu.make_async_remote_copy(
            src_ref=self.dst() if landing else self.src(),
            dst_ref=self.dst(),
            send_sem=self.copies.send_sem.at[self.number],
            recv_sem=self.copies.recv_sem.at[self.number],
            device_id=self.device,
            device_id_type=MESH,
        )

    def wait_recv(self):
        self.make(landing=True).wait_recv()

    def wait_send(self):
        if self.open:
            self.make().wait_send()
        self.open = False


class Local:
    def __init__(self, copies, number, src, dst):
        self.copies, self.number, self.src, self.dst = copies, number, src, dst

    def make(self):
        return pltpu.make_async_copy(self.src(), self.dst(), self.copies.local_sem.at[self.number])

    def wait(self):
        self.make().wait()


class Copies:
    def __init__(self, send_sem, recv_sem, local_sem):
        self.send_sem, self.recv_sem, self.local_sem = send_sem, recv_sem, local_sem
        self.local_count = 0
        self.sent = []

    def send(self, src, dst, device):
        copy = Remote(self, len(self.sent), src, dst, device)
        copy.make().start()
        self.sent.append(copy)
        return copy

    def local(self, src, dst):
        copy = Local(self, self.local_count, src, dst)
        self.local_count += 1
        copy.make().start()
        return copy

    def finish(self):
        for copy in self.sent:
            copy.wait_send()


def copy_semaphores(remote, local):
    return [
        pltpu.SemaphoreType.DMA((remote,)),
        pltpu.SemaphoreType.DMA((remote,)),
        pltpu.SemaphoreType.DMA((local,)),
    ]


ANY = pl.BlockSpec(memory_space=pl.ANY)
IN_VMEM = pl.BlockSpec(memory_space=pltpu.VMEM)


def call(kernel, outs, in_specs, out_specs, scratch, name, collective_id=None):
    params = {"vmem_limit_bytes": VMEM_BYTES}
    if collective_id is not None:
        params.update(collective_id=collective_id, has_side_effects=True)
    return pl.pallas_call(
        kernel,
        out_shape=[jax.ShapeDtypeStruct(shape, dtype) for shape, dtype in outs],
        in_specs=in_specs,
        out_specs=out_specs,
        scratch_shapes=scratch,
        compiler_params=pltpu.CompilerParams(**params),
        name=name,
    )


def fetch_kernel(nz, words, word_cot, ent_cot, ids, table, all_words, word_cots, ent_cots, all_ids, rows_out, *scratch):
    table_full, table_low, picked, answers, held, from_core, from_x, from_z, from_y, ids_here = scratch[:10]
    copies = Copies(*scratch[10:])
    place = Place(nz)
    z, x, y, core = place.z, place.x, place.y, place.core
    n_dp = 2 * nz
    word_here, ent_here = words.shape[1], ent_cot.shape[1]
    ents = ids.shape[1]
    dp_others = [((place.dp + k) % n_dp, place.seq) for k in range(1, n_dp)]
    meet([place.other_core, place.other_y, place.diagonal] + dp_others)
    whole_table = copies.local(lambda: table, lambda: table_full)
    ids_here[place.dp] = ids[...]
    id_copies = [copies.send(lambda: ids, lambda: ids_here.at[place.dp], device) for device in dp_others]
    quarter = span(place.seq * word_here, word_here, 128)
    word_copies = [
        copies.send(lambda: words.at[1 - core], lambda: all_words.at[quarter], place.diagonal),
        copies.send(lambda: words.at[core], lambda: all_words.at[quarter], place.other_y),
        copies.send(lambda: words.at[1 - core], lambda: all_words.at[quarter], place.other_core),
        copies.send(lambda: word_cot.at[1 - core], lambda: word_cots.at[span(core * word_here, word_here, 128)], place.other_core),
        copies.send(lambda: ent_cot.at[1 - core], lambda: ent_cots.at[span(core * ent_here, ent_here, 32)], place.other_core),
    ]
    all_words[quarter] = words[core]
    word_cots[span(core * word_here, word_here, 128)] = word_cot[core]
    ent_cots[span(core * ent_here, ent_here, 32)] = ent_cot[core]
    whole_table.wait()
    rows_dev = table.shape[0]

    def narrow(i, _):
        where = span(i * 128, 128, 128)
        table_low[where] = table_full[where].astype(LOW)
        return 0

    loop(rows_dev // 128, narrow)
    for copy in id_copies:
        copy.wait_recv()
    all_ids[...] = ids_here[...]
    base = (place.dp * 4 + place.seq) * rows_dev
    tiles = rows_dev // LANES

    def look_up(zz):
        for g in range(4):
            asked = ids_here[zz * 2 + g // 2, pl.ds(g % 2, 1), :] - base
            column = jnp.transpose(jnp.broadcast_to(asked, (ents, ents)))
            lane = lax.broadcasted_iota(jnp.int32, (ents, LANES), 1)
            low_hit = jnp.where((column & (LANES - 1)) == lane, 1.0, 0.0).astype(LOW)
            high = jnp.clip(column >> 7, -1, tiles).astype(F32).astype(LOW)
            for j in range(tiles):
                hit = jnp.where(high == jnp.asarray(j, LOW), low_hit, jnp.zeros_like(low_hit))
                picked[pl.ds(g * ents, ents), pl.ds(j * LANES, LANES)] = hit
        answer = dot(picked[...], table_low[...]).astype(LOW)
        answers[zz] = answer.reshape(2, 2, ents, answer.shape[-1])

    order = [place.z_ahead(k + 1) for k in range(nz)]
    core_copies, x_copies, z_copies = [], [], []

    def core_send(zz):
        return copies.send(lambda: answers.at[zz, :, 1 - core], lambda: from_core.at[zz], place.other_core)

    def after_core(k):
        zz = order[k]
        core_copies[k].wait_recv()
        held[zz] = answers[zz, :, core] + from_core[zz]
        x_copies.append(copies.send(lambda: held.at[zz, 1 - x], lambda: from_x.at[zz], place.other_x))

    def after_x(k):
        zz = order[k]
        x_copies[k].wait_recv()
        held[zz, x] = held[zz, x] + from_x[zz]
        if k < nz - 1:
            z_copies.append(copies.send(lambda: held.at[zz, x], lambda: from_z.at[k], place.ahead[k]))

    for k in range(nz + 2):
        if k < nz:
            look_up(order[k])
            core_copies.append(core_send(order[k]))
        if 0 <= k - 1 < nz:
            after_core(k - 1)
        if 0 <= k - 2:
            after_x(k - 2)
    total = held[z, x]
    for k in range(nz - 1):
        z_copies[k].wait_recv()
        total = total + from_z[k]
    from_y[0] = total
    y_copy = copies.send(lambda: from_y.at[0], lambda: from_y.at[1], place.other_y)
    y_copy.wait_recv()
    rows_out[...] = from_y[0] + from_y[1]
    for copy in word_copies:
        copy.wait_recv()
    copies.finish()


def fetch(nz, words, word_cot, ent_cot, ids, table):
    _, word_here, width = words.shape
    ent_here, ents, (rows_dev, edim) = ent_cot.shape[1], ids.shape[1], table.shape
    n_dp = 2 * nz
    return call(
        functools.partial(fetch_kernel, nz),
        [
            ((4 * word_here, width), LOW),
            ((2 * word_here, width), LOW),
            ((2 * ent_here, width), LOW),
            ((n_dp, 2, ents), jnp.int32),
            ((ents, edim), LOW),
        ],
        [IN_VMEM] * 4 + [ANY],
        [IN_VMEM] * 5,
        [
            pltpu.VMEM((rows_dev, edim), F32),
            pltpu.VMEM((rows_dev, edim), LOW),
            pltpu.VMEM((4 * ents, rows_dev), LOW),
            pltpu.VMEM((nz, 2, 2, ents, edim), LOW),
            pltpu.VMEM((nz, 2, ents, edim), LOW),
            pltpu.VMEM((nz, 2, ents, edim), LOW),
            pltpu.VMEM((nz, ents, edim), LOW),
            pltpu.VMEM((nz - 1, ents, edim), LOW),
            pltpu.VMEM((2, ents, edim), LOW),
            pltpu.VMEM((n_dp, 2, ents), jnp.int32),
        ]
        + copy_semaphores(n_dp + 4 + 3 * nz + 2, 1),
        "fetch",
        1,
    )(words, word_cot, ent_cot, ids, table)


def lane_mask(rows, head):
    lane = lax.broadcasted_iota(jnp.int32, (rows, LANES), 1)
    return (lane >= head * HEAD) & (lane < (head + 1) * HEAD)


def row_of(vector):
    return vector[...].astype(F32).reshape(1, vector.shape[0])


def own_half(vector, y):
    row = row_of(vector)
    half = row.shape[1] // 2
    return jnp.where(y == 0, row[:, :half], row[:, half:])


def as_column(row):
    parts = [
        jnp.transpose(jnp.broadcast_to(row[:, i : i + LANES], (LANES, LANES)))
        for i in range(0, row.shape[1], LANES)
    ]
    return jnp.concatenate(parts, axis=0) if len(parts) > 1 else parts[0]


def forward_kernel(
    words, rows, ent_pos, segments, ent_proj, pos_table, query_weight, query_bias, key_weight, key_bias, value_weight, value_bias,
    ent_hidden, hidden_turned, query_words, query_ents, keys, values, probs, mixed,
    hidden_low, query_here, key_here, value_here, values_turned, mask, local_sem,
):
    y, core = lax.axis_index("seq") // 2, lax.axis_index("seq") % 2
    half = keys.shape[1]
    all_words, ents = words.shape[0], rows.shape[0]
    ent_pos, segments = ent_pos[pl.ds(core, 1), :], segments[pl.ds(core, 1), :]
    tokens = all_words + ents
    columns = span(y * half, half, LANES)
    weight_copies = [
        pltpu.make_async_copy(query_weight.at[:, :, columns], query_here, local_sem.at[0]),
        pltpu.make_async_copy(key_weight.at[:, columns], key_here, local_sem.at[1]),
        pltpu.make_async_copy(value_weight.at[:, columns], value_here, local_sem.at[2]),
    ]
    for copy in weight_copies:
        copy.start()
    position = as_column(ent_pos)
    picks = []
    for j in range(all_words // LANES):
        number = lax.broadcasted_iota(jnp.int32, (ents, LANES), 1) + j * LANES
        picks.append(jnp.where(position == number, 1.0, 0.0))
    pick = jnp.concatenate(picks, axis=1)
    word_seg = segments.astype(F32)
    ent_seg = jnp.sum(pick * word_seg, axis=1, keepdims=True)
    ent_hidden[...] = dot(rows[...], ent_proj[...]) + dot(pick.astype(LOW), pos_table[...])
    hidden_low[:all_words] = words[...]
    hidden_low[all_words:] = ent_hidden[...].astype(LOW)
    ent_row = jnp.transpose(jnp.broadcast_to(ent_seg, (ents, LANES)))[:1]
    seg_row = jnp.concatenate([word_seg, ent_row], axis=1)
    seg_column = jnp.concatenate([as_column(word_seg), jnp.broadcast_to(ent_seg, (ents, LANES))], axis=0)
    for j in range(tokens // LANES):
        here = slice(j * LANES, (j + 1) * LANES)
        mask[:, here] = jnp.where(seg_column == seg_row[:, here], 0.0, masked_score)

    query_b = query_bias[:, columns].astype(F32)
    for copy in weight_copies:
        copy.wait()
    word_low, ent_low = hidden_low[:all_words], hidden_low[all_words:]
    query_words[:all_words] = (dot(word_low, query_here[0]) + query_b[0:1]).astype(LOW)
    query_ents[:all_words] = (dot(word_low, query_here[1]) + query_b[1:2]).astype(LOW)
    query_words[all_words:] = (dot(ent_low, query_here[2]) + query_b[2:3]).astype(LOW)
    query_ents[all_words:] = (dot(ent_low, query_here[3]) + query_b[3:4]).astype(LOW)
    keys[...] = (dot(hidden_low[...], key_here[...]) + own_half(key_bias, y)).astype(LOW)
    value = dot(hidden_low[...], value_here[...]) + own_half(value_bias, y)
    values[...] = value.astype(LOW)
    values_turned[...] = jnp.transpose(value).astype(LOW)
    for i in range(words.shape[1] // LANES):
        here = slice(i * LANES, (i + 1) * LANES)
        hidden_turned[here, :] = jnp.transpose(hidden_low[:, here].astype(F32)).astype(LOW)
    scale = 1.0 / math.sqrt(HEAD)
    tiles = tokens // LANES

    def pair_step(pair, _):
        lanes = span(pair * LANES, LANES, LANES)
        key, turned = keys[:, lanes], values_turned[lanes, :]
        row = lax.broadcasted_iota(jnp.int32, (LANES, tokens), 0)
        own_key, own_turned = [], []
        for head in range(2):
            own_key.append(jnp.where(lane_mask(tokens, head), key, jnp.zeros_like(key)))
            own_rows = (row >= head * HEAD) & (row < (head + 1) * HEAD)
            own_turned.append(jnp.where(own_rows, turned, jnp.zeros_like(turned)))
        for i in range(tiles):
            place = slice(i * LANES, (i + 1) * LANES)
            query_w, query_e = query_words[place, lanes], query_ents[place, lanes]
            total = None
            for head in range(2):
                raw = jnp.concatenate(
                    [dot_rows(own_key[head][:all_words], query_w), dot_rows(own_key[head][all_words:], query_e)], axis=0
                )
                score = raw * scale + mask[:, place]
                weight = jnp.exp(score - jnp.max(score, axis=0, keepdims=True))
                prob = (weight * (1.0 / jnp.sum(weight, axis=0, keepdims=True))).astype(LOW)
                probs[pair * 2 + head, :, place] = prob
                part = dot(own_turned[head], prob)
                total = part if total is None else total + part
            mixed[place, lanes] = jnp.transpose(total).astype(LOW)
        return 0

    loop(half // LANES, pair_step)


def forward(words, rows, ent_pos, segments, ent_proj, pos_table, query_weight, query_bias, key_weight, key_bias, value_weight, value_bias):
    all_words, width = words.shape
    ents = rows.shape[0]
    tokens, half = all_words + ents, width // 2
    return call(
        forward_kernel,
        [
            ((ents, width), F32),
            ((width, tokens), LOW),
            ((tokens, half), LOW),
            ((tokens, half), LOW),
            ((tokens, half), LOW),
            ((tokens, half), LOW),
            ((HEADS // 2, tokens, tokens), LOW),
            ((tokens, half), LOW),
        ],
        [IN_VMEM] * 6 + [ANY, IN_VMEM, ANY, IN_VMEM, ANY, IN_VMEM],
        [IN_VMEM] * 8,
        [
            pltpu.VMEM((tokens, width), LOW),
            pltpu.VMEM((4, width, half), LOW),
            pltpu.VMEM((width, half), LOW),
            pltpu.VMEM((width, half), LOW),
            pltpu.VMEM((half, tokens), LOW),
            pltpu.VMEM((tokens, tokens), F32),
            pltpu.SemaphoreType.DMA((3,)),
        ],
        "forward",
    )(words, rows, ent_pos, segments, ent_proj, pos_table, query_weight, query_bias, key_weight, key_bias, value_weight, value_bias)


class Engine:
    RATES = {"core": 200e3, "x": 60e3, "y": 60e3, "z": 15e3}
    LATENCY = 3.0

    def __init__(self):
        self.clock, self.free, self.streams = 0.0, {}, []

    def transfer(self, link, size):
        start = max(self.clock, self.free.get(link, 0.0))
        self.free[link] = start + size / self.RATES[link]
        return self.free[link] + self.LATENCY

    def add(self, steps):
        self.streams.append([self.clock, list(steps)])
        self.poll()

    def run(self, stream):
        self.clock = max(self.clock, stream[0])
        ready = stream[1].pop(0)()
        stream[0] = self.clock if ready is None else ready

    def next(self):
        live = [stream for stream in self.streams if stream[1]]
        return min(live, key=lambda stream: stream[0]) if live else None

    def poll(self):
        while (stream := self.next()) is not None and stream[0] <= self.clock:
            self.run(stream)

    def work(self, time):
        self.clock += time
        self.poll()

    def drain(self):
        while (stream := self.next()) is not None:
            self.run(stream)


def blocks_of(rows):
    for size in (96, 64, 48, 32):
        if rows % size == 0:
            return size
    return 16


def add_blocks(engine, target, parts, leading, rows, columns):
    size = blocks_of(rows)
    count = rows // size

    def block(i, _):
        lead, row = i // count, (i % count) * size
        where = span(row, size, 16)
        if len(parts) == 2:
            value = parts[0](lead, where) + parts[1](lead, where)
        else:
            value = parts[0](lead, where).astype(F32)
            for part in parts[1:]:
                value = value + part(lead, where).astype(F32)
            value = value.astype(LOW)
        target(lead, where, value)
        return 0

    loop(leading * count, block)
    engine.clock += 0.3 + leading * rows * columns / 1e6


class Job:
    def __init__(self, grads, reduced, base, size, order, columns):
        self.grads, self.reduced, self.base, self.size, self.order, self.columns = grads, reduced, base, size, order, columns
        self.half = size // 2
        self.part = size // 4 if order == "yxz" else size // 2

    def scratch(self, nz):
        shapes = [(nz, 2, self.half, self.columns)]
        if self.order == "yxz":
            shapes.append((nz, 2, self.part, self.columns))
        elif self.order == "xzy":
            shapes.append((2, self.part, self.columns))
        shapes += [(nz, self.part, self.columns), (nz - 1, self.part, self.columns)]
        return [pltpu.VMEM(shape, LOW) for shape in shapes]

    def remote_count(self, nz):
        return 1 + (1 if self.order != "xz" else 0) + 1 + (nz - 1) + 1 + 1

    def prepare(self, engine, place, copies, scratch):
        nz, z, x, y, core = place.nz, place.z, place.x, place.y, place.core
        base, half, part, order, columns = self.base, self.half, self.part, self.order, self.columns
        held = self.grads.at[:, :, span(base + core * half, half, 16)]
        from_core = scratch[0]
        from_y = scratch[1] if order != "xz" else None
        from_x, from_z = scratch[-2:]
        live = {}
        row_bytes = 2 * columns
        theirs = span(base + (1 - core) * half, half, 16)
        mine = span(base + core * half, half, 16)
        own_rows = span(y * part, part, 16) if order == "yxz" else pl.ds(0, part)
        final_rows = span(base + core * half + (y * part if order == "yxz" else 0), part, 16)

        def start():
            live["core"] = copies.send(lambda: self.grads.at[:, :, theirs], lambda: from_core, place.other_core)
            return engine.transfer("core", 2 * nz * half * row_bytes)

        def send_x():
            live["x"] = copies.send(lambda: held.at[:, 1 - x, own_rows], lambda: from_x, place.other_x)
            return engine.transfer("x", nz * part * row_bytes)

        def after_core():
            live["core"].wait_recv()

            def put(i, where, value):
                held[i // 2, i % 2, where] = value

            add_blocks(
                engine,
                put,
                [lambda i, where: held[i // 2, i % 2, where], lambda i, where: from_core[i // 2, i % 2, where]],
                2 * nz,
                half,
                columns,
            )
            if order == "yxz":
                live["y"] = copies.send(
                    lambda: held.at[:, :, span((1 - y) * part, part, 16)], lambda: from_y, place.other_y
                )
                return engine.transfer("y", 2 * nz * part * row_bytes)
            return send_x()

        def shifted(where):
            return span(y * part + where.start, where.size, 16) if order == "yxz" else where

        def after_y():
            live["y"].wait_recv()

            def put(i, where, value):
                held[i // 2, i % 2, shifted(where)] = value

            add_blocks(
                engine,
                put,
                [lambda i, where: held[i // 2, i % 2, shifted(where)], lambda i, where: from_y[i // 2, i % 2, where]],
                2 * nz,
                part,
                columns,
            )
            return send_x()

        def send_z(k):
            return copies.send(
                lambda: held.at[place.z_ahead(k + 1), x, own_rows], lambda: from_z.at[k], place.ahead[k]
            )

        def after_x():
            live["x"].wait_recv()

            def put(i, where, value):
                held[i, x, shifted(where)] = value

            add_blocks(
                engine,
                put,
                [lambda i, where: held[i, x, shifted(where)], lambda i, where: from_x[i, where]],
                nz,
                part,
                columns,
            )
            live["z"] = [send_z(k) for k in range(nz - 1)]
            return engine.transfer("z", part * row_bytes)

        def after_z():
            for copy in live["z"]:
                copy.wait_recv()

            def put(i, where, value):
                if order == "yxz":
                    self.reduced[span(base + core * half + y * part + where.start, where.size, 16)] = value
                elif order == "xz":
                    self.reduced[y, span(base + core * half + where.start, where.size, 16)] = value
                else:
                    from_y[0, where] = value

            def parts(k):
                return lambda i, where: from_z[k, where]

            add_blocks(
                engine,
                put,
                [lambda i, where: held[z, x, shifted(where)]] + [parts(k) for k in range(nz - 1)],
                1,
                part,
                columns,
            )
            if order == "xzy":
                live["y2"] = copies.send(lambda: from_y.at[0], lambda: from_y.at[1], place.other_y)
            else:
                view = lambda: self.reduced.at[final_rows] if order == "yxz" else self.reduced.at[y, final_rows]
                live["y2"] = copies.send(view, view, place.other_y)
            return engine.transfer("y", part * row_bytes)

        def after_gather():
            live["y2"].wait_recv()
            if order == "xzy":

                def put(i, where, value):
                    self.reduced[span(base + core * half + where.start, where.size, 16)] = value

                add_blocks(
                    engine, put, [lambda i, where: from_y[0, where], lambda i, where: from_y[1, where]], 1, part, columns
                )
            view = lambda: self.reduced.at[:, mine] if order == "xz" else self.reduced.at[mine]
            live["core2"] = copies.send(view, view, place.other_core)
            return engine.transfer("core", 2 * half * row_bytes)

        def end():
            live["core2"].wait_recv()

        middle_steps = [after_core, after_y, after_x] if order == "yxz" else [after_core, after_x]
        self.steps = [start] + middle_steps + [after_z, after_gather, end]


def lane_mean(value):
    return jnp.mean(value, axis=-1, keepdims=True)


def column_sum(value):
    return jnp.sum(value, axis=0, keepdims=True)


ROW_BLOCK = 32


def ffn_plan(n_dp, width, ff):
    down_rows, row_pad = ff // n_dp, padded(width // n_dp)
    size = 128 if down_rows % 128 == 0 else 32
    order = "yxz" if size % 64 == 0 else "xzy"
    plan = [(base, size, order) for base in range(0, down_rows, size)]
    base = down_rows
    for pair in range(ff // width // 2):
        order = "yxz" if pair % 2 == 0 and row_pad % 32 == 0 else "xzy"
        plan.append((base, 2 * row_pad, order))
        base += 2 * row_pad
    plan.append((base, row_pad, "xzy"))
    return plan


def layer_kernel(
    nz, plan, words, ent_hidden, mixed, out_weight, out_bias, gains, shifts, up_weight, up_bias, down_weight, down_bias, word_cots, ent_cots,
    hidden_turned_in, query_words_in, query_ents_in, keys_in, values_in, probs_in, query_weight, key_weight, value_weight, rows, ent_pos, ent_proj, ids,
    word_out, ent_out, word_grad, ffn_reduced, attn_reduced, ent_reduced, bias_out, table_grad, touched, *scratch,
):
    (from_y_mixed, grad_mixed, grad_one, given, ffn_sum, attn_sum, ent_sum, bias_held, bias_from, all_rows, bias_heads, bias_middle,
     ffn_grads, grad_mixed_here, row_parts) = scratch[:15]
    copies = Copies(*scratch[-3:])
    engine = Engine()
    place = Place(nz)
    z, x, y, core = place.z, place.x, place.y, place.core
    n_dp = 2 * nz
    tokens, half = mixed.shape
    width = 2 * half
    ents = ent_hidden.shape[0]
    all_words = tokens - ents
    word_half, ent_half = all_words // 2, ents // 2
    part_tokens = tokens // 2
    ff = up_weight.shape[1]
    parts = ff // width
    row_part, row_pad, down_rows = width // n_dp, padded(width // n_dp), ff // n_dp
    meet([place.other_core, place.other_y, place.other_x] + place.ahead)

    jobs = {"ffn": [], "attn": [], "ent": []}

    def make_jobs(names, sources):
        at = 15
        for name, number, base, size, order, columns in plan:
            grads, reduced = sources.get(name, (None, None))
            if name == "attn" and grads is not None:
                grads, reduced = grads.at[number], reduced.at[number]
            job = Job(grads, reduced, base, size, order, columns)
            used = len(job.scratch(nz))
            if name in names:
                job.prepare(engine, place, copies, scratch[at : at + used])
                jobs[name].append(job)
            at += used

    make_jobs(["ffn"], {"ffn": (ffn_grads, ffn_sum)})

    def token_rows(side):
        return span(side * word_half, word_half, LANES), span(all_words + side * ent_half, ent_half, 64)

    mine, theirs = token_rows(y), token_rows(1 - y)
    own_columns, other_columns = span(y * half, half, LANES), span((1 - y) * half, half, LANES)
    word_part, ent_part = pl.ds(0, word_half), pl.ds(word_half, ent_half)
    mixed_copies = [
        copies.send(lambda: mixed.at[theirs[0]], lambda: from_y_mixed.at[word_part], place.other_y),
        copies.send(lambda: mixed.at[theirs[1]], lambda: from_y_mixed.at[ent_part], place.other_y),
    ]
    engine.transfer("y", part_tokens * half * 2)
    out_copies, mixed_back = [], []

    def forward_phase(
        out_here, up_here, down_here, word_here, ent_here, mixed_full, work, normed_low, normal_one, inverse_one,
        act, slope, output, grad_two, grad_two_low, grad_one_low, normed_turned,
    ):
        cot, grad_up_low = output, slope
        weight_copies = [
            copies.local(lambda: out_weight, lambda: out_here),
            copies.local(lambda: words.at[mine[0]], lambda: word_here),
            copies.local(lambda: ent_hidden.at[span(y * ent_half, ent_half, 64)], lambda: ent_here),
            copies.local(lambda: up_weight, lambda: up_here),
            copies.local(lambda: down_weight, lambda: down_here),
            copies.local(lambda: word_cots, lambda: cot.at[word_part]),
            copies.local(lambda: ent_cots, lambda: cot.at[ent_part]),
        ]
        gain, shift = gains[...].astype(F32), shifts[...].astype(F32)
        out_b, down_b, up_b = row_of(out_bias), row_of(down_bias), row_of(up_bias)
        mixed_full[word_part, own_columns] = mixed[mine[0]]
        mixed_full[ent_part, own_columns] = mixed[mine[1]]
        for copy in weight_copies[:3]:
            copy.wait()
        for copy in mixed_copies:
            copy.wait_recv()
        mixed_full[:, other_columns] = from_y_mixed[...]
        work[...] = dot(mixed_full[...], out_here[...])

        def norm_one(residual):
            def step(i, _):
                rows = span(residual[1] + i * ROW_BLOCK, ROW_BLOCK, ROW_BLOCK)
                value = residual[0][span(i * ROW_BLOCK, ROW_BLOCK, ROW_BLOCK)].astype(F32) + (work[rows] + out_b)
                center = value - lane_mean(value)
                inverse = lax.rsqrt(lane_mean(center * center) + norm_eps)
                normal = center * inverse
                result = normal * gain[0:1] + shift[0:1]
                normal_one[rows] = normal
                inverse_one[rows] = jnp.broadcast_to(inverse, (ROW_BLOCK, LANES))
                normed_low[rows] = result.astype(LOW)
                return 0

            return step

        loop(word_half // ROW_BLOCK, norm_one((word_here, 0)), 0, 2)
        loop(ent_half // ROW_BLOCK, norm_one((ent_here, word_half)), 0, 2)
        weight_copies[3].wait()
        for j in range(parts):
            columns = slice(j * width, (j + 1) * width)
            work[...] = dot(normed_low[...], up_here[:, columns]) + up_b[:, columns]

            def gelu(i, _):
                rows = span(i * ROW_BLOCK, ROW_BLOCK, ROW_BLOCK)
                value = work[rows]
                below = 0.5 * (1.0 + lax.erf(value * (1.0 / math.sqrt(2.0))))
                density = jnp.exp(-0.5 * value * value) * (1.0 / math.sqrt(2.0 * math.pi))
                act[rows, columns] = (value * below).astype(LOW)
                slope[rows, columns] = (below + value * density).astype(LOW)
                return 0

            loop(part_tokens // ROW_BLOCK, gelu)
        normed_turned[...] = jnp.transpose(normed_low[...].astype(F32)).astype(LOW)
        for copy in weight_copies[4:]:
            copy.wait()
        work[...] = dot(act[...], down_here[...])

        def norm_two(i, sums):
            rows = span(i * ROW_BLOCK, ROW_BLOCK, ROW_BLOCK)
            value = (normal_one[rows] * gain[0:1] + shift[0:1]) + (work[rows] + down_b)
            center = value - lane_mean(value)
            inverse = lax.rsqrt(lane_mean(center * center) + norm_eps)
            normal = center * inverse
            cotangent = cot[rows].astype(F32)
            output[rows] = (normal * gain[1:2] + shift[1:2]).astype(LOW)
            scaled = cotangent * gain[1:2]
            result = inverse * (scaled - lane_mean(scaled) - normal * lane_mean(scaled * normal))
            grad_two[rows] = result
            grad_two_low[rows] = result.astype(LOW)
            return (
                sums[0] + column_sum(cotangent * normal),
                sums[1] + column_sum(cotangent),
                sums[2] + column_sum(result),
            )

        nothing = jnp.zeros((1, width), F32)
        gain_two, shift_two, down_sum = loop(part_tokens // ROW_BLOCK, norm_two, (nothing, nothing, nothing), 2)
        quarter, ent_quarter = word_half // 2, ent_half // 2
        out_copies.extend([
            copies.send(
                lambda: output.at[span((1 - core) * quarter, quarter, LANES)], lambda: word_out.at[core], place.other_core
            ),
            copies.send(
                lambda: output.at[span(word_half + (1 - core) * ent_quarter, ent_quarter, 32)],
                lambda: ent_out.at[core],
                place.other_core,
            ),
        ])
        out_local = [
            copies.local(lambda: output.at[span(core * quarter, quarter, LANES)], lambda: word_out.at[core]),
            copies.local(
                lambda: output.at[span(word_half + core * ent_quarter, ent_quarter, 32)], lambda: ent_out.at[core]
            ),
        ]
        engine.clock = 0.0
        engine.free = {}
        def put(base, value):
            ffn_grads[:, :, pl.ds(base, row_part)] = value.astype(LOW).reshape(nz, 2, row_part, width)

        def down_block(job):
            if down_rows % 128:
                per = width // down_rows
                for j in range(parts):
                    value = dot_columns(act[:, j * width : (j + 1) * width], grad_two_low[...])
                    value = value.reshape(per, down_rows, width)[:, job.base : job.base + job.size].astype(LOW)
                    for d in range(per):
                        slab = j * per + d
                        ffn_grads[slab // 2, slab % 2, pl.ds(job.base, job.size)] = value[d]
            else:
                for slab in range(n_dp):
                    start = slab * down_rows + job.base
                    value = dot_columns(act[:, start : start + job.size], grad_two_low[...])
                    ffn_grads[slab // 2, slab % 2, pl.ds(job.base, job.size)] = value.astype(LOW)
            engine.work(1.3)
            engine.add(job.steps)

        up_sums = []

        def grad_up(j):
            columns = slice(j * width, (j + 1) * width)
            work[...] = dot_rows(grad_two_low[...], down_here[columns, :])

            def grad_gelu(i, total_row):
                rows = span(i * ROW_BLOCK, ROW_BLOCK, ROW_BLOCK)
                value = work[rows] * slope[rows, columns].astype(F32)
                grad_up_low[rows, columns] = value.astype(LOW)
                return total_row + column_sum(value)

            up_sums.append(loop(part_tokens // ROW_BLOCK, grad_gelu, nothing, 2))
            engine.work(1.6)
            put(down_rows + j * row_pad, dot(normed_turned[...], grad_up_low[:, columns]))
            engine.work(0.9)

        downs = [job for job in jobs["ffn"] if job.base < down_rows]
        ups = [job for job in jobs["ffn"] if down_rows <= job.base][:-1]
        for job in downs:
            down_block(job)
        for j in range(parts):
            grad_up(j)
            if j % 2 == 1:
                engine.add(ups[j // 2].steps)
        work[...] = dot_rows(grad_up_low[...], up_here[...])
        engine.work(2.0)

        def back_one(i, sums):
            rows = span(i * ROW_BLOCK, ROW_BLOCK, ROW_BLOCK)
            upper = grad_two[rows] + work[rows]
            normal = normal_one[rows]
            inverse = inverse_one[rows, 0:1]
            scaled = upper * gain[0:1]
            result = inverse * (scaled - lane_mean(scaled) - normal * lane_mean(scaled * normal))
            grad_one[rows] = result
            grad_one_low[rows] = result.astype(LOW)
            return (
                sums[0] + column_sum(upper * normal),
                sums[1] + column_sum(upper),
                sums[2] + column_sum(result),
            )

        gain_one, shift_one, out_sum = loop(part_tokens // ROW_BLOCK, back_one, (nothing, nothing, nothing), 2)
        engine.work(1.0)
        grad_mixed_here[...] = dot_rows(grad_one_low[...], out_here[other_columns, :]).astype(LOW)
        mixed_back.extend([
            copies.send(lambda: grad_mixed_here.at[word_part], lambda: grad_mixed.at[mine[0]], place.other_y),
            copies.send(lambda: grad_mixed_here.at[ent_part], lambda: grad_mixed.at[mine[1]], place.other_y),
        ])
        engine.transfer("y", part_tokens * half * 2)
        own = dot_rows(grad_one_low[...], out_here[own_columns, :]).astype(LOW)
        grad_mixed[mine[0]] = own[:word_half]
        grad_mixed[mine[1]] = own[word_half:]
        engine.work(1.0)
        put(down_rows + parts * row_pad, dot_columns(mixed_full[...], grad_one_low[...]))
        engine.work(0.8)
        engine.add(jobs["ffn"][-1].steps)
        bias_rows = [out_sum, gain_one, gain_two, shift_one, shift_two] + up_sums + [down_sum]
        for i, row in enumerate(bias_rows):
            bias_middle[i : i + 1] = row
        for copy in out_copies:
            copy.wait_send()
        for copy in out_local:
            copy.wait()

    tall = lambda columns, dtype: pltpu.VMEM((part_tokens, columns), dtype)
    pl.run_scoped(
        forward_phase,
        pltpu.VMEM((width, width), LOW),
        pltpu.VMEM((width, ff), LOW),
        pltpu.VMEM((ff, width), LOW),
        pltpu.VMEM((word_half, width), LOW),
        pltpu.VMEM((ent_half, width), F32),
        tall(width, LOW),
        tall(width, F32),
        tall(width, LOW),
        tall(width, F32),
        tall(LANES, F32),
        tall(ff, LOW),
        tall(ff, LOW),
        tall(width, LOW),
        tall(width, F32),
        tall(width, LOW),
        tall(width, LOW),
        pltpu.VMEM((width, part_tokens), LOW),
    )
    live_words = {}

    def backward_phase(
        query_words, query_ents, keys, values, probs, query_here, key_here, value_here, keys_turned,
        grad_query_words, grad_query_ents, grad_keys, grad_values, hidden_turned, grad_hidden, hits, attn_grads, ent_grads, table_here, touched_here,
    ):
        total = grad_one
        make_jobs(["attn", "ent"], {"attn": (attn_grads, attn_sum), "ent": (ent_grads, ent_sum)})
        columns = span(y * half, half, LANES)
        copies_in = [
            copies.local(lambda: values_in, lambda: values),
            copies.local(lambda: keys_in, lambda: keys),
            copies.local(lambda: query_words_in, lambda: query_words),
            copies.local(lambda: query_ents_in, lambda: query_ents),
        ]
        prob_copies = []
        for head in range(probs.shape[0]):
            prob_copies.append(
                copies.local(lambda head=head: probs_in.at[head], lambda head=head: probs.at[head])
            )
        hidden_copy = copies.local(lambda: hidden_turned_in, lambda: hidden_turned)
        weight_copies = [
            copies.local(lambda: query_weight.at[:, :, columns], lambda: query_here),
            copies.local(lambda: key_weight.at[:, columns], lambda: key_here),
            copies.local(lambda: value_weight.at[:, columns], lambda: value_here),
        ]
        for copy in copies_in:
            copy.wait()
        for i in range(half // LANES):
            lanes = slice(i * LANES, (i + 1) * LANES)
            keys_turned[lanes, :] = jnp.transpose(keys[:, lanes].astype(F32)).astype(LOW)
        for copy in mixed_back:
            copy.wait_recv()
        engine.work(2.0)
        scale = 1.0 / math.sqrt(HEAD)
        tiles = tokens // LANES

        def pair_products(pair):
            lanes = slice(pair * LANES, (pair + 1) * LANES)
            word_turned, ent_turned = hidden_turned[:, :all_words], hidden_turned[:, all_words:]
            products = [
                dot(word_turned, grad_query_words[:all_words, lanes]),
                dot(word_turned, grad_query_ents[:all_words, lanes]),
                dot(ent_turned, grad_query_words[all_words:, lanes]),
                dot(ent_turned, grad_query_ents[all_words:, lanes]),
                dot(hidden_turned[...], grad_keys[:, lanes]),
                dot(hidden_turned[...], grad_values[:, lanes]),
            ]
            for i, value in enumerate(products):
                attn_grads[pair, :, :, pl.ds(i * row_pad, row_part)] = value.astype(LOW).reshape(nz, 2, row_part, LANES)
            engine.work(1.5)
            engine.add(jobs["attn"][pair].steps)

        for pair in range(half // LANES):
            lanes = slice(pair * LANES, (pair + 1) * LANES)
            grad_query_w = jnp.zeros((LANES, tokens), F32)
            grad_query_e = jnp.zeros((LANES, tokens), F32)
            grad_key_w = jnp.zeros((all_words, LANES), F32)
            grad_key_e = jnp.zeros((ents, LANES), F32)
            grad_value = jnp.zeros((tokens, LANES), F32)
            for head in range(2):
                own = lane_mask(tokens, head)
                value = values[:, lanes]
                own_value = jnp.where(own, value, jnp.zeros_like(value))
                prob_copies[pair * 2 + head].wait()

                given_heads = grad_mixed[:, lanes]
                grad_scores = probs.at[pair * 2 + head]
                grad_value += dot(grad_scores[...], jnp.where(own, given_heads, jnp.zeros_like(given_heads)))
                for i in range(tiles):
                    where = slice(i * LANES, (i + 1) * LANES)
                    grad_prob = dot_rows(own_value, grad_mixed[where, lanes])
                    prob = grad_scores[:, where].astype(F32)
                    both = prob * grad_prob
                    grad_scores[:, where] = (both - prob * jnp.sum(both, axis=0, keepdims=True)).astype(LOW)
                engine.work(1.7)
                query_w, query_e = query_words[:, lanes], query_ents[:, lanes]
                grad_key_w += dot(grad_scores[:all_words], jnp.where(own, query_w, jnp.zeros_like(query_w)))
                grad_key_e += dot(grad_scores[all_words:], jnp.where(own, query_e, jnp.zeros_like(query_e)))
                row = lax.broadcasted_iota(jnp.int32, (LANES, tokens), 0)
                own_rows = (row >= head * HEAD) & (row < (head + 1) * HEAD)
                turned = keys_turned[lanes, :]
                turned = jnp.where(own_rows, turned, jnp.zeros_like(turned))
                grad_query_w += dot(turned[:, :all_words], grad_scores[:all_words])
                grad_query_e += dot(turned[:, all_words:], grad_scores[all_words:])
                engine.work(1.7)
            grad_query_w = jnp.transpose(grad_query_w) * scale
            grad_query_e = jnp.transpose(grad_query_e) * scale
            grad_key_w, grad_key_e = grad_key_w * scale, grad_key_e * scale
            sums = [
                column_sum(grad_query_w[:all_words]),
                column_sum(grad_query_e[:all_words]),
                column_sum(grad_query_w[all_words:]),
                column_sum(grad_query_e[all_words:]),
                column_sum(grad_key_w) + column_sum(grad_key_e),
                column_sum(grad_value),
            ]
            for i, sum_row in enumerate(sums):
                bias_heads[i : i + 1, lanes] = sum_row
            grad_query_words[:, lanes] = grad_query_w.astype(LOW)
            grad_query_ents[:, lanes] = grad_query_e.astype(LOW)
            grad_keys[:all_words, lanes] = grad_key_w.astype(LOW)
            grad_keys[all_words:, lanes] = grad_key_e.astype(LOW)
            grad_values[:, lanes] = grad_value.astype(LOW)
            engine.work(0.5)
            if pair == 0:
                hidden_copy.wait()
            if pair + 1 < half // LANES:
                pair_products(pair)

        for copy in weight_copies:
            copy.wait()
        ent_rows, word_rows = slice(all_words, tokens), slice(0, all_words)

        def hidden_part(here, first, second):
            grad_hidden[here] = (
                dot_rows(grad_keys[here], key_here[...])
                + dot_rows(grad_values[here], value_here[...])
                + dot_rows(grad_query_words[here], query_here[first])
                + dot_rows(grad_query_ents[here], query_here[second])
            ).astype(LOW)

        hidden_part(ent_rows, 2, 3)
        own_ents = lax.broadcasted_iota(jnp.int32, (ents, width), 0) // ent_half == y
        twice = jnp.concatenate([grad_one[word_half:], grad_one[word_half:]], axis=0)
        ent_sum_part = grad_hidden[ent_rows].astype(F32) + jnp.where(own_ents, twice, 0.0)
        row_parts[0] = dot_rows(ent_sum_part.astype(LOW), ent_proj[...]).astype(LOW)
        rows_copy = copies.send(lambda: row_parts.at[0], lambda: row_parts.at[1], place.other_y)
        row_bytes = ents * ent_proj.shape[0] * 2
        rows_ready = engine.transfer("y", row_bytes)
        engine.work(0.7)
        pair_products(half // LANES - 1)
        ent_copy = copies.send(lambda: grad_hidden.at[theirs[1]], lambda: given.at[ent_part], place.other_y)
        ent_ready = engine.transfer("y", ent_half * width * 2)

        live_rows = {}

        def sum_hidden(start, count, own_start):
            def block(i, _):
                where = span(start + i * 32, 32, 32)
                own = span(own_start + i * 32, 32, 32)
                total[where] = grad_one[where] + (grad_hidden[own].astype(F32) + given[where].astype(F32))
                return 0

            loop(count // 32, block)

        def rows_z():
            rows_copy.wait_recv()
            all_rows[place.dp, core] = row_parts[0] + row_parts[1]
            view = lambda: all_rows.at[place.dp, core]
            live_rows["z"] = [copies.send(view, view, device) for device in place.ahead]
            return engine.transfer("z", row_bytes)

        def rows_x():
            for copy in live_rows["z"]:
                copy.wait_recv()
            live_rows["x"] = []
            for k in range(nz):
                view = lambda k=k: all_rows.at[place.z_ahead(k) * 2 + x, core]
                live_rows["x"].append(copies.send(view, view, place.other_x))
            return engine.transfer("x", nz * row_bytes)

        def rows_core():
            for copy in live_rows["x"]:
                copy.wait_recv()
            view = lambda: all_rows.at[:, core]
            live_rows["core"] = copies.send(view, view, place.other_core)
            return engine.transfer("core", n_dp * row_bytes)

        rows_dev = table_grad.shape[0]
        table_copies = []
        base_row = (place.dp * 4 + place.seq) * rows_dev

        def table_part(i):
            def step():
                if i == 0:
                    live_rows["core"].wait_recv()
                groups = ids.shape[0]
                block = min(table_block, LANES)
                counts = [jnp.zeros((block, ents), LOW) for _ in range(table_block // block)]
                for group in range(groups):
                    asked = ids[group : group + 1, :] - base_row
                    high = jnp.clip(asked >> 7, -1, rows_dev // LANES).astype(F32)
                    high = jnp.broadcast_to(high, (block, ents)).astype(LOW)
                    first_row = i * table_block
                    number = lax.broadcasted_iota(jnp.int32, (block, ents), 0) + first_row % LANES
                    low_hit = jnp.where((asked & (LANES - 1)) == number, 1.0, 0.0).astype(LOW)
                    for k in range(len(counts)):
                        hit = jnp.where(
                            high == jnp.asarray(first_row // LANES + k, LOW), low_hit, jnp.zeros_like(low_hit)
                        )
                        counts[k] = counts[k] + hit
                        hits[k * block : (k + 1) * block, group * ents : (group + 1) * ents] = hit
                count = jnp.concatenate(counts, axis=0).astype(F32)
                here = pl.ds(i * table_block, table_block)
                for copy in table_copies[2 * i - 4 : 2 * i - 2] if i >= 2 else []:
                    copy.wait()
                dps = min(n_dp, 8)
                grad = None
                for first in range(0, n_dp, dps):
                    given_rows = all_rows[first : first + dps].reshape(dps * 2 * ents, ent_proj.shape[0])
                    value = dot(hits[:, first * 2 * ents : (first + dps) * 2 * ents], given_rows)
                    grad = value if grad is None else grad + value
                table_here[i % 2] = grad
                named = jnp.sum(count, axis=1, keepdims=True)
                touched_here[i % 2] = jnp.broadcast_to(named, (table_block, LANES)).astype(LOW)
                table_copies.append(copies.local(lambda: table_here.at[i % 2], lambda: table_grad.at[here]))
                table_copies.append(copies.local(lambda: touched_here.at[i % 2], lambda: touched.at[here]))
                engine.clock += 0.7

            return step

        engine.add(
            [lambda: rows_ready, rows_z, rows_x, rows_core] + [table_part(i) for i in range(rows_dev // table_block)]
        )
        hidden_part(word_rows, 0, 1)
        word_copy = copies.send(lambda: grad_hidden.at[theirs[0]], lambda: given.at[word_part], place.other_y)
        word_ready = engine.transfer("y", word_half * width * 2)
        engine.work(1.5)

        bias_rows = bias_held.shape[0]
        bias_held[...] = jnp.zeros_like(bias_held)
        bias_held[0:6, columns] = bias_heads[0:6]
        bias_held[6:bias_rows] = bias_middle[0 : bias_rows - 6]
        live = {}
        bias_bytes = bias_rows * width * 2

        def bias_send(key, index, device):
            bias_from[2 * index] = bias_held[...].astype(LOW)
            live[key] = copies.send(lambda: bias_from.at[2 * index], lambda: bias_from.at[2 * index + 1], device)
            return engine.transfer(key, bias_bytes)

        def bias_take(key, index):
            live[key].wait_recv()
            bias_held[...] = bias_from[2 * index].astype(F32) + bias_from[2 * index + 1].astype(F32)

        def bias_core():
            return bias_send("core", 0, place.other_core)

        def bias_y():
            bias_take("core", 0)
            return bias_send("y", 1, place.other_y)

        def bias_x():
            bias_take("y", 1)
            return bias_send("x", 2, place.other_x)

        def bias_z():
            bias_take("x", 2)
            bias_from[6] = bias_held[...].astype(LOW)
            live["z"] = [
                copies.send(lambda: bias_from.at[6], lambda k=k: bias_from.at[7 + k], device)
                for k, device in enumerate(place.ahead)
            ]
            return engine.transfer("z", bias_bytes)

        def bias_end():
            value = bias_from[6].astype(F32)
            for k, copy in enumerate(live["z"]):
                copy.wait_recv()
                value = value + bias_from[7 + k].astype(F32)
            bias_out[...] = value

        engine.add([bias_core, bias_y, bias_x, bias_z, bias_end])
        quarter = word_half // 2

        def words_sum():
            word_copy.wait_recv()
            sum_hidden(0, word_half, y * word_half)
            engine.clock += 0.5
            live_words["send"] = copies.send(
                lambda: total.at[span((1 - core) * quarter, quarter, LANES)], lambda: word_grad.at[core], place.other_core
            )
            live_words["own"] = copies.local(
                lambda: total.at[span(core * quarter, quarter, LANES)], lambda: word_grad.at[core]
            )
            return engine.transfer("core", quarter * width * 4)

        def words_end():
            live_words["send"].wait_recv()
            live_words["own"].wait()

        engine.add([lambda: word_ready, words_sum, words_end])

        def ent_products():
            ent_copy.wait_recv()
            sum_hidden(word_half, ent_half, all_words + y * ent_half)
            proj_rows, pos_rows = rows.shape[1] // n_dp, all_words // n_dp
            proj_pad = padded(proj_rows)
            position = ent_pos[pl.ds(core, 1), :]
            picks = []
            for j in range(all_words // LANES):
                number = lax.broadcasted_iota(jnp.int32, (LANES, ents), 0) + j * LANES
                picks.append(jnp.where(number == position, 1.0, 0.0))
            pick = jnp.concatenate(picks, axis=0)
            here = lax.broadcasted_iota(jnp.int32, (all_words, ents), 1) // ent_half == y
            pick = jnp.where(here, pick, 0.0).astype(LOW)
            grad_ent = total[word_half:]
            grad_ent_low = grad_ent.astype(LOW)
            rest = (grad_ent - grad_ent_low.astype(F32)).astype(LOW)
            pos_grad = dot(pick, jnp.concatenate([grad_ent_low, grad_ent_low], axis=0)) + dot(
                pick, jnp.concatenate([rest, rest], axis=0)
            )
            proj_grad = dot_columns(rows[span(y * ent_half, ent_half, 64)], grad_ent_low)
            ent_grads[:, :, pl.ds(0, proj_rows)] = proj_grad.astype(LOW).reshape(nz, 2, proj_rows, width)
            ent_grads[:, :, pl.ds(proj_pad, pos_rows)] = pos_grad.astype(LOW).reshape(nz, 2, pos_rows, width)
            engine.clock += 1.0

        ent_job = jobs["ent"][0]
        engine.add([lambda: ent_ready, ent_products] + ent_job.steps)
        engine.drain()
        for copy in table_copies[-4:]:
            copy.wait()
        copies.finish()

    table_block = 256 if n_dp * 2 * ents <= 2048 else 32
    pl.run_scoped(
        backward_phase,
        pltpu.VMEM((tokens, half), LOW),
        pltpu.VMEM((tokens, half), LOW),
        pltpu.VMEM((tokens, half), LOW),
        pltpu.VMEM((tokens, half), LOW),
        pltpu.VMEM((HEADS // 2, tokens, tokens), LOW),
        pltpu.VMEM((4, width, half), LOW),
        pltpu.VMEM((width, half), LOW),
        pltpu.VMEM((width, half), LOW),
        pltpu.VMEM((half, tokens), LOW),
        pltpu.VMEM((tokens, half), LOW),
        pltpu.VMEM((tokens, half), LOW),
        pltpu.VMEM((tokens, half), LOW),
        pltpu.VMEM((tokens, half), LOW),
        pltpu.VMEM((width, tokens), LOW),
        pltpu.VMEM((tokens, width), LOW),
        pltpu.VMEM((table_block, n_dp * 2 * ents), LOW),
        pltpu.VMEM((half // LANES, nz, 2, 6 * row_pad, LANES), LOW),
        pltpu.VMEM((nz, 2, ent_sum.shape[0], width), LOW),
        pltpu.VMEM((2, table_block, ent_proj.shape[0]), F32),
        pltpu.VMEM((2, table_block, LANES), LOW),
    )
    last_copies = [
        copies.local(lambda: ffn_sum, lambda: ffn_reduced),
        copies.local(lambda: attn_sum, lambda: attn_reduced),
        copies.local(lambda: ent_sum, lambda: ent_reduced),
    ]
    for copy in out_copies:
        copy.wait_recv()
    for copy in last_copies:
        copy.wait()
    copies.finish()


def layer(
    nz, rows_dev, words, ent_hidden, mixed, out_weight, out_bias, gains, shifts, up_weight, up_bias, down_weight, down_bias, word_cots, ent_cots,
    hidden_turned, query_words, query_ents, keys, values, probs, query_weight, key_weight, value_weight, rows, ent_pos, ent_proj, ids,
):
    n_dp = 2 * nz
    width, tokens = hidden_turned.shape
    half = keys.shape[1]
    ents, edim = rows.shape
    all_words = tokens - ents
    part, ff = tokens // 2, up_weight.shape[1]
    ffn_blocks = ffn_plan(n_dp, width, ff)
    ffn_rows, attn_rows = ffn_blocks[-1][0] + ffn_blocks[-1][1], 6 * padded(width // n_dp)
    ent_pad = padded(edim // n_dp) + padded(all_words // n_dp)
    bias_rows = 12 + ff // width
    plan = [("ffn", 0, base, size, order, width) for base, size, order in ffn_blocks]
    plan += [("attn", pair, 0, attn_rows, "xz", LANES) for pair in range(half // LANES)]
    plan.append(("ent", 0, 0, ent_pad, "xzy", width))
    scratch = [
        pltpu.VMEM((part, half), LOW),
        pltpu.VMEM((tokens, half), LOW),
        pltpu.VMEM((part, width), F32),
        pltpu.VMEM((part, width), LOW),
        pltpu.VMEM((ffn_rows, width), LOW),
        pltpu.VMEM((half // LANES, 2, attn_rows, LANES), LOW),
        pltpu.VMEM((ent_pad, width), LOW),
        pltpu.VMEM((bias_rows, width), F32),
        pltpu.VMEM((6 + nz, bias_rows, width), LOW),
        pltpu.VMEM((n_dp, 2, ents, edim), LOW),
        pltpu.VMEM((8, half), F32),
        pltpu.VMEM((16, width), F32),
        pltpu.VMEM((nz, 2, ffn_rows, width), LOW),
        pltpu.VMEM((part, half), LOW),
        pltpu.VMEM((2, ents, edim), LOW),
    ]
    remote = 8 + 2 + 1 + 3 + nz + 1 + nz + nz + 2 + 4
    for name, _, base, size, order, columns in plan:
        job = Job(None, None, base, size, order, columns)
        scratch += job.scratch(nz)
        remote += job.remote_count(nz)
    scratch += copy_semaphores(remote, 40 + 2 * (rows_dev // 32))
    return call(
        functools.partial(layer_kernel, nz, plan),
        [
            ((2, all_words // 4, width), LOW),
            ((2, ents // 4, width), LOW),
            ((2, all_words // 4, width), F32),
            ((ffn_rows, width), LOW),
            ((half // LANES, 2, attn_rows, LANES), LOW),
            ((ent_pad, width), LOW),
            ((bias_rows, width), F32),
            ((rows_dev, edim), F32),
            ((rows_dev, LANES), LOW),
        ],
        [ANY] * 2 + [IN_VMEM, ANY] + [IN_VMEM] * 3 + [ANY, IN_VMEM, ANY, IN_VMEM] + [ANY] * 2 + [ANY] * 9 + [IN_VMEM] * 4,
        [ANY] * 6 + [IN_VMEM, ANY, ANY],
        scratch,
        "layer",
        2,
    )(words, ent_hidden, mixed, out_weight, out_bias, gains, shifts, up_weight, up_bias, down_weight, down_bias, word_cots, ent_cots,
      hidden_turned, query_words, query_ents, keys, values, probs, query_weight, key_weight, value_weight, rows, ent_pos, ent_proj, ids)


def last_kernel(
    n_dp, table_grad, touched, first, second, ffn, attn, ent, bias, words_low, ents_low, words_grad,
    table_out, update, new_second, proj_grad, pos_grad, query_grad, key_grad, value_grad, out_grad, up_grad, down_grad, query_bias, gain_grad, shift_grad, key_bias, value_bias, out_bias, down_bias, up_bias,
    word_out, ent_out, word_grad,
):
    step = pl.program_id(0)
    grad = table_grad[...]
    hit = touched[:, 0:1].astype(F32) > 0.0
    mean_new = beta_one * first[...] + (1.0 - beta_one) * grad
    square_new = beta_two * second[...] + (1.0 - beta_two) * grad * grad
    direction = (
        mean_new
        / (1.0 - beta_one**adam_step)
        / (jnp.sqrt(square_new / (1.0 - beta_two**adam_step)) + adam_eps)
    )
    table_out[...] = grad
    update[...] = jnp.where(hit, direction, 0.0)
    new_second[...] = jnp.where(hit, square_new, second[...])
    width = ffn.shape[1]
    part, down_rows = out_grad.shape[0], down_grad.shape[0]
    pad = padded(part)
    proj_pad = padded(proj_grad.shape[0])
    parts = up_grad.shape[1] // width
    pairs = attn.shape[0]
    half = pairs * LANES

    @pl.when(step == 0)
    def _():
        down_grad[...] = ffn[:down_rows].astype(F32)

    @pl.when(step == 1)
    def _():
        for j in range(parts):
            base = down_rows + j * pad
            up_grad[:, j * width : (j + 1) * width] = ffn[base : base + part].astype(F32)

    @pl.when(step == 2)
    def _():
        base = down_rows + parts * pad
        out_grad[...] = ffn[base : base + part].astype(F32)
        proj_grad[...] = ent[: proj_grad.shape[0]].astype(F32)
        pos_grad[...] = ent[proj_pad : proj_pad + pos_grad.shape[0]].astype(F32)
        for side in range(2):
            for pair in range(pairs):
                columns = slice(side * half + pair * LANES, side * half + (pair + 1) * LANES)
                key_grad[:, columns] = attn[pair, side, 4 * pad : 4 * pad + part].astype(F32)
                value_grad[:, columns] = attn[pair, side, 5 * pad : 5 * pad + part].astype(F32)

    @pl.when(step == 3)
    def _():
        for side in range(2):
            for pair in range(pairs):
                columns = slice(side * half + pair * LANES, side * half + (pair + 1) * LANES)
                for i in range(4):
                    query_grad[i, :, columns] = attn[pair, side, i * pad : i * pad + part].astype(F32)
        dp = lax.axis_index("dp")

        def own_columns(value, size, start):
            lane = lax.broadcasted_iota(jnp.int32, (value.shape[1], size), 0)
            want = lax.broadcasted_iota(jnp.int32, (value.shape[1], size), 1) + start
            pick = jnp.where(lane == want, 1.0, 0.0)
            return jnp.dot(value, pick, precision=lax.Precision.HIGHEST, preferred_element_type=F32)

        own = own_columns(bias[...], part, dp * part)
        query_bias[...] = own[0:4]
        gain_grad[...] = own[7:9]
        shift_grad[...] = own[9:11]
        for vector, i in ((key_bias, 4), (value_bias, 5), (out_bias, 6), (down_bias, 11 + parts)):
            vector[...] = own[i : i + 1].reshape(part)
        up = jnp.concatenate([bias[11 + j : 12 + j] for j in range(parts)], axis=1)
        size = up_bias.shape[0]
        if size % LANES == 0:
            per = width // size
            row = bias[pl.ds(11 + dp // per, 1), :]
            chosen = row[:, :size]
            for i in range(1, per):
                chosen = jnp.where(dp % per == i, row[:, i * size : (i + 1) * size], chosen)
            up_bias[...] = chosen.reshape(size)
        else:
            up_bias[...] = own_columns(up, size, dp * size).reshape(size)

    @pl.when(step == 0)
    def _():
        word_out[...] = words_low[...]
        ent_out[...] = ents_low[...]
        word_grad[...] = words_grad[...]


def last(n_dp, ff, all_words, table_grad, touched, first, second, ffn, attn, ent, bias, words_low, ents_low, words_grad):
    width = ffn.shape[1]
    rows, edim = first.shape
    part = width // n_dp
    block = 512
    blocked = lambda columns: pl.BlockSpec((block, columns), lambda i: (i, 0))
    whole = lambda shape: pl.BlockSpec(shape, lambda i: (0,) * len(shape))
    shapes = [
        (edim // n_dp, width),
        (all_words // n_dp, width),
        (4, part, width),
        (part, width),
        (part, width),
        (part, width),
        (part, ff),
        (ff // n_dp, width),
        (4, part),
        (2, part),
        (2, part),
        (part,),
        (part,),
        (part,),
        (part,),
        (ff // n_dp,),
    ]
    through = [words_low, ents_low, words_grad]
    return pl.pallas_call(
        functools.partial(last_kernel, n_dp),
        grid=(rows // block,),
        out_shape=[jax.ShapeDtypeStruct((rows, edim), F32)] * 3
        + [jax.ShapeDtypeStruct(shape, F32) for shape in shapes]
        + [jax.ShapeDtypeStruct(array.shape, array.dtype) for array in through],
        in_specs=[blocked(edim), blocked(LANES), blocked(edim), blocked(edim)]
        + [whole(array.shape) for array in (ffn, attn, ent, bias)]
        + [whole(array.shape) for array in through],
        out_specs=[blocked(edim)] * 3 + [whole(shape) for shape in shapes] + [whole(array.shape) for array in through],
        compiler_params=pltpu.CompilerParams(vmem_limit_bytes=VMEM_BYTES),
        name="last",
    )(table_grad, touched, first, second, ffn, attn, ent, bias, words_low, ents_low, words_grad)


def on_device(
    word_states,
    segments,
    entity_ids,
    entity_pos,
    ent_table,
    first_moment,
    second_moment,
    ent_proj,
    pos_table,
    query_weight,
    query_bias,
    key_weight,
    key_bias,
    value_weight,
    value_bias,
    out_weight,
    out_bias,
    norm_gain,
    norm_shift,
    up_weight,
    up_bias,
    down_weight,
    down_bias,
    word_cot,
    ent_cot,
):
    n_dp = lax.axis_size("dp")
    nz = n_dp // 2
    width, ff = up_weight.shape
    all_words = segments.shape[1]
    words, word_cots, ent_cots, all_ids, rows = fetch(nz, word_states, word_cot, ent_cot, entity_ids, ent_table)
    ent_hidden, hidden_turned, query_words, query_ents, keys, values, probs, mixed = forward(
        words,
        rows,
        entity_pos,
        segments,
        ent_proj,
        pos_table,
        query_weight,
        query_bias,
        key_weight,
        key_bias,
        value_weight,
        value_bias,
    )
    ents = entity_ids.shape[1]
    word_out, ent_out, word_grad, ffn_sum, attn_sum, ent_sum, bias_sum, table_grad, touched = layer(
        nz, ent_table.shape[0], words, ent_hidden, mixed, out_weight, out_bias, norm_gain, norm_shift, up_weight, up_bias, down_weight, down_bias,
        word_cots, ent_cots, hidden_turned, query_words, query_ents, keys, values, probs, query_weight, key_weight, value_weight,
        rows, entity_pos, ent_proj, all_ids.reshape(-1, ents),
    )
    (table_grad, table_update, new_second, proj_grad, pos_grad, query_grad, key_grad, value_grad, out_grad, up_grad, down_grad,
     query_bias_grad, gain_grad, shift_grad, key_bias_grad, value_bias_grad, out_bias_grad, down_bias_grad, up_bias_grad,
     word_out, ent_out, word_grad,
    ) = last(
        n_dp, ff, all_words, table_grad, touched, first_moment, second_moment, ffn_sum, attn_sum, ent_sum, bias_sum, word_out, ent_out, word_grad
    )
    return (
        word_out,
        ent_out,
        word_grad,
        proj_grad,
        pos_grad,
        query_grad,
        query_bias_grad,
        key_grad,
        key_bias_grad,
        value_grad,
        value_bias_grad,
        out_grad,
        out_bias_grad,
        gain_grad,
        shift_grad,
        up_grad,
        up_bias_grad,
        down_grad,
        down_bias_grad,
        table_grad,
        table_update,
        new_second,
    )


def solution(mesh):
    return jax.shard_map(
        on_device,
        mesh=mesh,
        in_specs=(
            P("dp", "seq", None),
            P("dp", None),
            P("dp", None),
            P("dp", None),
            P(("dp", "seq"), None),
            P(("dp", "seq"), None),
            P(("dp", "seq"), None),
            P(),
            P(),
            P(),
            P(),
            P(),
            P(),
            P(),
            P(),
            P(),
            P(),
            P(),
            P(),
            P(),
            P(),
            P(),
            P(),
            P("dp", "seq", None),
            P("dp", "seq", None),
        ),
        out_specs=(
            P("dp", "seq", None),
            P("dp", "seq", None),
            P("dp", "seq", None),
            P("dp", None),
            P("dp", None),
            P(None, "dp", None),
            P(None, "dp"),
            P("dp", None),
            P("dp"),
            P("dp", None),
            P("dp"),
            P("dp", None),
            P("dp"),
            P(None, "dp"),
            P(None, "dp"),
            P("dp", None),
            P("dp"),
            P("dp", None),
            P("dp"),
            P(("dp", "seq"), None),
            P(("dp", "seq"), None),
            P(("dp", "seq"), None),
        ),
        check_vma=False,
    )
```

```python
import functools
import math

import jax
import jax.numpy as jnp
from jax import lax
from jax.experimental import pallas as pl
from jax.experimental.pallas import tpu as pltpu
from jax.sharding import PartitionSpec as P

HEADS = 12
HEAD = 64
LANES = 128
MESH = pl.DeviceIdType.MESH
LOW = jnp.bfloat16
F32 = jnp.float32
VMEM_BYTES = 125 * 512 * 1024

norm_eps = 1e-05
beta_one = 0.9
beta_two = 0.98
adam_eps = 1e-06
adam_step = 10.0
masked_score = -1e30


def dot(left, right):
    return jnp.dot(left, right, preferred_element_type=F32)


def dot_rows(left, right):
    return lax.dot_general(left, right, (((1,), (1,)), ((), ())), preferred_element_type=F32)


def dot_columns(left, right):
    return lax.dot_general(left, right, (((0,), (0,)), ((), ())), preferred_element_type=F32)


def span(start, size, unit):
    if isinstance(start, int):
        return pl.ds(start, size)
    return pl.ds(pl.multiple_of(start, unit), size)


def padded(rows):
    return -(-rows // 16) * 16


def loop(count, body, carry=0, unroll=1):
    def steps(i, carried):
        for k in range(unroll):
            carried = body(i * unroll + k, carried)
        return carried

    return lax.fori_loop(0, count // unroll, steps, carry)


class Place:
    def __init__(self, nz):
        self.dp, self.seq = lax.axis_index("dp"), lax.axis_index("seq")
        self.z, self.x = self.dp // 2, self.dp % 2
        self.y, self.core = self.seq // 2, self.seq % 2
        self.nz = nz
        self.other_core = (self.dp, self.y * 2 + 1 - self.core)
        self.other_y = (self.dp, (1 - self.y) * 2 + self.core)
        self.diagonal = (self.dp, (1 - self.y) * 2 + 1 - self.core)
        self.other_x = (self.z * 2 + 1 - self.x, self.seq)
        self.ahead = [(((self.z + k) % nz) * 2 + self.x, self.seq) for k in range(1, nz)]

    def z_ahead(self, k):
        return (self.z + k) % self.nz


def meet(partners):
    barrier = pltpu.get_barrier_semaphore()
    for partner in partners:
        pl.semaphore_signal(barrier, inc=1, device_id=partner, device_id_type=MESH)
    pl.semaphore_wait(barrier, len(partners))


class Remote:
    def __init__(self, copies, number, src, dst, device):
        self.copies, self.number, self.src, self.dst, self.device = copies, number, src, dst, device
        self.open = True

    def make(self, landing=False):
        return pltpu.make_async_remote_copy(
            src_ref=self.dst() if landing else self.src(),
            dst_ref=self.dst(),
            send_sem=self.copies.send_sem.at[self.number],
            recv_sem=self.copies.recv_sem.at[self.number],
            device_id=self.device,
            device_id_type=MESH,
        )

    def wait_recv(self):
        self.make(landing=True).wait_recv()

    def wait_send(self):
        if self.open:
            self.make().wait_send()
        self.open = False


class Local:
    def __init__(self, copies, number, src, dst):
        self.copies, self.number, self.src, self.dst = copies, number, src, dst

    def make(self):
        return pltpu.make_async_copy(self.src(), self.dst(), self.copies.local_sem.at[self.number])

    def wait(self):
        self.make().wait()


class Copies:
    def __init__(self, send_sem, recv_sem, local_sem):
        self.send_sem, self.recv_sem, self.local_sem = send_sem, recv_sem, local_sem
        self.local_count = 0
        self.sent = []

    def send(self, src, dst, device):
        copy = Remote(self, len(self.sent), src, dst, device)
        copy.make().start()
        self.sent.append(copy)
        return copy

    def local(self, src, dst):
        copy = Local(self, self.local_count, src, dst)
        self.local_count += 1
        copy.make().start()
        return copy

    def finish(self):
        for copy in self.sent:
            copy.wait_send()


def copy_semaphores(remote, local):
    return [
        pltpu.SemaphoreType.DMA((remote,)),
        pltpu.SemaphoreType.DMA((remote,)),
        pltpu.SemaphoreType.DMA((local,)),
    ]


ANY = pl.BlockSpec(memory_space=pl.ANY)
IN_VMEM = pl.BlockSpec(memory_space=pltpu.VMEM)


def call(kernel, outs, in_specs, out_specs, scratch, name, collective_id=None):
    params = {"vmem_limit_bytes": VMEM_BYTES}
    if collective_id is not None:
        params.update(collective_id=collective_id, has_side_effects=True)
    return pl.pallas_call(
        kernel,
        out_shape=[jax.ShapeDtypeStruct(shape, dtype) for shape, dtype in outs],
        in_specs=in_specs,
        out_specs=out_specs,
        scratch_shapes=scratch,
        compiler_params=pltpu.CompilerParams(**params),
        name=name,
    )


def fetch_kernel(nz, words, word_cot, ent_cot, ids, table, all_words, word_cots, ent_cots, all_ids, rows_out, *scratch):
    table_full, table_low, picked, answers, held, from_core, from_x, from_z, from_y, ids_here = scratch[:10]
    copies = Copies(*scratch[10:])
    place = Place(nz)
    z, x, y, core = place.z, place.x, place.y, place.core
    n_dp = 2 * nz
    word_here, ent_here = words.shape[1], ent_cot.shape[1]
    ents = ids.shape[1]
    dp_others = [((place.dp + k) % n_dp, place.seq) for k in range(1, n_dp)]
    meet([place.other_core, place.other_y, place.diagonal] + dp_others)
    whole_table = copies.local(lambda: table, lambda: table_full)
    ids_here[place.dp] = ids[...]
    id_copies = [copies.send(lambda: ids, lambda: ids_here.at[place.dp], device) for device in dp_others]
    quarter = span(place.seq * word_here, word_here, 128)
    word_copies = [
        copies.send(lambda: words.at[1 - core], lambda: all_words.at[quarter], place.diagonal),
        copies.send(lambda: words.at[core], lambda: all_words.at[quarter], place.other_y),
        copies.send(lambda: words.at[1 - core], lambda: all_words.at[quarter], place.other_core),
        copies.send(lambda: word_cot.at[1 - core], lambda: word_cots.at[span(core * word_here, word_here, 128)], place.other_core),
        copies.send(lambda: ent_cot.at[1 - core], lambda: ent_cots.at[span(core * ent_here, ent_here, 32)], place.other_core),
    ]
    all_words[quarter] = words[core]
    word_cots[span(core * word_here, word_here, 128)] = word_cot[core]
    ent_cots[span(core * ent_here, ent_here, 32)] = ent_cot[core]
    whole_table.wait()
    rows_dev = table.shape[0]

    def narrow(i, _):
        where = span(i * 128, 128, 128)
        table_low[where] = table_full[where].astype(LOW)
        return 0

    loop(rows_dev // 128, narrow)
    for copy in id_copies:
        copy.wait_recv()
    all_ids[...] = ids_here[...]
    base = (place.dp * 4 + place.seq) * rows_dev
    tiles = rows_dev // LANES

    def look_up(zz):
        for g in range(4):
            asked = ids_here[zz * 2 + g // 2, pl.ds(g % 2, 1), :] - base
            column = jnp.transpose(jnp.broadcast_to(asked, (ents, ents)))
            lane = lax.broadcasted_iota(jnp.int32, (ents, LANES), 1)
            low_hit = jnp.where((column & (LANES - 1)) == lane, 1.0, 0.0).astype(LOW)
            high = jnp.clip(column >> 7, -1, tiles).astype(F32).astype(LOW)
            for j in range(tiles):
                hit = jnp.where(high == jnp.asarray(j, LOW), low_hit, jnp.zeros_like(low_hit))
                picked[pl.ds(g * ents, ents), pl.ds(j * LANES, LANES)] = hit
        answer = dot(picked[...], table_low[...]).astype(LOW)
        answers[zz] = answer.reshape(2, 2, ents, answer.shape[-1])

    order = [place.z_ahead(k + 1) for k in range(nz)]
    core_copies, x_copies, z_copies = [], [], []

    def core_send(zz):
        return copies.send(lambda: answers.at[zz, :, 1 - core], lambda: from_core.at[zz], place.other_core)

    def after_core(k):
        zz = order[k]
        core_copies[k].wait_recv()
        held[zz] = answers[zz, :, core] + from_core[zz]
        x_copies.append(copies.send(lambda: held.at[zz, 1 - x], lambda: from_x.at[zz], place.other_x))

    def after_x(k):
        zz = order[k]
        x_copies[k].wait_recv()
        held[zz, x] = held[zz, x] + from_x[zz]
        if k < nz - 1:
            z_copies.append(copies.send(lambda: held.at[zz, x], lambda: from_z.at[k], place.ahead[k]))

    for k in range(nz + 2):
        if k < nz:
            look_up(order[k])
            core_copies.append(core_send(order[k]))
        if 0 <= k - 1 < nz:
            after_core(k - 1)
        if 0 <= k - 2:
            after_x(k - 2)
    total = held[z, x]
    for k in range(nz - 1):
        z_copies[k].wait_recv()
        total = total + from_z[k]
    from_y[0] = total
    y_copy = copies.send(lambda: from_y.at[0], lambda: from_y.at[1], place.other_y)
    y_copy.wait_recv()
    rows_out[...] = from_y[0] + from_y[1]
    for copy in word_copies:
        copy.wait_recv()
    copies.finish()


def fetch(nz, words, word_cot, ent_cot, ids, table):
    _, word_here, width = words.shape
    ent_here, ents, (rows_dev, edim) = ent_cot.shape[1], ids.shape[1], table.shape
    n_dp = 2 * nz
    return call(
        functools.partial(fetch_kernel, nz),
        [
            ((4 * word_here, width), LOW),
            ((2 * word_here, width), LOW),
            ((2 * ent_here, width), LOW),
            ((n_dp, 2, ents), jnp.int32),
            ((ents, edim), LOW),
        ],
        [IN_VMEM] * 4 + [ANY],
        [IN_VMEM] * 5,
        [
            pltpu.VMEM((rows_dev, edim), F32),
            pltpu.VMEM((rows_dev, edim), LOW),
            pltpu.VMEM((4 * ents, rows_dev), LOW),
            pltpu.VMEM((nz, 2, 2, ents, edim), LOW),
            pltpu.VMEM((nz, 2, ents, edim), LOW),
            pltpu.VMEM((nz, 2, ents, edim), LOW),
            pltpu.VMEM((nz, ents, edim), LOW),
            pltpu.VMEM((nz - 1, ents, edim), LOW),
            pltpu.VMEM((2, ents, edim), LOW),
            pltpu.VMEM((n_dp, 2, ents), jnp.int32),
        ]
        + copy_semaphores(n_dp + 4 + 3 * nz + 2, 1),
        "fetch",
        1,
    )(words, word_cot, ent_cot, ids, table)


def lane_mask(rows, head):
    lane = lax.broadcasted_iota(jnp.int32, (rows, LANES), 1)
    return (lane >= head * HEAD) & (lane < (head + 1) * HEAD)


def row_of(vector):
    return vector[...].astype(F32).reshape(1, vector.shape[0])


def own_half(vector, y):
    row = row_of(vector)
    half = row.shape[1] // 2
    return jnp.where(y == 0, row[:, :half], row[:, half:])


def as_column(row):
    parts = [
        jnp.transpose(jnp.broadcast_to(row[:, i : i + LANES], (LANES, LANES)))
        for i in range(0, row.shape[1], LANES)
    ]
    return jnp.concatenate(parts, axis=0) if len(parts) > 1 else parts[0]


class Engine:
    RATES = {"core": 300e3, "x": 52e3, "y": 52e3, "z": 13e3}
    LATENCY = 2.0

    def __init__(self):
        self.clock, self.free, self.streams = 0.0, {}, []

    def transfer(self, link, size):
        start = max(self.clock, self.free.get(link, 0.0))
        self.free[link] = start + size / self.RATES[link]
        return self.free[link] + self.LATENCY

    def add(self, steps):
        self.streams.append([self.clock, list(steps)])
        self.poll()

    def run(self, stream):
        self.clock = max(self.clock, stream[0])
        ready = stream[1].pop(0)()
        stream[0] = self.clock if ready is None else ready

    def next(self):
        live = [stream for stream in self.streams if stream[1]]
        return min(live, key=lambda stream: stream[0]) if live else None

    def poll(self):
        while (stream := self.next()) is not None and stream[0] <= self.clock:
            self.run(stream)

    def work(self, time):
        self.clock += time
        self.poll()

    def drain(self):
        while (stream := self.next()) is not None:
            self.run(stream)


def blocks_of(rows):
    for size in (96, 64, 48, 32):
        if rows % size == 0:
            return size
    return 16


def add_blocks(engine, target, parts, leading, rows, columns):
    size = blocks_of(rows)
    count = rows // size

    def block(i, _):
        lead, row = i // count, (i % count) * size
        where = span(row, size, 16)
        if len(parts) == 2:
            value = parts[0](lead, where) + parts[1](lead, where)
        else:
            value = parts[0](lead, where).astype(F32)
            for part in parts[1:]:
                value = value + part(lead, where).astype(F32)
            value = value.astype(LOW)
        target(lead, where, value)
        return 0

    loop(leading * count, block)
    engine.clock += 0.3 + leading * rows * columns / 1e6


class Job:
    def __init__(self, grads, reduced, base, size, order, columns):
        self.grads, self.reduced, self.base, self.size, self.order, self.columns = grads, reduced, base, size, order, columns
        self.half = size // 2
        self.part = size // 4 if order == "yxz" else size // 2

    def scratch(self, nz):
        shapes = [(nz, 2, self.half, self.columns)]
        if self.order == "yxz":
            shapes.append((nz, 2, self.part, self.columns))
        elif self.order == "xzy":
            shapes.append((2, self.part, self.columns))
        shapes += [(nz, self.part, self.columns), (nz - 1, self.part, self.columns)]
        return [pltpu.VMEM(shape, LOW) for shape in shapes]

    def remote_count(self, nz):
        return 1 + (1 if self.order != "xz" else 0) + 1 + (nz - 1) + 1 + 1

    def prepare(self, engine, place, copies, scratch):
        nz, z, x, y, core = place.nz, place.z, place.x, place.y, place.core
        base, half, part, order, columns = self.base, self.half, self.part, self.order, self.columns
        held = self.grads.at[:, :, span(base + core * half, half, 16)]
        from_core = scratch[0]
        from_y = scratch[1] if order != "xz" else None
        from_x, from_z = scratch[-2:]
        live = {}
        row_bytes = 2 * columns
        theirs = span(base + (1 - core) * half, half, 16)
        mine = span(base + core * half, half, 16)
        own_rows = span(y * part, part, 16) if order == "yxz" else pl.ds(0, part)
        final_rows = span(base + core * half + (y * part if order == "yxz" else 0), part, 16)

        def start():
            live["core"] = copies.send(lambda: self.grads.at[:, :, theirs], lambda: from_core, place.other_core)
            return engine.transfer("core", 2 * nz * half * row_bytes)

        def send_x():
            live["x"] = copies.send(lambda: held.at[:, 1 - x, own_rows], lambda: from_x, place.other_x)
            return engine.transfer("x", nz * part * row_bytes)

        def after_core():
            live["core"].wait_recv()

            def put(i, where, value):
                held[i // 2, i % 2, where] = value

            add_blocks(
                engine,
                put,
                [lambda i, where: held[i // 2, i % 2, where], lambda i, where: from_core[i // 2, i % 2, where]],
                2 * nz,
                half,
                columns,
            )
            if order == "yxz":
                live["y"] = copies.send(
                    lambda: held.at[:, :, span((1 - y) * part, part, 16)], lambda: from_y, place.other_y
                )
                return engine.transfer("y", 2 * nz * part * row_bytes)
            return send_x()

        def shifted(where):
            return span(y * part + where.start, where.size, 16) if order == "yxz" else where

        def after_y():
            live["y"].wait_recv()

            def put(i, where, value):
                held[i // 2, i % 2, shifted(where)] = value

            add_blocks(
                engine,
                put,
                [lambda i, where: held[i // 2, i % 2, shifted(where)], lambda i, where: from_y[i // 2, i % 2, where]],
                2 * nz,
                part,
                columns,
            )
            return send_x()

        def send_z(k):
            return copies.send(
                lambda: held.at[place.z_ahead(k + 1), x, own_rows], lambda: from_z.at[k], place.ahead[k]
            )

        def after_x():
            live["x"].wait_recv()

            def put(i, where, value):
                held[i, x, shifted(where)] = value

            add_blocks(
                engine,
                put,
                [lambda i, where: held[i, x, shifted(where)], lambda i, where: from_x[i, where]],
                nz,
                part,
                columns,
            )
            live["z"] = [send_z(k) for k in range(nz - 1)]
            return engine.transfer("z", part * row_bytes)

        def after_z():
            for copy in live["z"]:
                copy.wait_recv()

            def put(i, where, value):
                if order == "yxz":
                    self.reduced[span(base + core * half + y * part + where.start, where.size, 16)] = value
                elif order == "xz":
                    self.reduced[y, span(base + core * half + where.start, where.size, 16)] = value
                else:
                    from_y[0, where] = value

            def parts(k):
                return lambda i, where: from_z[k, where]

            add_blocks(
                engine,
                put,
                [lambda i, where: held[z, x, shifted(where)]] + [parts(k) for k in range(nz - 1)],
                1,
                part,
                columns,
            )
            if order == "xzy":
                live["y2"] = copies.send(lambda: from_y.at[0], lambda: from_y.at[1], place.other_y)
            else:
                view = lambda: self.reduced.at[final_rows] if order == "yxz" else self.reduced.at[y, final_rows]
                live["y2"] = copies.send(view, view, place.other_y)
            return engine.transfer("y", part * row_bytes)

        def after_gather():
            live["y2"].wait_recv()
            if order == "xzy":

                def put(i, where, value):
                    self.reduced[span(base + core * half + where.start, where.size, 16)] = value

                add_blocks(
                    engine, put, [lambda i, where: from_y[0, where], lambda i, where: from_y[1, where]], 1, part, columns
                )
            view = lambda: self.reduced.at[:, mine] if order == "xz" else self.reduced.at[mine]
            live["core2"] = copies.send(view, view, place.other_core)
            return engine.transfer("core", 2 * half * row_bytes)

        def end():
            live["core2"].wait_recv()

        middle_steps = [after_core, after_y, after_x] if order == "yxz" else [after_core, after_x]
        self.steps = [start] + middle_steps + [after_z, after_gather, end]


def lane_mean(value):
    return jnp.mean(value, axis=-1, keepdims=True)


def column_sum(value):
    return jnp.sum(value, axis=0, keepdims=True)


ROW_BLOCK = 32


def ffn_plan(n_dp, width, ff):
    down_rows, row_pad = ff // n_dp, padded(width // n_dp)
    size = 128 if down_rows % 128 == 0 else 32
    order = "yxz" if size % 64 == 0 else "xzy"
    plan = [(base, size, order) for base in range(0, down_rows, size)]
    base = down_rows
    for pair in range(ff // width // 2):
        order = "yxz" if row_pad % 32 == 0 else "xzy"
        plan.append((base, 2 * row_pad, order))
        base += 2 * row_pad
    plan.append((base, row_pad, "xzy"))
    return plan


def layer_kernel(
    nz, plan, words, segments, pos_table, query_bias, key_bias, value_bias, out_weight, out_bias, gains, shifts, up_weight, up_bias, down_weight, down_bias, word_cots, ent_cots,
    query_weight, key_weight, value_weight, rows, ent_pos, ent_proj, ids,
    word_out, ent_out, word_grad, ffn_reduced, attn_reduced, ent_reduced, bias_out, table_grad, touched,
    hidden_turned_in, query_words_in, query_ents_in, keys_in, values_in, probs_in, *scratch,
):
    (from_y_mixed, grad_mixed, grad_one, given, ffn_sum, attn_sum, ent_sum, bias_held, bias_from, all_rows, bias_heads, bias_middle,
     ffn_grads, grad_mixed_here, row_parts, mixed, ent_keep) = scratch[:17]
    copies = Copies(*scratch[-3:])
    engine = Engine()
    place = Place(nz)
    z, x, y, core = place.z, place.x, place.y, place.core
    n_dp = 2 * nz
    tokens, half = mixed.shape
    width = 2 * half
    ents = rows.shape[0]
    all_words = tokens - ents
    word_half, ent_half = all_words // 2, ents // 2
    part_tokens = tokens // 2
    ff = up_weight.shape[1]
    parts = ff // width
    row_part, row_pad, down_rows = width // n_dp, padded(width // n_dp), ff // n_dp
    meet([place.other_core, place.other_y, place.other_x] + place.ahead)

    jobs = {"ffn": [], "attn": [], "ent": []}

    def make_jobs(names, sources):
        at = 17
        for name, number, base, size, order, columns in plan:
            grads, reduced = sources.get(name, (None, None))
            if name == "attn" and grads is not None:
                grads, reduced = grads.at[number], reduced.at[number]
            job = Job(grads, reduced, base, size, order, columns)
            used = len(job.scratch(nz))
            if name in names:
                job.prepare(engine, place, copies, scratch[at : at + used])
                jobs[name].append(job)
            at += used

    make_jobs(["ffn"], {"ffn": (ffn_grads, ffn_sum)})

    def token_rows(side):
        return span(side * word_half, word_half, LANES), span(all_words + side * ent_half, ent_half, 64)

    mine, theirs = token_rows(y), token_rows(1 - y)
    own_columns, other_columns = span(y * half, half, LANES), span((1 - y) * half, half, LANES)
    word_part, ent_part = pl.ds(0, word_half), pl.ds(word_half, ent_half)
    mixed_copies = []
    scale = 1.0 / math.sqrt(HEAD)
    tiles = tokens // LANES

    def attend_phase(
        hidden_low, hidden_turned, query_words, query_ents, keys, values, probs, query_here, key_here, value_here, pos_here, values_turned, mask,
    ):
        weight_copies = [
            copies.local(lambda: words, lambda: hidden_low.at[pl.ds(0, all_words)]),
            copies.local(lambda: pos_table, lambda: pos_here),
            copies.local(lambda: query_weight.at[:, :, own_columns], lambda: query_here),
            copies.local(lambda: key_weight.at[:, own_columns], lambda: key_here),
            copies.local(lambda: value_weight.at[:, own_columns], lambda: value_here),
        ]
        position = as_column(ent_pos[pl.ds(core, 1), :])
        picks = []
        for j in range(all_words // LANES):
            number = lax.broadcasted_iota(jnp.int32, (ents, LANES), 1) + j * LANES
            picks.append(jnp.where(position == number, 1.0, 0.0))
        pick = jnp.concatenate(picks, axis=1)
        word_seg = segments[pl.ds(core, 1), :].astype(F32)
        ent_seg = jnp.sum(pick * word_seg, axis=1, keepdims=True)
        for copy in weight_copies[:2]:
            copy.wait()
        ent_hidden = dot(rows[...], ent_proj[...]) + dot(pick.astype(LOW), pos_here[...])
        ent_keep[...] = jnp.where(y == 0, ent_hidden[:ent_half], ent_hidden[ent_half:])
        hidden_low[all_words:] = ent_hidden.astype(LOW)
        ent_row = jnp.transpose(jnp.broadcast_to(ent_seg, (ents, LANES)))[:1]
        seg_row = jnp.concatenate([word_seg, ent_row], axis=1)
        seg_column = jnp.concatenate([as_column(word_seg), jnp.broadcast_to(ent_seg, (ents, LANES))], axis=0)
        for j in range(tiles):
            here = slice(j * LANES, (j + 1) * LANES)
            mask[:, here] = jnp.where(seg_column == seg_row[:, here], 0.0, masked_score)
        query_b = query_bias[:, own_columns].astype(F32)
        for copy in weight_copies[2:]:
            copy.wait()
        word_low, ent_low = hidden_low[:all_words], hidden_low[all_words:]
        query_words[:all_words] = (dot(word_low, query_here[0]) + query_b[0:1]).astype(LOW)
        query_ents[:all_words] = (dot(word_low, query_here[1]) + query_b[1:2]).astype(LOW)
        query_words[all_words:] = (dot(ent_low, query_here[2]) + query_b[2:3]).astype(LOW)
        query_ents[all_words:] = (dot(ent_low, query_here[3]) + query_b[3:4]).astype(LOW)
        keys[...] = (dot(hidden_low[...], key_here[...]) + own_half(key_bias, y)).astype(LOW)
        value = dot(hidden_low[...], value_here[...]) + own_half(value_bias, y)
        values[...] = value.astype(LOW)
        values_turned[...] = jnp.transpose(value).astype(LOW)
        spills = [
            copies.local(lambda: query_words, lambda: query_words_in),
            copies.local(lambda: query_ents, lambda: query_ents_in),
            copies.local(lambda: keys, lambda: keys_in),
            copies.local(lambda: values, lambda: values_in),
        ]
        for pair in range(half // LANES):
            lanes = slice(pair * LANES, (pair + 1) * LANES)
            key, turned = keys[:, lanes], values_turned[lanes, :]
            row = lax.broadcasted_iota(jnp.int32, (LANES, tokens), 0)
            own_key, own_turned = [], []
            for head in range(2):
                own_key.append(jnp.where(lane_mask(tokens, head), key, jnp.zeros_like(key)))
                own_rows = (row >= head * HEAD) & (row < (head + 1) * HEAD)
                own_turned.append(jnp.where(own_rows, turned, jnp.zeros_like(turned)))
            for i in range(tiles):
                here = slice(i * LANES, (i + 1) * LANES)
                query_w, query_e = query_words[here, lanes], query_ents[here, lanes]
                part_sum = None
                for head in range(2):
                    raw = jnp.concatenate(
                        [dot_rows(own_key[head][:all_words], query_w), dot_rows(own_key[head][all_words:], query_e)], axis=0
                    )
                    score = raw * scale + mask[:, here]
                    weight = jnp.exp(score - jnp.max(score, axis=0, keepdims=True))
                    prob = (weight * (1.0 / jnp.sum(weight, axis=0, keepdims=True))).astype(LOW)
                    probs[pair * 2 + head, :, here] = prob
                    part = dot(own_turned[head], prob)
                    part_sum = part if part_sum is None else part_sum + part
                mixed[here, lanes] = jnp.transpose(part_sum).astype(LOW)
            heads = pl.ds(pair * 2, 2)
            mixed_copies.extend([
                copies.send(
                    lambda lanes=lanes: mixed.at[theirs[0], lanes], lambda lanes=lanes: from_y_mixed.at[word_part, lanes], place.other_y
                ),
                copies.send(
                    lambda lanes=lanes: mixed.at[theirs[1], lanes], lambda lanes=lanes: from_y_mixed.at[ent_part, lanes], place.other_y
                ),
            ])
            spills.append(copies.local(lambda heads=heads: probs.at[heads], lambda heads=heads: probs_in.at[heads]))
        for i in range(width // LANES):
            here = slice(i * LANES, (i + 1) * LANES)
            hidden_turned[here, :] = jnp.transpose(hidden_low[:, here].astype(F32)).astype(LOW)
        spills.append(copies.local(lambda: hidden_turned, lambda: hidden_turned_in))
        for copy in spills:
            copy.wait()

    pl.run_scoped(
        attend_phase,
        pltpu.VMEM((tokens, width), LOW),
        pltpu.VMEM((width, tokens), LOW),
        pltpu.VMEM((tokens, half), LOW),
        pltpu.VMEM((tokens, half), LOW),
        pltpu.VMEM((tokens, half), LOW),
        pltpu.VMEM((tokens, half), LOW),
        pltpu.VMEM((HEADS // 2, tokens, tokens), LOW),
        pltpu.VMEM((4, width, half), LOW),
        pltpu.VMEM((width, half), LOW),
        pltpu.VMEM((width, half), LOW),
        pltpu.VMEM((all_words, width), LOW),
        pltpu.VMEM((half, tokens), LOW),
        pltpu.VMEM((tokens, tokens), F32),
    )
    out_copies, mixed_back = [], []

    def forward_phase(
        out_here, up_here, down_here, word_here, mixed_full, work, normed_low, normal_one, inverse_one,
        act, slope, output, grad_two, grad_two_low, grad_one_low, normed_turned,
    ):
        cot, grad_up_low = output, slope
        weight_copies = [
            copies.local(lambda: out_weight, lambda: out_here),
            copies.local(lambda: words.at[mine[0]], lambda: word_here),
            copies.local(lambda: up_weight, lambda: up_here),
            copies.local(lambda: down_weight, lambda: down_here),
            copies.local(lambda: word_cots, lambda: cot.at[word_part]),
            copies.local(lambda: ent_cots, lambda: cot.at[ent_part]),
        ]
        gain, shift = gains[...].astype(F32), shifts[...].astype(F32)
        out_b, down_b, up_b = row_of(out_bias), row_of(down_bias), row_of(up_bias)
        mixed_full[word_part, own_columns] = mixed[mine[0]]
        mixed_full[ent_part, own_columns] = mixed[mine[1]]
        for copy in weight_copies[:2]:
            copy.wait()
        for copy in mixed_copies:
            copy.wait_recv()
        mixed_full[:, other_columns] = from_y_mixed[...]
        work[...] = dot(mixed_full[...], out_here[...])

        def norm_one(residual):
            def step(i, _):
                rows = span(residual[1] + i * ROW_BLOCK, ROW_BLOCK, ROW_BLOCK)
                value = residual[0][span(i * ROW_BLOCK, ROW_BLOCK, ROW_BLOCK)].astype(F32) + (work[rows] + out_b)
                center = value - lane_mean(value)
                inverse = lax.rsqrt(lane_mean(center * center) + norm_eps)
                normal = center * inverse
                result = normal * gain[0:1] + shift[0:1]
                normal_one[rows] = normal
                inverse_one[rows] = jnp.broadcast_to(inverse, (ROW_BLOCK, LANES))
                normed_low[rows] = result.astype(LOW)
                return 0

            return step

        loop(word_half // ROW_BLOCK, norm_one((word_here, 0)), 0, 2)
        loop(ent_half // ROW_BLOCK, norm_one((ent_keep, word_half)), 0, 2)
        weight_copies[2].wait()
        for j in range(parts):
            columns = slice(j * width, (j + 1) * width)
            work[...] = dot(normed_low[...], up_here[:, columns]) + up_b[:, columns]

            def gelu(i, _):
                rows = span(i * ROW_BLOCK, ROW_BLOCK, ROW_BLOCK)
                value = work[rows]
                below = 0.5 * (1.0 + lax.erf(value * (1.0 / math.sqrt(2.0))))
                density = jnp.exp(-0.5 * value * value) * (1.0 / math.sqrt(2.0 * math.pi))
                act[rows, columns] = (value * below).astype(LOW)
                slope[rows, columns] = (below + value * density).astype(LOW)
                return 0

            loop(part_tokens // ROW_BLOCK, gelu)
        normed_turned[...] = jnp.transpose(normed_low[...].astype(F32)).astype(LOW)
        for copy in weight_copies[3:]:
            copy.wait()
        work[...] = dot(act[...], down_here[...])

        def norm_two(i, sums):
            rows = span(i * ROW_BLOCK, ROW_BLOCK, ROW_BLOCK)
            value = (normal_one[rows] * gain[0:1] + shift[0:1]) + (work[rows] + down_b)
            center = value - lane_mean(value)
            inverse = lax.rsqrt(lane_mean(center * center) + norm_eps)
            normal = center * inverse
            cotangent = cot[rows].astype(F32)
            output[rows] = (normal * gain[1:2] + shift[1:2]).astype(LOW)
            scaled = cotangent * gain[1:2]
            result = inverse * (scaled - lane_mean(scaled) - normal * lane_mean(scaled * normal))
            grad_two[rows] = result
            grad_two_low[rows] = result.astype(LOW)
            return (
                sums[0] + column_sum(cotangent * normal),
                sums[1] + column_sum(cotangent),
                sums[2] + column_sum(result),
            )

        nothing = jnp.zeros((1, width), F32)
        gain_two, shift_two, down_sum = loop(part_tokens // ROW_BLOCK, norm_two, (nothing, nothing, nothing), 2)
        quarter, ent_quarter = word_half // 2, ent_half // 2
        out_copies.extend([
            copies.send(
                lambda: output.at[span((1 - core) * quarter, quarter, LANES)], lambda: word_out.at[core], place.other_core
            ),
            copies.send(
                lambda: output.at[span(word_half + (1 - core) * ent_quarter, ent_quarter, 32)],
                lambda: ent_out.at[core],
                place.other_core,
            ),
        ])
        out_local = [
            copies.local(lambda: output.at[span(core * quarter, quarter, LANES)], lambda: word_out.at[core]),
            copies.local(
                lambda: output.at[span(word_half + core * ent_quarter, ent_quarter, 32)], lambda: ent_out.at[core]
            ),
        ]
        engine.clock = 0.0
        engine.free = {}
        def put(base, value):
            ffn_grads[:, :, pl.ds(base, row_part)] = value.astype(LOW).reshape(nz, 2, row_part, width)

        def down_block(job):
            if down_rows % 128:
                per = width // down_rows
                for j in range(parts):
                    value = dot_columns(act[:, j * width : (j + 1) * width], grad_two_low[...])
                    value = value.reshape(per, down_rows, width)[:, job.base : job.base + job.size].astype(LOW)
                    for d in range(per):
                        slab = j * per + d
                        ffn_grads[slab // 2, slab % 2, pl.ds(job.base, job.size)] = value[d]
            else:
                for slab in range(n_dp):
                    start = slab * down_rows + job.base
                    value = dot_columns(act[:, start : start + job.size], grad_two_low[...])
                    ffn_grads[slab // 2, slab % 2, pl.ds(job.base, job.size)] = value.astype(LOW)
            engine.work(1.3)
            engine.add(job.steps)

        up_sums = []

        def grad_up(j):
            columns = slice(j * width, (j + 1) * width)
            work[...] = dot_rows(grad_two_low[...], down_here[columns, :])

            def grad_gelu(i, total_row):
                rows = span(i * ROW_BLOCK, ROW_BLOCK, ROW_BLOCK)
                value = work[rows] * slope[rows, columns].astype(F32)
                grad_up_low[rows, columns] = value.astype(LOW)
                return total_row + column_sum(value)

            up_sums.append(loop(part_tokens // ROW_BLOCK, grad_gelu, nothing, 2))
            engine.work(1.6)
            put(down_rows + j * row_pad, dot(normed_turned[...], grad_up_low[:, columns]))
            engine.work(0.9)

        downs = [job for job in jobs["ffn"] if job.base < down_rows]
        ups = [job for job in jobs["ffn"] if down_rows <= job.base][:-1]
        for job in downs:
            down_block(job)
        for j in range(parts):
            grad_up(j)
            if j % 2 == 1:
                engine.add(ups[j // 2].steps)
        work[...] = dot_rows(grad_up_low[...], up_here[...])
        engine.work(2.0)

        def back_one(i, sums):
            rows = span(i * ROW_BLOCK, ROW_BLOCK, ROW_BLOCK)
            upper = grad_two[rows] + work[rows]
            normal = normal_one[rows]
            inverse = inverse_one[rows, 0:1]
            scaled = upper * gain[0:1]
            result = inverse * (scaled - lane_mean(scaled) - normal * lane_mean(scaled * normal))
            grad_one[rows] = result
            grad_one_low[rows] = result.astype(LOW)
            return (
                sums[0] + column_sum(upper * normal),
                sums[1] + column_sum(upper),
                sums[2] + column_sum(result),
            )

        gain_one, shift_one, out_sum = loop(part_tokens // ROW_BLOCK, back_one, (nothing, nothing, nothing), 2)
        engine.work(1.0)
        grad_mixed_here[...] = dot_rows(grad_one_low[...], out_here[other_columns, :]).astype(LOW)
        mixed_back.extend([
            copies.send(lambda: grad_mixed_here.at[word_part], lambda: grad_mixed.at[mine[0]], place.other_y),
            copies.send(lambda: grad_mixed_here.at[ent_part], lambda: grad_mixed.at[mine[1]], place.other_y),
        ])
        engine.transfer("y", part_tokens * half * 2)
        own = dot_rows(grad_one_low[...], out_here[own_columns, :]).astype(LOW)
        grad_mixed[mine[0]] = own[:word_half]
        grad_mixed[mine[1]] = own[word_half:]
        engine.work(1.0)
        put(down_rows + parts * row_pad, dot_columns(mixed_full[...], grad_one_low[...]))
        engine.work(0.8)
        engine.add(jobs["ffn"][-1].steps)
        bias_rows = [out_sum, gain_one, gain_two, shift_one, shift_two] + up_sums + [down_sum]
        for i, row in enumerate(bias_rows):
            bias_middle[i : i + 1] = row
        for copy in out_copies:
            copy.wait_send()
        for copy in out_local:
            copy.wait()

    tall = lambda columns, dtype: pltpu.VMEM((part_tokens, columns), dtype)
    pl.run_scoped(
        forward_phase,
        pltpu.VMEM((width, width), LOW),
        pltpu.VMEM((width, ff), LOW),
        pltpu.VMEM((ff, width), LOW),
        pltpu.VMEM((word_half, width), LOW),
        tall(width, LOW),
        tall(width, F32),
        tall(width, LOW),
        tall(width, F32),
        tall(LANES, F32),
        tall(ff, LOW),
        tall(ff, LOW),
        tall(width, LOW),
        tall(width, F32),
        tall(width, LOW),
        tall(width, LOW),
        pltpu.VMEM((width, part_tokens), LOW),
    )
    live_words = {}

    def backward_phase(
        query_words, query_ents, keys, values, probs, query_here, key_here, value_here, keys_turned,
        grad_query_words, grad_query_ents, grad_keys, grad_values, hidden_turned, grad_hidden, hits, attn_grads, ent_grads, table_here, touched_here,
    ):
        total = grad_one
        make_jobs(["attn", "ent"], {"attn": (attn_grads, attn_sum), "ent": (ent_grads, ent_sum)})
        columns = span(y * half, half, LANES)
        copies_in = [
            copies.local(lambda: values_in, lambda: values),
            copies.local(lambda: keys_in, lambda: keys),
            copies.local(lambda: query_words_in, lambda: query_words),
            copies.local(lambda: query_ents_in, lambda: query_ents),
        ]
        prob_copies = []
        for head in range(probs.shape[0]):
            prob_copies.append(
                copies.local(lambda head=head: probs_in.at[head], lambda head=head: probs.at[head])
            )
        hidden_copy = copies.local(lambda: hidden_turned_in, lambda: hidden_turned)
        weight_copies = [
            copies.local(lambda: query_weight.at[:, :, columns], lambda: query_here),
            copies.local(lambda: key_weight.at[:, columns], lambda: key_here),
            copies.local(lambda: value_weight.at[:, columns], lambda: value_here),
        ]
        for copy in copies_in:
            copy.wait()
        for i in range(half // LANES):
            lanes = slice(i * LANES, (i + 1) * LANES)
            keys_turned[lanes, :] = jnp.transpose(keys[:, lanes].astype(F32)).astype(LOW)
        for copy in mixed_back:
            copy.wait_recv()
        engine.work(2.0)
        def pair_products(pair):
            lanes = slice(pair * LANES, (pair + 1) * LANES)
            word_turned, ent_turned = hidden_turned[:, :all_words], hidden_turned[:, all_words:]
            products = [
                dot(word_turned, grad_query_words[:all_words, lanes]),
                dot(word_turned, grad_query_ents[:all_words, lanes]),
                dot(ent_turned, grad_query_words[all_words:, lanes]),
                dot(ent_turned, grad_query_ents[all_words:, lanes]),
                dot(hidden_turned[...], grad_keys[:, lanes]),
                dot(hidden_turned[...], grad_values[:, lanes]),
            ]
            for i, value in enumerate(products):
                attn_grads[pair, :, :, pl.ds(i * row_pad, row_part)] = value.astype(LOW).reshape(nz, 2, row_part, LANES)
            engine.work(1.5)
            engine.add(jobs["attn"][pair].steps)

        for pair in range(half // LANES):
            lanes = slice(pair * LANES, (pair + 1) * LANES)
            grad_query_w = jnp.zeros((LANES, tokens), F32)
            grad_query_e = jnp.zeros((LANES, tokens), F32)
            grad_key_w = jnp.zeros((all_words, LANES), F32)
            grad_key_e = jnp.zeros((ents, LANES), F32)
            grad_value = jnp.zeros((tokens, LANES), F32)
            for head in range(2):
                own = lane_mask(tokens, head)
                value = values[:, lanes]
                own_value = jnp.where(own, value, jnp.zeros_like(value))
                prob_copies[pair * 2 + head].wait()

                given_heads = grad_mixed[:, lanes]
                grad_scores = probs.at[pair * 2 + head]
                grad_value += dot(grad_scores[...], jnp.where(own, given_heads, jnp.zeros_like(given_heads)))
                for i in range(tiles):
                    where = slice(i * LANES, (i + 1) * LANES)
                    grad_prob = dot_rows(own_value, grad_mixed[where, lanes])
                    prob = grad_scores[:, where].astype(F32)
                    both = prob * grad_prob
                    grad_scores[:, where] = (both - prob * jnp.sum(both, axis=0, keepdims=True)).astype(LOW)
                engine.work(1.7)
                query_w, query_e = query_words[:, lanes], query_ents[:, lanes]
                grad_key_w += dot(grad_scores[:all_words], jnp.where(own, query_w, jnp.zeros_like(query_w)))
                grad_key_e += dot(grad_scores[all_words:], jnp.where(own, query_e, jnp.zeros_like(query_e)))
                row = lax.broadcasted_iota(jnp.int32, (LANES, tokens), 0)
                own_rows = (row >= head * HEAD) & (row < (head + 1) * HEAD)
                turned = keys_turned[lanes, :]
                turned = jnp.where(own_rows, turned, jnp.zeros_like(turned))
                grad_query_w += dot(turned[:, :all_words], grad_scores[:all_words])
                grad_query_e += dot(turned[:, all_words:], grad_scores[all_words:])
                engine.work(1.7)
            grad_query_w = jnp.transpose(grad_query_w) * scale
            grad_query_e = jnp.transpose(grad_query_e) * scale
            grad_key_w, grad_key_e = grad_key_w * scale, grad_key_e * scale
            sums = [
                column_sum(grad_query_w[:all_words]),
                column_sum(grad_query_e[:all_words]),
                column_sum(grad_query_w[all_words:]),
                column_sum(grad_query_e[all_words:]),
                column_sum(grad_key_w) + column_sum(grad_key_e),
                column_sum(grad_value),
            ]
            for i, sum_row in enumerate(sums):
                bias_heads[i : i + 1, lanes] = sum_row
            grad_query_words[:, lanes] = grad_query_w.astype(LOW)
            grad_query_ents[:, lanes] = grad_query_e.astype(LOW)
            grad_keys[:all_words, lanes] = grad_key_w.astype(LOW)
            grad_keys[all_words:, lanes] = grad_key_e.astype(LOW)
            grad_values[:, lanes] = grad_value.astype(LOW)
            engine.work(0.5)
            if pair == 0:
                hidden_copy.wait()
            if pair + 1 < half // LANES:
                pair_products(pair)

        for copy in weight_copies:
            copy.wait()
        ent_rows, word_rows = slice(all_words, tokens), slice(0, all_words)

        def hidden_part(here, first, second):
            grad_hidden[here] = (
                dot_rows(grad_keys[here], key_here[...])
                + dot_rows(grad_values[here], value_here[...])
                + dot_rows(grad_query_words[here], query_here[first])
                + dot_rows(grad_query_ents[here], query_here[second])
            ).astype(LOW)

        hidden_part(ent_rows, 2, 3)
        own_ents = lax.broadcasted_iota(jnp.int32, (ents, width), 0) // ent_half == y
        twice = jnp.concatenate([grad_one[word_half:], grad_one[word_half:]], axis=0)
        ent_sum_part = grad_hidden[ent_rows].astype(F32) + jnp.where(own_ents, twice, 0.0)
        row_parts[0] = dot_rows(ent_sum_part.astype(LOW), ent_proj[...]).astype(LOW)
        rows_copy = copies.send(lambda: row_parts.at[0], lambda: row_parts.at[1], place.other_y)
        row_bytes = ents * ent_proj.shape[0] * 2
        rows_ready = engine.transfer("y", row_bytes)
        engine.work(0.7)
        pair_products(half // LANES - 1)
        ent_copy = copies.send(lambda: grad_hidden.at[theirs[1]], lambda: given.at[ent_part], place.other_y)
        ent_ready = engine.transfer("y", ent_half * width * 2)

        live_rows = {}

        def sum_hidden(start, count, own_start):
            def block(i, _):
                where = span(start + i * 32, 32, 32)
                own = span(own_start + i * 32, 32, 32)
                total[where] = grad_one[where] + (grad_hidden[own].astype(F32) + given[where].astype(F32))
                return 0

            loop(count // 32, block)

        def rows_z():
            rows_copy.wait_recv()
            all_rows[place.dp, core] = row_parts[0] + row_parts[1]
            view = lambda: all_rows.at[place.dp, core]
            live_rows["z"] = [copies.send(view, view, device) for device in place.ahead]
            return engine.transfer("z", row_bytes)

        def rows_x():
            for copy in live_rows["z"]:
                copy.wait_recv()
            live_rows["x"] = []
            for k in range(nz):
                view = lambda k=k: all_rows.at[place.z_ahead(k) * 2 + x, core]
                live_rows["x"].append(copies.send(view, view, place.other_x))
            return engine.transfer("x", nz * row_bytes)

        def rows_core():
            for copy in live_rows["x"]:
                copy.wait_recv()
            view = lambda: all_rows.at[:, core]
            live_rows["core"] = copies.send(view, view, place.other_core)
            return engine.transfer("core", n_dp * row_bytes)

        rows_dev = table_grad.shape[0]
        table_copies = []
        base_row = (place.dp * 4 + place.seq) * rows_dev

        def table_part(i):
            def step():
                if i == 0:
                    live_rows["core"].wait_recv()
                groups = ids.shape[0]
                block = min(table_block, LANES)
                counts = [jnp.zeros((block, ents), LOW) for _ in range(table_block // block)]
                for group in range(groups):
                    asked = ids[group : group + 1, :] - base_row
                    high = jnp.clip(asked >> 7, -1, rows_dev // LANES).astype(F32)
                    high = jnp.broadcast_to(high, (block, ents)).astype(LOW)
                    first_row = i * table_block
                    number = lax.broadcasted_iota(jnp.int32, (block, ents), 0) + first_row % LANES
                    low_hit = jnp.where((asked & (LANES - 1)) == number, 1.0, 0.0).astype(LOW)
                    for k in range(len(counts)):
                        hit = jnp.where(
                            high == jnp.asarray(first_row // LANES + k, LOW), low_hit, jnp.zeros_like(low_hit)
                        )
                        counts[k] = counts[k] + hit
                        hits[k * block : (k + 1) * block, group * ents : (group + 1) * ents] = hit
                count = jnp.concatenate(counts, axis=0).astype(F32)
                here = pl.ds(i * table_block, table_block)
                for copy in table_copies[2 * i - 4 : 2 * i - 2] if i >= 2 else []:
                    copy.wait()
                dps = min(n_dp, 8)
                grad = None
                for first in range(0, n_dp, dps):
                    given_rows = all_rows[first : first + dps].reshape(dps * 2 * ents, ent_proj.shape[0])
                    value = dot(hits[:, first * 2 * ents : (first + dps) * 2 * ents], given_rows)
                    grad = value if grad is None else grad + value
                table_here[i % 2] = grad
                named = jnp.sum(count, axis=1, keepdims=True)
                touched_here[i % 2] = jnp.broadcast_to(named, (table_block, LANES)).astype(LOW)
                table_copies.append(copies.local(lambda: table_here.at[i % 2], lambda: table_grad.at[here]))
                table_copies.append(copies.local(lambda: touched_here.at[i % 2], lambda: touched.at[here]))
                engine.clock += 0.7

            return step

        engine.add(
            [lambda: rows_ready, rows_z, rows_x, rows_core] + [table_part(i) for i in range(rows_dev // table_block)]
        )
        hidden_part(word_rows, 0, 1)
        word_copy = copies.send(lambda: grad_hidden.at[theirs[0]], lambda: given.at[word_part], place.other_y)
        word_ready = engine.transfer("y", word_half * width * 2)
        engine.work(1.5)

        bias_rows = bias_held.shape[0]
        bias_held[...] = jnp.zeros_like(bias_held)
        bias_held[0:6, columns] = bias_heads[0:6]
        bias_held[6:bias_rows] = bias_middle[0 : bias_rows - 6]
        live = {}
        bias_bytes = bias_rows * width * 2

        def bias_send(key, index, device):
            bias_from[2 * index] = bias_held[...].astype(LOW)
            live[key] = copies.send(lambda: bias_from.at[2 * index], lambda: bias_from.at[2 * index + 1], device)
            return engine.transfer(key, bias_bytes)

        def bias_take(key, index):
            live[key].wait_recv()
            bias_held[...] = bias_from[2 * index].astype(F32) + bias_from[2 * index + 1].astype(F32)

        def bias_core():
            return bias_send("core", 0, place.other_core)

        def bias_y():
            bias_take("core", 0)
            return bias_send("y", 1, place.other_y)

        def bias_x():
            bias_take("y", 1)
            return bias_send("x", 2, place.other_x)

        def bias_z():
            bias_take("x", 2)
            bias_from[6] = bias_held[...].astype(LOW)
            live["z"] = [
                copies.send(lambda: bias_from.at[6], lambda k=k: bias_from.at[7 + k], device)
                for k, device in enumerate(place.ahead)
            ]
            return engine.transfer("z", bias_bytes)

        def bias_end():
            value = bias_from[6].astype(F32)
            for k, copy in enumerate(live["z"]):
                copy.wait_recv()
                value = value + bias_from[7 + k].astype(F32)
            bias_out[...] = value

        engine.add([bias_core, bias_y, bias_x, bias_z, bias_end])
        quarter = word_half // 2

        def words_sum():
            word_copy.wait_recv()
            sum_hidden(0, word_half, y * word_half)
            engine.clock += 0.5
            live_words["send"] = copies.send(
                lambda: total.at[span((1 - core) * quarter, quarter, LANES)], lambda: word_grad.at[core], place.other_core
            )
            live_words["own"] = copies.local(
                lambda: total.at[span(core * quarter, quarter, LANES)], lambda: word_grad.at[core]
            )
            return engine.transfer("core", quarter * width * 4)

        def words_end():
            live_words["send"].wait_recv()
            live_words["own"].wait()

        engine.add([lambda: word_ready, words_sum, words_end])

        def ent_products():
            ent_copy.wait_recv()
            sum_hidden(word_half, ent_half, all_words + y * ent_half)
            proj_rows, pos_rows = rows.shape[1] // n_dp, all_words // n_dp
            proj_pad = padded(proj_rows)
            position = ent_pos[pl.ds(core, 1), :]
            picks = []
            for j in range(all_words // LANES):
                number = lax.broadcasted_iota(jnp.int32, (LANES, ents), 0) + j * LANES
                picks.append(jnp.where(number == position, 1.0, 0.0))
            pick = jnp.concatenate(picks, axis=0)
            here = lax.broadcasted_iota(jnp.int32, (all_words, ents), 1) // ent_half == y
            pick = jnp.where(here, pick, 0.0).astype(LOW)
            grad_ent = total[word_half:]
            grad_ent_low = grad_ent.astype(LOW)
            rest = (grad_ent - grad_ent_low.astype(F32)).astype(LOW)
            pos_grad = dot(pick, jnp.concatenate([grad_ent_low, grad_ent_low], axis=0)) + dot(
                pick, jnp.concatenate([rest, rest], axis=0)
            )
            proj_grad = dot_columns(rows[span(y * ent_half, ent_half, 64)], grad_ent_low)
            ent_grads[:, :, pl.ds(0, proj_rows)] = proj_grad.astype(LOW).reshape(nz, 2, proj_rows, width)
            ent_grads[:, :, pl.ds(proj_pad, pos_rows)] = pos_grad.astype(LOW).reshape(nz, 2, pos_rows, width)
            engine.clock += 1.0

        ent_job = jobs["ent"][0]
        engine.add([lambda: ent_ready, ent_products] + ent_job.steps)
        engine.drain()
        for copy in table_copies[-4:]:
            copy.wait()
        copies.finish()

    table_block = 256 if n_dp * 2 * ents <= 2048 else 32
    pl.run_scoped(
        backward_phase,
        pltpu.VMEM((tokens, half), LOW),
        pltpu.VMEM((tokens, half), LOW),
        pltpu.VMEM((tokens, half), LOW),
        pltpu.VMEM((tokens, half), LOW),
        pltpu.VMEM((HEADS // 2, tokens, tokens), LOW),
        pltpu.VMEM((4, width, half), LOW),
        pltpu.VMEM((width, half), LOW),
        pltpu.VMEM((width, half), LOW),
        pltpu.VMEM((half, tokens), LOW),
        pltpu.VMEM((tokens, half), LOW),
        pltpu.VMEM((tokens, half), LOW),
        pltpu.VMEM((tokens, half), LOW),
        pltpu.VMEM((tokens, half), LOW),
        pltpu.VMEM((width, tokens), LOW),
        pltpu.VMEM((tokens, width), LOW),
        pltpu.VMEM((table_block, n_dp * 2 * ents), LOW),
        pltpu.VMEM((half // LANES, nz, 2, 6 * row_pad, LANES), LOW),
        pltpu.VMEM((nz, 2, ent_sum.shape[0], width), LOW),
        pltpu.VMEM((2, table_block, ent_proj.shape[0]), F32),
        pltpu.VMEM((2, table_block, LANES), LOW),
    )
    last_copies = [
        copies.local(lambda: ffn_sum, lambda: ffn_reduced),
        copies.local(lambda: attn_sum, lambda: attn_reduced),
        copies.local(lambda: ent_sum, lambda: ent_reduced),
    ]
    for copy in out_copies:
        copy.wait_recv()
    for copy in last_copies:
        copy.wait()
    copies.finish()


def layer(
    nz, rows_dev, words, segments, pos_table, query_bias, key_bias, value_bias, out_weight, out_bias, gains, shifts, up_weight, up_bias, down_weight, down_bias, word_cots, ent_cots,
    query_weight, key_weight, value_weight, rows, ent_pos, ent_proj, ids,
):
    n_dp = 2 * nz
    all_words, width = words.shape
    half = width // 2
    ents, edim = rows.shape
    tokens = all_words + ents
    part, ff = tokens // 2, up_weight.shape[1]
    ffn_blocks = ffn_plan(n_dp, width, ff)
    ffn_rows, attn_rows = ffn_blocks[-1][0] + ffn_blocks[-1][1], 6 * padded(width // n_dp)
    ent_pad = padded(edim // n_dp) + padded(all_words // n_dp)
    bias_rows = 12 + ff // width
    plan = [("ffn", 0, base, size, order, width) for base, size, order in ffn_blocks]
    plan += [("attn", pair, 0, attn_rows, "xz", LANES) for pair in range(half // LANES)]
    plan.append(("ent", 0, 0, ent_pad, "xzy", width))
    scratch = [
        pltpu.VMEM((part, half), LOW),
        pltpu.VMEM((tokens, half), LOW),
        pltpu.VMEM((part, width), F32),
        pltpu.VMEM((part, width), LOW),
        pltpu.VMEM((ffn_rows, width), LOW),
        pltpu.VMEM((half // LANES, 2, attn_rows, LANES), LOW),
        pltpu.VMEM((ent_pad, width), LOW),
        pltpu.VMEM((bias_rows, width), F32),
        pltpu.VMEM((6 + nz, bias_rows, width), LOW),
        pltpu.VMEM((n_dp, 2, ents, edim), LOW),
        pltpu.VMEM((8, half), F32),
        pltpu.VMEM((16, width), F32),
        pltpu.VMEM((nz, 2, ffn_rows, width), LOW),
        pltpu.VMEM((part, half), LOW),
        pltpu.VMEM((2, ents, edim), LOW),
        pltpu.VMEM((tokens, half), LOW),
        pltpu.VMEM((ents // 2, width), F32),
    ]
    remote = 8 + 6 + 1 + 3 + nz + 1 + nz + nz + 2 + 4
    for name, _, base, size, order, columns in plan:
        job = Job(None, None, base, size, order, columns)
        scratch += job.scratch(nz)
        remote += job.remote_count(nz)
    scratch += copy_semaphores(remote, 60 + 2 * (rows_dev // 32))
    return call(
        functools.partial(layer_kernel, nz, plan),
        [
            ((2, all_words // 4, width), LOW),
            ((2, ents // 4, width), LOW),
            ((2, all_words // 4, width), F32),
            ((ffn_rows, width), LOW),
            ((half // LANES, 2, attn_rows, LANES), LOW),
            ((ent_pad, width), LOW),
            ((bias_rows, width), F32),
            ((rows_dev, edim), F32),
            ((rows_dev, LANES), LOW),
            ((width, tokens), LOW),
            ((tokens, half), LOW),
            ((tokens, half), LOW),
            ((tokens, half), LOW),
            ((tokens, half), LOW),
            ((HEADS // 2, tokens, tokens), LOW),
        ],
        [ANY, IN_VMEM, ANY] + [IN_VMEM] * 3 + [ANY] + [IN_VMEM] * 3 + [ANY, IN_VMEM, ANY, IN_VMEM] + [ANY] * 2 + [ANY] * 3 + [IN_VMEM] * 4,
        [ANY] * 6 + [IN_VMEM] + [ANY] * 8,
        scratch,
        "layer",
        2,
    )(words, segments, pos_table, query_bias, key_bias, value_bias, out_weight, out_bias, gains, shifts, up_weight, up_bias, down_weight, down_bias, word_cots, ent_cots,
      query_weight, key_weight, value_weight, rows, ent_pos, ent_proj, ids)[:9]


def last_kernel(
    n_dp, table_grad, touched, first, second, ffn, attn, ent, bias, words_low, ents_low, words_grad,
    table_out, update, new_second, proj_grad, pos_grad, query_grad, key_grad, value_grad, out_grad, up_grad, down_grad, query_bias, gain_grad, shift_grad, key_bias, value_bias, out_bias, down_bias, up_bias,
    word_out, ent_out, word_grad,
):
    step = pl.program_id(0)
    grad = table_grad[...]
    hit = touched[:, 0:1].astype(F32) > 0.0
    mean_new = beta_one * first[...] + (1.0 - beta_one) * grad
    square_new = beta_two * second[...] + (1.0 - beta_two) * grad * grad
    direction = (
        mean_new
        / (1.0 - beta_one**adam_step)
        / (jnp.sqrt(square_new / (1.0 - beta_two**adam_step)) + adam_eps)
    )
    table_out[...] = grad
    update[...] = jnp.where(hit, direction, 0.0)
    new_second[...] = jnp.where(hit, square_new, second[...])
    width = ffn.shape[1]
    part, down_rows = out_grad.shape[0], down_grad.shape[0]
    pad = padded(part)
    proj_pad = padded(proj_grad.shape[0])
    parts = up_grad.shape[1] // width
    pairs = attn.shape[0]
    half = pairs * LANES

    @pl.when(step == 0)
    def _():
        down_grad[...] = ffn[:down_rows].astype(F32)

    @pl.when(step == 1)
    def _():
        for j in range(parts):
            base = down_rows + j * pad
            up_grad[:, j * width : (j + 1) * width] = ffn[base : base + part].astype(F32)

    @pl.when(step == 2)
    def _():
        base = down_rows + parts * pad
        out_grad[...] = ffn[base : base + part].astype(F32)
        proj_grad[...] = ent[: proj_grad.shape[0]].astype(F32)
        pos_grad[...] = ent[proj_pad : proj_pad + pos_grad.shape[0]].astype(F32)
        for side in range(2):
            for pair in range(pairs):
                columns = slice(side * half + pair * LANES, side * half + (pair + 1) * LANES)
                key_grad[:, columns] = attn[pair, side, 4 * pad : 4 * pad + part].astype(F32)
                value_grad[:, columns] = attn[pair, side, 5 * pad : 5 * pad + part].astype(F32)

    @pl.when(step == 3)
    def _():
        for side in range(2):
            for pair in range(pairs):
                columns = slice(side * half + pair * LANES, side * half + (pair + 1) * LANES)
                for i in range(4):
                    query_grad[i, :, columns] = attn[pair, side, i * pad : i * pad + part].astype(F32)
        dp = lax.axis_index("dp")

        def own_columns(value, size, start):
            lane = lax.broadcasted_iota(jnp.int32, (value.shape[1], size), 0)
            want = lax.broadcasted_iota(jnp.int32, (value.shape[1], size), 1) + start
            pick = jnp.where(lane == want, 1.0, 0.0)
            return jnp.dot(value, pick, precision=lax.Precision.HIGHEST, preferred_element_type=F32)

        own = own_columns(bias[...], part, dp * part)
        query_bias[...] = own[0:4]
        gain_grad[...] = own[7:9]
        shift_grad[...] = own[9:11]
        for vector, i in ((key_bias, 4), (value_bias, 5), (out_bias, 6), (down_bias, 11 + parts)):
            vector[...] = own[i : i + 1].reshape(part)
        up = jnp.concatenate([bias[11 + j : 12 + j] for j in range(parts)], axis=1)
        size = up_bias.shape[0]
        if size % LANES == 0:
            per = width // size
            row = bias[pl.ds(11 + dp // per, 1), :]
            chosen = row[:, :size]
            for i in range(1, per):
                chosen = jnp.where(dp % per == i, row[:, i * size : (i + 1) * size], chosen)
            up_bias[...] = chosen.reshape(size)
        else:
            up_bias[...] = own_columns(up, size, dp * size).reshape(size)

    @pl.when(step == 0)
    def _():
        word_out[...] = words_low[...]
        ent_out[...] = ents_low[...]
        word_grad[...] = words_grad[...]


def last(n_dp, ff, all_words, table_grad, touched, first, second, ffn, attn, ent, bias, words_low, ents_low, words_grad):
    width = ffn.shape[1]
    rows, edim = first.shape
    part = width // n_dp
    block = 512
    blocked = lambda columns: pl.BlockSpec((block, columns), lambda i: (i, 0))
    whole = lambda shape: pl.BlockSpec(shape, lambda i: (0,) * len(shape))
    shapes = [
        (edim // n_dp, width),
        (all_words // n_dp, width),
        (4, part, width),
        (part, width),
        (part, width),
        (part, width),
        (part, ff),
        (ff // n_dp, width),
        (4, part),
        (2, part),
        (2, part),
        (part,),
        (part,),
        (part,),
        (part,),
        (ff // n_dp,),
    ]
    through = [words_low, ents_low, words_grad]
    return pl.pallas_call(
        functools.partial(last_kernel, n_dp),
        grid=(rows // block,),
        out_shape=[jax.ShapeDtypeStruct((rows, edim), F32)] * 3
        + [jax.ShapeDtypeStruct(shape, F32) for shape in shapes]
        + [jax.ShapeDtypeStruct(array.shape, array.dtype) for array in through],
        in_specs=[blocked(edim), blocked(LANES), blocked(edim), blocked(edim)]
        + [whole(array.shape) for array in (ffn, attn, ent, bias)]
        + [whole(array.shape) for array in through],
        out_specs=[blocked(edim)] * 3 + [whole(shape) for shape in shapes] + [whole(array.shape) for array in through],
        compiler_params=pltpu.CompilerParams(vmem_limit_bytes=VMEM_BYTES),
        name="last",
    )(table_grad, touched, first, second, ffn, attn, ent, bias, words_low, ents_low, words_grad)


def on_device(
    word_states,
    segments,
    entity_ids,
    entity_pos,
    ent_table,
    first_moment,
    second_moment,
    ent_proj,
    pos_table,
    query_weight,
    query_bias,
    key_weight,
    key_bias,
    value_weight,
    value_bias,
    out_weight,
    out_bias,
    norm_gain,
    norm_shift,
    up_weight,
    up_bias,
    down_weight,
    down_bias,
    word_cot,
    ent_cot,
):
    n_dp = lax.axis_size("dp")
    nz = n_dp // 2
    width, ff = up_weight.shape
    all_words = segments.shape[1]
    words, word_cots, ent_cots, all_ids, rows = fetch(nz, word_states, word_cot, ent_cot, entity_ids, ent_table)
    ents = entity_ids.shape[1]
    word_out, ent_out, word_grad, ffn_sum, attn_sum, ent_sum, bias_sum, table_grad, touched = layer(
        nz, ent_table.shape[0], words, segments, pos_table, query_bias, key_bias, value_bias, out_weight, out_bias, norm_gain, norm_shift, up_weight, up_bias, down_weight, down_bias,
        word_cots, ent_cots, query_weight, key_weight, value_weight,
        rows, entity_pos, ent_proj, all_ids.reshape(-1, ents),
    )
    (table_grad, table_update, new_second, proj_grad, pos_grad, query_grad, key_grad, value_grad, out_grad, up_grad, down_grad,
     query_bias_grad, gain_grad, shift_grad, key_bias_grad, value_bias_grad, out_bias_grad, down_bias_grad, up_bias_grad,
     word_out, ent_out, word_grad,
    ) = last(
        n_dp, ff, all_words, table_grad, touched, first_moment, second_moment, ffn_sum, attn_sum, ent_sum, bias_sum, word_out, ent_out, word_grad
    )
    return (
        word_out,
        ent_out,
        word_grad,
        proj_grad,
        pos_grad,
        query_grad,
        query_bias_grad,
        key_grad,
        key_bias_grad,
        value_grad,
        value_bias_grad,
        out_grad,
        out_bias_grad,
        gain_grad,
        shift_grad,
        up_grad,
        up_bias_grad,
        down_grad,
        down_bias_grad,
        table_grad,
        table_update,
        new_second,
    )


def solution(mesh):
    return jax.shard_map(
        on_device,
        mesh=mesh,
        in_specs=(
            P("dp", "seq", None),
            P("dp", None),
            P("dp", None),
            P("dp", None),
            P(("dp", "seq"), None),
            P(("dp", "seq"), None),
            P(("dp", "seq"), None),
            P(),
            P(),
            P(),
            P(),
            P(),
            P(),
            P(),
            P(),
            P(),
            P(),
            P(),
            P(),
            P(),
            P(),
            P(),
            P(),
            P("dp", "seq", None),
            P("dp", "seq", None),
        ),
        out_specs=(
            P("dp", "seq", None),
            P("dp", "seq", None),
            P("dp", "seq", None),
            P("dp", None),
            P("dp", None),
            P(None, "dp", None),
            P(None, "dp"),
            P("dp", None),
            P("dp"),
            P("dp", None),
            P("dp"),
            P("dp", None),
            P("dp"),
            P(None, "dp"),
            P(None, "dp"),
            P("dp", None),
            P("dp"),
            P("dp", None),
            P("dp"),
            P(("dp", "seq"), None),
            P(("dp", "seq"), None),
            P(("dp", "seq"), None),
        ),
        check_vma=False,
    )
```

```python
import functools
import math

import jax
import jax.numpy as jnp
from jax import lax
from jax.experimental import pallas as pl
from jax.experimental.pallas import tpu as pltpu
from jax.sharding import PartitionSpec as P

HEADS = 12
HEAD = 64
LANES = 128
MESH = pl.DeviceIdType.MESH
LOW = jnp.bfloat16
F32 = jnp.float32
VMEM_BYTES = 125 * 512 * 1024

norm_eps = 1e-05
beta_one = 0.9
beta_two = 0.98
adam_eps = 1e-06
adam_step = 10.0
masked_score = -1e30


def dot(left, right):
    return jnp.dot(left, right, preferred_element_type=F32)


def dot_rows(left, right):
    return lax.dot_general(left, right, (((1,), (1,)), ((), ())), preferred_element_type=F32)


def dot_columns(left, right):
    return lax.dot_general(left, right, (((0,), (0,)), ((), ())), preferred_element_type=F32)


def span(start, size, unit):
    if isinstance(start, int):
        return pl.ds(start, size)
    return pl.ds(pl.multiple_of(start, unit), size)


def padded(rows):
    return -(-rows // 16) * 16


def loop(count, body, carry=0, unroll=1):
    def steps(i, carried):
        for k in range(unroll):
            carried = body(i * unroll + k, carried)
        return carried

    return lax.fori_loop(0, count // unroll, steps, carry)


class Place:
    def __init__(self, nz):
        self.dp, self.seq = lax.axis_index("dp"), lax.axis_index("seq")
        self.z, self.x = self.dp // 2, self.dp % 2
        self.y, self.core = self.seq // 2, self.seq % 2
        self.nz = nz
        self.other_core = (self.dp, self.y * 2 + 1 - self.core)
        self.other_y = (self.dp, (1 - self.y) * 2 + self.core)
        self.diagonal = (self.dp, (1 - self.y) * 2 + 1 - self.core)
        self.other_x = (self.z * 2 + 1 - self.x, self.seq)
        self.ahead = [(((self.z + k) % nz) * 2 + self.x, self.seq) for k in range(1, nz)]

    def z_ahead(self, k):
        return (self.z + k) % self.nz


def meet(partners):
    barrier = pltpu.get_barrier_semaphore()
    for partner in partners:
        pl.semaphore_signal(barrier, inc=1, device_id=partner, device_id_type=MESH)
    pl.semaphore_wait(barrier, len(partners))


class Remote:
    def __init__(self, copies, number, src, dst, device):
        self.copies, self.number, self.src, self.dst, self.device = copies, number, src, dst, device
        self.open = True

    def make(self, landing=False):
        return pltpu.make_async_remote_copy(
            src_ref=self.dst() if landing else self.src(),
            dst_ref=self.dst(),
            send_sem=self.copies.send_sem.at[self.number],
            recv_sem=self.copies.recv_sem.at[self.number],
            device_id=self.device,
            device_id_type=MESH,
        )

    def wait_recv(self):
        self.make(landing=True).wait_recv()

    def wait_send(self):
        if self.open:
            self.make().wait_send()
        self.open = False


class Local:
    def __init__(self, copies, number, src, dst):
        self.copies, self.number, self.src, self.dst = copies, number, src, dst

    def make(self):
        return pltpu.make_async_copy(self.src(), self.dst(), self.copies.local_sem.at[self.number])

    def wait(self):
        self.make().wait()


class Copies:
    def __init__(self, send_sem, recv_sem, local_sem):
        self.send_sem, self.recv_sem, self.local_sem = send_sem, recv_sem, local_sem
        self.local_count = 0
        self.sent = []

    def send(self, src, dst, device):
        copy = Remote(self, len(self.sent), src, dst, device)
        copy.make().start()
        self.sent.append(copy)
        return copy

    def local(self, src, dst):
        copy = Local(self, self.local_count, src, dst)
        self.local_count += 1
        copy.make().start()
        return copy

    def finish(self):
        for copy in self.sent:
            copy.wait_send()


def copy_semaphores(remote, local):
    return [
        pltpu.SemaphoreType.DMA((remote,)),
        pltpu.SemaphoreType.DMA((remote,)),
        pltpu.SemaphoreType.DMA((local,)),
    ]


ANY = pl.BlockSpec(memory_space=pl.ANY)
IN_VMEM = pl.BlockSpec(memory_space=pltpu.VMEM)


def call(kernel, outs, in_specs, out_specs, scratch, name, collective_id=None):
    params = {"vmem_limit_bytes": VMEM_BYTES}
    if collective_id is not None:
        params.update(collective_id=collective_id, has_side_effects=True)
    return pl.pallas_call(
        kernel,
        out_shape=[jax.ShapeDtypeStruct(shape, dtype) for shape, dtype in outs],
        in_specs=in_specs,
        out_specs=out_specs,
        scratch_shapes=scratch,
        compiler_params=pltpu.CompilerParams(**params),
        name=name,
    )


def fetch_kernel(nz, words, word_cot, ent_cot, ids, table, all_words, word_cots, ent_cots, all_ids, rows_out, *scratch):
    table_full, table_low, picked, answers, held, from_core, from_x, from_z, from_y, ids_here = scratch[:10]
    copies = Copies(*scratch[10:])
    place = Place(nz)
    z, x, y, core = place.z, place.x, place.y, place.core
    n_dp = 2 * nz
    word_here, ent_here = words.shape[1], ent_cot.shape[1]
    ents = ids.shape[1]
    dp_others = [((place.dp + k) % n_dp, place.seq) for k in range(1, n_dp)]
    meet([place.other_core, place.other_y, place.diagonal] + dp_others)
    whole_table = copies.local(lambda: table, lambda: table_full)
    ids_here[place.dp] = ids[...]
    id_copies = [copies.send(lambda: ids, lambda: ids_here.at[place.dp], device) for device in dp_others]
    quarter = span(place.seq * word_here, word_here, 128)
    word_copies = [
        copies.send(lambda: words.at[1 - core], lambda: all_words.at[quarter], place.diagonal),
        copies.send(lambda: words.at[core], lambda: all_words.at[quarter], place.other_y),
        copies.send(lambda: words.at[1 - core], lambda: all_words.at[quarter], place.other_core),
        copies.send(lambda: word_cot.at[1 - core], lambda: word_cots.at[span(core * word_here, word_here, 128)], place.other_core),
        copies.send(lambda: ent_cot.at[1 - core], lambda: ent_cots.at[span(core * ent_here, ent_here, 32)], place.other_core),
    ]
    all_words[quarter] = words[core]
    word_cots[span(core * word_here, word_here, 128)] = word_cot[core]
    ent_cots[span(core * ent_here, ent_here, 32)] = ent_cot[core]
    whole_table.wait()
    rows_dev = table.shape[0]

    def narrow(i, _):
        where = span(i * 128, 128, 128)
        table_low[where] = table_full[where].astype(LOW)
        return 0

    loop(rows_dev // 128, narrow)
    for copy in id_copies:
        copy.wait_recv()
    all_ids[...] = ids_here[...]
    base = (place.dp * 4 + place.seq) * rows_dev
    tiles = rows_dev // LANES

    def look_up(zz):
        for g in range(4):
            asked = ids_here[zz * 2 + g // 2, pl.ds(g % 2, 1), :] - base
            column = jnp.transpose(jnp.broadcast_to(asked, (ents, ents)))
            lane = lax.broadcasted_iota(jnp.int32, (ents, LANES), 1)
            low_hit = jnp.where((column & (LANES - 1)) == lane, 1.0, 0.0).astype(LOW)
            high = jnp.clip(column >> 7, -1, tiles).astype(F32).astype(LOW)
            for j in range(tiles):
                hit = jnp.where(high == jnp.asarray(j, LOW), low_hit, jnp.zeros_like(low_hit))
                picked[pl.ds(g * ents, ents), pl.ds(j * LANES, LANES)] = hit
        answer = dot(picked[...], table_low[...]).astype(LOW)
        answers[zz] = answer.reshape(2, 2, ents, answer.shape[-1])

    order = [place.z_ahead(k + 1) for k in range(nz)]
    core_copies, x_copies, z_copies = [], [], []

    def core_send(zz):
        return copies.send(lambda: answers.at[zz, :, 1 - core], lambda: from_core.at[zz], place.other_core)

    def after_core(k):
        zz = order[k]
        core_copies[k].wait_recv()
        held[zz] = answers[zz, :, core] + from_core[zz]
        x_copies.append(copies.send(lambda: held.at[zz, 1 - x], lambda: from_x.at[zz], place.other_x))

    def after_x(k):
        zz = order[k]
        x_copies[k].wait_recv()
        held[zz, x] = held[zz, x] + from_x[zz]
        if k < nz - 1:
            z_copies.append(copies.send(lambda: held.at[zz, x], lambda: from_z.at[k], place.ahead[k]))

    for k in range(nz + 2):
        if k < nz:
            look_up(order[k])
            core_copies.append(core_send(order[k]))
        if 0 <= k - 1 < nz:
            after_core(k - 1)
        if 0 <= k - 2:
            after_x(k - 2)
    total = held[z, x]
    for k in range(nz - 1):
        z_copies[k].wait_recv()
        total = total + from_z[k]
    from_y[0] = total
    y_copy = copies.send(lambda: from_y.at[0], lambda: from_y.at[1], place.other_y)
    y_copy.wait_recv()
    rows_out[...] = from_y[0] + from_y[1]
    for copy in word_copies:
        copy.wait_recv()
    copies.finish()


def fetch(nz, words, word_cot, ent_cot, ids, table):
    _, word_here, width = words.shape
    ent_here, ents, (rows_dev, edim) = ent_cot.shape[1], ids.shape[1], table.shape
    n_dp = 2 * nz
    return call(
        functools.partial(fetch_kernel, nz),
        [
            ((4 * word_here, width), LOW),
            ((2 * word_here, width), LOW),
            ((2 * ent_here, width), LOW),
            ((n_dp, 2, ents), jnp.int32),
            ((ents, edim), LOW),
        ],
        [IN_VMEM] * 4 + [ANY],
        [IN_VMEM] * 5,
        [
            pltpu.VMEM((rows_dev, edim), F32),
            pltpu.VMEM((rows_dev, edim), LOW),
            pltpu.VMEM((4 * ents, rows_dev), LOW),
            pltpu.VMEM((nz, 2, 2, ents, edim), LOW),
            pltpu.VMEM((nz, 2, ents, edim), LOW),
            pltpu.VMEM((nz, 2, ents, edim), LOW),
            pltpu.VMEM((nz, ents, edim), LOW),
            pltpu.VMEM((nz - 1, ents, edim), LOW),
            pltpu.VMEM((2, ents, edim), LOW),
            pltpu.VMEM((n_dp, 2, ents), jnp.int32),
        ]
        + copy_semaphores(n_dp + 4 + 3 * nz + 2, 1),
        "fetch",
        1,
    )(words, word_cot, ent_cot, ids, table)


def lane_mask(rows, head):
    lane = lax.broadcasted_iota(jnp.int32, (rows, LANES), 1)
    return (lane >= head * HEAD) & (lane < (head + 1) * HEAD)


def row_of(vector):
    return vector[...].astype(F32).reshape(1, vector.shape[0])


def own_half(vector, y):
    row = row_of(vector)
    half = row.shape[1] // 2
    return jnp.where(y == 0, row[:, :half], row[:, half:])


def as_column(row):
    parts = [
        jnp.transpose(jnp.broadcast_to(row[:, i : i + LANES], (LANES, LANES)))
        for i in range(0, row.shape[1], LANES)
    ]
    return jnp.concatenate(parts, axis=0) if len(parts) > 1 else parts[0]


class Engine:
    RATES = {"core": 300e3, "x": 52e3, "y": 52e3, "z": 13e3}
    LATENCY = 2.0

    def __init__(self):
        self.clock, self.free, self.streams = 0.0, {}, []

    def transfer(self, link, size):
        start = max(self.clock, self.free.get(link, 0.0))
        self.free[link] = start + size / self.RATES[link]
        return self.free[link] + self.LATENCY

    def add(self, steps):
        self.streams.append([self.clock, list(steps)])
        self.poll()

    def run(self, stream):
        self.clock = max(self.clock, stream[0])
        ready = stream[1].pop(0)()
        stream[0] = self.clock if ready is None else ready

    def next(self):
        live = [stream for stream in self.streams if stream[1]]
        return min(live, key=lambda stream: stream[0]) if live else None

    def poll(self):
        while (stream := self.next()) is not None and stream[0] <= self.clock:
            self.run(stream)

    def work(self, time):
        self.clock += time
        self.poll()

    def drain(self):
        while (stream := self.next()) is not None:
            self.run(stream)


def blocks_of(rows):
    for size in (96, 64, 48, 32):
        if rows % size == 0:
            return size
    return 16


def add_blocks(engine, target, parts, leading, rows, columns):
    size = blocks_of(rows)
    count = rows // size

    def block(i, _):
        lead, row = i // count, (i % count) * size
        where = span(row, size, 16)
        if len(parts) == 2:
            value = parts[0](lead, where) + parts[1](lead, where)
        else:
            value = parts[0](lead, where).astype(F32)
            for part in parts[1:]:
                value = value + part(lead, where).astype(F32)
            value = value.astype(LOW)
        target(lead, where, value)
        return 0

    loop(leading * count, block)
    engine.clock += 0.3 + leading * rows * columns / 1e6


class Job:
    def __init__(self, grads, reduced, base, size, order, columns):
        self.grads, self.reduced, self.base, self.size, self.order, self.columns = grads, reduced, base, size, order, columns
        self.half = size // 2
        self.part = size // 4 if order == "yxz" else size // 2

    def scratch(self, nz):
        shapes = [(nz, 2, self.half, self.columns)]
        if self.order == "yxz":
            shapes.append((nz, 2, self.part, self.columns))
        elif self.order == "xzy":
            shapes.append((2, self.part, self.columns))
        shapes += [(nz, self.part, self.columns), (nz - 1, self.part, self.columns)]
        return [pltpu.VMEM(shape, LOW) for shape in shapes]

    def remote_count(self, nz):
        return 1 + (1 if self.order != "xz" else 0) + 1 + (nz - 1) + 1 + 1

    def prepare(self, engine, place, copies, scratch):
        nz, z, x, y, core = place.nz, place.z, place.x, place.y, place.core
        base, half, part, order, columns = self.base, self.half, self.part, self.order, self.columns
        held = self.grads.at[:, :, span(base + core * half, half, 16)]
        from_core = scratch[0]
        from_y = scratch[1] if order != "xz" else None
        from_x, from_z = scratch[-2:]
        live = {}
        row_bytes = 2 * columns
        theirs = span(base + (1 - core) * half, half, 16)
        mine = span(base + core * half, half, 16)
        own_rows = span(y * part, part, 16) if order == "yxz" else pl.ds(0, part)
        final_rows = span(base + core * half + (y * part if order == "yxz" else 0), part, 16)

        def start():
            live["core"] = copies.send(lambda: self.grads.at[:, :, theirs], lambda: from_core, place.other_core)
            return engine.transfer("core", 2 * nz * half * row_bytes)

        def send_x():
            live["x"] = copies.send(lambda: held.at[:, 1 - x, own_rows], lambda: from_x, place.other_x)
            return engine.transfer("x", nz * part * row_bytes)

        def after_core():
            live["core"].wait_recv()

            def put(i, where, value):
                held[i // 2, i % 2, where] = value

            add_blocks(
                engine,
                put,
                [lambda i, where: held[i // 2, i % 2, where], lambda i, where: from_core[i // 2, i % 2, where]],
                2 * nz,
                half,
                columns,
            )
            if order == "yxz":
                live["y"] = copies.send(
                    lambda: held.at[:, :, span((1 - y) * part, part, 16)], lambda: from_y, place.other_y
                )
                return engine.transfer("y", 2 * nz * part * row_bytes)
            return send_x()

        def shifted(where):
            return span(y * part + where.start, where.size, 16) if order == "yxz" else where

        def after_y():
            live["y"].wait_recv()

            def put(i, where, value):
                held[i // 2, i % 2, shifted(where)] = value

            add_blocks(
                engine,
                put,
                [lambda i, where: held[i // 2, i % 2, shifted(where)], lambda i, where: from_y[i // 2, i % 2, where]],
                2 * nz,
                part,
                columns,
            )
            return send_x()

        def send_z(k):
            return copies.send(
                lambda: held.at[place.z_ahead(k + 1), x, own_rows], lambda: from_z.at[k], place.ahead[k]
            )

        def after_x():
            live["x"].wait_recv()

            def put(i, where, value):
                held[i, x, shifted(where)] = value

            add_blocks(
                engine,
                put,
                [lambda i, where: held[i, x, shifted(where)], lambda i, where: from_x[i, where]],
                nz,
                part,
                columns,
            )
            live["z"] = [send_z(k) for k in range(nz - 1)]
            return engine.transfer("z", part * row_bytes)

        def after_z():
            for copy in live["z"]:
                copy.wait_recv()

            def put(i, where, value):
                if order == "yxz":
                    self.reduced[span(base + core * half + y * part + where.start, where.size, 16)] = value
                elif order == "xz":
                    self.reduced[y, span(base + core * half + where.start, where.size, 16)] = value
                else:
                    from_y[0, where] = value

            def parts(k):
                return lambda i, where: from_z[k, where]

            add_blocks(
                engine,
                put,
                [lambda i, where: held[z, x, shifted(where)]] + [parts(k) for k in range(nz - 1)],
                1,
                part,
                columns,
            )
            if order == "xzy":
                live["y2"] = copies.send(lambda: from_y.at[0], lambda: from_y.at[1], place.other_y)
            else:
                view = lambda: self.reduced.at[final_rows] if order == "yxz" else self.reduced.at[y, final_rows]
                live["y2"] = copies.send(view, view, place.other_y)
            return engine.transfer("y", part * row_bytes)

        def after_gather():
            live["y2"].wait_recv()
            if order == "xzy":

                def put(i, where, value):
                    self.reduced[span(base + core * half + where.start, where.size, 16)] = value

                add_blocks(
                    engine, put, [lambda i, where: from_y[0, where], lambda i, where: from_y[1, where]], 1, part, columns
                )
            view = lambda: self.reduced.at[:, mine] if order == "xz" else self.reduced.at[mine]
            live["core2"] = copies.send(view, view, place.other_core)
            return engine.transfer("core", 2 * half * row_bytes)

        def end():
            live["core2"].wait_recv()

        middle_steps = [after_core, after_y, after_x] if order == "yxz" else [after_core, after_x]
        self.steps = [start] + middle_steps + [after_z, after_gather, end]


def lane_mean(value):
    return jnp.mean(value, axis=-1, keepdims=True)


def column_sum(value):
    return jnp.sum(value, axis=0, keepdims=True)


ROW_BLOCK = 32


def ffn_plan(n_dp, width, ff):
    down_rows, row_pad = ff // n_dp, padded(width // n_dp)
    size = 128 if down_rows % 128 == 0 else 32
    order = "yxz" if size % 64 == 0 else "xzy"
    plan = [(base, size, order) for base in range(0, down_rows, size)]
    base = down_rows
    for pair in range(ff // width // 2):
        order = "yxz" if row_pad % 32 == 0 else "xzy"
        plan.append((base, 2 * row_pad, order))
        base += 2 * row_pad
    plan.append((base, row_pad, "xzy"))
    return plan


def layer_kernel(
    nz, plan, words, segments, pos_table, query_bias, key_bias, value_bias, out_weight, out_bias, gains, shifts, up_weight, up_bias, down_weight, down_bias, word_cots, ent_cots,
    query_weight, key_weight, value_weight, rows, ent_pos, ent_proj, ids,
    word_out, ent_out, word_grad, ffn_reduced, attn_reduced, ent_reduced, bias_out, table_grad, touched,
    hidden_turned_in, query_words_in, query_ents_in, keys_in, values_in, probs_in, *scratch,
):
    (from_y_mixed, grad_mixed, grad_one, given, ffn_sum, attn_sum, ent_sum, bias_held, bias_from, all_rows, bias_heads, bias_middle,
     ffn_grads, grad_mixed_here, row_parts, mixed, ent_keep) = scratch[:17]
    copies = Copies(*scratch[-3:])
    engine = Engine()
    place = Place(nz)
    z, x, y, core = place.z, place.x, place.y, place.core
    n_dp = 2 * nz
    tokens, half = mixed.shape
    width = 2 * half
    ents = rows.shape[0]
    all_words = tokens - ents
    word_half, ent_half = all_words // 2, ents // 2
    part_tokens = tokens // 2
    ff = up_weight.shape[1]
    parts = ff // width
    row_part, row_pad, down_rows = width // n_dp, padded(width // n_dp), ff // n_dp
    meet([place.other_core, place.other_y, place.other_x] + place.ahead)

    jobs = {"ffn": [], "attn": [], "ent": []}

    def make_jobs(names, sources):
        at = 17
        for name, number, base, size, order, columns in plan:
            grads, reduced = sources.get(name, (None, None))
            if name == "attn" and grads is not None:
                grads, reduced = grads.at[number], reduced.at[number]
            job = Job(grads, reduced, base, size, order, columns)
            used = len(job.scratch(nz))
            if name in names:
                job.prepare(engine, place, copies, scratch[at : at + used])
                jobs[name].append(job)
            at += used

    make_jobs(["ffn"], {"ffn": (ffn_grads, ffn_sum)})

    def token_rows(side):
        return span(side * word_half, word_half, LANES), span(all_words + side * ent_half, ent_half, 64)

    mine, theirs = token_rows(y), token_rows(1 - y)
    own_columns, other_columns = span(y * half, half, LANES), span((1 - y) * half, half, LANES)
    word_part, ent_part = pl.ds(0, word_half), pl.ds(word_half, ent_half)
    mixed_copies = []
    scale = 1.0 / math.sqrt(HEAD)
    tiles = tokens // LANES

    def attend_phase(
        hidden_low, hidden_turned, query_words, query_ents, keys, values, probs, query_here, key_here, value_here, pos_here, values_turned, mask,
    ):
        weight_copies = [
            copies.local(lambda: words, lambda: hidden_low.at[pl.ds(0, all_words)]),
            copies.local(lambda: pos_table, lambda: pos_here),
            copies.local(lambda: query_weight.at[:, :, own_columns], lambda: query_here),
            copies.local(lambda: key_weight.at[:, own_columns], lambda: key_here),
            copies.local(lambda: value_weight.at[:, own_columns], lambda: value_here),
        ]
        position = as_column(ent_pos[pl.ds(core, 1), :])
        picks = []
        for j in range(all_words // LANES):
            number = lax.broadcasted_iota(jnp.int32, (ents, LANES), 1) + j * LANES
            picks.append(jnp.where(position == number, 1.0, 0.0))
        pick = jnp.concatenate(picks, axis=1)
        word_seg = segments[pl.ds(core, 1), :].astype(F32)
        ent_seg = jnp.sum(pick * word_seg, axis=1, keepdims=True)
        for copy in weight_copies[:2]:
            copy.wait()
        ent_hidden = dot(rows[...], ent_proj[...]) + dot(pick.astype(LOW), pos_here[...])
        ent_keep[...] = jnp.where(y == 0, ent_hidden[:ent_half], ent_hidden[ent_half:])
        hidden_low[all_words:] = ent_hidden.astype(LOW)
        ent_row = jnp.transpose(jnp.broadcast_to(ent_seg, (ents, LANES)))[:1]
        seg_row = jnp.concatenate([word_seg, ent_row], axis=1)
        seg_column = jnp.concatenate([as_column(word_seg), jnp.broadcast_to(ent_seg, (ents, LANES))], axis=0)
        for j in range(tiles):
            here = slice(j * LANES, (j + 1) * LANES)
            mask[:, here] = jnp.where(seg_column == seg_row[:, here], 0.0, masked_score)
        query_b = query_bias[:, own_columns].astype(F32)
        for copy in weight_copies[2:]:
            copy.wait()
        word_low, ent_low = hidden_low[:all_words], hidden_low[all_words:]
        query_words[:all_words] = (dot(word_low, query_here[0]) + query_b[0:1]).astype(LOW)
        query_ents[:all_words] = (dot(word_low, query_here[1]) + query_b[1:2]).astype(LOW)
        query_words[all_words:] = (dot(ent_low, query_here[2]) + query_b[2:3]).astype(LOW)
        query_ents[all_words:] = (dot(ent_low, query_here[3]) + query_b[3:4]).astype(LOW)
        keys[...] = (dot(hidden_low[...], key_here[...]) + own_half(key_bias, y)).astype(LOW)
        value = dot(hidden_low[...], value_here[...]) + own_half(value_bias, y)
        values[...] = value.astype(LOW)
        values_turned[...] = jnp.transpose(value).astype(LOW)
        spills = [
            copies.local(lambda: query_words, lambda: query_words_in),
            copies.local(lambda: query_ents, lambda: query_ents_in),
            copies.local(lambda: keys, lambda: keys_in),
            copies.local(lambda: values, lambda: values_in),
        ]
        for pair in range(half // LANES):
            lanes = slice(pair * LANES, (pair + 1) * LANES)
            key, turned = keys[:, lanes], values_turned[lanes, :]
            row = lax.broadcasted_iota(jnp.int32, (LANES, tokens), 0)
            own_key, own_turned = [], []
            for head in range(2):
                own_key.append(jnp.where(lane_mask(tokens, head), key, jnp.zeros_like(key)))
                own_rows = (row >= head * HEAD) & (row < (head + 1) * HEAD)
                own_turned.append(jnp.where(own_rows, turned, jnp.zeros_like(turned)))
            for i in range(tiles):
                here = slice(i * LANES, (i + 1) * LANES)
                query_w, query_e = query_words[here, lanes], query_ents[here, lanes]
                part_sum = None
                for head in range(2):
                    raw = jnp.concatenate(
                        [dot_rows(own_key[head][:all_words], query_w), dot_rows(own_key[head][all_words:], query_e)], axis=0
                    )
                    score = raw * scale + mask[:, here]
                    weight = jnp.exp(score - jnp.max(score, axis=0, keepdims=True))
                    prob = (weight * (1.0 / jnp.sum(weight, axis=0, keepdims=True))).astype(LOW)
                    probs[pair * 2 + head, :, here] = prob
                    part = dot(own_turned[head], prob)
                    part_sum = part if part_sum is None else part_sum + part
                mixed[here, lanes] = jnp.transpose(part_sum).astype(LOW)
            heads = pl.ds(pair * 2, 2)
            mixed_copies.extend([
                copies.send(
                    lambda lanes=lanes: mixed.at[theirs[0], lanes], lambda lanes=lanes: from_y_mixed.at[word_part, lanes], place.other_y
                ),
                copies.send(
                    lambda lanes=lanes: mixed.at[theirs[1], lanes], lambda lanes=lanes: from_y_mixed.at[ent_part, lanes], place.other_y
                ),
            ])
            spills.append(copies.local(lambda heads=heads: probs.at[heads], lambda heads=heads: probs_in.at[heads]))
        for i in range(width // LANES):
            here = slice(i * LANES, (i + 1) * LANES)
            hidden_turned[here, :] = jnp.transpose(hidden_low[:, here].astype(F32)).astype(LOW)
        spills.append(copies.local(lambda: hidden_turned, lambda: hidden_turned_in))
        for copy in spills:
            copy.wait()

    pl.run_scoped(
        attend_phase,
        pltpu.VMEM((tokens, width), LOW),
        pltpu.VMEM((width, tokens), LOW),
        pltpu.VMEM((tokens, half), LOW),
        pltpu.VMEM((tokens, half), LOW),
        pltpu.VMEM((tokens, half), LOW),
        pltpu.VMEM((tokens, half), LOW),
        pltpu.VMEM((HEADS // 2, tokens, tokens), LOW),
        pltpu.VMEM((4, width, half), LOW),
        pltpu.VMEM((width, half), LOW),
        pltpu.VMEM((width, half), LOW),
        pltpu.VMEM((all_words, width), LOW),
        pltpu.VMEM((half, tokens), LOW),
        pltpu.VMEM((tokens, tokens), F32),
    )
    out_copies, mixed_back = [], []

    def forward_phase(
        out_here, up_here, down_here, word_here, mixed_full, work, normed_low, normal_one, inverse_one,
        act, slope, output, grad_two, grad_two_low, grad_one_low, normed_turned,
    ):
        cot, grad_up_low = output, slope
        weight_copies = [
            copies.local(lambda: out_weight, lambda: out_here),
            copies.local(lambda: words.at[mine[0]], lambda: word_here),
            copies.local(lambda: up_weight, lambda: up_here),
            copies.local(lambda: down_weight, lambda: down_here),
            copies.local(lambda: word_cots, lambda: cot.at[word_part]),
            copies.local(lambda: ent_cots, lambda: cot.at[ent_part]),
        ]
        gain, shift = gains[...].astype(F32), shifts[...].astype(F32)
        out_b, down_b, up_b = row_of(out_bias), row_of(down_bias), row_of(up_bias)
        mixed_full[word_part, own_columns] = mixed[mine[0]]
        mixed_full[ent_part, own_columns] = mixed[mine[1]]
        for copy in weight_copies[:2]:
            copy.wait()
        for copy in mixed_copies:
            copy.wait_recv()
        mixed_full[:, other_columns] = from_y_mixed[...]
        work[...] = dot(mixed_full[...], out_here[...])

        def norm_one(residual):
            def step(i, _):
                rows = span(residual[1] + i * ROW_BLOCK, ROW_BLOCK, ROW_BLOCK)
                value = residual[0][span(i * ROW_BLOCK, ROW_BLOCK, ROW_BLOCK)].astype(F32) + (work[rows] + out_b)
                center = value - lane_mean(value)
                inverse = lax.rsqrt(lane_mean(center * center) + norm_eps)
                normal = center * inverse
                result = normal * gain[0:1] + shift[0:1]
                normal_one[rows] = normal
                inverse_one[rows] = jnp.broadcast_to(inverse, (ROW_BLOCK, LANES))
                normed_low[rows] = result.astype(LOW)
                return 0

            return step

        loop(word_half // ROW_BLOCK, norm_one((word_here, 0)), 0, 2)
        loop(ent_half // ROW_BLOCK, norm_one((ent_keep, word_half)), 0, 2)
        weight_copies[2].wait()
        for j in range(parts):
            columns = slice(j * width, (j + 1) * width)
            work[...] = dot(normed_low[...], up_here[:, columns]) + up_b[:, columns]

            def gelu(i, _):
                rows = span(i * ROW_BLOCK, ROW_BLOCK, ROW_BLOCK)
                value = work[rows]
                below = 0.5 * (1.0 + lax.erf(value * (1.0 / math.sqrt(2.0))))
                density = jnp.exp(-0.5 * value * value) * (1.0 / math.sqrt(2.0 * math.pi))
                act[rows, columns] = (value * below).astype(LOW)
                slope[rows, columns] = (below + value * density).astype(LOW)
                return 0

            loop(part_tokens // ROW_BLOCK, gelu)
        normed_turned[...] = jnp.transpose(normed_low[...].astype(F32)).astype(LOW)
        for copy in weight_copies[3:]:
            copy.wait()
        work[...] = dot(act[...], down_here[...])

        def norm_two(i, sums):
            rows = span(i * ROW_BLOCK, ROW_BLOCK, ROW_BLOCK)
            value = (normal_one[rows] * gain[0:1] + shift[0:1]) + (work[rows] + down_b)
            center = value - lane_mean(value)
            inverse = lax.rsqrt(lane_mean(center * center) + norm_eps)
            normal = center * inverse
            cotangent = cot[rows].astype(F32)
            output[rows] = (normal * gain[1:2] + shift[1:2]).astype(LOW)
            scaled = cotangent * gain[1:2]
            result = inverse * (scaled - lane_mean(scaled) - normal * lane_mean(scaled * normal))
            grad_two[rows] = result
            grad_two_low[rows] = result.astype(LOW)
            return (
                sums[0] + column_sum(cotangent * normal),
                sums[1] + column_sum(cotangent),
                sums[2] + column_sum(result),
            )

        nothing = jnp.zeros((1, width), F32)
        gain_two, shift_two, down_sum = loop(part_tokens // ROW_BLOCK, norm_two, (nothing, nothing, nothing), 2)
        quarter, ent_quarter = word_half // 2, ent_half // 2
        out_copies.extend([
            copies.send(
                lambda: output.at[span((1 - core) * quarter, quarter, LANES)], lambda: word_out.at[core], place.other_core
            ),
            copies.send(
                lambda: output.at[span(word_half + (1 - core) * ent_quarter, ent_quarter, 32)],
                lambda: ent_out.at[core],
                place.other_core,
            ),
        ])
        out_local = [
            copies.local(lambda: output.at[span(core * quarter, quarter, LANES)], lambda: word_out.at[core]),
            copies.local(
                lambda: output.at[span(word_half + core * ent_quarter, ent_quarter, 32)], lambda: ent_out.at[core]
            ),
        ]
        engine.clock = 0.0
        engine.free = {}
        def put(base, value):
            ffn_grads[:, :, pl.ds(base, row_part)] = value.astype(LOW).reshape(nz, 2, row_part, width)

        def down_products():
            per = width // down_rows
            for j in range(parts):
                value = dot_columns(act[:, j * width : (j + 1) * width], grad_two_low[...])
                value = value.astype(LOW).reshape(per, down_rows, width)
                for d in range(per):
                    slab = j * per + d
                    ffn_grads[slab // 2, slab % 2, pl.ds(0, down_rows)] = value[d]

        up_sums = []

        def grad_up(j):
            columns = slice(j * width, (j + 1) * width)
            work[...] = dot_rows(grad_two_low[...], down_here[columns, :])

            def grad_gelu(i, total_row):
                rows = span(i * ROW_BLOCK, ROW_BLOCK, ROW_BLOCK)
                value = work[rows] * slope[rows, columns].astype(F32)
                grad_up_low[rows, columns] = value.astype(LOW)
                return total_row + column_sum(value)

            up_sums.append(loop(part_tokens // ROW_BLOCK, grad_gelu, nothing, 2))
            engine.work(1.6)

        def up_product(j):
            columns = slice(j * width, (j + 1) * width)
            put(down_rows + j * row_pad, dot(normed_turned[...], grad_up_low[:, columns]))
            engine.work(0.9)

        downs = [job for job in jobs["ffn"] if job.base < down_rows]
        ups = [job for job in jobs["ffn"] if down_rows <= job.base][:-1]
        down_products()
        engine.clock += 3.0
        for job in downs:
            engine.add(job.steps)
        for j in range(parts):
            grad_up(j)
        work[...] = dot_rows(grad_up_low[...], up_here[...])
        engine.work(2.0)

        def back_one(i, sums):
            rows = span(i * ROW_BLOCK, ROW_BLOCK, ROW_BLOCK)
            upper = grad_two[rows] + work[rows]
            normal = normal_one[rows]
            inverse = inverse_one[rows, 0:1]
            scaled = upper * gain[0:1]
            result = inverse * (scaled - lane_mean(scaled) - normal * lane_mean(scaled * normal))
            grad_one[rows] = result
            grad_one_low[rows] = result.astype(LOW)
            return (
                sums[0] + column_sum(upper * normal),
                sums[1] + column_sum(upper),
                sums[2] + column_sum(result),
            )

        gain_one, shift_one, out_sum = loop(part_tokens // ROW_BLOCK, back_one, (nothing, nothing, nothing), 2)
        engine.work(1.0)
        grad_mixed_here[...] = dot_rows(grad_one_low[...], out_here[other_columns, :]).astype(LOW)
        mixed_back.extend([
            copies.send(lambda: grad_mixed_here.at[word_part], lambda: grad_mixed.at[mine[0]], place.other_y),
            copies.send(lambda: grad_mixed_here.at[ent_part], lambda: grad_mixed.at[mine[1]], place.other_y),
        ])
        engine.transfer("y", part_tokens * half * 2)
        own = dot_rows(grad_one_low[...], out_here[own_columns, :]).astype(LOW)
        grad_mixed[mine[0]] = own[:word_half]
        grad_mixed[mine[1]] = own[word_half:]
        engine.work(1.0)
        for j in range(parts):
            up_product(j)
            if j % 2 == 1:
                engine.add(ups[j // 2].steps)
        put(down_rows + parts * row_pad, dot_columns(mixed_full[...], grad_one_low[...]))
        engine.work(0.8)
        engine.add(jobs["ffn"][-1].steps)
        bias_rows = [out_sum, gain_one, gain_two, shift_one, shift_two] + up_sums + [down_sum]
        for i, row in enumerate(bias_rows):
            bias_middle[i : i + 1] = row
        for copy in out_copies:
            copy.wait_send()
        for copy in out_local:
            copy.wait()

    tall = lambda columns, dtype: pltpu.VMEM((part_tokens, columns), dtype)
    pl.run_scoped(
        forward_phase,
        pltpu.VMEM((width, width), LOW),
        pltpu.VMEM((width, ff), LOW),
        pltpu.VMEM((ff, width), LOW),
        pltpu.VMEM((word_half, width), LOW),
        tall(width, LOW),
        tall(width, F32),
        tall(width, LOW),
        tall(width, F32),
        tall(LANES, F32),
        tall(ff, LOW),
        tall(ff, LOW),
        tall(width, LOW),
        tall(width, F32),
        tall(width, LOW),
        tall(width, LOW),
        pltpu.VMEM((width, part_tokens), LOW),
    )
    live_words = {}

    def backward_phase(
        query_words, query_ents, keys, values, probs, query_here, key_here, value_here, keys_turned,
        grad_query_words, grad_query_ents, grad_keys, grad_values, hidden_turned, grad_hidden, hits, attn_grads, ent_grads, table_here, touched_here,
    ):
        total = grad_one
        make_jobs(["attn", "ent"], {"attn": (attn_grads, attn_sum), "ent": (ent_grads, ent_sum)})
        columns = span(y * half, half, LANES)
        copies_in = [
            copies.local(lambda: values_in, lambda: values),
            copies.local(lambda: keys_in, lambda: keys),
            copies.local(lambda: query_words_in, lambda: query_words),
            copies.local(lambda: query_ents_in, lambda: query_ents),
        ]
        prob_copies = []
        for head in range(probs.shape[0]):
            prob_copies.append(
                copies.local(lambda head=head: probs_in.at[head], lambda head=head: probs.at[head])
            )
        hidden_copy = copies.local(lambda: hidden_turned_in, lambda: hidden_turned)
        weight_copies = [
            copies.local(lambda: query_weight.at[:, :, columns], lambda: query_here),
            copies.local(lambda: key_weight.at[:, columns], lambda: key_here),
            copies.local(lambda: value_weight.at[:, columns], lambda: value_here),
        ]
        for copy in copies_in:
            copy.wait()
        for i in range(half // LANES):
            lanes = slice(i * LANES, (i + 1) * LANES)
            keys_turned[lanes, :] = jnp.transpose(keys[:, lanes].astype(F32)).astype(LOW)
        for copy in mixed_back:
            copy.wait_recv()
        engine.work(2.0)
        def pair_products(pair):
            lanes = slice(pair * LANES, (pair + 1) * LANES)
            word_turned, ent_turned = hidden_turned[:, :all_words], hidden_turned[:, all_words:]
            products = [
                dot(word_turned, grad_query_words[:all_words, lanes]),
                dot(word_turned, grad_query_ents[:all_words, lanes]),
                dot(ent_turned, grad_query_words[all_words:, lanes]),
                dot(ent_turned, grad_query_ents[all_words:, lanes]),
                dot(hidden_turned[...], grad_keys[:, lanes]),
                dot(hidden_turned[...], grad_values[:, lanes]),
            ]
            for i, value in enumerate(products):
                attn_grads[pair, :, :, pl.ds(i * row_pad, row_part)] = value.astype(LOW).reshape(nz, 2, row_part, LANES)
            engine.work(1.5)
            engine.add(jobs["attn"][pair].steps)

        for pair in range(half // LANES):
            lanes = slice(pair * LANES, (pair + 1) * LANES)
            grad_query_w = jnp.zeros((LANES, tokens), F32)
            grad_query_e = jnp.zeros((LANES, tokens), F32)
            grad_key_w = jnp.zeros((all_words, LANES), F32)
            grad_key_e = jnp.zeros((ents, LANES), F32)
            grad_value = jnp.zeros((tokens, LANES), F32)
            for head in range(2):
                own = lane_mask(tokens, head)
                value = values[:, lanes]
                own_value = jnp.where(own, value, jnp.zeros_like(value))
                prob_copies[pair * 2 + head].wait()

                given_heads = grad_mixed[:, lanes]
                grad_scores = probs.at[pair * 2 + head]
                grad_value += dot(grad_scores[...], jnp.where(own, given_heads, jnp.zeros_like(given_heads)))
                for i in range(tiles):
                    where = slice(i * LANES, (i + 1) * LANES)
                    grad_prob = dot_rows(own_value, grad_mixed[where, lanes])
                    prob = grad_scores[:, where].astype(F32)
                    both = prob * grad_prob
                    grad_scores[:, where] = (both - prob * jnp.sum(both, axis=0, keepdims=True)).astype(LOW)
                engine.work(1.7)
                query_w, query_e = query_words[:, lanes], query_ents[:, lanes]
                grad_key_w += dot(grad_scores[:all_words], jnp.where(own, query_w, jnp.zeros_like(query_w)))
                grad_key_e += dot(grad_scores[all_words:], jnp.where(own, query_e, jnp.zeros_like(query_e)))
                row = lax.broadcasted_iota(jnp.int32, (LANES, tokens), 0)
                own_rows = (row >= head * HEAD) & (row < (head + 1) * HEAD)
                turned = keys_turned[lanes, :]
                turned = jnp.where(own_rows, turned, jnp.zeros_like(turned))
                grad_query_w += dot(turned[:, :all_words], grad_scores[:all_words])
                grad_query_e += dot(turned[:, all_words:], grad_scores[all_words:])
                engine.work(1.7)
            grad_query_w = jnp.transpose(grad_query_w) * scale
            grad_query_e = jnp.transpose(grad_query_e) * scale
            grad_key_w, grad_key_e = grad_key_w * scale, grad_key_e * scale
            sums = [
                column_sum(grad_query_w[:all_words]),
                column_sum(grad_query_e[:all_words]),
                column_sum(grad_query_w[all_words:]),
                column_sum(grad_query_e[all_words:]),
                column_sum(grad_key_w) + column_sum(grad_key_e),
                column_sum(grad_value),
            ]
            for i, sum_row in enumerate(sums):
                bias_heads[i : i + 1, lanes] = sum_row
            grad_query_words[:, lanes] = grad_query_w.astype(LOW)
            grad_query_ents[:, lanes] = grad_query_e.astype(LOW)
            grad_keys[:all_words, lanes] = grad_key_w.astype(LOW)
            grad_keys[all_words:, lanes] = grad_key_e.astype(LOW)
            grad_values[:, lanes] = grad_value.astype(LOW)
            engine.work(0.5)
            if pair == 0:
                hidden_copy.wait()
            if pair + 1 < half // LANES:
                pair_products(pair)

        for copy in weight_copies:
            copy.wait()
        ent_rows, word_rows = slice(all_words, tokens), slice(0, all_words)

        def hidden_part(here, first, second):
            grad_hidden[here] = (
                dot_rows(grad_keys[here], key_here[...])
                + dot_rows(grad_values[here], value_here[...])
                + dot_rows(grad_query_words[here], query_here[first])
                + dot_rows(grad_query_ents[here], query_here[second])
            ).astype(LOW)

        hidden_part(ent_rows, 2, 3)
        own_ents = lax.broadcasted_iota(jnp.int32, (ents, width), 0) // ent_half == y
        twice = jnp.concatenate([grad_one[word_half:], grad_one[word_half:]], axis=0)
        ent_sum_part = grad_hidden[ent_rows].astype(F32) + jnp.where(own_ents, twice, 0.0)
        row_parts[0] = dot_rows(ent_sum_part.astype(LOW), ent_proj[...]).astype(LOW)
        rows_copy = copies.send(lambda: row_parts.at[0], lambda: row_parts.at[1], place.other_y)
        row_bytes = ents * ent_proj.shape[0] * 2
        rows_ready = engine.transfer("y", row_bytes)
        engine.work(0.7)
        pair_products(half // LANES - 1)
        ent_copy = copies.send(lambda: grad_hidden.at[theirs[1]], lambda: given.at[ent_part], place.other_y)
        ent_ready = engine.transfer("y", ent_half * width * 2)

        live_rows = {}

        def sum_hidden(start, count, own_start):
            def block(i, _):
                where = span(start + i * 32, 32, 32)
                own = span(own_start + i * 32, 32, 32)
                total[where] = grad_one[where] + (grad_hidden[own].astype(F32) + given[where].astype(F32))
                return 0

            loop(count // 32, block)

        def rows_z():
            rows_copy.wait_recv()
            all_rows[place.dp, core] = row_parts[0] + row_parts[1]
            view = lambda: all_rows.at[place.dp, core]
            live_rows["z"] = [copies.send(view, view, device) for device in place.ahead]
            return engine.transfer("z", row_bytes)

        def rows_x():
            for copy in live_rows["z"]:
                copy.wait_recv()
            live_rows["x"] = []
            for k in range(nz):
                view = lambda k=k: all_rows.at[place.z_ahead(k) * 2 + x, core]
                live_rows["x"].append(copies.send(view, view, place.other_x))
            return engine.transfer("x", nz * row_bytes)

        def rows_core():
            for copy in live_rows["x"]:
                copy.wait_recv()
            view = lambda: all_rows.at[:, core]
            live_rows["core"] = copies.send(view, view, place.other_core)
            return engine.transfer("core", n_dp * row_bytes)

        rows_dev = table_grad.shape[0]
        table_copies = []
        base_row = (place.dp * 4 + place.seq) * rows_dev

        def table_part(i):
            def step():
                if i == 0:
                    live_rows["core"].wait_recv()
                groups = ids.shape[0]
                block = min(table_block, LANES)
                counts = [jnp.zeros((block, ents), LOW) for _ in range(table_block // block)]
                for group in range(groups):
                    asked = ids[group : group + 1, :] - base_row
                    high = jnp.clip(asked >> 7, -1, rows_dev // LANES).astype(F32)
                    high = jnp.broadcast_to(high, (block, ents)).astype(LOW)
                    first_row = i * table_block
                    number = lax.broadcasted_iota(jnp.int32, (block, ents), 0) + first_row % LANES
                    low_hit = jnp.where((asked & (LANES - 1)) == number, 1.0, 0.0).astype(LOW)
                    for k in range(len(counts)):
                        hit = jnp.where(
                            high == jnp.asarray(first_row // LANES + k, LOW), low_hit, jnp.zeros_like(low_hit)
                        )
                        counts[k] = counts[k] + hit
                        hits[k * block : (k + 1) * block, group * ents : (group + 1) * ents] = hit
                count = jnp.concatenate(counts, axis=0).astype(F32)
                here = pl.ds(i * table_block, table_block)
                for copy in table_copies[2 * i - 4 : 2 * i - 2] if i >= 2 else []:
                    copy.wait()
                dps = min(n_dp, 8)
                grad = None
                for first in range(0, n_dp, dps):
                    given_rows = all_rows[first : first + dps].reshape(dps * 2 * ents, ent_proj.shape[0])
                    value = dot(hits[:, first * 2 * ents : (first + dps) * 2 * ents], given_rows)
                    grad = value if grad is None else grad + value
                table_here[i % 2] = grad
                named = jnp.sum(count, axis=1, keepdims=True)
                touched_here[i % 2] = jnp.broadcast_to(named, (table_block, LANES)).astype(LOW)
                table_copies.append(copies.local(lambda: table_here.at[i % 2], lambda: table_grad.at[here]))
                table_copies.append(copies.local(lambda: touched_here.at[i % 2], lambda: touched.at[here]))
                engine.clock += 0.7

            return step

        engine.add(
            [lambda: rows_ready, rows_z, rows_x, rows_core] + [table_part(i) for i in range(rows_dev // table_block)]
        )
        hidden_part(word_rows, 0, 1)
        word_copy = copies.send(lambda: grad_hidden.at[theirs[0]], lambda: given.at[word_part], place.other_y)
        word_ready = engine.transfer("y", word_half * width * 2)
        engine.work(1.5)

        bias_rows = bias_held.shape[0]
        bias_held[...] = jnp.zeros_like(bias_held)
        bias_held[0:6, columns] = bias_heads[0:6]
        bias_held[6:bias_rows] = bias_middle[0 : bias_rows - 6]
        live = {}
        bias_bytes = bias_rows * width * 2

        def bias_send(key, index, device):
            bias_from[2 * index] = bias_held[...].astype(LOW)
            live[key] = copies.send(lambda: bias_from.at[2 * index], lambda: bias_from.at[2 * index + 1], device)
            return engine.transfer(key, bias_bytes)

        def bias_take(key, index):
            live[key].wait_recv()
            bias_held[...] = bias_from[2 * index].astype(F32) + bias_from[2 * index + 1].astype(F32)

        def bias_core():
            return bias_send("core", 0, place.other_core)

        def bias_y():
            bias_take("core", 0)
            return bias_send("y", 1, place.other_y)

        def bias_x():
            bias_take("y", 1)
            return bias_send("x", 2, place.other_x)

        def bias_z():
            bias_take("x", 2)
            bias_from[6] = bias_held[...].astype(LOW)
            live["z"] = [
                copies.send(lambda: bias_from.at[6], lambda k=k: bias_from.at[7 + k], device)
                for k, device in enumerate(place.ahead)
            ]
            return engine.transfer("z", bias_bytes)

        def bias_end():
            value = bias_from[6].astype(F32)
            for k, copy in enumerate(live["z"]):
                copy.wait_recv()
                value = value + bias_from[7 + k].astype(F32)
            bias_out[...] = value

        engine.add([bias_core, bias_y, bias_x, bias_z, bias_end])
        quarter = word_half // 2

        def words_sum():
            word_copy.wait_recv()
            sum_hidden(0, word_half, y * word_half)
            engine.clock += 0.5
            live_words["send"] = copies.send(
                lambda: total.at[span((1 - core) * quarter, quarter, LANES)], lambda: word_grad.at[core], place.other_core
            )
            live_words["own"] = copies.local(
                lambda: total.at[span(core * quarter, quarter, LANES)], lambda: word_grad.at[core]
            )
            return engine.transfer("core", quarter * width * 4)

        def words_end():
            live_words["send"].wait_recv()
            live_words["own"].wait()

        engine.add([lambda: word_ready, words_sum, words_end])

        def ent_products():
            ent_copy.wait_recv()
            sum_hidden(word_half, ent_half, all_words + y * ent_half)
            proj_rows, pos_rows = rows.shape[1] // n_dp, all_words // n_dp
            proj_pad = padded(proj_rows)
            position = ent_pos[pl.ds(core, 1), :]
            picks = []
            for j in range(all_words // LANES):
                number = lax.broadcasted_iota(jnp.int32, (LANES, ents), 0) + j * LANES
                picks.append(jnp.where(number == position, 1.0, 0.0))
            pick = jnp.concatenate(picks, axis=0)
            here = lax.broadcasted_iota(jnp.int32, (all_words, ents), 1) // ent_half == y
            pick = jnp.where(here, pick, 0.0).astype(LOW)
            grad_ent = total[word_half:]
            grad_ent_low = grad_ent.astype(LOW)
            rest = (grad_ent - grad_ent_low.astype(F32)).astype(LOW)
            pos_grad = dot(pick, jnp.concatenate([grad_ent_low, grad_ent_low], axis=0)) + dot(
                pick, jnp.concatenate([rest, rest], axis=0)
            )
            proj_grad = dot_columns(rows[span(y * ent_half, ent_half, 64)], grad_ent_low)
            ent_grads[:, :, pl.ds(0, proj_rows)] = proj_grad.astype(LOW).reshape(nz, 2, proj_rows, width)
            ent_grads[:, :, pl.ds(proj_pad, pos_rows)] = pos_grad.astype(LOW).reshape(nz, 2, pos_rows, width)
            engine.clock += 1.0

        ent_job = jobs["ent"][0]
        engine.add([lambda: ent_ready, ent_products] + ent_job.steps)
        engine.drain()
        for copy in table_copies[-4:]:
            copy.wait()
        copies.finish()

    table_block = 256 if n_dp * 2 * ents <= 2048 else 32
    pl.run_scoped(
        backward_phase,
        pltpu.VMEM((tokens, half), LOW),
        pltpu.VMEM((tokens, half), LOW),
        pltpu.VMEM((tokens, half), LOW),
        pltpu.VMEM((tokens, half), LOW),
        pltpu.VMEM((HEADS // 2, tokens, tokens), LOW),
        pltpu.VMEM((4, width, half), LOW),
        pltpu.VMEM((width, half), LOW),
        pltpu.VMEM((width, half), LOW),
        pltpu.VMEM((half, tokens), LOW),
        pltpu.VMEM((tokens, half), LOW),
        pltpu.VMEM((tokens, half), LOW),
        pltpu.VMEM((tokens, half), LOW),
        pltpu.VMEM((tokens, half), LOW),
        pltpu.VMEM((width, tokens), LOW),
        pltpu.VMEM((tokens, width), LOW),
        pltpu.VMEM((table_block, n_dp * 2 * ents), LOW),
        pltpu.VMEM((half // LANES, nz, 2, 6 * row_pad, LANES), LOW),
        pltpu.VMEM((nz, 2, ent_sum.shape[0], width), LOW),
        pltpu.VMEM((2, table_block, ent_proj.shape[0]), F32),
        pltpu.VMEM((2, table_block, LANES), LOW),
    )
    last_copies = [
        copies.local(lambda: ffn_sum, lambda: ffn_reduced),
        copies.local(lambda: attn_sum, lambda: attn_reduced),
        copies.local(lambda: ent_sum, lambda: ent_reduced),
    ]
    for copy in out_copies:
        copy.wait_recv()
    for copy in last_copies:
        copy.wait()
    copies.finish()


def layer(
    nz, rows_dev, words, segments, pos_table, query_bias, key_bias, value_bias, out_weight, out_bias, gains, shifts, up_weight, up_bias, down_weight, down_bias, word_cots, ent_cots,
    query_weight, key_weight, value_weight, rows, ent_pos, ent_proj, ids,
):
    n_dp = 2 * nz
    all_words, width = words.shape
    half = width // 2
    ents, edim = rows.shape
    tokens = all_words + ents
    part, ff = tokens // 2, up_weight.shape[1]
    ffn_blocks = ffn_plan(n_dp, width, ff)
    ffn_rows, attn_rows = ffn_blocks[-1][0] + ffn_blocks[-1][1], 6 * padded(width // n_dp)
    ent_pad = padded(edim // n_dp) + padded(all_words // n_dp)
    bias_rows = 12 + ff // width
    plan = [("ffn", 0, base, size, order, width) for base, size, order in ffn_blocks]
    plan += [("attn", pair, 0, attn_rows, "xz", LANES) for pair in range(half // LANES)]
    plan.append(("ent", 0, 0, ent_pad, "xzy", width))
    scratch = [
        pltpu.VMEM((part, half), LOW),
        pltpu.VMEM((tokens, half), LOW),
        pltpu.VMEM((part, width), F32),
        pltpu.VMEM((part, width), LOW),
        pltpu.VMEM((ffn_rows, width), LOW),
        pltpu.VMEM((half // LANES, 2, attn_rows, LANES), LOW),
        pltpu.VMEM((ent_pad, width), LOW),
        pltpu.VMEM((bias_rows, width), F32),
        pltpu.VMEM((6 + nz, bias_rows, width), LOW),
        pltpu.VMEM((n_dp, 2, ents, edim), LOW),
        pltpu.VMEM((8, half), F32),
        pltpu.VMEM((16, width), F32),
        pltpu.VMEM((nz, 2, ffn_rows, width), LOW),
        pltpu.VMEM((part, half), LOW),
        pltpu.VMEM((2, ents, edim), LOW),
        pltpu.VMEM((tokens, half), LOW),
        pltpu.VMEM((ents // 2, width), F32),
    ]
    remote = 8 + 6 + 1 + 3 + nz + 1 + nz + nz + 2 + 4
    for name, _, base, size, order, columns in plan:
        job = Job(None, None, base, size, order, columns)
        scratch += job.scratch(nz)
        remote += job.remote_count(nz)
    scratch += copy_semaphores(remote, 60 + 2 * (rows_dev // 32))
    return call(
        functools.partial(layer_kernel, nz, plan),
        [
            ((2, all_words // 4, width), LOW),
            ((2, ents // 4, width), LOW),
            ((2, all_words // 4, width), F32),
            ((ffn_rows, width), LOW),
            ((half // LANES, 2, attn_rows, LANES), LOW),
            ((ent_pad, width), LOW),
            ((bias_rows, width), F32),
            ((rows_dev, edim), F32),
            ((rows_dev, LANES), LOW),
            ((width, tokens), LOW),
            ((tokens, half), LOW),
            ((tokens, half), LOW),
            ((tokens, half), LOW),
            ((tokens, half), LOW),
            ((HEADS // 2, tokens, tokens), LOW),
        ],
        [ANY, IN_VMEM, ANY] + [IN_VMEM] * 3 + [ANY] + [IN_VMEM] * 3 + [ANY, IN_VMEM, ANY, IN_VMEM] + [ANY] * 2 + [ANY] * 3 + [IN_VMEM] * 4,
        [ANY] * 6 + [IN_VMEM] + [ANY] * 8,
        scratch,
        "layer",
        2,
    )(words, segments, pos_table, query_bias, key_bias, value_bias, out_weight, out_bias, gains, shifts, up_weight, up_bias, down_weight, down_bias, word_cots, ent_cots,
      query_weight, key_weight, value_weight, rows, ent_pos, ent_proj, ids)[:9]


def last_kernel(
    n_dp, table_grad, touched, first, second, ffn_in, attn_in, ent_in, bias, words_in, ents_in, words_grad_in,
    table_out, update, new_second, proj_out, pos_out, query_out, key_out, value_out, out_out, up_out, down_out,
    query_bias, gain_grad, shift_grad, key_bias, value_bias, out_bias, down_bias, up_bias, word_out, ent_out, word_grad,
    ffn, attn, ent, words, ents, words_grad, proj_grad, pos_grad, query_grad, key_grad, value_grad, out_grad, up_grad, down_grad, sems,
):
    into = [(ffn_in, ffn), (attn_in, attn), (ent_in, ent), (words_in, words), (ents_in, ents), (words_grad_in, words_grad)]
    arrive = [pltpu.make_async_copy(src, dst, sems.at[i]) for i, (src, dst) in enumerate(into)]
    onward = [(down_grad, down_out), (up_grad, up_out), (out_grad, out_out), (proj_grad, proj_out), (pos_grad, pos_out)]
    onward += [(key_grad, key_out), (value_grad, value_out), (query_grad, query_out)]
    onward += [(words, word_out), (ents, ent_out), (words_grad, word_grad)]
    leave = [pltpu.make_async_copy(src, dst, sems.at[len(into) + i]) for i, (src, dst) in enumerate(onward)]

    @pl.when(pl.program_id(0) == 0)
    def _():
        for copy in arrive:
            copy.start()

    step = pl.program_id(0)
    grad = table_grad[...]
    hit = touched[:, 0:1].astype(F32) > 0.0
    mean_new = beta_one * first[...] + (1.0 - beta_one) * grad
    square_new = beta_two * second[...] + (1.0 - beta_two) * grad * grad
    direction = (
        mean_new
        / (1.0 - beta_one**adam_step)
        / (jnp.sqrt(square_new / (1.0 - beta_two**adam_step)) + adam_eps)
    )
    table_out[...] = grad
    update[...] = jnp.where(hit, direction, 0.0)
    new_second[...] = jnp.where(hit, square_new, second[...])
    width = ffn.shape[1]
    part, down_rows = out_grad.shape[0], down_grad.shape[0]
    pad = padded(part)
    proj_pad = padded(proj_grad.shape[0])
    parts = up_grad.shape[1] // width
    pairs = attn.shape[0]
    half = pairs * LANES

    @pl.when(step == 0)
    def _():
        arrive[0].wait()
        down_grad[...] = ffn[:down_rows].astype(F32)
        leave[0].start()
        for copy in arrive[3:]:
            copy.wait()
        for copy in leave[8:]:
            copy.start()

    @pl.when(step == 1)
    def _():
        for j in range(parts):
            base = down_rows + j * pad
            up_grad[:, j * width : (j + 1) * width] = ffn[base : base + part].astype(F32)
        leave[1].start()
        arrive[1].wait()
        arrive[2].wait()

    @pl.when(step == 2)
    def _():
        base = down_rows + parts * pad
        out_grad[...] = ffn[base : base + part].astype(F32)
        proj_grad[...] = ent[: proj_grad.shape[0]].astype(F32)
        pos_grad[...] = ent[proj_pad : proj_pad + pos_grad.shape[0]].astype(F32)
        for side in range(2):
            for pair in range(pairs):
                columns = slice(side * half + pair * LANES, side * half + (pair + 1) * LANES)
                key_grad[:, columns] = attn[pair, side, 4 * pad : 4 * pad + part].astype(F32)
                value_grad[:, columns] = attn[pair, side, 5 * pad : 5 * pad + part].astype(F32)
        for copy in leave[2:7]:
            copy.start()

    @pl.when(step == 2)
    def _():
        for side in range(2):
            for pair in range(pairs):
                columns = slice(side * half + pair * LANES, side * half + (pair + 1) * LANES)
                for i in range(4):
                    query_grad[i, :, columns] = attn[pair, side, i * pad : i * pad + part].astype(F32)
        leave[7].start()

    @pl.when(step == 3)
    def _():
        dp = lax.axis_index("dp")

        def own_columns(value, size, start):
            lane = lax.broadcasted_iota(jnp.int32, (value.shape[1], size), 0)
            want = lax.broadcasted_iota(jnp.int32, (value.shape[1], size), 1) + start
            pick = jnp.where(lane == want, 1.0, 0.0)
            return jnp.dot(value, pick, precision=lax.Precision.HIGHEST, preferred_element_type=F32)

        own = own_columns(bias[...], part, dp * part)
        query_bias[...] = own[0:4]
        gain_grad[...] = own[7:9]
        shift_grad[...] = own[9:11]
        for vector, i in ((key_bias, 4), (value_bias, 5), (out_bias, 6), (down_bias, 11 + parts)):
            vector[...] = own[i : i + 1].reshape(part)
        up = jnp.concatenate([bias[11 + j : 12 + j] for j in range(parts)], axis=1)
        size = up_bias.shape[0]
        if size % LANES == 0:
            per = width // size
            row = bias[pl.ds(11 + dp // per, 1), :]
            chosen = row[:, :size]
            for i in range(1, per):
                chosen = jnp.where(dp % per == i, row[:, i * size : (i + 1) * size], chosen)
            up_bias[...] = chosen.reshape(size)
        else:
            up_bias[...] = own_columns(up, size, dp * size).reshape(size)

    @pl.when(step == pl.num_programs(0) - 1)
    def _():
        for copy in leave:
            copy.wait()


def last(n_dp, ff, all_words, table_grad, touched, first, second, ffn, attn, ent, bias, words_low, ents_low, words_grad):
    width = ffn.shape[1]
    rows, edim = first.shape
    part = width // n_dp
    block = 256
    blocked = lambda columns: pl.BlockSpec((block, columns), lambda i: (i, 0))
    whole = lambda shape: pl.BlockSpec(shape, lambda i: (0,) * len(shape))
    shapes = [
        (edim // n_dp, width),
        (all_words // n_dp, width),
        (4, part, width),
        (part, width),
        (part, width),
        (part, width),
        (part, ff),
        (ff // n_dp, width),
        (4, part),
        (2, part),
        (2, part),
        (part,),
        (part,),
        (part,),
        (part,),
        (ff // n_dp,),
    ]
    through = [words_low, ents_low, words_grad]
    return pl.pallas_call(
        functools.partial(last_kernel, n_dp),
        grid=(rows // block,),
        out_shape=[jax.ShapeDtypeStruct((rows, edim), F32)] * 3
        + [jax.ShapeDtypeStruct(shape, F32) for shape in shapes]
        + [jax.ShapeDtypeStruct(array.shape, array.dtype) for array in through],
        in_specs=[blocked(edim), blocked(LANES), blocked(edim), blocked(edim)]
        + [ANY] * 3
        + [whole(bias.shape)]
        + [ANY] * 3,
        out_specs=[blocked(edim)] * 3 + [ANY] * 8 + [whole(shape) for shape in shapes[8:]] + [ANY] * 3,
        scratch_shapes=[pltpu.VMEM(array.shape, array.dtype) for array in [ffn, attn, ent] + through]
        + [pltpu.VMEM(shape, F32) for shape in shapes[:8]]
        + [pltpu.SemaphoreType.DMA((17,))],
        compiler_params=pltpu.CompilerParams(vmem_limit_bytes=VMEM_BYTES),
        name="last",
    )(table_grad, touched, first, second, ffn, attn, ent, bias, words_low, ents_low, words_grad)


def on_device(
    word_states,
    segments,
    entity_ids,
    entity_pos,
    ent_table,
    first_moment,
    second_moment,
    ent_proj,
    pos_table,
    query_weight,
    query_bias,
    key_weight,
    key_bias,
    value_weight,
    value_bias,
    out_weight,
    out_bias,
    norm_gain,
    norm_shift,
    up_weight,
    up_bias,
    down_weight,
    down_bias,
    word_cot,
    ent_cot,
):
    n_dp = lax.axis_size("dp")
    nz = n_dp // 2
    width, ff = up_weight.shape
    all_words = segments.shape[1]
    words, word_cots, ent_cots, all_ids, rows = fetch(nz, word_states, word_cot, ent_cot, entity_ids, ent_table)
    ents = entity_ids.shape[1]
    word_out, ent_out, word_grad, ffn_sum, attn_sum, ent_sum, bias_sum, table_grad, touched = layer(
        nz, ent_table.shape[0], words, segments, pos_table, query_bias, key_bias, value_bias, out_weight, out_bias, norm_gain, norm_shift, up_weight, up_bias, down_weight, down_bias,
        word_cots, ent_cots, query_weight, key_weight, value_weight,
        rows, entity_pos, ent_proj, all_ids.reshape(-1, ents),
    )
    (table_grad, table_update, new_second, proj_grad, pos_grad, query_grad, key_grad, value_grad, out_grad, up_grad, down_grad,
     query_bias_grad, gain_grad, shift_grad, key_bias_grad, value_bias_grad, out_bias_grad, down_bias_grad, up_bias_grad,
     word_out, ent_out, word_grad,
    ) = last(
        n_dp, ff, all_words, table_grad, touched, first_moment, second_moment, ffn_sum, attn_sum, ent_sum, bias_sum, word_out, ent_out, word_grad
    )
    return (
        word_out,
        ent_out,
        word_grad,
        proj_grad,
        pos_grad,
        query_grad,
        query_bias_grad,
        key_grad,
        key_bias_grad,
        value_grad,
        value_bias_grad,
        out_grad,
        out_bias_grad,
        gain_grad,
        shift_grad,
        up_grad,
        up_bias_grad,
        down_grad,
        down_bias_grad,
        table_grad,
        table_update,
        new_second,
    )


def solution(mesh):
    return jax.shard_map(
        on_device,
        mesh=mesh,
        in_specs=(
            P("dp", "seq", None),
            P("dp", None),
            P("dp", None),
            P("dp", None),
            P(("dp", "seq"), None),
            P(("dp", "seq"), None),
            P(("dp", "seq"), None),
            P(),
            P(),
            P(),
            P(),
            P(),
            P(),
            P(),
            P(),
            P(),
            P(),
            P(),
            P(),
            P(),
            P(),
            P(),
            P(),
            P("dp", "seq", None),
            P("dp", "seq", None),
        ),
        out_specs=(
            P("dp", "seq", None),
            P("dp", "seq", None),
            P("dp", "seq", None),
            P("dp", None),
            P("dp", None),
            P(None, "dp", None),
            P(None, "dp"),
            P("dp", None),
            P("dp"),
            P("dp", None),
            P("dp"),
            P("dp", None),
            P("dp"),
            P(None, "dp"),
            P(None, "dp"),
            P("dp", None),
            P("dp"),
            P("dp", None),
            P("dp"),
            P(("dp", "seq"), None),
            P(("dp", "seq"), None),
            P(("dp", "seq"), None),
        ),
        check_vma=False,
    )
```

```python
import functools
import math

import jax
import jax.numpy as jnp
from jax import lax
from jax.experimental import pallas as pl
from jax.experimental.pallas import tpu as pltpu
from jax.sharding import PartitionSpec as P

HEADS = 12
HEAD = 64
LANES = 128
MESH = pl.DeviceIdType.MESH
LOW = jnp.bfloat16
F32 = jnp.float32
VMEM_BYTES = 125 * 512 * 1024

norm_eps = 1e-05
beta_one = 0.9
beta_two = 0.98
adam_eps = 1e-06
adam_step = 10.0
masked_score = -1e30


def dot(left, right):
    return jnp.dot(left, right, preferred_element_type=F32)


def dot_rows(left, right):
    return lax.dot_general(left, right, (((1,), (1,)), ((), ())), preferred_element_type=F32)


def dot_columns(left, right):
    return lax.dot_general(left, right, (((0,), (0,)), ((), ())), preferred_element_type=F32)


def span(start, size, unit):
    if isinstance(start, int):
        return pl.ds(start, size)
    return pl.ds(pl.multiple_of(start, unit), size)


def padded(rows):
    return -(-rows // 16) * 16


def loop(count, body, carry=0, unroll=1):
    def steps(i, carried):
        for k in range(unroll):
            carried = body(i * unroll + k, carried)
        return carried

    return lax.fori_loop(0, count // unroll, steps, carry)


class Place:
    def __init__(self, nz):
        self.dp, self.seq = lax.axis_index("dp"), lax.axis_index("seq")
        self.z, self.x = self.dp // 2, self.dp % 2
        self.y, self.core = self.seq // 2, self.seq % 2
        self.nz = nz
        self.other_core = (self.dp, self.y * 2 + 1 - self.core)
        self.other_y = (self.dp, (1 - self.y) * 2 + self.core)
        self.diagonal = (self.dp, (1 - self.y) * 2 + 1 - self.core)
        self.other_x = (self.z * 2 + 1 - self.x, self.seq)
        self.ahead = [(((self.z + k) % nz) * 2 + self.x, self.seq) for k in range(1, nz)]

    def z_ahead(self, k):
        return (self.z + k) % self.nz


def announce(partners):
    barrier = pltpu.get_barrier_semaphore()
    for partner in partners:
        pl.semaphore_signal(barrier, inc=1, device_id=partner, device_id_type=MESH)


def meet(partners):
    pl.semaphore_wait(pltpu.get_barrier_semaphore(), len(partners))


class Remote:
    def __init__(self, copies, number, src, dst, device):
        self.copies, self.number, self.src, self.dst, self.device = copies, number, src, dst, device
        self.open = True

    def make(self, landing=False):
        return pltpu.make_async_remote_copy(
            src_ref=self.dst() if landing else self.src(),
            dst_ref=self.dst(),
            send_sem=self.copies.send_sem.at[self.number],
            recv_sem=self.copies.recv_sem.at[self.number],
            device_id=self.device,
            device_id_type=MESH,
        )

    def wait_recv(self):
        self.make(landing=True).wait_recv()

    def wait_send(self):
        if self.open:
            self.make().wait_send()
        self.open = False


class Local:
    def __init__(self, copies, number, src, dst):
        self.copies, self.number, self.src, self.dst = copies, number, src, dst

    def make(self):
        return pltpu.make_async_copy(self.src(), self.dst(), self.copies.local_sem.at[self.number])

    def wait(self):
        self.make().wait()


class Copies:
    def __init__(self, send_sem, recv_sem, local_sem):
        self.send_sem, self.recv_sem, self.local_sem = send_sem, recv_sem, local_sem
        self.local_count = 0
        self.sent = []

    def send(self, src, dst, device):
        copy = Remote(self, len(self.sent), src, dst, device)
        copy.make().start()
        self.sent.append(copy)
        return copy

    def local(self, src, dst):
        copy = Local(self, self.local_count, src, dst)
        self.local_count += 1
        copy.make().start()
        return copy

    def finish(self):
        for copy in self.sent:
            copy.wait_send()


def copy_semaphores(remote, local):
    return [
        pltpu.SemaphoreType.DMA((remote,)),
        pltpu.SemaphoreType.DMA((remote,)),
        pltpu.SemaphoreType.DMA((local,)),
    ]


ANY = pl.BlockSpec(memory_space=pl.ANY)
IN_VMEM = pl.BlockSpec(memory_space=pltpu.VMEM)


def call(kernel, outs, in_specs, out_specs, scratch, name, collective_id=None):
    params = {"vmem_limit_bytes": VMEM_BYTES}
    if collective_id is not None:
        params.update(collective_id=collective_id, has_side_effects=True)
    return pl.pallas_call(
        kernel,
        out_shape=[jax.ShapeDtypeStruct(shape, dtype) for shape, dtype in outs],
        in_specs=in_specs,
        out_specs=out_specs,
        scratch_shapes=scratch,
        compiler_params=pltpu.CompilerParams(**params),
        name=name,
    )


def lane_mask(rows, head):
    lane = lax.broadcasted_iota(jnp.int32, (rows, LANES), 1)
    return (lane >= head * HEAD) & (lane < (head + 1) * HEAD)


def row_of(vector):
    return vector[...].astype(F32).reshape(1, vector.shape[0])


def own_half(vector, y):
    row = row_of(vector)
    half = row.shape[1] // 2
    return jnp.where(y == 0, row[:, :half], row[:, half:])


def as_column(row):
    parts = [
        jnp.transpose(jnp.broadcast_to(row[:, i : i + LANES], (LANES, LANES)))
        for i in range(0, row.shape[1], LANES)
    ]
    return jnp.concatenate(parts, axis=0) if len(parts) > 1 else parts[0]


def fetch_kernel(
    nz, words, word_cot, ent_cot, ids, query_bias, key_bias, value_bias, table, query_weight, key_weight, value_weight,
    all_words, word_cots, ent_cots, all_ids, rows_out, projected, words_turned, *scratch,
):
    (table_full, table_low, picked, answers, held, from_core, from_x, from_z, from_y, ids_here, query_here, key_here, value_here) = scratch[:13]
    copies = Copies(*scratch[13:])
    place = Place(nz)
    z, x, y, core = place.z, place.x, place.y, place.core
    n_dp = 2 * nz
    word_here, ent_here = words.shape[1], ent_cot.shape[1]
    ents = ids.shape[1]
    dp_others = [((place.dp + k) % n_dp, place.seq) for k in range(1, n_dp)]
    partners = [place.other_core, place.other_y, place.diagonal] + dp_others
    announce(partners)
    half = key_here.shape[1]
    columns = span(y * half, half, LANES)
    whole_table = copies.local(lambda: table, lambda: table_full)
    weight_copies = [
        copies.local(lambda: query_weight.at[pl.ds(0, 2), :, columns], lambda: query_here),
        copies.local(lambda: key_weight.at[:, columns], lambda: key_here),
        copies.local(lambda: value_weight.at[:, columns], lambda: value_here),
    ]
    ids_here[place.dp] = ids[...]
    meet(partners)
    id_copies = [copies.send(lambda: ids, lambda: ids_here.at[place.dp], device) for device in dp_others]
    quarter = span(place.seq * word_here, word_here, 128)
    word_copies = [
        copies.send(lambda: words.at[1 - core], lambda: all_words.at[quarter], place.diagonal),
        copies.send(lambda: words.at[core], lambda: all_words.at[quarter], place.other_y),
        copies.send(lambda: words.at[1 - core], lambda: all_words.at[quarter], place.other_core),
        copies.send(lambda: word_cot.at[1 - core], lambda: word_cots.at[span(core * word_here, word_here, 128)], place.other_core),
        copies.send(lambda: ent_cot.at[1 - core], lambda: ent_cots.at[span(core * ent_here, ent_here, 32)], place.other_core),
    ]
    all_words[quarter] = words[core]
    word_cots[span(core * word_here, word_here, 128)] = word_cot[core]
    ent_cots[span(core * ent_here, ent_here, 32)] = ent_cot[core]
    whole_table.wait()
    rows_dev = table.shape[0]

    def narrow(i, _):
        where = span(i * 128, 128, 128)
        table_low[where] = table_full[where].astype(LOW)
        return 0

    loop(rows_dev // 128, narrow)
    for copy in id_copies:
        copy.wait_recv()
    all_ids[...] = ids_here[...]
    base = (place.dp * 4 + place.seq) * rows_dev
    tiles = rows_dev // LANES

    def look_up(zz):
        for g in range(4):
            asked = ids_here[zz * 2 + g // 2, pl.ds(g % 2, 1), :] - base
            column = jnp.transpose(jnp.broadcast_to(asked, (ents, ents)))
            lane = lax.broadcasted_iota(jnp.int32, (ents, LANES), 1)
            low_hit = jnp.where((column & (LANES - 1)) == lane, 1.0, 0.0).astype(LOW)
            high = jnp.clip(column >> 7, -1, tiles).astype(F32).astype(LOW)
            for j in range(tiles):
                hit = jnp.where(high == jnp.asarray(j, LOW), low_hit, jnp.zeros_like(low_hit))
                picked[pl.ds(g * ents, ents), pl.ds(j * LANES, LANES)] = hit
        answer = dot(picked[...], table_low[...]).astype(LOW)
        answers[zz] = answer.reshape(2, 2, ents, answer.shape[-1])

    order = [place.z_ahead(k + 1) for k in range(nz)]
    core_copies, x_copies, z_copies = [], [], []

    def core_send(zz):
        return copies.send(lambda: answers.at[zz, :, 1 - core], lambda: from_core.at[zz], place.other_core)

    def after_core(k):
        zz = order[k]
        core_copies[k].wait_recv()
        held[zz] = answers[zz, :, core] + from_core[zz]
        x_copies.append(copies.send(lambda: held.at[zz, 1 - x], lambda: from_x.at[zz], place.other_x))

    def after_x(k):
        zz = order[k]
        x_copies[k].wait_recv()
        held[zz, x] = held[zz, x] + from_x[zz]
        if k < nz - 1:
            z_copies.append(copies.send(lambda: held.at[zz, x], lambda: from_z.at[k], place.ahead[k]))

    query_b = query_bias[:, columns].astype(F32)

    def project(i):
        weight = (query_here.at[0], query_here.at[1], key_here, value_here)[i]
        bias = query_b[i : i + 1] if i < 2 else own_half((key_bias, value_bias)[i - 2], y)
        projected[i] = (dot(all_words[...], weight[...]) + bias).astype(LOW)

    def turn_words(part):
        for i in range(part, words.shape[2] // LANES, 2):
            here = slice(i * LANES, (i + 1) * LANES)
            words_turned[here, :] = jnp.transpose(all_words[:, here].astype(F32)).astype(LOW)

    for k in range(nz + 2):
        if k == nz:
            for copy in word_copies[:3]:
                copy.wait_recv()
            for copy in weight_copies:
                copy.wait()
            project(0)
            project(1)
        if k == nz + 1:
            project(2)
        if k < nz:
            look_up(order[k])
            core_copies.append(core_send(order[k]))
        if 0 <= k - 1 < nz:
            after_core(k - 1)
        if 0 <= k - 2:
            after_x(k - 2)
    project(3)
    total = held[z, x]
    for k in range(nz - 1):
        z_copies[k].wait_recv()
        total = total + from_z[k]
    from_y[0] = total
    y_copy = copies.send(lambda: from_y.at[0], lambda: from_y.at[1], place.other_y)
    turn_words(0)
    turn_words(1)
    y_copy.wait_recv()
    rows_out[...] = from_y[0] + from_y[1]
    for copy in word_copies[3:]:
        copy.wait_recv()
    copies.finish()


def fetch(nz, words, word_cot, ent_cot, ids, query_bias, key_bias, value_bias, table, query_weight, key_weight, value_weight):
    _, word_here, width = words.shape
    ent_here, ents, (rows_dev, edim) = ent_cot.shape[1], ids.shape[1], table.shape
    n_dp = 2 * nz
    return call(
        functools.partial(fetch_kernel, nz),
        [
            ((4 * word_here, width), LOW),
            ((2 * word_here, width), LOW),
            ((2 * ent_here, width), LOW),
            ((n_dp, 2, ents), jnp.int32),
            ((ents, edim), LOW),
            ((4, 4 * word_here, width // 2), LOW),
            ((width, 4 * word_here), LOW),
        ],
        [IN_VMEM] * 7 + [ANY] * 4,
        [IN_VMEM] * 7,
        [
            pltpu.VMEM((rows_dev, edim), F32),
            pltpu.VMEM((rows_dev, edim), LOW),
            pltpu.VMEM((4 * ents, rows_dev), LOW),
            pltpu.VMEM((nz, 2, 2, ents, edim), LOW),
            pltpu.VMEM((nz, 2, ents, edim), LOW),
            pltpu.VMEM((nz, 2, ents, edim), LOW),
            pltpu.VMEM((nz, ents, edim), LOW),
            pltpu.VMEM((nz - 1, ents, edim), LOW),
            pltpu.VMEM((2, ents, edim), LOW),
            pltpu.VMEM((n_dp, 2, ents), jnp.int32),
            pltpu.VMEM((2, width, width // 2), LOW),
            pltpu.VMEM((width, width // 2), LOW),
            pltpu.VMEM((width, width // 2), LOW),
        ]
        + copy_semaphores(n_dp + 4 + 3 * nz + 2, 4),
        "fetch",
        1,
    )(words, word_cot, ent_cot, ids, query_bias, key_bias, value_bias, table, query_weight, key_weight, value_weight)


class Engine:
    RATES = {"core": 300e3, "x": 52e3, "y": 52e3, "z": 13e3}
    LATENCY = 2.0

    def __init__(self):
        self.clock, self.free, self.streams = 0.0, {}, []

    def transfer(self, link, size):
        start = max(self.clock, self.free.get(link, 0.0))
        self.free[link] = start + size / self.RATES[link]
        return self.free[link] + self.LATENCY

    def add(self, steps):
        self.streams.append([self.clock, list(steps)])
        self.poll()

    def run(self, stream):
        self.clock = max(self.clock, stream[0])
        ready = stream[1].pop(0)()
        stream[0] = self.clock if ready is None else ready

    def next(self):
        live = [stream for stream in self.streams if stream[1]]
        return min(live, key=lambda stream: stream[0]) if live else None

    def poll(self):
        while (stream := self.next()) is not None and stream[0] <= self.clock:
            self.run(stream)

    def work(self, time):
        self.clock += time
        self.poll()

    def drain(self):
        while (stream := self.next()) is not None:
            self.run(stream)


def blocks_of(rows):
    for size in (96, 64, 48, 32):
        if rows % size == 0:
            return size
    return 16


def add_blocks(engine, target, parts, leading, rows, columns):
    size = blocks_of(rows)
    count = rows // size

    def block(i, _):
        lead, row = i // count, (i % count) * size
        where = span(row, size, 16)
        if len(parts) == 2:
            value = parts[0](lead, where) + parts[1](lead, where)
        else:
            value = parts[0](lead, where).astype(F32)
            for part in parts[1:]:
                value = value + part(lead, where).astype(F32)
            value = value.astype(LOW)
        target(lead, where, value)
        return 0

    loop(leading * count, block)
    engine.clock += 0.3 + leading * rows * columns / 1e6


class Job:
    def __init__(self, grads, reduced, base, size, order, columns):
        self.grads, self.reduced, self.base, self.size, self.order, self.columns = grads, reduced, base, size, order, columns
        self.half = size // 2
        self.part = size // 4 if order == "yxz" else size // 2

    def scratch(self, nz):
        shapes = [(nz, 2, self.half, self.columns)]
        if self.order == "yxz":
            shapes.append((nz, 2, self.part, self.columns))
        elif self.order == "xzy":
            shapes.append((2, self.part, self.columns))
        shapes += [(nz, self.part, self.columns), (nz - 1, self.part, self.columns)]
        return [pltpu.VMEM(shape, LOW) for shape in shapes]

    def remote_count(self, nz):
        return 1 + (1 if self.order != "xz" else 0) + 1 + (nz - 1) + 1 + 1

    def prepare(self, engine, place, copies, scratch):
        nz, z, x, y, core = place.nz, place.z, place.x, place.y, place.core
        base, half, part, order, columns = self.base, self.half, self.part, self.order, self.columns
        held = self.grads.at[:, :, span(base + core * half, half, 16)]
        from_core = scratch[0]
        from_y = scratch[1] if order != "xz" else None
        from_x, from_z = scratch[-2:]
        live = {}
        row_bytes = 2 * columns
        theirs = span(base + (1 - core) * half, half, 16)
        mine = span(base + core * half, half, 16)
        own_rows = span(y * part, part, 16) if order == "yxz" else pl.ds(0, part)
        final_rows = span(base + core * half + (y * part if order == "yxz" else 0), part, 16)

        def start():
            live["core"] = copies.send(lambda: self.grads.at[:, :, theirs], lambda: from_core, place.other_core)
            return engine.transfer("core", 2 * nz * half * row_bytes)

        def send_x():
            live["x"] = copies.send(lambda: held.at[:, 1 - x, own_rows], lambda: from_x, place.other_x)
            return engine.transfer("x", nz * part * row_bytes)

        def after_core():
            live["core"].wait_recv()

            def put(i, where, value):
                held[i // 2, i % 2, where] = value

            add_blocks(
                engine,
                put,
                [lambda i, where: held[i // 2, i % 2, where], lambda i, where: from_core[i // 2, i % 2, where]],
                2 * nz,
                half,
                columns,
            )
            if order == "yxz":
                live["y"] = copies.send(
                    lambda: held.at[:, :, span((1 - y) * part, part, 16)], lambda: from_y, place.other_y
                )
                return engine.transfer("y", 2 * nz * part * row_bytes)
            return send_x()

        def shifted(where):
            return span(y * part + where.start, where.size, 16) if order == "yxz" else where

        def after_y():
            live["y"].wait_recv()

            def put(i, where, value):
                held[i // 2, i % 2, shifted(where)] = value

            add_blocks(
                engine,
                put,
                [lambda i, where: held[i // 2, i % 2, shifted(where)], lambda i, where: from_y[i // 2, i % 2, where]],
                2 * nz,
                part,
                columns,
            )
            return send_x()

        def send_z(k):
            return copies.send(
                lambda: held.at[place.z_ahead(k + 1), x, own_rows], lambda: from_z.at[k], place.ahead[k]
            )

        def after_x():
            live["x"].wait_recv()

            def put(i, where, value):
                held[i, x, shifted(where)] = value

            add_blocks(
                engine,
                put,
                [lambda i, where: held[i, x, shifted(where)], lambda i, where: from_x[i, where]],
                nz,
                part,
                columns,
            )
            live["z"] = [send_z(k) for k in range(nz - 1)]
            return engine.transfer("z", part * row_bytes)

        def after_z():
            for copy in live["z"]:
                copy.wait_recv()

            def put(i, where, value):
                if order == "yxz":
                    self.reduced[span(base + core * half + y * part + where.start, where.size, 16)] = value
                elif order == "xz":
                    self.reduced[y, span(base + core * half + where.start, where.size, 16)] = value
                else:
                    from_y[0, where] = value

            def parts(k):
                return lambda i, where: from_z[k, where]

            add_blocks(
                engine,
                put,
                [lambda i, where: held[z, x, shifted(where)]] + [parts(k) for k in range(nz - 1)],
                1,
                part,
                columns,
            )
            if order == "xzy":
                live["y2"] = copies.send(lambda: from_y.at[0], lambda: from_y.at[1], place.other_y)
            else:
                view = lambda: self.reduced.at[final_rows] if order == "yxz" else self.reduced.at[y, final_rows]
                live["y2"] = copies.send(view, view, place.other_y)
            return engine.transfer("y", part * row_bytes)

        def after_gather():
            live["y2"].wait_recv()
            if order == "xzy":

                def put(i, where, value):
                    self.reduced[span(base + core * half + where.start, where.size, 16)] = value

                add_blocks(
                    engine, put, [lambda i, where: from_y[0, where], lambda i, where: from_y[1, where]], 1, part, columns
                )
            view = lambda: self.reduced.at[:, mine] if order == "xz" else self.reduced.at[mine]
            live["core2"] = copies.send(view, view, place.other_core)
            return engine.transfer("core", 2 * half * row_bytes)

        def end():
            live["core2"].wait_recv()

        middle_steps = [after_core, after_y, after_x] if order == "yxz" else [after_core, after_x]
        self.steps = [start] + middle_steps + [after_z, after_gather, end]


def lane_mean(value):
    return jnp.mean(value, axis=-1, keepdims=True)


def column_sum(value):
    return jnp.sum(value, axis=0, keepdims=True)


ROW_BLOCK = 32


def ffn_plan(n_dp, width, ff):
    down_rows, row_pad = ff // n_dp, padded(width // n_dp)
    size = 128 if down_rows % 128 == 0 else 32
    order = "yxz" if size % 64 == 0 else "xzy"
    plan = [(base, size, order) for base in range(0, down_rows, size)]
    base = down_rows
    for pair in range(ff // width // 2):
        order = "yxz" if row_pad % 32 == 0 else "xzy"
        plan.append((base, 2 * row_pad, order))
        base += 2 * row_pad
    plan.append((base, row_pad, "xzy"))
    return plan


def layer_kernel(
    nz, plan, words, projected, words_turned, segments, pos_table, query_bias, key_bias, value_bias, out_weight, out_bias, gains, shifts, up_weight, up_bias, down_weight, down_bias, word_cots, ent_cots,
    query_weight, key_weight, value_weight, rows, ent_pos, ent_proj, ids,
    word_out, ent_out, word_grad, ffn_reduced, attn_reduced, ent_reduced, bias_out, table_grad, touched,
    hidden_turned_in, query_words_in, query_ents_in, keys_in, values_in, probs_in, *scratch,
):
    (from_y_mixed, grad_mixed, grad_one, given, ffn_sum, attn_sum, ent_sum, bias_held, bias_from, all_rows, bias_heads, bias_middle,
     ffn_grads, grad_mixed_here, row_parts, mixed, ent_keep) = scratch[:17]
    copies = Copies(*scratch[-3:])
    engine = Engine()
    place = Place(nz)
    z, x, y, core = place.z, place.x, place.y, place.core
    n_dp = 2 * nz
    tokens, half = mixed.shape
    width = 2 * half
    ents = rows.shape[0]
    all_words = tokens - ents
    word_half, ent_half = all_words // 2, ents // 2
    part_tokens = tokens // 2
    ff = up_weight.shape[1]
    parts = ff // width
    row_part, row_pad, down_rows = width // n_dp, padded(width // n_dp), ff // n_dp
    partners = [place.other_core, place.other_y, place.other_x] + place.ahead
    announce(partners)

    jobs = {"ffn": [], "attn": [], "ent": []}

    def make_jobs(names, sources):
        at = 17
        for name, number, base, size, order, columns in plan:
            grads, reduced = sources.get(name, (None, None))
            if name == "attn" and grads is not None:
                grads, reduced = grads.at[number], reduced.at[number]
            job = Job(grads, reduced, base, size, order, columns)
            used = len(job.scratch(nz))
            if name in names:
                job.prepare(engine, place, copies, scratch[at : at + used])
                jobs[name].append(job)
            at += used

    make_jobs(["ffn"], {"ffn": (ffn_grads, ffn_sum)})

    def token_rows(side):
        return span(side * word_half, word_half, LANES), span(all_words + side * ent_half, ent_half, 64)

    mine, theirs = token_rows(y), token_rows(1 - y)
    own_columns, other_columns = span(y * half, half, LANES), span((1 - y) * half, half, LANES)
    word_part, ent_part = pl.ds(0, word_half), pl.ds(word_half, ent_half)
    mixed_copies = []
    scale = 1.0 / math.sqrt(HEAD)
    tiles = tokens // LANES

    def attend_phase(
        hidden_turned, query_words, query_ents, keys, values, probs, query_here, key_here, value_here, pos_here, values_turned, mask,
    ):
        weight_copies = [
            copies.local(lambda: pos_table, lambda: pos_here),
            copies.local(lambda: query_weight.at[pl.ds(2, 2), :, own_columns], lambda: query_here),
            copies.local(lambda: key_weight.at[:, own_columns], lambda: key_here),
            copies.local(lambda: value_weight.at[:, own_columns], lambda: value_here),
        ]
        word_rows = pl.ds(0, all_words)
        targets = [query_words, query_ents, keys, values]
        for i, target in enumerate(targets):
            weight_copies.append(
                copies.local(lambda i=i: projected.at[i], lambda target=target: target.at[word_rows])
            )
        weight_copies.append(copies.local(lambda: words_turned, lambda: hidden_turned.at[:, word_rows]))
        position = as_column(ent_pos[pl.ds(core, 1), :])
        picks = []
        for j in range(all_words // LANES):
            number = lax.broadcasted_iota(jnp.int32, (ents, LANES), 1) + j * LANES
            picks.append(jnp.where(position == number, 1.0, 0.0))
        pick = jnp.concatenate(picks, axis=1)
        word_seg = segments[pl.ds(core, 1), :].astype(F32)
        ent_seg = jnp.sum(pick * word_seg, axis=1, keepdims=True)
        weight_copies[0].wait()
        ent_hidden = dot(rows[...], ent_proj[...]) + dot(pick.astype(LOW), pos_here[...])
        ent_keep[...] = jnp.where(y == 0, ent_hidden[:ent_half], ent_hidden[ent_half:])
        ent_row = jnp.transpose(jnp.broadcast_to(ent_seg, (ents, LANES)))[:1]
        seg_row = jnp.concatenate([word_seg, ent_row], axis=1)
        seg_column = jnp.concatenate([as_column(word_seg), jnp.broadcast_to(ent_seg, (ents, LANES))], axis=0)
        for j in range(tiles):
            here = slice(j * LANES, (j + 1) * LANES)
            mask[:, here] = jnp.where(seg_column == seg_row[:, here], 0.0, masked_score)
        query_b = query_bias[:, own_columns].astype(F32)
        for copy in weight_copies[1:]:
            copy.wait()
        ent_low = ent_hidden.astype(LOW)
        query_words[all_words:] = (dot(ent_low, query_here[0]) + query_b[2:3]).astype(LOW)
        query_ents[all_words:] = (dot(ent_low, query_here[1]) + query_b[3:4]).astype(LOW)
        keys[all_words:] = (dot(ent_low, key_here[...]) + own_half(key_bias, y)).astype(LOW)
        values[all_words:] = (dot(ent_low, value_here[...]) + own_half(value_bias, y)).astype(LOW)
        hidden_turned[:, all_words:] = jnp.transpose(ent_hidden).astype(LOW)
        values_turned[...] = jnp.transpose(values[...].astype(F32)).astype(LOW)
        spills = [
            copies.local(lambda: query_words, lambda: query_words_in),
            copies.local(lambda: query_ents, lambda: query_ents_in),
            copies.local(lambda: keys, lambda: keys_in),
            copies.local(lambda: values, lambda: values_in),
        ]
        for pair in range(half // LANES):
            lanes = slice(pair * LANES, (pair + 1) * LANES)
            key, turned = keys[:, lanes], values_turned[lanes, :]
            row = lax.broadcasted_iota(jnp.int32, (LANES, tokens), 0)
            own_key, own_turned = [], []
            for head in range(2):
                own_key.append(jnp.where(lane_mask(tokens, head), key, jnp.zeros_like(key)))
                own_rows = (row >= head * HEAD) & (row < (head + 1) * HEAD)
                own_turned.append(jnp.where(own_rows, turned, jnp.zeros_like(turned)))
            for i in range(tiles):
                here = slice(i * LANES, (i + 1) * LANES)
                query_w, query_e = query_words[here, lanes], query_ents[here, lanes]
                part_sum = None
                for head in range(2):
                    raw = jnp.concatenate(
                        [dot_rows(own_key[head][:all_words], query_w), dot_rows(own_key[head][all_words:], query_e)], axis=0
                    )
                    score = raw * scale + mask[:, here]
                    weight = jnp.exp(score - jnp.max(score, axis=0, keepdims=True))
                    prob = (weight * (1.0 / jnp.sum(weight, axis=0, keepdims=True))).astype(LOW)
                    probs[pair * 2 + head, :, here] = prob
                    part = dot(own_turned[head], prob)
                    part_sum = part if part_sum is None else part_sum + part
                mixed[here, lanes] = jnp.transpose(part_sum).astype(LOW)
            heads = pl.ds(pair * 2, 2)
            if pair == 0:
                meet(partners)
            mixed_copies.extend([
                copies.send(
                    lambda lanes=lanes: mixed.at[theirs[0], lanes], lambda lanes=lanes: from_y_mixed.at[word_part, lanes], place.other_y
                ),
                copies.send(
                    lambda lanes=lanes: mixed.at[theirs[1], lanes], lambda lanes=lanes: from_y_mixed.at[ent_part, lanes], place.other_y
                ),
            ])
            spills.append(copies.local(lambda heads=heads: probs.at[heads], lambda heads=heads: probs_in.at[heads]))
        spills.append(copies.local(lambda: hidden_turned, lambda: hidden_turned_in))
        for copy in spills:
            copy.wait()

    pl.run_scoped(
        attend_phase,
        pltpu.VMEM((width, tokens), LOW),
        pltpu.VMEM((tokens, half), LOW),
        pltpu.VMEM((tokens, half), LOW),
        pltpu.VMEM((tokens, half), LOW),
        pltpu.VMEM((tokens, half), LOW),
        pltpu.VMEM((HEADS // 2, tokens, tokens), LOW),
        pltpu.VMEM((2, width, half), LOW),
        pltpu.VMEM((width, half), LOW),
        pltpu.VMEM((width, half), LOW),
        pltpu.VMEM((all_words, width), LOW),
        pltpu.VMEM((half, tokens), LOW),
        pltpu.VMEM((tokens, tokens), F32),
    )
    out_copies, mixed_back = [], []

    def forward_phase(
        out_here, up_here, down_here, word_here, mixed_full, work, normed_low, normal_one, inverse_one,
        act, slope, output, grad_two, grad_two_low, grad_one_low, normed_turned,
    ):
        cot, grad_up_low = output, slope
        weight_copies = [
            copies.local(lambda: out_weight, lambda: out_here),
            copies.local(lambda: words.at[mine[0]], lambda: word_here),
            copies.local(lambda: up_weight, lambda: up_here),
            copies.local(lambda: down_weight, lambda: down_here),
            copies.local(lambda: word_cots, lambda: cot.at[word_part]),
            copies.local(lambda: ent_cots, lambda: cot.at[ent_part]),
        ]
        gain, shift = gains[...].astype(F32), shifts[...].astype(F32)
        out_b, down_b, up_b = row_of(out_bias), row_of(down_bias), row_of(up_bias)
        mixed_full[word_part, own_columns] = mixed[mine[0]]
        mixed_full[ent_part, own_columns] = mixed[mine[1]]
        for copy in weight_copies[:2]:
            copy.wait()
        work[...] = dot(mixed_full[:, own_columns], out_here[own_columns, :])
        for copy in mixed_copies:
            copy.wait_recv()
        mixed_full[:, other_columns] = from_y_mixed[...]
        work[...] += dot(from_y_mixed[...], out_here[other_columns, :])

        def norm_one(residual):
            def step(i, _):
                rows = span(residual[1] + i * ROW_BLOCK, ROW_BLOCK, ROW_BLOCK)
                value = residual[0][span(i * ROW_BLOCK, ROW_BLOCK, ROW_BLOCK)].astype(F32) + (work[rows] + out_b)
                center = value - lane_mean(value)
                inverse = lax.rsqrt(lane_mean(center * center) + norm_eps)
                normal = center * inverse
                result = normal * gain[0:1] + shift[0:1]
                normal_one[rows] = normal
                inverse_one[rows] = jnp.broadcast_to(inverse, (ROW_BLOCK, LANES))
                normed_low[rows] = result.astype(LOW)
                return 0

            return step

        loop(word_half // ROW_BLOCK, norm_one((word_here, 0)), 0, 2)
        loop(ent_half // ROW_BLOCK, norm_one((ent_keep, word_half)), 0, 2)
        weight_copies[2].wait()
        for j in range(parts):
            columns = slice(j * width, (j + 1) * width)
            work[...] = dot(normed_low[...], up_here[:, columns]) + up_b[:, columns]

            def gelu(i, _):
                rows = span(i * ROW_BLOCK, ROW_BLOCK, ROW_BLOCK)
                value = work[rows]
                below = 0.5 * (1.0 + lax.erf(value * (1.0 / math.sqrt(2.0))))
                density = jnp.exp(-0.5 * value * value) * (1.0 / math.sqrt(2.0 * math.pi))
                act[rows, columns] = (value * below).astype(LOW)
                slope[rows, columns] = (below + value * density).astype(LOW)
                return 0

            loop(part_tokens // ROW_BLOCK, gelu)
        normed_turned[...] = jnp.transpose(normed_low[...].astype(F32)).astype(LOW)
        for copy in weight_copies[3:]:
            copy.wait()
        work[...] = dot(act[...], down_here[...])

        def norm_two(i, sums):
            rows = span(i * ROW_BLOCK, ROW_BLOCK, ROW_BLOCK)
            value = (normal_one[rows] * gain[0:1] + shift[0:1]) + (work[rows] + down_b)
            center = value - lane_mean(value)
            inverse = lax.rsqrt(lane_mean(center * center) + norm_eps)
            normal = center * inverse
            cotangent = cot[rows].astype(F32)
            output[rows] = (normal * gain[1:2] + shift[1:2]).astype(LOW)
            scaled = cotangent * gain[1:2]
            result = inverse * (scaled - lane_mean(scaled) - normal * lane_mean(scaled * normal))
            grad_two[rows] = result
            grad_two_low[rows] = result.astype(LOW)
            return (
                sums[0] + column_sum(cotangent * normal),
                sums[1] + column_sum(cotangent),
                sums[2] + column_sum(result),
            )

        nothing = jnp.zeros((1, width), F32)
        gain_two, shift_two, down_sum = loop(part_tokens // ROW_BLOCK, norm_two, (nothing, nothing, nothing), 2)
        quarter, ent_quarter = word_half // 2, ent_half // 2
        out_copies.extend([
            copies.send(
                lambda: output.at[span((1 - core) * quarter, quarter, LANES)], lambda: word_out.at[core], place.other_core
            ),
            copies.send(
                lambda: output.at[span(word_half + (1 - core) * ent_quarter, ent_quarter, 32)],
                lambda: ent_out.at[core],
                place.other_core,
            ),
        ])
        out_local = [
            copies.local(lambda: output.at[span(core * quarter, quarter, LANES)], lambda: word_out.at[core]),
            copies.local(
                lambda: output.at[span(word_half + core * ent_quarter, ent_quarter, 32)], lambda: ent_out.at[core]
            ),
        ]
        engine.clock = 0.0
        engine.free = {}
        def put(base, value):
            ffn_grads[:, :, pl.ds(base, row_part)] = value.astype(LOW).reshape(nz, 2, row_part, width)

        def down_products():
            per = width // down_rows
            for j in range(parts):
                value = dot_columns(act[:, j * width : (j + 1) * width], grad_two_low[...])
                value = value.astype(LOW).reshape(per, down_rows, width)
                for d in range(per):
                    slab = j * per + d
                    ffn_grads[slab // 2, slab % 2, pl.ds(0, down_rows)] = value[d]

        up_sums = []

        def grad_up(j):
            columns = slice(j * width, (j + 1) * width)
            work[...] = dot_rows(grad_two_low[...], down_here[columns, :])

            def grad_gelu(i, total_row):
                rows = span(i * ROW_BLOCK, ROW_BLOCK, ROW_BLOCK)
                value = work[rows] * slope[rows, columns].astype(F32)
                grad_up_low[rows, columns] = value.astype(LOW)
                return total_row + column_sum(value)

            up_sums.append(loop(part_tokens // ROW_BLOCK, grad_gelu, nothing, 2))
            engine.work(1.6)

        def up_product(j):
            columns = slice(j * width, (j + 1) * width)
            put(down_rows + j * row_pad, dot(normed_turned[...], grad_up_low[:, columns]))
            engine.work(0.9)

        downs = [job for job in jobs["ffn"] if job.base < down_rows]
        ups = [job for job in jobs["ffn"] if down_rows <= job.base][:-1]
        down_products()
        engine.clock += 3.0
        for job in downs:
            engine.add(job.steps)
        for j in range(parts):
            grad_up(j)
        work[...] = dot_rows(grad_up_low[...], up_here[...])
        engine.work(2.0)

        def back_one(i, sums):
            rows = span(i * ROW_BLOCK, ROW_BLOCK, ROW_BLOCK)
            upper = grad_two[rows] + work[rows]
            normal = normal_one[rows]
            inverse = inverse_one[rows, 0:1]
            scaled = upper * gain[0:1]
            result = inverse * (scaled - lane_mean(scaled) - normal * lane_mean(scaled * normal))
            grad_one[rows] = result
            grad_one_low[rows] = result.astype(LOW)
            return (
                sums[0] + column_sum(upper * normal),
                sums[1] + column_sum(upper),
                sums[2] + column_sum(result),
            )

        gain_one, shift_one, out_sum = loop(part_tokens // ROW_BLOCK, back_one, (nothing, nothing, nothing), 2)
        engine.work(1.0)
        grad_mixed_here[...] = dot_rows(grad_one_low[...], out_here[other_columns, :]).astype(LOW)
        mixed_back.extend([
            copies.send(lambda: grad_mixed_here.at[word_part], lambda: grad_mixed.at[mine[0]], place.other_y),
            copies.send(lambda: grad_mixed_here.at[ent_part], lambda: grad_mixed.at[mine[1]], place.other_y),
        ])
        engine.transfer("y", part_tokens * half * 2)
        own = dot_rows(grad_one_low[...], out_here[own_columns, :]).astype(LOW)
        grad_mixed[mine[0]] = own[:word_half]
        grad_mixed[mine[1]] = own[word_half:]
        engine.work(1.0)
        for j in range(parts):
            up_product(j)
            if j % 2 == 1:
                engine.add(ups[j // 2].steps)
        put(down_rows + parts * row_pad, dot_columns(mixed_full[...], grad_one_low[...]))
        engine.work(0.8)
        engine.add(jobs["ffn"][-1].steps)
        bias_rows = [out_sum, gain_one, gain_two, shift_one, shift_two] + up_sums + [down_sum]
        for i, row in enumerate(bias_rows):
            bias_middle[i : i + 1] = row
        for copy in out_copies:
            copy.wait_send()
        for copy in out_local:
            copy.wait()

    tall = lambda columns, dtype: pltpu.VMEM((part_tokens, columns), dtype)
    pl.run_scoped(
        forward_phase,
        pltpu.VMEM((width, width), LOW),
        pltpu.VMEM((width, ff), LOW),
        pltpu.VMEM((ff, width), LOW),
        pltpu.VMEM((word_half, width), LOW),
        tall(width, LOW),
        tall(width, F32),
        tall(width, LOW),
        tall(width, F32),
        tall(LANES, F32),
        tall(ff, LOW),
        tall(ff, LOW),
        tall(width, LOW),
        tall(width, F32),
        tall(width, LOW),
        tall(width, LOW),
        pltpu.VMEM((width, part_tokens), LOW),
    )
    live_words = {}

    def backward_phase(
        query_words, query_ents, keys, values, probs, query_here, key_here, value_here, keys_turned,
        grad_query_words, grad_query_ents, grad_keys, grad_values, hidden_turned, grad_hidden, hits, attn_grads, ent_grads, table_here, touched_here,
    ):
        total = grad_one
        make_jobs(["attn", "ent"], {"attn": (attn_grads, attn_sum), "ent": (ent_grads, ent_sum)})
        columns = span(y * half, half, LANES)
        copies_in = [
            copies.local(lambda: values_in, lambda: values),
            copies.local(lambda: keys_in, lambda: keys),
            copies.local(lambda: query_words_in, lambda: query_words),
            copies.local(lambda: query_ents_in, lambda: query_ents),
        ]
        prob_copies = []
        for head in range(probs.shape[0]):
            prob_copies.append(
                copies.local(lambda head=head: probs_in.at[head], lambda head=head: probs.at[head])
            )
        hidden_copy = copies.local(lambda: hidden_turned_in, lambda: hidden_turned)
        weight_copies = [
            copies.local(lambda: query_weight.at[:, :, columns], lambda: query_here),
            copies.local(lambda: key_weight.at[:, columns], lambda: key_here),
            copies.local(lambda: value_weight.at[:, columns], lambda: value_here),
        ]
        for copy in copies_in:
            copy.wait()
        for i in range(half // LANES):
            lanes = slice(i * LANES, (i + 1) * LANES)
            keys_turned[lanes, :] = jnp.transpose(keys[:, lanes].astype(F32)).astype(LOW)
        for copy in mixed_back:
            copy.wait_recv()
        engine.work(2.0)
        def pair_products(pair):
            lanes = slice(pair * LANES, (pair + 1) * LANES)
            word_turned, ent_turned = hidden_turned[:, :all_words], hidden_turned[:, all_words:]
            products = [
                dot(word_turned, grad_query_words[:all_words, lanes]),
                dot(word_turned, grad_query_ents[:all_words, lanes]),
                dot(ent_turned, grad_query_words[all_words:, lanes]),
                dot(ent_turned, grad_query_ents[all_words:, lanes]),
                dot(hidden_turned[...], grad_keys[:, lanes]),
                dot(hidden_turned[...], grad_values[:, lanes]),
            ]
            for i, value in enumerate(products):
                attn_grads[pair, :, :, pl.ds(i * row_pad, row_part)] = value.astype(LOW).reshape(nz, 2, row_part, LANES)
            engine.work(1.5)
            engine.add(jobs["attn"][pair].steps)

        for pair in range(half // LANES):
            lanes = slice(pair * LANES, (pair + 1) * LANES)
            grad_query_w = jnp.zeros((LANES, tokens), F32)
            grad_query_e = jnp.zeros((LANES, tokens), F32)
            grad_key_w = jnp.zeros((all_words, LANES), F32)
            grad_key_e = jnp.zeros((ents, LANES), F32)
            grad_value = jnp.zeros((tokens, LANES), F32)
            for head in range(2):
                own = lane_mask(tokens, head)
                value = values[:, lanes]
                own_value = jnp.where(own, value, jnp.zeros_like(value))
                prob_copies[pair * 2 + head].wait()

                given_heads = grad_mixed[:, lanes]
                grad_scores = probs.at[pair * 2 + head]
                grad_value += dot(grad_scores[...], jnp.where(own, given_heads, jnp.zeros_like(given_heads)))
                for i in range(tiles):
                    where = slice(i * LANES, (i + 1) * LANES)
                    grad_prob = dot_rows(own_value, grad_mixed[where, lanes])
                    prob = grad_scores[:, where].astype(F32)
                    both = prob * grad_prob
                    grad_scores[:, where] = (both - prob * jnp.sum(both, axis=0, keepdims=True)).astype(LOW)
                engine.work(1.7)
                query_w, query_e = query_words[:, lanes], query_ents[:, lanes]
                grad_key_w += dot(grad_scores[:all_words], jnp.where(own, query_w, jnp.zeros_like(query_w)))
                grad_key_e += dot(grad_scores[all_words:], jnp.where(own, query_e, jnp.zeros_like(query_e)))
                row = lax.broadcasted_iota(jnp.int32, (LANES, tokens), 0)
                own_rows = (row >= head * HEAD) & (row < (head + 1) * HEAD)
                turned = keys_turned[lanes, :]
                turned = jnp.where(own_rows, turned, jnp.zeros_like(turned))
                grad_query_w += dot(turned[:, :all_words], grad_scores[:all_words])
                grad_query_e += dot(turned[:, all_words:], grad_scores[all_words:])
                engine.work(1.7)
            grad_query_w = jnp.transpose(grad_query_w) * scale
            grad_query_e = jnp.transpose(grad_query_e) * scale
            grad_key_w, grad_key_e = grad_key_w * scale, grad_key_e * scale
            sums = [
                column_sum(grad_query_w[:all_words]),
                column_sum(grad_query_e[:all_words]),
                column_sum(grad_query_w[all_words:]),
                column_sum(grad_query_e[all_words:]),
                column_sum(grad_key_w) + column_sum(grad_key_e),
                column_sum(grad_value),
            ]
            for i, sum_row in enumerate(sums):
                bias_heads[i : i + 1, lanes] = sum_row
            grad_query_words[:, lanes] = grad_query_w.astype(LOW)
            grad_query_ents[:, lanes] = grad_query_e.astype(LOW)
            grad_keys[:all_words, lanes] = grad_key_w.astype(LOW)
            grad_keys[all_words:, lanes] = grad_key_e.astype(LOW)
            grad_values[:, lanes] = grad_value.astype(LOW)
            engine.work(0.5)
            if pair == 0:
                hidden_copy.wait()
            if pair + 1 < half // LANES:
                pair_products(pair)

        for copy in weight_copies:
            copy.wait()
        ent_rows, word_rows = slice(all_words, tokens), slice(0, all_words)

        def hidden_part(here, first, second):
            grad_hidden[here] = (
                dot_rows(grad_keys[here], key_here[...])
                + dot_rows(grad_values[here], value_here[...])
                + dot_rows(grad_query_words[here], query_here[first])
                + dot_rows(grad_query_ents[here], query_here[second])
            ).astype(LOW)

        hidden_part(ent_rows, 2, 3)
        own_ents = lax.broadcasted_iota(jnp.int32, (ents, width), 0) // ent_half == y
        twice = jnp.concatenate([grad_one[word_half:], grad_one[word_half:]], axis=0)
        ent_sum_part = grad_hidden[ent_rows].astype(F32) + jnp.where(own_ents, twice, 0.0)
        row_parts[0] = dot_rows(ent_sum_part.astype(LOW), ent_proj[...]).astype(LOW)
        rows_copy = copies.send(lambda: row_parts.at[0], lambda: row_parts.at[1], place.other_y)
        row_bytes = ents * ent_proj.shape[0] * 2
        rows_ready = engine.transfer("y", row_bytes)
        engine.work(0.7)
        pair_products(half // LANES - 1)
        ent_copy = copies.send(lambda: grad_hidden.at[theirs[1]], lambda: given.at[ent_part], place.other_y)
        ent_ready = engine.transfer("y", ent_half * width * 2)

        live_rows = {}

        def sum_hidden(start, count, own_start):
            def block(i, _):
                where = span(start + i * 32, 32, 32)
                own = span(own_start + i * 32, 32, 32)
                total[where] = grad_one[where] + (grad_hidden[own].astype(F32) + given[where].astype(F32))
                return 0

            loop(count // 32, block)

        def rows_z():
            rows_copy.wait_recv()
            all_rows[place.dp, core] = row_parts[0] + row_parts[1]
            view = lambda: all_rows.at[place.dp, core]
            live_rows["z"] = [copies.send(view, view, device) for device in place.ahead]
            return engine.transfer("z", row_bytes)

        def rows_x():
            for copy in live_rows["z"]:
                copy.wait_recv()
            live_rows["x"] = []
            for k in range(nz):
                view = lambda k=k: all_rows.at[place.z_ahead(k) * 2 + x, core]
                live_rows["x"].append(copies.send(view, view, place.other_x))
            return engine.transfer("x", nz * row_bytes)

        def rows_core():
            for copy in live_rows["x"]:
                copy.wait_recv()
            view = lambda: all_rows.at[:, core]
            live_rows["core"] = copies.send(view, view, place.other_core)
            return engine.transfer("core", n_dp * row_bytes)

        rows_dev = table_grad.shape[0]
        table_copies = []
        base_row = (place.dp * 4 + place.seq) * rows_dev

        def table_part(i):
            def step():
                if i == 0:
                    live_rows["core"].wait_recv()
                groups = ids.shape[0]
                block = min(table_block, LANES)
                counts = [jnp.zeros((block, ents), LOW) for _ in range(table_block // block)]
                for group in range(groups):
                    asked = ids[group : group + 1, :] - base_row
                    high = jnp.clip(asked >> 7, -1, rows_dev // LANES).astype(F32)
                    high = jnp.broadcast_to(high, (block, ents)).astype(LOW)
                    first_row = i * table_block
                    number = lax.broadcasted_iota(jnp.int32, (block, ents), 0) + first_row % LANES
                    low_hit = jnp.where((asked & (LANES - 1)) == number, 1.0, 0.0).astype(LOW)
                    for k in range(len(counts)):
                        hit = jnp.where(
                            high == jnp.asarray(first_row // LANES + k, LOW), low_hit, jnp.zeros_like(low_hit)
                        )
                        counts[k] = counts[k] + hit
                        hits[k * block : (k + 1) * block, group * ents : (group + 1) * ents] = hit
                count = jnp.concatenate(counts, axis=0).astype(F32)
                here = pl.ds(i * table_block, table_block)
                for copy in table_copies[2 * i - 4 : 2 * i - 2] if i >= 2 else []:
                    copy.wait()
                dps = min(n_dp, 8)
                grad = None
                for first in range(0, n_dp, dps):
                    given_rows = all_rows[first : first + dps].reshape(dps * 2 * ents, ent_proj.shape[0])
                    value = dot(hits[:, first * 2 * ents : (first + dps) * 2 * ents], given_rows)
                    grad = value if grad is None else grad + value
                table_here[i % 2] = grad
                named = jnp.sum(count, axis=1, keepdims=True)
                touched_here[i % 2] = jnp.broadcast_to(named, (table_block, LANES)).astype(LOW)
                table_copies.append(copies.local(lambda: table_here.at[i % 2], lambda: table_grad.at[here]))
                table_copies.append(copies.local(lambda: touched_here.at[i % 2], lambda: touched.at[here]))
                engine.clock += 0.7

            return step

        engine.add(
            [lambda: rows_ready, rows_z, rows_x, rows_core] + [table_part(i) for i in range(rows_dev // table_block)]
        )
        hidden_part(word_rows, 0, 1)
        word_copy = copies.send(lambda: grad_hidden.at[theirs[0]], lambda: given.at[word_part], place.other_y)
        word_ready = engine.transfer("y", word_half * width * 2)
        engine.work(1.5)

        bias_rows = bias_held.shape[0]
        bias_held[...] = jnp.zeros_like(bias_held)
        bias_held[0:6, columns] = bias_heads[0:6]
        bias_held[6:bias_rows] = bias_middle[0 : bias_rows - 6]
        live = {}
        bias_bytes = bias_rows * width * 2

        def bias_send(key, index, device):
            bias_from[2 * index] = bias_held[...].astype(LOW)
            live[key] = copies.send(lambda: bias_from.at[2 * index], lambda: bias_from.at[2 * index + 1], device)
            return engine.transfer(key, bias_bytes)

        def bias_take(key, index):
            live[key].wait_recv()
            bias_held[...] = bias_from[2 * index].astype(F32) + bias_from[2 * index + 1].astype(F32)

        def bias_core():
            return bias_send("core", 0, place.other_core)

        def bias_y():
            bias_take("core", 0)
            return bias_send("y", 1, place.other_y)

        def bias_x():
            bias_take("y", 1)
            return bias_send("x", 2, place.other_x)

        def bias_z():
            bias_take("x", 2)
            bias_from[6] = bias_held[...].astype(LOW)
            live["z"] = [
                copies.send(lambda: bias_from.at[6], lambda k=k: bias_from.at[7 + k], device)
                for k, device in enumerate(place.ahead)
            ]
            return engine.transfer("z", bias_bytes)

        def bias_end():
            value = bias_from[6].astype(F32)
            for k, copy in enumerate(live["z"]):
                copy.wait_recv()
                value = value + bias_from[7 + k].astype(F32)
            bias_out[...] = value

        engine.add([bias_core, bias_y, bias_x, bias_z, bias_end])
        quarter = word_half // 2

        def words_sum():
            word_copy.wait_recv()
            sum_hidden(0, word_half, y * word_half)
            engine.clock += 0.5
            live_words["send"] = copies.send(
                lambda: total.at[span((1 - core) * quarter, quarter, LANES)], lambda: word_grad.at[core], place.other_core
            )
            live_words["own"] = copies.local(
                lambda: total.at[span(core * quarter, quarter, LANES)], lambda: word_grad.at[core]
            )
            return engine.transfer("core", quarter * width * 4)

        def words_end():
            live_words["send"].wait_recv()
            live_words["own"].wait()

        engine.add([lambda: word_ready, words_sum, words_end])

        def ent_products():
            ent_copy.wait_recv()
            sum_hidden(word_half, ent_half, all_words + y * ent_half)
            proj_rows, pos_rows = rows.shape[1] // n_dp, all_words // n_dp
            proj_pad = padded(proj_rows)
            position = ent_pos[pl.ds(core, 1), :]
            picks = []
            for j in range(all_words // LANES):
                number = lax.broadcasted_iota(jnp.int32, (LANES, ents), 0) + j * LANES
                picks.append(jnp.where(number == position, 1.0, 0.0))
            pick = jnp.concatenate(picks, axis=0)
            here = lax.broadcasted_iota(jnp.int32, (all_words, ents), 1) // ent_half == y
            pick = jnp.where(here, pick, 0.0).astype(LOW)
            grad_ent = total[word_half:]
            grad_ent_low = grad_ent.astype(LOW)
            rest = (grad_ent - grad_ent_low.astype(F32)).astype(LOW)
            pos_grad = dot(pick, jnp.concatenate([grad_ent_low, grad_ent_low], axis=0)) + dot(
                pick, jnp.concatenate([rest, rest], axis=0)
            )
            proj_grad = dot_columns(rows[span(y * ent_half, ent_half, 64)], grad_ent_low)
            ent_grads[:, :, pl.ds(0, proj_rows)] = proj_grad.astype(LOW).reshape(nz, 2, proj_rows, width)
            ent_grads[:, :, pl.ds(proj_pad, pos_rows)] = pos_grad.astype(LOW).reshape(nz, 2, pos_rows, width)
            engine.clock += 1.0

        ent_job = jobs["ent"][0]
        engine.add([lambda: ent_ready, ent_products] + ent_job.steps)
        engine.drain()
        for copy in table_copies[-4:]:
            copy.wait()
        copies.finish()

    table_block = 256 if n_dp * 2 * ents <= 2048 else 32
    pl.run_scoped(
        backward_phase,
        pltpu.VMEM((tokens, half), LOW),
        pltpu.VMEM((tokens, half), LOW),
        pltpu.VMEM((tokens, half), LOW),
        pltpu.VMEM((tokens, half), LOW),
        pltpu.VMEM((HEADS // 2, tokens, tokens), LOW),
        pltpu.VMEM((4, width, half), LOW),
        pltpu.VMEM((width, half), LOW),
        pltpu.VMEM((width, half), LOW),
        pltpu.VMEM((half, tokens), LOW),
        pltpu.VMEM((tokens, half), LOW),
        pltpu.VMEM((tokens, half), LOW),
        pltpu.VMEM((tokens, half), LOW),
        pltpu.VMEM((tokens, half), LOW),
        pltpu.VMEM((width, tokens), LOW),
        pltpu.VMEM((tokens, width), LOW),
        pltpu.VMEM((table_block, n_dp * 2 * ents), LOW),
        pltpu.VMEM((half // LANES, nz, 2, 6 * row_pad, LANES), LOW),
        pltpu.VMEM((nz, 2, ent_sum.shape[0], width), LOW),
        pltpu.VMEM((2, table_block, ent_proj.shape[0]), F32),
        pltpu.VMEM((2, table_block, LANES), LOW),
    )
    last_copies = [
        copies.local(lambda: ffn_sum, lambda: ffn_reduced),
        copies.local(lambda: attn_sum, lambda: attn_reduced),
        copies.local(lambda: ent_sum, lambda: ent_reduced),
    ]
    for copy in out_copies:
        copy.wait_recv()
    for copy in last_copies:
        copy.wait()
    copies.finish()


def layer(
    nz, rows_dev, words, projected, words_turned, segments, pos_table, query_bias, key_bias, value_bias, out_weight, out_bias, gains, shifts, up_weight, up_bias, down_weight, down_bias, word_cots, ent_cots,
    query_weight, key_weight, value_weight, rows, ent_pos, ent_proj, ids,
):
    n_dp = 2 * nz
    all_words, width = words.shape
    half = width // 2
    ents, edim = rows.shape
    tokens = all_words + ents
    part, ff = tokens // 2, up_weight.shape[1]
    ffn_blocks = ffn_plan(n_dp, width, ff)
    ffn_rows, attn_rows = ffn_blocks[-1][0] + ffn_blocks[-1][1], 6 * padded(width // n_dp)
    ent_pad = padded(edim // n_dp) + padded(all_words // n_dp)
    bias_rows = 12 + ff // width
    plan = [("ffn", 0, base, size, order, width) for base, size, order in ffn_blocks]
    plan += [("attn", pair, 0, attn_rows, "xz", LANES) for pair in range(half // LANES)]
    plan.append(("ent", 0, 0, ent_pad, "xzy", width))
    scratch = [
        pltpu.VMEM((part, half), LOW),
        pltpu.VMEM((tokens, half), LOW),
        pltpu.VMEM((part, width), F32),
        pltpu.VMEM((part, width), LOW),
        pltpu.VMEM((ffn_rows, width), LOW),
        pltpu.VMEM((half // LANES, 2, attn_rows, LANES), LOW),
        pltpu.VMEM((ent_pad, width), LOW),
        pltpu.VMEM((bias_rows, width), F32),
        pltpu.VMEM((6 + nz, bias_rows, width), LOW),
        pltpu.VMEM((n_dp, 2, ents, edim), LOW),
        pltpu.VMEM((8, half), F32),
        pltpu.VMEM((16, width), F32),
        pltpu.VMEM((nz, 2, ffn_rows, width), LOW),
        pltpu.VMEM((part, half), LOW),
        pltpu.VMEM((2, ents, edim), LOW),
        pltpu.VMEM((tokens, half), LOW),
        pltpu.VMEM((ents // 2, width), F32),
    ]
    remote = 8 + 6 + 1 + 3 + nz + 1 + nz + nz + 2 + 4
    for name, _, base, size, order, columns in plan:
        job = Job(None, None, base, size, order, columns)
        scratch += job.scratch(nz)
        remote += job.remote_count(nz)
    scratch += copy_semaphores(remote, 60 + 2 * (rows_dev // 32))
    return call(
        functools.partial(layer_kernel, nz, plan),
        [
            ((2, all_words // 4, width), LOW),
            ((2, ents // 4, width), LOW),
            ((2, all_words // 4, width), F32),
            ((ffn_rows, width), LOW),
            ((half // LANES, 2, attn_rows, LANES), LOW),
            ((ent_pad, width), LOW),
            ((bias_rows, width), F32),
            ((rows_dev, edim), F32),
            ((rows_dev, LANES), LOW),
            ((width, tokens), LOW),
            ((tokens, half), LOW),
            ((tokens, half), LOW),
            ((tokens, half), LOW),
            ((tokens, half), LOW),
            ((HEADS // 2, tokens, tokens), LOW),
        ],
        [ANY, ANY, ANY, IN_VMEM, ANY] + [IN_VMEM] * 3 + [ANY] + [IN_VMEM] * 3 + [ANY, IN_VMEM, ANY, IN_VMEM] + [ANY] * 2 + [ANY] * 3 + [IN_VMEM] * 4,
        [ANY] * 6 + [IN_VMEM] + [ANY] * 8,
        scratch,
        "layer",
        2,
    )(words, projected, words_turned, segments, pos_table, query_bias, key_bias, value_bias, out_weight, out_bias, gains, shifts, up_weight, up_bias, down_weight, down_bias, word_cots, ent_cots,
      query_weight, key_weight, value_weight, rows, ent_pos, ent_proj, ids)[:9]


def last_kernel(
    n_dp, table_grad, touched, first, second, ffn_in, attn_in, ent_in, bias, words_in, ents_in, words_grad_in,
    table_out, update, new_second, proj_out, pos_out, query_out, key_out, value_out, out_out, up_out, down_out,
    query_bias, gain_grad, shift_grad, key_bias, value_bias, out_bias, down_bias, up_bias, word_out, ent_out, word_grad,
    ffn, attn, ent, words, ents, words_grad, proj_grad, pos_grad, query_grad, key_grad, value_grad, out_grad, up_grad, down_grad, sems,
):
    into = [(ffn_in, ffn), (attn_in, attn), (ent_in, ent), (words_in, words), (ents_in, ents), (words_grad_in, words_grad)]
    arrive = [pltpu.make_async_copy(src, dst, sems.at[i]) for i, (src, dst) in enumerate(into)]
    onward = [(down_grad, down_out), (up_grad, up_out), (out_grad, out_out), (proj_grad, proj_out), (pos_grad, pos_out)]
    onward += [(key_grad, key_out), (value_grad, value_out), (query_grad, query_out)]
    onward += [(words, word_out), (ents, ent_out), (words_grad, word_grad)]
    leave = [pltpu.make_async_copy(src, dst, sems.at[len(into) + i]) for i, (src, dst) in enumerate(onward)]

    @pl.when(pl.program_id(0) == 0)
    def _():
        for copy in arrive:
            copy.start()

    step = pl.program_id(0)
    grad = table_grad[...]
    hit = touched[:, 0:1].astype(F32) > 0.0
    mean_new = beta_one * first[...] + (1.0 - beta_one) * grad
    square_new = beta_two * second[...] + (1.0 - beta_two) * grad * grad
    direction = (
        mean_new
        / (1.0 - beta_one**adam_step)
        / (jnp.sqrt(square_new / (1.0 - beta_two**adam_step)) + adam_eps)
    )
    table_out[...] = grad
    update[...] = jnp.where(hit, direction, 0.0)
    new_second[...] = jnp.where(hit, square_new, second[...])
    width = ffn.shape[1]
    part, down_rows = out_grad.shape[0], down_grad.shape[0]
    pad = padded(part)
    proj_pad = padded(proj_grad.shape[0])
    parts = up_grad.shape[1] // width
    pairs = attn.shape[0]
    half = pairs * LANES

    @pl.when(step == 0)
    def _():
        arrive[0].wait()
        down_grad[...] = ffn[:down_rows].astype(F32)
        leave[0].start()
        for copy in arrive[3:]:
            copy.wait()
        for copy in leave[8:]:
            copy.start()

    @pl.when(step == 1)
    def _():
        for j in range(parts):
            base = down_rows + j * pad
            up_grad[:, j * width : (j + 1) * width] = ffn[base : base + part].astype(F32)
        leave[1].start()
        arrive[1].wait()
        arrive[2].wait()

    @pl.when(step == 2)
    def _():
        base = down_rows + parts * pad
        out_grad[...] = ffn[base : base + part].astype(F32)
        proj_grad[...] = ent[: proj_grad.shape[0]].astype(F32)
        pos_grad[...] = ent[proj_pad : proj_pad + pos_grad.shape[0]].astype(F32)
        for side in range(2):
            for pair in range(pairs):
                columns = slice(side * half + pair * LANES, side * half + (pair + 1) * LANES)
                key_grad[:, columns] = attn[pair, side, 4 * pad : 4 * pad + part].astype(F32)
                value_grad[:, columns] = attn[pair, side, 5 * pad : 5 * pad + part].astype(F32)
        for copy in leave[2:7]:
            copy.start()

    @pl.when(step == 2)
    def _():
        for side in range(2):
            for pair in range(pairs):
                columns = slice(side * half + pair * LANES, side * half + (pair + 1) * LANES)
                for i in range(4):
                    query_grad[i, :, columns] = attn[pair, side, i * pad : i * pad + part].astype(F32)
        leave[7].start()

    @pl.when(step == 3)
    def _():
        dp = lax.axis_index("dp")

        def own_columns(value, size, start):
            lane = lax.broadcasted_iota(jnp.int32, (value.shape[1], size), 0)
            want = lax.broadcasted_iota(jnp.int32, (value.shape[1], size), 1) + start
            pick = jnp.where(lane == want, 1.0, 0.0)
            return jnp.dot(value, pick, precision=lax.Precision.HIGHEST, preferred_element_type=F32)

        own = own_columns(bias[...], part, dp * part)
        query_bias[...] = own[0:4]
        gain_grad[...] = own[7:9]
        shift_grad[...] = own[9:11]
        for vector, i in ((key_bias, 4), (value_bias, 5), (out_bias, 6), (down_bias, 11 + parts)):
            vector[...] = own[i : i + 1].reshape(part)
        up = jnp.concatenate([bias[11 + j : 12 + j] for j in range(parts)], axis=1)
        size = up_bias.shape[0]
        if size % LANES == 0:
            per = width // size
            row = bias[pl.ds(11 + dp // per, 1), :]
            chosen = row[:, :size]
            for i in range(1, per):
                chosen = jnp.where(dp % per == i, row[:, i * size : (i + 1) * size], chosen)
            up_bias[...] = chosen.reshape(size)
        else:
            up_bias[...] = own_columns(up, size, dp * size).reshape(size)

    @pl.when(step == pl.num_programs(0) - 1)
    def _():
        for copy in leave:
            copy.wait()


def last(n_dp, ff, all_words, table_grad, touched, first, second, ffn, attn, ent, bias, words_low, ents_low, words_grad):
    width = ffn.shape[1]
    rows, edim = first.shape
    part = width // n_dp
    block = 512
    blocked = lambda columns: pl.BlockSpec((block, columns), lambda i: (i, 0))
    whole = lambda shape: pl.BlockSpec(shape, lambda i: (0,) * len(shape))
    shapes = [
        (edim // n_dp, width),
        (all_words // n_dp, width),
        (4, part, width),
        (part, width),
        (part, width),
        (part, width),
        (part, ff),
        (ff // n_dp, width),
        (4, part),
        (2, part),
        (2, part),
        (part,),
        (part,),
        (part,),
        (part,),
        (ff // n_dp,),
    ]
    through = [words_low, ents_low, words_grad]
    return pl.pallas_call(
        functools.partial(last_kernel, n_dp),
        grid=(rows // block,),
        out_shape=[jax.ShapeDtypeStruct((rows, edim), F32)] * 3
        + [jax.ShapeDtypeStruct(shape, F32) for shape in shapes]
        + [jax.ShapeDtypeStruct(array.shape, array.dtype) for array in through],
        in_specs=[blocked(edim), blocked(LANES), blocked(edim), blocked(edim)]
        + [ANY] * 3
        + [whole(bias.shape)]
        + [ANY] * 3,
        out_specs=[blocked(edim)] * 3 + [ANY] * 8 + [whole(shape) for shape in shapes[8:]] + [ANY] * 3,
        scratch_shapes=[pltpu.VMEM(array.shape, array.dtype) for array in [ffn, attn, ent] + through]
        + [pltpu.VMEM(shape, F32) for shape in shapes[:8]]
        + [pltpu.SemaphoreType.DMA((17,))],
        compiler_params=pltpu.CompilerParams(vmem_limit_bytes=VMEM_BYTES),
        name="last",
    )(table_grad, touched, first, second, ffn, attn, ent, bias, words_low, ents_low, words_grad)


def on_device(
    word_states,
    segments,
    entity_ids,
    entity_pos,
    ent_table,
    first_moment,
    second_moment,
    ent_proj,
    pos_table,
    query_weight,
    query_bias,
    key_weight,
    key_bias,
    value_weight,
    value_bias,
    out_weight,
    out_bias,
    norm_gain,
    norm_shift,
    up_weight,
    up_bias,
    down_weight,
    down_bias,
    word_cot,
    ent_cot,
):
    n_dp = lax.axis_size("dp")
    nz = n_dp // 2
    width, ff = up_weight.shape
    all_words = segments.shape[1]
    words, word_cots, ent_cots, all_ids, rows, projected, words_turned = fetch(
        nz, word_states, word_cot, ent_cot, entity_ids, query_bias, key_bias, value_bias, ent_table, query_weight, key_weight, value_weight
    )
    ents = entity_ids.shape[1]
    word_out, ent_out, word_grad, ffn_sum, attn_sum, ent_sum, bias_sum, table_grad, touched = layer(
        nz, ent_table.shape[0], words, projected, words_turned, segments, pos_table, query_bias, key_bias, value_bias, out_weight, out_bias, norm_gain, norm_shift, up_weight, up_bias, down_weight, down_bias,
        word_cots, ent_cots, query_weight, key_weight, value_weight,
        rows, entity_pos, ent_proj, all_ids.reshape(-1, ents),
    )
    (table_grad, table_update, new_second, proj_grad, pos_grad, query_grad, key_grad, value_grad, out_grad, up_grad, down_grad,
     query_bias_grad, gain_grad, shift_grad, key_bias_grad, value_bias_grad, out_bias_grad, down_bias_grad, up_bias_grad,
     word_out, ent_out, word_grad,
    ) = last(
        n_dp, ff, all_words, table_grad, touched, first_moment, second_moment, ffn_sum, attn_sum, ent_sum, bias_sum, word_out, ent_out, word_grad
    )
    return (
        word_out,
        ent_out,
        word_grad,
        proj_grad,
        pos_grad,
        query_grad,
        query_bias_grad,
        key_grad,
        key_bias_grad,
        value_grad,
        value_bias_grad,
        out_grad,
        out_bias_grad,
        gain_grad,
        shift_grad,
        up_grad,
        up_bias_grad,
        down_grad,
        down_bias_grad,
        table_grad,
        table_update,
        new_second,
    )


def solution(mesh):
    return jax.shard_map(
        on_device,
        mesh=mesh,
        in_specs=(
            P("dp", "seq", None),
            P("dp", None),
            P("dp", None),
            P("dp", None),
            P(("dp", "seq"), None),
            P(("dp", "seq"), None),
            P(("dp", "seq"), None),
            P(),
            P(),
            P(),
            P(),
            P(),
            P(),
            P(),
            P(),
            P(),
            P(),
            P(),
            P(),
            P(),
            P(),
            P(),
            P(),
            P("dp", "seq", None),
            P("dp", "seq", None),
        ),
        out_specs=(
            P("dp", "seq", None),
            P("dp", "seq", None),
            P("dp", "seq", None),
            P("dp", None),
            P("dp", None),
            P(None, "dp", None),
            P(None, "dp"),
            P("dp", None),
            P("dp"),
            P("dp", None),
            P("dp"),
            P("dp", None),
            P("dp"),
            P(None, "dp"),
            P(None, "dp"),
            P("dp", None),
            P("dp"),
            P("dp", None),
            P("dp"),
            P(("dp", "seq"), None),
            P(("dp", "seq"), None),
            P(("dp", "seq"), None),
        ),
        check_vma=False,
    )
```

```python
import functools
import math

import jax
import jax.numpy as jnp
from jax import lax
from jax.experimental import pallas as pl
from jax.experimental.pallas import tpu as pltpu
from jax.sharding import PartitionSpec as P

HEADS = 12
HEAD = 64
LANES = 128
MESH = pl.DeviceIdType.MESH
LOW = jnp.bfloat16
F32 = jnp.float32
VMEM_BYTES = 125 * 512 * 1024

norm_eps = 1e-05
beta_one = 0.9
beta_two = 0.98
adam_eps = 1e-06
adam_step = 10.0
masked_score = -1e30


def dot(left, right):
    return jnp.dot(left, right, preferred_element_type=F32)


def dot_rows(left, right):
    return lax.dot_general(left, right, (((1,), (1,)), ((), ())), preferred_element_type=F32)


def dot_columns(left, right):
    return lax.dot_general(left, right, (((0,), (0,)), ((), ())), preferred_element_type=F32)


def span(start, size, unit):
    if isinstance(start, int):
        return pl.ds(start, size)
    return pl.ds(pl.multiple_of(start, unit), size)


def padded(rows):
    return -(-rows // 16) * 16


def loop(count, body, carry=0, unroll=1):
    def steps(i, carried):
        for k in range(unroll):
            carried = body(i * unroll + k, carried)
        return carried

    return lax.fori_loop(0, count // unroll, steps, carry)


class Place:
    def __init__(self, nz):
        self.dp, self.seq = lax.axis_index("dp"), lax.axis_index("seq")
        self.z, self.x = self.dp // 2, self.dp % 2
        self.y, self.core = self.seq // 2, self.seq % 2
        self.nz = nz
        self.other_core = (self.dp, self.y * 2 + 1 - self.core)
        self.other_y = (self.dp, (1 - self.y) * 2 + self.core)
        self.diagonal = (self.dp, (1 - self.y) * 2 + 1 - self.core)
        self.other_x = (self.z * 2 + 1 - self.x, self.seq)
        self.ahead = [(((self.z + k) % nz) * 2 + self.x, self.seq) for k in range(1, nz)]

    def z_ahead(self, k):
        return (self.z + k) % self.nz


def announce(partners):
    barrier = pltpu.get_barrier_semaphore()
    for partner in partners:
        pl.semaphore_signal(barrier, inc=1, device_id=partner, device_id_type=MESH)


def meet(partners):
    pl.semaphore_wait(pltpu.get_barrier_semaphore(), len(partners))


class Remote:
    def __init__(self, copies, number, src, dst, device):
        self.copies, self.number, self.src, self.dst, self.device = copies, number, src, dst, device
        self.open = True

    def make(self, landing=False):
        return pltpu.make_async_remote_copy(
            src_ref=self.dst() if landing else self.src(),
            dst_ref=self.dst(),
            send_sem=self.copies.send_sem.at[self.number],
            recv_sem=self.copies.recv_sem.at[self.number],
            device_id=self.device,
            device_id_type=MESH,
        )

    def wait_recv(self):
        self.make(landing=True).wait_recv()

    def wait_send(self):
        if self.open:
            self.make().wait_send()
        self.open = False


class Local:
    def __init__(self, copies, number, src, dst):
        self.copies, self.number, self.src, self.dst = copies, number, src, dst

    def make(self):
        return pltpu.make_async_copy(self.src(), self.dst(), self.copies.local_sem.at[self.number])

    def wait(self):
        self.make().wait()


class Copies:
    def __init__(self, send_sem, recv_sem, local_sem):
        self.send_sem, self.recv_sem, self.local_sem = send_sem, recv_sem, local_sem
        self.local_count = 0
        self.sent = []

    def send(self, src, dst, device):
        copy = Remote(self, len(self.sent), src, dst, device)
        copy.make().start()
        self.sent.append(copy)
        return copy

    def local(self, src, dst):
        copy = Local(self, self.local_count, src, dst)
        self.local_count += 1
        copy.make().start()
        return copy

    def finish(self):
        for copy in self.sent:
            copy.wait_send()


def copy_semaphores(remote, local):
    return [
        pltpu.SemaphoreType.DMA((remote,)),
        pltpu.SemaphoreType.DMA((remote,)),
        pltpu.SemaphoreType.DMA((local,)),
    ]


ANY = pl.BlockSpec(memory_space=pl.ANY)
IN_VMEM = pl.BlockSpec(memory_space=pltpu.VMEM)


def call(kernel, outs, in_specs, out_specs, scratch, name, collective_id=None):
    params = {"vmem_limit_bytes": VMEM_BYTES}
    if collective_id is not None:
        params.update(collective_id=collective_id, has_side_effects=True)
    return pl.pallas_call(
        kernel,
        out_shape=[jax.ShapeDtypeStruct(shape, dtype) for shape, dtype in outs],
        in_specs=in_specs,
        out_specs=out_specs,
        scratch_shapes=scratch,
        compiler_params=pltpu.CompilerParams(**params),
        name=name,
    )


def lane_mask(rows, head):
    lane = lax.broadcasted_iota(jnp.int32, (rows, LANES), 1)
    return (lane >= head * HEAD) & (lane < (head + 1) * HEAD)


def row_of(vector):
    return vector[...].astype(F32).reshape(1, vector.shape[0])


def own_half(vector, y):
    row = row_of(vector)
    half = row.shape[1] // 2
    return jnp.where(y == 0, row[:, :half], row[:, half:])


def as_column(row):
    parts = [
        jnp.transpose(jnp.broadcast_to(row[:, i : i + LANES], (LANES, LANES)))
        for i in range(0, row.shape[1], LANES)
    ]
    return jnp.concatenate(parts, axis=0) if len(parts) > 1 else parts[0]


def fetch_kernel(
    nz, words, word_cot, ent_cot, ids, query_bias, key_bias, value_bias, table, query_weight, key_weight, value_weight,
    all_words, word_cots, ent_cots, all_ids, rows_out, projected, words_turned, *scratch,
):
    (table_full, table_low, picked, answers, held, from_core, from_x, from_z, from_y, ids_here, query_here, key_here, value_here) = scratch[:13]
    copies = Copies(*scratch[13:])
    place = Place(nz)
    z, x, y, core = place.z, place.x, place.y, place.core
    n_dp = 2 * nz
    word_here, ent_here = words.shape[1], ent_cot.shape[1]
    ents = ids.shape[1]
    dp_others = [((place.dp + k) % n_dp, place.seq) for k in range(1, n_dp)]
    partners = [place.other_core, place.other_y, place.diagonal] + dp_others
    announce(partners)
    half = key_here.shape[1]
    columns = span(y * half, half, LANES)
    whole_table = copies.local(lambda: table, lambda: table_full)
    weight_copies = [
        copies.local(lambda: query_weight.at[pl.ds(0, 2), :, columns], lambda: query_here),
        copies.local(lambda: key_weight.at[:, columns], lambda: key_here),
        copies.local(lambda: value_weight.at[:, columns], lambda: value_here),
    ]
    ids_here[place.dp] = ids[...]
    meet(partners)
    id_copies = [copies.send(lambda: ids, lambda: ids_here.at[place.dp], device) for device in dp_others]
    quarter = span(place.seq * word_here, word_here, 128)
    word_copies = [
        copies.send(lambda: words.at[1 - core], lambda: all_words.at[quarter], place.diagonal),
        copies.send(lambda: words.at[core], lambda: all_words.at[quarter], place.other_y),
        copies.send(lambda: words.at[1 - core], lambda: all_words.at[quarter], place.other_core),
        copies.send(lambda: word_cot.at[1 - core], lambda: word_cots.at[span(core * word_here, word_here, 128)], place.other_core),
        copies.send(lambda: ent_cot.at[1 - core], lambda: ent_cots.at[span(core * ent_here, ent_here, 32)], place.other_core),
    ]
    all_words[quarter] = words[core]
    word_cots[span(core * word_here, word_here, 128)] = word_cot[core]
    ent_cots[span(core * ent_here, ent_here, 32)] = ent_cot[core]
    whole_table.wait()
    rows_dev = table.shape[0]

    def narrow(i, _):
        where = span(i * 128, 128, 128)
        table_low[where] = table_full[where].astype(LOW)
        return 0

    loop(rows_dev // 128, narrow)
    for copy in id_copies:
        copy.wait_recv()
    all_ids[...] = ids_here[...]
    base = (place.dp * 4 + place.seq) * rows_dev
    tiles = rows_dev // LANES

    def look_up(zz):
        for g in range(4):
            asked = ids_here[zz * 2 + g // 2, pl.ds(g % 2, 1), :] - base
            column = jnp.transpose(jnp.broadcast_to(asked, (ents, ents)))
            lane = lax.broadcasted_iota(jnp.int32, (ents, LANES), 1)
            low_hit = jnp.where((column & (LANES - 1)) == lane, 1.0, 0.0).astype(LOW)
            high = jnp.clip(column >> 7, -1, tiles).astype(F32).astype(LOW)
            for j in range(tiles):
                hit = jnp.where(high == jnp.asarray(j, LOW), low_hit, jnp.zeros_like(low_hit))
                picked[pl.ds(g * ents, ents), pl.ds(j * LANES, LANES)] = hit
        answer = dot(picked[...], table_low[...]).astype(LOW)
        answers[zz] = answer.reshape(2, 2, ents, answer.shape[-1])

    order = [place.z_ahead(k + 1) for k in range(nz)]
    core_copies, x_copies, z_copies = [], [], []

    def core_send(zz):
        return copies.send(lambda: answers.at[zz, :, 1 - core], lambda: from_core.at[zz], place.other_core)

    def after_core(k):
        zz = order[k]
        core_copies[k].wait_recv()
        held[zz] = answers[zz, :, core] + from_core[zz]
        x_copies.append(copies.send(lambda: held.at[zz, 1 - x], lambda: from_x.at[zz], place.other_x))

    def after_x(k):
        zz = order[k]
        x_copies[k].wait_recv()
        held[zz, x] = held[zz, x] + from_x[zz]
        if k < nz - 1:
            z_copies.append(copies.send(lambda: held.at[zz, x], lambda: from_z.at[k], place.ahead[k]))

    query_b = query_bias[:, columns].astype(F32)

    def project(i):
        weight = (query_here.at[0], query_here.at[1], key_here, value_here)[i]
        bias = query_b[i : i + 1] if i < 2 else own_half((key_bias, value_bias)[i - 2], y)
        projected[i] = (dot(all_words[...], weight[...]) + bias).astype(LOW)

    def turn_words(part):
        for i in range(part, words.shape[2] // LANES, 2):
            here = slice(i * LANES, (i + 1) * LANES)
            words_turned[here, :] = jnp.transpose(all_words[:, here].astype(F32)).astype(LOW)

    for k in range(nz + 2):
        if k == nz:
            for copy in word_copies[:3]:
                copy.wait_recv()
            for copy in weight_copies:
                copy.wait()
            project(0)
            project(1)
        if k == nz + 1:
            project(2)
        if k < nz:
            look_up(order[k])
            core_copies.append(core_send(order[k]))
        if 0 <= k - 1 < nz:
            after_core(k - 1)
        if 0 <= k - 2:
            after_x(k - 2)
    project(3)
    total = held[z, x]
    for k in range(nz - 1):
        z_copies[k].wait_recv()
        total = total + from_z[k]
    from_y[0] = total
    y_copy = copies.send(lambda: from_y.at[0], lambda: from_y.at[1], place.other_y)
    turn_words(0)
    turn_words(1)
    y_copy.wait_recv()
    rows_out[...] = from_y[0] + from_y[1]
    for copy in word_copies[3:]:
        copy.wait_recv()
    copies.finish()


def fetch(nz, words, word_cot, ent_cot, ids, query_bias, key_bias, value_bias, table, query_weight, key_weight, value_weight):
    _, word_here, width = words.shape
    ent_here, ents, (rows_dev, edim) = ent_cot.shape[1], ids.shape[1], table.shape
    n_dp = 2 * nz
    return call(
        functools.partial(fetch_kernel, nz),
        [
            ((4 * word_here, width), LOW),
            ((2 * word_here, width), LOW),
            ((2 * ent_here, width), LOW),
            ((n_dp, 2, ents), jnp.int32),
            ((ents, edim), LOW),
            ((4, 4 * word_here, width // 2), LOW),
            ((width, 4 * word_here), LOW),
        ],
        [IN_VMEM] * 7 + [ANY] * 4,
        [IN_VMEM] * 7,
        [
            pltpu.VMEM((rows_dev, edim), F32),
            pltpu.VMEM((rows_dev, edim), LOW),
            pltpu.VMEM((4 * ents, rows_dev), LOW),
            pltpu.VMEM((nz, 2, 2, ents, edim), LOW),
            pltpu.VMEM((nz, 2, ents, edim), LOW),
            pltpu.VMEM((nz, 2, ents, edim), LOW),
            pltpu.VMEM((nz, ents, edim), LOW),
            pltpu.VMEM((nz - 1, ents, edim), LOW),
            pltpu.VMEM((2, ents, edim), LOW),
            pltpu.VMEM((n_dp, 2, ents), jnp.int32),
            pltpu.VMEM((2, width, width // 2), LOW),
            pltpu.VMEM((width, width // 2), LOW),
            pltpu.VMEM((width, width // 2), LOW),
        ]
        + copy_semaphores(n_dp + 4 + 3 * nz + 2, 4),
        "fetch",
        1,
    )(words, word_cot, ent_cot, ids, query_bias, key_bias, value_bias, table, query_weight, key_weight, value_weight)


class Engine:
    RATES = {"core": 300e3, "x": 52e3, "y": 52e3, "z": 13e3}
    LATENCY = 2.0

    def __init__(self):
        self.clock, self.free, self.streams = 0.0, {}, []

    def transfer(self, link, size):
        start = max(self.clock, self.free.get(link, 0.0))
        self.free[link] = start + size / self.RATES[link]
        return self.free[link] + self.LATENCY

    def add(self, steps):
        self.streams.append([self.clock, list(steps)])
        self.poll()

    def run(self, stream):
        self.clock = max(self.clock, stream[0])
        ready = stream[1].pop(0)()
        stream[0] = self.clock if ready is None else ready

    def next(self):
        live = [stream for stream in self.streams if stream[1]]
        return min(live, key=lambda stream: stream[0]) if live else None

    def poll(self):
        while (stream := self.next()) is not None and stream[0] <= self.clock:
            self.run(stream)

    def work(self, time):
        self.clock += time
        self.poll()

    def drain(self):
        while (stream := self.next()) is not None:
            self.run(stream)


def blocks_of(rows):
    for size in (96, 64, 48, 32):
        if rows % size == 0:
            return size
    return 16


def add_blocks(engine, target, parts, leading, rows, columns):
    size = blocks_of(rows)
    count = rows // size

    def block(i, _):
        lead, row = i // count, (i % count) * size
        where = span(row, size, 16)
        if len(parts) == 2:
            value = parts[0](lead, where) + parts[1](lead, where)
        else:
            value = parts[0](lead, where).astype(F32)
            for part in parts[1:]:
                value = value + part(lead, where).astype(F32)
            value = value.astype(LOW)
        target(lead, where, value)
        return 0

    loop(leading * count, block)
    engine.clock += 0.3 + leading * rows * columns / 1e6


class Job:
    def __init__(self, grads, reduced, base, size, order, columns):
        self.grads, self.reduced, self.base, self.size, self.order, self.columns = grads, reduced, base, size, order, columns
        self.half = size // 2
        self.part = size // 4 if order == "yxz" else size // 2

    def scratch(self, nz):
        shapes = [(nz, 2, self.half, self.columns)]
        if self.order == "yxz":
            shapes.append((nz, 2, self.part, self.columns))
        elif self.order == "xzy":
            shapes.append((2, self.part, self.columns))
        shapes += [(nz, self.part, self.columns), (nz - 1, self.part, self.columns)]
        return [pltpu.VMEM(shape, LOW) for shape in shapes]

    def remote_count(self, nz):
        return 1 + (1 if self.order != "xz" else 0) + 1 + (nz - 1) + 1 + 1

    def prepare(self, engine, place, copies, scratch):
        nz, z, x, y, core = place.nz, place.z, place.x, place.y, place.core
        base, half, part, order, columns = self.base, self.half, self.part, self.order, self.columns
        held = self.grads.at[:, :, span(base + core * half, half, 16)]
        from_core = scratch[0]
        from_y = scratch[1] if order != "xz" else None
        from_x, from_z = scratch[-2:]
        live = {}
        row_bytes = 2 * columns
        theirs = span(base + (1 - core) * half, half, 16)
        mine = span(base + core * half, half, 16)
        own_rows = span(y * part, part, 16) if order == "yxz" else pl.ds(0, part)
        final_rows = span(base + core * half + (y * part if order == "yxz" else 0), part, 16)

        def start():
            live["core"] = copies.send(lambda: self.grads.at[:, :, theirs], lambda: from_core, place.other_core)
            return engine.transfer("core", 2 * nz * half * row_bytes)

        def send_x():
            live["x"] = copies.send(lambda: held.at[:, 1 - x, own_rows], lambda: from_x, place.other_x)
            return engine.transfer("x", nz * part * row_bytes)

        def after_core():
            live["core"].wait_recv()

            def put(i, where, value):
                held[i // 2, i % 2, where] = value

            add_blocks(
                engine,
                put,
                [lambda i, where: held[i // 2, i % 2, where], lambda i, where: from_core[i // 2, i % 2, where]],
                2 * nz,
                half,
                columns,
            )
            if order == "yxz":
                live["y"] = copies.send(
                    lambda: held.at[:, :, span((1 - y) * part, part, 16)], lambda: from_y, place.other_y
                )
                return engine.transfer("y", 2 * nz * part * row_bytes)
            return send_x()

        def shifted(where):
            return span(y * part + where.start, where.size, 16) if order == "yxz" else where

        def after_y():
            live["y"].wait_recv()

            def put(i, where, value):
                held[i // 2, i % 2, shifted(where)] = value

            add_blocks(
                engine,
                put,
                [lambda i, where: held[i // 2, i % 2, shifted(where)], lambda i, where: from_y[i // 2, i % 2, where]],
                2 * nz,
                part,
                columns,
            )
            return send_x()

        def send_z(k):
            return copies.send(
                lambda: held.at[place.z_ahead(k + 1), x, own_rows], lambda: from_z.at[k], place.ahead[k]
            )

        def after_x():
            live["x"].wait_recv()

            def put(i, where, value):
                held[i, x, shifted(where)] = value

            add_blocks(
                engine,
                put,
                [lambda i, where: held[i, x, shifted(where)], lambda i, where: from_x[i, where]],
                nz,
                part,
                columns,
            )
            live["z"] = [send_z(k) for k in range(nz - 1)]
            return engine.transfer("z", part * row_bytes)

        def after_z():
            for copy in live["z"]:
                copy.wait_recv()

            def put(i, where, value):
                if order == "yxz":
                    self.reduced[span(base + core * half + y * part + where.start, where.size, 16)] = value
                elif order == "xz":
                    self.reduced[y, span(base + core * half + where.start, where.size, 16)] = value
                else:
                    from_y[0, where] = value

            def parts(k):
                return lambda i, where: from_z[k, where]

            add_blocks(
                engine,
                put,
                [lambda i, where: held[z, x, shifted(where)]] + [parts(k) for k in range(nz - 1)],
                1,
                part,
                columns,
            )
            if order == "xzy":
                live["y2"] = copies.send(lambda: from_y.at[0], lambda: from_y.at[1], place.other_y)
            else:
                view = lambda: self.reduced.at[final_rows] if order == "yxz" else self.reduced.at[y, final_rows]
                live["y2"] = copies.send(view, view, place.other_y)
            return engine.transfer("y", part * row_bytes)

        def after_gather():
            live["y2"].wait_recv()
            if order == "xzy":

                def put(i, where, value):
                    self.reduced[span(base + core * half + where.start, where.size, 16)] = value

                add_blocks(
                    engine, put, [lambda i, where: from_y[0, where], lambda i, where: from_y[1, where]], 1, part, columns
                )
            view = lambda: self.reduced.at[:, mine] if order == "xz" else self.reduced.at[mine]
            live["core2"] = copies.send(view, view, place.other_core)
            return engine.transfer("core", 2 * half * row_bytes)

        def end():
            live["core2"].wait_recv()

        middle_steps = [after_core, after_y, after_x] if order == "yxz" else [after_core, after_x]
        self.steps = [start] + middle_steps + [after_z, after_gather, end]


def lane_mean(value):
    return jnp.mean(value, axis=-1, keepdims=True)


def column_sum(value):
    return jnp.sum(value, axis=0, keepdims=True)


ROW_BLOCK = 32


def ffn_plan(n_dp, width, ff):
    down_rows, row_pad = ff // n_dp, padded(width // n_dp)
    size = 128 if down_rows % 128 == 0 else 32
    order = "yxz" if size % 64 == 0 else "xzy"
    plan = [(base, size, order) for base in range(0, down_rows, size)]
    base = down_rows
    for pair in range(ff // width // 2):
        order = "yxz" if row_pad % 32 == 0 else "xzy"
        plan.append((base, 2 * row_pad, order))
        base += 2 * row_pad
    plan.append((base, row_pad, "xzy"))
    return plan


def layer_kernel(
    nz, plan, words, projected, words_turned, segments, pos_table, query_bias, key_bias, value_bias, out_weight, out_bias, gains, shifts, up_weight, up_bias, down_weight, down_bias, word_cots, ent_cots,
    query_weight, key_weight, value_weight, rows, ent_pos, ent_proj, ids,
    word_out, ent_out, word_grad, ffn_reduced, attn_reduced, ent_reduced, bias_out, table_grad, touched,
    hidden_turned_in, query_words_in, query_ents_in, keys_in, values_in, probs_in, *scratch,
):
    (from_y_mixed, grad_mixed, grad_one, given, ffn_sum, attn_sum, ent_sum, bias_held, bias_from, all_rows, bias_heads, bias_middle,
     ffn_grads, grad_mixed_here, row_parts, mixed, ent_keep) = scratch[:17]
    copies = Copies(*scratch[-3:])
    engine = Engine()
    place = Place(nz)
    z, x, y, core = place.z, place.x, place.y, place.core
    n_dp = 2 * nz
    tokens, half = mixed.shape
    width = 2 * half
    ents = rows.shape[0]
    all_words = tokens - ents
    word_half, ent_half = all_words // 2, ents // 2
    part_tokens = tokens // 2
    ff = up_weight.shape[1]
    parts = ff // width
    row_part, row_pad, down_rows = width // n_dp, padded(width // n_dp), ff // n_dp
    partners = [place.other_core, place.other_y, place.other_x] + place.ahead
    announce(partners)

    jobs = {"ffn": [], "attn": [], "ent": []}

    def make_jobs(names, sources):
        at = 17
        for name, number, base, size, order, columns in plan:
            grads, reduced = sources.get(name, (None, None))
            if name == "attn" and grads is not None:
                grads, reduced = grads.at[number], reduced.at[number]
            job = Job(grads, reduced, base, size, order, columns)
            used = len(job.scratch(nz))
            if name in names:
                job.prepare(engine, place, copies, scratch[at : at + used])
                jobs[name].append(job)
            at += used

    make_jobs(["ffn"], {"ffn": (ffn_grads, ffn_sum)})

    def token_rows(side):
        return span(side * word_half, word_half, LANES), span(all_words + side * ent_half, ent_half, 64)

    mine, theirs = token_rows(y), token_rows(1 - y)
    own_columns, other_columns = span(y * half, half, LANES), span((1 - y) * half, half, LANES)
    word_part, ent_part = pl.ds(0, word_half), pl.ds(word_half, ent_half)
    mixed_copies = []
    scale = 1.0 / math.sqrt(HEAD)
    tiles = tokens // LANES

    def attend_phase(
        hidden_turned, query_words, query_ents, keys, values, probs, query_here, key_here, value_here, pos_here, values_turned, mask,
    ):
        weight_copies = [
            copies.local(lambda: pos_table, lambda: pos_here),
            copies.local(lambda: query_weight.at[pl.ds(2, 2), :, own_columns], lambda: query_here),
            copies.local(lambda: key_weight.at[:, own_columns], lambda: key_here),
            copies.local(lambda: value_weight.at[:, own_columns], lambda: value_here),
        ]
        word_rows = pl.ds(0, all_words)
        targets = [query_words, query_ents, keys, values]
        for i, target in enumerate(targets):
            weight_copies.append(
                copies.local(lambda i=i: projected.at[i], lambda target=target: target.at[word_rows])
            )
        weight_copies.append(copies.local(lambda: words_turned, lambda: hidden_turned.at[:, word_rows]))
        position = as_column(ent_pos[pl.ds(core, 1), :])
        picks = []
        for j in range(all_words // LANES):
            number = lax.broadcasted_iota(jnp.int32, (ents, LANES), 1) + j * LANES
            picks.append(jnp.where(position == number, 1.0, 0.0))
        pick = jnp.concatenate(picks, axis=1)
        word_seg = segments[pl.ds(core, 1), :].astype(F32)
        ent_seg = jnp.sum(pick * word_seg, axis=1, keepdims=True)
        weight_copies[0].wait()
        ent_hidden = dot(rows[...], ent_proj[...]) + dot(pick.astype(LOW), pos_here[...])
        ent_keep[...] = jnp.where(y == 0, ent_hidden[:ent_half], ent_hidden[ent_half:])
        ent_row = jnp.transpose(jnp.broadcast_to(ent_seg, (ents, LANES)))[:1]
        seg_row = jnp.concatenate([word_seg, ent_row], axis=1)
        seg_column = jnp.concatenate([as_column(word_seg), jnp.broadcast_to(ent_seg, (ents, LANES))], axis=0)
        for j in range(tiles):
            here = slice(j * LANES, (j + 1) * LANES)
            mask[:, here] = jnp.where(seg_column == seg_row[:, here], 0.0, masked_score)
        query_b = query_bias[:, own_columns].astype(F32)
        for copy in weight_copies[1:]:
            copy.wait()
        ent_low = ent_hidden.astype(LOW)
        query_words[all_words:] = (dot(ent_low, query_here[0]) + query_b[2:3]).astype(LOW)
        query_ents[all_words:] = (dot(ent_low, query_here[1]) + query_b[3:4]).astype(LOW)
        keys[all_words:] = (dot(ent_low, key_here[...]) + own_half(key_bias, y)).astype(LOW)
        values[all_words:] = (dot(ent_low, value_here[...]) + own_half(value_bias, y)).astype(LOW)
        hidden_turned[:, all_words:] = jnp.transpose(ent_hidden).astype(LOW)
        values_turned[...] = jnp.transpose(values[...].astype(F32)).astype(LOW)
        spills = [
            copies.local(lambda: query_words, lambda: query_words_in),
            copies.local(lambda: query_ents, lambda: query_ents_in),
            copies.local(lambda: keys, lambda: keys_in),
            copies.local(lambda: values, lambda: values_in),
        ]
        for pair in range(half // LANES):
            lanes = slice(pair * LANES, (pair + 1) * LANES)
            key, turned = keys[:, lanes], values_turned[lanes, :]
            row = lax.broadcasted_iota(jnp.int32, (LANES, tokens), 0)
            own_key, own_turned = [], []
            for head in range(2):
                own_key.append(jnp.where(lane_mask(tokens, head), key, jnp.zeros_like(key)))
                own_rows = (row >= head * HEAD) & (row < (head + 1) * HEAD)
                own_turned.append(jnp.where(own_rows, turned, jnp.zeros_like(turned)))
            for i in range(tiles):
                here = slice(i * LANES, (i + 1) * LANES)
                query_w, query_e = query_words[here, lanes], query_ents[here, lanes]
                part_sum = None
                for head in range(2):
                    raw = jnp.concatenate(
                        [dot_rows(own_key[head][:all_words], query_w), dot_rows(own_key[head][all_words:], query_e)], axis=0
                    )
                    score = raw * scale + mask[:, here]
                    weight = jnp.exp(score - jnp.max(score, axis=0, keepdims=True))
                    prob = (weight * (1.0 / jnp.sum(weight, axis=0, keepdims=True))).astype(LOW)
                    probs[pair * 2 + head, :, here] = prob
                    part = dot(own_turned[head], prob)
                    part_sum = part if part_sum is None else part_sum + part
                mixed[here, lanes] = jnp.transpose(part_sum).astype(LOW)
            heads = pl.ds(pair * 2, 2)
            if pair == 0:
                meet(partners)
            mixed_copies.extend([
                copies.send(
                    lambda lanes=lanes: mixed.at[theirs[0], lanes], lambda lanes=lanes: from_y_mixed.at[word_part, lanes], place.other_y
                ),
                copies.send(
                    lambda lanes=lanes: mixed.at[theirs[1], lanes], lambda lanes=lanes: from_y_mixed.at[ent_part, lanes], place.other_y
                ),
            ])
            spills.append(copies.local(lambda heads=heads: probs.at[heads], lambda heads=heads: probs_in.at[heads]))
        spills.append(copies.local(lambda: hidden_turned, lambda: hidden_turned_in))
        for copy in spills:
            copy.wait()

    pl.run_scoped(
        attend_phase,
        pltpu.VMEM((width, tokens), LOW),
        pltpu.VMEM((tokens, half), LOW),
        pltpu.VMEM((tokens, half), LOW),
        pltpu.VMEM((tokens, half), LOW),
        pltpu.VMEM((tokens, half), LOW),
        pltpu.VMEM((HEADS // 2, tokens, tokens), LOW),
        pltpu.VMEM((2, width, half), LOW),
        pltpu.VMEM((width, half), LOW),
        pltpu.VMEM((width, half), LOW),
        pltpu.VMEM((all_words, width), LOW),
        pltpu.VMEM((half, tokens), LOW),
        pltpu.VMEM((tokens, tokens), F32),
    )
    out_copies, mixed_back = [], []

    def forward_phase(
        out_here, up_here, down_here, word_here, mixed_full, work, normed_low, normal_one, inverse_one,
        act, slope, output, grad_two, grad_two_low, grad_one_low, normed_turned,
    ):
        cot, grad_up_low = output, slope
        weight_copies = [
            copies.local(lambda: out_weight, lambda: out_here),
            copies.local(lambda: words.at[mine[0]], lambda: word_here),
            copies.local(lambda: up_weight, lambda: up_here),
            copies.local(lambda: down_weight, lambda: down_here),
            copies.local(lambda: word_cots, lambda: cot.at[word_part]),
            copies.local(lambda: ent_cots, lambda: cot.at[ent_part]),
        ]
        gain, shift = gains[...].astype(F32), shifts[...].astype(F32)
        out_b, down_b, up_b = row_of(out_bias), row_of(down_bias), row_of(up_bias)
        mixed_full[word_part, own_columns] = mixed[mine[0]]
        mixed_full[ent_part, own_columns] = mixed[mine[1]]
        for copy in weight_copies[:2]:
            copy.wait()
        work[...] = dot(mixed_full[:, own_columns], out_here[own_columns, :])
        for copy in mixed_copies:
            copy.wait_recv()
        mixed_full[:, other_columns] = from_y_mixed[...]
        work[...] += dot(from_y_mixed[...], out_here[other_columns, :])

        def norm_one(residual):
            def step(i, _):
                rows = span(residual[1] + i * ROW_BLOCK, ROW_BLOCK, ROW_BLOCK)
                value = residual[0][span(i * ROW_BLOCK, ROW_BLOCK, ROW_BLOCK)].astype(F32) + (work[rows] + out_b)
                center = value - lane_mean(value)
                inverse = lax.rsqrt(lane_mean(center * center) + norm_eps)
                normal = center * inverse
                result = normal * gain[0:1] + shift[0:1]
                normal_one[rows] = normal
                inverse_one[rows] = jnp.broadcast_to(inverse, (ROW_BLOCK, LANES))
                normed_low[rows] = result.astype(LOW)
                return 0

            return step

        loop(word_half // ROW_BLOCK, norm_one((word_here, 0)), 0, 2)
        loop(ent_half // ROW_BLOCK, norm_one((ent_keep, word_half)), 0, 2)
        weight_copies[2].wait()
        for j in range(parts):
            columns = slice(j * width, (j + 1) * width)
            work[...] = dot(normed_low[...], up_here[:, columns]) + up_b[:, columns]

            def gelu(i, _):
                rows = span(i * ROW_BLOCK, ROW_BLOCK, ROW_BLOCK)
                value = work[rows]
                below = 0.5 * (1.0 + lax.erf(value * (1.0 / math.sqrt(2.0))))
                density = jnp.exp(-0.5 * value * value) * (1.0 / math.sqrt(2.0 * math.pi))
                act[rows, columns] = (value * below).astype(LOW)
                slope[rows, columns] = (below + value * density).astype(LOW)
                return 0

            loop(part_tokens // ROW_BLOCK, gelu)
        normed_turned[...] = jnp.transpose(normed_low[...].astype(F32)).astype(LOW)
        for copy in weight_copies[3:]:
            copy.wait()
        work[...] = dot(act[...], down_here[...])

        def norm_two(i, sums):
            rows = span(i * ROW_BLOCK, ROW_BLOCK, ROW_BLOCK)
            value = (normal_one[rows] * gain[0:1] + shift[0:1]) + (work[rows] + down_b)
            center = value - lane_mean(value)
            inverse = lax.rsqrt(lane_mean(center * center) + norm_eps)
            normal = center * inverse
            cotangent = cot[rows].astype(F32)
            output[rows] = (normal * gain[1:2] + shift[1:2]).astype(LOW)
            scaled = cotangent * gain[1:2]
            result = inverse * (scaled - lane_mean(scaled) - normal * lane_mean(scaled * normal))
            grad_two[rows] = result
            grad_two_low[rows] = result.astype(LOW)
            return (
                sums[0] + column_sum(cotangent * normal),
                sums[1] + column_sum(cotangent),
                sums[2] + column_sum(result),
            )

        nothing = jnp.zeros((1, width), F32)
        gain_two, shift_two, down_sum = loop(part_tokens // ROW_BLOCK, norm_two, (nothing, nothing, nothing), 2)
        quarter, ent_quarter = word_half // 2, ent_half // 2
        out_copies.extend([
            copies.send(
                lambda: output.at[span((1 - core) * quarter, quarter, LANES)], lambda: word_out.at[core], place.other_core
            ),
            copies.send(
                lambda: output.at[span(word_half + (1 - core) * ent_quarter, ent_quarter, 32)],
                lambda: ent_out.at[core],
                place.other_core,
            ),
        ])
        out_local = [
            copies.local(lambda: output.at[span(core * quarter, quarter, LANES)], lambda: word_out.at[core]),
            copies.local(
                lambda: output.at[span(word_half + core * ent_quarter, ent_quarter, 32)], lambda: ent_out.at[core]
            ),
        ]
        engine.clock = 0.0
        engine.free = {}
        def put(base, value):
            ffn_grads[:, :, pl.ds(base, row_part)] = value.astype(LOW).reshape(nz, 2, row_part, width)

        def down_products():
            per = width // down_rows
            for j in range(parts):
                value = dot_columns(act[:, j * width : (j + 1) * width], grad_two_low[...])
                value = value.astype(LOW).reshape(per, down_rows, width)
                for d in range(per):
                    slab = j * per + d
                    ffn_grads[slab // 2, slab % 2, pl.ds(0, down_rows)] = value[d]

        up_sums = []

        def grad_up(j):
            columns = slice(j * width, (j + 1) * width)
            work[...] = dot_rows(grad_two_low[...], down_here[columns, :])

            def grad_gelu(i, total_row):
                rows = span(i * ROW_BLOCK, ROW_BLOCK, ROW_BLOCK)
                value = work[rows] * slope[rows, columns].astype(F32)
                grad_up_low[rows, columns] = value.astype(LOW)
                return total_row + column_sum(value)

            up_sums.append(loop(part_tokens // ROW_BLOCK, grad_gelu, nothing, 2))
            engine.work(1.6)

        def up_product(j):
            columns = slice(j * width, (j + 1) * width)
            put(down_rows + j * row_pad, dot(normed_turned[...], grad_up_low[:, columns]))
            engine.work(0.9)

        downs = [job for job in jobs["ffn"] if job.base < down_rows]
        ups = [job for job in jobs["ffn"] if down_rows <= job.base][:-1]
        down_products()
        engine.clock += 3.0
        for job in downs:
            engine.add(job.steps)
        for j in range(parts):
            grad_up(j)
        work[...] = dot_rows(grad_up_low[...], up_here[...])
        engine.work(2.0)

        def back_one(i, sums):
            rows = span(i * ROW_BLOCK, ROW_BLOCK, ROW_BLOCK)
            upper = grad_two[rows] + work[rows]
            normal = normal_one[rows]
            inverse = inverse_one[rows, 0:1]
            scaled = upper * gain[0:1]
            result = inverse * (scaled - lane_mean(scaled) - normal * lane_mean(scaled * normal))
            grad_one[rows] = result
            grad_one_low[rows] = result.astype(LOW)
            return (
                sums[0] + column_sum(upper * normal),
                sums[1] + column_sum(upper),
                sums[2] + column_sum(result),
            )

        gain_one, shift_one, out_sum = loop(part_tokens // ROW_BLOCK, back_one, (nothing, nothing, nothing), 2)
        engine.work(1.0)
        grad_mixed_here[...] = dot_rows(grad_one_low[...], out_here[other_columns, :]).astype(LOW)
        mixed_back.extend([
            copies.send(lambda: grad_mixed_here.at[word_part], lambda: grad_mixed.at[mine[0]], place.other_y),
            copies.send(lambda: grad_mixed_here.at[ent_part], lambda: grad_mixed.at[mine[1]], place.other_y),
        ])
        engine.transfer("y", part_tokens * half * 2)
        own = dot_rows(grad_one_low[...], out_here[own_columns, :]).astype(LOW)
        grad_mixed[mine[0]] = own[:word_half]
        grad_mixed[mine[1]] = own[word_half:]
        engine.work(1.0)
        for j in range(parts):
            up_product(j)
            if j % 2 == 1:
                engine.add(ups[j // 2].steps)
        put(down_rows + parts * row_pad, dot_columns(mixed_full[...], grad_one_low[...]))
        engine.work(0.8)
        engine.add(jobs["ffn"][-1].steps)
        bias_rows = [out_sum, gain_one, gain_two, shift_one, shift_two] + up_sums + [down_sum]
        for i, row in enumerate(bias_rows):
            bias_middle[i : i + 1] = row
        for copy in out_copies:
            copy.wait_send()
        for copy in out_local:
            copy.wait()

    tall = lambda columns, dtype: pltpu.VMEM((part_tokens, columns), dtype)
    pl.run_scoped(
        forward_phase,
        pltpu.VMEM((width, width), LOW),
        pltpu.VMEM((width, ff), LOW),
        pltpu.VMEM((ff, width), LOW),
        pltpu.VMEM((word_half, width), LOW),
        tall(width, LOW),
        tall(width, F32),
        tall(width, LOW),
        tall(width, F32),
        tall(LANES, F32),
        tall(ff, LOW),
        tall(ff, LOW),
        tall(width, LOW),
        tall(width, F32),
        tall(width, LOW),
        tall(width, LOW),
        pltpu.VMEM((width, part_tokens), LOW),
    )
    live_words = {}

    def backward_phase(
        query_words, query_ents, keys, values, probs, query_here, key_here, value_here, keys_turned,
        grad_query_words, grad_query_ents, grad_keys, grad_values, hidden_turned, grad_hidden, hits, attn_grads, ent_grads, table_here, touched_here,
    ):
        total = grad_one
        make_jobs(["attn", "ent"], {"attn": (attn_grads, attn_sum), "ent": (ent_grads, ent_sum)})
        columns = span(y * half, half, LANES)
        copies_in = [
            copies.local(lambda: values_in, lambda: values),
            copies.local(lambda: keys_in, lambda: keys),
            copies.local(lambda: query_words_in, lambda: query_words),
            copies.local(lambda: query_ents_in, lambda: query_ents),
        ]
        prob_copies = []
        for head in range(probs.shape[0]):
            prob_copies.append(
                copies.local(lambda head=head: probs_in.at[head], lambda head=head: probs.at[head])
            )
        hidden_copy = copies.local(lambda: hidden_turned_in, lambda: hidden_turned)
        weight_copies = [
            copies.local(lambda: query_weight.at[:, :, columns], lambda: query_here),
            copies.local(lambda: key_weight.at[:, columns], lambda: key_here),
            copies.local(lambda: value_weight.at[:, columns], lambda: value_here),
        ]
        for copy in copies_in:
            copy.wait()
        for i in range(half // LANES):
            lanes = slice(i * LANES, (i + 1) * LANES)
            keys_turned[lanes, :] = jnp.transpose(keys[:, lanes].astype(F32)).astype(LOW)
        for copy in mixed_back:
            copy.wait_recv()
        engine.work(2.0)
        def pair_products(pair):
            lanes = slice(pair * LANES, (pair + 1) * LANES)
            word_turned, ent_turned = hidden_turned[:, :all_words], hidden_turned[:, all_words:]
            products = [
                dot(word_turned, grad_query_words[:all_words, lanes]),
                dot(word_turned, grad_query_ents[:all_words, lanes]),
                dot(ent_turned, grad_query_words[all_words:, lanes]),
                dot(ent_turned, grad_query_ents[all_words:, lanes]),
                dot(hidden_turned[...], grad_keys[:, lanes]),
                dot(hidden_turned[...], grad_values[:, lanes]),
            ]
            for i, value in enumerate(products):
                attn_grads[pair, :, :, pl.ds(i * row_pad, row_part)] = value.astype(LOW).reshape(nz, 2, row_part, LANES)
            engine.work(1.5)
            for job in jobs["attn"][pair:] if pair + 1 == half // LANES else jobs["attn"][pair : pair + 1]:
                engine.add(job.steps)

        for pair in range(half // LANES):
            lanes = slice(pair * LANES, (pair + 1) * LANES)
            grad_query_w = jnp.zeros((LANES, tokens), F32)
            grad_query_e = jnp.zeros((LANES, tokens), F32)
            grad_key_w = jnp.zeros((all_words, LANES), F32)
            grad_key_e = jnp.zeros((ents, LANES), F32)
            grad_value = jnp.zeros((tokens, LANES), F32)
            for head in range(2):
                own = lane_mask(tokens, head)
                value = values[:, lanes]
                own_value = jnp.where(own, value, jnp.zeros_like(value))
                prob_copies[pair * 2 + head].wait()

                given_heads = grad_mixed[:, lanes]
                grad_scores = probs.at[pair * 2 + head]
                grad_value += dot(grad_scores[...], jnp.where(own, given_heads, jnp.zeros_like(given_heads)))
                for i in range(tiles):
                    where = slice(i * LANES, (i + 1) * LANES)
                    grad_prob = dot_rows(own_value, grad_mixed[where, lanes])
                    prob = grad_scores[:, where].astype(F32)
                    both = prob * grad_prob
                    grad_scores[:, where] = (both - prob * jnp.sum(both, axis=0, keepdims=True)).astype(LOW)
                engine.work(1.7)
                query_w, query_e = query_words[:, lanes], query_ents[:, lanes]
                grad_key_w += dot(grad_scores[:all_words], jnp.where(own, query_w, jnp.zeros_like(query_w)))
                grad_key_e += dot(grad_scores[all_words:], jnp.where(own, query_e, jnp.zeros_like(query_e)))
                row = lax.broadcasted_iota(jnp.int32, (LANES, tokens), 0)
                own_rows = (row >= head * HEAD) & (row < (head + 1) * HEAD)
                turned = keys_turned[lanes, :]
                turned = jnp.where(own_rows, turned, jnp.zeros_like(turned))
                grad_query_w += dot(turned[:, :all_words], grad_scores[:all_words])
                grad_query_e += dot(turned[:, all_words:], grad_scores[all_words:])
                engine.work(1.7)
            grad_query_w = jnp.transpose(grad_query_w) * scale
            grad_query_e = jnp.transpose(grad_query_e) * scale
            grad_key_w, grad_key_e = grad_key_w * scale, grad_key_e * scale
            sums = [
                column_sum(grad_query_w[:all_words]),
                column_sum(grad_query_e[:all_words]),
                column_sum(grad_query_w[all_words:]),
                column_sum(grad_query_e[all_words:]),
                column_sum(grad_key_w) + column_sum(grad_key_e),
                column_sum(grad_value),
            ]
            for i, sum_row in enumerate(sums):
                bias_heads[i : i + 1, lanes] = sum_row
            grad_query_words[:, lanes] = grad_query_w.astype(LOW)
            grad_query_ents[:, lanes] = grad_query_e.astype(LOW)
            grad_keys[:all_words, lanes] = grad_key_w.astype(LOW)
            grad_keys[all_words:, lanes] = grad_key_e.astype(LOW)
            grad_values[:, lanes] = grad_value.astype(LOW)
            engine.work(0.5)
            if pair == 0:
                hidden_copy.wait()
            if pair + 1 < half // LANES:
                pair_products(pair)

        for copy in weight_copies:
            copy.wait()
        ent_rows, word_rows = slice(all_words, tokens), slice(0, all_words)

        def hidden_part(here, first, second):
            grad_hidden[here] = (
                dot_rows(grad_keys[here], key_here[...])
                + dot_rows(grad_values[here], value_here[...])
                + dot_rows(grad_query_words[here], query_here[first])
                + dot_rows(grad_query_ents[here], query_here[second])
            ).astype(LOW)

        hidden_part(ent_rows, 2, 3)
        own_ents = lax.broadcasted_iota(jnp.int32, (ents, width), 0) // ent_half == y
        twice = jnp.concatenate([grad_one[word_half:], grad_one[word_half:]], axis=0)
        ent_sum_part = grad_hidden[ent_rows].astype(F32) + jnp.where(own_ents, twice, 0.0)
        row_parts[0] = dot_rows(ent_sum_part.astype(LOW), ent_proj[...]).astype(LOW)
        rows_copy = copies.send(lambda: row_parts.at[0], lambda: row_parts.at[1], place.other_y)
        row_bytes = ents * ent_proj.shape[0] * 2
        rows_ready = engine.transfer("y", row_bytes)
        engine.work(0.7)
        pair_products(half // LANES - 1)
        ent_copy = copies.send(lambda: grad_hidden.at[theirs[1]], lambda: given.at[ent_part], place.other_y)
        ent_ready = engine.transfer("y", ent_half * width * 2)

        live_rows = {}

        def sum_hidden(start, count, own_start):
            def block(i, _):
                where = span(start + i * 32, 32, 32)
                own = span(own_start + i * 32, 32, 32)
                total[where] = grad_one[where] + (grad_hidden[own].astype(F32) + given[where].astype(F32))
                return 0

            loop(count // 32, block)

        def rows_z():
            rows_copy.wait_recv()
            all_rows[place.dp, core] = row_parts[0] + row_parts[1]
            view = lambda: all_rows.at[place.dp, core]
            live_rows["z"] = [copies.send(view, view, device) for device in place.ahead]
            return engine.transfer("z", row_bytes)

        def rows_x():
            for copy in live_rows["z"]:
                copy.wait_recv()
            live_rows["x"] = []
            for k in range(nz):
                view = lambda k=k: all_rows.at[place.z_ahead(k) * 2 + x, core]
                live_rows["x"].append(copies.send(view, view, place.other_x))
            return engine.transfer("x", nz * row_bytes)

        def rows_core():
            for copy in live_rows["x"]:
                copy.wait_recv()
            view = lambda: all_rows.at[:, core]
            live_rows["core"] = copies.send(view, view, place.other_core)
            return engine.transfer("core", n_dp * row_bytes)

        rows_dev = table_grad.shape[0]
        table_copies = []
        base_row = (place.dp * 4 + place.seq) * rows_dev

        def table_part(i):
            def step():
                if i == 0:
                    live_rows["core"].wait_recv()
                groups = ids.shape[0]
                block = min(table_block, LANES)
                counts = [jnp.zeros((block, ents), LOW) for _ in range(table_block // block)]
                for group in range(groups):
                    asked = ids[group : group + 1, :] - base_row
                    high = jnp.clip(asked >> 7, -1, rows_dev // LANES).astype(F32)
                    high = jnp.broadcast_to(high, (block, ents)).astype(LOW)
                    first_row = i * table_block
                    number = lax.broadcasted_iota(jnp.int32, (block, ents), 0) + first_row % LANES
                    low_hit = jnp.where((asked & (LANES - 1)) == number, 1.0, 0.0).astype(LOW)
                    for k in range(len(counts)):
                        hit = jnp.where(
                            high == jnp.asarray(first_row // LANES + k, LOW), low_hit, jnp.zeros_like(low_hit)
                        )
                        counts[k] = counts[k] + hit
                        hits[k * block : (k + 1) * block, group * ents : (group + 1) * ents] = hit
                count = jnp.concatenate(counts, axis=0).astype(F32)
                here = pl.ds(i * table_block, table_block)
                for copy in table_copies[2 * i - 4 : 2 * i - 2] if i >= 2 else []:
                    copy.wait()
                dps = min(n_dp, 8)
                grad = None
                for first in range(0, n_dp, dps):
                    given_rows = all_rows[first : first + dps].reshape(dps * 2 * ents, ent_proj.shape[0])
                    value = dot(hits[:, first * 2 * ents : (first + dps) * 2 * ents], given_rows)
                    grad = value if grad is None else grad + value
                table_here[i % 2] = grad
                named = jnp.sum(count, axis=1, keepdims=True)
                touched_here[i % 2] = jnp.broadcast_to(named, (table_block, LANES)).astype(LOW)
                table_copies.append(copies.local(lambda: table_here.at[i % 2], lambda: table_grad.at[here]))
                table_copies.append(copies.local(lambda: touched_here.at[i % 2], lambda: touched.at[here]))
                engine.clock += 0.7

            return step

        engine.add(
            [lambda: rows_ready, rows_z, rows_x, rows_core] + [table_part(i) for i in range(rows_dev // table_block)]
        )
        hidden_part(word_rows, 0, 1)
        word_copy = copies.send(lambda: grad_hidden.at[theirs[0]], lambda: given.at[word_part], place.other_y)
        word_ready = engine.transfer("y", word_half * width * 2)
        engine.work(1.5)

        bias_rows = bias_held.shape[0]
        bias_held[...] = jnp.zeros_like(bias_held)
        bias_held[0:6, columns] = bias_heads[0:6]
        bias_held[6:bias_rows] = bias_middle[0 : bias_rows - 6]
        live = {}
        bias_bytes = bias_rows * width * 2

        def bias_send(key, index, device):
            bias_from[2 * index] = bias_held[...].astype(LOW)
            live[key] = copies.send(lambda: bias_from.at[2 * index], lambda: bias_from.at[2 * index + 1], device)
            return engine.transfer(key, bias_bytes)

        def bias_take(key, index):
            live[key].wait_recv()
            bias_held[...] = bias_from[2 * index].astype(F32) + bias_from[2 * index + 1].astype(F32)

        def bias_core():
            return bias_send("core", 0, place.other_core)

        def bias_y():
            bias_take("core", 0)
            return bias_send("y", 1, place.other_y)

        def bias_x():
            bias_take("y", 1)
            return bias_send("x", 2, place.other_x)

        def bias_z():
            bias_take("x", 2)
            bias_from[6] = bias_held[...].astype(LOW)
            live["z"] = [
                copies.send(lambda: bias_from.at[6], lambda k=k: bias_from.at[7 + k], device)
                for k, device in enumerate(place.ahead)
            ]
            return engine.transfer("z", bias_bytes)

        def bias_end():
            value = bias_from[6].astype(F32)
            for k, copy in enumerate(live["z"]):
                copy.wait_recv()
                value = value + bias_from[7 + k].astype(F32)
            bias_out[...] = value

        engine.add([bias_core, bias_y, bias_x, bias_z, bias_end])
        quarter = word_half // 2

        def words_sum():
            word_copy.wait_recv()
            sum_hidden(0, word_half, y * word_half)
            engine.clock += 0.5
            live_words["send"] = copies.send(
                lambda: total.at[span((1 - core) * quarter, quarter, LANES)], lambda: word_grad.at[core], place.other_core
            )
            live_words["own"] = copies.local(
                lambda: total.at[span(core * quarter, quarter, LANES)], lambda: word_grad.at[core]
            )
            return engine.transfer("core", quarter * width * 4)

        def words_end():
            live_words["send"].wait_recv()
            live_words["own"].wait()

        engine.add([lambda: word_ready, words_sum, words_end])

        def ent_products():
            ent_copy.wait_recv()
            sum_hidden(word_half, ent_half, all_words + y * ent_half)
            proj_rows, pos_rows = rows.shape[1] // n_dp, all_words // n_dp
            proj_pad = padded(proj_rows)
            position = ent_pos[pl.ds(core, 1), :]
            picks = []
            for j in range(all_words // LANES):
                number = lax.broadcasted_iota(jnp.int32, (LANES, ents), 0) + j * LANES
                picks.append(jnp.where(number == position, 1.0, 0.0))
            pick = jnp.concatenate(picks, axis=0)
            here = lax.broadcasted_iota(jnp.int32, (all_words, ents), 1) // ent_half == y
            pick = jnp.where(here, pick, 0.0).astype(LOW)
            grad_ent = total[word_half:]
            grad_ent_low = grad_ent.astype(LOW)
            rest = (grad_ent - grad_ent_low.astype(F32)).astype(LOW)
            pos_grad = dot(pick, jnp.concatenate([grad_ent_low, grad_ent_low], axis=0)) + dot(
                pick, jnp.concatenate([rest, rest], axis=0)
            )
            proj_grad = dot_columns(rows[span(y * ent_half, ent_half, 64)], grad_ent_low)
            ent_grads[:, :, pl.ds(0, proj_rows)] = proj_grad.astype(LOW).reshape(nz, 2, proj_rows, width)
            ent_grads[:, :, pl.ds(proj_pad, pos_rows)] = pos_grad.astype(LOW).reshape(nz, 2, pos_rows, width)
            engine.clock += 1.0

        ent_job = jobs["ent"][0]
        engine.add([lambda: ent_ready, ent_products] + ent_job.steps)
        engine.drain()
        for copy in table_copies[-4:]:
            copy.wait()
        copies.finish()

    table_block = 256 if n_dp * 2 * ents <= 2048 else 32
    pl.run_scoped(
        backward_phase,
        pltpu.VMEM((tokens, half), LOW),
        pltpu.VMEM((tokens, half), LOW),
        pltpu.VMEM((tokens, half), LOW),
        pltpu.VMEM((tokens, half), LOW),
        pltpu.VMEM((HEADS // 2, tokens, tokens), LOW),
        pltpu.VMEM((4, width, half), LOW),
        pltpu.VMEM((width, half), LOW),
        pltpu.VMEM((width, half), LOW),
        pltpu.VMEM((half, tokens), LOW),
        pltpu.VMEM((tokens, half), LOW),
        pltpu.VMEM((tokens, half), LOW),
        pltpu.VMEM((tokens, half), LOW),
        pltpu.VMEM((tokens, half), LOW),
        pltpu.VMEM((width, tokens), LOW),
        pltpu.VMEM((tokens, width), LOW),
        pltpu.VMEM((table_block, n_dp * 2 * ents), LOW),
        pltpu.VMEM((half // LANES, nz, 2, 6 * row_pad, LANES), LOW),
        pltpu.VMEM((nz, 2, ent_sum.shape[0], width), LOW),
        pltpu.VMEM((2, table_block, ent_proj.shape[0]), F32),
        pltpu.VMEM((2, table_block, LANES), LOW),
    )
    last_copies = [
        copies.local(lambda: ffn_sum, lambda: ffn_reduced),
        copies.local(lambda: attn_sum, lambda: attn_reduced),
        copies.local(lambda: ent_sum, lambda: ent_reduced),
    ]
    for copy in out_copies:
        copy.wait_recv()
    for copy in last_copies:
        copy.wait()
    copies.finish()


def layer(
    nz, rows_dev, words, projected, words_turned, segments, pos_table, query_bias, key_bias, value_bias, out_weight, out_bias, gains, shifts, up_weight, up_bias, down_weight, down_bias, word_cots, ent_cots,
    query_weight, key_weight, value_weight, rows, ent_pos, ent_proj, ids,
):
    n_dp = 2 * nz
    all_words, width = words.shape
    half = width // 2
    ents, edim = rows.shape
    tokens = all_words + ents
    part, ff = tokens // 2, up_weight.shape[1]
    ffn_blocks = ffn_plan(n_dp, width, ff)
    ffn_rows, attn_rows = ffn_blocks[-1][0] + ffn_blocks[-1][1], 6 * padded(width // n_dp)
    ent_pad = padded(edim // n_dp) + padded(all_words // n_dp)
    bias_rows = 12 + ff // width
    plan = [("ffn", 0, base, size, order, width) for base, size, order in ffn_blocks]
    last_pair = half // LANES - 1
    plan += [("attn", pair, 0, attn_rows, "xz", LANES) for pair in range(last_pair)]
    plan += [("attn", last_pair, base, attn_rows // 2, "xz", LANES) for base in (0, attn_rows // 2)]
    plan.append(("ent", 0, 0, ent_pad, "xzy", width))
    scratch = [
        pltpu.VMEM((part, half), LOW),
        pltpu.VMEM((tokens, half), LOW),
        pltpu.VMEM((part, width), F32),
        pltpu.VMEM((part, width), LOW),
        pltpu.VMEM((ffn_rows, width), LOW),
        pltpu.VMEM((half // LANES, 2, attn_rows, LANES), LOW),
        pltpu.VMEM((ent_pad, width), LOW),
        pltpu.VMEM((bias_rows, width), F32),
        pltpu.VMEM((6 + nz, bias_rows, width), LOW),
        pltpu.VMEM((n_dp, 2, ents, edim), LOW),
        pltpu.VMEM((8, half), F32),
        pltpu.VMEM((16, width), F32),
        pltpu.VMEM((nz, 2, ffn_rows, width), LOW),
        pltpu.VMEM((part, half), LOW),
        pltpu.VMEM((2, ents, edim), LOW),
        pltpu.VMEM((tokens, half), LOW),
        pltpu.VMEM((ents // 2, width), F32),
    ]
    remote = 8 + 6 + 1 + 3 + nz + 1 + nz + nz + 2 + 4
    for name, _, base, size, order, columns in plan:
        job = Job(None, None, base, size, order, columns)
        scratch += job.scratch(nz)
        remote += job.remote_count(nz)
    scratch += copy_semaphores(remote, 60 + 2 * (rows_dev // 32))
    return call(
        functools.partial(layer_kernel, nz, plan),
        [
            ((2, all_words // 4, width), LOW),
            ((2, ents // 4, width), LOW),
            ((2, all_words // 4, width), F32),
            ((ffn_rows, width), LOW),
            ((half // LANES, 2, attn_rows, LANES), LOW),
            ((ent_pad, width), LOW),
            ((bias_rows, width), F32),
            ((rows_dev, edim), F32),
            ((rows_dev, LANES), LOW),
            ((width, tokens), LOW),
            ((tokens, half), LOW),
            ((tokens, half), LOW),
            ((tokens, half), LOW),
            ((tokens, half), LOW),
            ((HEADS // 2, tokens, tokens), LOW),
        ],
        [ANY, ANY, ANY, IN_VMEM, ANY] + [IN_VMEM] * 3 + [ANY] + [IN_VMEM] * 3 + [ANY, IN_VMEM, ANY, IN_VMEM] + [ANY] * 2 + [ANY] * 3 + [IN_VMEM] * 4,
        [ANY] * 6 + [IN_VMEM] + [ANY] * 8,
        scratch,
        "layer",
        2,
    )(words, projected, words_turned, segments, pos_table, query_bias, key_bias, value_bias, out_weight, out_bias, gains, shifts, up_weight, up_bias, down_weight, down_bias, word_cots, ent_cots,
      query_weight, key_weight, value_weight, rows, ent_pos, ent_proj, ids)[:9]


def last_kernel(
    n_dp, table_grad, touched, first, second, ffn_in, attn_in, ent_in, bias, words_in, ents_in, words_grad_in,
    table_out, update, new_second, proj_out, pos_out, query_out, key_out, value_out, out_out, up_out, down_out,
    query_bias, gain_grad, shift_grad, key_bias, value_bias, out_bias, down_bias, up_bias, word_out, ent_out, word_grad,
    ffn, attn, ent, words, ents, words_grad, proj_grad, pos_grad, query_grad, key_grad, value_grad, out_grad, up_grad, down_grad, sems,
):
    into = [(ffn_in, ffn), (attn_in, attn), (ent_in, ent), (words_in, words), (ents_in, ents), (words_grad_in, words_grad)]
    arrive = [pltpu.make_async_copy(src, dst, sems.at[i]) for i, (src, dst) in enumerate(into)]
    onward = [(down_grad, down_out), (up_grad, up_out), (out_grad, out_out), (proj_grad, proj_out), (pos_grad, pos_out)]
    onward += [(key_grad, key_out), (value_grad, value_out), (query_grad, query_out)]
    onward += [(words, word_out), (ents, ent_out), (words_grad, word_grad)]
    leave = [pltpu.make_async_copy(src, dst, sems.at[len(into) + i]) for i, (src, dst) in enumerate(onward)]

    @pl.when(pl.program_id(0) == 0)
    def _():
        for copy in arrive:
            copy.start()

    step = pl.program_id(0)
    grad = table_grad[...]
    hit = touched[:, 0:1].astype(F32) > 0.0
    mean_new = beta_one * first[...] + (1.0 - beta_one) * grad
    square_new = beta_two * second[...] + (1.0 - beta_two) * grad * grad
    direction = (mean_new * (1.0 / (1.0 - beta_one**adam_step))) / (
        jnp.sqrt(square_new * (1.0 / (1.0 - beta_two**adam_step))) + adam_eps
    )
    table_out[...] = grad
    update[...] = jnp.where(hit, direction, 0.0)
    new_second[...] = jnp.where(hit, square_new, second[...])
    width = ffn.shape[1]
    part, down_rows = out_grad.shape[0], down_grad.shape[0]
    pad = padded(part)
    proj_pad = padded(proj_grad.shape[0])
    parts = up_grad.shape[1] // width
    pairs = attn.shape[0]
    half = pairs * LANES

    @pl.when(step == 0)
    def _():
        arrive[0].wait()
        down_grad[...] = ffn[:down_rows].astype(F32)
        leave[0].start()
        for copy in arrive[3:]:
            copy.wait()
        for copy in leave[8:]:
            copy.start()

    @pl.when(step == 1)
    def _():
        for j in range(parts):
            base = down_rows + j * pad
            up_grad[:, j * width : (j + 1) * width] = ffn[base : base + part].astype(F32)
        leave[1].start()
        arrive[1].wait()
        arrive[2].wait()

    @pl.when(step == 2)
    def _():
        base = down_rows + parts * pad
        out_grad[...] = ffn[base : base + part].astype(F32)
        proj_grad[...] = ent[: proj_grad.shape[0]].astype(F32)
        pos_grad[...] = ent[proj_pad : proj_pad + pos_grad.shape[0]].astype(F32)
        for side in range(2):
            for pair in range(pairs):
                columns = slice(side * half + pair * LANES, side * half + (pair + 1) * LANES)
                key_grad[:, columns] = attn[pair, side, 4 * pad : 4 * pad + part].astype(F32)
                value_grad[:, columns] = attn[pair, side, 5 * pad : 5 * pad + part].astype(F32)
        for copy in leave[2:7]:
            copy.start()

    @pl.when(step == 2)
    def _():
        for side in range(2):
            for pair in range(pairs):
                columns = slice(side * half + pair * LANES, side * half + (pair + 1) * LANES)
                for i in range(4):
                    query_grad[i, :, columns] = attn[pair, side, i * pad : i * pad + part].astype(F32)
        leave[7].start()

    @pl.when(step == 3)
    def _():
        dp = lax.axis_index("dp")

        def own_columns(value, size, start):
            lane = lax.broadcasted_iota(jnp.int32, (value.shape[1], size), 0)
            want = lax.broadcasted_iota(jnp.int32, (value.shape[1], size), 1) + start
            pick = jnp.where(lane == want, 1.0, 0.0)
            return jnp.dot(value, pick, precision=lax.Precision.HIGHEST, preferred_element_type=F32)

        own = own_columns(bias[...], part, dp * part)
        query_bias[...] = own[0:4]
        gain_grad[...] = own[7:9]
        shift_grad[...] = own[9:11]
        for vector, i in ((key_bias, 4), (value_bias, 5), (out_bias, 6), (down_bias, 11 + parts)):
            vector[...] = own[i : i + 1].reshape(part)
        up = jnp.concatenate([bias[11 + j : 12 + j] for j in range(parts)], axis=1)
        size = up_bias.shape[0]
        if size % LANES == 0:
            per = width // size
            row = bias[pl.ds(11 + dp // per, 1), :]
            chosen = row[:, :size]
            for i in range(1, per):
                chosen = jnp.where(dp % per == i, row[:, i * size : (i + 1) * size], chosen)
            up_bias[...] = chosen.reshape(size)
        else:
            up_bias[...] = own_columns(up, size, dp * size).reshape(size)

    @pl.when(step == pl.num_programs(0) - 1)
    def _():
        for copy in leave:
            copy.wait()


def last(n_dp, ff, all_words, table_grad, touched, first, second, ffn, attn, ent, bias, words_low, ents_low, words_grad):
    width = ffn.shape[1]
    rows, edim = first.shape
    part = width // n_dp
    block = 512
    blocked = lambda columns: pl.BlockSpec((block, columns), lambda i: (i, 0))
    whole = lambda shape: pl.BlockSpec(shape, lambda i: (0,) * len(shape))
    shapes = [
        (edim // n_dp, width),
        (all_words // n_dp, width),
        (4, part, width),
        (part, width),
        (part, width),
        (part, width),
        (part, ff),
        (ff // n_dp, width),
        (4, part),
        (2, part),
        (2, part),
        (part,),
        (part,),
        (part,),
        (part,),
        (ff // n_dp,),
    ]
    through = [words_low, ents_low, words_grad]
    return pl.pallas_call(
        functools.partial(last_kernel, n_dp),
        grid=(rows // block,),
        out_shape=[jax.ShapeDtypeStruct((rows, edim), F32)] * 3
        + [jax.ShapeDtypeStruct(shape, F32) for shape in shapes]
        + [jax.ShapeDtypeStruct(array.shape, array.dtype) for array in through],
        in_specs=[blocked(edim), blocked(LANES), blocked(edim), blocked(edim)]
        + [ANY] * 3
        + [whole(bias.shape)]
        + [ANY] * 3,
        out_specs=[blocked(edim)] * 3 + [ANY] * 8 + [whole(shape) for shape in shapes[8:]] + [ANY] * 3,
        scratch_shapes=[pltpu.VMEM(array.shape, array.dtype) for array in [ffn, attn, ent] + through]
        + [pltpu.VMEM(shape, F32) for shape in shapes[:8]]
        + [pltpu.SemaphoreType.DMA((17,))],
        compiler_params=pltpu.CompilerParams(vmem_limit_bytes=VMEM_BYTES),
        name="last",
    )(table_grad, touched, first, second, ffn, attn, ent, bias, words_low, ents_low, words_grad)


def on_device(
    word_states,
    segments,
    entity_ids,
    entity_pos,
    ent_table,
    first_moment,
    second_moment,
    ent_proj,
    pos_table,
    query_weight,
    query_bias,
    key_weight,
    key_bias,
    value_weight,
    value_bias,
    out_weight,
    out_bias,
    norm_gain,
    norm_shift,
    up_weight,
    up_bias,
    down_weight,
    down_bias,
    word_cot,
    ent_cot,
):
    n_dp = lax.axis_size("dp")
    nz = n_dp // 2
    width, ff = up_weight.shape
    all_words = segments.shape[1]
    words, word_cots, ent_cots, all_ids, rows, projected, words_turned = fetch(
        nz, word_states, word_cot, ent_cot, entity_ids, query_bias, key_bias, value_bias, ent_table, query_weight, key_weight, value_weight
    )
    ents = entity_ids.shape[1]
    word_out, ent_out, word_grad, ffn_sum, attn_sum, ent_sum, bias_sum, table_grad, touched = layer(
        nz, ent_table.shape[0], words, projected, words_turned, segments, pos_table, query_bias, key_bias, value_bias, out_weight, out_bias, norm_gain, norm_shift, up_weight, up_bias, down_weight, down_bias,
        word_cots, ent_cots, query_weight, key_weight, value_weight,
        rows, entity_pos, ent_proj, all_ids.reshape(-1, ents),
    )
    (table_grad, table_update, new_second, proj_grad, pos_grad, query_grad, key_grad, value_grad, out_grad, up_grad, down_grad,
     query_bias_grad, gain_grad, shift_grad, key_bias_grad, value_bias_grad, out_bias_grad, down_bias_grad, up_bias_grad,
     word_out, ent_out, word_grad,
    ) = last(
        n_dp, ff, all_words, table_grad, touched, first_moment, second_moment, ffn_sum, attn_sum, ent_sum, bias_sum, word_out, ent_out, word_grad
    )
    return (
        word_out,
        ent_out,
        word_grad,
        proj_grad,
        pos_grad,
        query_grad,
        query_bias_grad,
        key_grad,
        key_bias_grad,
        value_grad,
        value_bias_grad,
        out_grad,
        out_bias_grad,
        gain_grad,
        shift_grad,
        up_grad,
        up_bias_grad,
        down_grad,
        down_bias_grad,
        table_grad,
        table_update,
        new_second,
    )


def solution(mesh):
    return jax.shard_map(
        on_device,
        mesh=mesh,
        in_specs=(
            P("dp", "seq", None),
            P("dp", None),
            P("dp", None),
            P("dp", None),
            P(("dp", "seq"), None),
            P(("dp", "seq"), None),
            P(("dp", "seq"), None),
            P(),
            P(),
            P(),
            P(),
            P(),
            P(),
            P(),
            P(),
            P(),
            P(),
            P(),
            P(),
            P(),
            P(),
            P(),
            P(),
            P("dp", "seq", None),
            P("dp", "seq", None),
        ),
        out_specs=(
            P("dp", "seq", None),
            P("dp", "seq", None),
            P("dp", "seq", None),
            P("dp", None),
            P("dp", None),
            P(None, "dp", None),
            P(None, "dp"),
            P("dp", None),
            P("dp"),
            P("dp", None),
            P("dp"),
            P("dp", None),
            P("dp"),
            P(None, "dp"),
            P(None, "dp"),
            P("dp", None),
            P("dp"),
            P("dp", None),
            P("dp"),
            P(("dp", "seq"), None),
            P(("dp", "seq"), None),
            P(("dp", "seq"), None),
        ),
        check_vma=False,
    )
```

```python
import functools
import math

import jax
import jax.numpy as jnp
from jax import lax
from jax.experimental import pallas as pl
from jax.experimental.pallas import tpu as pltpu
from jax.sharding import PartitionSpec as P

HEADS = 12
HEAD = 64
LANES = 128
MESH = pl.DeviceIdType.MESH
LOW = jnp.bfloat16
F32 = jnp.float32
VMEM_BYTES = 125 * 512 * 1024

norm_eps = 1e-05
beta_one = 0.9
beta_two = 0.98
adam_eps = 1e-06
adam_step = 10.0
masked_score = -1e30


def dot(left, right):
    return jnp.dot(left, right, preferred_element_type=F32)


def dot_rows(left, right):
    return lax.dot_general(left, right, (((1,), (1,)), ((), ())), preferred_element_type=F32)


def dot_columns(left, right):
    return lax.dot_general(left, right, (((0,), (0,)), ((), ())), preferred_element_type=F32)


def span(start, size, unit):
    if isinstance(start, int):
        return pl.ds(start, size)
    return pl.ds(pl.multiple_of(start, unit), size)


def padded(rows):
    return -(-rows // 16) * 16


def loop(count, body, carry=0, unroll=1):
    def steps(i, carried):
        for k in range(unroll):
            carried = body(i * unroll + k, carried)
        return carried

    return lax.fori_loop(0, count // unroll, steps, carry)


class Place:
    def __init__(self, nz):
        self.dp, self.seq = lax.axis_index("dp"), lax.axis_index("seq")
        self.z, self.x = self.dp // 2, self.dp % 2
        self.y, self.core = self.seq // 2, self.seq % 2
        self.nz = nz
        self.other_core = (self.dp, self.y * 2 + 1 - self.core)
        self.other_y = (self.dp, (1 - self.y) * 2 + self.core)
        self.diagonal = (self.dp, (1 - self.y) * 2 + 1 - self.core)
        self.other_x = (self.z * 2 + 1 - self.x, self.seq)
        self.ahead = [(((self.z + k) % nz) * 2 + self.x, self.seq) for k in range(1, nz)]

    def z_ahead(self, k):
        return (self.z + k) % self.nz


def announce(partners):
    barrier = pltpu.get_barrier_semaphore()
    for partner in partners:
        pl.semaphore_signal(barrier, inc=1, device_id=partner, device_id_type=MESH)


def meet(partners):
    pl.semaphore_wait(pltpu.get_barrier_semaphore(), len(partners))


class Remote:
    def __init__(self, copies, number, src, dst, device):
        self.copies, self.number, self.src, self.dst, self.device = copies, number, src, dst, device
        self.open = True

    def make(self, landing=False):
        return pltpu.make_async_remote_copy(
            src_ref=self.dst() if landing else self.src(),
            dst_ref=self.dst(),
            send_sem=self.copies.send_sem.at[self.number],
            recv_sem=self.copies.recv_sem.at[self.number],
            device_id=self.device,
            device_id_type=MESH,
        )

    def wait_recv(self):
        self.make(landing=True).wait_recv()

    def wait_send(self):
        if self.open:
            self.make().wait_send()
        self.open = False


class Local:
    def __init__(self, copies, number, src, dst):
        self.copies, self.number, self.src, self.dst = copies, number, src, dst

    def make(self):
        return pltpu.make_async_copy(self.src(), self.dst(), self.copies.local_sem.at[self.number])

    def wait(self):
        self.make().wait()


class Copies:
    def __init__(self, send_sem, recv_sem, local_sem):
        self.send_sem, self.recv_sem, self.local_sem = send_sem, recv_sem, local_sem
        self.local_count = 0
        self.sent = []

    def send(self, src, dst, device):
        copy = Remote(self, len(self.sent), src, dst, device)
        copy.make().start()
        self.sent.append(copy)
        return copy

    def local(self, src, dst):
        copy = Local(self, self.local_count, src, dst)
        self.local_count += 1
        copy.make().start()
        return copy

    def finish(self):
        for copy in self.sent:
            copy.wait_send()


def copy_semaphores(remote, local):
    return [
        pltpu.SemaphoreType.DMA((remote,)),
        pltpu.SemaphoreType.DMA((remote,)),
        pltpu.SemaphoreType.DMA((local,)),
    ]


ANY = pl.BlockSpec(memory_space=pl.ANY)
IN_VMEM = pl.BlockSpec(memory_space=pltpu.VMEM)


def call(kernel, outs, in_specs, out_specs, scratch, name, collective_id=None):
    params = {"vmem_limit_bytes": VMEM_BYTES}
    if collective_id is not None:
        params.update(collective_id=collective_id, has_side_effects=True)
    return pl.pallas_call(
        kernel,
        out_shape=[jax.ShapeDtypeStruct(shape, dtype) for shape, dtype in outs],
        in_specs=in_specs,
        out_specs=out_specs,
        scratch_shapes=scratch,
        compiler_params=pltpu.CompilerParams(**params),
        name=name,
    )


def lane_mask(rows, head):
    lane = lax.broadcasted_iota(jnp.int32, (rows, LANES), 1)
    return (lane >= head * HEAD) & (lane < (head + 1) * HEAD)


def row_of(vector):
    return vector[...].astype(F32).reshape(1, vector.shape[0])


def own_half(vector, y):
    row = row_of(vector)
    half = row.shape[1] // 2
    return jnp.where(y == 0, row[:, :half], row[:, half:])


def as_column(row):
    parts = [
        jnp.transpose(jnp.broadcast_to(row[:, i : i + LANES], (LANES, LANES)))
        for i in range(0, row.shape[1], LANES)
    ]
    return jnp.concatenate(parts, axis=0) if len(parts) > 1 else parts[0]


def fetch_kernel(
    nz, words, word_cot, ent_cot, ids, query_bias, key_bias, value_bias, table, query_weight, key_weight, value_weight,
    all_words, word_cots, ent_cots, all_ids, rows_out, projected, words_turned, *scratch,
):
    (table_full, table_low, picked, answers, held, from_core, from_x, from_z, from_y, ids_here, query_here, key_here, value_here) = scratch[:13]
    copies = Copies(*scratch[13:])
    place = Place(nz)
    z, x, y, core = place.z, place.x, place.y, place.core
    n_dp = 2 * nz
    word_here, ent_here = words.shape[1], ent_cot.shape[1]
    ents = ids.shape[1]
    dp_others = [((place.dp + k) % n_dp, place.seq) for k in range(1, n_dp)]
    partners = [place.other_core, place.other_y, place.diagonal] + dp_others
    announce(partners)
    half = key_here.shape[1]
    columns = span(y * half, half, LANES)
    whole_table = copies.local(lambda: table, lambda: table_full)
    weight_copies = [
        copies.local(lambda: query_weight.at[pl.ds(0, 2), :, columns], lambda: query_here),
        copies.local(lambda: key_weight.at[:, columns], lambda: key_here),
        copies.local(lambda: value_weight.at[:, columns], lambda: value_here),
    ]
    ids_here[place.dp] = ids[...]
    meet(partners)
    id_copies = [copies.send(lambda: ids, lambda: ids_here.at[place.dp], device) for device in dp_others]
    quarter = span(place.seq * word_here, word_here, 128)
    word_copies = [
        copies.send(lambda: words.at[1 - core], lambda: all_words.at[quarter], place.diagonal),
        copies.send(lambda: words.at[core], lambda: all_words.at[quarter], place.other_y),
        copies.send(lambda: words.at[1 - core], lambda: all_words.at[quarter], place.other_core),
        copies.send(lambda: word_cot.at[1 - core], lambda: word_cots.at[span(core * word_here, word_here, 128)], place.other_core),
        copies.send(lambda: ent_cot.at[1 - core], lambda: ent_cots.at[span(core * ent_here, ent_here, 32)], place.other_core),
    ]
    all_words[quarter] = words[core]
    word_cots[span(core * word_here, word_here, 128)] = word_cot[core]
    ent_cots[span(core * ent_here, ent_here, 32)] = ent_cot[core]
    whole_table.wait()
    rows_dev = table.shape[0]

    def narrow(i, _):
        where = span(i * 128, 128, 128)
        table_low[where] = table_full[where].astype(LOW)
        return 0

    loop(rows_dev // 128, narrow)
    for copy in id_copies:
        copy.wait_recv()
    all_ids[...] = ids_here[...]
    base = (place.dp * 4 + place.seq) * rows_dev
    tiles = rows_dev // LANES

    def look_up(zz):
        for g in range(4):
            asked = ids_here[zz * 2 + g // 2, pl.ds(g % 2, 1), :] - base
            column = jnp.transpose(jnp.broadcast_to(asked, (ents, ents)))
            lane = lax.broadcasted_iota(jnp.int32, (ents, LANES), 1)
            low_hit = jnp.where((column & (LANES - 1)) == lane, 1.0, 0.0).astype(LOW)
            high = jnp.clip(column >> 7, -1, tiles).astype(F32).astype(LOW)
            for j in range(tiles):
                hit = jnp.where(high == jnp.asarray(j, LOW), low_hit, jnp.zeros_like(low_hit))
                picked[pl.ds(g * ents, ents), pl.ds(j * LANES, LANES)] = hit
        answer = dot(picked[...], table_low[...]).astype(LOW)
        answers[zz] = answer.reshape(2, 2, ents, answer.shape[-1])

    order = [place.z_ahead(k + 1) for k in range(nz)]
    core_copies, x_copies, z_copies = [], [], []

    def core_send(zz):
        return copies.send(lambda: answers.at[zz, :, 1 - core], lambda: from_core.at[zz], place.other_core)

    def after_core(k):
        zz = order[k]
        core_copies[k].wait_recv()
        held[zz] = answers[zz, :, core] + from_core[zz]
        x_copies.append(copies.send(lambda: held.at[zz, 1 - x], lambda: from_x.at[zz], place.other_x))

    def after_x(k):
        zz = order[k]
        x_copies[k].wait_recv()
        held[zz, x] = held[zz, x] + from_x[zz]
        if k < nz - 1:
            z_copies.append(copies.send(lambda: held.at[zz, x], lambda: from_z.at[k], place.ahead[k]))

    query_b = query_bias[:, columns].astype(F32)

    def project(i):
        weight = (query_here.at[0], query_here.at[1], key_here, value_here)[i]
        bias = query_b[i : i + 1] if i < 2 else own_half((key_bias, value_bias)[i - 2], y)
        projected[i] = (dot(all_words[...], weight[...]) + bias).astype(LOW)

    def turn_words(part):
        for i in range(part, words.shape[2] // LANES, 2):
            here = slice(i * LANES, (i + 1) * LANES)
            words_turned[here, :] = jnp.transpose(all_words[:, here].astype(F32)).astype(LOW)

    for k in range(nz + 2):
        if k == nz:
            for copy in word_copies[:3]:
                copy.wait_recv()
            for copy in weight_copies:
                copy.wait()
            project(0)
            project(1)
        if k == nz + 1:
            project(2)
        if k < nz:
            look_up(order[k])
            core_copies.append(core_send(order[k]))
        if 0 <= k - 1 < nz:
            after_core(k - 1)
        if 0 <= k - 2:
            after_x(k - 2)
    project(3)
    total = held[z, x]
    for k in range(nz - 1):
        z_copies[k].wait_recv()
        total = total + from_z[k]
    from_y[0] = total
    y_copy = copies.send(lambda: from_y.at[0], lambda: from_y.at[1], place.other_y)
    turn_words(0)
    turn_words(1)
    y_copy.wait_recv()
    rows_out[...] = from_y[0] + from_y[1]
    for copy in word_copies[3:]:
        copy.wait_recv()
    copies.finish()


def fetch(nz, words, word_cot, ent_cot, ids, query_bias, key_bias, value_bias, table, query_weight, key_weight, value_weight):
    _, word_here, width = words.shape
    ent_here, ents, (rows_dev, edim) = ent_cot.shape[1], ids.shape[1], table.shape
    n_dp = 2 * nz
    return call(
        functools.partial(fetch_kernel, nz),
        [
            ((4 * word_here, width), LOW),
            ((2 * word_here, width), LOW),
            ((2 * ent_here, width), LOW),
            ((n_dp, 2, ents), jnp.int32),
            ((ents, edim), LOW),
            ((4, 4 * word_here, width // 2), LOW),
            ((width, 4 * word_here), LOW),
        ],
        [IN_VMEM] * 7 + [ANY] * 4,
        [IN_VMEM] * 7,
        [
            pltpu.VMEM((rows_dev, edim), F32),
            pltpu.VMEM((rows_dev, edim), LOW),
            pltpu.VMEM((4 * ents, rows_dev), LOW),
            pltpu.VMEM((nz, 2, 2, ents, edim), LOW),
            pltpu.VMEM((nz, 2, ents, edim), LOW),
            pltpu.VMEM((nz, 2, ents, edim), LOW),
            pltpu.VMEM((nz, ents, edim), LOW),
            pltpu.VMEM((nz - 1, ents, edim), LOW),
            pltpu.VMEM((2, ents, edim), LOW),
            pltpu.VMEM((n_dp, 2, ents), jnp.int32),
            pltpu.VMEM((2, width, width // 2), LOW),
            pltpu.VMEM((width, width // 2), LOW),
            pltpu.VMEM((width, width // 2), LOW),
        ]
        + copy_semaphores(n_dp + 4 + 3 * nz + 2, 4),
        "fetch",
        1,
    )(words, word_cot, ent_cot, ids, query_bias, key_bias, value_bias, table, query_weight, key_weight, value_weight)


class Engine:
    RATES = {"core": 300e3, "x": 52e3, "y": 52e3, "z": 13e3}
    LATENCY = 2.0

    def __init__(self):
        self.clock, self.free, self.streams = 0.0, {}, []

    def transfer(self, link, size):
        start = max(self.clock, self.free.get(link, 0.0))
        self.free[link] = start + size / self.RATES[link]
        return self.free[link] + self.LATENCY

    def add(self, steps):
        self.streams.append([self.clock, list(steps)])
        self.poll()

    def run(self, stream):
        self.clock = max(self.clock, stream[0])
        ready = stream[1].pop(0)()
        stream[0] = self.clock if ready is None else ready

    def next(self):
        live = [stream for stream in self.streams if stream[1]]
        return min(live, key=lambda stream: stream[0]) if live else None

    def poll(self):
        while (stream := self.next()) is not None and stream[0] <= self.clock:
            self.run(stream)

    def work(self, time):
        self.clock += time
        self.poll()

    def drain(self):
        while (stream := self.next()) is not None:
            self.run(stream)


def blocks_of(rows):
    for size in (96, 64, 48, 32):
        if rows % size == 0:
            return size
    return 16


def add_blocks(engine, target, parts, leading, rows, columns):
    size = blocks_of(rows)
    count = rows // size

    def block(i, _):
        lead, row = i // count, (i % count) * size
        where = span(row, size, 16)
        if len(parts) == 2:
            value = parts[0](lead, where) + parts[1](lead, where)
        else:
            value = parts[0](lead, where).astype(F32)
            for part in parts[1:]:
                value = value + part(lead, where).astype(F32)
            value = value.astype(LOW)
        target(lead, where, value)
        return 0

    loop(leading * count, block, 0, 2 if leading * count % 2 == 0 else 1)
    engine.clock += 0.3 + leading * rows * columns / 1e6


class Job:
    def __init__(self, grads, reduced, base, size, order, columns):
        self.grads, self.reduced, self.base, self.size, self.order, self.columns = grads, reduced, base, size, order, columns
        self.half = size // 2
        self.part = size // 4 if order == "yxz" else size // 2

    def scratch(self, nz):
        shapes = [(nz, 2, self.half, self.columns)]
        if self.order == "yxz":
            shapes.append((nz, 2, self.part, self.columns))
        elif self.order == "xzy":
            shapes.append((2, self.part, self.columns))
        shapes += [(nz, self.part, self.columns), (nz - 1, self.part, self.columns)]
        return [pltpu.VMEM(shape, LOW) for shape in shapes]

    def remote_count(self, nz):
        return 1 + (1 if self.order != "xz" else 0) + 1 + (nz - 1) + 1 + 1

    def prepare(self, engine, place, copies, scratch):
        nz, z, x, y, core = place.nz, place.z, place.x, place.y, place.core
        base, half, part, order, columns = self.base, self.half, self.part, self.order, self.columns
        held = self.grads.at[:, :, span(base + core * half, half, 16)]
        from_core = scratch[0]
        from_y = scratch[1] if order != "xz" else None
        from_x, from_z = scratch[-2:]
        live = {}
        row_bytes = 2 * columns
        theirs = span(base + (1 - core) * half, half, 16)
        mine = span(base + core * half, half, 16)
        own_rows = span(y * part, part, 16) if order == "yxz" else pl.ds(0, part)
        final_rows = span(base + core * half + (y * part if order == "yxz" else 0), part, 16)

        def start():
            live["core"] = copies.send(lambda: self.grads.at[:, :, theirs], lambda: from_core, place.other_core)
            return engine.transfer("core", 2 * nz * half * row_bytes)

        def send_x():
            live["x"] = copies.send(lambda: held.at[:, 1 - x, own_rows], lambda: from_x, place.other_x)
            return engine.transfer("x", nz * part * row_bytes)

        def after_core():
            live["core"].wait_recv()

            def put(i, where, value):
                held[i // 2, i % 2, where] = value

            add_blocks(
                engine,
                put,
                [lambda i, where: held[i // 2, i % 2, where], lambda i, where: from_core[i // 2, i % 2, where]],
                2 * nz,
                half,
                columns,
            )
            if order == "yxz":
                live["y"] = copies.send(
                    lambda: held.at[:, :, span((1 - y) * part, part, 16)], lambda: from_y, place.other_y
                )
                return engine.transfer("y", 2 * nz * part * row_bytes)
            return send_x()

        def shifted(where):
            return span(y * part + where.start, where.size, 16) if order == "yxz" else where

        def after_y():
            live["y"].wait_recv()

            def put(i, where, value):
                held[i // 2, i % 2, shifted(where)] = value

            add_blocks(
                engine,
                put,
                [lambda i, where: held[i // 2, i % 2, shifted(where)], lambda i, where: from_y[i // 2, i % 2, where]],
                2 * nz,
                part,
                columns,
            )
            return send_x()

        def send_z(k):
            return copies.send(
                lambda: held.at[place.z_ahead(k + 1), x, own_rows], lambda: from_z.at[k], place.ahead[k]
            )

        def after_x():
            live["x"].wait_recv()

            def put(i, where, value):
                held[i, x, shifted(where)] = value

            add_blocks(
                engine,
                put,
                [lambda i, where: held[i, x, shifted(where)], lambda i, where: from_x[i, where]],
                nz,
                part,
                columns,
            )
            live["z"] = [send_z(k) for k in range(nz - 1)]
            return engine.transfer("z", part * row_bytes)

        def after_z():
            for copy in live["z"]:
                copy.wait_recv()

            def put(i, where, value):
                if order == "yxz":
                    self.reduced[span(base + core * half + y * part + where.start, where.size, 16)] = value
                elif order == "xz":
                    self.reduced[y, span(base + core * half + where.start, where.size, 16)] = value
                else:
                    from_y[0, where] = value

            def parts(k):
                return lambda i, where: from_z[k, where]

            add_blocks(
                engine,
                put,
                [lambda i, where: held[z, x, shifted(where)]] + [parts(k) for k in range(nz - 1)],
                1,
                part,
                columns,
            )
            if order == "xzy":
                live["y2"] = copies.send(lambda: from_y.at[0], lambda: from_y.at[1], place.other_y)
            else:
                view = lambda: self.reduced.at[final_rows] if order == "yxz" else self.reduced.at[y, final_rows]
                live["y2"] = copies.send(view, view, place.other_y)
            return engine.transfer("y", part * row_bytes)

        def after_gather():
            live["y2"].wait_recv()
            if order == "xzy":

                def put(i, where, value):
                    self.reduced[span(base + core * half + where.start, where.size, 16)] = value

                add_blocks(
                    engine, put, [lambda i, where: from_y[0, where], lambda i, where: from_y[1, where]], 1, part, columns
                )
            view = lambda: self.reduced.at[:, mine] if order == "xz" else self.reduced.at[mine]
            live["core2"] = copies.send(view, view, place.other_core)
            return engine.transfer("core", 2 * half * row_bytes)

        def end():
            live["core2"].wait_recv()

        middle_steps = [after_core, after_y, after_x] if order == "yxz" else [after_core, after_x]
        self.steps = [start] + middle_steps + [after_z, after_gather, end]


def lane_mean(value):
    return jnp.mean(value, axis=-1, keepdims=True)


def column_sum(value):
    return jnp.sum(value, axis=0, keepdims=True)


ROW_BLOCK = 32


def ffn_plan(n_dp, width, ff):
    down_rows, row_pad = ff // n_dp, padded(width // n_dp)
    size = 192 if down_rows % 192 == 0 else 32
    order = "yxz" if size % 64 == 0 else "xzy"
    plan = [(base, size, order) for base in range(0, down_rows, size)]
    base = down_rows
    for pair in range(ff // width // 2):
        order = "yxz" if row_pad % 32 == 0 else "xzy"
        plan.append((base, 2 * row_pad, order))
        base += 2 * row_pad
    plan.append((base, row_pad, "xzy"))
    return plan


def layer_kernel(
    nz, plan, words, projected, words_turned, segments, pos_table, query_bias, key_bias, value_bias, out_weight, out_bias, gains, shifts, up_weight, up_bias, down_weight, down_bias, word_cots, ent_cots,
    query_weight, key_weight, value_weight, rows, ent_pos, ent_proj, ids,
    word_out, ent_out, word_grad, ffn_reduced, attn_reduced, ent_reduced, bias_out, table_grad, touched,
    hidden_turned_in, query_words_in, query_ents_in, keys_in, values_in, probs_in, *scratch,
):
    (from_y_mixed, grad_mixed, grad_one, given, ffn_sum, attn_sum, ent_sum, bias_held, bias_from, all_rows, bias_heads, bias_middle,
     ffn_grads, grad_mixed_here, row_parts, mixed, ent_keep) = scratch[:17]
    copies = Copies(*scratch[-3:])
    engine = Engine()
    place = Place(nz)
    z, x, y, core = place.z, place.x, place.y, place.core
    n_dp = 2 * nz
    tokens, half = mixed.shape
    width = 2 * half
    ents = rows.shape[0]
    all_words = tokens - ents
    word_half, ent_half = all_words // 2, ents // 2
    part_tokens = tokens // 2
    ff = up_weight.shape[1]
    parts = ff // width
    row_part, row_pad, down_rows = width // n_dp, padded(width // n_dp), ff // n_dp
    partners = [place.other_core, place.other_y, place.other_x] + place.ahead
    announce(partners)

    jobs = {"ffn": [], "attn": [], "ent": []}

    def make_jobs(names, sources):
        at = 17
        for name, number, base, size, order, columns in plan:
            grads, reduced = sources.get(name, (None, None))
            if name == "attn" and grads is not None:
                grads, reduced = grads.at[number], reduced.at[number]
            job = Job(grads, reduced, base, size, order, columns)
            used = len(job.scratch(nz))
            if name in names:
                job.prepare(engine, place, copies, scratch[at : at + used])
                jobs[name].append(job)
            at += used

    make_jobs(["ffn"], {"ffn": (ffn_grads, ffn_sum)})

    def token_rows(side):
        return span(side * word_half, word_half, LANES), span(all_words + side * ent_half, ent_half, 64)

    mine, theirs = token_rows(y), token_rows(1 - y)
    own_columns, other_columns = span(y * half, half, LANES), span((1 - y) * half, half, LANES)
    word_part, ent_part = pl.ds(0, word_half), pl.ds(word_half, ent_half)
    mixed_copies = []
    scale = 1.0 / math.sqrt(HEAD)
    tiles = tokens // LANES

    def attend_phase(
        hidden_turned, query_words, query_ents, keys, values, probs, query_here, key_here, value_here, pos_here, values_turned, mask,
    ):
        weight_copies = [
            copies.local(lambda: pos_table, lambda: pos_here),
            copies.local(lambda: query_weight.at[pl.ds(2, 2), :, own_columns], lambda: query_here),
            copies.local(lambda: key_weight.at[:, own_columns], lambda: key_here),
            copies.local(lambda: value_weight.at[:, own_columns], lambda: value_here),
        ]
        word_rows = pl.ds(0, all_words)
        targets = [query_words, query_ents, keys, values]
        for i, target in enumerate(targets):
            weight_copies.append(
                copies.local(lambda i=i: projected.at[i], lambda target=target: target.at[word_rows])
            )
        weight_copies.append(copies.local(lambda: words_turned, lambda: hidden_turned.at[:, word_rows]))
        position = as_column(ent_pos[pl.ds(core, 1), :])
        picks = []
        for j in range(all_words // LANES):
            number = lax.broadcasted_iota(jnp.int32, (ents, LANES), 1) + j * LANES
            picks.append(jnp.where(position == number, 1.0, 0.0))
        pick = jnp.concatenate(picks, axis=1)
        word_seg = segments[pl.ds(core, 1), :].astype(F32)
        ent_seg = jnp.sum(pick * word_seg, axis=1, keepdims=True)
        weight_copies[0].wait()
        ent_hidden = dot(rows[...], ent_proj[...]) + dot(pick.astype(LOW), pos_here[...])
        ent_keep[...] = jnp.where(y == 0, ent_hidden[:ent_half], ent_hidden[ent_half:])
        ent_row = jnp.transpose(jnp.broadcast_to(ent_seg, (ents, LANES)))[:1]
        seg_row = jnp.concatenate([word_seg, ent_row], axis=1)
        seg_column = jnp.concatenate([as_column(word_seg), jnp.broadcast_to(ent_seg, (ents, LANES))], axis=0)
        for j in range(tiles):
            here = slice(j * LANES, (j + 1) * LANES)
            mask[:, here] = jnp.where(seg_column == seg_row[:, here], 0.0, masked_score)
        query_b = query_bias[:, own_columns].astype(F32)
        for copy in weight_copies[1:]:
            copy.wait()
        ent_low = ent_hidden.astype(LOW)
        query_words[all_words:] = (dot(ent_low, query_here[0]) + query_b[2:3]).astype(LOW)
        query_ents[all_words:] = (dot(ent_low, query_here[1]) + query_b[3:4]).astype(LOW)
        keys[all_words:] = (dot(ent_low, key_here[...]) + own_half(key_bias, y)).astype(LOW)
        values[all_words:] = (dot(ent_low, value_here[...]) + own_half(value_bias, y)).astype(LOW)
        hidden_turned[:, all_words:] = jnp.transpose(ent_hidden).astype(LOW)
        values_turned[...] = jnp.transpose(values[...].astype(F32)).astype(LOW)
        spills = [
            copies.local(lambda: query_words, lambda: query_words_in),
            copies.local(lambda: query_ents, lambda: query_ents_in),
            copies.local(lambda: keys, lambda: keys_in),
            copies.local(lambda: values, lambda: values_in),
        ]
        for pair in range(half // LANES):
            lanes = slice(pair * LANES, (pair + 1) * LANES)
            key, turned = keys[:, lanes], values_turned[lanes, :]
            row = lax.broadcasted_iota(jnp.int32, (LANES, tokens), 0)
            own_key, own_turned = [], []
            for head in range(2):
                own_key.append(jnp.where(lane_mask(tokens, head), key, jnp.zeros_like(key)))
                own_rows = (row >= head * HEAD) & (row < (head + 1) * HEAD)
                own_turned.append(jnp.where(own_rows, turned, jnp.zeros_like(turned)))
            for i in range(tiles):
                here = slice(i * LANES, (i + 1) * LANES)
                query_w, query_e = query_words[here, lanes], query_ents[here, lanes]
                part_sum = None
                for head in range(2):
                    raw = jnp.concatenate(
                        [dot_rows(own_key[head][:all_words], query_w), dot_rows(own_key[head][all_words:], query_e)], axis=0
                    )
                    score = raw * scale + mask[:, here]
                    weight = jnp.exp(score - jnp.max(score, axis=0, keepdims=True))
                    prob = (weight * (1.0 / jnp.sum(weight, axis=0, keepdims=True))).astype(LOW)
                    probs[pair * 2 + head, :, here] = prob
                    part = dot(own_turned[head], prob)
                    part_sum = part if part_sum is None else part_sum + part
                mixed[here, lanes] = jnp.transpose(part_sum).astype(LOW)
            heads = pl.ds(pair * 2, 2)
            if pair == 0:
                meet(partners)
            mixed_copies.extend([
                copies.send(
                    lambda lanes=lanes: mixed.at[theirs[0], lanes], lambda lanes=lanes: from_y_mixed.at[word_part, lanes], place.other_y
                ),
                copies.send(
                    lambda lanes=lanes: mixed.at[theirs[1], lanes], lambda lanes=lanes: from_y_mixed.at[ent_part, lanes], place.other_y
                ),
            ])
            spills.append(copies.local(lambda heads=heads: probs.at[heads], lambda heads=heads: probs_in.at[heads]))
        spills.append(copies.local(lambda: hidden_turned, lambda: hidden_turned_in))
        for copy in spills:
            copy.wait()

    pl.run_scoped(
        attend_phase,
        pltpu.VMEM((width, tokens), LOW),
        pltpu.VMEM((tokens, half), LOW),
        pltpu.VMEM((tokens, half), LOW),
        pltpu.VMEM((tokens, half), LOW),
        pltpu.VMEM((tokens, half), LOW),
        pltpu.VMEM((HEADS // 2, tokens, tokens), LOW),
        pltpu.VMEM((2, width, half), LOW),
        pltpu.VMEM((width, half), LOW),
        pltpu.VMEM((width, half), LOW),
        pltpu.VMEM((all_words, width), LOW),
        pltpu.VMEM((half, tokens), LOW),
        pltpu.VMEM((tokens, tokens), F32),
    )
    out_copies, mixed_back = [], []

    def forward_phase(
        out_here, up_here, down_here, word_here, mixed_full, work, normed_low, normal_one, inverse_one,
        act, slope, output, grad_two, grad_two_low, grad_one_low, normed_turned,
    ):
        cot, grad_up_low = output, slope
        weight_copies = [
            copies.local(lambda: out_weight, lambda: out_here),
            copies.local(lambda: words.at[mine[0]], lambda: word_here),
            copies.local(lambda: up_weight, lambda: up_here),
            copies.local(lambda: down_weight, lambda: down_here),
            copies.local(lambda: word_cots, lambda: cot.at[word_part]),
            copies.local(lambda: ent_cots, lambda: cot.at[ent_part]),
        ]
        gain, shift = gains[...].astype(F32), shifts[...].astype(F32)
        out_b, down_b, up_b = row_of(out_bias), row_of(down_bias), row_of(up_bias)
        mixed_full[word_part, own_columns] = mixed[mine[0]]
        mixed_full[ent_part, own_columns] = mixed[mine[1]]
        for copy in weight_copies[:2]:
            copy.wait()
        work[...] = dot(mixed_full[:, own_columns], out_here[own_columns, :])
        for copy in mixed_copies:
            copy.wait_recv()
        mixed_full[:, other_columns] = from_y_mixed[...]
        work[...] += dot(from_y_mixed[...], out_here[other_columns, :])

        def norm_one(residual):
            def step(i, _):
                rows = span(residual[1] + i * ROW_BLOCK, ROW_BLOCK, ROW_BLOCK)
                value = residual[0][span(i * ROW_BLOCK, ROW_BLOCK, ROW_BLOCK)].astype(F32) + (work[rows] + out_b)
                center = value - lane_mean(value)
                inverse = lax.rsqrt(lane_mean(center * center) + norm_eps)
                normal = center * inverse
                result = normal * gain[0:1] + shift[0:1]
                normal_one[rows] = normal
                inverse_one[rows] = jnp.broadcast_to(inverse, (ROW_BLOCK, LANES))
                normed_low[rows] = result.astype(LOW)
                return 0

            return step

        loop(word_half // ROW_BLOCK, norm_one((word_here, 0)), 0, 2)
        loop(ent_half // ROW_BLOCK, norm_one((ent_keep, word_half)), 0, 2)
        weight_copies[2].wait()
        for j in range(parts):
            columns = slice(j * width, (j + 1) * width)
            work[...] = dot(normed_low[...], up_here[:, columns]) + up_b[:, columns]

            def gelu(i, _):
                rows = span(i * ROW_BLOCK, ROW_BLOCK, ROW_BLOCK)
                value = work[rows]
                below = 0.5 * (1.0 + lax.erf(value * (1.0 / math.sqrt(2.0))))
                density = jnp.exp(-0.5 * value * value) * (1.0 / math.sqrt(2.0 * math.pi))
                act[rows, columns] = (value * below).astype(LOW)
                slope[rows, columns] = (below + value * density).astype(LOW)
                return 0

            loop(part_tokens // ROW_BLOCK, gelu)
        normed_turned[...] = jnp.transpose(normed_low[...].astype(F32)).astype(LOW)
        for copy in weight_copies[3:]:
            copy.wait()
        work[...] = dot(act[...], down_here[...])

        def norm_two(i, sums):
            rows = span(i * ROW_BLOCK, ROW_BLOCK, ROW_BLOCK)
            value = (normal_one[rows] * gain[0:1] + shift[0:1]) + (work[rows] + down_b)
            center = value - lane_mean(value)
            inverse = lax.rsqrt(lane_mean(center * center) + norm_eps)
            normal = center * inverse
            cotangent = cot[rows].astype(F32)
            output[rows] = (normal * gain[1:2] + shift[1:2]).astype(LOW)
            scaled = cotangent * gain[1:2]
            result = inverse * (scaled - lane_mean(scaled) - normal * lane_mean(scaled * normal))
            grad_two[rows] = result
            grad_two_low[rows] = result.astype(LOW)
            return (
                sums[0] + column_sum(cotangent * normal),
                sums[1] + column_sum(cotangent),
                sums[2] + column_sum(result),
            )

        nothing = jnp.zeros((1, width), F32)
        gain_two, shift_two, down_sum = loop(part_tokens // ROW_BLOCK, norm_two, (nothing, nothing, nothing), 2)
        quarter, ent_quarter = word_half // 2, ent_half // 2
        out_copies.extend([
            copies.send(
                lambda: output.at[span((1 - core) * quarter, quarter, LANES)], lambda: word_out.at[core], place.other_core
            ),
            copies.send(
                lambda: output.at[span(word_half + (1 - core) * ent_quarter, ent_quarter, 32)],
                lambda: ent_out.at[core],
                place.other_core,
            ),
        ])
        out_local = [
            copies.local(lambda: output.at[span(core * quarter, quarter, LANES)], lambda: word_out.at[core]),
            copies.local(
                lambda: output.at[span(word_half + core * ent_quarter, ent_quarter, 32)], lambda: ent_out.at[core]
            ),
        ]
        engine.clock = 0.0
        engine.free = {}
        def put(base, value):
            ffn_grads[:, :, pl.ds(base, row_part)] = value.astype(LOW).reshape(nz, 2, row_part, width)

        def down_products():
            per = width // down_rows
            for j in range(parts):
                value = dot_columns(act[:, j * width : (j + 1) * width], grad_two_low[...])
                value = value.astype(LOW).reshape(per, down_rows, width)
                for d in range(per):
                    slab = j * per + d
                    ffn_grads[slab // 2, slab % 2, pl.ds(0, down_rows)] = value[d]

        up_sums = []

        def grad_up(j):
            columns = slice(j * width, (j + 1) * width)
            work[...] = dot_rows(grad_two_low[...], down_here[columns, :])

            def grad_gelu(i, total_row):
                rows = span(i * ROW_BLOCK, ROW_BLOCK, ROW_BLOCK)
                value = work[rows] * slope[rows, columns].astype(F32)
                grad_up_low[rows, columns] = value.astype(LOW)
                return total_row + column_sum(value)

            up_sums.append(loop(part_tokens // ROW_BLOCK, grad_gelu, nothing, 2))
            engine.work(1.6)

        def up_product(j):
            columns = slice(j * width, (j + 1) * width)
            put(down_rows + j * row_pad, dot(normed_turned[...], grad_up_low[:, columns]))
            engine.work(0.9)

        downs = [job for job in jobs["ffn"] if job.base < down_rows]
        ups = [job for job in jobs["ffn"] if down_rows <= job.base][:-1]
        down_products()
        engine.clock += 3.0
        for job in downs:
            engine.add(job.steps)
        for j in range(parts):
            grad_up(j)
        work[...] = dot_rows(grad_up_low[...], up_here[...])
        engine.work(2.0)

        def back_one(i, sums):
            rows = span(i * ROW_BLOCK, ROW_BLOCK, ROW_BLOCK)
            upper = grad_two[rows] + work[rows]
            normal = normal_one[rows]
            inverse = inverse_one[rows, 0:1]
            scaled = upper * gain[0:1]
            result = inverse * (scaled - lane_mean(scaled) - normal * lane_mean(scaled * normal))
            grad_one[rows] = result
            grad_one_low[rows] = result.astype(LOW)
            return (
                sums[0] + column_sum(upper * normal),
                sums[1] + column_sum(upper),
                sums[2] + column_sum(result),
            )

        gain_one, shift_one, out_sum = loop(part_tokens // ROW_BLOCK, back_one, (nothing, nothing, nothing), 2)
        engine.work(1.0)
        grad_mixed_here[...] = dot_rows(grad_one_low[...], out_here[other_columns, :]).astype(LOW)
        mixed_back.extend([
            copies.send(lambda: grad_mixed_here.at[word_part], lambda: grad_mixed.at[mine[0]], place.other_y),
            copies.send(lambda: grad_mixed_here.at[ent_part], lambda: grad_mixed.at[mine[1]], place.other_y),
        ])
        engine.transfer("y", part_tokens * half * 2)
        own = dot_rows(grad_one_low[...], out_here[own_columns, :]).astype(LOW)
        grad_mixed[mine[0]] = own[:word_half]
        grad_mixed[mine[1]] = own[word_half:]
        engine.work(1.0)
        for j in range(parts):
            up_product(j)
            if j % 2 == 1:
                engine.add(ups[j // 2].steps)
        put(down_rows + parts * row_pad, dot_columns(mixed_full[...], grad_one_low[...]))
        engine.work(0.8)
        engine.add(jobs["ffn"][-1].steps)
        bias_rows = [out_sum, gain_one, gain_two, shift_one, shift_two] + up_sums + [down_sum]
        for i, row in enumerate(bias_rows):
            bias_middle[i : i + 1] = row
        for copy in out_copies:
            copy.wait_send()
        for copy in out_local:
            copy.wait()

    tall = lambda columns, dtype: pltpu.VMEM((part_tokens, columns), dtype)
    pl.run_scoped(
        forward_phase,
        pltpu.VMEM((width, width), LOW),
        pltpu.VMEM((width, ff), LOW),
        pltpu.VMEM((ff, width), LOW),
        pltpu.VMEM((word_half, width), LOW),
        tall(width, LOW),
        tall(width, F32),
        tall(width, LOW),
        tall(width, F32),
        tall(LANES, F32),
        tall(ff, LOW),
        tall(ff, LOW),
        tall(width, LOW),
        tall(width, F32),
        tall(width, LOW),
        tall(width, LOW),
        pltpu.VMEM((width, part_tokens), LOW),
    )
    live_words = {}

    def backward_phase(
        query_words, query_ents, keys, values, probs, query_here, key_here, value_here, keys_turned,
        grad_query_words, grad_query_ents, grad_keys, grad_values, hidden_turned, grad_hidden, hits, attn_grads, ent_grads, table_here, touched_here,
    ):
        total = grad_one
        make_jobs(["attn", "ent"], {"attn": (attn_grads, attn_sum), "ent": (ent_grads, ent_sum)})
        columns = span(y * half, half, LANES)
        copies_in = [
            copies.local(lambda: values_in, lambda: values),
            copies.local(lambda: keys_in, lambda: keys),
            copies.local(lambda: query_words_in, lambda: query_words),
            copies.local(lambda: query_ents_in, lambda: query_ents),
        ]
        prob_copies = []
        for head in range(probs.shape[0]):
            prob_copies.append(
                copies.local(lambda head=head: probs_in.at[head], lambda head=head: probs.at[head])
            )
        hidden_copy = copies.local(lambda: hidden_turned_in, lambda: hidden_turned)
        weight_copies = [
            copies.local(lambda: query_weight.at[:, :, columns], lambda: query_here),
            copies.local(lambda: key_weight.at[:, columns], lambda: key_here),
            copies.local(lambda: value_weight.at[:, columns], lambda: value_here),
        ]
        for copy in copies_in:
            copy.wait()
        for i in range(half // LANES):
            lanes = slice(i * LANES, (i + 1) * LANES)
            keys_turned[lanes, :] = jnp.transpose(keys[:, lanes].astype(F32)).astype(LOW)
        for copy in mixed_back:
            copy.wait_recv()
        engine.work(2.0)
        def pair_products(pair):
            lanes = slice(pair * LANES, (pair + 1) * LANES)
            word_turned, ent_turned = hidden_turned[:, :all_words], hidden_turned[:, all_words:]
            products = [
                dot(word_turned, grad_query_words[:all_words, lanes]),
                dot(word_turned, grad_query_ents[:all_words, lanes]),
                dot(ent_turned, grad_query_words[all_words:, lanes]),
                dot(ent_turned, grad_query_ents[all_words:, lanes]),
                dot(hidden_turned[...], grad_keys[:, lanes]),
                dot(hidden_turned[...], grad_values[:, lanes]),
            ]
            for i, value in enumerate(products):
                attn_grads[pair, :, :, pl.ds(i * row_pad, row_part)] = value.astype(LOW).reshape(nz, 2, row_part, LANES)
            engine.work(1.5)
            engine.add(jobs["attn"][pair].steps)

        for pair in range(half // LANES):
            lanes = slice(pair * LANES, (pair + 1) * LANES)
            grad_query_w = jnp.zeros((LANES, tokens), F32)
            grad_query_e = jnp.zeros((LANES, tokens), F32)
            grad_key_w = jnp.zeros((all_words, LANES), F32)
            grad_key_e = jnp.zeros((ents, LANES), F32)
            grad_value = jnp.zeros((tokens, LANES), F32)
            for head in range(2):
                own = lane_mask(tokens, head)
                value = values[:, lanes]
                own_value = jnp.where(own, value, jnp.zeros_like(value))
                prob_copies[pair * 2 + head].wait()

                given_heads = grad_mixed[:, lanes]
                grad_scores = probs.at[pair * 2 + head]
                grad_value += dot(grad_scores[...], jnp.where(own, given_heads, jnp.zeros_like(given_heads)))
                for i in range(tiles):
                    where = slice(i * LANES, (i + 1) * LANES)
                    grad_prob = dot_rows(own_value, grad_mixed[where, lanes])
                    prob = grad_scores[:, where].astype(F32)
                    both = prob * grad_prob
                    grad_scores[:, where] = (both - prob * jnp.sum(both, axis=0, keepdims=True)).astype(LOW)
                engine.work(1.7)
                query_w, query_e = query_words[:, lanes], query_ents[:, lanes]
                grad_key_w += dot(grad_scores[:all_words], jnp.where(own, query_w, jnp.zeros_like(query_w)))
                grad_key_e += dot(grad_scores[all_words:], jnp.where(own, query_e, jnp.zeros_like(query_e)))
                row = lax.broadcasted_iota(jnp.int32, (LANES, tokens), 0)
                own_rows = (row >= head * HEAD) & (row < (head + 1) * HEAD)
                turned = keys_turned[lanes, :]
                turned = jnp.where(own_rows, turned, jnp.zeros_like(turned))
                grad_query_w += dot(turned[:, :all_words], grad_scores[:all_words])
                grad_query_e += dot(turned[:, all_words:], grad_scores[all_words:])
                engine.work(1.7)
            grad_query_w = jnp.transpose(grad_query_w) * scale
            grad_query_e = jnp.transpose(grad_query_e) * scale
            grad_key_w, grad_key_e = grad_key_w * scale, grad_key_e * scale
            sums = [
                column_sum(grad_query_w[:all_words]),
                column_sum(grad_query_e[:all_words]),
                column_sum(grad_query_w[all_words:]),
                column_sum(grad_query_e[all_words:]),
                column_sum(grad_key_w) + column_sum(grad_key_e),
                column_sum(grad_value),
            ]
            for i, sum_row in enumerate(sums):
                bias_heads[i : i + 1, lanes] = sum_row
            grad_query_words[:, lanes] = grad_query_w.astype(LOW)
            grad_query_ents[:, lanes] = grad_query_e.astype(LOW)
            grad_keys[:all_words, lanes] = grad_key_w.astype(LOW)
            grad_keys[all_words:, lanes] = grad_key_e.astype(LOW)
            grad_values[:, lanes] = grad_value.astype(LOW)
            engine.work(0.5)
            if pair == 0:
                hidden_copy.wait()
            if pair + 1 < half // LANES:
                pair_products(pair)

        for copy in weight_copies:
            copy.wait()
        ent_rows, word_rows = slice(all_words, tokens), slice(0, all_words)

        def hidden_part(here, first, second):
            grad_hidden[here] = (
                dot_rows(grad_keys[here], key_here[...])
                + dot_rows(grad_values[here], value_here[...])
                + dot_rows(grad_query_words[here], query_here[first])
                + dot_rows(grad_query_ents[here], query_here[second])
            ).astype(LOW)

        hidden_part(ent_rows, 2, 3)
        own_ents = lax.broadcasted_iota(jnp.int32, (ents, width), 0) // ent_half == y
        twice = jnp.concatenate([grad_one[word_half:], grad_one[word_half:]], axis=0)
        ent_sum_part = grad_hidden[ent_rows].astype(F32) + jnp.where(own_ents, twice, 0.0)
        row_parts[0] = dot_rows(ent_sum_part.astype(LOW), ent_proj[...]).astype(LOW)
        rows_copy = copies.send(lambda: row_parts.at[0], lambda: row_parts.at[1], place.other_y)
        row_bytes = ents * ent_proj.shape[0] * 2
        rows_ready = engine.transfer("y", row_bytes)
        engine.work(0.7)
        pair_products(half // LANES - 1)
        ent_copy = copies.send(lambda: grad_hidden.at[theirs[1]], lambda: given.at[ent_part], place.other_y)
        ent_ready = engine.transfer("y", ent_half * width * 2)

        live_rows = {}

        def sum_hidden(start, count, own_start):
            def block(i, _):
                where = span(start + i * 32, 32, 32)
                own = span(own_start + i * 32, 32, 32)
                total[where] = grad_one[where] + (grad_hidden[own].astype(F32) + given[where].astype(F32))
                return 0

            loop(count // 32, block)

        def rows_z():
            rows_copy.wait_recv()
            all_rows[place.dp, core] = row_parts[0] + row_parts[1]
            view = lambda: all_rows.at[place.dp, core]
            live_rows["z"] = [copies.send(view, view, device) for device in place.ahead]
            return engine.transfer("z", row_bytes)

        def rows_x():
            for copy in live_rows["z"]:
                copy.wait_recv()
            live_rows["x"] = []
            for k in range(nz):
                view = lambda k=k: all_rows.at[place.z_ahead(k) * 2 + x, core]
                live_rows["x"].append(copies.send(view, view, place.other_x))
            return engine.transfer("x", nz * row_bytes)

        def rows_core():
            for copy in live_rows["x"]:
                copy.wait_recv()
            view = lambda: all_rows.at[:, core]
            live_rows["core"] = copies.send(view, view, place.other_core)
            return engine.transfer("core", n_dp * row_bytes)

        rows_dev = table_grad.shape[0]
        table_copies = []
        base_row = (place.dp * 4 + place.seq) * rows_dev

        def table_part(i):
            def step():
                if i == 0:
                    live_rows["core"].wait_recv()
                groups = ids.shape[0]
                block = min(table_block, LANES)
                counts = [jnp.zeros((block, ents), LOW) for _ in range(table_block // block)]
                for group in range(groups):
                    asked = ids[group : group + 1, :] - base_row
                    high = jnp.clip(asked >> 7, -1, rows_dev // LANES).astype(F32)
                    high = jnp.broadcast_to(high, (block, ents)).astype(LOW)
                    first_row = i * table_block
                    number = lax.broadcasted_iota(jnp.int32, (block, ents), 0) + first_row % LANES
                    low_hit = jnp.where((asked & (LANES - 1)) == number, 1.0, 0.0).astype(LOW)
                    for k in range(len(counts)):
                        hit = jnp.where(
                            high == jnp.asarray(first_row // LANES + k, LOW), low_hit, jnp.zeros_like(low_hit)
                        )
                        counts[k] = counts[k] + hit
                        hits[k * block : (k + 1) * block, group * ents : (group + 1) * ents] = hit
                count = jnp.concatenate(counts, axis=0).astype(F32)
                here = pl.ds(i * table_block, table_block)
                for copy in table_copies[2 * i - 4 : 2 * i - 2] if i >= 2 else []:
                    copy.wait()
                dps = min(n_dp, 8)
                grad = None
                for first in range(0, n_dp, dps):
                    given_rows = all_rows[first : first + dps].reshape(dps * 2 * ents, ent_proj.shape[0])
                    value = dot(hits[:, first * 2 * ents : (first + dps) * 2 * ents], given_rows)
                    grad = value if grad is None else grad + value
                table_here[i % 2] = grad
                named = jnp.sum(count, axis=1, keepdims=True)
                touched_here[i % 2] = jnp.broadcast_to(named, (table_block, LANES)).astype(LOW)
                table_copies.append(copies.local(lambda: table_here.at[i % 2], lambda: table_grad.at[here]))
                table_copies.append(copies.local(lambda: touched_here.at[i % 2], lambda: touched.at[here]))
                engine.clock += 0.7

            return step

        engine.add(
            [lambda: rows_ready, rows_z, rows_x, rows_core] + [table_part(i) for i in range(rows_dev // table_block)]
        )
        hidden_part(word_rows, 0, 1)
        word_copy = copies.send(lambda: grad_hidden.at[theirs[0]], lambda: given.at[word_part], place.other_y)
        word_ready = engine.transfer("y", word_half * width * 2)
        engine.work(1.5)

        bias_rows = bias_held.shape[0]
        bias_held[...] = jnp.zeros_like(bias_held)
        bias_held[0:6, columns] = bias_heads[0:6]
        bias_held[6:bias_rows] = bias_middle[0 : bias_rows - 6]
        live = {}
        bias_bytes = bias_rows * width * 2

        def bias_send(key, index, device):
            bias_from[2 * index] = bias_held[...].astype(LOW)
            live[key] = copies.send(lambda: bias_from.at[2 * index], lambda: bias_from.at[2 * index + 1], device)
            return engine.transfer(key, bias_bytes)

        def bias_take(key, index):
            live[key].wait_recv()
            bias_held[...] = bias_from[2 * index].astype(F32) + bias_from[2 * index + 1].astype(F32)

        def bias_core():
            return bias_send("core", 0, place.other_core)

        def bias_y():
            bias_take("core", 0)
            return bias_send("y", 1, place.other_y)

        def bias_x():
            bias_take("y", 1)
            return bias_send("x", 2, place.other_x)

        def bias_z():
            bias_take("x", 2)
            bias_from[6] = bias_held[...].astype(LOW)
            live["z"] = [
                copies.send(lambda: bias_from.at[6], lambda k=k: bias_from.at[7 + k], device)
                for k, device in enumerate(place.ahead)
            ]
            return engine.transfer("z", bias_bytes)

        def bias_end():
            value = bias_from[6].astype(F32)
            for k, copy in enumerate(live["z"]):
                copy.wait_recv()
                value = value + bias_from[7 + k].astype(F32)
            bias_out[...] = value

        engine.add([bias_core, bias_y, bias_x, bias_z, bias_end])
        quarter = word_half // 2

        def words_sum():
            word_copy.wait_recv()
            sum_hidden(0, word_half, y * word_half)
            engine.clock += 0.5
            live_words["send"] = copies.send(
                lambda: total.at[span((1 - core) * quarter, quarter, LANES)], lambda: word_grad.at[core], place.other_core
            )
            live_words["own"] = copies.local(
                lambda: total.at[span(core * quarter, quarter, LANES)], lambda: word_grad.at[core]
            )
            return engine.transfer("core", quarter * width * 4)

        def words_end():
            live_words["send"].wait_recv()
            live_words["own"].wait()

        engine.add([lambda: word_ready, words_sum, words_end])

        def ent_products():
            ent_copy.wait_recv()
            sum_hidden(word_half, ent_half, all_words + y * ent_half)
            proj_rows, pos_rows = rows.shape[1] // n_dp, all_words // n_dp
            proj_pad = padded(proj_rows)
            position = ent_pos[pl.ds(core, 1), :]
            picks = []
            for j in range(all_words // LANES):
                number = lax.broadcasted_iota(jnp.int32, (LANES, ents), 0) + j * LANES
                picks.append(jnp.where(number == position, 1.0, 0.0))
            pick = jnp.concatenate(picks, axis=0)
            here = lax.broadcasted_iota(jnp.int32, (all_words, ents), 1) // ent_half == y
            pick = jnp.where(here, pick, 0.0).astype(LOW)
            grad_ent = total[word_half:]
            grad_ent_low = grad_ent.astype(LOW)
            rest = (grad_ent - grad_ent_low.astype(F32)).astype(LOW)
            pos_grad = dot(pick, jnp.concatenate([grad_ent_low, grad_ent_low], axis=0)) + dot(
                pick, jnp.concatenate([rest, rest], axis=0)
            )
            proj_grad = dot_columns(rows[span(y * ent_half, ent_half, 64)], grad_ent_low)
            ent_grads[:, :, pl.ds(0, proj_rows)] = proj_grad.astype(LOW).reshape(nz, 2, proj_rows, width)
            ent_grads[:, :, pl.ds(proj_pad, pos_rows)] = pos_grad.astype(LOW).reshape(nz, 2, pos_rows, width)
            engine.clock += 1.0

        ent_job = jobs["ent"][0]
        engine.add([lambda: ent_ready, ent_products] + ent_job.steps)
        engine.drain()
        for copy in table_copies[-4:]:
            copy.wait()
        copies.finish()

    table_block = 256 if n_dp * 2 * ents <= 2048 else 32
    pl.run_scoped(
        backward_phase,
        pltpu.VMEM((tokens, half), LOW),
        pltpu.VMEM((tokens, half), LOW),
        pltpu.VMEM((tokens, half), LOW),
        pltpu.VMEM((tokens, half), LOW),
        pltpu.VMEM((HEADS // 2, tokens, tokens), LOW),
        pltpu.VMEM((4, width, half), LOW),
        pltpu.VMEM((width, half), LOW),
        pltpu.VMEM((width, half), LOW),
        pltpu.VMEM((half, tokens), LOW),
        pltpu.VMEM((tokens, half), LOW),
        pltpu.VMEM((tokens, half), LOW),
        pltpu.VMEM((tokens, half), LOW),
        pltpu.VMEM((tokens, half), LOW),
        pltpu.VMEM((width, tokens), LOW),
        pltpu.VMEM((tokens, width), LOW),
        pltpu.VMEM((table_block, n_dp * 2 * ents), LOW),
        pltpu.VMEM((half // LANES, nz, 2, 6 * row_pad, LANES), LOW),
        pltpu.VMEM((nz, 2, ent_sum.shape[0], width), LOW),
        pltpu.VMEM((2, table_block, ent_proj.shape[0]), F32),
        pltpu.VMEM((2, table_block, LANES), LOW),
    )
    last_copies = [
        copies.local(lambda: ffn_sum, lambda: ffn_reduced),
        copies.local(lambda: attn_sum, lambda: attn_reduced),
        copies.local(lambda: ent_sum, lambda: ent_reduced),
    ]
    for copy in out_copies:
        copy.wait_recv()
    for copy in last_copies:
        copy.wait()
    copies.finish()


def layer(
    nz, rows_dev, words, projected, words_turned, segments, pos_table, query_bias, key_bias, value_bias, out_weight, out_bias, gains, shifts, up_weight, up_bias, down_weight, down_bias, word_cots, ent_cots,
    query_weight, key_weight, value_weight, rows, ent_pos, ent_proj, ids,
):
    n_dp = 2 * nz
    all_words, width = words.shape
    half = width // 2
    ents, edim = rows.shape
    tokens = all_words + ents
    part, ff = tokens // 2, up_weight.shape[1]
    ffn_blocks = ffn_plan(n_dp, width, ff)
    ffn_rows, attn_rows = ffn_blocks[-1][0] + ffn_blocks[-1][1], 6 * padded(width // n_dp)
    ent_pad = padded(edim // n_dp) + padded(all_words // n_dp)
    bias_rows = 12 + ff // width
    plan = [("ffn", 0, base, size, order, width) for base, size, order in ffn_blocks]
    plan += [("attn", pair, 0, attn_rows, "xz", LANES) for pair in range(half // LANES)]
    plan.append(("ent", 0, 0, ent_pad, "xzy", width))
    scratch = [
        pltpu.VMEM((part, half), LOW),
        pltpu.VMEM((tokens, half), LOW),
        pltpu.VMEM((part, width), F32),
        pltpu.VMEM((part, width), LOW),
        pltpu.VMEM((ffn_rows, width), LOW),
        pltpu.VMEM((half // LANES, 2, attn_rows, LANES), LOW),
        pltpu.VMEM((ent_pad, width), LOW),
        pltpu.VMEM((bias_rows, width), F32),
        pltpu.VMEM((6 + nz, bias_rows, width), LOW),
        pltpu.VMEM((n_dp, 2, ents, edim), LOW),
        pltpu.VMEM((8, half), F32),
        pltpu.VMEM((16, width), F32),
        pltpu.VMEM((nz, 2, ffn_rows, width), LOW),
        pltpu.VMEM((part, half), LOW),
        pltpu.VMEM((2, ents, edim), LOW),
        pltpu.VMEM((tokens, half), LOW),
        pltpu.VMEM((ents // 2, width), F32),
    ]
    remote = 8 + 6 + 1 + 3 + nz + 1 + nz + nz + 2 + 4
    for name, _, base, size, order, columns in plan:
        job = Job(None, None, base, size, order, columns)
        scratch += job.scratch(nz)
        remote += job.remote_count(nz)
    scratch += copy_semaphores(remote, 60 + 2 * (rows_dev // 32))
    return call(
        functools.partial(layer_kernel, nz, plan),
        [
            ((2, all_words // 4, width), LOW),
            ((2, ents // 4, width), LOW),
            ((2, all_words // 4, width), F32),
            ((ffn_rows, width), LOW),
            ((half // LANES, 2, attn_rows, LANES), LOW),
            ((ent_pad, width), LOW),
            ((bias_rows, width), F32),
            ((rows_dev, edim), F32),
            ((rows_dev, LANES), LOW),
            ((width, tokens), LOW),
            ((tokens, half), LOW),
            ((tokens, half), LOW),
            ((tokens, half), LOW),
            ((tokens, half), LOW),
            ((HEADS // 2, tokens, tokens), LOW),
        ],
        [ANY, ANY, ANY, IN_VMEM, ANY] + [IN_VMEM] * 3 + [ANY] + [IN_VMEM] * 3 + [ANY, IN_VMEM, ANY, IN_VMEM] + [ANY] * 2 + [ANY] * 3 + [IN_VMEM] * 4,
        [ANY] * 6 + [IN_VMEM] + [ANY] * 8,
        scratch,
        "layer",
        2,
    )(words, projected, words_turned, segments, pos_table, query_bias, key_bias, value_bias, out_weight, out_bias, gains, shifts, up_weight, up_bias, down_weight, down_bias, word_cots, ent_cots,
      query_weight, key_weight, value_weight, rows, ent_pos, ent_proj, ids)[:9]


def last_kernel(
    n_dp, table_grad, touched, first, second, ffn_in, attn_in, ent_in, bias, words_in, ents_in, words_grad_in,
    table_out, update, new_second, proj_out, pos_out, query_out, key_out, value_out, out_out, up_out, down_out,
    query_bias, gain_grad, shift_grad, key_bias, value_bias, out_bias, down_bias, up_bias, word_out, ent_out, word_grad,
    ffn, attn, ent, words, ents, words_grad, proj_grad, pos_grad, query_grad, key_grad, value_grad, out_grad, up_grad, down_grad, sems,
):
    into = [(ffn_in, ffn), (attn_in, attn), (ent_in, ent), (words_in, words), (ents_in, ents), (words_grad_in, words_grad)]
    arrive = [pltpu.make_async_copy(src, dst, sems.at[i]) for i, (src, dst) in enumerate(into)]
    onward = [(down_grad, down_out), (up_grad, up_out), (out_grad, out_out), (proj_grad, proj_out), (pos_grad, pos_out)]
    onward += [(key_grad, key_out), (value_grad, value_out), (query_grad, query_out)]
    onward += [(words, word_out), (ents, ent_out), (words_grad, word_grad)]
    leave = [pltpu.make_async_copy(src, dst, sems.at[len(into) + i]) for i, (src, dst) in enumerate(onward)]

    @pl.when(pl.program_id(0) == 0)
    def _():
        for copy in arrive:
            copy.start()

    step = pl.program_id(0)
    grad = table_grad[...]
    hit = touched[:, 0:1].astype(F32) > 0.0
    mean_new = beta_one * first[...] + (1.0 - beta_one) * grad
    square_new = beta_two * second[...] + (1.0 - beta_two) * grad * grad
    direction = (mean_new * (1.0 / (1.0 - beta_one**adam_step))) / (
        jnp.sqrt(square_new * (1.0 / (1.0 - beta_two**adam_step))) + adam_eps
    )
    table_out[...] = grad
    update[...] = jnp.where(hit, direction, 0.0)
    new_second[...] = jnp.where(hit, square_new, second[...])
    width = ffn.shape[1]
    part, down_rows = out_grad.shape[0], down_grad.shape[0]
    pad = padded(part)
    proj_pad = padded(proj_grad.shape[0])
    parts = up_grad.shape[1] // width
    pairs = attn.shape[0]
    half = pairs * LANES

    @pl.when(step == 0)
    def _():
        arrive[0].wait()
        down_grad[...] = ffn[:down_rows].astype(F32)
        leave[0].start()
        for copy in arrive[3:]:
            copy.wait()
        for copy in leave[8:]:
            copy.start()

    @pl.when(step == 1)
    def _():
        for j in range(parts):
            base = down_rows + j * pad
            up_grad[:, j * width : (j + 1) * width] = ffn[base : base + part].astype(F32)
        leave[1].start()
        arrive[1].wait()
        arrive[2].wait()

    @pl.when(step == 2)
    def _():
        base = down_rows + parts * pad
        out_grad[...] = ffn[base : base + part].astype(F32)
        proj_grad[...] = ent[: proj_grad.shape[0]].astype(F32)
        pos_grad[...] = ent[proj_pad : proj_pad + pos_grad.shape[0]].astype(F32)
        for side in range(2):
            for pair in range(pairs):
                columns = slice(side * half + pair * LANES, side * half + (pair + 1) * LANES)
                key_grad[:, columns] = attn[pair, side, 4 * pad : 4 * pad + part].astype(F32)
                value_grad[:, columns] = attn[pair, side, 5 * pad : 5 * pad + part].astype(F32)
        for copy in leave[2:7]:
            copy.start()

    @pl.when(step == 2)
    def _():
        for side in range(2):
            for pair in range(pairs):
                columns = slice(side * half + pair * LANES, side * half + (pair + 1) * LANES)
                for i in range(4):
                    query_grad[i, :, columns] = attn[pair, side, i * pad : i * pad + part].astype(F32)
        leave[7].start()

    @pl.when(step == 3)
    def _():
        dp = lax.axis_index("dp")

        def own_columns(value, size, start):
            lane = lax.broadcasted_iota(jnp.int32, (value.shape[1], size), 0)
            want = lax.broadcasted_iota(jnp.int32, (value.shape[1], size), 1) + start
            pick = jnp.where(lane == want, 1.0, 0.0)
            return jnp.dot(value, pick, precision=lax.Precision.HIGHEST, preferred_element_type=F32)

        own = own_columns(bias[...], part, dp * part)
        query_bias[...] = own[0:4]
        gain_grad[...] = own[7:9]
        shift_grad[...] = own[9:11]
        for vector, i in ((key_bias, 4), (value_bias, 5), (out_bias, 6), (down_bias, 11 + parts)):
            vector[...] = own[i : i + 1].reshape(part)
        up = jnp.concatenate([bias[11 + j : 12 + j] for j in range(parts)], axis=1)
        size = up_bias.shape[0]
        if size % LANES == 0:
            per = width // size
            row = bias[pl.ds(11 + dp // per, 1), :]
            chosen = row[:, :size]
            for i in range(1, per):
                chosen = jnp.where(dp % per == i, row[:, i * size : (i + 1) * size], chosen)
            up_bias[...] = chosen.reshape(size)
        else:
            up_bias[...] = own_columns(up, size, dp * size).reshape(size)

    @pl.when(step == pl.num_programs(0) - 1)
    def _():
        for copy in leave:
            copy.wait()


def last(n_dp, ff, all_words, table_grad, touched, first, second, ffn, attn, ent, bias, words_low, ents_low, words_grad):
    width = ffn.shape[1]
    rows, edim = first.shape
    part = width // n_dp
    block = 512
    blocked = lambda columns: pl.BlockSpec((block, columns), lambda i: (i, 0))
    whole = lambda shape: pl.BlockSpec(shape, lambda i: (0,) * len(shape))
    shapes = [
        (edim // n_dp, width),
        (all_words // n_dp, width),
        (4, part, width),
        (part, width),
        (part, width),
        (part, width),
        (part, ff),
        (ff // n_dp, width),
        (4, part),
        (2, part),
        (2, part),
        (part,),
        (part,),
        (part,),
        (part,),
        (ff // n_dp,),
    ]
    through = [words_low, ents_low, words_grad]
    return pl.pallas_call(
        functools.partial(last_kernel, n_dp),
        grid=(rows // block,),
        out_shape=[jax.ShapeDtypeStruct((rows, edim), F32)] * 3
        + [jax.ShapeDtypeStruct(shape, F32) for shape in shapes]
        + [jax.ShapeDtypeStruct(array.shape, array.dtype) for array in through],
        in_specs=[blocked(edim), blocked(LANES), blocked(edim), blocked(edim)]
        + [ANY] * 3
        + [whole(bias.shape)]
        + [ANY] * 3,
        out_specs=[blocked(edim)] * 3 + [ANY] * 8 + [whole(shape) for shape in shapes[8:]] + [ANY] * 3,
        scratch_shapes=[pltpu.VMEM(array.shape, array.dtype) for array in [ffn, attn, ent] + through]
        + [pltpu.VMEM(shape, F32) for shape in shapes[:8]]
        + [pltpu.SemaphoreType.DMA((17,))],
        compiler_params=pltpu.CompilerParams(vmem_limit_bytes=VMEM_BYTES),
        name="last",
    )(table_grad, touched, first, second, ffn, attn, ent, bias, words_low, ents_low, words_grad)


def on_device(
    word_states,
    segments,
    entity_ids,
    entity_pos,
    ent_table,
    first_moment,
    second_moment,
    ent_proj,
    pos_table,
    query_weight,
    query_bias,
    key_weight,
    key_bias,
    value_weight,
    value_bias,
    out_weight,
    out_bias,
    norm_gain,
    norm_shift,
    up_weight,
    up_bias,
    down_weight,
    down_bias,
    word_cot,
    ent_cot,
):
    n_dp = lax.axis_size("dp")
    nz = n_dp // 2
    width, ff = up_weight.shape
    all_words = segments.shape[1]
    words, word_cots, ent_cots, all_ids, rows, projected, words_turned = fetch(
        nz, word_states, word_cot, ent_cot, entity_ids, query_bias, key_bias, value_bias, ent_table, query_weight, key_weight, value_weight
    )
    ents = entity_ids.shape[1]
    word_out, ent_out, word_grad, ffn_sum, attn_sum, ent_sum, bias_sum, table_grad, touched = layer(
        nz, ent_table.shape[0], words, projected, words_turned, segments, pos_table, query_bias, key_bias, value_bias, out_weight, out_bias, norm_gain, norm_shift, up_weight, up_bias, down_weight, down_bias,
        word_cots, ent_cots, query_weight, key_weight, value_weight,
        rows, entity_pos, ent_proj, all_ids.reshape(-1, ents),
    )
    (table_grad, table_update, new_second, proj_grad, pos_grad, query_grad, key_grad, value_grad, out_grad, up_grad, down_grad,
     query_bias_grad, gain_grad, shift_grad, key_bias_grad, value_bias_grad, out_bias_grad, down_bias_grad, up_bias_grad,
     word_out, ent_out, word_grad,
    ) = last(
        n_dp, ff, all_words, table_grad, touched, first_moment, second_moment, ffn_sum, attn_sum, ent_sum, bias_sum, word_out, ent_out, word_grad
    )
    return (
        word_out,
        ent_out,
        word_grad,
        proj_grad,
        pos_grad,
        query_grad,
        query_bias_grad,
        key_grad,
        key_bias_grad,
        value_grad,
        value_bias_grad,
        out_grad,
        out_bias_grad,
        gain_grad,
        shift_grad,
        up_grad,
        up_bias_grad,
        down_grad,
        down_bias_grad,
        table_grad,
        table_update,
        new_second,
    )


def solution(mesh):
    return jax.shard_map(
        on_device,
        mesh=mesh,
        in_specs=(
            P("dp", "seq", None),
            P("dp", None),
            P("dp", None),
            P("dp", None),
            P(("dp", "seq"), None),
            P(("dp", "seq"), None),
            P(("dp", "seq"), None),
            P(),
            P(),
            P(),
            P(),
            P(),
            P(),
            P(),
            P(),
            P(),
            P(),
            P(),
            P(),
            P(),
            P(),
            P(),
            P(),
            P("dp", "seq", None),
            P("dp", "seq", None),
        ),
        out_specs=(
            P("dp", "seq", None),
            P("dp", "seq", None),
            P("dp", "seq", None),
            P("dp", None),
            P("dp", None),
            P(None, "dp", None),
            P(None, "dp"),
            P("dp", None),
            P("dp"),
            P("dp", None),
            P("dp"),
            P("dp", None),
            P("dp"),
            P(None, "dp"),
            P(None, "dp"),
            P("dp", None),
            P("dp"),
            P("dp", None),
            P("dp"),
            P(("dp", "seq"), None),
            P(("dp", "seq"), None),
            P(("dp", "seq"), None),
        ),
        check_vma=False,
    )
```

```python
import functools
import math

import jax
import jax.numpy as jnp
from jax import lax
from jax.experimental import pallas as pl
from jax.experimental.pallas import tpu as pltpu
from jax.sharding import PartitionSpec as P

HEADS = 12
HEAD = 64
LANES = 128
MESH = pl.DeviceIdType.MESH
LOW = jnp.bfloat16
F32 = jnp.float32
VMEM_BYTES = 125 * 512 * 1024

norm_eps = 1e-05
beta_one = 0.9
beta_two = 0.98
adam_eps = 1e-06
adam_step = 10.0
masked_score = -1e30


def dot(left, right):
    return jnp.dot(left, right, preferred_element_type=F32)


def dot_rows(left, right):
    return lax.dot_general(left, right, (((1,), (1,)), ((), ())), preferred_element_type=F32)


def dot_columns(left, right):
    return lax.dot_general(left, right, (((0,), (0,)), ((), ())), preferred_element_type=F32)


def span(start, size, unit):
    if isinstance(start, int):
        return pl.ds(start, size)
    return pl.ds(pl.multiple_of(start, unit), size)


def padded(rows):
    return -(-rows // 16) * 16


def loop(count, body, carry=0, unroll=1):
    def steps(i, carried):
        for k in range(unroll):
            carried = body(i * unroll + k, carried)
        return carried

    return lax.fori_loop(0, count // unroll, steps, carry)


class Place:
    def __init__(self, nz):
        self.dp, self.seq = lax.axis_index("dp"), lax.axis_index("seq")
        self.z, self.x = self.dp // 2, self.dp % 2
        self.y, self.core = self.seq // 2, self.seq % 2
        self.nz = nz
        self.other_core = (self.dp, self.y * 2 + 1 - self.core)
        self.other_y = (self.dp, (1 - self.y) * 2 + self.core)
        self.diagonal = (self.dp, (1 - self.y) * 2 + 1 - self.core)
        self.other_x = (self.z * 2 + 1 - self.x, self.seq)
        self.ahead = [(((self.z + k) % nz) * 2 + self.x, self.seq) for k in range(1, nz)]

    def z_ahead(self, k):
        return (self.z + k) % self.nz


def announce(partners):
    barrier = pltpu.get_barrier_semaphore()
    for partner in partners:
        pl.semaphore_signal(barrier, inc=1, device_id=partner, device_id_type=MESH)


def meet(partners):
    pl.semaphore_wait(pltpu.get_barrier_semaphore(), len(partners))


class Remote:
    def __init__(self, copies, number, src, dst, device):
        self.copies, self.number, self.src, self.dst, self.device = copies, number, src, dst, device
        self.open = True

    def make(self, landing=False):
        return pltpu.make_async_remote_copy(
            src_ref=self.dst() if landing else self.src(),
            dst_ref=self.dst(),
            send_sem=self.copies.send_sem.at[self.number],
            recv_sem=self.copies.recv_sem.at[self.number],
            device_id=self.device,
            device_id_type=MESH,
        )

    def wait_recv(self):
        self.make(landing=True).wait_recv()

    def wait_send(self):
        if self.open:
            self.make().wait_send()
        self.open = False


class Local:
    def __init__(self, copies, number, src, dst):
        self.copies, self.number, self.src, self.dst = copies, number, src, dst

    def make(self):
        return pltpu.make_async_copy(self.src(), self.dst(), self.copies.local_sem.at[self.number])

    def wait(self):
        self.make().wait()


class Copies:
    def __init__(self, send_sem, recv_sem, local_sem):
        self.send_sem, self.recv_sem, self.local_sem = send_sem, recv_sem, local_sem
        self.local_count = 0
        self.sent = []

    def send(self, src, dst, device):
        copy = Remote(self, len(self.sent), src, dst, device)
        copy.make().start()
        self.sent.append(copy)
        return copy

    def local(self, src, dst):
        copy = Local(self, self.local_count, src, dst)
        self.local_count += 1
        copy.make().start()
        return copy

    def finish(self):
        for copy in self.sent:
            copy.wait_send()


def copy_semaphores(remote, local):
    return [
        pltpu.SemaphoreType.DMA((remote,)),
        pltpu.SemaphoreType.DMA((remote,)),
        pltpu.SemaphoreType.DMA((local,)),
    ]


ANY = pl.BlockSpec(memory_space=pl.ANY)
IN_VMEM = pl.BlockSpec(memory_space=pltpu.VMEM)


def call(kernel, outs, in_specs, out_specs, scratch, name, collective_id=None):
    params = {"vmem_limit_bytes": VMEM_BYTES}
    if collective_id is not None:
        params.update(collective_id=collective_id, has_side_effects=True)
    return pl.pallas_call(
        kernel,
        out_shape=[jax.ShapeDtypeStruct(shape, dtype) for shape, dtype in outs],
        in_specs=in_specs,
        out_specs=out_specs,
        scratch_shapes=scratch,
        compiler_params=pltpu.CompilerParams(**params),
        name=name,
    )


def lane_mask(rows, head):
    lane = lax.broadcasted_iota(jnp.int32, (rows, LANES), 1)
    return (lane >= head * HEAD) & (lane < (head + 1) * HEAD)


def row_of(vector):
    return vector[...].astype(F32).reshape(1, vector.shape[0])


def own_half(vector, y):
    row = row_of(vector)
    half = row.shape[1] // 2
    return jnp.where(y == 0, row[:, :half], row[:, half:])


def as_column(row):
    parts = [
        jnp.transpose(jnp.broadcast_to(row[:, i : i + LANES], (LANES, LANES)))
        for i in range(0, row.shape[1], LANES)
    ]
    return jnp.concatenate(parts, axis=0) if len(parts) > 1 else parts[0]


def fetch_kernel(
    nz, words, word_cot, ent_cot, ids, query_bias, key_bias, value_bias, table, query_weight, key_weight, value_weight,
    all_words, word_cots, ent_cots, all_ids, rows_out, projected, words_turned, *scratch,
):
    (table_full, table_low, picked, answers, held, from_core, from_x, from_z, from_y, ids_here, query_here, key_here, value_here) = scratch[:13]
    copies = Copies(*scratch[13:])
    place = Place(nz)
    z, x, y, core = place.z, place.x, place.y, place.core
    n_dp = 2 * nz
    word_here, ent_here = words.shape[1], ent_cot.shape[1]
    ents = ids.shape[1]
    dp_others = [((place.dp + k) % n_dp, place.seq) for k in range(1, n_dp)]
    partners = [place.other_core, place.other_y, place.diagonal] + dp_others
    announce(partners)
    half = key_here.shape[1]
    columns = span(y * half, half, LANES)
    whole_table = copies.local(lambda: table, lambda: table_full)
    weight_copies = [
        copies.local(lambda: query_weight.at[pl.ds(0, 2), :, columns], lambda: query_here),
        copies.local(lambda: key_weight.at[:, columns], lambda: key_here),
        copies.local(lambda: value_weight.at[:, columns], lambda: value_here),
    ]
    ids_here[place.dp] = ids[...]
    meet(partners)
    id_copies = [copies.send(lambda: ids, lambda: ids_here.at[place.dp], device) for device in dp_others]
    quarter = span(place.seq * word_here, word_here, 128)
    word_copies = [
        copies.send(lambda: words.at[1 - core], lambda: all_words.at[quarter], place.diagonal),
        copies.send(lambda: words.at[core], lambda: all_words.at[quarter], place.other_y),
        copies.send(lambda: words.at[1 - core], lambda: all_words.at[quarter], place.other_core),
        copies.send(lambda: word_cot.at[1 - core], lambda: word_cots.at[span(core * word_here, word_here, 128)], place.other_core),
        copies.send(lambda: ent_cot.at[1 - core], lambda: ent_cots.at[span(core * ent_here, ent_here, 32)], place.other_core),
    ]
    all_words[quarter] = words[core]
    word_cots[span(core * word_here, word_here, 128)] = word_cot[core]
    ent_cots[span(core * ent_here, ent_here, 32)] = ent_cot[core]
    whole_table.wait()
    rows_dev = table.shape[0]

    def narrow(i, _):
        where = span(i * 128, 128, 128)
        table_low[where] = table_full[where].astype(LOW)
        return 0

    loop(rows_dev // 128, narrow)
    for copy in id_copies:
        copy.wait_recv()
    all_ids[...] = ids_here[...]
    base = (place.dp * 4 + place.seq) * rows_dev
    tiles = rows_dev // LANES

    def look_up(zz):
        for g in range(4):
            asked = ids_here[zz * 2 + g // 2, pl.ds(g % 2, 1), :] - base
            column = jnp.transpose(jnp.broadcast_to(asked, (ents, ents)))
            lane = lax.broadcasted_iota(jnp.int32, (ents, LANES), 1)
            low_hit = jnp.where((column & (LANES - 1)) == lane, 1.0, 0.0).astype(LOW)
            high = jnp.clip(column >> 7, -1, tiles).astype(F32).astype(LOW)
            for j in range(tiles):
                hit = jnp.where(high == jnp.asarray(j, LOW), low_hit, jnp.zeros_like(low_hit))
                picked[pl.ds(g * ents, ents), pl.ds(j * LANES, LANES)] = hit
        answer = dot(picked[...], table_low[...]).astype(LOW)
        answers[zz] = answer.reshape(2, 2, ents, answer.shape[-1])

    order = [place.z_ahead(k + 1) for k in range(nz)]
    core_copies, x_copies, z_copies = [], [], []

    def core_send(zz):
        return copies.send(lambda: answers.at[zz, :, 1 - core], lambda: from_core.at[zz], place.other_core)

    def after_core(k):
        zz = order[k]
        core_copies[k].wait_recv()
        held[zz] = answers[zz, :, core] + from_core[zz]
        x_copies.append(copies.send(lambda: held.at[zz, 1 - x], lambda: from_x.at[zz], place.other_x))

    def after_x(k):
        zz = order[k]
        x_copies[k].wait_recv()
        held[zz, x] = held[zz, x] + from_x[zz]
        if k < nz - 1:
            z_copies.append(copies.send(lambda: held.at[zz, x], lambda: from_z.at[k], place.ahead[k]))

    query_b = query_bias[:, columns].astype(F32)

    def project(i):
        weight = (query_here.at[0], query_here.at[1], key_here, value_here)[i]
        bias = query_b[i : i + 1] if i < 2 else own_half((key_bias, value_bias)[i - 2], y)
        projected[i] = (dot(all_words[...], weight[...]) + bias).astype(LOW)

    def turn_words(part):
        for i in range(part, words.shape[2] // LANES, 2):
            here = slice(i * LANES, (i + 1) * LANES)
            words_turned[here, :] = jnp.transpose(all_words[:, here].astype(F32)).astype(LOW)

    for k in range(nz + 2):
        if k == nz:
            for copy in word_copies[:3]:
                copy.wait_recv()
            for copy in weight_copies:
                copy.wait()
            project(0)
            project(1)
        if k == nz + 1:
            project(2)
        if k < nz:
            look_up(order[k])
            core_copies.append(core_send(order[k]))
        if 0 <= k - 1 < nz:
            after_core(k - 1)
        if 0 <= k - 2:
            after_x(k - 2)
    project(3)
    total = held[z, x]
    for k in range(nz - 1):
        z_copies[k].wait_recv()
        total = total + from_z[k]
    from_y[0] = total
    y_copy = copies.send(lambda: from_y.at[0], lambda: from_y.at[1], place.other_y)
    turn_words(0)
    turn_words(1)
    y_copy.wait_recv()
    rows_out[...] = from_y[0] + from_y[1]
    for copy in word_copies[3:]:
        copy.wait_recv()
    copies.finish()


def fetch(nz, words, word_cot, ent_cot, ids, query_bias, key_bias, value_bias, table, query_weight, key_weight, value_weight):
    _, word_here, width = words.shape
    ent_here, ents, (rows_dev, edim) = ent_cot.shape[1], ids.shape[1], table.shape
    n_dp = 2 * nz
    return call(
        functools.partial(fetch_kernel, nz),
        [
            ((4 * word_here, width), LOW),
            ((2 * word_here, width), LOW),
            ((2 * ent_here, width), LOW),
            ((n_dp, 2, ents), jnp.int32),
            ((ents, edim), LOW),
            ((4, 4 * word_here, width // 2), LOW),
            ((width, 4 * word_here), LOW),
        ],
        [IN_VMEM] * 7 + [ANY] * 4,
        [IN_VMEM] * 7,
        [
            pltpu.VMEM((rows_dev, edim), F32),
            pltpu.VMEM((rows_dev, edim), LOW),
            pltpu.VMEM((4 * ents, rows_dev), LOW),
            pltpu.VMEM((nz, 2, 2, ents, edim), LOW),
            pltpu.VMEM((nz, 2, ents, edim), LOW),
            pltpu.VMEM((nz, 2, ents, edim), LOW),
            pltpu.VMEM((nz, ents, edim), LOW),
            pltpu.VMEM((nz - 1, ents, edim), LOW),
            pltpu.VMEM((2, ents, edim), LOW),
            pltpu.VMEM((n_dp, 2, ents), jnp.int32),
            pltpu.VMEM((2, width, width // 2), LOW),
            pltpu.VMEM((width, width // 2), LOW),
            pltpu.VMEM((width, width // 2), LOW),
        ]
        + copy_semaphores(n_dp + 4 + 3 * nz + 2, 4),
        "fetch",
        1,
    )(words, word_cot, ent_cot, ids, query_bias, key_bias, value_bias, table, query_weight, key_weight, value_weight)


class Engine:
    RATES = {"core": 300e3, "x": 52e3, "y": 52e3, "z": 13e3}
    LATENCY = 2.0

    def __init__(self):
        self.clock, self.free, self.streams = 0.0, {}, []

    def transfer(self, link, size):
        start = max(self.clock, self.free.get(link, 0.0))
        self.free[link] = start + size / self.RATES[link]
        return self.free[link] + self.LATENCY

    def add(self, steps):
        self.streams.append([self.clock, list(steps)])
        self.poll()

    def run(self, stream):
        self.clock = max(self.clock, stream[0])
        ready = stream[1].pop(0)()
        stream[0] = self.clock if ready is None else ready

    def next(self):
        live = [stream for stream in self.streams if stream[1]]
        return min(live, key=lambda stream: stream[0]) if live else None

    def poll(self):
        while (stream := self.next()) is not None and stream[0] <= self.clock:
            self.run(stream)

    def work(self, time):
        self.clock += time
        self.poll()

    def drain(self):
        while (stream := self.next()) is not None:
            self.run(stream)


def blocks_of(rows):
    for size in (96, 64, 48, 32):
        if rows % size == 0:
            return size
    return 16


def add_blocks(engine, target, parts, leading, rows, columns):
    size = blocks_of(rows)
    count = rows // size

    def block(i, _):
        lead, row = i // count, (i % count) * size
        where = span(row, size, 16)
        if len(parts) == 2:
            value = parts[0](lead, where) + parts[1](lead, where)
        else:
            value = parts[0](lead, where).astype(F32)
            for part in parts[1:]:
                value = value + part(lead, where).astype(F32)
            value = value.astype(LOW)
        target(lead, where, value)
        return 0

    loop(leading * count, block)
    engine.clock += 0.3 + leading * rows * columns / 1e6


class Job:
    def __init__(self, grads, reduced, base, size, order, columns):
        self.grads, self.reduced, self.base, self.size, self.order, self.columns = grads, reduced, base, size, order, columns
        self.half = size // 2
        self.part = size // 4 if order == "yxz" else size // 2

    def scratch(self, nz):
        shapes = [(nz, 2, self.half, self.columns)]
        if self.order == "yxz":
            shapes.append((nz, 2, self.part, self.columns))
        elif self.order == "xzy":
            shapes.append((2, self.part, self.columns))
        shapes += [(nz, self.part, self.columns), (nz - 1, self.part, self.columns)]
        return [pltpu.VMEM(shape, LOW) for shape in shapes]

    def remote_count(self, nz):
        return 1 + (1 if self.order != "xz" else 0) + 1 + (nz - 1) + 1 + 1

    def prepare(self, engine, place, copies, scratch):
        nz, z, x, y, core = place.nz, place.z, place.x, place.y, place.core
        base, half, part, order, columns = self.base, self.half, self.part, self.order, self.columns
        held = self.grads.at[:, :, span(base + core * half, half, 16)]
        from_core = scratch[0]
        from_y = scratch[1] if order != "xz" else None
        from_x, from_z = scratch[-2:]
        live = {}
        row_bytes = 2 * columns
        theirs = span(base + (1 - core) * half, half, 16)
        mine = span(base + core * half, half, 16)
        own_rows = span(y * part, part, 16) if order == "yxz" else pl.ds(0, part)
        final_rows = span(base + core * half + (y * part if order == "yxz" else 0), part, 16)

        def start():
            live["core"] = copies.send(lambda: self.grads.at[:, :, theirs], lambda: from_core, place.other_core)
            return engine.transfer("core", 2 * nz * half * row_bytes)

        def send_x():
            live["x"] = copies.send(lambda: held.at[:, 1 - x, own_rows], lambda: from_x, place.other_x)
            return engine.transfer("x", nz * part * row_bytes)

        def after_core():
            live["core"].wait_recv()

            def put(i, where, value):
                held[i // 2, i % 2, where] = value

            add_blocks(
                engine,
                put,
                [lambda i, where: held[i // 2, i % 2, where], lambda i, where: from_core[i // 2, i % 2, where]],
                2 * nz,
                half,
                columns,
            )
            if order == "yxz":
                live["y"] = copies.send(
                    lambda: held.at[:, :, span((1 - y) * part, part, 16)], lambda: from_y, place.other_y
                )
                return engine.transfer("y", 2 * nz * part * row_bytes)
            return send_x()

        def shifted(where):
            return span(y * part + where.start, where.size, 16) if order == "yxz" else where

        def after_y():
            live["y"].wait_recv()

            def put(i, where, value):
                held[i // 2, i % 2, shifted(where)] = value

            add_blocks(
                engine,
                put,
                [lambda i, where: held[i // 2, i % 2, shifted(where)], lambda i, where: from_y[i // 2, i % 2, where]],
                2 * nz,
                part,
                columns,
            )
            return send_x()

        def send_z(k):
            return copies.send(
                lambda: held.at[place.z_ahead(k + 1), x, own_rows], lambda: from_z.at[k], place.ahead[k]
            )

        def after_x():
            live["x"].wait_recv()

            def put(i, where, value):
                held[i, x, shifted(where)] = value

            add_blocks(
                engine,
                put,
                [lambda i, where: held[i, x, shifted(where)], lambda i, where: from_x[i, where]],
                nz,
                part,
                columns,
            )
            live["z"] = [send_z(k) for k in range(nz - 1)]
            return engine.transfer("z", part * row_bytes)

        def after_z():
            for copy in live["z"]:
                copy.wait_recv()

            def put(i, where, value):
                if order == "yxz":
                    self.reduced[span(base + core * half + y * part + where.start, where.size, 16)] = value
                elif order == "xz":
                    self.reduced[y, span(base + core * half + where.start, where.size, 16)] = value
                else:
                    from_y[0, where] = value

            def parts(k):
                return lambda i, where: from_z[k, where]

            add_blocks(
                engine,
                put,
                [lambda i, where: held[z, x, shifted(where)]] + [parts(k) for k in range(nz - 1)],
                1,
                part,
                columns,
            )
            if order == "xzy":
                live["y2"] = copies.send(lambda: from_y.at[0], lambda: from_y.at[1], place.other_y)
            else:
                view = lambda: self.reduced.at[final_rows] if order == "yxz" else self.reduced.at[y, final_rows]
                live["y2"] = copies.send(view, view, place.other_y)
            return engine.transfer("y", part * row_bytes)

        def after_gather():
            live["y2"].wait_recv()
            if order == "xzy":

                def put(i, where, value):
                    self.reduced[span(base + core * half + where.start, where.size, 16)] = value

                add_blocks(
                    engine, put, [lambda i, where: from_y[0, where], lambda i, where: from_y[1, where]], 1, part, columns
                )
            view = lambda: self.reduced.at[:, mine] if order == "xz" else self.reduced.at[mine]
            live["core2"] = copies.send(view, view, place.other_core)
            return engine.transfer("core", 2 * half * row_bytes)

        def end():
            live["core2"].wait_recv()

        middle_steps = [after_core, after_y, after_x] if order == "yxz" else [after_core, after_x]
        self.steps = [start] + middle_steps + [after_z, after_gather, end]


def lane_mean(value):
    return jnp.mean(value, axis=-1, keepdims=True)


def column_sum(value):
    return jnp.sum(value, axis=0, keepdims=True)


ROW_BLOCK = 32


def ffn_plan(n_dp, width, ff):
    down_rows, row_pad = ff // n_dp, padded(width // n_dp)
    sizes = [64, 64] + [128] * (down_rows // 128 - 1) if down_rows % 128 == 0 else [32] * (down_rows // 32)
    plan, base = [], 0
    for size in sizes:
        plan.append((base, size, "yxz" if size % 64 == 0 else "xzy"))
        base += size
    for pair in range(ff // width // 2):
        order = "yxz" if row_pad % 32 == 0 else "xzy"
        plan.append((base, 2 * row_pad, order))
        base += 2 * row_pad
    plan.append((base, row_pad, "xzy"))
    return plan


def layer_kernel(
    nz, plan, words, projected, words_turned, segments, pos_table, query_bias, key_bias, value_bias, out_weight, out_bias, gains, shifts, up_weight, up_bias, down_weight, down_bias, word_cots, ent_cots,
    query_weight, key_weight, value_weight, rows, ent_pos, ent_proj, ids,
    word_out, ent_out, word_grad, ffn_reduced, attn_reduced, ent_reduced, bias_out, table_grad, touched,
    hidden_turned_in, query_words_in, query_ents_in, keys_in, values_in, probs_in, *scratch,
):
    (from_y_mixed, grad_mixed, grad_one, given, ffn_sum, attn_sum, ent_sum, bias_held, bias_from, all_rows, bias_heads, bias_middle,
     ffn_grads, grad_mixed_here, row_parts, mixed, ent_keep) = scratch[:17]
    copies = Copies(*scratch[-3:])
    engine = Engine()
    place = Place(nz)
    z, x, y, core = place.z, place.x, place.y, place.core
    n_dp = 2 * nz
    tokens, half = mixed.shape
    width = 2 * half
    ents = rows.shape[0]
    all_words = tokens - ents
    word_half, ent_half = all_words // 2, ents // 2
    part_tokens = tokens // 2
    ff = up_weight.shape[1]
    parts = ff // width
    row_part, row_pad, down_rows = width // n_dp, padded(width // n_dp), ff // n_dp
    partners = [place.other_core, place.other_y, place.other_x] + place.ahead
    announce(partners)

    jobs = {"ffn": [], "attn": [], "ent": []}

    def make_jobs(names, sources):
        at = 17
        for name, number, base, size, order, columns in plan:
            grads, reduced = sources.get(name, (None, None))
            if name == "attn" and grads is not None:
                grads, reduced = grads.at[number], reduced.at[number]
            job = Job(grads, reduced, base, size, order, columns)
            used = len(job.scratch(nz))
            if name in names:
                job.prepare(engine, place, copies, scratch[at : at + used])
                jobs[name].append(job)
            at += used

    make_jobs(["ffn"], {"ffn": (ffn_grads, ffn_sum)})

    def token_rows(side):
        return span(side * word_half, word_half, LANES), span(all_words + side * ent_half, ent_half, 64)

    mine, theirs = token_rows(y), token_rows(1 - y)
    own_columns, other_columns = span(y * half, half, LANES), span((1 - y) * half, half, LANES)
    word_part, ent_part = pl.ds(0, word_half), pl.ds(word_half, ent_half)
    mixed_copies = []
    scale = 1.0 / math.sqrt(HEAD)
    tiles = tokens // LANES

    def attend_phase(
        hidden_turned, query_words, query_ents, keys, values, probs, query_here, key_here, value_here, pos_here, values_turned, mask,
    ):
        weight_copies = [
            copies.local(lambda: pos_table, lambda: pos_here),
            copies.local(lambda: query_weight.at[pl.ds(2, 2), :, own_columns], lambda: query_here),
            copies.local(lambda: key_weight.at[:, own_columns], lambda: key_here),
            copies.local(lambda: value_weight.at[:, own_columns], lambda: value_here),
        ]
        word_rows = pl.ds(0, all_words)
        targets = [query_words, query_ents, keys, values]
        for i, target in enumerate(targets):
            weight_copies.append(
                copies.local(lambda i=i: projected.at[i], lambda target=target: target.at[word_rows])
            )
        weight_copies.append(copies.local(lambda: words_turned, lambda: hidden_turned.at[:, word_rows]))
        position = as_column(ent_pos[pl.ds(core, 1), :])
        picks = []
        for j in range(all_words // LANES):
            number = lax.broadcasted_iota(jnp.int32, (ents, LANES), 1) + j * LANES
            picks.append(jnp.where(position == number, 1.0, 0.0))
        pick = jnp.concatenate(picks, axis=1)
        word_seg = segments[pl.ds(core, 1), :].astype(F32)
        ent_seg = jnp.sum(pick * word_seg, axis=1, keepdims=True)
        weight_copies[0].wait()
        ent_hidden = dot(rows[...], ent_proj[...]) + dot(pick.astype(LOW), pos_here[...])
        ent_keep[...] = jnp.where(y == 0, ent_hidden[:ent_half], ent_hidden[ent_half:])
        ent_row = jnp.transpose(jnp.broadcast_to(ent_seg, (ents, LANES)))[:1]
        seg_row = jnp.concatenate([word_seg, ent_row], axis=1)
        seg_column = jnp.concatenate([as_column(word_seg), jnp.broadcast_to(ent_seg, (ents, LANES))], axis=0)
        for j in range(tiles):
            here = slice(j * LANES, (j + 1) * LANES)
            mask[:, here] = jnp.where(seg_column == seg_row[:, here], 0.0, masked_score)
        query_b = query_bias[:, own_columns].astype(F32)
        for copy in weight_copies[1:]:
            copy.wait()
        ent_low = ent_hidden.astype(LOW)
        query_words[all_words:] = (dot(ent_low, query_here[0]) + query_b[2:3]).astype(LOW)
        query_ents[all_words:] = (dot(ent_low, query_here[1]) + query_b[3:4]).astype(LOW)
        keys[all_words:] = (dot(ent_low, key_here[...]) + own_half(key_bias, y)).astype(LOW)
        values[all_words:] = (dot(ent_low, value_here[...]) + own_half(value_bias, y)).astype(LOW)
        hidden_turned[:, all_words:] = jnp.transpose(ent_hidden).astype(LOW)
        values_turned[...] = jnp.transpose(values[...].astype(F32)).astype(LOW)
        spills = [
            copies.local(lambda: query_words, lambda: query_words_in),
            copies.local(lambda: query_ents, lambda: query_ents_in),
            copies.local(lambda: keys, lambda: keys_in),
            copies.local(lambda: values, lambda: values_in),
        ]
        for pair in range(half // LANES):
            lanes = slice(pair * LANES, (pair + 1) * LANES)
            key, turned = keys[:, lanes], values_turned[lanes, :]
            row = lax.broadcasted_iota(jnp.int32, (LANES, tokens), 0)
            own_key, own_turned = [], []
            for head in range(2):
                own_key.append(jnp.where(lane_mask(tokens, head), key, jnp.zeros_like(key)))
                own_rows = (row >= head * HEAD) & (row < (head + 1) * HEAD)
                own_turned.append(jnp.where(own_rows, turned, jnp.zeros_like(turned)))
            for i in range(tiles):
                here = slice(i * LANES, (i + 1) * LANES)
                query_w, query_e = query_words[here, lanes], query_ents[here, lanes]
                part_sum = None
                for head in range(2):
                    raw = jnp.concatenate(
                        [dot_rows(own_key[head][:all_words], query_w), dot_rows(own_key[head][all_words:], query_e)], axis=0
                    )
                    score = raw * scale + mask[:, here]
                    weight = jnp.exp(score - jnp.max(score, axis=0, keepdims=True))
                    prob = (weight * (1.0 / jnp.sum(weight, axis=0, keepdims=True))).astype(LOW)
                    probs[pair * 2 + head, :, here] = prob
                    part = dot(own_turned[head], prob)
                    part_sum = part if part_sum is None else part_sum + part
                mixed[here, lanes] = jnp.transpose(part_sum).astype(LOW)
            heads = pl.ds(pair * 2, 2)
            if pair == 0:
                meet(partners)
            mixed_copies.extend([
                copies.send(
                    lambda lanes=lanes: mixed.at[theirs[0], lanes], lambda lanes=lanes: from_y_mixed.at[word_part, lanes], place.other_y
                ),
                copies.send(
                    lambda lanes=lanes: mixed.at[theirs[1], lanes], lambda lanes=lanes: from_y_mixed.at[ent_part, lanes], place.other_y
                ),
            ])
            spills.append(copies.local(lambda heads=heads: probs.at[heads], lambda heads=heads: probs_in.at[heads]))
        spills.append(copies.local(lambda: hidden_turned, lambda: hidden_turned_in))
        for copy in spills:
            copy.wait()

    pl.run_scoped(
        attend_phase,
        pltpu.VMEM((width, tokens), LOW),
        pltpu.VMEM((tokens, half), LOW),
        pltpu.VMEM((tokens, half), LOW),
        pltpu.VMEM((tokens, half), LOW),
        pltpu.VMEM((tokens, half), LOW),
        pltpu.VMEM((HEADS // 2, tokens, tokens), LOW),
        pltpu.VMEM((2, width, half), LOW),
        pltpu.VMEM((width, half), LOW),
        pltpu.VMEM((width, half), LOW),
        pltpu.VMEM((all_words, width), LOW),
        pltpu.VMEM((half, tokens), LOW),
        pltpu.VMEM((tokens, tokens), F32),
    )
    out_copies, mixed_back = [], []

    def forward_phase(
        out_here, up_here, down_here, word_here, mixed_full, work, normed_low, normal_one, inverse_one,
        act, slope, output, grad_two, grad_two_low, grad_one_low, normed_turned,
    ):
        cot, grad_up_low = output, slope
        weight_copies = [
            copies.local(lambda: out_weight, lambda: out_here),
            copies.local(lambda: words.at[mine[0]], lambda: word_here),
            copies.local(lambda: up_weight, lambda: up_here),
            copies.local(lambda: down_weight, lambda: down_here),
            copies.local(lambda: word_cots, lambda: cot.at[word_part]),
            copies.local(lambda: ent_cots, lambda: cot.at[ent_part]),
        ]
        gain, shift = gains[...].astype(F32), shifts[...].astype(F32)
        out_b, down_b, up_b = row_of(out_bias), row_of(down_bias), row_of(up_bias)
        mixed_full[word_part, own_columns] = mixed[mine[0]]
        mixed_full[ent_part, own_columns] = mixed[mine[1]]
        for copy in weight_copies[:2]:
            copy.wait()
        work[...] = dot(mixed_full[:, own_columns], out_here[own_columns, :])
        for copy in mixed_copies:
            copy.wait_recv()
        mixed_full[:, other_columns] = from_y_mixed[...]
        work[...] += dot(from_y_mixed[...], out_here[other_columns, :])

        def norm_one(residual):
            def step(i, _):
                rows = span(residual[1] + i * ROW_BLOCK, ROW_BLOCK, ROW_BLOCK)
                value = residual[0][span(i * ROW_BLOCK, ROW_BLOCK, ROW_BLOCK)].astype(F32) + (work[rows] + out_b)
                center = value - lane_mean(value)
                inverse = lax.rsqrt(lane_mean(center * center) + norm_eps)
                normal = center * inverse
                result = normal * gain[0:1] + shift[0:1]
                normal_one[rows] = normal
                inverse_one[rows] = jnp.broadcast_to(inverse, (ROW_BLOCK, LANES))
                normed_low[rows] = result.astype(LOW)
                return 0

            return step

        loop(word_half // ROW_BLOCK, norm_one((word_here, 0)), 0, 2)
        loop(ent_half // ROW_BLOCK, norm_one((ent_keep, word_half)), 0, 2)
        weight_copies[2].wait()
        for j in range(parts):
            columns = slice(j * width, (j + 1) * width)
            work[...] = dot(normed_low[...], up_here[:, columns]) + up_b[:, columns]

            def gelu(i, _):
                rows = span(i * ROW_BLOCK, ROW_BLOCK, ROW_BLOCK)
                value = work[rows]
                below = 0.5 * (1.0 + lax.erf(value * (1.0 / math.sqrt(2.0))))
                density = jnp.exp(-0.5 * value * value) * (1.0 / math.sqrt(2.0 * math.pi))
                act[rows, columns] = (value * below).astype(LOW)
                slope[rows, columns] = (below + value * density).astype(LOW)
                return 0

            loop(part_tokens // ROW_BLOCK, gelu)
        normed_turned[...] = jnp.transpose(normed_low[...].astype(F32)).astype(LOW)
        for copy in weight_copies[3:]:
            copy.wait()
        work[...] = dot(act[...], down_here[...])

        def norm_two(i, sums):
            rows = span(i * ROW_BLOCK, ROW_BLOCK, ROW_BLOCK)
            value = (normal_one[rows] * gain[0:1] + shift[0:1]) + (work[rows] + down_b)
            center = value - lane_mean(value)
            inverse = lax.rsqrt(lane_mean(center * center) + norm_eps)
            normal = center * inverse
            cotangent = cot[rows].astype(F32)
            output[rows] = (normal * gain[1:2] + shift[1:2]).astype(LOW)
            scaled = cotangent * gain[1:2]
            result = inverse * (scaled - lane_mean(scaled) - normal * lane_mean(scaled * normal))
            grad_two[rows] = result
            grad_two_low[rows] = result.astype(LOW)
            return (
                sums[0] + column_sum(cotangent * normal),
                sums[1] + column_sum(cotangent),
                sums[2] + column_sum(result),
            )

        nothing = jnp.zeros((1, width), F32)
        gain_two, shift_two, down_sum = loop(part_tokens // ROW_BLOCK, norm_two, (nothing, nothing, nothing), 2)
        quarter, ent_quarter = word_half // 2, ent_half // 2
        out_copies.extend([
            copies.send(
                lambda: output.at[span((1 - core) * quarter, quarter, LANES)], lambda: word_out.at[core], place.other_core
            ),
            copies.send(
                lambda: output.at[span(word_half + (1 - core) * ent_quarter, ent_quarter, 32)],
                lambda: ent_out.at[core],
                place.other_core,
            ),
        ])
        out_local = [
            copies.local(lambda: output.at[span(core * quarter, quarter, LANES)], lambda: word_out.at[core]),
            copies.local(
                lambda: output.at[span(word_half + core * ent_quarter, ent_quarter, 32)], lambda: ent_out.at[core]
            ),
        ]
        engine.clock = 0.0
        engine.free = {}
        def put(base, value):
            ffn_grads[:, :, pl.ds(base, row_part)] = value.astype(LOW).reshape(nz, 2, row_part, width)

        def down_products():
            per = width // down_rows
            for j in range(parts):
                value = dot_columns(act[:, j * width : (j + 1) * width], grad_two_low[...])
                value = value.astype(LOW).reshape(per, down_rows, width)
                for d in range(per):
                    slab = j * per + d
                    ffn_grads[slab // 2, slab % 2, pl.ds(0, down_rows)] = value[d]

        up_sums = []

        def grad_up(j):
            columns = slice(j * width, (j + 1) * width)
            work[...] = dot_rows(grad_two_low[...], down_here[columns, :])

            def grad_gelu(i, total_row):
                rows = span(i * ROW_BLOCK, ROW_BLOCK, ROW_BLOCK)
                value = work[rows] * slope[rows, columns].astype(F32)
                grad_up_low[rows, columns] = value.astype(LOW)
                return total_row + column_sum(value)

            up_sums.append(loop(part_tokens // ROW_BLOCK, grad_gelu, nothing, 2))
            engine.work(1.6)

        def up_product(j):
            columns = slice(j * width, (j + 1) * width)
            put(down_rows + j * row_pad, dot(normed_turned[...], grad_up_low[:, columns]))
            engine.work(0.9)

        downs = [job for job in jobs["ffn"] if job.base < down_rows]
        ups = [job for job in jobs["ffn"] if down_rows <= job.base][:-1]
        down_products()
        engine.clock += 3.0
        for job in downs:
            engine.add(job.steps)
        for j in range(parts):
            grad_up(j)
        work[...] = dot_rows(grad_up_low[...], up_here[...])
        engine.work(2.0)

        def back_one(i, sums):
            rows = span(i * ROW_BLOCK, ROW_BLOCK, ROW_BLOCK)
            upper = grad_two[rows] + work[rows]
            normal = normal_one[rows]
            inverse = inverse_one[rows, 0:1]
            scaled = upper * gain[0:1]
            result = inverse * (scaled - lane_mean(scaled) - normal * lane_mean(scaled * normal))
            grad_one[rows] = result
            grad_one_low[rows] = result.astype(LOW)
            return (
                sums[0] + column_sum(upper * normal),
                sums[1] + column_sum(upper),
                sums[2] + column_sum(result),
            )

        gain_one, shift_one, out_sum = loop(part_tokens // ROW_BLOCK, back_one, (nothing, nothing, nothing), 2)
        engine.work(1.0)
        grad_mixed_here[...] = dot_rows(grad_one_low[...], out_here[other_columns, :]).astype(LOW)
        mixed_back.extend([
            copies.send(lambda: grad_mixed_here.at[word_part], lambda: grad_mixed.at[mine[0]], place.other_y),
            copies.send(lambda: grad_mixed_here.at[ent_part], lambda: grad_mixed.at[mine[1]], place.other_y),
        ])
        engine.transfer("y", part_tokens * half * 2)
        own = dot_rows(grad_one_low[...], out_here[own_columns, :]).astype(LOW)
        grad_mixed[mine[0]] = own[:word_half]
        grad_mixed[mine[1]] = own[word_half:]
        engine.work(1.0)
        for j in range(parts):
            up_product(j)
            if j % 2 == 1:
                engine.add(ups[j // 2].steps)
        put(down_rows + parts * row_pad, dot_columns(mixed_full[...], grad_one_low[...]))
        engine.work(0.8)
        engine.add(jobs["ffn"][-1].steps)
        bias_rows = [out_sum, gain_one, gain_two, shift_one, shift_two] + up_sums + [down_sum]
        for i, row in enumerate(bias_rows):
            bias_middle[i : i + 1] = row
        for copy in out_copies:
            copy.wait_send()
        for copy in out_local:
            copy.wait()

    tall = lambda columns, dtype: pltpu.VMEM((part_tokens, columns), dtype)
    pl.run_scoped(
        forward_phase,
        pltpu.VMEM((width, width), LOW),
        pltpu.VMEM((width, ff), LOW),
        pltpu.VMEM((ff, width), LOW),
        pltpu.VMEM((word_half, width), LOW),
        tall(width, LOW),
        tall(width, F32),
        tall(width, LOW),
        tall(width, F32),
        tall(LANES, F32),
        tall(ff, LOW),
        tall(ff, LOW),
        tall(width, LOW),
        tall(width, F32),
        tall(width, LOW),
        tall(width, LOW),
        pltpu.VMEM((width, part_tokens), LOW),
    )
    live_words = {}

    def backward_phase(
        query_words, query_ents, keys, values, probs, query_here, key_here, value_here, keys_turned,
        grad_query_words, grad_query_ents, grad_keys, grad_values, hidden_turned, grad_hidden, hits, attn_grads, ent_grads, table_here, touched_here,
    ):
        total = grad_one
        make_jobs(["attn", "ent"], {"attn": (attn_grads, attn_sum), "ent": (ent_grads, ent_sum)})
        columns = span(y * half, half, LANES)
        copies_in = [
            copies.local(lambda: values_in, lambda: values),
            copies.local(lambda: keys_in, lambda: keys),
            copies.local(lambda: query_words_in, lambda: query_words),
            copies.local(lambda: query_ents_in, lambda: query_ents),
        ]
        prob_copies = []
        for head in range(probs.shape[0]):
            prob_copies.append(
                copies.local(lambda head=head: probs_in.at[head], lambda head=head: probs.at[head])
            )
        hidden_copy = copies.local(lambda: hidden_turned_in, lambda: hidden_turned)
        weight_copies = [
            copies.local(lambda: query_weight.at[:, :, columns], lambda: query_here),
            copies.local(lambda: key_weight.at[:, columns], lambda: key_here),
            copies.local(lambda: value_weight.at[:, columns], lambda: value_here),
        ]
        for copy in copies_in:
            copy.wait()
        for i in range(half // LANES):
            lanes = slice(i * LANES, (i + 1) * LANES)
            keys_turned[lanes, :] = jnp.transpose(keys[:, lanes].astype(F32)).astype(LOW)
        for copy in mixed_back:
            copy.wait_recv()
        engine.work(2.0)
        def pair_products(pair):
            lanes = slice(pair * LANES, (pair + 1) * LANES)
            word_turned, ent_turned = hidden_turned[:, :all_words], hidden_turned[:, all_words:]
            products = [
                dot(word_turned, grad_query_words[:all_words, lanes]),
                dot(word_turned, grad_query_ents[:all_words, lanes]),
                dot(ent_turned, grad_query_words[all_words:, lanes]),
                dot(ent_turned, grad_query_ents[all_words:, lanes]),
                dot(hidden_turned[...], grad_keys[:, lanes]),
                dot(hidden_turned[...], grad_values[:, lanes]),
            ]
            for i, value in enumerate(products):
                attn_grads[pair, :, :, pl.ds(i * row_pad, row_part)] = value.astype(LOW).reshape(nz, 2, row_part, LANES)
            engine.work(1.5)
            engine.add(jobs["attn"][pair].steps)

        for pair in range(half // LANES):
            lanes = slice(pair * LANES, (pair + 1) * LANES)
            grad_query_w = jnp.zeros((LANES, tokens), F32)
            grad_query_e = jnp.zeros((LANES, tokens), F32)
            grad_key_w = jnp.zeros((all_words, LANES), F32)
            grad_key_e = jnp.zeros((ents, LANES), F32)
            grad_value = jnp.zeros((tokens, LANES), F32)
            for head in range(2):
                own = lane_mask(tokens, head)
                value = values[:, lanes]
                own_value = jnp.where(own, value, jnp.zeros_like(value))
                prob_copies[pair * 2 + head].wait()

                given_heads = grad_mixed[:, lanes]
                grad_scores = probs.at[pair * 2 + head]
                grad_value += dot(grad_scores[...], jnp.where(own, given_heads, jnp.zeros_like(given_heads)))
                for i in range(tiles):
                    where = slice(i * LANES, (i + 1) * LANES)
                    grad_prob = dot_rows(own_value, grad_mixed[where, lanes])
                    prob = grad_scores[:, where].astype(F32)
                    both = prob * grad_prob
                    grad_scores[:, where] = (both - prob * jnp.sum(both, axis=0, keepdims=True)).astype(LOW)
                engine.work(1.7)
                query_w, query_e = query_words[:, lanes], query_ents[:, lanes]
                grad_key_w += dot(grad_scores[:all_words], jnp.where(own, query_w, jnp.zeros_like(query_w)))
                grad_key_e += dot(grad_scores[all_words:], jnp.where(own, query_e, jnp.zeros_like(query_e)))
                row = lax.broadcasted_iota(jnp.int32, (LANES, tokens), 0)
                own_rows = (row >= head * HEAD) & (row < (head + 1) * HEAD)
                turned = keys_turned[lanes, :]
                turned = jnp.where(own_rows, turned, jnp.zeros_like(turned))
                grad_query_w += dot(turned[:, :all_words], grad_scores[:all_words])
                grad_query_e += dot(turned[:, all_words:], grad_scores[all_words:])
                engine.work(1.7)
            grad_query_w = jnp.transpose(grad_query_w) * scale
            grad_query_e = jnp.transpose(grad_query_e) * scale
            grad_key_w, grad_key_e = grad_key_w * scale, grad_key_e * scale
            sums = [
                column_sum(grad_query_w[:all_words]),
                column_sum(grad_query_e[:all_words]),
                column_sum(grad_query_w[all_words:]),
                column_sum(grad_query_e[all_words:]),
                column_sum(grad_key_w) + column_sum(grad_key_e),
                column_sum(grad_value),
            ]
            for i, sum_row in enumerate(sums):
                bias_heads[i : i + 1, lanes] = sum_row
            grad_query_words[:, lanes] = grad_query_w.astype(LOW)
            grad_query_ents[:, lanes] = grad_query_e.astype(LOW)
            grad_keys[:all_words, lanes] = grad_key_w.astype(LOW)
            grad_keys[all_words:, lanes] = grad_key_e.astype(LOW)
            grad_values[:, lanes] = grad_value.astype(LOW)
            engine.work(0.5)
            if pair == 0:
                hidden_copy.wait()
            if pair + 1 < half // LANES:
                pair_products(pair)

        for copy in weight_copies:
            copy.wait()
        ent_rows, word_rows = slice(all_words, tokens), slice(0, all_words)

        def hidden_part(here, first, second):
            grad_hidden[here] = (
                dot_rows(grad_keys[here], key_here[...])
                + dot_rows(grad_values[here], value_here[...])
                + dot_rows(grad_query_words[here], query_here[first])
                + dot_rows(grad_query_ents[here], query_here[second])
            ).astype(LOW)

        hidden_part(ent_rows, 2, 3)
        own_ents = lax.broadcasted_iota(jnp.int32, (ents, width), 0) // ent_half == y
        twice = jnp.concatenate([grad_one[word_half:], grad_one[word_half:]], axis=0)
        ent_sum_part = grad_hidden[ent_rows].astype(F32) + jnp.where(own_ents, twice, 0.0)
        row_parts[0] = dot_rows(ent_sum_part.astype(LOW), ent_proj[...]).astype(LOW)
        rows_copy = copies.send(lambda: row_parts.at[0], lambda: row_parts.at[1], place.other_y)
        row_bytes = ents * ent_proj.shape[0] * 2
        rows_ready = engine.transfer("y", row_bytes)
        engine.work(0.7)
        pair_products(half // LANES - 1)
        ent_copy = copies.send(lambda: grad_hidden.at[theirs[1]], lambda: given.at[ent_part], place.other_y)
        ent_ready = engine.transfer("y", ent_half * width * 2)

        live_rows = {}

        def sum_hidden(start, count, own_start):
            def block(i, _):
                where = span(start + i * 32, 32, 32)
                own = span(own_start + i * 32, 32, 32)
                total[where] = grad_one[where] + (grad_hidden[own].astype(F32) + given[where].astype(F32))
                return 0

            loop(count // 32, block)

        def rows_z():
            rows_copy.wait_recv()
            all_rows[place.dp, core] = row_parts[0] + row_parts[1]
            view = lambda: all_rows.at[place.dp, core]
            live_rows["z"] = [copies.send(view, view, device) for device in place.ahead]
            return engine.transfer("z", row_bytes)

        def rows_x():
            for copy in live_rows["z"]:
                copy.wait_recv()
            live_rows["x"] = []
            for k in range(nz):
                view = lambda k=k: all_rows.at[place.z_ahead(k) * 2 + x, core]
                live_rows["x"].append(copies.send(view, view, place.other_x))
            return engine.transfer("x", nz * row_bytes)

        def rows_core():
            for copy in live_rows["x"]:
                copy.wait_recv()
            view = lambda: all_rows.at[:, core]
            live_rows["core"] = copies.send(view, view, place.other_core)
            return engine.transfer("core", n_dp * row_bytes)

        rows_dev = table_grad.shape[0]
        table_copies = []
        base_row = (place.dp * 4 + place.seq) * rows_dev

        def table_part(i):
            def step():
                if i == 0:
                    live_rows["core"].wait_recv()
                groups = ids.shape[0]
                block = min(table_block, LANES)
                counts = [jnp.zeros((block, ents), LOW) for _ in range(table_block // block)]
                for group in range(groups):
                    asked = ids[group : group + 1, :] - base_row
                    high = jnp.clip(asked >> 7, -1, rows_dev // LANES).astype(F32)
                    high = jnp.broadcast_to(high, (block, ents)).astype(LOW)
                    first_row = i * table_block
                    number = lax.broadcasted_iota(jnp.int32, (block, ents), 0) + first_row % LANES
                    low_hit = jnp.where((asked & (LANES - 1)) == number, 1.0, 0.0).astype(LOW)
                    for k in range(len(counts)):
                        hit = jnp.where(
                            high == jnp.asarray(first_row // LANES + k, LOW), low_hit, jnp.zeros_like(low_hit)
                        )
                        counts[k] = counts[k] + hit
                        hits[k * block : (k + 1) * block, group * ents : (group + 1) * ents] = hit
                count = jnp.concatenate(counts, axis=0).astype(F32)
                here = pl.ds(i * table_block, table_block)
                for copy in table_copies[2 * i - 4 : 2 * i - 2] if i >= 2 else []:
                    copy.wait()
                dps = min(n_dp, 8)
                grad = None
                for first in range(0, n_dp, dps):
                    given_rows = all_rows[first : first + dps].reshape(dps * 2 * ents, ent_proj.shape[0])
                    value = dot(hits[:, first * 2 * ents : (first + dps) * 2 * ents], given_rows)
                    grad = value if grad is None else grad + value
                table_here[i % 2] = grad
                named = jnp.sum(count, axis=1, keepdims=True)
                touched_here[i % 2] = jnp.broadcast_to(named, (table_block, LANES)).astype(LOW)
                table_copies.append(copies.local(lambda: table_here.at[i % 2], lambda: table_grad.at[here]))
                table_copies.append(copies.local(lambda: touched_here.at[i % 2], lambda: touched.at[here]))
                engine.clock += 0.7

            return step

        engine.add(
            [lambda: rows_ready, rows_z, rows_x, rows_core] + [table_part(i) for i in range(rows_dev // table_block)]
        )
        hidden_part(word_rows, 0, 1)
        word_copy = copies.send(lambda: grad_hidden.at[theirs[0]], lambda: given.at[word_part], place.other_y)
        word_ready = engine.transfer("y", word_half * width * 2)
        engine.work(1.5)

        bias_rows = bias_held.shape[0]
        bias_held[...] = jnp.zeros_like(bias_held)
        bias_held[0:6, columns] = bias_heads[0:6]
        bias_held[6:bias_rows] = bias_middle[0 : bias_rows - 6]
        live = {}
        bias_bytes = bias_rows * width * 2

        def bias_send(key, index, device):
            bias_from[2 * index] = bias_held[...].astype(LOW)
            live[key] = copies.send(lambda: bias_from.at[2 * index], lambda: bias_from.at[2 * index + 1], device)
            return engine.transfer(key, bias_bytes)

        def bias_take(key, index):
            live[key].wait_recv()
            bias_held[...] = bias_from[2 * index].astype(F32) + bias_from[2 * index + 1].astype(F32)

        def bias_core():
            return bias_send("core", 0, place.other_core)

        def bias_y():
            bias_take("core", 0)
            return bias_send("y", 1, place.other_y)

        def bias_x():
            bias_take("y", 1)
            return bias_send("x", 2, place.other_x)

        def bias_z():
            bias_take("x", 2)
            bias_from[6] = bias_held[...].astype(LOW)
            live["z"] = [
                copies.send(lambda: bias_from.at[6], lambda k=k: bias_from.at[7 + k], device)
                for k, device in enumerate(place.ahead)
            ]
            return engine.transfer("z", bias_bytes)

        def bias_end():
            value = bias_from[6].astype(F32)
            for k, copy in enumerate(live["z"]):
                copy.wait_recv()
                value = value + bias_from[7 + k].astype(F32)
            bias_out[...] = value

        engine.add([bias_core, bias_y, bias_x, bias_z, bias_end])
        quarter = word_half // 2

        def words_sum():
            word_copy.wait_recv()
            sum_hidden(0, word_half, y * word_half)
            engine.clock += 0.5
            live_words["send"] = copies.send(
                lambda: total.at[span((1 - core) * quarter, quarter, LANES)], lambda: word_grad.at[core], place.other_core
            )
            live_words["own"] = copies.local(
                lambda: total.at[span(core * quarter, quarter, LANES)], lambda: word_grad.at[core]
            )
            return engine.transfer("core", quarter * width * 4)

        def words_end():
            live_words["send"].wait_recv()
            live_words["own"].wait()

        engine.add([lambda: word_ready, words_sum, words_end])

        def ent_products():
            ent_copy.wait_recv()
            sum_hidden(word_half, ent_half, all_words + y * ent_half)
            proj_rows, pos_rows = rows.shape[1] // n_dp, all_words // n_dp
            proj_pad = padded(proj_rows)
            position = ent_pos[pl.ds(core, 1), :]
            picks = []
            for j in range(all_words // LANES):
                number = lax.broadcasted_iota(jnp.int32, (LANES, ents), 0) + j * LANES
                picks.append(jnp.where(number == position, 1.0, 0.0))
            pick = jnp.concatenate(picks, axis=0)
            here = lax.broadcasted_iota(jnp.int32, (all_words, ents), 1) // ent_half == y
            pick = jnp.where(here, pick, 0.0).astype(LOW)
            grad_ent = total[word_half:]
            grad_ent_low = grad_ent.astype(LOW)
            rest = (grad_ent - grad_ent_low.astype(F32)).astype(LOW)
            pos_grad = dot(pick, jnp.concatenate([grad_ent_low, grad_ent_low], axis=0)) + dot(
                pick, jnp.concatenate([rest, rest], axis=0)
            )
            proj_grad = dot_columns(rows[span(y * ent_half, ent_half, 64)], grad_ent_low)
            ent_grads[:, :, pl.ds(0, proj_rows)] = proj_grad.astype(LOW).reshape(nz, 2, proj_rows, width)
            ent_grads[:, :, pl.ds(proj_pad, pos_rows)] = pos_grad.astype(LOW).reshape(nz, 2, pos_rows, width)
            engine.clock += 1.0

        ent_job = jobs["ent"][0]
        engine.add([lambda: ent_ready, ent_products] + ent_job.steps)
        engine.drain()
        for copy in table_copies[-4:]:
            copy.wait()
        copies.finish()

    table_block = 256 if n_dp * 2 * ents <= 2048 else 32
    pl.run_scoped(
        backward_phase,
        pltpu.VMEM((tokens, half), LOW),
        pltpu.VMEM((tokens, half), LOW),
        pltpu.VMEM((tokens, half), LOW),
        pltpu.VMEM((tokens, half), LOW),
        pltpu.VMEM((HEADS // 2, tokens, tokens), LOW),
        pltpu.VMEM((4, width, half), LOW),
        pltpu.VMEM((width, half), LOW),
        pltpu.VMEM((width, half), LOW),
        pltpu.VMEM((half, tokens), LOW),
        pltpu.VMEM((tokens, half), LOW),
        pltpu.VMEM((tokens, half), LOW),
        pltpu.VMEM((tokens, half), LOW),
        pltpu.VMEM((tokens, half), LOW),
        pltpu.VMEM((width, tokens), LOW),
        pltpu.VMEM((tokens, width), LOW),
        pltpu.VMEM((table_block, n_dp * 2 * ents), LOW),
        pltpu.VMEM((half // LANES, nz, 2, 6 * row_pad, LANES), LOW),
        pltpu.VMEM((nz, 2, ent_sum.shape[0], width), LOW),
        pltpu.VMEM((2, table_block, ent_proj.shape[0]), F32),
        pltpu.VMEM((2, table_block, LANES), LOW),
    )
    last_copies = [
        copies.local(lambda: ffn_sum, lambda: ffn_reduced),
        copies.local(lambda: attn_sum, lambda: attn_reduced),
        copies.local(lambda: ent_sum, lambda: ent_reduced),
    ]
    for copy in out_copies:
        copy.wait_recv()
    for copy in last_copies:
        copy.wait()
    copies.finish()


def layer(
    nz, rows_dev, words, projected, words_turned, segments, pos_table, query_bias, key_bias, value_bias, out_weight, out_bias, gains, shifts, up_weight, up_bias, down_weight, down_bias, word_cots, ent_cots,
    query_weight, key_weight, value_weight, rows, ent_pos, ent_proj, ids,
):
    n_dp = 2 * nz
    all_words, width = words.shape
    half = width // 2
    ents, edim = rows.shape
    tokens = all_words + ents
    part, ff = tokens // 2, up_weight.shape[1]
    ffn_blocks = ffn_plan(n_dp, width, ff)
    ffn_rows, attn_rows = ffn_blocks[-1][0] + ffn_blocks[-1][1], 6 * padded(width // n_dp)
    ent_pad = padded(edim // n_dp) + padded(all_words // n_dp)
    bias_rows = 12 + ff // width
    plan = [("ffn", 0, base, size, order, width) for base, size, order in ffn_blocks]
    plan += [("attn", pair, 0, attn_rows, "xz", LANES) for pair in range(half // LANES)]
    plan.append(("ent", 0, 0, ent_pad, "xzy", width))
    scratch = [
        pltpu.VMEM((part, half), LOW),
        pltpu.VMEM((tokens, half), LOW),
        pltpu.VMEM((part, width), F32),
        pltpu.VMEM((part, width), LOW),
        pltpu.VMEM((ffn_rows, width), LOW),
        pltpu.VMEM((half // LANES, 2, attn_rows, LANES), LOW),
        pltpu.VMEM((ent_pad, width), LOW),
        pltpu.VMEM((bias_rows, width), F32),
        pltpu.VMEM((6 + nz, bias_rows, width), LOW),
        pltpu.VMEM((n_dp, 2, ents, edim), LOW),
        pltpu.VMEM((8, half), F32),
        pltpu.VMEM((16, width), F32),
        pltpu.VMEM((nz, 2, ffn_rows, width), LOW),
        pltpu.VMEM((part, half), LOW),
        pltpu.VMEM((2, ents, edim), LOW),
        pltpu.VMEM((tokens, half), LOW),
        pltpu.VMEM((ents // 2, width), F32),
    ]
    remote = 8 + 6 + 1 + 3 + nz + 1 + nz + nz + 2 + 4
    for name, _, base, size, order, columns in plan:
        job = Job(None, None, base, size, order, columns)
        scratch += job.scratch(nz)
        remote += job.remote_count(nz)
    scratch += copy_semaphores(remote, 60 + 2 * (rows_dev // 32))
    return call(
        functools.partial(layer_kernel, nz, plan),
        [
            ((2, all_words // 4, width), LOW),
            ((2, ents // 4, width), LOW),
            ((2, all_words // 4, width), F32),
            ((ffn_rows, width), LOW),
            ((half // LANES, 2, attn_rows, LANES), LOW),
            ((ent_pad, width), LOW),
            ((bias_rows, width), F32),
            ((rows_dev, edim), F32),
            ((rows_dev, LANES), LOW),
            ((width, tokens), LOW),
            ((tokens, half), LOW),
            ((tokens, half), LOW),
            ((tokens, half), LOW),
            ((tokens, half), LOW),
            ((HEADS // 2, tokens, tokens), LOW),
        ],
        [ANY, ANY, ANY, IN_VMEM, ANY] + [IN_VMEM] * 3 + [ANY] + [IN_VMEM] * 3 + [ANY, IN_VMEM, ANY, IN_VMEM] + [ANY] * 2 + [ANY] * 3 + [IN_VMEM] * 4,
        [ANY] * 6 + [IN_VMEM] + [ANY] * 8,
        scratch,
        "layer",
        2,
    )(words, projected, words_turned, segments, pos_table, query_bias, key_bias, value_bias, out_weight, out_bias, gains, shifts, up_weight, up_bias, down_weight, down_bias, word_cots, ent_cots,
      query_weight, key_weight, value_weight, rows, ent_pos, ent_proj, ids)[:9]


def last_kernel(
    n_dp, table_grad, touched, first, second, ffn_in, attn_in, ent_in, bias, words_in, ents_in, words_grad_in,
    table_out, update, new_second, proj_out, pos_out, query_out, key_out, value_out, out_out, up_out, down_out,
    query_bias, gain_grad, shift_grad, key_bias, value_bias, out_bias, down_bias, up_bias, word_out, ent_out, word_grad,
    ffn, attn, ent, words, ents, words_grad, proj_grad, pos_grad, query_grad, key_grad, value_grad, out_grad, up_grad, down_grad, sems,
):
    into = [(ffn_in, ffn), (attn_in, attn), (ent_in, ent), (words_in, words), (ents_in, ents), (words_grad_in, words_grad)]
    arrive = [pltpu.make_async_copy(src, dst, sems.at[i]) for i, (src, dst) in enumerate(into)]
    onward = [(down_grad, down_out), (up_grad, up_out), (out_grad, out_out), (proj_grad, proj_out), (pos_grad, pos_out)]
    onward += [(key_grad, key_out), (value_grad, value_out), (query_grad, query_out)]
    onward += [(words, word_out), (ents, ent_out), (words_grad, word_grad)]
    leave = [pltpu.make_async_copy(src, dst, sems.at[len(into) + i]) for i, (src, dst) in enumerate(onward)]

    @pl.when(pl.program_id(0) == 0)
    def _():
        for copy in arrive:
            copy.start()

    step = pl.program_id(0)
    grad = table_grad[...]
    hit = touched[:, 0:1].astype(F32) > 0.0
    mean_new = beta_one * first[...] + (1.0 - beta_one) * grad
    square_new = beta_two * second[...] + (1.0 - beta_two) * grad * grad
    direction = (
        mean_new
        / (1.0 - beta_one**adam_step)
        / (jnp.sqrt(square_new / (1.0 - beta_two**adam_step)) + adam_eps)
    )
    table_out[...] = grad
    update[...] = jnp.where(hit, direction, 0.0)
    new_second[...] = jnp.where(hit, square_new, second[...])
    width = ffn.shape[1]
    part, down_rows = out_grad.shape[0], down_grad.shape[0]
    pad = padded(part)
    proj_pad = padded(proj_grad.shape[0])
    parts = up_grad.shape[1] // width
    pairs = attn.shape[0]
    half = pairs * LANES

    @pl.when(step == 0)
    def _():
        arrive[0].wait()
        down_grad[...] = ffn[:down_rows].astype(F32)
        leave[0].start()
        for copy in arrive[3:]:
            copy.wait()
        for copy in leave[8:]:
            copy.start()

    @pl.when(step == 1)
    def _():
        for j in range(parts):
            base = down_rows + j * pad
            up_grad[:, j * width : (j + 1) * width] = ffn[base : base + part].astype(F32)
        leave[1].start()
        arrive[1].wait()
        arrive[2].wait()

    @pl.when(step == 2)
    def _():
        base = down_rows + parts * pad
        out_grad[...] = ffn[base : base + part].astype(F32)
        proj_grad[...] = ent[: proj_grad.shape[0]].astype(F32)
        pos_grad[...] = ent[proj_pad : proj_pad + pos_grad.shape[0]].astype(F32)
        for side in range(2):
            for pair in range(pairs):
                columns = slice(side * half + pair * LANES, side * half + (pair + 1) * LANES)
                key_grad[:, columns] = attn[pair, side, 4 * pad : 4 * pad + part].astype(F32)
                value_grad[:, columns] = attn[pair, side, 5 * pad : 5 * pad + part].astype(F32)
        for copy in leave[2:7]:
            copy.start()

    @pl.when(step == 2)
    def _():
        for side in range(2):
            for pair in range(pairs):
                columns = slice(side * half + pair * LANES, side * half + (pair + 1) * LANES)
                for i in range(4):
                    query_grad[i, :, columns] = attn[pair, side, i * pad : i * pad + part].astype(F32)
        leave[7].start()

    @pl.when(step == 3)
    def _():
        dp = lax.axis_index("dp")

        def own_columns(value, size, start):
            lane = lax.broadcasted_iota(jnp.int32, (value.shape[1], size), 0)
            want = lax.broadcasted_iota(jnp.int32, (value.shape[1], size), 1) + start
            pick = jnp.where(lane == want, 1.0, 0.0)
            return jnp.dot(value, pick, precision=lax.Precision.HIGHEST, preferred_element_type=F32)

        own = own_columns(bias[...], part, dp * part)
        query_bias[...] = own[0:4]
        gain_grad[...] = own[7:9]
        shift_grad[...] = own[9:11]
        for vector, i in ((key_bias, 4), (value_bias, 5), (out_bias, 6), (down_bias, 11 + parts)):
            vector[...] = own[i : i + 1].reshape(part)
        up = jnp.concatenate([bias[11 + j : 12 + j] for j in range(parts)], axis=1)
        size = up_bias.shape[0]
        if size % LANES == 0:
            per = width // size
            row = bias[pl.ds(11 + dp // per, 1), :]
            chosen = row[:, :size]
            for i in range(1, per):
                chosen = jnp.where(dp % per == i, row[:, i * size : (i + 1) * size], chosen)
            up_bias[...] = chosen.reshape(size)
        else:
            up_bias[...] = own_columns(up, size, dp * size).reshape(size)

    @pl.when(step == pl.num_programs(0) - 1)
    def _():
        for copy in leave:
            copy.wait()


def last(n_dp, ff, all_words, table_grad, touched, first, second, ffn, attn, ent, bias, words_low, ents_low, words_grad):
    width = ffn.shape[1]
    rows, edim = first.shape
    part = width // n_dp
    block = 512
    blocked = lambda columns: pl.BlockSpec((block, columns), lambda i: (i, 0))
    whole = lambda shape: pl.BlockSpec(shape, lambda i: (0,) * len(shape))
    shapes = [
        (edim // n_dp, width),
        (all_words // n_dp, width),
        (4, part, width),
        (part, width),
        (part, width),
        (part, width),
        (part, ff),
        (ff // n_dp, width),
        (4, part),
        (2, part),
        (2, part),
        (part,),
        (part,),
        (part,),
        (part,),
        (ff // n_dp,),
    ]
    through = [words_low, ents_low, words_grad]
    return pl.pallas_call(
        functools.partial(last_kernel, n_dp),
        grid=(rows // block,),
        out_shape=[jax.ShapeDtypeStruct((rows, edim), F32)] * 3
        + [jax.ShapeDtypeStruct(shape, F32) for shape in shapes]
        + [jax.ShapeDtypeStruct(array.shape, array.dtype) for array in through],
        in_specs=[blocked(edim), blocked(LANES), blocked(edim), blocked(edim)]
        + [ANY] * 3
        + [whole(bias.shape)]
        + [ANY] * 3,
        out_specs=[blocked(edim)] * 3 + [ANY] * 8 + [whole(shape) for shape in shapes[8:]] + [ANY] * 3,
        scratch_shapes=[pltpu.VMEM(array.shape, array.dtype) for array in [ffn, attn, ent] + through]
        + [pltpu.VMEM(shape, F32) for shape in shapes[:8]]
        + [pltpu.SemaphoreType.DMA((17,))],
        compiler_params=pltpu.CompilerParams(vmem_limit_bytes=VMEM_BYTES),
        name="last",
    )(table_grad, touched, first, second, ffn, attn, ent, bias, words_low, ents_low, words_grad)


def on_device(
    word_states,
    segments,
    entity_ids,
    entity_pos,
    ent_table,
    first_moment,
    second_moment,
    ent_proj,
    pos_table,
    query_weight,
    query_bias,
    key_weight,
    key_bias,
    value_weight,
    value_bias,
    out_weight,
    out_bias,
    norm_gain,
    norm_shift,
    up_weight,
    up_bias,
    down_weight,
    down_bias,
    word_cot,
    ent_cot,
):
    n_dp = lax.axis_size("dp")
    nz = n_dp // 2
    width, ff = up_weight.shape
    all_words = segments.shape[1]
    words, word_cots, ent_cots, all_ids, rows, projected, words_turned = fetch(
        nz, word_states, word_cot, ent_cot, entity_ids, query_bias, key_bias, value_bias, ent_table, query_weight, key_weight, value_weight
    )
    ents = entity_ids.shape[1]
    word_out, ent_out, word_grad, ffn_sum, attn_sum, ent_sum, bias_sum, table_grad, touched = layer(
        nz, ent_table.shape[0], words, projected, words_turned, segments, pos_table, query_bias, key_bias, value_bias, out_weight, out_bias, norm_gain, norm_shift, up_weight, up_bias, down_weight, down_bias,
        word_cots, ent_cots, query_weight, key_weight, value_weight,
        rows, entity_pos, ent_proj, all_ids.reshape(-1, ents),
    )
    (table_grad, table_update, new_second, proj_grad, pos_grad, query_grad, key_grad, value_grad, out_grad, up_grad, down_grad,
     query_bias_grad, gain_grad, shift_grad, key_bias_grad, value_bias_grad, out_bias_grad, down_bias_grad, up_bias_grad,
     word_out, ent_out, word_grad,
    ) = last(
        n_dp, ff, all_words, table_grad, touched, first_moment, second_moment, ffn_sum, attn_sum, ent_sum, bias_sum, word_out, ent_out, word_grad
    )
    return (
        word_out,
        ent_out,
        word_grad,
        proj_grad,
        pos_grad,
        query_grad,
        query_bias_grad,
        key_grad,
        key_bias_grad,
        value_grad,
        value_bias_grad,
        out_grad,
        out_bias_grad,
        gain_grad,
        shift_grad,
        up_grad,
        up_bias_grad,
        down_grad,
        down_bias_grad,
        table_grad,
        table_update,
        new_second,
    )


def solution(mesh):
    return jax.shard_map(
        on_device,
        mesh=mesh,
        in_specs=(
            P("dp", "seq", None),
            P("dp", None),
            P("dp", None),
            P("dp", None),
            P(("dp", "seq"), None),
            P(("dp", "seq"), None),
            P(("dp", "seq"), None),
            P(),
            P(),
            P(),
            P(),
            P(),
            P(),
            P(),
            P(),
            P(),
            P(),
            P(),
            P(),
            P(),
            P(),
            P(),
            P(),
            P("dp", "seq", None),
            P("dp", "seq", None),
        ),
        out_specs=(
            P("dp", "seq", None),
            P("dp", "seq", None),
            P("dp", "seq", None),
            P("dp", None),
            P("dp", None),
            P(None, "dp", None),
            P(None, "dp"),
            P("dp", None),
            P("dp"),
            P("dp", None),
            P("dp"),
            P("dp", None),
            P("dp"),
            P(None, "dp"),
            P(None, "dp"),
            P("dp", None),
            P("dp"),
            P("dp", None),
            P("dp"),
            P(("dp", "seq"), None),
            P(("dp", "seq"), None),
            P(("dp", "seq"), None),
        ),
        check_vma=False,
    )
```
